32 devices in a mesh: ctx: 8 (over y, x, core), head: 4 (over z).
Axes of the slice: x: 2, y: 2, z: 4, core: 2. Of those that a mesh axis runs over, the one named last changes fastest.
Arguments:
- xbc: bfloat16 [2048, 20480], P(('ctx', 'head')), may hold values from -6 to 6
- dt_raw: bfloat16 [2048, 256], P(('ctx', 'head')), may hold values from -7.5 to -0.5
- conv_weight: float32 [4, 20480], replicated, may hold values from -0.6 to 0.6
- conv_bias: float32 [20480], replicated, may hold values from -0.7 to -0.3
- a_log: float32 [256], replicated, may hold values from -5.6 to 2.8
- dt_bias: float32 [256], replicated, may hold values from -0.5 to 0.5
- skip_gain: float32 [256], replicated, may hold values from 0.5 to 1.5
Outputs:
- mixed: bfloat16 [2048, 16384], P('ctx', 'head')
The draws below stay inside these ranges and needn't reach their ends.
All inputs are finite; a program needn't handle non-finite values.
Results may differ from the reference program's by a relative error of at most 0.0067.
Values may be sent and summed in bfloat16 or wider, within the bound.
No kernel may reach another device: no remote copies, remote signals or barrier semaphores. Data moves between devices by JAX's collectives and lax.ppermute only.
A program may use at most 192 MiB of HBM per device.

```python
import math
import jax
import jax.numpy as jnp
from jax import lax

HEADS = 256
HEAD_DIM = 64
STATE = 256
GROUPS = 8
BLOCK = 256
CONV_DIM = 20480
SEQUENCE_TOKENS = 2048


segment_count = 12


def draw_xbc(key, part):
    key = jax.random.fold_in(key, 31)
    values = jnp.clip(jax.random.normal(key, (SEQUENCE_TOKENS, CONV_DIM), jnp.float32), -6.0, 6.0)
    return values.astype(jnp.bfloat16)


def draw_conv_weight(key, part):
    key = jax.random.fold_in(key, 37)
    first, second = jax.random.split(key, 2)
    flipped = jnp.where(jax.random.bernoulli(first, 0.5, (4, CONV_DIM)), 1.0, -1.0)
    magnitude = jax.random.uniform(second, (4, CONV_DIM), jnp.float32, 0.4, 0.6)
    return (flipped * magnitude).astype(jnp.float32)


def draw_conv_bias(key, part):
    key = jax.random.fold_in(key, 41)
    offset = jax.random.uniform(key, (CONV_DIM,), jnp.float32, -0.2, 0.2)
    return (offset - 0.5).astype(jnp.float32)


def draw_dt_raw(key, part):
    key = jax.random.fold_in(key, 11)
    first, secondary_pass, third = jax.random.split(key, 3)
    base = jax.random.uniform(first, (SEQUENCE_TOKENS, HEADS), jnp.float32, -7.0, -5.0)
    token_positions = jax.random.randint(secondary_pass, (segment_count,), 0, SEQUENCE_TOKENS)
    struck = jnp.any(jnp.arange(SEQUENCE_TOKENS)[:, None] == token_positions[None, :], axis=1)
    lifted = jax.random.uniform(third, (SEQUENCE_TOKENS, HEADS), jnp.float32, -2.5, -0.5)
    return jnp.where(struck[:, None], lifted, base).astype(jnp.bfloat16)


def draw_a_log(key, part):
    key = jax.random.fold_in(key, 23)
    first, secondary_pass, third = jax.random.split(key, 3)
    slow = jax.random.uniform(first, (HEADS,), jnp.float32, math.log(0.004), math.log(0.02))
    fast = jax.random.uniform(secondary_pass, (HEADS,), jnp.float32, math.log(3.0), math.log(16.0))
    share = 0.5
    picked = jax.random.uniform(third, (HEADS,), jnp.float32) < share
    return jnp.where(picked, fast, slow).astype(jnp.float32)


def setup_inputs(seed: int = 0) -> dict:
    key_list = jax.random.split(jax.random.key(seed), 8)
    return {
        "xbc": draw_xbc(jax.random.fold_in(key_list[7], 71), 0),
        "dt_raw": draw_dt_raw(jax.random.fold_in(key_list[7], 71), 0),
        "conv_weight": draw_conv_weight(jax.random.fold_in(key_list[7], 71), 0),
        "conv_bias": draw_conv_bias(jax.random.fold_in(key_list[7], 71), 0),
        "a_log": draw_a_log(jax.random.fold_in(key_list[7], 71), 0),
        "dt_bias": jnp.clip(jax.random.uniform(key_list[5], (HEADS,), jnp.float32, -0.5, 0.5), -0.5, 0.5),
        "skip_gain": jnp.clip(jax.random.uniform(key_list[6], (HEADS,), jnp.float32, 0.5, 1.5), 0.5, 1.5),
    }


def convolve(rows, edge, conv_weight, conv_bias):
    count = rows.shape[0]
    wide = jnp.concatenate([edge, rows], 0).astype(jnp.float32)
    acc = conv_bias[None, :] + conv_weight[0] * wide[0:count]
    acc = acc + conv_weight[1] * wide[1:count + 1]
    acc = acc + conv_weight[2] * wide[2:count + 2]
    acc = acc + conv_weight[3] * wide[3:count + 3]
    return jax.nn.silu(acc).astype(jnp.bfloat16)


def reference(xbc, dt_raw, conv_weight, conv_bias, a_log, dt_bias, skip_gain):
    inner = HEADS * HEAD_DIM
    per_group = HEADS // GROUPS
    nchunk = SEQUENCE_TOKENS // BLOCK
    rate = (-jnp.exp(a_log)).reshape(GROUPS, per_group)
    bias_dt = dt_bias.reshape(GROUPS, per_group)
    skip = skip_gain.reshape(GROUPS, per_group)
    lower = jnp.arange(BLOCK)[:, None] >= jnp.arange(BLOCK)[None, :]
    high = lax.Precision.HIGHEST

    def step_fn(carry, item):
        state, edge = carry
        rows, raw_dt = item
        act = convolve(rows, edge, conv_weight, conv_bias)
        xs = act[:, :inner].reshape(BLOCK, GROUPS, per_group, HEAD_DIM).astype(jnp.float32)
        bmat = act[:, inner:inner + GROUPS * STATE].reshape(BLOCK, GROUPS, STATE).astype(jnp.float32)
        cmat = act[:, inner + GROUPS * STATE:].reshape(BLOCK, GROUPS, STATE).astype(jnp.float32)
        steps = jax.nn.softplus(raw_dt.astype(jnp.float32).reshape(BLOCK, GROUPS, per_group) + bias_dt)
        cum = jnp.cumsum(steps * rate, axis=0)
        scores = jnp.einsum('qgn,kgn->gqk', cmat, bmat, precision=high)
        order = jnp.transpose(cum, (1, 2, 0))
        gap = order[..., :, None] - order[..., None, :]
        decay = jnp.exp(jnp.where(lower, gap, -jnp.inf))
        mixing = (scores[:, None] * decay * jnp.transpose(steps, (1, 2, 0))[..., None, :]).astype(jnp.bfloat16)
        local = jnp.einsum('gjqk,kgjp->qgjp', mixing.astype(jnp.float32), xs, precision=high)
        lifted = cmat[:, :, None, :] * jnp.exp(cum)[..., None]
        carried = jnp.einsum('qgjn,gjnp->qgjp', lifted, state, precision=high)
        total = local + carried + skip[..., None] * xs
        tail = jnp.exp(cum[BLOCK - 1][None] - cum) * steps
        loaded = (bmat[:, :, None, :] * tail[..., None]).astype(jnp.bfloat16)
        block_state = jnp.einsum('kgjn,kgjp->gjnp', loaded.astype(jnp.float32), xs, precision=high)
        new_state = jnp.exp(cum[BLOCK - 1])[..., None, None] * state + block_state
        return (new_state, rows[BLOCK - 3:]), total.astype(jnp.bfloat16).reshape(BLOCK, inner)

    start = (jnp.zeros((GROUPS, per_group, STATE, HEAD_DIM), jnp.float32), jnp.zeros((3, CONV_DIM), jnp.bfloat16))
    items = (xbc.reshape(nchunk, BLOCK, CONV_DIM), dt_raw.reshape(nchunk, BLOCK, HEADS))
    _, outputs = lax.scan(step_fn, start, items)
    return outputs.reshape(SEQUENCE_TOKENS, inner)
```

```python
import functools

import jax
import jax.numpy as jnp
from jax import lax
from jax.experimental import pallas as pl
from jax.experimental.pallas import tpu as pltpu
from jax.sharding import PartitionSpec as P

HEADS = 256
HEAD_DIM = 64
STATE = 256
GROUPS = 8
BLOCK = 256


def from_behind(block, axis, distance):
    devices = range(lax.axis_size(axis))
    route = [(i - distance, i) for i in devices if i - distance in devices]
    return lax.ppermute(block, axis, route)


def carried_in(array, axis, combine, identity):
    length, index = (lax.axis_size(axis), lax.axis_index(axis))
    everything = jax.tree.map(lambda part: lax.all_gather(part, axis), array)
    start = jax.tree.map(
        lambda part, zero: jnp.broadcast_to(jnp.asarray(zero, part.dtype), part.shape),
        array,
        identity,
    )

    def hop(k, before):
        reached = k < index
        new = combine(before, jax.tree.map(lambda part: part[k], everything))
        return jax.tree.map(lambda a, b: jnp.where(reached, a, b), new, before)

    return lax.fori_loop(0, length, hop, start)


def convolve(rows, edge, weight, bias):
    count = rows.shape[0]
    wide = jnp.concatenate([edge, rows], 0).astype(jnp.float32)
    acc = bias[None, :] + weight[0] * wide[0:count]
    acc = acc + weight[1] * wide[1 : count + 1]
    acc = acc + weight[2] * wide[2 : count + 2]
    acc = acc + weight[3] * wide[3 : count + 3]
    return jax.nn.silu(acc).astype(jnp.bfloat16)


def rearrange_heads(rows, shards, per_dev, groups_dev, per_group):
    count = rows.shape[0]
    inner = HEADS * HEAD_DIM
    replicate_groups = max(1, per_group // per_dev)
    heads_part = rows[:, :inner].reshape(count, shards, per_dev * HEAD_DIM)
    b_part = rows[:, inner : inner + GROUPS * STATE].reshape(count, GROUPS, STATE)
    c_part = rows[:, inner + GROUPS * STATE :].reshape(count, GROUPS, STATE)
    b_part = jnp.repeat(b_part, replicate_groups, axis=1).reshape(count, shards, groups_dev * STATE)
    c_part = jnp.repeat(c_part, replicate_groups, axis=1).reshape(count, shards, groups_dev * STATE)
    return jnp.concatenate([heads_part, b_part, c_part], axis=2)


def inner_block(xs, bmat, cmat, steps, cum):
    size = xs.shape[0]
    lower = jnp.arange(size)[:, None] >= jnp.arange(size)[None, :]
    scores = jnp.einsum("qgn,kgn->gqk", cmat, bmat, preferred_element_type=jnp.float32)
    order = jnp.transpose(cum, (1, 2, 0))
    gap = order[..., :, None] - order[..., None, :]
    decay = jnp.exp(jnp.where(lower, gap, -jnp.inf))
    mixing = (scores[:, None] * decay * jnp.transpose(steps, (1, 2, 0))[..., None, :]).astype(
        jnp.bfloat16
    )
    local = jnp.einsum("gjqk,kgjp->qgjp", mixing, xs, preferred_element_type=jnp.float32)
    tail = jnp.exp(cum[size - 1][None] - cum) * steps
    loaded = (bmat[:, :, None, :].astype(jnp.float32) * tail[..., None]).astype(jnp.bfloat16)
    block_state = jnp.einsum("kgjn,kgjp->gjnp", loaded, xs, preferred_element_type=jnp.float32)
    return (local, block_state)


def on_device(xbc, dt_raw, conv_weight, conv_bias, a_log, dt_bias, skip_gain):
    tok = xbc.shape[0]
    shards = lax.axis_size("head")
    per_dev = HEADS // shards
    per_group = HEADS // GROUPS
    groups_dev = max(1, per_dev // per_group)
    heads_per_cluster = per_dev // groups_dev
    sent = rearrange_heads(xbc, shards, per_dev, groups_dev, per_group)
    mine, rates = (
        lax.all_to_all(sent, "head", split_axis=1, concat_axis=0, tiled=True),
        lax.all_to_all(
            dt_raw.reshape(tok, shards, per_dev), "head", split_axis=1, concat_axis=0, tiled=True
        ),
    )
    slab = tok * shards
    mine = mine.reshape(slab, mine.shape[2])
    rates = rates.reshape(slab, per_dev)
    shard = lax.axis_index("head")
    taps = lax.dynamic_index_in_dim(
        rearrange_heads(conv_weight, shards, per_dev, groups_dev, per_group),
        shard,
        1,
        keepdims=False,
    )
    offset = lax.dynamic_index_in_dim(
        rearrange_heads(conv_bias[None, :], shards, per_dev, groups_dev, per_group),
        shard,
        1,
        keepdims=False,
    )
    edge = from_behind(mine[slab - 3 :], "ctx", 1)
    mine = convolve(mine, edge, taps, offset[0])
    nchunk = slab // BLOCK
    width = per_dev * HEAD_DIM
    xs = mine[:, :width].reshape(nchunk, BLOCK, groups_dev, heads_per_cluster, HEAD_DIM)
    bmat = mine[:, width : width + groups_dev * STATE].reshape(nchunk, BLOCK, groups_dev, STATE)
    cmat = mine[:, width + groups_dev * STATE :].reshape(nchunk, BLOCK, groups_dev, STATE)
    first = shard * per_dev
    rate = (-jnp.exp(lax.dynamic_slice_in_dim(a_log, first, per_dev))).reshape(
        groups_dev, heads_per_cluster
    )
    bias_dt = lax.dynamic_slice_in_dim(dt_bias, first, per_dev).reshape(
        groups_dev, heads_per_cluster
    )
    skip = lax.dynamic_slice_in_dim(skip_gain, first, per_dev).reshape(
        groups_dev, heads_per_cluster
    )
    steps = jax.nn.softplus(
        rates.astype(jnp.float32).reshape(nchunk, BLOCK, groups_dev, heads_per_cluster) + bias_dt
    )
    cum = jnp.cumsum(steps * rate, axis=1)

    def block_step(carry, item):
        held, product = carry
        x_part, b_part, c_part, step_part, cum_part = item
        local, block_state = inner_block(x_part, b_part, c_part, step_part, cum_part)
        lifted = c_part.astype(jnp.float32)[:, :, None, :] * jnp.exp(cum_part)[..., None]
        carried = jnp.einsum("qgjn,gjnp->qgjp", lifted, held, precision=lax.Precision.HIGHEST)
        partial_out = local + carried + skip[..., None] * x_part.astype(jnp.float32)
        end = jnp.exp(cum_part[BLOCK - 1])
        return ((end[..., None, None] * held + block_state, product * end), (partial_out, product))

    zero_state = jnp.zeros((groups_dev, heads_per_cluster, STATE, HEAD_DIM), jnp.float32)
    unit = jnp.ones((groups_dev, heads_per_cluster), jnp.float32)
    (slab_state, slab_decay), (partials, product_in) = lax.scan(
        block_step, (zero_state, unit), (xs, bmat, cmat, steps, cum)
    )

    def combine(preceding_state, later):
        return (
            preceding_state[0] * later[0],
            later[0][..., None, None] * preceding_state[1] + later[1],
        )

    _, entering = carried_in((slab_decay, slab_state), "ctx", combine, (unit, zero_state))
    projected = jnp.einsum(
        "cqgn,gjnp->cqgjp", cmat.astype(jnp.float32), entering, precision=lax.Precision.HIGHEST
    )
    factor = jnp.exp(cum) * product_in[:, None]
    total = partials + factor[..., None] * projected
    return total.astype(jnp.bfloat16).reshape(slab, width)


PAIR = 2
LANES = 128
SUB = 512
PIECES = (1, 1, 1, 1)
LOG2E = 1.4426950408889634
F32, BF16 = jnp.float32, jnp.bfloat16


def halves(value, count):
    parts = []
    for _ in range(count):
        part = value.astype(BF16)
        parts.append(part)
        value = value - part.astype(F32)
    return parts


def spread(first_head, width, copies):
    lane = lax.broadcasted_iota(jnp.int32, (copies * LANES, width), 0) % LANES
    column = lax.broadcasted_iota(jnp.int32, (copies * LANES, width), 1)
    return (lane == first_head + column // HEAD_DIM).astype(BF16)


def dot(a, b):
    return jnp.dot(a, b, preferred_element_type=F32)


def conv_kernel(blocks, has_step, *refs):
    rows = refs[0 : 4 * blocks : 4]
    edges = refs[1 : 4 * blocks : 4]
    taps = refs[2 : 4 * blocks : 4]
    biases = refs[3 : 4 * blocks : 4]
    refs = refs[4 * blocks :]
    if has_step:
        step_ref, out, *wides = refs
    else:
        out, *wides = refs
    start = 0
    for row, edge, tap, bias, wide in zip(rows, edges, taps, biases, wides):
        count, width = row.shape
        wide[5:8] = edge[...].astype(F32)
        wide[8:] = row[...].astype(F32)
        acc = bias[...] + tap[0:1] * wide[5 : 5 + count]
        acc = acc + tap[1:2] * wide[6 : 6 + count]
        acc = acc + tap[2:3] * wide[7 : 7 + count]
        acc = acc + tap[3:4] * wide[8 : 8 + count]
        out[0, :, start : start + width] = (acc / (1.0 + jnp.exp(-acc))).astype(BF16)
        start += width
    if has_step:
        out[0, :, start : start + LANES] = step_ref[...]


def activate(xbc, dt_raw, edge, weight, bias, first, count, with_rest, shards):
    tok = xbc.shape[0]
    inner = HEADS * HEAD_DIM
    per_group = inner // GROUPS

    def group(p):
        return (p % shards) * PAIR + p // shards

    blocks = [(SUB, lambda p, i=i: (0, group(p) * (per_group // SUB) + i)) for i in range(first, first + count)]
    if with_rest:
        blocks.append((STATE, lambda p: (0, inner // STATE + group(p))))
        blocks.append((STATE, lambda p: (0, inner // STATE + GROUPS + group(p))))
    operands, specs, wides = [], [], []
    for width, index in blocks:
        operands += [xbc, edge, weight, bias]
        specs += [pl.BlockSpec((height, width), index) for height in (tok, 3, 4, 1)]
        wides.append(pltpu.VMEM((tok + 8, width), F32))
    total = sum(width for width, _ in blocks)
    if with_rest:
        per_tile = LANES * GROUPS // HEADS
        operands.append(dt_raw)
        specs.append(pl.BlockSpec((tok, LANES), lambda p: (0, group(p) // per_tile)))
        total += LANES
    peers = shards * PAIR
    return pl.pallas_call(
        functools.partial(conv_kernel, len(blocks), with_rest),
        grid=(peers,),
        in_specs=specs,
        out_specs=pl.BlockSpec((1, tok, total), lambda p: (p, 0, 0)),
        out_shape=jax.ShapeDtypeStruct((peers, tok, total), BF16),
        scratch_shapes=wides,
        cost_estimate=pl.CostEstimate(
            flops=peers * tok * total * 12,
            bytes_accessed=peers * tok * total * 4,
            transcendentals=peers * tok * total,
        ),
        name="conv",
    )(*operands)


def prep_kernel(place, b_ref, c_ref, dt_ref, a_ref, bias_ref, skip_ref, cum_ref, row_ref, factor_ref, tail_ref, skip_out, score_ref):
    per_tile = LANES * GROUPS // HEADS
    group = place[0]
    tile = group // per_tile
    shift = (LANES - (group % per_tile) * (HEADS // GROUPS)) % LANES
    rate = -jnp.exp(a_ref[pl.ds(tile, 1), :])
    raw = dt_ref[...].astype(F32) + bias_ref[pl.ds(tile, 1), :]
    step = jnp.maximum(raw, 0.0) + jnp.log1p(jnp.exp(-jnp.abs(raw)))
    step = pltpu.roll(step, shift, 1)
    rate = pltpu.roll(jnp.broadcast_to(rate, (8, LANES)), shift, 1)[0:1]
    skip = pltpu.roll(jnp.broadcast_to(skip_ref[pl.ds(tile, 1), :], (8, LANES)), shift, 1)
    skip_out[...] = jnp.concatenate(halves(jnp.concatenate([skip, skip], 0), 3), 1)
    lower = (
        lax.broadcasted_iota(jnp.int32, (BLOCK, BLOCK), 0)
        >= lax.broadcasted_iota(jnp.int32, (BLOCK, BLOCK), 1)
    ).astype(BF16)
    for block in range(PAIR):
        at = slice(block * BLOCK, (block + 1) * BLOCK)
        here = step[at]
        parts = halves(here * rate, 3)
        cum = dot(lower, parts[0]) + (dot(lower, parts[1]) + dot(lower, parts[2]))
        cum = cum * LOG2E
        cum_ref[at] = cum
        row_ref[:, at] = jnp.transpose(cum - jnp.log2(here))
        factor_ref[at] = jnp.concatenate(halves(jnp.exp2(cum), 2), 1)
        tail = jnp.exp2(cum[BLOCK - 1 :] - cum) * here
        tail_ref[at] = jnp.concatenate(halves(tail, 2), 1)
        score_ref[at] = lax.dot_general(
            c_ref[at], b_ref[at], (((1,), (1,)), ((), ())), preferred_element_type=F32
        )


def state_kernel(first_head, x_ref, b_ref, factor_ref, tail_ref, send_ref, own_ref):
    width = x_ref.shape[1]
    wide = spread(first_head, width, 2)
    both = []
    for block in range(PAIR):
        at = slice(block * BLOCK, (block + 1) * BLOCK)
        loaded = (x_ref[at].astype(F32) * dot(tail_ref[at], wide)).astype(BF16)
        both.append(
            lax.dot_general(b_ref[at], loaded, (((0,), (0,)), ((), ())), preferred_element_type=F32)
        )
    ends = [dot(factor_ref[(i + 1) * BLOCK - 16 : (i + 1) * BLOCK], wide)[15:16] for i in range(PAIR)]
    own_ref[...] = both[0]
    send_ref[0:STATE] = (ends[1] * both[0] + both[1]).astype(BF16)
    row = lax.broadcasted_iota(jnp.int32, (16, width), 0)
    high, middle, low = (part.astype(F32) for part in halves(ends[0] * ends[1], 3))
    packed = jnp.where(row == 0, high, jnp.where(row == 1, middle, jnp.where(row == 2, low, 0.0)))
    send_ref[STATE:] = packed.astype(BF16)


def local_kernel(first_head, x_ref, cum_ref, row_ref, score_ref, skip_ref, out_ref):
    width = x_ref.shape[1]
    half = BLOCK // 2
    wide = spread(first_head, width, 3)
    skip = dot(skip_ref[...], wide)[0:1]
    lower = lax.broadcasted_iota(jnp.int32, (half, half), 0) >= lax.broadcasted_iota(
        jnp.int32, (half, half), 1
    )
    lane = lax.broadcasted_iota(jnp.int32, (BLOCK, LANES), 1)
    for block in range(PAIR):
        base = block * BLOCK
        for tile in range(width // LANES):
            columns = slice(tile * LANES, (tile + 1) * LANES)
            x = x_ref[base : base + BLOCK, columns]
            top = skip[:, columns] * x[:half].astype(F32)
            bottom = skip[:, columns] * x[half:].astype(F32)
            for side in range(LANES // HEAD_DIM):
                head = first_head + tile * (LANES // HEAD_DIM) + side
                own = jnp.where(lane // HEAD_DIM == side, x, jnp.zeros_like(x))
                cum = cum_ref[base : base + BLOCK, head : head + 1]
                row = row_ref[head : head + 1, base : base + BLOCK]
                diag = jnp.where(lower, cum[:half] - row[:, :half], -1e30)
                mixing = jnp.exp2(diag) * score_ref[base : base + half, :half]
                top = top + dot(mixing.astype(BF16), own[:half])
                left = jnp.exp2(cum[half:] - row[:, :half]) * score_ref[base + half : base + BLOCK, :half]
                diag = jnp.where(lower, cum[half:] - row[:, half:], -1e30)
                right = jnp.exp2(diag) * score_ref[base + half : base + BLOCK, half:]
                mixing = jnp.concatenate([left.astype(BF16), right.astype(BF16)], 1)
                bottom = bottom + dot(mixing, own)
            out_ref[base : base + half, columns] = top
            out_ref[base + half : base + BLOCK, columns] = bottom


def final_kernel(first_head, place, all_ref, own_ref, c_ref, factor_ref, partial_ref, keep_ref, send_ref):
    width = own_ref.shape[1]
    pair, core = place[1], place[2]
    wide = spread(first_head, width, 2)
    held = jnp.zeros((STATE, width), F32)
    for k in range(all_ref.shape[0] - 1):
        decay = all_ref[k, STATE : STATE + 16].astype(F32)
        decay = decay[0:1] + (decay[1:2] + decay[2:3])
        held = jnp.where(k < pair, decay * held + all_ref[k, :STATE].astype(F32), held)
    factor = dot(factor_ref[...], wide)
    outs = []
    for block in range(PAIR):
        at = slice(block * BLOCK, (block + 1) * BLOCK)
        carried = dot(c_ref[at], held.astype(BF16))
        outs.append((partial_ref[at] + factor[at] * carried).astype(BF16))
        held = factor[BLOCK - 1 : BLOCK] * held + own_ref[...]

    @pl.when(core == 0)
    def _():
        keep_ref[...] = outs[0]
        send_ref[...] = outs[1]

    @pl.when(core == 1)
    def _():
        keep_ref[...] = outs[1]
        send_ref[...] = outs[0]


def assemble_kernel(count, place, *refs):
    keeps, gots, out = refs[:count], refs[count : 2 * count], refs[2 * count]
    core = place[2]
    half = out.shape[1] // PAIR

    def put(own, other):
        start = 0
        for keep, got in zip(keeps, gots):
            width = keep.shape[1]
            out[:, own + start : own + start + width] = keep[...]
            out[:, other + start : other + start + width] = got[...]
            start += width

    pl.when(core == 0)(lambda: put(0, half))
    pl.when(core == 1)(lambda: put(half, 0))


def local_call(body, outs, operands, specs=None, flops=0, transcendentals=0, name=None):
    shapes = [jax.ShapeDtypeStruct(shape, dtype) for shape, dtype in outs]
    vmem = pl.BlockSpec(memory_space=pltpu.VMEM)
    specs = specs or [vmem] * len(operands)
    moved = sum(o.size * o.dtype.itemsize for o in shapes) * 2
    return pl.pallas_call(
        body,
        out_shape=shapes,
        in_specs=specs,
        out_specs=[vmem] * len(outs),
        compiler_params=pltpu.CompilerParams(vmem_limit_bytes=32 << 20),
        cost_estimate=pl.CostEstimate(flops=flops, bytes_accessed=moved, transcendentals=transcendentals),
        name=name,
    )(*operands)


def paired(xbc, dt_raw, conv_weight, conv_bias, a_log, dt_bias, skip_gain):
    axes = ("ctx", "head")
    shards, length = lax.axis_size("head"), lax.axis_size("ctx")
    devices, peers, pairs = shards * length, shards * PAIR, length // PAIR
    tok = xbc.shape[0]
    slab = tok * peers
    per_group = HEADS // GROUPS
    context, shard = lax.axis_index("ctx"), lax.axis_index("head")
    pair, core = context // PAIR, context % PAIR
    group = shard * PAIR + core
    place = jnp.stack([group, pair, core]).astype(jnp.int32)
    smem, vmem = pl.BlockSpec(memory_space=pltpu.SMEM), pl.BlockSpec(memory_space=pltpu.VMEM)

    edge = lax.ppermute(xbc[tok - 3 :], axes, [(i, i + 1) for i in range(devices - 1)])
    exchange = [[k * peers + i for i in range(peers)] for k in range(pairs)]
    gather = [[k * peers + i for k in range(pairs)] for i in range(peers)]
    swap = [(i * shards + j, (i ^ 1) * shards + j) for i in range(length) for j in range(shards)]

    received = []
    first = 0
    for index, count in enumerate(PIECES):
        sent = activate(
            xbc, dt_raw, edge, conv_weight, conv_bias[None], first, count, index == 0, shards
        )
        got = lax.all_to_all(sent, axes, 0, 0, axis_index_groups=exchange, tiled=True)
        received.append(got.reshape(slab, got.shape[2]))
        first += count

    start = PIECES[0] * SUB
    b = received[0][:, start : start + STATE]
    c = received[0][:, start + STATE : start + 2 * STATE]
    raw = received[0][:, start + 2 * STATE :]
    received[0] = received[0][:, :start]
    tiles = [p.reshape(HEADS // LANES, LANES) for p in (a_log, dt_bias, skip_gain)]
    cum, row, factor, tail, skip, score = local_call(
        prep_kernel,
        [
            ((slab, LANES), F32),
            ((LANES, slab), F32),
            ((slab, 2 * LANES), BF16),
            ((slab, 2 * LANES), BF16),
            ((16, 3 * LANES), BF16),
            ((slab, BLOCK), F32),
        ],
        [place, b, c, raw] + tiles,
        [smem] + [vmem] * 6,
        flops=2 * slab * BLOCK * (STATE + 3 * LANES),
        name="prep",
    )
    heads, gathered, owns, partials = [], [], [], []
    head = 0
    for x in received:
        width = x.shape[1]
        sent, own = local_call(
            functools.partial(state_kernel, head),
            [((STATE + 16, width), BF16), ((STATE, width), F32)],
            [x, b, factor, tail],
            flops=4 * slab * STATE * width,
            name="state",
        )
        gathered.append(lax.all_gather(sent, axes, axis_index_groups=gather))
        (partial,) = local_call(
            functools.partial(local_kernel, head),
            [((slab, width), F32)],
            [x, cum, row, score, skip],
            flops=8 * slab * STATE * width,
            transcendentals=slab * BLOCK * width // HEAD_DIM,
            name="local",
        )
        owns.append(own)
        partials.append(partial)
        heads.append(head)
        head += width // HEAD_DIM
    keeps, gots = [], []
    for head, everything, own, partial in zip(heads, gathered, owns, partials):
        width = own.shape[1]
        keep, send = local_call(
            functools.partial(final_kernel, head),
            [((BLOCK, width), BF16)] * 2,
            [place, everything, own, c, factor, partial],
            [smem] + [vmem] * 5,
            flops=4 * slab * STATE * width,
            name="final",
        )
        keeps.append(keep)
        gots.append(lax.ppermute(send, axes, swap))
    (out,) = local_call(
        functools.partial(assemble_kernel, len(keeps)),
        [((BLOCK, PAIR * per_group * HEAD_DIM), BF16)],
        [place] + keeps + gots,
        [smem] + [vmem] * (2 * len(keeps)),
        name="assemble",
    )
    return out


def solution(mesh):
    in_specs = (P(("ctx", "head"), None), P(("ctx", "head"), None), P(), P(), P(), P(), P())
    out_specs = P("ctx", "head")
    shards, length = mesh.shape["head"], mesh.shape["ctx"]

    def program(xbc, *rest):
        slab = xbc.shape[0] // length
        fits = GROUPS == shards * PAIR and length % PAIR == 0 and slab == BLOCK and slab % (16 * shards) == 0
        return jax.shard_map(
            paired if fits else on_device,
            mesh=mesh,
            in_specs=in_specs,
            out_specs=out_specs,
            check_vma=False,
        )(xbc, *rest)

    return program
```

```python
import functools

import jax
import jax.numpy as jnp
from jax import lax
from jax.experimental import pallas as pl
from jax.experimental.pallas import tpu as pltpu
from jax.sharding import PartitionSpec as P

HEADS = 256
HEAD_DIM = 64
STATE = 256
GROUPS = 8
BLOCK = 256


def from_behind(block, axis, distance):
    devices = range(lax.axis_size(axis))
    route = [(i - distance, i) for i in devices if i - distance in devices]
    return lax.ppermute(block, axis, route)


def carried_in(array, axis, combine, identity):
    length, index = (lax.axis_size(axis), lax.axis_index(axis))
    everything = jax.tree.map(lambda part: lax.all_gather(part, axis), array)
    start = jax.tree.map(
        lambda part, zero: jnp.broadcast_to(jnp.asarray(zero, part.dtype), part.shape),
        array,
        identity,
    )

    def hop(k, before):
        reached = k < index
        new = combine(before, jax.tree.map(lambda part: part[k], everything))
        return jax.tree.map(lambda a, b: jnp.where(reached, a, b), new, before)

    return lax.fori_loop(0, length, hop, start)


def convolve(rows, edge, weight, bias):
    count = rows.shape[0]
    wide = jnp.concatenate([edge, rows], 0).astype(jnp.float32)
    acc = bias[None, :] + weight[0] * wide[0:count]
    acc = acc + weight[1] * wide[1 : count + 1]
    acc = acc + weight[2] * wide[2 : count + 2]
    acc = acc + weight[3] * wide[3 : count + 3]
    return jax.nn.silu(acc).astype(jnp.bfloat16)


def rearrange_heads(rows, shards, per_dev, groups_dev, per_group):
    count = rows.shape[0]
    inner = HEADS * HEAD_DIM
    replicate_groups = max(1, per_group // per_dev)
    heads_part = rows[:, :inner].reshape(count, shards, per_dev * HEAD_DIM)
    b_part = rows[:, inner : inner + GROUPS * STATE].reshape(count, GROUPS, STATE)
    c_part = rows[:, inner + GROUPS * STATE :].reshape(count, GROUPS, STATE)
    b_part = jnp.repeat(b_part, replicate_groups, axis=1).reshape(count, shards, groups_dev * STATE)
    c_part = jnp.repeat(c_part, replicate_groups, axis=1).reshape(count, shards, groups_dev * STATE)
    return jnp.concatenate([heads_part, b_part, c_part], axis=2)


def inner_block(xs, bmat, cmat, steps, cum):
    size = xs.shape[0]
    lower = jnp.arange(size)[:, None] >= jnp.arange(size)[None, :]
    scores = jnp.einsum("qgn,kgn->gqk", cmat, bmat, preferred_element_type=jnp.float32)
    order = jnp.transpose(cum, (1, 2, 0))
    gap = order[..., :, None] - order[..., None, :]
    decay = jnp.exp(jnp.where(lower, gap, -jnp.inf))
    mixing = (scores[:, None] * decay * jnp.transpose(steps, (1, 2, 0))[..., None, :]).astype(
        jnp.bfloat16
    )
    local = jnp.einsum("gjqk,kgjp->qgjp", mixing, xs, preferred_element_type=jnp.float32)
    tail = jnp.exp(cum[size - 1][None] - cum) * steps
    loaded = (bmat[:, :, None, :].astype(jnp.float32) * tail[..., None]).astype(jnp.bfloat16)
    block_state = jnp.einsum("kgjn,kgjp->gjnp", loaded, xs, preferred_element_type=jnp.float32)
    return (local, block_state)


def on_device(xbc, dt_raw, conv_weight, conv_bias, a_log, dt_bias, skip_gain):
    tok = xbc.shape[0]
    shards = lax.axis_size("head")
    per_dev = HEADS // shards
    per_group = HEADS // GROUPS
    groups_dev = max(1, per_dev // per_group)
    heads_per_cluster = per_dev // groups_dev
    sent = rearrange_heads(xbc, shards, per_dev, groups_dev, per_group)
    mine, rates = (
        lax.all_to_all(sent, "head", split_axis=1, concat_axis=0, tiled=True),
        lax.all_to_all(
            dt_raw.reshape(tok, shards, per_dev), "head", split_axis=1, concat_axis=0, tiled=True
        ),
    )
    slab = tok * shards
    mine = mine.reshape(slab, mine.shape[2])
    rates = rates.reshape(slab, per_dev)
    shard = lax.axis_index("head")
    taps = lax.dynamic_index_in_dim(
        rearrange_heads(conv_weight, shards, per_dev, groups_dev, per_group),
        shard,
        1,
        keepdims=False,
    )
    offset = lax.dynamic_index_in_dim(
        rearrange_heads(conv_bias[None, :], shards, per_dev, groups_dev, per_group),
        shard,
        1,
        keepdims=False,
    )
    edge = from_behind(mine[slab - 3 :], "ctx", 1)
    mine = convolve(mine, edge, taps, offset[0])
    nchunk = slab // BLOCK
    width = per_dev * HEAD_DIM
    xs = mine[:, :width].reshape(nchunk, BLOCK, groups_dev, heads_per_cluster, HEAD_DIM)
    bmat = mine[:, width : width + groups_dev * STATE].reshape(nchunk, BLOCK, groups_dev, STATE)
    cmat = mine[:, width + groups_dev * STATE :].reshape(nchunk, BLOCK, groups_dev, STATE)
    first = shard * per_dev
    rate = (-jnp.exp(lax.dynamic_slice_in_dim(a_log, first, per_dev))).reshape(
        groups_dev, heads_per_cluster
    )
    bias_dt = lax.dynamic_slice_in_dim(dt_bias, first, per_dev).reshape(
        groups_dev, heads_per_cluster
    )
    skip = lax.dynamic_slice_in_dim(skip_gain, first, per_dev).reshape(
        groups_dev, heads_per_cluster
    )
    steps = jax.nn.softplus(
        rates.astype(jnp.float32).reshape(nchunk, BLOCK, groups_dev, heads_per_cluster) + bias_dt
    )
    cum = jnp.cumsum(steps * rate, axis=1)

    def block_step(carry, item):
        held, product = carry
        x_part, b_part, c_part, step_part, cum_part = item
        local, block_state = inner_block(x_part, b_part, c_part, step_part, cum_part)
        lifted = c_part.astype(jnp.float32)[:, :, None, :] * jnp.exp(cum_part)[..., None]
        carried = jnp.einsum("qgjn,gjnp->qgjp", lifted, held, precision=lax.Precision.HIGHEST)
        partial_out = local + carried + skip[..., None] * x_part.astype(jnp.float32)
        end = jnp.exp(cum_part[BLOCK - 1])
        return ((end[..., None, None] * held + block_state, product * end), (partial_out, product))

    zero_state = jnp.zeros((groups_dev, heads_per_cluster, STATE, HEAD_DIM), jnp.float32)
    unit = jnp.ones((groups_dev, heads_per_cluster), jnp.float32)
    (slab_state, slab_decay), (partials, product_in) = lax.scan(
        block_step, (zero_state, unit), (xs, bmat, cmat, steps, cum)
    )

    def combine(preceding_state, later):
        return (
            preceding_state[0] * later[0],
            later[0][..., None, None] * preceding_state[1] + later[1],
        )

    _, entering = carried_in((slab_decay, slab_state), "ctx", combine, (unit, zero_state))
    projected = jnp.einsum(
        "cqgn,gjnp->cqgjp", cmat.astype(jnp.float32), entering, precision=lax.Precision.HIGHEST
    )
    factor = jnp.exp(cum) * product_in[:, None]
    total = partials + factor[..., None] * projected
    return total.astype(jnp.bfloat16).reshape(slab, width)


PAIR = 2
LANES = 128
PIECES = (512, 512, 512, 512)
LOG2E = 1.4426950408889634
F32, BF16 = jnp.float32, jnp.bfloat16


def halves(value, count):
    parts = []
    for _ in range(count):
        part = value.astype(BF16)
        parts.append(part)
        value = value - part.astype(F32)
    return parts


def spread(first_head, width, copies):
    lane = lax.broadcasted_iota(jnp.int32, (copies * LANES, width), 0) % LANES
    column = lax.broadcasted_iota(jnp.int32, (copies * LANES, width), 1)
    return (lane == first_head + column // HEAD_DIM).astype(BF16)


def dot(a, b):
    return jnp.dot(a, b, preferred_element_type=F32)


def conv_kernel(parts, shards, with_step, place, xbc, edge, weight, bias, *refs):
    peers = shards * PAIR
    if with_step:
        dt_ref, refs = refs[0], refs[1:]
    outs, wide = refs[:peers], refs[peers]
    count = xbc.shape[0]
    for r in range(peers):
        peer = place[3] ^ r
        group = (peer % shards) * PAIR + peer // shards
        start = 0
        for origin, stride, width in parts:
            at = pl.ds(pl.multiple_of(origin + group * stride, LANES), width)
            wide[5:8, :width] = edge[:, at].astype(F32)
            wide[8:, :width] = xbc[:, at].astype(F32)
            tap = weight[:, at] * 0.5
            acc = bias[:, at] * 0.5 + tap[0:1] * wide[5 : 5 + count, :width]
            acc = acc + tap[1:2] * wide[6 : 6 + count, :width]
            acc = acc + tap[2:3] * wide[7 : 7 + count, :width]
            acc = acc + tap[3:4] * wide[8 : 8 + count, :width]
            outs[r][:, start : start + width] = (acc + acc * jnp.tanh(acc)).astype(BF16)
            start += width
        if with_step:
            tile = group // (LANES * GROUPS // HEADS)
            outs[r][:, start : start + LANES] = dt_ref[:, pl.ds(pl.multiple_of(tile * LANES, LANES), LANES)]


def activate(place, xbc, dt_raw, edge, weight, bias, first, width, with_rest, shards):
    tok = xbc.shape[0]
    inner = HEADS * HEAD_DIM
    parts = [(first, inner // GROUPS, width)]
    operands = [place, xbc, edge, weight, bias]
    total = width
    if with_rest:
        parts += [(inner, STATE, STATE), (inner + GROUPS * STATE, STATE, STATE)]
        operands.append(dt_raw)
        total += 2 * STATE + LANES
    peers = shards * PAIR
    return local_call(
        functools.partial(conv_kernel, parts, shards, with_rest),
        [((tok, total), BF16)] * peers,
        operands,
        scratch=[pltpu.VMEM((tok + 8, max(p[2] for p in parts)), F32)],
        flops=peers * tok * total * 12,
        transcendentals=peers * tok * total,
        name="conv",
    )


def exchange(blocks, axes, pairs):
    peers = len(blocks)
    got = [blocks[0]]
    for r in range(1, peers):
        route = [(k * peers + i, k * peers + (i ^ r)) for k in range(pairs) for i in range(peers)]
        got.append(lax.ppermute(blocks[r], axes, route))
    return got


def in_order(place, blocks, columns, out):
    count = blocks[0].shape[0]
    for r, block in enumerate(blocks):
        at = pl.multiple_of((place[3] ^ r) * count, count)
        out[pl.ds(at, count), :] = block[:, columns]


def prep_kernel(peers, place, *refs):
    blocks, (a_ref, bias_ref, skip_ref) = refs[:peers], refs[peers : peers + 3]
    b_ref, c_ref, cum_ref, row_ref, factor_ref, tail_ref, skip_out, score_ref, dt_ref = refs[peers + 3 :]
    start = blocks[0].shape[1] - 2 * STATE - LANES
    in_order(place, blocks, slice(start, start + STATE), b_ref)
    in_order(place, blocks, slice(start + STATE, start + 2 * STATE), c_ref)
    in_order(place, blocks, slice(start + 2 * STATE, start + 2 * STATE + LANES), dt_ref)
    per_tile = LANES * GROUPS // HEADS
    group = place[0]
    tile = group // per_tile
    shift = (LANES - (group % per_tile) * (HEADS // GROUPS)) % LANES
    rate = -jnp.exp(a_ref[pl.ds(tile, 1), :])
    raw = dt_ref[...].astype(F32) + bias_ref[pl.ds(tile, 1), :]
    step = jnp.maximum(raw, 0.0) + jnp.log1p(jnp.exp(-jnp.abs(raw)))
    step = pltpu.roll(step, shift, 1)
    rate = pltpu.roll(jnp.broadcast_to(rate, (8, LANES)), shift, 1)[0:1]
    skip = pltpu.roll(jnp.broadcast_to(skip_ref[pl.ds(tile, 1), :], (8, LANES)), shift, 1)
    skip_out[...] = jnp.concatenate(halves(jnp.concatenate([skip, skip], 0), 3), 1)
    lower = (
        lax.broadcasted_iota(jnp.int32, (BLOCK, BLOCK), 0)
        >= lax.broadcasted_iota(jnp.int32, (BLOCK, BLOCK), 1)
    ).astype(BF16)
    for block in range(PAIR):
        at = slice(block * BLOCK, (block + 1) * BLOCK)
        here = step[at]
        parts = halves(here * rate, 3)
        cum = dot(lower, parts[0]) + (dot(lower, parts[1]) + dot(lower, parts[2]))
        cum = cum * LOG2E
        cum_ref[at] = cum
        row_ref[:, at] = jnp.transpose(cum - jnp.log2(here))
        factor_ref[at] = jnp.concatenate(halves(jnp.exp2(cum), 2), 1)
        tail = jnp.exp2(cum[BLOCK - 1 :] - cum) * here
        tail_ref[at] = jnp.concatenate(halves(tail, 2), 1)
        score_ref[at] = lax.dot_general(
            c_ref[at], b_ref[at], (((1,), (1,)), ((), ())), preferred_element_type=F32
        )


def state_kernel(first_head, peers, place, *refs):
    blocks, (b_ref, factor_ref, tail_ref, x_ref, send_ref, own_ref) = refs[:peers], refs[peers:]
    width = x_ref.shape[1]
    in_order(place, blocks, slice(0, width), x_ref)
    wide = spread(first_head, width, 2)
    both = []
    for block in range(PAIR):
        at = slice(block * BLOCK, (block + 1) * BLOCK)
        loaded = (x_ref[at].astype(F32) * dot(tail_ref[at], wide)).astype(BF16)
        both.append(
            lax.dot_general(b_ref[at], loaded, (((0,), (0,)), ((), ())), preferred_element_type=F32)
        )
    ends = [dot(factor_ref[(i + 1) * BLOCK - 16 : (i + 1) * BLOCK], wide)[15:16] for i in range(PAIR)]
    own_ref[...] = both[0]
    send_ref[0:STATE] = (ends[1] * both[0] + both[1]).astype(BF16)
    row = lax.broadcasted_iota(jnp.int32, (16, width), 0)
    high, middle, low = (part.astype(F32) for part in halves(ends[0] * ends[1], 3))
    packed = jnp.where(row == 0, high, jnp.where(row == 1, middle, jnp.where(row == 2, low, 0.0)))
    send_ref[STATE:] = packed.astype(BF16)


def local_kernel(first_head, x_ref, cum_ref, row_ref, score_ref, skip_ref, out_ref):
    width = x_ref.shape[1]
    half = BLOCK // 2
    wide = spread(first_head, width, 3)
    skip = dot(skip_ref[...], wide)[0:1]
    lower = lax.broadcasted_iota(jnp.int32, (half, half), 0) >= lax.broadcasted_iota(
        jnp.int32, (half, half), 1
    )
    lane = lax.broadcasted_iota(jnp.int32, (BLOCK, LANES), 1)
    for block in range(PAIR):
        base = block * BLOCK
        for tile in range(width // LANES):
            columns = slice(tile * LANES, (tile + 1) * LANES)
            x = x_ref[base : base + BLOCK, columns]
            top = skip[:, columns] * x[:half].astype(F32)
            bottom = skip[:, columns] * x[half:].astype(F32)
            for side in range(LANES // HEAD_DIM):
                head = first_head + tile * (LANES // HEAD_DIM) + side
                own = jnp.where(lane // HEAD_DIM == side, x, jnp.zeros_like(x))
                cum = cum_ref[base : base + BLOCK, head : head + 1]
                row = row_ref[head : head + 1, base : base + BLOCK]
                diag = jnp.where(lower, cum[:half] - row[:, :half], -1e30)
                mixing = jnp.exp2(diag) * score_ref[base : base + half, :half]
                top = top + dot(mixing.astype(BF16), own[:half])
                left = jnp.exp2(cum[half:] - row[:, :half]) * score_ref[base + half : base + BLOCK, :half]
                diag = jnp.where(lower, cum[half:] - row[:, half:], -1e30)
                right = jnp.exp2(diag) * score_ref[base + half : base + BLOCK, half:]
                mixing = jnp.concatenate([left.astype(BF16), right.astype(BF16)], 1)
                bottom = bottom + dot(mixing, own)
            out_ref[base : base + half, columns] = top
            out_ref[base + half : base + BLOCK, columns] = bottom


def final_kernel(first_head, place, *refs):
    earlier, (own_ref, c_ref, factor_ref, partial_ref, keep_ref, send_ref) = refs[:-6], refs[-6:]
    width = own_ref.shape[1]
    core = place[2]
    wide = spread(first_head, width, 2)
    held = jnp.zeros((STATE, width), F32)
    for got in reversed(earlier):
        decay = got[STATE : STATE + 16].astype(F32)
        decay = decay[0:1] + (decay[1:2] + decay[2:3])
        held = decay * held + got[:STATE].astype(F32)
    factor = dot(factor_ref[...], wide)
    outs = []
    for block in range(PAIR):
        at = slice(block * BLOCK, (block + 1) * BLOCK)
        carried = dot(c_ref[at], held.astype(BF16))
        outs.append((partial_ref[at] + factor[at] * carried).astype(BF16))
        held = factor[BLOCK - 1 : BLOCK] * held + own_ref[...]

    @pl.when(core == 0)
    def _():
        keep_ref[...] = outs[0]
        send_ref[...] = outs[1]

    @pl.when(core == 1)
    def _():
        keep_ref[...] = outs[1]
        send_ref[...] = outs[0]


def assemble_kernel(count, place, *refs):
    keeps, gots, out = refs[:count], refs[count : 2 * count], refs[2 * count]
    core = place[2]
    half = out.shape[1] // PAIR

    def put(own, other):
        start = 0
        for keep, got in zip(keeps, gots):
            width = keep.shape[1]
            out[:, own + start : own + start + width] = keep[...]
            out[:, other + start : other + start + width] = got[...]
            start += width

    pl.when(core == 0)(lambda: put(0, half))
    pl.when(core == 1)(lambda: put(half, 0))


def local_call(body, outs, operands, scratch=(), flops=0, transcendentals=0, name=None):
    shapes = [jax.ShapeDtypeStruct(shape, dtype) for shape, dtype in outs]
    smem, vmem = pl.BlockSpec(memory_space=pltpu.SMEM), pl.BlockSpec(memory_space=pltpu.VMEM)
    specs = [smem if o.dtype == jnp.int32 else vmem for o in operands]
    moved = sum(o.size * o.dtype.itemsize for o in shapes) * 2
    return pl.pallas_call(
        body,
        out_shape=shapes,
        in_specs=specs,
        out_specs=[vmem] * len(outs),
        scratch_shapes=scratch,
        compiler_params=pltpu.CompilerParams(vmem_limit_bytes=16 << 20),
        cost_estimate=pl.CostEstimate(flops=flops, bytes_accessed=moved, transcendentals=transcendentals),
        name=name,
    )(*operands)


def paired(xbc, dt_raw, conv_weight, conv_bias, a_log, dt_bias, skip_gain):
    axes = ("ctx", "head")
    shards, length = lax.axis_size("head"), lax.axis_size("ctx")
    devices, peers, pairs = shards * length, shards * PAIR, length // PAIR
    tok = xbc.shape[0]
    slab = tok * peers
    per_group = HEADS // GROUPS
    context, shard = lax.axis_index("ctx"), lax.axis_index("head")
    pair, core = context // PAIR, context % PAIR
    group = shard * PAIR + core
    place = jnp.stack([group, pair, core, core * shards + shard]).astype(jnp.int32)

    edge = lax.ppermute(xbc[tok - 3 :], axes, [(i, i + 1) for i in range(devices - 1)])
    swap = [(i * shards + j, (i ^ 1) * shards + j) for i in range(length) for j in range(shards)]

    received, starts = [], []
    first = 0
    for index, width in enumerate(PIECES):
        sent = activate(
            place, xbc, dt_raw, edge, conv_weight, conv_bias[None], first, width, index == 0, shards
        )
        received.append(exchange(sent, axes, pairs))
        starts.append(first // HEAD_DIM)
        first += width

    tiles = [p.reshape(HEADS // LANES, LANES) for p in (a_log, dt_bias, skip_gain)]
    b, c, cum, row, factor, tail, skip, score = local_call(
        functools.partial(prep_kernel, peers),
        [
            ((slab, STATE), BF16),
            ((slab, STATE), BF16),
            ((slab, LANES), F32),
            ((LANES, slab), F32),
            ((slab, 2 * LANES), BF16),
            ((slab, 2 * LANES), BF16),
            ((16, 3 * LANES), BF16),
            ((slab, BLOCK), F32),
        ],
        [place] + received[0] + tiles,
        scratch=[pltpu.VMEM((slab, LANES), BF16)],
        flops=2 * slab * BLOCK * (STATE + 3 * LANES),
        name="prep",
    )
    pieces = []
    for head, width, blocks in zip(starts, PIECES, received):
        x, sent, own = local_call(
            functools.partial(state_kernel, head, peers),
            [((slab, width), BF16), ((STATE + 16, width), BF16), ((STATE, width), F32)],
            [place] + blocks + [b, factor, tail],
            flops=4 * slab * STATE * width,
            name="state",
        )
        earlier = [
            lax.ppermute(sent, axes, [(i, i + d * peers) for i in range(devices - d * peers)])
            for d in range(1, pairs)
        ]
        (partial,) = local_call(
            functools.partial(local_kernel, head),
            [((slab, width), F32)],
            [x, cum, row, score, skip],
            flops=8 * slab * STATE * width,
            transcendentals=slab * BLOCK * width // HEAD_DIM,
            name="local",
        )
        pieces.append((head, width, earlier, own, partial))
    keeps, gots = [], []
    for head, width, earlier, own, partial in pieces:
        keep, send = local_call(
            functools.partial(final_kernel, head),
            [((BLOCK, width), BF16)] * 2,
            [place] + earlier + [own, c, factor, partial],
            flops=4 * slab * STATE * width,
            name="final",
        )
        keeps.append(keep)
        gots.append(lax.ppermute(send, axes, swap))
    (out,) = local_call(
        functools.partial(assemble_kernel, len(keeps)),
        [((BLOCK, PAIR * per_group * HEAD_DIM), BF16)],
        [place] + keeps + gots,
        name="assemble",
    )
    return out


def solution(mesh):
    in_specs = (P(("ctx", "head"), None), P(("ctx", "head"), None), P(), P(), P(), P(), P())
    out_specs = P("ctx", "head")
    shards, length = mesh.shape["head"], mesh.shape["ctx"]

    def program(xbc, *rest):
        slab = xbc.shape[0] // length
        fits = GROUPS == shards * PAIR and length % PAIR == 0 and slab == BLOCK and slab % (16 * shards) == 0
        return jax.shard_map(
            paired if fits else on_device,
            mesh=mesh,
            in_specs=in_specs,
            out_specs=out_specs,
            check_vma=False,
        )(xbc, *rest)

    return program
```

```python
import functools

import jax
import jax.numpy as jnp
from jax import lax
from jax.experimental import pallas as pl
from jax.experimental.pallas import tpu as pltpu
from jax.sharding import PartitionSpec as P

HEADS = 256
HEAD_DIM = 64
STATE = 256
GROUPS = 8
BLOCK = 256


def from_behind(block, axis, distance):
    devices = range(lax.axis_size(axis))
    route = [(i - distance, i) for i in devices if i - distance in devices]
    return lax.ppermute(block, axis, route)


def carried_in(array, axis, combine, identity):
    length, index = (lax.axis_size(axis), lax.axis_index(axis))
    everything = jax.tree.map(lambda part: lax.all_gather(part, axis), array)
    start = jax.tree.map(
        lambda part, zero: jnp.broadcast_to(jnp.asarray(zero, part.dtype), part.shape),
        array,
        identity,
    )

    def hop(k, before):
        reached = k < index
        new = combine(before, jax.tree.map(lambda part: part[k], everything))
        return jax.tree.map(lambda a, b: jnp.where(reached, a, b), new, before)

    return lax.fori_loop(0, length, hop, start)


def convolve(rows, edge, weight, bias):
    count = rows.shape[0]
    wide = jnp.concatenate([edge, rows], 0).astype(jnp.float32)
    acc = bias[None, :] + weight[0] * wide[0:count]
    acc = acc + weight[1] * wide[1 : count + 1]
    acc = acc + weight[2] * wide[2 : count + 2]
    acc = acc + weight[3] * wide[3 : count + 3]
    return jax.nn.silu(acc).astype(jnp.bfloat16)


def rearrange_heads(rows, shards, per_dev, groups_dev, per_group):
    count = rows.shape[0]
    inner = HEADS * HEAD_DIM
    replicate_groups = max(1, per_group // per_dev)
    heads_part = rows[:, :inner].reshape(count, shards, per_dev * HEAD_DIM)
    b_part = rows[:, inner : inner + GROUPS * STATE].reshape(count, GROUPS, STATE)
    c_part = rows[:, inner + GROUPS * STATE :].reshape(count, GROUPS, STATE)
    b_part = jnp.repeat(b_part, replicate_groups, axis=1).reshape(count, shards, groups_dev * STATE)
    c_part = jnp.repeat(c_part, replicate_groups, axis=1).reshape(count, shards, groups_dev * STATE)
    return jnp.concatenate([heads_part, b_part, c_part], axis=2)


def inner_block(xs, bmat, cmat, steps, cum):
    size = xs.shape[0]
    lower = jnp.arange(size)[:, None] >= jnp.arange(size)[None, :]
    scores = jnp.einsum("qgn,kgn->gqk", cmat, bmat, preferred_element_type=jnp.float32)
    order = jnp.transpose(cum, (1, 2, 0))
    gap = order[..., :, None] - order[..., None, :]
    decay = jnp.exp(jnp.where(lower, gap, -jnp.inf))
    mixing = (scores[:, None] * decay * jnp.transpose(steps, (1, 2, 0))[..., None, :]).astype(
        jnp.bfloat16
    )
    local = jnp.einsum("gjqk,kgjp->qgjp", mixing, xs, preferred_element_type=jnp.float32)
    tail = jnp.exp(cum[size - 1][None] - cum) * steps
    loaded = (bmat[:, :, None, :].astype(jnp.float32) * tail[..., None]).astype(jnp.bfloat16)
    block_state = jnp.einsum("kgjn,kgjp->gjnp", loaded, xs, preferred_element_type=jnp.float32)
    return (local, block_state)


def on_device(xbc, dt_raw, conv_weight, conv_bias, a_log, dt_bias, skip_gain):
    tok = xbc.shape[0]
    shards = lax.axis_size("head")
    per_dev = HEADS // shards
    per_group = HEADS // GROUPS
    groups_dev = max(1, per_dev // per_group)
    heads_per_cluster = per_dev // groups_dev
    sent = rearrange_heads(xbc, shards, per_dev, groups_dev, per_group)
    mine, rates = (
        lax.all_to_all(sent, "head", split_axis=1, concat_axis=0, tiled=True),
        lax.all_to_all(
            dt_raw.reshape(tok, shards, per_dev), "head", split_axis=1, concat_axis=0, tiled=True
        ),
    )
    slab = tok * shards
    mine = mine.reshape(slab, mine.shape[2])
    rates = rates.reshape(slab, per_dev)
    shard = lax.axis_index("head")
    taps = lax.dynamic_index_in_dim(
        rearrange_heads(conv_weight, shards, per_dev, groups_dev, per_group),
        shard,
        1,
        keepdims=False,
    )
    offset = lax.dynamic_index_in_dim(
        rearrange_heads(conv_bias[None, :], shards, per_dev, groups_dev, per_group),
        shard,
        1,
        keepdims=False,
    )
    edge = from_behind(mine[slab - 3 :], "ctx", 1)
    mine = convolve(mine, edge, taps, offset[0])
    nchunk = slab // BLOCK
    width = per_dev * HEAD_DIM
    xs = mine[:, :width].reshape(nchunk, BLOCK, groups_dev, heads_per_cluster, HEAD_DIM)
    bmat = mine[:, width : width + groups_dev * STATE].reshape(nchunk, BLOCK, groups_dev, STATE)
    cmat = mine[:, width + groups_dev * STATE :].reshape(nchunk, BLOCK, groups_dev, STATE)
    first = shard * per_dev
    rate = (-jnp.exp(lax.dynamic_slice_in_dim(a_log, first, per_dev))).reshape(
        groups_dev, heads_per_cluster
    )
    bias_dt = lax.dynamic_slice_in_dim(dt_bias, first, per_dev).reshape(
        groups_dev, heads_per_cluster
    )
    skip = lax.dynamic_slice_in_dim(skip_gain, first, per_dev).reshape(
        groups_dev, heads_per_cluster
    )
    steps = jax.nn.softplus(
        rates.astype(jnp.float32).reshape(nchunk, BLOCK, groups_dev, heads_per_cluster) + bias_dt
    )
    cum = jnp.cumsum(steps * rate, axis=1)

    def block_step(carry, item):
        held, product = carry
        x_part, b_part, c_part, step_part, cum_part = item
        local, block_state = inner_block(x_part, b_part, c_part, step_part, cum_part)
        lifted = c_part.astype(jnp.float32)[:, :, None, :] * jnp.exp(cum_part)[..., None]
        carried = jnp.einsum("qgjn,gjnp->qgjp", lifted, held, precision=lax.Precision.HIGHEST)
        partial_out = local + carried + skip[..., None] * x_part.astype(jnp.float32)
        end = jnp.exp(cum_part[BLOCK - 1])
        return ((end[..., None, None] * held + block_state, product * end), (partial_out, product))

    zero_state = jnp.zeros((groups_dev, heads_per_cluster, STATE, HEAD_DIM), jnp.float32)
    unit = jnp.ones((groups_dev, heads_per_cluster), jnp.float32)
    (slab_state, slab_decay), (partials, product_in) = lax.scan(
        block_step, (zero_state, unit), (xs, bmat, cmat, steps, cum)
    )

    def combine(preceding_state, later):
        return (
            preceding_state[0] * later[0],
            later[0][..., None, None] * preceding_state[1] + later[1],
        )

    _, entering = carried_in((slab_decay, slab_state), "ctx", combine, (unit, zero_state))
    projected = jnp.einsum(
        "cqgn,gjnp->cqgjp", cmat.astype(jnp.float32), entering, precision=lax.Precision.HIGHEST
    )
    factor = jnp.exp(cum) * product_in[:, None]
    total = partials + factor[..., None] * projected
    return total.astype(jnp.bfloat16).reshape(slab, width)


PAIR = 2
LANES = 128
PIECES = ((384, "BD"), (640, "C"), (640, ""), (384, ""))
LOG2E = 1.4426950408889634
F32, BF16 = jnp.float32, jnp.bfloat16


def halves(value, count):
    parts = []
    for _ in range(count):
        part = value.astype(BF16)
        parts.append(part)
        value = value - part.astype(F32)
    return parts


def spread(first_head, width, copies):
    lane = lax.broadcasted_iota(jnp.int32, (copies * LANES, width), 0) % LANES
    column = lax.broadcasted_iota(jnp.int32, (copies * LANES, width), 1)
    return (lane == first_head + column // HEAD_DIM).astype(BF16)


def dot(a, b):
    return jnp.dot(a, b, preferred_element_type=F32)


def pack_kernel(shards, place, xbc, dt_raw, weight, bias, own, send, taps, offset, near, far, tail, sems):
    core, shard = place[2], place[4]
    inner = HEADS * HEAD_DIM
    count = xbc.shape[0]
    per_group = inner // GROUPS
    rest = per_group * shards

    def columns(z, side):
        for r in range(shards):
            group = (z ^ r) * PAIR + side
            yield r * per_group, group * per_group, per_group
            yield rest + r * STATE, inner + group * STATE, STATE
            yield rest + (shards + r) * STATE, inner + (GROUPS + group) * STATE, STATE

    def ds(start, width):
        return pl.ds(pl.multiple_of(start, LANES), width)

    copies = [(xbc.at[count - 16 :], tail)]
    for side, out in ((1 - core, send), (core, own)):
        for to, start, width in columns(shard, side):
            copies.append((xbc.at[:, ds(start, width)], out.at[:, to : to + width]))
        copies.append((dt_raw, out.at[:, out.shape[1] - HEADS :]))
    for to, start, width in columns(shard, core):
        copies.append((weight.at[:, ds(start, width)], taps.at[:, to : to + width]))
        copies.append((bias.at[:, ds(start, width)], offset.at[:, to : to + width]))
    started = []
    for i, (source, target) in enumerate(copies):
        copy = pltpu.make_async_copy(source, target, sems.at[i])
        copy.start()
        started.append(copy)
    started[0].wait()
    next_shard = jnp.where(shard == shards - 1, 0, shard + 1)
    side = jnp.where(shard == shards - 1, 1 - core, core)
    for edge, towards in ((near, side), (far, 1 - side)):
        for to, start, width in columns(next_shard, towards):
            rows = tail[:, ds(start, width)].astype(F32)
            edge[:, to : to + width] = rows[13:16].astype(BF16)
    for copy in started[1:]:
        copy.wait()


def pack(place, xbc, dt_raw, weight, bias, shards):
    tok, channels = xbc.shape
    half = channels // PAIR
    smem, vmem, anywhere = (pl.BlockSpec(memory_space=m) for m in (pltpu.SMEM, pltpu.VMEM, pl.ANY))
    outs = [((tok, half + HEADS), BF16)] * 2 + [((4, half), F32), ((1, half), F32)] + [((3, half), BF16)] * 2
    return pl.pallas_call(
        functools.partial(pack_kernel, shards),
        out_shape=[jax.ShapeDtypeStruct(shape, dtype) for shape, dtype in outs],
        in_specs=[smem] + [anywhere] * 4,
        out_specs=[vmem] * len(outs),
        scratch_shapes=[pltpu.VMEM((16, channels), BF16), pltpu.SemaphoreType.DMA((3 + 12 * shards,))],
        compiler_params=pltpu.CompilerParams(vmem_limit_bytes=16 << 20),
        name="pack",
    )(place, xbc, dt_raw, weight, bias)


def conv_kernel(parts, shards, place, *refs):
    rows, edges, (weight, bias), outs, wide = refs[0:2], refs[2:4], refs[4:6], refs[6:-1], refs[-1]
    count, total = rows[0].shape
    core, shard = place[2], place[4]
    for side in range(PAIR):
        here = pl.ds(pl.multiple_of(jnp.where(core == 0, side, 1 - side) * count, count), count)
        for r in range(shards):
            start = 0
            for origin, stride, width in parts:
                to = slice(start, start + width)
                start += width
                if stride == 0:
                    tile = ((shard ^ r) * PAIR + core) // (LANES * GROUPS // HEADS)
                    at = pl.ds(pl.multiple_of(total - HEADS + tile * LANES, LANES), LANES)
                    outs[r][here, to] = rows[side][:, at]
                    continue
                at = slice(origin + r * stride, origin + r * stride + width)
                wide[5:8, :width] = edges[side][:, at].astype(F32)
                wide[8:, :width] = rows[side][:, at].astype(F32)
                tap = weight[:, at] * 0.5
                acc = bias[:, at] * 0.5 + tap[0:1] * wide[5 : 5 + count, :width]
                acc = acc + tap[1:2] * wide[6 : 6 + count, :width]
                acc = acc + tap[2:3] * wide[7 : 7 + count, :width]
                acc = acc + tap[3:4] * wide[8 : 8 + count, :width]
                outs[r][here, to] = (acc + acc * jnp.tanh(acc)).astype(BF16)


def activate(place, rows, edges, taps, bias, first, width, rest, shards):
    tok = rows[0].shape[0]
    per_group = HEADS * HEAD_DIM // GROUPS
    inner = per_group * shards
    parts = [(first, per_group, width)]
    for kind in rest:
        parts.append({"B": (inner, STATE, STATE), "C": (inner + shards * STATE, STATE, STATE), "D": (0, 0, LANES)}[kind])
    total = sum(part[2] for part in parts)
    return local_call(
        functools.partial(conv_kernel, parts, shards),
        [((PAIR * tok, total), BF16)] * shards,
        [place, *rows, *edges, taps, bias],
        scratch=[pltpu.VMEM((tok + 8, max(p[2] for p in parts)), F32)],
        flops=shards * PAIR * tok * total * 12,
        transcendentals=shards * PAIR * tok * total,
        name="conv",
    )


def exchange(blocks, axes, length):
    shards = len(blocks)
    got = {0: blocks[0]}
    for r in [*range(2, shards), 1]:
        route = [(k * shards + i, k * shards + (i ^ r)) for k in range(length) for i in range(shards)]
        got[r] = lax.ppermute(blocks[r], axes, route)
    return [got[r] for r in range(shards)]


def in_order(place, blocks, columns, out):
    count = blocks[0].shape[0] // PAIR
    for r, block in enumerate(blocks):
        for core in range(PAIR):
            at = pl.multiple_of((core * len(blocks) + (place[4] ^ r)) * count, count)
            out[pl.ds(at, count), :] = block[core * count : (core + 1) * count, columns]


def prep_kernel(peers, place, *refs):
    blocks, (a_ref, bias_ref, skip_ref) = refs[:peers], refs[peers : peers + 3]
    b_ref, cum_ref, row_ref, factor_ref, tail_ref, skip_out, dt_ref = refs[peers + 3 :]
    start = blocks[0].shape[1] - STATE - LANES
    in_order(place, blocks, slice(start, start + STATE), b_ref)
    in_order(place, blocks, slice(start + STATE, start + STATE + LANES), dt_ref)
    per_tile = LANES * GROUPS // HEADS
    group = place[0]
    tile = group // per_tile
    shift = (LANES - (group % per_tile) * (HEADS // GROUPS)) % LANES
    rate = -jnp.exp(a_ref[pl.ds(tile, 1), :])
    raw = dt_ref[...].astype(F32) + bias_ref[pl.ds(tile, 1), :]
    step = jnp.maximum(raw, 0.0) + jnp.log1p(jnp.exp(-jnp.abs(raw)))
    step = pltpu.roll(step, shift, 1)
    rate = pltpu.roll(jnp.broadcast_to(rate, (8, LANES)), shift, 1)[0:1]
    skip = pltpu.roll(jnp.broadcast_to(skip_ref[pl.ds(tile, 1), :], (8, LANES)), shift, 1)
    skip_out[...] = jnp.concatenate(halves(jnp.concatenate([skip, skip], 0), 3), 1)
    lower = (
        lax.broadcasted_iota(jnp.int32, (BLOCK, BLOCK), 0)
        >= lax.broadcasted_iota(jnp.int32, (BLOCK, BLOCK), 1)
    ).astype(BF16)
    for block in range(PAIR):
        at = slice(block * BLOCK, (block + 1) * BLOCK)
        here = step[at]
        parts = halves(here * rate, 3)
        cum = dot(lower, parts[0]) + (dot(lower, parts[1]) + dot(lower, parts[2]))
        cum = cum * LOG2E
        cum_ref[at] = cum
        row_ref[:, at] = jnp.transpose(cum - jnp.log2(here))
        factor_ref[at] = jnp.concatenate(halves(jnp.exp2(cum), 2), 1)
        tail = jnp.exp2(cum[BLOCK - 1 :] - cum) * here
        tail_ref[at] = jnp.concatenate(halves(tail, 2), 1)


def score_kernel(peers, place, *refs):
    blocks, (b_ref, c_ref, score_ref) = refs[:peers], refs[peers:]
    start = blocks[0].shape[1] - STATE
    in_order(place, blocks, slice(start, start + STATE), c_ref)
    for block in range(PAIR):
        at = slice(block * BLOCK, (block + 1) * BLOCK)
        score_ref[at] = lax.dot_general(
            c_ref[at], b_ref[at], (((1,), (1,)), ((), ())), preferred_element_type=F32
        )


def state_kernel(first_head, peers, place, *refs):
    blocks, (b_ref, factor_ref, tail_ref, x_ref, send_ref, own_ref) = refs[:peers], refs[peers:]
    width = x_ref.shape[1]
    in_order(place, blocks, slice(0, width), x_ref)
    wide = spread(first_head, width, 2)
    both = []
    for block in range(PAIR):
        at = slice(block * BLOCK, (block + 1) * BLOCK)
        loaded = (x_ref[at].astype(F32) * dot(tail_ref[at], wide)).astype(BF16)
        both.append(
            lax.dot_general(b_ref[at], loaded, (((0,), (0,)), ((), ())), preferred_element_type=F32)
        )
    ends = [dot(factor_ref[(i + 1) * BLOCK - 16 : (i + 1) * BLOCK], wide)[15:16] for i in range(PAIR)]
    own_ref[...] = both[0]
    send_ref[0:STATE] = (ends[1] * both[0] + both[1]).astype(BF16)
    put_decay(send_ref, ends[0] * ends[1])


def local_kernel(first_head, x_ref, cum_ref, row_ref, score_ref, skip_ref, out_ref):
    width = x_ref.shape[1]
    half = BLOCK // 2
    wide = spread(first_head, width, 3)
    skip = dot(skip_ref[...], wide)[0:1]
    lower = lax.broadcasted_iota(jnp.int32, (half, half), 0) >= lax.broadcasted_iota(
        jnp.int32, (half, half), 1
    )
    lane = lax.broadcasted_iota(jnp.int32, (BLOCK, LANES), 1)
    for block in range(PAIR):
        base = block * BLOCK
        for tile in range(width // LANES):
            columns = slice(tile * LANES, (tile + 1) * LANES)
            x = x_ref[base : base + BLOCK, columns]
            top = skip[:, columns] * x[:half].astype(F32)
            bottom = skip[:, columns] * x[half:].astype(F32)
            for side in range(LANES // HEAD_DIM):
                head = first_head + tile * (LANES // HEAD_DIM) + side
                own = jnp.where(lane // HEAD_DIM == side, x, jnp.zeros_like(x))
                cum = cum_ref[base : base + BLOCK, head : head + 1]
                row = row_ref[head : head + 1, base : base + BLOCK]
                diag = jnp.where(lower, cum[:half] - row[:, :half], -1e30)
                mixing = jnp.exp2(diag) * score_ref[base : base + half, :half]
                top = top + dot(mixing.astype(BF16), own[:half])
                left = jnp.exp2(cum[half:] - row[:, :half]) * score_ref[base + half : base + BLOCK, :half]
                diag = jnp.where(lower, cum[half:] - row[:, half:], -1e30)
                right = jnp.exp2(diag) * score_ref[base + half : base + BLOCK, half:]
                mixing = jnp.concatenate([left.astype(BF16), right.astype(BF16)], 1)
                bottom = bottom + dot(mixing, own)
            out_ref[base : base + half, columns] = top
            out_ref[base + half : base + BLOCK, columns] = bottom


def decay_of(ref):
    decay = ref[STATE : STATE + 16].astype(F32)
    return decay[0:1] + (decay[1:2] + decay[2:3])


def put_decay(ref, decay):
    row = lax.broadcasted_iota(jnp.int32, (16, ref.shape[1]), 0)
    high, middle, low = (part.astype(F32) for part in halves(decay, 3))
    packed = jnp.where(row == 0, high, jnp.where(row == 1, middle, jnp.where(row == 2, low, 0.0)))
    ref[STATE:] = packed.astype(BF16)


def combine_kernel(early_ref, late_ref, out_ref):
    decay = decay_of(late_ref)
    out_ref[:STATE] = (decay * early_ref[:STATE].astype(F32) + late_ref[:STATE].astype(F32)).astype(BF16)
    put_decay(out_ref, decay * decay_of(early_ref))


def final_kernel(first_head, place, *refs):
    last, before, alone, own_ref, c_ref, factor_ref, partial_ref, keep_ref, send_ref = refs
    width = own_ref.shape[1]
    core = place[2]
    wide = spread(first_head, width, 2)
    held = last[:STATE].astype(F32) + decay_of(last) * before[:STATE].astype(F32)
    held = held + alone[:STATE].astype(F32)
    factor = dot(factor_ref[...], wide)
    outs = []
    for block in range(PAIR):
        at = slice(block * BLOCK, (block + 1) * BLOCK)
        carried = dot(c_ref[at], held.astype(BF16))
        outs.append((partial_ref[at] + factor[at] * carried).astype(BF16))
        held = factor[BLOCK - 1 : BLOCK] * held + own_ref[...]

    @pl.when(core == 0)
    def _():
        keep_ref[...] = outs[0]
        send_ref[...] = outs[1]

    @pl.when(core == 1)
    def _():
        keep_ref[...] = outs[1]
        send_ref[...] = outs[0]


def assemble_kernel(count, place, *refs):
    keeps, gots, out = refs[:count], refs[count : 2 * count], refs[2 * count]
    core = place[2]
    half = out.shape[1] // PAIR

    def put(own, other):
        start = 0
        for keep, got in zip(keeps, gots):
            width = keep.shape[1]
            out[:, own + start : own + start + width] = keep[...]
            out[:, other + start : other + start + width] = got[...]
            start += width

    pl.when(core == 0)(lambda: put(0, half))
    pl.when(core == 1)(lambda: put(half, 0))


def local_call(body, outs, operands, scratch=(), flops=0, transcendentals=0, name=None):
    shapes = [jax.ShapeDtypeStruct(shape, dtype) for shape, dtype in outs]
    smem, vmem = pl.BlockSpec(memory_space=pltpu.SMEM), pl.BlockSpec(memory_space=pltpu.VMEM)
    specs = [smem if o.dtype == jnp.int32 else vmem for o in operands]
    moved = sum(o.size * o.dtype.itemsize for o in shapes) * 2
    return pl.pallas_call(
        body,
        out_shape=shapes,
        in_specs=specs,
        out_specs=[vmem] * len(outs),
        scratch_shapes=scratch,
        compiler_params=pltpu.CompilerParams(vmem_limit_bytes=16 << 20),
        cost_estimate=pl.CostEstimate(flops=flops, bytes_accessed=moved, transcendentals=transcendentals),
        name=name,
    )(*operands)


def paired(xbc, dt_raw, conv_weight, conv_bias, a_log, dt_bias, skip_gain):
    axes = ("ctx", "head")
    shards, length = lax.axis_size("head"), lax.axis_size("ctx")
    devices, peers, pairs = shards * length, shards * PAIR, length // PAIR
    tok = xbc.shape[0]
    slab = tok * peers
    per_group = HEADS // GROUPS
    context, shard = lax.axis_index("ctx"), lax.axis_index("head")
    pair, core = context // PAIR, context % PAIR
    group = shard * PAIR + core
    place = jnp.stack([group, pair, core, core * shards + shard, shard]).astype(jnp.int32)

    def over(block, target):
        route = [(i, target(i)) for i in range(devices)]
        return lax.ppermute(block, axes, [(i, j) for i, j in route if j is not None and j < devices])

    own, send, taps, bias, near, far = pack(place, xbc, dt_raw, conv_weight, conv_bias[None], shards)
    near = over(near, lambda i: i + 1)
    far = over(far, lambda i: (i + 1) ^ shards)
    rows = (own, over(send, lambda i: i ^ shards))

    received, starts = [], []
    first = 0
    for width, rest in PIECES:
        sent = activate(place, rows, (near, far), taps, bias, first, width, rest, shards)
        received.append(exchange(sent, axes, length))
        starts.append(first // HEAD_DIM)
        first += width

    tiles = [p.reshape(HEADS // LANES, LANES) for p in (a_log, dt_bias, skip_gain)]
    b, cum, row, factor, tail, skip = local_call(
        functools.partial(prep_kernel, shards),
        [
            ((slab, STATE), BF16),
            ((slab, LANES), F32),
            ((LANES, slab), F32),
            ((slab, 2 * LANES), BF16),
            ((slab, 2 * LANES), BF16),
            ((16, 3 * LANES), BF16),
        ],
        [place] + received[0] + tiles,
        scratch=[pltpu.VMEM((slab, LANES), BF16)],
        flops=2 * slab * BLOCK * 3 * LANES,
        name="prep",
    )
    c, score = local_call(
        functools.partial(score_kernel, shards),
        [((slab, STATE), BF16), ((slab, BLOCK), F32)],
        [place] + received[1] + [b],
        flops=2 * slab * BLOCK * STATE,
        name="score",
    )
    pieces = []
    for head, (width, _), blocks in zip(starts, PIECES, received):
        x, sent, own = local_call(
            functools.partial(state_kernel, head, shards),
            [((slab, width), BF16), ((STATE + 16, width), BF16), ((STATE, width), F32)],
            [place] + blocks + [b, factor, tail],
            flops=4 * slab * STATE * width,
            name="state",
        )
        last = over(sent, lambda i: i + peers if i // peers % 2 == 0 else None)
        (joined,) = local_call(combine_kernel, [(sent.shape, BF16)], [last, sent], name="combine")
        before = over(joined, lambda i: i + 2 * peers if i // peers == 1 else None)
        alone = over(joined, lambda i: i + peers if i // peers == 1 else None)
        (partial,) = local_call(
            functools.partial(local_kernel, head),
            [((slab, width), F32)],
            [x, cum, row, score, skip],
            flops=8 * slab * STATE * width,
            transcendentals=slab * BLOCK * width // HEAD_DIM,
            name="local",
        )
        pieces.append((head, width, [last, before, alone], own, partial))
    keeps, gots = [], []
    for head, width, earlier, own, partial in pieces:
        keep, send = local_call(
            functools.partial(final_kernel, head),
            [((BLOCK, width), BF16)] * 2,
            [place] + earlier + [own, c, factor, partial],
            flops=4 * slab * STATE * width,
            name="final",
        )
        keeps.append(keep)
        gots.append(over(send, lambda i: i ^ shards))
    (out,) = local_call(
        functools.partial(assemble_kernel, len(keeps)),
        [((BLOCK, PAIR * per_group * HEAD_DIM), BF16)],
        [place] + keeps + gots,
        name="assemble",
    )
    return out


def solution(mesh):
    in_specs = (P(("ctx", "head"), None), P(("ctx", "head"), None), P(), P(), P(), P(), P())
    out_specs = P("ctx", "head")
    shards, length = mesh.shape["head"], mesh.shape["ctx"]

    def program(xbc, *rest):
        slab = xbc.shape[0] // length
        fits = shards == GROUPS // PAIR and length == 4 * PAIR and slab == BLOCK
        return jax.shard_map(
            paired if fits else on_device,
            mesh=mesh,
            in_specs=in_specs,
            out_specs=out_specs,
            check_vma=False,
        )(xbc, *rest)

    return program
```

```python
import functools

import jax
import jax.numpy as jnp
from jax import lax
from jax.experimental import pallas as pl
from jax.experimental.pallas import tpu as pltpu
from jax.sharding import PartitionSpec as P

HEADS = 256
HEAD_DIM = 64
STATE = 256
GROUPS = 8
BLOCK = 256


def from_behind(block, axis, distance):
    devices = range(lax.axis_size(axis))
    route = [(i - distance, i) for i in devices if i - distance in devices]
    return lax.ppermute(block, axis, route)


def carried_in(array, axis, combine, identity):
    length, index = (lax.axis_size(axis), lax.axis_index(axis))
    everything = jax.tree.map(lambda part: lax.all_gather(part, axis), array)
    start = jax.tree.map(
        lambda part, zero: jnp.broadcast_to(jnp.asarray(zero, part.dtype), part.shape),
        array,
        identity,
    )

    def hop(k, before):
        reached = k < index
        new = combine(before, jax.tree.map(lambda part: part[k], everything))
        return jax.tree.map(lambda a, b: jnp.where(reached, a, b), new, before)

    return lax.fori_loop(0, length, hop, start)


def convolve(rows, edge, weight, bias):
    count = rows.shape[0]
    wide = jnp.concatenate([edge, rows], 0).astype(jnp.float32)
    acc = bias[None, :] + weight[0] * wide[0:count]
    acc = acc + weight[1] * wide[1 : count + 1]
    acc = acc + weight[2] * wide[2 : count + 2]
    acc = acc + weight[3] * wide[3 : count + 3]
    return jax.nn.silu(acc).astype(jnp.bfloat16)


def rearrange_heads(rows, shards, per_dev, groups_dev, per_group):
    count = rows.shape[0]
    inner = HEADS * HEAD_DIM
    replicate_groups = max(1, per_group // per_dev)
    heads_part = rows[:, :inner].reshape(count, shards, per_dev * HEAD_DIM)
    b_part = rows[:, inner : inner + GROUPS * STATE].reshape(count, GROUPS, STATE)
    c_part = rows[:, inner + GROUPS * STATE :].reshape(count, GROUPS, STATE)
    b_part = jnp.repeat(b_part, replicate_groups, axis=1).reshape(count, shards, groups_dev * STATE)
    c_part = jnp.repeat(c_part, replicate_groups, axis=1).reshape(count, shards, groups_dev * STATE)
    return jnp.concatenate([heads_part, b_part, c_part], axis=2)


def inner_block(xs, bmat, cmat, steps, cum):
    size = xs.shape[0]
    lower = jnp.arange(size)[:, None] >= jnp.arange(size)[None, :]
    scores = jnp.einsum("qgn,kgn->gqk", cmat, bmat, preferred_element_type=jnp.float32)
    order = jnp.transpose(cum, (1, 2, 0))
    gap = order[..., :, None] - order[..., None, :]
    decay = jnp.exp(jnp.where(lower, gap, -jnp.inf))
    mixing = (scores[:, None] * decay * jnp.transpose(steps, (1, 2, 0))[..., None, :]).astype(
        jnp.bfloat16
    )
    local = jnp.einsum("gjqk,kgjp->qgjp", mixing, xs, preferred_element_type=jnp.float32)
    tail = jnp.exp(cum[size - 1][None] - cum) * steps
    loaded = (bmat[:, :, None, :].astype(jnp.float32) * tail[..., None]).astype(jnp.bfloat16)
    block_state = jnp.einsum("kgjn,kgjp->gjnp", loaded, xs, preferred_element_type=jnp.float32)
    return (local, block_state)


def on_device(xbc, dt_raw, conv_weight, conv_bias, a_log, dt_bias, skip_gain):
    tok = xbc.shape[0]
    shards = lax.axis_size("head")
    per_dev = HEADS // shards
    per_group = HEADS // GROUPS
    groups_dev = max(1, per_dev // per_group)
    heads_per_cluster = per_dev // groups_dev
    sent = rearrange_heads(xbc, shards, per_dev, groups_dev, per_group)
    mine, rates = (
        lax.all_to_all(sent, "head", split_axis=1, concat_axis=0, tiled=True),
        lax.all_to_all(
            dt_raw.reshape(tok, shards, per_dev), "head", split_axis=1, concat_axis=0, tiled=True
        ),
    )
    slab = tok * shards
    mine = mine.reshape(slab, mine.shape[2])
    rates = rates.reshape(slab, per_dev)
    shard = lax.axis_index("head")
    taps = lax.dynamic_index_in_dim(
        rearrange_heads(conv_weight, shards, per_dev, groups_dev, per_group),
        shard,
        1,
        keepdims=False,
    )
    offset = lax.dynamic_index_in_dim(
        rearrange_heads(conv_bias[None, :], shards, per_dev, groups_dev, per_group),
        shard,
        1,
        keepdims=False,
    )
    edge = from_behind(mine[slab - 3 :], "ctx", 1)
    mine = convolve(mine, edge, taps, offset[0])
    nchunk = slab // BLOCK
    width = per_dev * HEAD_DIM
    xs = mine[:, :width].reshape(nchunk, BLOCK, groups_dev, heads_per_cluster, HEAD_DIM)
    bmat = mine[:, width : width + groups_dev * STATE].reshape(nchunk, BLOCK, groups_dev, STATE)
    cmat = mine[:, width + groups_dev * STATE :].reshape(nchunk, BLOCK, groups_dev, STATE)
    first = shard * per_dev
    rate = (-jnp.exp(lax.dynamic_slice_in_dim(a_log, first, per_dev))).reshape(
        groups_dev, heads_per_cluster
    )
    bias_dt = lax.dynamic_slice_in_dim(dt_bias, first, per_dev).reshape(
        groups_dev, heads_per_cluster
    )
    skip = lax.dynamic_slice_in_dim(skip_gain, first, per_dev).reshape(
        groups_dev, heads_per_cluster
    )
    steps = jax.nn.softplus(
        rates.astype(jnp.float32).reshape(nchunk, BLOCK, groups_dev, heads_per_cluster) + bias_dt
    )
    cum = jnp.cumsum(steps * rate, axis=1)

    def block_step(carry, item):
        held, product = carry
        x_part, b_part, c_part, step_part, cum_part = item
        local, block_state = inner_block(x_part, b_part, c_part, step_part, cum_part)
        lifted = c_part.astype(jnp.float32)[:, :, None, :] * jnp.exp(cum_part)[..., None]
        carried = jnp.einsum("qgjn,gjnp->qgjp", lifted, held, precision=lax.Precision.HIGHEST)
        partial_out = local + carried + skip[..., None] * x_part.astype(jnp.float32)
        end = jnp.exp(cum_part[BLOCK - 1])
        return ((end[..., None, None] * held + block_state, product * end), (partial_out, product))

    zero_state = jnp.zeros((groups_dev, heads_per_cluster, STATE, HEAD_DIM), jnp.float32)
    unit = jnp.ones((groups_dev, heads_per_cluster), jnp.float32)
    (slab_state, slab_decay), (partials, product_in) = lax.scan(
        block_step, (zero_state, unit), (xs, bmat, cmat, steps, cum)
    )

    def combine(preceding_state, later):
        return (
            preceding_state[0] * later[0],
            later[0][..., None, None] * preceding_state[1] + later[1],
        )

    _, entering = carried_in((slab_decay, slab_state), "ctx", combine, (unit, zero_state))
    projected = jnp.einsum(
        "cqgn,gjnp->cqgjp", cmat.astype(jnp.float32), entering, precision=lax.Precision.HIGHEST
    )
    factor = jnp.exp(cum) * product_in[:, None]
    total = partials + factor[..., None] * projected
    return total.astype(jnp.bfloat16).reshape(slab, width)


PAIR = 2
LANES = 128
LOG2E = 1.4426950408889634
F32, BF16 = jnp.float32, jnp.bfloat16
WIDTHS = (512, 512, 640, 384)
RESTS = ("", "BD", "C", "")
JOINED = ((0, 1), (2,), (3,))


def halves(value, count):
    parts = []
    for _ in range(count):
        part = value.astype(BF16)
        parts.append(part)
        value = value - part.astype(F32)
    return parts


def spread(first_head, width, copies):
    lane = lax.broadcasted_iota(jnp.int32, (copies * LANES, width), 0) % LANES
    column = lax.broadcasted_iota(jnp.int32, (copies * LANES, width), 1)
    return (lane == first_head + column // HEAD_DIM).astype(BF16)


def dot(a, b):
    return jnp.dot(a, b, preferred_element_type=F32)


def ds(start, width):
    return pl.ds(pl.multiple_of(start, LANES), width)


def run(copies, sems):
    started = []
    for i, (source, target) in enumerate(copies):
        copy = pltpu.make_async_copy(source, target, sems.at[i])
        copy.start()
        started.append(copy)
    return started


PER_GROUP = HEADS * HEAD_DIM // GROUPS
INNER = HEADS * HEAD_DIM


def channels(group, first, width):
    return ds(group * PER_GROUP + first, width)


def pack_first_kernel(shards, place, xbc, send, sems):
    core, shard = place[2], place[4]
    width = send.shape[1] // shards
    copies = []
    for r in range(shards):
        group = (shard ^ r) * PAIR + 1 - core
        copies.append((xbc.at[:, channels(group, 0, width)], send.at[:, r * width : (r + 1) * width]))
    for copy in run(copies, sems):
        copy.wait()


def pack_kernel(shards, place, xbc, dt_raw, weight, bias, order, send, taps, offset, near, far, tail, sems):
    core, shard = place[2], place[4]
    count = xbc.shape[0]
    first = WIDTHS[0]
    width = PER_GROUP - first
    rest = width * shards
    copies = [(xbc.at[count - 16 :], tail)]
    for r in range(shards):
        group = (shard ^ r) * PAIR + 1 - core
        copies.append((xbc.at[:, channels(group, first, width)], send.at[:, r * width : (r + 1) * width]))
        for i in range(2):
            to = rest + (i * shards + r) * STATE
            copies.append((xbc.at[:, ds(INNER + (i * GROUPS + group) * STATE, STATE)], send.at[:, to : to + STATE]))
    copies.append((dt_raw, send.at[:, send.shape[1] - HEADS :]))
    for source, target in ((weight, taps), (bias, offset)):
        copies.append((source.at[:, channels(place[0], 0, PER_GROUP)], target.at[:, :PER_GROUP]))
        for i in range(2):
            to = PER_GROUP + i * STATE
            at = ds(INNER + (i * GROUPS + place[0]) * STATE, STATE)
            copies.append((source.at[:, at], target.at[:, to : to + STATE]))
    started = run(copies, sems)
    started[0].wait()
    for edge, side in ((near, 1), (far, 0)):
        for r in range(shards):
            group = ((shards - 1) ^ r) * PAIR + side
            to = r * (PER_GROUP + 2 * STATE)
            parts = [(group * PER_GROUP, PER_GROUP)]
            parts += [(INNER + (i * GROUPS + group) * STATE, STATE) for i in range(2)]
            for start, size in parts:
                edge[:, to : to + size] = tail[:, start : start + size].astype(F32)[13:16].astype(BF16)
                to += size
    for copy in started[1:]:
        copy.wait()


def merge_kernel(shards, piece, place, xbc, dt_raw, got, near, far, order, *refs):
    outs, sems = refs[:shards], refs[shards]
    core, shard = place[2], place[4]
    count = xbc.shape[0]
    first = sum(WIDTHS[:piece])
    width = WIDTHS[piece]
    stride = WIDTHS[0] if piece == 0 else PER_GROUP - WIDTHS[0]
    base = 0 if piece == 0 else first - WIDTHS[0]
    mine = pl.ds(pl.multiple_of(core * count, count), count)
    other = pl.ds(pl.multiple_of((1 - core) * count, count), count)
    copies = []
    for r in range(shards):
        group = (shard ^ r) * PAIR + core
        copies.append((xbc.at[:, channels(group, first, width)], outs[r].at[mine, :width]))
        at = r * stride + base
        copies.append((got.at[:, at : at + width], outs[r].at[other, :width]))
        to = width
        for kind in RESTS[piece]:
            if kind in "BC":
                i = "BC".index(kind)
                copies.append((xbc.at[:, ds(INNER + (i * GROUPS + group) * STATE, STATE)], outs[r].at[mine, to : to + STATE]))
                at = stride * shards + (i * shards + r) * STATE
                copies.append((got.at[:, at : at + STATE], outs[r].at[other, to : to + STATE]))
                to += STATE
    started = run(copies, sems)
    if "D" in RESTS[piece]:
        lane = lax.broadcasted_iota(jnp.int32, (count, LANES), 1)
        per_tile = LANES * GROUPS // HEADS
        heads = HEADS // GROUPS
        for r in range(shards):
            group = (shard ^ r) * PAIR + core
            tile, shift = group // per_tile, (LANES - (group % per_tile) * heads) % LANES
            own = dt_raw[:, ds(tile * LANES, LANES)].astype(F32)
            theirs = got[:, ds(got.shape[1] - HEADS + tile * LANES, LANES)].astype(F32)
            low = jnp.where(core == 0, own, theirs)
            high = jnp.where(core == 0, theirs, own)
            packed = jnp.zeros((count // 2, LANES), F32)
            for j, rows in enumerate((low, high)):
                rows = jnp.where(lane < heads, pltpu.roll(rows, shift, 1), 0.0)
                for i in range(2):
                    part = rows[i * count // 2 : (i + 1) * count // 2]
                    packed = packed + pltpu.roll(part, (2 * j + i) * heads, 1)
            outs[r][: count // 2, to : to + LANES] = packed.astype(BF16)
            size = PER_GROUP + 2 * STATE
            at = slice(r * size, (r + 1) * size)
            edge = near[:, at].astype(F32) + far[:, at].astype(F32)
            edge = jnp.concatenate([edge, jnp.zeros((1, size), F32)], 0)
            edge = jnp.concatenate([edge[:, q * LANES : (q + 1) * LANES] for q in range(size // LANES)], 0)
            fill = jnp.zeros((PAIR * count - count // 2 - edge.shape[0], LANES), F32)
            outs[r][count // 2 :, to : to + LANES] = jnp.concatenate([edge, fill], 0).astype(BF16)
    for copy in started:
        copy.wait()


def exchange(blocks, axes, length):
    shards = len(blocks)
    got = {0: blocks[0]}
    for r in [*range(2, shards), 1]:
        route = [(k * shards + i, k * shards + (i ^ r)) for k in range(length) for i in range(shards)]
        got[r] = lax.ppermute(blocks[r], axes, route)
    return [got[r] for r in range(shards)]


def convolve_in_order(place, blocks, columns, edge, tap, bias, wide, put):
    width = columns.stop - columns.start
    count = blocks[0].shape[0] // PAIR
    wide[5:8, :width] = edge
    for r, block in enumerate(blocks):
        for core in range(PAIR):
            at = pl.multiple_of((core * len(blocks) + (place[4] ^ r)) * count + 8, 8)
            wide[pl.ds(at, count), :width] = block[core * count : (core + 1) * count, columns].astype(F32)
    tap, bias = tap * 0.5, bias * 0.5
    for start in range(0, PAIR * len(blocks) * count, count):
        acc = bias + tap[0:1] * wide[start + 5 : start + 5 + count, :width]
        acc = acc + tap[1:2] * wide[start + 6 : start + 6 + count, :width]
        acc = acc + tap[2:3] * wide[start + 7 : start + 7 + count, :width]
        acc = acc + tap[3:4] * wide[start + 8 : start + 8 + count, :width]
        put(start, count, (acc + acc * jnp.tanh(acc)).astype(BF16))


def prep_kernel(shards, place, *refs):
    blocks, (taps, offset, a_ref, bias_ref, skip_ref) = refs[:shards], refs[shards : shards + 5]
    b_ref, edge_ref, cum_ref, row_ref, factor_ref, tail_ref, skip_out, dt_ref, wide = refs[shards + 5 :]
    start = blocks[0].shape[1] - STATE - LANES
    last = slice(start + STATE, start + STATE + LANES)
    size = edge_ref.shape[1]
    count = blocks[0].shape[0] // PAIR
    half, heads = count // 2, HEADS // GROUPS
    edge = blocks[0][half : half + 4 * size // LANES, last].astype(F32)
    for block in blocks[1:]:
        edge = edge + block[half : half + 4 * size // LANES, last].astype(F32)
    for q in range(size // LANES):
        edge_ref[:, q * LANES : (q + 1) * LANES] = edge[4 * q : 4 * q + 4]
    for r, block in enumerate(blocks):
        packed = block[:half, last].astype(F32)
        for j in range(2 * PAIR):
            at = ((j // 2) * shards + (place[4] ^ r)) * count + (j % 2) * half
            rows = packed if j == 0 else pltpu.roll(packed, LANES - j * heads, 1)
            dt_ref[pl.ds(pl.multiple_of(at, half), half), :] = rows

    def put(start, count, value):
        b_ref[start : start + count] = value

    at = slice(PER_GROUP, PER_GROUP + STATE)
    convolve_in_order(
        place, blocks, slice(start, start + STATE), edge_ref[0:3, at], taps[:, at], offset[:, at], wide, put
    )
    per_tile = LANES * GROUPS // HEADS
    group = place[0]
    tile = group // per_tile
    shift = (LANES - (group % per_tile) * heads) % LANES

    def lanes_of(ref):
        return pltpu.roll(jnp.broadcast_to(ref[pl.ds(tile, 1), :], (8, LANES)), shift, 1)

    rate = -jnp.exp(lanes_of(a_ref)[0:1])
    raw = dt_ref[...] + lanes_of(bias_ref)[0:1]
    step = jnp.maximum(raw, 0.0) + jnp.log1p(jnp.exp(-jnp.abs(raw)))
    skip = lanes_of(skip_ref)
    skip_out[...] = jnp.concatenate(halves(jnp.concatenate([skip, skip], 0), 3), 1)
    lower = (
        lax.broadcasted_iota(jnp.int32, (BLOCK, BLOCK), 0)
        >= lax.broadcasted_iota(jnp.int32, (BLOCK, BLOCK), 1)
    ).astype(BF16)
    valid = lax.broadcasted_iota(jnp.int32, (BLOCK, LANES), 1) < heads
    for block in range(PAIR):
        at = slice(block * BLOCK, (block + 1) * BLOCK)
        here = jnp.where(valid, step[at], 1.0)
        parts = halves(here * rate, 3)
        cum = dot(lower, parts[0]) + (dot(lower, parts[1]) + dot(lower, parts[2]))
        cum = cum * LOG2E
        cum_ref[at] = cum
        row_ref[:, at] = jnp.transpose(cum - jnp.log2(here))
        factor_ref[at] = jnp.concatenate(halves(jnp.exp2(cum), 2), 1)
        tail = jnp.exp2(cum[BLOCK - 1 :] - cum) * here
        tail_ref[at] = jnp.concatenate(halves(tail, 2), 1)


def score_kernel(shards, place, *refs):
    blocks, (taps, offset, edge_ref, b_ref, order, c_ref, score_ref, wide) = refs[:shards], refs[shards:]
    start = blocks[0].shape[1] - STATE
    at = slice(PER_GROUP + STATE, PER_GROUP + 2 * STATE)

    def put(start, count, value):
        c_ref[start : start + count] = value

    convolve_in_order(
        place, blocks, slice(start, start + STATE), edge_ref[0:3, at], taps[:, at], offset[:, at], wide, put
    )
    for block in range(PAIR):
        at = slice(block * BLOCK, (block + 1) * BLOCK)
        score_ref[at] = lax.dot_general(
            c_ref[at], b_ref[at], (((1,), (1,)), ((), ())), preferred_element_type=F32
        )


def decay_of(ref):
    decay = ref[STATE : STATE + 16].astype(F32)
    return decay[0:1] + (decay[1:2] + decay[2:3])


def put_decay(ref, decay):
    row = lax.broadcasted_iota(jnp.int32, (16, ref.shape[1]), 0)
    high, middle, low = (part.astype(F32) for part in halves(decay, 3))
    packed = jnp.where(row == 0, high, jnp.where(row == 1, middle, jnp.where(row == 2, low, 0.0)))
    ref[STATE:] = packed.astype(BF16)


def state_kernel(shards, pieces, place, *refs):
    blocks, refs = refs[: shards * len(pieces)], refs[shards * len(pieces) :]
    taps, offset, edge_ref, b_ref, factor_ref, tail_ref, order, x_ref, send_ref, own_ref, wide = refs
    width = x_ref.shape[1]
    first = sum(WIDTHS[: pieces[0]])
    start = 0
    for i, piece in enumerate(pieces):
        to = slice(start, start + WIDTHS[piece])
        at = slice(first + start, first + start + WIDTHS[piece])
        start += WIDTHS[piece]

        def put(row, count, value, to=to):
            x_ref[row : row + count, to] = value

        convolve_in_order(
            place,
            blocks[i * shards : (i + 1) * shards],
            slice(0, WIDTHS[piece]),
            edge_ref[0:3, at],
            taps[:, at],
            offset[:, at],
            wide,
            put,
        )
    expand = spread(first // HEAD_DIM, width, 2)
    both = []
    for block in range(PAIR):
        at = slice(block * BLOCK, (block + 1) * BLOCK)
        loaded = (x_ref[at].astype(F32) * dot(tail_ref[at], expand)).astype(BF16)
        both.append(
            lax.dot_general(b_ref[at], loaded, (((0,), (0,)), ((), ())), preferred_element_type=F32)
        )
    ends = [dot(factor_ref[(i + 1) * BLOCK - 16 : (i + 1) * BLOCK], expand)[15:16] for i in range(PAIR)]
    own_ref[...] = both[0]
    send_ref[0:STATE] = (ends[1] * both[0] + both[1]).astype(BF16)
    put_decay(send_ref, ends[0] * ends[1])


def combine_kernel(early_ref, late_ref, order, out_ref):
    decay = decay_of(late_ref)
    out_ref[:STATE] = (decay * early_ref[:STATE].astype(F32) + late_ref[:STATE].astype(F32)).astype(BF16)
    put_decay(out_ref, decay * decay_of(early_ref))


def local_kernel(first_head, x_ref, cum_ref, row_ref, score_ref, skip_ref, order, out_ref):
    width = x_ref.shape[1]
    half = BLOCK // 2
    expand = spread(first_head, width, 3)
    skip = dot(skip_ref[...], expand)[0:1]
    lower = lax.broadcasted_iota(jnp.int32, (half, half), 0) >= lax.broadcasted_iota(
        jnp.int32, (half, half), 1
    )
    lane = lax.broadcasted_iota(jnp.int32, (BLOCK, LANES), 1)
    for block in range(PAIR):
        base = block * BLOCK
        for tile in range(width // LANES):
            columns = slice(tile * LANES, (tile + 1) * LANES)
            x = x_ref[base : base + BLOCK, columns]
            top = skip[:, columns] * x[:half].astype(F32)
            bottom = skip[:, columns] * x[half:].astype(F32)
            for side in range(LANES // HEAD_DIM):
                head = first_head + tile * (LANES // HEAD_DIM) + side
                own = jnp.where(lane // HEAD_DIM == side, x, jnp.zeros_like(x))
                cum = cum_ref[base : base + BLOCK, head : head + 1]
                row = row_ref[head : head + 1, base : base + BLOCK]
                diag = jnp.where(lower, cum[:half] - row[:, :half], -1e30)
                mixing = jnp.exp2(diag) * score_ref[base : base + half, :half]
                top = top + dot(mixing.astype(BF16), own[:half])
                left = jnp.exp2(cum[half:] - row[:, :half]) * score_ref[base + half : base + BLOCK, :half]
                diag = jnp.where(lower, cum[half:] - row[:, half:], -1e30)
                right = jnp.exp2(diag) * score_ref[base + half : base + BLOCK, half:]
                mixing = jnp.concatenate([left.astype(BF16), right.astype(BF16)], 1)
                bottom = bottom + dot(mixing, own)
            out_ref[base : base + half, columns] = top
            out_ref[base + half : base + BLOCK, columns] = bottom


def final_kernel(first_head, place, *refs):
    last, before, alone, own_ref, c_ref, factor_ref, partial_ref, keep_ref, send_ref = refs
    width = own_ref.shape[1]
    core = place[2]
    expand = spread(first_head, width, 2)
    held = last[:STATE].astype(F32) + decay_of(last) * before[:STATE].astype(F32)
    held = held + alone[:STATE].astype(F32)
    factor = dot(factor_ref[...], expand)
    outs = []
    for block in range(PAIR):
        at = slice(block * BLOCK, (block + 1) * BLOCK)
        carried = dot(c_ref[at], held.astype(BF16))
        outs.append((partial_ref[at] + factor[at] * carried).astype(BF16))
        held = factor[BLOCK - 1 : BLOCK] * held + own_ref[...]

    @pl.when(core == 0)
    def _():
        keep_ref[...] = outs[0]
        send_ref[...] = outs[1]

    @pl.when(core == 1)
    def _():
        keep_ref[...] = outs[1]
        send_ref[...] = outs[0]


def assemble_kernel(count, place, *refs):
    keeps, gots, out = refs[:count], refs[count : 2 * count], refs[2 * count]
    core = place[2]
    half = out.shape[1] // PAIR

    def put(own, other):
        start = 0
        for keep, got in zip(keeps, gots):
            width = keep.shape[1]
            out[:, own + start : own + start + width] = keep[...]
            out[:, other + start : other + start + width] = got[...]
            start += width

    pl.when(core == 0)(lambda: put(0, half))
    pl.when(core == 1)(lambda: put(half, 0))


class Stay:
    def __init__(self, array):
        self.array = array


def call(body, outs, operands, scratch=(), flops=0, transcendentals=0, name=None):
    shapes = [jax.ShapeDtypeStruct(shape, dtype) for shape, dtype in outs]
    smem, vmem, hbm = (pl.BlockSpec(memory_space=m) for m in (pltpu.SMEM, pltpu.VMEM, pltpu.HBM))
    specs = [
        hbm if isinstance(o, Stay) else smem if o.dtype == jnp.int32 else vmem for o in operands
    ]
    moved = sum(o.size * o.dtype.itemsize for o in shapes) * 2
    return pl.pallas_call(
        body,
        out_shape=shapes,
        in_specs=specs,
        out_specs=[vmem] * len(outs),
        scratch_shapes=scratch,
        compiler_params=pltpu.CompilerParams(vmem_limit_bytes=16 << 20),
        cost_estimate=pl.CostEstimate(flops=flops, bytes_accessed=moved, transcendentals=transcendentals),
        name=name,
    )(*[o.array if isinstance(o, Stay) else o for o in operands])


def paired(xbc, dt_raw, conv_weight, conv_bias, a_log, dt_bias, skip_gain):
    axes = ("ctx", "head")
    shards, length = lax.axis_size("head"), lax.axis_size("ctx")
    devices, peers = shards * length, shards * PAIR
    tok = xbc.shape[0]
    slab = tok * peers
    context, shard = lax.axis_index("ctx"), lax.axis_index("head")
    pair, core = context // PAIR, context % PAIR
    group = shard * PAIR + core
    place = jnp.stack([group, pair, core, core * shards + shard, shard]).astype(jnp.int32)

    def over(block, target):
        route = [(i, target(i)) for i in range(devices)]
        return lax.ppermute(block, axes, [(i, j) for i, j in route if j is not None and j < devices])

    def swap(block):
        return over(block, lambda i: i ^ shards)

    rows = Stay(xbc)
    (sent,) = call(
        functools.partial(pack_first_kernel, shards),
        [((tok, shards * WIDTHS[0]), BF16)],
        [place, rows],
        scratch=[pltpu.SemaphoreType.DMA((shards,))],
        name="pack_first",
    )
    got_first = swap(sent)
    size = PER_GROUP + 2 * STATE
    sent, taps, offset, near, far = call(
        functools.partial(pack_kernel, shards),
        [
            ((tok, shards * (size - WIDTHS[0]) + HEADS), BF16),
            ((4, size), F32),
            ((1, size), F32),
            ((3, shards * size), BF16),
            ((3, shards * size), BF16),
        ],
        [place, rows, Stay(dt_raw), Stay(conv_weight), Stay(conv_bias[None]), Stay(sent)],
        scratch=[pltpu.VMEM((16, xbc.shape[1]), BF16), pltpu.SemaphoreType.DMA((3 * shards + 8,))],
        name="pack",
    )
    near = over(near, lambda i: i + peers if i % peers == peers - 1 else None)
    far = over(far, lambda i: i + shards if i % peers == peers - 1 else None)
    got_rest = swap(sent)

    received, order = [], place
    for piece, (width, rest) in enumerate(zip(WIDTHS, RESTS)):
        total = width + sum(LANES if kind == "D" else STATE for kind in rest)
        blocks = call(
            functools.partial(merge_kernel, shards, piece),
            [((PAIR * tok, total), BF16)] * shards,
            [
                place,
                rows,
                dt_raw if "D" in rest else Stay(dt_raw),
                got_rest if piece else got_first,
                near if "D" in rest else Stay(got_first),
                far if "D" in rest else Stay(got_first),
                Stay(received[piece - 2][2] if piece > 1 else got_first),
            ],
            scratch=[pltpu.SemaphoreType.DMA((2 * shards * (1 + len(rest)),))],
            name="merge",
        )
        received.append(exchange(blocks, axes, length))

    tiles = [p.reshape(HEADS // LANES, LANES) for p in (a_log, dt_bias, skip_gain)]
    b, edge, cum, row, factor, tail, skip = call(
        functools.partial(prep_kernel, shards),
        [
            ((slab, STATE), BF16),
            ((4, size), F32),
            ((slab, LANES), F32),
            ((LANES, slab), F32),
            ((slab, 2 * LANES), BF16),
            ((slab, 2 * LANES), BF16),
            ((16, 3 * LANES), BF16),
        ],
        [place] + received[1] + [taps, offset] + tiles,
        scratch=[pltpu.VMEM((slab, LANES), F32), pltpu.VMEM((slab + 8, STATE), F32)],
        flops=2 * slab * BLOCK * 3 * LANES,
        transcendentals=slab * STATE,
        name="prep",
    )
    pieces, order = [], place
    for joined in JOINED:
        width = sum(WIDTHS[piece] for piece in joined)
        x, sent, own = call(
            functools.partial(state_kernel, shards, joined),
            [((slab, width), BF16), ((STATE + 16, width), BF16), ((STATE, width), F32)],
            [place]
            + [block for piece in joined for block in received[piece]]
            + [taps, offset, edge, b, factor, tail, Stay(order)],
            scratch=[pltpu.VMEM((slab + 8, max(WIDTHS)), F32)],
            flops=4 * slab * STATE * width,
            transcendentals=slab * width,
            name="state",
        )
        last = over(sent, lambda i: i + peers if i // peers % 2 == 0 else None)
        (combined,) = call(
            combine_kernel,
            [(sent.shape, BF16)],
            [last, sent, Stay(order)],
            flops=4 * sent.size,
            name="combine",
        )
        before = over(combined, lambda i: i + 2 * peers if i // peers == 1 else None)
        alone = over(combined, lambda i: i + peers if i // peers == 1 else None)
        pieces.append((sum(WIDTHS[: joined[0]]) // HEAD_DIM, width, [last, before, alone], own, x, sent))
        order = sent
    c, score = call(
        functools.partial(score_kernel, shards),
        [((slab, STATE), BF16), ((slab, BLOCK), F32)],
        [place] + received[2] + [taps, offset, edge, b, Stay(pieces[1][5])],
        scratch=[pltpu.VMEM((slab + 8, STATE), F32)],
        flops=2 * slab * BLOCK * STATE,
        transcendentals=slab * STATE,
        name="score",
    )
    keeps, gots = [], []
    for head, width, earlier, own, x, _ in pieces:
        (partial,) = call(
            functools.partial(local_kernel, head),
            [((slab, width), F32)],
            [x, cum, row, score, skip, Stay(score)],
            flops=8 * slab * STATE * width,
            transcendentals=slab * BLOCK * width // HEAD_DIM,
            name="local",
        )
        keep, send = call(
            functools.partial(final_kernel, head),
            [((BLOCK, width), BF16)] * 2,
            [place] + earlier + [own, c, factor, partial],
            flops=4 * slab * STATE * width,
            name="final",
        )
        keeps.append(keep)
        gots.append(swap(send))
    (out,) = call(
        functools.partial(assemble_kernel, len(keeps)),
        [((BLOCK, PAIR * PER_GROUP), BF16)],
        [place] + keeps + gots,
        name="assemble",
    )
    return out


def solution(mesh):
    in_specs = (P(("ctx", "head"), None), P(("ctx", "head"), None), P(), P(), P(), P(), P())
    out_specs = P("ctx", "head")
    shards, length = mesh.shape["head"], mesh.shape["ctx"]

    def program(xbc, *rest):
        slab = xbc.shape[0] // length
        fits = shards == GROUPS // PAIR and length == 4 * PAIR and slab == BLOCK
        return jax.shard_map(
            paired if fits else on_device,
            mesh=mesh,
            in_specs=in_specs,
            out_specs=out_specs,
            check_vma=False,
        )(xbc, *rest)

    return program
```

```python
import functools

import jax
import jax.numpy as jnp
from jax import lax
from jax.experimental import pallas as pl
from jax.experimental.pallas import tpu as pltpu
from jax.sharding import PartitionSpec as P

HEADS = 256
HEAD_DIM = 64
STATE = 256
GROUPS = 8
BLOCK = 256


def from_behind(block, axis, distance):
    devices = range(lax.axis_size(axis))
    route = [(i - distance, i) for i in devices if i - distance in devices]
    return lax.ppermute(block, axis, route)


def carried_in(array, axis, combine, identity):
    length, index = (lax.axis_size(axis), lax.axis_index(axis))
    everything = jax.tree.map(lambda part: lax.all_gather(part, axis), array)
    start = jax.tree.map(
        lambda part, zero: jnp.broadcast_to(jnp.asarray(zero, part.dtype), part.shape),
        array,
        identity,
    )

    def hop(k, before):
        reached = k < index
        new = combine(before, jax.tree.map(lambda part: part[k], everything))
        return jax.tree.map(lambda a, b: jnp.where(reached, a, b), new, before)

    return lax.fori_loop(0, length, hop, start)


def convolve(rows, edge, weight, bias):
    count = rows.shape[0]
    wide = jnp.concatenate([edge, rows], 0).astype(jnp.float32)
    acc = bias[None, :] + weight[0] * wide[0:count]
    acc = acc + weight[1] * wide[1 : count + 1]
    acc = acc + weight[2] * wide[2 : count + 2]
    acc = acc + weight[3] * wide[3 : count + 3]
    return jax.nn.silu(acc).astype(jnp.bfloat16)


def rearrange_heads(rows, shards, per_dev, groups_dev, per_group):
    count = rows.shape[0]
    inner = HEADS * HEAD_DIM
    replicate_groups = max(1, per_group // per_dev)
    heads_part = rows[:, :inner].reshape(count, shards, per_dev * HEAD_DIM)
    b_part = rows[:, inner : inner + GROUPS * STATE].reshape(count, GROUPS, STATE)
    c_part = rows[:, inner + GROUPS * STATE :].reshape(count, GROUPS, STATE)
    b_part = jnp.repeat(b_part, replicate_groups, axis=1).reshape(count, shards, groups_dev * STATE)
    c_part = jnp.repeat(c_part, replicate_groups, axis=1).reshape(count, shards, groups_dev * STATE)
    return jnp.concatenate([heads_part, b_part, c_part], axis=2)


def inner_block(xs, bmat, cmat, steps, cum):
    size = xs.shape[0]
    lower = jnp.arange(size)[:, None] >= jnp.arange(size)[None, :]
    scores = jnp.einsum("qgn,kgn->gqk", cmat, bmat, preferred_element_type=jnp.float32)
    order = jnp.transpose(cum, (1, 2, 0))
    gap = order[..., :, None] - order[..., None, :]
    decay = jnp.exp(jnp.where(lower, gap, -jnp.inf))
    mixing = (scores[:, None] * decay * jnp.transpose(steps, (1, 2, 0))[..., None, :]).astype(
        jnp.bfloat16
    )
    local = jnp.einsum("gjqk,kgjp->qgjp", mixing, xs, preferred_element_type=jnp.float32)
    tail = jnp.exp(cum[size - 1][None] - cum) * steps
    loaded = (bmat[:, :, None, :].astype(jnp.float32) * tail[..., None]).astype(jnp.bfloat16)
    block_state = jnp.einsum("kgjn,kgjp->gjnp", loaded, xs, preferred_element_type=jnp.float32)
    return (local, block_state)


def on_device(xbc, dt_raw, conv_weight, conv_bias, a_log, dt_bias, skip_gain):
    tok = xbc.shape[0]
    shards = lax.axis_size("head")
    per_dev = HEADS // shards
    per_group = HEADS // GROUPS
    groups_dev = max(1, per_dev // per_group)
    heads_per_cluster = per_dev // groups_dev
    sent = rearrange_heads(xbc, shards, per_dev, groups_dev, per_group)
    mine, rates = (
        lax.all_to_all(sent, "head", split_axis=1, concat_axis=0, tiled=True),
        lax.all_to_all(
            dt_raw.reshape(tok, shards, per_dev), "head", split_axis=1, concat_axis=0, tiled=True
        ),
    )
    slab = tok * shards
    mine = mine.reshape(slab, mine.shape[2])
    rates = rates.reshape(slab, per_dev)
    shard = lax.axis_index("head")
    taps = lax.dynamic_index_in_dim(
        rearrange_heads(conv_weight, shards, per_dev, groups_dev, per_group),
        shard,
        1,
        keepdims=False,
    )
    offset = lax.dynamic_index_in_dim(
        rearrange_heads(conv_bias[None, :], shards, per_dev, groups_dev, per_group),
        shard,
        1,
        keepdims=False,
    )
    edge = from_behind(mine[slab - 3 :], "ctx", 1)
    mine = convolve(mine, edge, taps, offset[0])
    nchunk = slab // BLOCK
    width = per_dev * HEAD_DIM
    xs = mine[:, :width].reshape(nchunk, BLOCK, groups_dev, heads_per_cluster, HEAD_DIM)
    bmat = mine[:, width : width + groups_dev * STATE].reshape(nchunk, BLOCK, groups_dev, STATE)
    cmat = mine[:, width + groups_dev * STATE :].reshape(nchunk, BLOCK, groups_dev, STATE)
    first = shard * per_dev
    rate = (-jnp.exp(lax.dynamic_slice_in_dim(a_log, first, per_dev))).reshape(
        groups_dev, heads_per_cluster
    )
    bias_dt = lax.dynamic_slice_in_dim(dt_bias, first, per_dev).reshape(
        groups_dev, heads_per_cluster
    )
    skip = lax.dynamic_slice_in_dim(skip_gain, first, per_dev).reshape(
        groups_dev, heads_per_cluster
    )
    steps = jax.nn.softplus(
        rates.astype(jnp.float32).reshape(nchunk, BLOCK, groups_dev, heads_per_cluster) + bias_dt
    )
    cum = jnp.cumsum(steps * rate, axis=1)

    def block_step(carry, item):
        held, product = carry
        x_part, b_part, c_part, step_part, cum_part = item
        local, block_state = inner_block(x_part, b_part, c_part, step_part, cum_part)
        lifted = c_part.astype(jnp.float32)[:, :, None, :] * jnp.exp(cum_part)[..., None]
        carried = jnp.einsum("qgjn,gjnp->qgjp", lifted, held, precision=lax.Precision.HIGHEST)
        partial_out = local + carried + skip[..., None] * x_part.astype(jnp.float32)
        end = jnp.exp(cum_part[BLOCK - 1])
        return ((end[..., None, None] * held + block_state, product * end), (partial_out, product))

    zero_state = jnp.zeros((groups_dev, heads_per_cluster, STATE, HEAD_DIM), jnp.float32)
    unit = jnp.ones((groups_dev, heads_per_cluster), jnp.float32)
    (slab_state, slab_decay), (partials, product_in) = lax.scan(
        block_step, (zero_state, unit), (xs, bmat, cmat, steps, cum)
    )

    def combine(preceding_state, later):
        return (
            preceding_state[0] * later[0],
            later[0][..., None, None] * preceding_state[1] + later[1],
        )

    _, entering = carried_in((slab_decay, slab_state), "ctx", combine, (unit, zero_state))
    projected = jnp.einsum(
        "cqgn,gjnp->cqgjp", cmat.astype(jnp.float32), entering, precision=lax.Precision.HIGHEST
    )
    factor = jnp.exp(cum) * product_in[:, None]
    total = partials + factor[..., None] * projected
    return total.astype(jnp.bfloat16).reshape(slab, width)


PAIR = 2
LANES = 128
LOG2E = 1.4426950408889634
F32, BF16 = jnp.float32, jnp.bfloat16
WIDTHS = (512, 0, 768, 768)
RESTS = ("", "BD", "", "C")
GROUPED = ((0, 0, 512), (2, 0, 768), (3, 0, 384), (3, 384, 384))
FIRST_ROUND = ((256, 256), (384, 384), (384,), (384,))
SECOND_ROUND = ((512,), (384, 384), (384,), (384,))


def halves(value, count):
    parts = []
    for _ in range(count):
        part = value.astype(BF16)
        parts.append(part)
        value = value - part.astype(F32)
    return parts


def spread(first_head, width, copies):
    lane = lax.broadcasted_iota(jnp.int32, (copies * LANES, width), 0) % LANES
    column = lax.broadcasted_iota(jnp.int32, (copies * LANES, width), 1)
    return (lane == first_head + column // HEAD_DIM).astype(BF16)


def dot(a, b):
    return jnp.dot(a, b, preferred_element_type=F32)


def ds(start, width):
    return pl.ds(pl.multiple_of(start, LANES), width)


def run(copies, sems):
    started = []
    for i, (source, target) in enumerate(copies):
        copy = pltpu.make_async_copy(source, target, sems.at[i])
        copy.start()
        started.append(copy)
    return started


PER_GROUP = HEADS * HEAD_DIM // GROUPS
INNER = HEADS * HEAD_DIM


def channels(group, first, width):
    return ds(group * PER_GROUP + first, width)


def pack_first_kernel(shards, place, xbc, send, sems):
    core, shard = place[2], place[4]
    count = xbc.shape[0]
    width = WIDTHS[0]
    copies = []
    for r in range(shards):
        group = (shard ^ r) * PAIR + 1 - core
        copies.append((xbc.at[:, channels(group, 0, width)], send.at[:, r * width : (r + 1) * width]))
        last, rows = xbc.at[count - 16 :], slice(16 * r, 16 * r + 16)
        to = shards * width
        copies.append((last.at[:, channels(group, width, PER_GROUP - width)], send.at[rows, to : to + PER_GROUP - width]))
        to += PER_GROUP - width
        for i in range(2):
            at = ds(INNER + (i * GROUPS + group) * STATE, STATE)
            copies.append((last.at[:, at], send.at[rows, to + i * STATE : to + (i + 1) * STATE]))
    for copy in run(copies, sems):
        copy.wait()


def pack_kernel(shards, place, xbc, dt_raw, weight, bias, order, send, taps, offset, tail, sems):
    core, shard = place[2], place[4]
    count = xbc.shape[0]
    first = WIDTHS[0]
    width = PER_GROUP - first
    rest = width * shards
    size = PER_GROUP + 2 * STATE
    copies = []
    for r in range(shards):
        group = (shard ^ r) * PAIR + 1 - core
        copies.append((xbc.at[:, channels(group, first, width)], send.at[:, r * width : (r + 1) * width]))
        for i in range(2):
            to = rest + (i * shards + r) * STATE
            copies.append((xbc.at[:, ds(INNER + (i * GROUPS + group) * STATE, STATE)], send.at[:, to : to + STATE]))
    copies.append((dt_raw, send.at[:, send.shape[1] - HEADS :]))
    everything = [(weight, taps, place[0], 0), (bias, offset, place[0], 0)]
    for r in range(shards):
        everything.append((xbc.at[count - 16 :], tail, (shard ^ r) * PAIR + core, r * size))
    for source, target, group, to in everything:
        copies.append((source.at[:, channels(group, 0, PER_GROUP)], target.at[:, to : to + PER_GROUP]))
        for i in range(2):
            at = ds(INNER + (i * GROUPS + group) * STATE, STATE)
            start = to + PER_GROUP + i * STATE
            copies.append((source.at[:, at], target.at[:, start : start + STATE]))
    for copy in run(copies, sems):
        copy.wait()


def put_edge(shards, place, got, tail, out):
    count = got.shape[0]
    first = WIDTHS[0]
    size = PER_GROUP + 2 * STATE
    for r in range(shards):
        theirs = [got[count - 16 :, r * first : (r + 1) * first]]
        theirs.append(got[16 * r : 16 * r + 16, shards * first :])
        to = r * size
        for part in theirs:
            at = slice(to, to + part.shape[1])
            rows = jnp.where(place[2] == 0, part.astype(F32), tail[:, at].astype(F32))
            out[:, at] = rows[13:16].astype(BF16)
            to = at.stop


def total_of(piece):
    return WIDTHS[piece] + sum(LANES if kind == "D" else STATE for kind in RESTS[piece])


def merge_kernel(shards, plan, unread, place, xbc, dt_raw, got_first, got, edges, *refs):
    refs = refs[unread:]
    outs, sems = refs[: len(plan)], refs[-1]
    core, shard = place[2], place[4]
    count = xbc.shape[0]
    stride = PER_GROUP - WIDTHS[0]
    mine = pl.ds(pl.multiple_of(core * count, count), count)
    other = pl.ds(pl.multiple_of((1 - core) * count, count), count)
    copies, steps = [], []
    for out, (r, pieces) in zip(outs, plan):
        group = (shard ^ r) * PAIR + core
        to = 0
        for piece in pieces:
            first, width = sum(WIDTHS[:piece]), WIDTHS[piece]
            if piece == 0:
                source = got_first.at[:, r * width : (r + 1) * width]
            else:
                at = r * stride + first - WIDTHS[0]
                source = got.at[:, at : at + width]
            if width:
                copies.append((xbc.at[:, channels(group, first, width)], out.at[mine, to : to + width]))
                copies.append((source, out.at[other, to : to + width]))
            to += width
            for kind in RESTS[piece]:
                if kind == "D":
                    steps.append((out, r, to))
                    to += LANES
                    continue
                i = "BC".index(kind)
                at = ds(INNER + (i * GROUPS + group) * STATE, STATE)
                copies.append((xbc.at[:, at], out.at[mine, to : to + STATE]))
                at = stride * shards + (i * shards + r) * STATE
                copies.append((got.at[:, at : at + STATE], out.at[other, to : to + STATE]))
                to += STATE
    started = run(copies, sems)
    if len(refs) > len(plan) + 1:
        put_edge(shards, place, got_first, edges, refs[-2])
    if steps:
        lane = lax.broadcasted_iota(jnp.int32, (count, LANES), 1)
        per_tile = LANES * GROUPS // HEADS
        heads = HEADS // GROUPS
        for out, r, to in steps:
            group = (shard ^ r) * PAIR + core
            tile, shift = group // per_tile, (LANES - (group % per_tile) * heads) % LANES
            own = dt_raw[:, ds(tile * LANES, LANES)].astype(F32)
            theirs = got[:, ds(got.shape[1] - HEADS + tile * LANES, LANES)].astype(F32)
            low = jnp.where(core == 0, own, theirs)
            high = jnp.where(core == 0, theirs, own)
            packed = jnp.zeros((count // 2, LANES), F32)
            for j, rows in enumerate((low, high)):
                rows = jnp.where(lane < heads, pltpu.roll(rows, shift, 1), 0.0)
                for i in range(2):
                    part = rows[i * count // 2 : (i + 1) * count // 2]
                    packed = packed + pltpu.roll(part, (2 * j + i) * heads, 1)
            out[: count // 2, to : to + LANES] = packed.astype(BF16)
            size = PER_GROUP + 2 * STATE
            at = slice(r * size, (r + 1) * size)
            edge = jnp.concatenate([edges[:, at].astype(F32), jnp.zeros((1, size), F32)], 0)
            edge = jnp.concatenate([edge[:, q * LANES : (q + 1) * LANES] for q in range(size // LANES)], 0)
            fill = jnp.zeros((PAIR * count - count // 2 - edge.shape[0], LANES), F32)
            out[count // 2 :, to : to + LANES] = jnp.concatenate([edge, fill], 0).astype(BF16)
    for copy in started:
        copy.wait()


def convolve_in_order(place, blocks, columns, edge, tap, bias, wide, put):
    width = columns.stop - columns.start
    count = blocks[0].shape[0] // PAIR
    wide[5:8, :width] = edge
    for r, block in enumerate(blocks):
        for core in range(PAIR):
            at = pl.multiple_of((core * len(blocks) + (place[4] ^ r)) * count + 8, 8)
            part = block[core * count : (core + 1) * count, columns]
            wide[pl.ds(at, count), :width] = part.astype(F32)
    tap, bias = tap * 0.5, bias * 0.5
    for start in range(0, PAIR * len(blocks) * count, count):
        acc = bias + tap[0:1] * wide[start + 5 : start + 5 + count, :width]
        acc = acc + tap[1:2] * wide[start + 6 : start + 6 + count, :width]
        acc = acc + tap[2:3] * wide[start + 7 : start + 7 + count, :width]
        acc = acc + tap[3:4] * wide[start + 8 : start + 8 + count, :width]
        put(start, count, (acc + acc * jnp.tanh(acc)).astype(BF16))


def prep_kernel(shards, place, *refs):
    blocks, (taps, offset, a_ref, bias_ref, skip_ref, order) = refs[:shards], refs[shards : shards + 6]
    b_ref, edge_ref, cum_ref, row_ref, factor_ref, tail_ref, skip_out, dt_ref, wide = refs[shards + 6 :]
    start = WIDTHS[1]
    last = total_of(1) - LANES
    size = edge_ref.shape[1]
    count = blocks[0].shape[0] // PAIR
    half, heads = count // 2, HEADS // GROUPS
    columns = [block[:, last : last + LANES].astype(F32) for block in blocks]
    edge = columns[0][half : half + 4 * size // LANES]
    for column in columns[1:]:
        edge = edge + column[half : half + 4 * size // LANES]
    for q in range(size // LANES):
        edge_ref[:, q * LANES : (q + 1) * LANES] = edge[4 * q : 4 * q + 4]
    for r, column in enumerate(columns):
        packed = column[:half]
        for j in range(2 * PAIR):
            at = ((j // 2) * shards + (place[4] ^ r)) * count + (j % 2) * half
            rows = packed if j == 0 else pltpu.roll(packed, LANES - j * heads, 1)
            dt_ref[pl.ds(pl.multiple_of(at, half), half), :] = rows

    def put(start, count, value):
        b_ref[start : start + count] = value

    at = slice(PER_GROUP, PER_GROUP + STATE)
    convolve_in_order(
        place, blocks, slice(start, start + STATE), edge_ref[0:3, at], taps[:, at], offset[:, at], wide, put
    )
    per_tile = LANES * GROUPS // HEADS
    group = place[0]
    tile = group // per_tile
    shift = (LANES - (group % per_tile) * heads) % LANES

    def lanes_of(ref):
        return pltpu.roll(jnp.broadcast_to(ref[pl.ds(tile, 1), :], (8, LANES)), shift, 1)

    rate = -jnp.exp(lanes_of(a_ref)[0:1])
    raw = dt_ref[...] + lanes_of(bias_ref)[0:1]
    step = jnp.maximum(raw, 0.0) + jnp.log1p(jnp.exp(-jnp.abs(raw)))
    skip = lanes_of(skip_ref)
    skip_out[...] = jnp.concatenate(halves(jnp.concatenate([skip, skip], 0), 3), 1)
    lower = (
        lax.broadcasted_iota(jnp.int32, (BLOCK, BLOCK), 0)
        >= lax.broadcasted_iota(jnp.int32, (BLOCK, BLOCK), 1)
    ).astype(BF16)
    valid = lax.broadcasted_iota(jnp.int32, (BLOCK, LANES), 1) < heads
    for block in range(PAIR):
        at = slice(block * BLOCK, (block + 1) * BLOCK)
        here = jnp.where(valid, step[at], 1.0)
        parts = halves(here * rate, 3)
        cum = dot(lower, parts[0]) + (dot(lower, parts[1]) + dot(lower, parts[2]))
        cum = cum * LOG2E
        cum_ref[at] = cum
        row_ref[:, at] = jnp.transpose(cum - jnp.log2(here))
        factor_ref[at] = jnp.concatenate(halves(jnp.exp2(cum), 2), 1)
        tail = jnp.exp2(cum[BLOCK - 1 :] - cum) * here
        tail_ref[at] = jnp.concatenate(halves(tail, 2), 1)


def score_kernel(shards, place, *refs):
    blocks, refs = refs[:shards], refs[shards:]
    taps, offset, edge_ref, b_ref, c_ref, score_ref, wide = (*refs[:4], *refs[-3:])
    start = WIDTHS[3]
    at = slice(PER_GROUP + STATE, PER_GROUP + 2 * STATE)

    def put(start, count, value):
        c_ref[start : start + count] = value

    convolve_in_order(
        place, blocks, slice(start, start + STATE), edge_ref[0:3, at], taps[:, at], offset[:, at], wide, put
    )
    for block in range(PAIR):
        at = slice(block * BLOCK, (block + 1) * BLOCK)
        score_ref[at] = lax.dot_general(
            c_ref[at], b_ref[at], (((1,), (1,)), ((), ())), preferred_element_type=F32
        )


def decay_of(ref):
    decay = ref[STATE : STATE + 16].astype(F32)
    return decay[0:1] + (decay[1:2] + decay[2:3])


def put_decay(ref, decay):
    row = lax.broadcasted_iota(jnp.int32, (16, ref.shape[1]), 0)
    high, middle, low = (part.astype(F32) for part in halves(decay, 3))
    packed = jnp.where(row == 0, high, jnp.where(row == 1, middle, jnp.where(row == 2, low, 0.0)))
    ref[STATE:] = packed.astype(BF16)


def state_kernel(shards, part, sizes, place, *refs):
    blocks, refs = refs[:shards], refs[shards:]
    taps, offset, edge_ref, b_ref, factor_ref, tail_ref = refs[:6]
    x_ref, own_ref, *sends, wide = refs[-3 - len(sizes) :]
    piece, start, width = part
    first = sum(WIDTHS[:piece]) + start
    at = slice(first, first + width)

    def put(row, count, value):
        x_ref[row : row + count] = value

    columns = slice(start, start + width)
    convolve_in_order(place, blocks, columns, edge_ref[0:3, at], taps[:, at], offset[:, at], wide, put)
    expand = spread(first // HEAD_DIM, width, 2)
    both = []
    for block in range(PAIR):
        at = slice(block * BLOCK, (block + 1) * BLOCK)
        loaded = (x_ref[at].astype(F32) * dot(tail_ref[at], expand)).astype(BF16)
        both.append(
            lax.dot_general(b_ref[at], loaded, (((0,), (0,)), ((), ())), preferred_element_type=F32)
        )
    ends = [dot(factor_ref[(i + 1) * BLOCK - 16 : (i + 1) * BLOCK], expand)[15:16] for i in range(PAIR)]
    own_ref[...] = both[0]
    end = (ends[1] * both[0] + both[1]).astype(BF16)
    decay = ends[0] * ends[1]
    start = 0
    for send_ref in sends:
        at = slice(start, start + send_ref.shape[1])
        send_ref[0:STATE] = end[:, at]
        put_decay(send_ref, decay[:, at])
        start = at.stop


def combine_kernel(count, *refs):
    early, late, out_ref = refs[:count], refs[count : 2 * count], refs[-1]
    start = 0
    for early_ref, late_ref in zip(early, late):
        at = slice(start, start + late_ref.shape[1])
        decay = decay_of(late_ref)
        total = decay * early_ref[:STATE].astype(F32) + late_ref[:STATE].astype(F32)
        out_ref[:STATE, at] = total.astype(BF16)
        put_decay(out_ref.at[:, at], decay * decay_of(early_ref))
        start = at.stop


def mix(first_head, x_ref, cum_ref, row_ref, score_ref, skip_ref, put):
    width = x_ref.shape[1]
    half = BLOCK // 2
    expand = spread(first_head, width, 3)
    skip = dot(skip_ref[...], expand)[0:1]
    lower = lax.broadcasted_iota(jnp.int32, (half, half), 0) >= lax.broadcasted_iota(
        jnp.int32, (half, half), 1
    )
    lane = lax.broadcasted_iota(jnp.int32, (BLOCK, LANES), 1)
    for block in range(PAIR):
        base = block * BLOCK
        for tile in range(width // LANES):
            columns = slice(tile * LANES, (tile + 1) * LANES)
            x = x_ref[base : base + BLOCK, columns]
            top = skip[:, columns] * x[:half].astype(F32)
            bottom = skip[:, columns] * x[half:].astype(F32)
            for side in range(LANES // HEAD_DIM):
                head = first_head + tile * (LANES // HEAD_DIM) + side
                own = jnp.where(lane // HEAD_DIM == side, x, jnp.zeros_like(x))
                cum = cum_ref[base : base + BLOCK, head : head + 1]
                row = row_ref[head : head + 1, base : base + BLOCK]
                diag = jnp.where(lower, cum[:half] - row[:, :half], -1e30)
                mixing = jnp.exp2(diag) * score_ref[base : base + half, :half]
                top = top + dot(mixing.astype(BF16), own[:half])
                left = jnp.exp2(cum[half:] - row[:, :half]) * score_ref[base + half : base + BLOCK, :half]
                diag = jnp.where(lower, cum[half:] - row[:, half:], -1e30)
                right = jnp.exp2(diag) * score_ref[base + half : base + BLOCK, half:]
                mixing = jnp.concatenate([left.astype(BF16), right.astype(BF16)], 1)
                bottom = bottom + dot(mixing, own)
            put(block, slice(base, base + half), columns, top)
            put(block, slice(base + half, base + BLOCK), columns, bottom)


def local_kernel(first_head, x_ref, cum_ref, row_ref, score_ref, skip_ref, *refs):
    out_ref = refs[-1]

    def put(block, rows, columns, value):
        out_ref[rows, columns] = value

    mix(first_head, x_ref, cum_ref, row_ref, score_ref, skip_ref, put)


def carry(first_head, core, lasts, befores, own_ref, c_ref, factor_ref, add, keep_ref, send_ref):
    expand = spread(first_head, own_ref.shape[1], 2)
    last, before = (
        refs[0][...] if len(refs) == 1 else jnp.concatenate([ref[...] for ref in refs], 1)
        for refs in (lasts, befores)
    )
    held = last[:STATE].astype(F32) + decay_of(last) * before[:STATE].astype(F32)
    factor = dot(factor_ref[...], expand)
    outs = []
    for block in range(PAIR):
        at = slice(block * BLOCK, (block + 1) * BLOCK)
        carried = dot(c_ref[at], held.astype(BF16))
        outs.append((add[at] + factor[at] * carried).astype(BF16))
        held = factor[BLOCK - 1 : BLOCK] * held + own_ref[...]

    @pl.when(core == 0)
    def _():
        keep_ref[...] = outs[0]
        send_ref[...] = outs[1]

    @pl.when(core == 1)
    def _():
        keep_ref[...] = outs[1]
        send_ref[...] = outs[0]


def final_kernel(first_head, lasts, befores, place, *refs):
    last, refs = refs[:lasts], refs[lasts:]
    before, refs = refs[:befores], refs[befores:]
    carry(first_head, place[2], last, before, *refs[:4], *refs[-2:])


def finish_kernel(first_head, lasts, befores, place, *refs):
    last, refs = refs[:lasts], refs[lasts:]
    before, refs = refs[:befores], refs[befores:]
    own_ref, c_ref, factor_ref = refs[:3]
    keep_ref, send_ref, partial = refs[-3:]
    local_kernel(first_head, *refs[3:8], partial)
    carry(first_head, place[2], last, before, own_ref, c_ref, factor_ref, partial, keep_ref, send_ref)


def place_kernel(first, place, keep, got, *refs):
    out, sems = refs[-2:]
    core = place[2]
    width = keep.shape[1]
    half = out.shape[1] // PAIR
    copies = [
        (keep, out.at[:, ds(core * half + first, width)]),
        (got, out.at[:, ds((1 - core) * half + first, width)]),
    ]
    for copy in run(copies, sems):
        copy.wait()


def put_in_place(first, shape, place, keep, got, before):
    smem, vmem, hbm = (pl.BlockSpec(memory_space=m) for m in (pltpu.SMEM, pltpu.VMEM, pltpu.HBM))
    return pl.pallas_call(
        functools.partial(place_kernel, first),
        out_shape=jax.ShapeDtypeStruct(shape, BF16),
        in_specs=[smem, vmem, vmem] + [hbm] * len(before),
        out_specs=hbm,
        input_output_aliases={3: 0} if before else {},
        scratch_shapes=[pltpu.SemaphoreType.DMA((2,))],
        compiler_params=pltpu.CompilerParams(vmem_limit_bytes=16 << 20),
        cost_estimate=pl.CostEstimate(flops=1, bytes_accessed=1, transcendentals=0),
        name="place",
    )(place, keep, got, *before)


class Stay:
    def __init__(self, array):
        self.array = array


def call(body, outs, operands, scratch=(), flops=0, transcendentals=0, name=None, limit=16 << 20):
    shapes = [jax.ShapeDtypeStruct(shape, dtype) for shape, dtype in outs]
    smem, vmem, hbm = (pl.BlockSpec(memory_space=m) for m in (pltpu.SMEM, pltpu.VMEM, pltpu.HBM))
    specs = [
        hbm if isinstance(o, Stay) else smem if o.dtype == jnp.int32 else vmem for o in operands
    ]
    moved = sum(o.size * o.dtype.itemsize for o in shapes) * 2
    return pl.pallas_call(
        body,
        out_shape=shapes,
        in_specs=specs,
        out_specs=[vmem] * len(outs),
        scratch_shapes=scratch,
        compiler_params=pltpu.CompilerParams(vmem_limit_bytes=limit),
        cost_estimate=pl.CostEstimate(flops=1, bytes_accessed=1, transcendentals=0),
        name=name,
    )(*[o.array if isinstance(o, Stay) else o for o in operands])


def paired(xbc, dt_raw, conv_weight, conv_bias, a_log, dt_bias, skip_gain):
    axes = ("ctx", "head")
    shards, length = lax.axis_size("head"), lax.axis_size("ctx")
    devices, peers = shards * length, shards * PAIR
    tok = xbc.shape[0]
    slab = tok * peers
    context, shard = lax.axis_index("ctx"), lax.axis_index("head")
    pair, core = context // PAIR, context % PAIR
    group = shard * PAIR + core
    place = jnp.stack([group, pair, core, core * shards + shard, shard]).astype(jnp.int32)

    def over(block, target):
        route = [(i, target(i)) for i in range(devices)]
        return lax.ppermute(block, axes, [(i, j) for i, j in route if j is not None and j < devices])

    def swap(block):
        return over(block, lambda i: i ^ shards)

    rows = Stay(xbc)
    size = PER_GROUP + 2 * STATE
    (sent,) = call(
        functools.partial(pack_first_kernel, shards),
        [((tok, shards * WIDTHS[0] + size - WIDTHS[0]), BF16)],
        [place, rows],
        scratch=[pltpu.SemaphoreType.DMA((4 * shards,))],
        name="pack_first",
        limit=None,
    )
    got_first = swap(sent)
    sent, taps, offset, tail = call(
        functools.partial(pack_kernel, shards),
        [
            ((tok, shards * (size - WIDTHS[0]) + HEADS), BF16),
            ((4, size), F32),
            ((1, size), F32),
            ((16, shards * size), BF16),
        ],
        [place, rows, Stay(dt_raw), Stay(conv_weight), Stay(conv_bias[None]), Stay(sent)],
        scratch=[pltpu.SemaphoreType.DMA((6 * shards + 7,))],
        name="pack",
        limit=None,
    )
    got_rest = swap(sent)

    def send_on(piece, order, edges=None):
        unused = Stay(got_first)
        plan = [(r, (piece,)) for r in range(shards)]
        made = [((3, shards * size), BF16)] if piece == 0 else []
        return call(
            functools.partial(merge_kernel, shards, plan, len(order)),
            [((PAIR * tok, total_of(piece)), BF16)] * shards + made,
            [
                place,
                rows,
                dt_raw if piece == 1 else Stay(dt_raw),
                got_first if piece == 0 else unused,
                unused if piece == 0 else got_rest,
                unused if edges is None else edges,
            ]
            + [Stay(o) for o in order],
            scratch=[pltpu.SemaphoreType.DMA((2 * shards * (1 + len(RESTS[piece])),))],
            name="merge",
        )

    def travel(blocks):
        got = [blocks[0]]
        for r in range(1, shards):
            got.append(over(blocks[r], lambda i, r=r: i ^ r))
        return got

    *first_blocks, edges = send_on(0, [], tail)
    message = {0: travel(first_blocks)}
    edges = over(edges, lambda i: i + peers if i % shards == shards - 1 else None)
    second_blocks = send_on(1, [first_blocks[0], message[0][1]], edges)
    message[1] = travel(second_blocks)
    third_blocks = send_on(2, [second_blocks[0], *message[0][2:]])
    message[2] = travel(third_blocks)

    tiles = [p.reshape(HEADS // LANES, LANES) for p in (a_log, dt_bias, skip_gain)]
    b, edge, cum, row, factor, tail, skip = call(
        functools.partial(prep_kernel, shards),
        [
            ((slab, STATE), BF16),
            ((4, size), F32),
            ((slab, LANES), F32),
            ((LANES, slab), F32),
            ((slab, 2 * LANES), BF16),
            ((slab, 2 * LANES), BF16),
            ((16, 3 * LANES), BF16),
        ],
        [place] + message[1] + [taps, offset] + tiles + [Stay(third_blocks[0])],
        scratch=[pltpu.VMEM((slab, LANES), F32), pltpu.VMEM((slab + 8, STATE), F32)],
        name="prep",
    )
    count = len(GROUPED)
    x, sent, own, last, joined, before, keep, send = ([None] * count for _ in range(8))

    def first_head(i):
        return (sum(WIDTHS[: GROUPED[i][0]]) + GROUPED[i][1]) // HEAD_DIM

    def state_of(i, order):
        piece, _, width = GROUPED[i]
        x[i], own[i], *sent[i] = call(
            functools.partial(state_kernel, shards, GROUPED[i], FIRST_ROUND[i]),
            [((slab, width), BF16), ((STATE, width), F32)] + [((STATE + 16, w), BF16) for w in FIRST_ROUND[i]],
            [place] + message[piece] + [taps, offset, edge, b, factor, tail] + [Stay(o) for o in order],
            scratch=[pltpu.VMEM((slab + 8, width), F32)],
            name="state",
        )
        last[i] = [over(part, lambda i: i + peers) for part in sent[i]]

    def combine_of(i, order):
        joined[i], before[i] = [], []
        step = len(FIRST_ROUND[i]) // len(SECOND_ROUND[i])
        for j, width in enumerate(SECOND_ROUND[i]):
            early, late = last[i][j * step : (j + 1) * step], sent[i][j * step : (j + 1) * step]
            (total,) = call(
                functools.partial(combine_kernel, len(early)),
                [((STATE + 16, width), BF16)],
                early + late + [Stay(o) for o in order],
                name="combine",
            )
            joined[i].append(total)
            before[i].append(over(total, lambda i: i + 2 * peers))
            order = [total]

    def finish_of(body, i, operands, order, **more):
        keep[i], send[i] = call(
            functools.partial(body, first_head(i), len(last[i]), len(before[i])),
            [((BLOCK, GROUPED[i][2]), BF16)] * 2,
            [place, *last[i], *before[i], own[i], c, factor] + operands + [Stay(o) for o in order],
            name="final",
            **more,
        )

    state_of(0, [])
    combine_of(0, [])
    fourth_blocks = send_on(3, [joined[0][0]])
    message[3] = travel(fourth_blocks)
    state_of(1, [fourth_blocks[0]])
    combine_of(1, [])
    state_of(2, joined[1])
    state_of(3, sent[2])
    c, score = call(
        functools.partial(score_kernel, shards),
        [((slab, STATE), BF16), ((slab, BLOCK), F32)],
        [place] + message[3] + [taps, offset, edge, b] + [Stay(o) for o in sent[3] + before[1]],
        scratch=[pltpu.VMEM((slab + 8, STATE), F32)],
        name="score",
    )
    mixes = [cum, row, score, skip]

    def in_full(i, order):
        wide = [pltpu.VMEM((slab, GROUPED[i][2]), F32)]
        finish_of(finish_kernel, i, [x[i]] + mixes, order, scratch=wide)

    in_full(1, [score])
    combine_of(2, [keep[1]])
    combine_of(3, joined[2])
    order, partial = joined[3][0], {}
    for i in (2, 3):
        (partial[i],) = call(
            functools.partial(local_kernel, first_head(i)),
            [(x[i].shape, F32)],
            [x[i]] + mixes + [Stay(order)],
            name="local",
        )
        order = partial[i]
    in_full(0, [order])
    order = keep[0]
    for i in (2, 3):
        finish_of(final_kernel, i, [partial[i]], [order])
        order = keep[i]
    out = []
    for i in range(count):
        shape = (BLOCK, PAIR * PER_GROUP)
        out = [put_in_place(first_head(i) * HEAD_DIM, shape, place, keep[i], swap(send[i]), out)]
    return out[0]


def solution(mesh):
    in_specs = (P(("ctx", "head"), None), P(("ctx", "head"), None), P(), P(), P(), P(), P())
    out_specs = P("ctx", "head")
    shards, length = mesh.shape["head"], mesh.shape["ctx"]

    def program(xbc, *rest):
        slab = xbc.shape[0] // length
        fits = shards == GROUPS // PAIR and length == 4 * PAIR and slab == BLOCK
        return jax.shard_map(
            paired if fits else on_device,
            mesh=mesh,
            in_specs=in_specs,
            out_specs=out_specs,
            check_vma=False,
        )(xbc, *rest)

    return program
```

```python
import functools

import jax
import jax.numpy as jnp
from jax import lax
from jax.experimental import pallas as pl
from jax.experimental.pallas import tpu as pltpu
from jax.sharding import PartitionSpec as P

HEADS = 256
HEAD_DIM = 64
STATE = 256
GROUPS = 8
BLOCK = 256


def from_behind(block, axis, distance):
    devices = range(lax.axis_size(axis))
    route = [(i - distance, i) for i in devices if i - distance in devices]
    return lax.ppermute(block, axis, route)


def carried_in(array, axis, combine, identity):
    length, index = (lax.axis_size(axis), lax.axis_index(axis))
    everything = jax.tree.map(lambda part: lax.all_gather(part, axis), array)
    start = jax.tree.map(
        lambda part, zero: jnp.broadcast_to(jnp.asarray(zero, part.dtype), part.shape),
        array,
        identity,
    )

    def hop(k, before):
        reached = k < index
        new = combine(before, jax.tree.map(lambda part: part[k], everything))
        return jax.tree.map(lambda a, b: jnp.where(reached, a, b), new, before)

    return lax.fori_loop(0, length, hop, start)


def convolve(rows, edge, weight, bias):
    count = rows.shape[0]
    wide = jnp.concatenate([edge, rows], 0).astype(jnp.float32)
    acc = bias[None, :] + weight[0] * wide[0:count]
    acc = acc + weight[1] * wide[1 : count + 1]
    acc = acc + weight[2] * wide[2 : count + 2]
    acc = acc + weight[3] * wide[3 : count + 3]
    return jax.nn.silu(acc).astype(jnp.bfloat16)


def rearrange_heads(rows, shards, per_dev, groups_dev, per_group):
    count = rows.shape[0]
    inner = HEADS * HEAD_DIM
    replicate_groups = max(1, per_group // per_dev)
    heads_part = rows[:, :inner].reshape(count, shards, per_dev * HEAD_DIM)
    b_part = rows[:, inner : inner + GROUPS * STATE].reshape(count, GROUPS, STATE)
    c_part = rows[:, inner + GROUPS * STATE :].reshape(count, GROUPS, STATE)
    b_part = jnp.repeat(b_part, replicate_groups, axis=1).reshape(count, shards, groups_dev * STATE)
    c_part = jnp.repeat(c_part, replicate_groups, axis=1).reshape(count, shards, groups_dev * STATE)
    return jnp.concatenate([heads_part, b_part, c_part], axis=2)


def inner_block(xs, bmat, cmat, steps, cum):
    size = xs.shape[0]
    lower = jnp.arange(size)[:, None] >= jnp.arange(size)[None, :]
    scores = jnp.einsum("qgn,kgn->gqk", cmat, bmat, preferred_element_type=jnp.float32)
    order = jnp.transpose(cum, (1, 2, 0))
    gap = order[..., :, None] - order[..., None, :]
    decay = jnp.exp(jnp.where(lower, gap, -jnp.inf))
    mixing = (scores[:, None] * decay * jnp.transpose(steps, (1, 2, 0))[..., None, :]).astype(
        jnp.bfloat16
    )
    local = jnp.einsum("gjqk,kgjp->qgjp", mixing, xs, preferred_element_type=jnp.float32)
    tail = jnp.exp(cum[size - 1][None] - cum) * steps
    loaded = (bmat[:, :, None, :].astype(jnp.float32) * tail[..., None]).astype(jnp.bfloat16)
    block_state = jnp.einsum("kgjn,kgjp->gjnp", loaded, xs, preferred_element_type=jnp.float32)
    return (local, block_state)


def on_device(xbc, dt_raw, conv_weight, conv_bias, a_log, dt_bias, skip_gain):
    tok = xbc.shape[0]
    shards = lax.axis_size("head")
    per_dev = HEADS // shards
    per_group = HEADS // GROUPS
    groups_dev = max(1, per_dev // per_group)
    heads_per_cluster = per_dev // groups_dev
    sent = rearrange_heads(xbc, shards, per_dev, groups_dev, per_group)
    mine, rates = (
        lax.all_to_all(sent, "head", split_axis=1, concat_axis=0, tiled=True),
        lax.all_to_all(
            dt_raw.reshape(tok, shards, per_dev), "head", split_axis=1, concat_axis=0, tiled=True
        ),
    )
    slab = tok * shards
    mine = mine.reshape(slab, mine.shape[2])
    rates = rates.reshape(slab, per_dev)
    shard = lax.axis_index("head")
    taps = lax.dynamic_index_in_dim(
        rearrange_heads(conv_weight, shards, per_dev, groups_dev, per_group),
        shard,
        1,
        keepdims=False,
    )
    offset = lax.dynamic_index_in_dim(
        rearrange_heads(conv_bias[None, :], shards, per_dev, groups_dev, per_group),
        shard,
        1,
        keepdims=False,
    )
    edge = from_behind(mine[slab - 3 :], "ctx", 1)
    mine = convolve(mine, edge, taps, offset[0])
    nchunk = slab // BLOCK
    width = per_dev * HEAD_DIM
    xs = mine[:, :width].reshape(nchunk, BLOCK, groups_dev, heads_per_cluster, HEAD_DIM)
    bmat = mine[:, width : width + groups_dev * STATE].reshape(nchunk, BLOCK, groups_dev, STATE)
    cmat = mine[:, width + groups_dev * STATE :].reshape(nchunk, BLOCK, groups_dev, STATE)
    first = shard * per_dev
    rate = (-jnp.exp(lax.dynamic_slice_in_dim(a_log, first, per_dev))).reshape(
        groups_dev, heads_per_cluster
    )
    bias_dt = lax.dynamic_slice_in_dim(dt_bias, first, per_dev).reshape(
        groups_dev, heads_per_cluster
    )
    skip = lax.dynamic_slice_in_dim(skip_gain, first, per_dev).reshape(
        groups_dev, heads_per_cluster
    )
    steps = jax.nn.softplus(
        rates.astype(jnp.float32).reshape(nchunk, BLOCK, groups_dev, heads_per_cluster) + bias_dt
    )
    cum = jnp.cumsum(steps * rate, axis=1)

    def block_step(carry, item):
        held, product = carry
        x_part, b_part, c_part, step_part, cum_part = item
        local, block_state = inner_block(x_part, b_part, c_part, step_part, cum_part)
        lifted = c_part.astype(jnp.float32)[:, :, None, :] * jnp.exp(cum_part)[..., None]
        carried = jnp.einsum("qgjn,gjnp->qgjp", lifted, held, precision=lax.Precision.HIGHEST)
        partial_out = local + carried + skip[..., None] * x_part.astype(jnp.float32)
        end = jnp.exp(cum_part[BLOCK - 1])
        return ((end[..., None, None] * held + block_state, product * end), (partial_out, product))

    zero_state = jnp.zeros((groups_dev, heads_per_cluster, STATE, HEAD_DIM), jnp.float32)
    unit = jnp.ones((groups_dev, heads_per_cluster), jnp.float32)
    (slab_state, slab_decay), (partials, product_in) = lax.scan(
        block_step, (zero_state, unit), (xs, bmat, cmat, steps, cum)
    )

    def combine(preceding_state, later):
        return (
            preceding_state[0] * later[0],
            later[0][..., None, None] * preceding_state[1] + later[1],
        )

    _, entering = carried_in((slab_decay, slab_state), "ctx", combine, (unit, zero_state))
    projected = jnp.einsum(
        "cqgn,gjnp->cqgjp", cmat.astype(jnp.float32), entering, precision=lax.Precision.HIGHEST
    )
    factor = jnp.exp(cum) * product_in[:, None]
    total = partials + factor[..., None] * projected
    return total.astype(jnp.bfloat16).reshape(slab, width)


PAIR = 2
LANES = 128
LOG2E = 1.4426950408889634
F32, BF16 = jnp.float32, jnp.bfloat16
WIDTHS = (768, 1280)
RESTS = ("BCD", "")
GROUPED = ((0, 0, 768), (1, 0, 512), (1, 512, 384), (1, 896, 384))
ROUNDS = ((256, 256, 256), (512,), (384,), (384,))


def halves(value, count):
    parts = []
    for _ in range(count):
        part = value.astype(BF16)
        parts.append(part)
        value = value - part.astype(F32)
    return parts


def spread(first_head, width, copies):
    lane = lax.broadcasted_iota(jnp.int32, (copies * LANES, width), 0) % LANES
    column = lax.broadcasted_iota(jnp.int32, (copies * LANES, width), 1)
    return (lane == first_head + column // HEAD_DIM).astype(BF16)


def dot(a, b):
    return jnp.dot(a, b, preferred_element_type=F32)


def ds(start, width):
    return pl.ds(pl.multiple_of(start, LANES), width)


def run(copies, sems):
    started = []
    for i, (source, target) in enumerate(copies):
        copy = pltpu.make_async_copy(source, target, sems.at[i])
        copy.start()
        started.append(copy)
    return started


PER_GROUP = HEADS * HEAD_DIM // GROUPS
INNER = HEADS * HEAD_DIM


def channels(group, first, width):
    return ds(group * PER_GROUP + first, width)


def runs(group):
    yield group * PER_GROUP, PER_GROUP
    yield INNER + group * STATE, STATE
    yield INNER + (GROUPS + group) * STATE, STATE


def pack_kernel(shards, place, xbc, dt_raw, send, near, far, tail, sems):
    core, shard = place[2], place[4]
    count = xbc.shape[0]
    copies = [(xbc.at[count - 16 :], tail)]
    to = 0
    for r in range(shards):
        for start, width in runs((shard ^ r) * PAIR + 1 - core):
            copies.append((xbc.at[:, ds(start, width)], send.at[:, to : to + width]))
            to += width
    copies.append((dt_raw, send.at[:, to:]))
    started = run(copies, sems)
    started[0].wait()
    for edge, side in ((near, 1), (far, 0)):
        to = 0
        for r in range(shards):
            for start, width in runs(((shards - 1) ^ r) * PAIR + side):
                rows = tail[:, start : start + width].astype(F32)
                edge[:, to : to + width] = rows[13:16].astype(BF16)
                to += width
    for copy in started[1:]:
        copy.wait()


def taps_kernel(place, weight, bias, order, taps, offset, sems):
    copies, to = [], 0
    for start, width in runs(place[0]):
        copies.append((weight.at[:, ds(start, width)], taps.at[:, to : to + width]))
        copies.append((bias.at[:, ds(start, width)], offset.at[:, to : to + width]))
        to += width
    for copy in run(copies, sems):
        copy.wait()


def total_of(piece):
    return WIDTHS[piece] + sum(LANES if kind == "D" else STATE for kind in RESTS[piece])


def view(refs, piece):
    origin = sum(map(total_of, range(piece)))
    return [(ref, origin if r < 2 else 0) for r, ref in enumerate(refs)]


def merge_kernel(shards, plan, unread, place, xbc, dt_raw, got, near, far, *refs):
    refs = refs[unread:]
    outs, sems = refs[: len(plan)], refs[len(plan)]
    core, shard = place[2], place[4]
    count = xbc.shape[0]
    size = PER_GROUP + 2 * STATE
    mine = pl.ds(pl.multiple_of(core * count, count), count)
    other = pl.ds(pl.multiple_of((1 - core) * count, count), count)
    copies, steps = [], []
    for out, (r, pieces) in zip(outs, plan):
        group = (shard ^ r) * PAIR + core
        to = 0
        for piece in pieces:
            first, width = sum(WIDTHS[:piece]), WIDTHS[piece]
            parts = [(group * PER_GROUP + first, r * size + first, width)]
            for i, kind in enumerate("BC"):
                if kind in RESTS[piece]:
                    at = INNER + (i * GROUPS + group) * STATE
                    parts.append((at, r * size + PER_GROUP + i * STATE, STATE))
            for own, theirs, width in parts:
                copies.append((xbc.at[:, ds(own, width)], out.at[mine, to : to + width]))
                copies.append((got.at[:, theirs : theirs + width], out.at[other, to : to + width]))
                to += width
            if "D" in RESTS[piece]:
                steps.append((out, r, to))
                to += LANES
    started = run(copies, sems)
    if steps:
        lane = lax.broadcasted_iota(jnp.int32, (count, LANES), 1)
        per_tile = LANES * GROUPS // HEADS
        heads = HEADS // GROUPS
        for out, r, to in steps:
            group = (shard ^ r) * PAIR + core
            tile, shift = group // per_tile, (LANES - (group % per_tile) * heads) % LANES
            own = dt_raw[:, ds(tile * LANES, LANES)].astype(F32)
            theirs = got[:, ds(got.shape[1] - HEADS + tile * LANES, LANES)].astype(F32)
            low = jnp.where(core == 0, own, theirs)
            high = jnp.where(core == 0, theirs, own)
            packed = jnp.zeros((count // 2, LANES), F32)
            for j, rows in enumerate((low, high)):
                rows = jnp.where(lane < heads, pltpu.roll(rows, shift, 1), 0.0)
                for i in range(2):
                    part = rows[i * count // 2 : (i + 1) * count // 2]
                    packed = packed + pltpu.roll(part, (2 * j + i) * heads, 1)
            out[: count // 2, to : to + LANES] = packed.astype(BF16)
            size = PER_GROUP + 2 * STATE
            at = slice(r * size, (r + 1) * size)
            edge = near[:, at].astype(F32) + far[:, at].astype(F32)
            edge = jnp.concatenate([edge, jnp.zeros((1, size), F32)], 0)
            edge = jnp.concatenate([edge[:, q * LANES : (q + 1) * LANES] for q in range(size // LANES)], 0)
            fill = jnp.zeros((PAIR * count - count // 2 - edge.shape[0], LANES), F32)
            out[count // 2 :, to : to + LANES] = jnp.concatenate([edge, fill], 0).astype(BF16)
    for copy in started:
        copy.wait()


def convolve_in_order(place, blocks, columns, edge, tap, bias, wide, put):
    width = columns.stop - columns.start
    count = blocks[0][0].shape[0] // PAIR
    wide[5:8, :width] = edge
    for r, (block, origin) in enumerate(blocks):
        for core in range(PAIR):
            at = pl.multiple_of((core * len(blocks) + (place[4] ^ r)) * count + 8, 8)
            part = block[core * count : (core + 1) * count, origin + columns.start : origin + columns.stop]
            wide[pl.ds(at, count), :width] = part.astype(F32)
    tap, bias = tap * 0.5, bias * 0.5
    for start in range(0, PAIR * len(blocks) * count, count):
        acc = bias + tap[0:1] * wide[start + 5 : start + 5 + count, :width]
        acc = acc + tap[1:2] * wide[start + 6 : start + 6 + count, :width]
        acc = acc + tap[2:3] * wide[start + 7 : start + 7 + count, :width]
        acc = acc + tap[3:4] * wide[start + 8 : start + 8 + count, :width]
        put(start, count, (acc + acc * jnp.tanh(acc)).astype(BF16))


def prep_kernel(shards, place, *refs):
    blocks, (taps, offset, a_ref, bias_ref, skip_ref, order) = refs[:shards], refs[shards : shards + 6]
    b_ref, edge_ref, cum_ref, row_ref, factor_ref, tail_ref, skip_out, dt_ref, wide = refs[shards + 6 :]
    blocks = view(blocks, 0)
    start = WIDTHS[0]
    last = total_of(0) - LANES
    size = edge_ref.shape[1]
    count = blocks[0][0].shape[0] // PAIR
    half, heads = count // 2, HEADS // GROUPS
    columns = [block[:, last : last + LANES].astype(F32) for block, _ in blocks]
    edge = columns[0][half : half + 4 * size // LANES]
    for column in columns[1:]:
        edge = edge + column[half : half + 4 * size // LANES]
    for q in range(size // LANES):
        edge_ref[:, q * LANES : (q + 1) * LANES] = edge[4 * q : 4 * q + 4]
    for r, column in enumerate(columns):
        packed = column[:half]
        for j in range(2 * PAIR):
            at = ((j // 2) * shards + (place[4] ^ r)) * count + (j % 2) * half
            rows = packed if j == 0 else pltpu.roll(packed, LANES - j * heads, 1)
            dt_ref[pl.ds(pl.multiple_of(at, half), half), :] = rows

    def put(start, count, value):
        b_ref[start : start + count] = value

    at = slice(PER_GROUP, PER_GROUP + STATE)
    convolve_in_order(
        place, blocks, slice(start, start + STATE), edge_ref[0:3, at], taps[:, at], offset[:, at], wide, put
    )
    per_tile = LANES * GROUPS // HEADS
    group = place[0]
    tile = group // per_tile
    shift = (LANES - (group % per_tile) * heads) % LANES

    def lanes_of(ref):
        return pltpu.roll(jnp.broadcast_to(ref[pl.ds(tile, 1), :], (8, LANES)), shift, 1)

    rate = -jnp.exp(lanes_of(a_ref)[0:1])
    raw = dt_ref[...] + lanes_of(bias_ref)[0:1]
    step = jnp.maximum(raw, 0.0) + jnp.log1p(jnp.exp(-jnp.abs(raw)))
    skip = lanes_of(skip_ref)
    skip_out[...] = jnp.concatenate(halves(jnp.concatenate([skip, skip], 0), 3), 1)
    lower = (
        lax.broadcasted_iota(jnp.int32, (BLOCK, BLOCK), 0)
        >= lax.broadcasted_iota(jnp.int32, (BLOCK, BLOCK), 1)
    ).astype(BF16)
    valid = lax.broadcasted_iota(jnp.int32, (BLOCK, LANES), 1) < heads
    for block in range(PAIR):
        at = slice(block * BLOCK, (block + 1) * BLOCK)
        here = jnp.where(valid, step[at], 1.0)
        parts = halves(here * rate, 3)
        cum = dot(lower, parts[0]) + (dot(lower, parts[1]) + dot(lower, parts[2]))
        cum = cum * LOG2E
        cum_ref[at] = cum
        row_ref[:, at] = jnp.transpose(cum - jnp.log2(here))
        factor_ref[at] = jnp.concatenate(halves(jnp.exp2(cum), 2), 1)
        tail = jnp.exp2(cum[BLOCK - 1 :] - cum) * here
        tail_ref[at] = jnp.concatenate(halves(tail, 2), 1)


def score_kernel(shards, place, *refs):
    blocks, refs = refs[:shards], refs[shards:]
    taps, offset, edge_ref, b_ref, c_ref, score_ref, wide = (*refs[:4], *refs[-3:])
    blocks = view(blocks, 0)
    start = WIDTHS[0] + STATE
    at = slice(PER_GROUP + STATE, PER_GROUP + 2 * STATE)

    def put(start, count, value):
        c_ref[start : start + count] = value

    convolve_in_order(
        place, blocks, slice(start, start + STATE), edge_ref[0:3, at], taps[:, at], offset[:, at], wide, put
    )
    for block in range(PAIR):
        at = slice(block * BLOCK, (block + 1) * BLOCK)
        score_ref[at] = lax.dot_general(
            c_ref[at], b_ref[at], (((1,), (1,)), ((), ())), preferred_element_type=F32
        )


def decay_of(ref):
    decay = ref[STATE : STATE + 16].astype(F32)
    return decay[0:1] + (decay[1:2] + decay[2:3])


def put_decay(ref, decay):
    row = lax.broadcasted_iota(jnp.int32, (16, ref.shape[1]), 0)
    high, middle, low = (part.astype(F32) for part in halves(decay, 3))
    packed = jnp.where(row == 0, high, jnp.where(row == 1, middle, jnp.where(row == 2, low, 0.0)))
    ref[STATE:] = packed.astype(BF16)


def state_kernel(shards, part, sizes, place, *refs):
    blocks, refs = refs[:shards], refs[shards:]
    taps, offset, edge_ref, b_ref, factor_ref, tail_ref = refs[:6]
    x_ref, own_ref, *sends, wide = refs[-3 - len(sizes) :]
    piece, start, width = part
    first = sum(WIDTHS[:piece]) + start
    at = slice(first, first + width)

    def put(row, count, value):
        x_ref[row : row + count] = value

    blocks = view(blocks, piece)
    columns = slice(start, start + width)
    convolve_in_order(place, blocks, columns, edge_ref[0:3, at], taps[:, at], offset[:, at], wide, put)
    expand = spread(first // HEAD_DIM, width, 2)
    both = []
    for block in range(PAIR):
        at = slice(block * BLOCK, (block + 1) * BLOCK)
        loaded = (x_ref[at].astype(F32) * dot(tail_ref[at], expand)).astype(BF16)
        both.append(
            lax.dot_general(b_ref[at], loaded, (((0,), (0,)), ((), ())), preferred_element_type=F32)
        )
    ends = [dot(factor_ref[(i + 1) * BLOCK - 16 : (i + 1) * BLOCK], expand)[15:16] for i in range(PAIR)]
    own_ref[...] = both[0]
    end = (ends[1] * both[0] + both[1]).astype(BF16)
    decay = ends[0] * ends[1]
    start = 0
    for send_ref in sends:
        at = slice(start, start + send_ref.shape[1])
        send_ref[0:STATE] = end[:, at]
        put_decay(send_ref, decay[:, at])
        start = at.stop


def combine_kernel(count, *refs):
    early, late, out_ref = refs[:count], refs[count : 2 * count], refs[-1]
    start = 0
    for early_ref, late_ref in zip(early, late):
        at = slice(start, start + late_ref.shape[1])
        decay = decay_of(late_ref)
        total = decay * early_ref[:STATE].astype(F32) + late_ref[:STATE].astype(F32)
        out_ref[:STATE, at] = total.astype(BF16)
        put_decay(out_ref.at[:, at], decay * decay_of(early_ref))
        start = at.stop


def mix(first_head, x_ref, cum_ref, row_ref, score_ref, skip_ref, put):
    width = x_ref.shape[1]
    half = BLOCK // 2
    expand = spread(first_head, width, 3)
    skip = dot(skip_ref[...], expand)[0:1]
    lower = lax.broadcasted_iota(jnp.int32, (half, half), 0) >= lax.broadcasted_iota(
        jnp.int32, (half, half), 1
    )
    lane = lax.broadcasted_iota(jnp.int32, (BLOCK, LANES), 1)
    for block in range(PAIR):
        base = block * BLOCK
        for tile in range(width // LANES):
            columns = slice(tile * LANES, (tile + 1) * LANES)
            x = x_ref[base : base + BLOCK, columns]
            top = skip[:, columns] * x[:half].astype(F32)
            bottom = skip[:, columns] * x[half:].astype(F32)
            for side in range(LANES // HEAD_DIM):
                head = first_head + tile * (LANES // HEAD_DIM) + side
                own = jnp.where(lane // HEAD_DIM == side, x, jnp.zeros_like(x))
                cum = cum_ref[base : base + BLOCK, head : head + 1]
                row = row_ref[head : head + 1, base : base + BLOCK]
                diag = jnp.where(lower, cum[:half] - row[:, :half], -1e30)
                mixing = jnp.exp2(diag) * score_ref[base : base + half, :half]
                top = top + dot(mixing.astype(BF16), own[:half])
                left = jnp.exp2(cum[half:] - row[:, :half]) * score_ref[base + half : base + BLOCK, :half]
                diag = jnp.where(lower, cum[half:] - row[:, half:], -1e30)
                right = jnp.exp2(diag) * score_ref[base + half : base + BLOCK, half:]
                mixing = jnp.concatenate([left.astype(BF16), right.astype(BF16)], 1)
                bottom = bottom + dot(mixing, own)
            put(block, slice(base, base + half), columns, top)
            put(block, slice(base + half, base + BLOCK), columns, bottom)


def local_kernel(first_head, x_ref, cum_ref, row_ref, score_ref, skip_ref, *refs):
    out_ref = refs[-1]

    def put(block, rows, columns, value):
        out_ref[rows, columns] = value

    mix(first_head, x_ref, cum_ref, row_ref, score_ref, skip_ref, put)


def carry(first_head, core, lasts, befores, own_ref, c_ref, factor_ref, add, keep_ref, send_ref):
    expand = spread(first_head, own_ref.shape[1], 2)
    last, before = (
        refs[0][...] if len(refs) == 1 else jnp.concatenate([ref[...] for ref in refs], 1)
        for refs in (lasts, befores)
    )
    held = last[:STATE].astype(F32) + decay_of(last) * before[:STATE].astype(F32)
    factor = dot(factor_ref[...], expand)
    outs = []
    for block in range(PAIR):
        at = slice(block * BLOCK, (block + 1) * BLOCK)
        carried = dot(c_ref[at], held.astype(BF16))
        outs.append((add[at] + factor[at] * carried).astype(BF16))
        held = factor[BLOCK - 1 : BLOCK] * held + own_ref[...]

    @pl.when(core == 0)
    def _():
        keep_ref[...] = outs[0]
        send_ref[...] = outs[1]

    @pl.when(core == 1)
    def _():
        keep_ref[...] = outs[1]
        send_ref[...] = outs[0]


def final_kernel(first_head, lasts, befores, place, *refs):
    last, refs = refs[:lasts], refs[lasts:]
    before, refs = refs[:befores], refs[befores:]
    carry(first_head, place[2], last, before, *refs[:4], *refs[-2:])


def finish_kernel(first_head, lasts, befores, place, *refs):
    last, refs = refs[:lasts], refs[lasts:]
    before, refs = refs[:befores], refs[befores:]
    own_ref, c_ref, factor_ref = refs[:3]
    keep_ref, send_ref, partial = refs[-3:]
    local_kernel(first_head, *refs[3:8], partial)
    carry(first_head, place[2], last, before, own_ref, c_ref, factor_ref, partial, keep_ref, send_ref)


def place_kernel(firsts, place, *refs):
    count = len(firsts)
    keeps, gots = refs[:count], refs[count : 2 * count]
    out, sems = refs[-2:]
    core = place[2]
    half = out.shape[1] // PAIR
    copies = []
    for first, keep, got in zip(firsts, keeps, gots):
        width = keep.shape[1]
        copies.append((keep, out.at[:, ds(core * half + first, width)]))
        copies.append((got, out.at[:, ds((1 - core) * half + first, width)]))
    for copy in run(copies, sems):
        copy.wait()


def put_in_place(firsts, shape, place, keeps, gots, before):
    smem, vmem, hbm = (pl.BlockSpec(memory_space=m) for m in (pltpu.SMEM, pltpu.VMEM, pltpu.HBM))
    count = len(firsts)
    return pl.pallas_call(
        functools.partial(place_kernel, firsts),
        out_shape=jax.ShapeDtypeStruct(shape, BF16),
        in_specs=[smem] + [vmem] * (2 * count) + [hbm] * len(before),
        out_specs=hbm,
        input_output_aliases={2 * count + 1: 0} if before else {},
        scratch_shapes=[pltpu.SemaphoreType.DMA((2 * count,))],
        compiler_params=pltpu.CompilerParams(vmem_limit_bytes=16 << 20),
        cost_estimate=pl.CostEstimate(flops=1, bytes_accessed=1, transcendentals=0),
        name="place",
    )(place, *keeps, *gots, *before)


class Stay:
    def __init__(self, array):
        self.array = array


def call(body, outs, operands, scratch=(), flops=0, transcendentals=0, name=None, limit=16 << 20):
    shapes = [jax.ShapeDtypeStruct(shape, dtype) for shape, dtype in outs]
    smem, vmem, hbm = (pl.BlockSpec(memory_space=m) for m in (pltpu.SMEM, pltpu.VMEM, pltpu.HBM))
    specs = [
        hbm if isinstance(o, Stay) else smem if o.dtype == jnp.int32 else vmem for o in operands
    ]
    moved = sum(o.size * o.dtype.itemsize for o in shapes) * 2
    return pl.pallas_call(
        body,
        out_shape=shapes,
        in_specs=specs,
        out_specs=[vmem] * len(outs),
        scratch_shapes=scratch,
        compiler_params=pltpu.CompilerParams(vmem_limit_bytes=limit),
        cost_estimate=pl.CostEstimate(flops=1, bytes_accessed=1, transcendentals=0),
        name=name,
    )(*[o.array if isinstance(o, Stay) else o for o in operands])


def paired(xbc, dt_raw, conv_weight, conv_bias, a_log, dt_bias, skip_gain):
    axes = ("ctx", "head")
    shards, length = lax.axis_size("head"), lax.axis_size("ctx")
    devices, peers = shards * length, shards * PAIR
    tok = xbc.shape[0]
    slab = tok * peers
    context, shard = lax.axis_index("ctx"), lax.axis_index("head")
    pair, core = context // PAIR, context % PAIR
    group = shard * PAIR + core
    place = jnp.stack([group, pair, core, core * shards + shard, shard]).astype(jnp.int32)

    def over(block, target):
        route = [(i, target(i)) for i in range(devices)]
        return lax.ppermute(block, axes, [(i, j) for i, j in route if j is not None and j < devices])

    def swap(block):
        return over(block, lambda i: i ^ shards)

    rows = Stay(xbc)
    size = PER_GROUP + 2 * STATE
    sent, near, far = call(
        functools.partial(pack_kernel, shards),
        [((tok, shards * size + HEADS), BF16), ((3, shards * size), BF16), ((3, shards * size), BF16)],
        [place, rows, Stay(dt_raw)],
        scratch=[pltpu.VMEM((16, xbc.shape[1]), BF16), pltpu.SemaphoreType.DMA((3 * shards + 2,))],
        name="pack",
    )
    near = over(near, lambda i: i + peers if i % peers == peers - 1 else None)
    far = over(far, lambda i: i + shards if i % peers == peers - 1 else None)
    got = swap(sent)
    taps, offset = call(
        taps_kernel,
        [((4, size), F32), ((1, size), F32)],
        [place, Stay(conv_weight), Stay(conv_bias[None]), Stay(got)],
        scratch=[pltpu.SemaphoreType.DMA((6,))],
        name="taps",
    )

    def merge(plan, order):
        steps = any("D" in RESTS[p] for _, pieces in plan for p in pieces)
        parts = [p for _, pieces in plan for p in pieces]
        return call(
            functools.partial(merge_kernel, shards, plan, len(order)),
            [((PAIR * tok, sum(map(total_of, pieces))), BF16) for _, pieces in plan],
            [place, rows] + [o if steps else Stay(o) for o in (dt_raw,)] + [got]
            + [o if steps else Stay(o) for o in (near, far)]
            + [Stay(o) for o in order],
            scratch=[pltpu.SemaphoreType.DMA((sum(2 + 4 * ("C" in RESTS[p]) for p in parts),))],
            name="merge",
        )

    def across(block, r):
        return over(block, lambda i: i ^ r)

    far_apart = list(range(2, shards))
    first_blocks = merge([(r, (0,)) for r in far_apart] + [(1, (0, 1))], [])
    *far_blocks, near_block = first_blocks
    arrived = [across(block, r) for r, block in zip(far_apart, far_blocks)]
    near_got = across(near_block, 1)
    *third_blocks, own_block = merge([(r, (1,)) for r in far_apart] + [(0, (0, 1))], [first_blocks[0]])
    message = [[own_block, near_got, *arrived]]
    message.append([own_block, near_got] + [across(block, r) for r, block in zip(far_apart, third_blocks)])

    tiles = [p.reshape(HEADS // LANES, LANES) for p in (a_log, dt_bias, skip_gain)]
    b, edge, cum, row, factor, tail, skip = call(
        functools.partial(prep_kernel, shards),
        [
            ((slab, STATE), BF16),
            ((4, size), F32),
            ((slab, LANES), F32),
            ((LANES, slab), F32),
            ((slab, 2 * LANES), BF16),
            ((slab, 2 * LANES), BF16),
            ((16, 3 * LANES), BF16),
        ],
        [place] + message[0] + [taps, offset] + tiles + [Stay(third_blocks[0])],
        scratch=[pltpu.VMEM((slab, LANES), F32), pltpu.VMEM((slab + 8, STATE), F32)],
        name="prep",
    )
    count = len(GROUPED)
    x, sent, own, last, joined, before, keep, send = ([None] * count for _ in range(8))

    def first_head(i):
        return (sum(WIDTHS[: GROUPED[i][0]]) + GROUPED[i][1]) // HEAD_DIM

    def state_of(i, order):
        piece, _, width = GROUPED[i]
        x[i], own[i], *sent[i] = call(
            functools.partial(state_kernel, shards, GROUPED[i], ROUNDS[i]),
            [((slab, width), BF16), ((STATE, width), F32)] + [((STATE + 16, w), BF16) for w in ROUNDS[i]],
            [place] + message[piece] + [taps, offset, edge, b, factor, tail] + [Stay(o) for o in order],
            scratch=[pltpu.VMEM((slab + 8, width), F32)],
            name="state",
        )
        last[i] = [over(part, lambda i: i + peers) for part in sent[i]]

    def combine_of(i, order):
        joined[i], before[i] = [], []
        for j, width in enumerate(ROUNDS[i]):
            (total,) = call(
                functools.partial(combine_kernel, 1),
                [((STATE + 16, width), BF16)],
                [last[i][j], sent[i][j]] + [Stay(o) for o in order],
                name="combine",
            )
            joined[i].append(total)
            before[i].append(over(total, lambda i: i + 2 * peers))
            order = [total]

    def finish_of(body, i, operands, order, **more):
        keep[i], send[i] = call(
            functools.partial(body, first_head(i), len(last[i]), len(before[i])),
            [((BLOCK, GROUPED[i][2]), BF16)] * 2,
            [place, *last[i], *before[i], own[i], c, factor] + operands + [Stay(o) for o in order],
            name="final",
            **more,
        )

    state_of(0, [])
    c, score = call(
        functools.partial(score_kernel, shards),
        [((slab, STATE), BF16), ((slab, BLOCK), F32)],
        [place] + message[0] + [taps, offset, edge, b] + [Stay(o) for o in sent[0]],
        scratch=[pltpu.VMEM((slab + 8, STATE), F32)],
        name="score",
    )
    mixes = [cum, row, score, skip]

    def in_full(i, order):
        wide = [pltpu.VMEM((slab, GROUPED[i][2]), F32)]
        finish_of(finish_kernel, i, [x[i]] + mixes, order, scratch=wide)

    shape = (BLOCK, PAIR * PER_GROUP)
    combine_of(0, [score])
    in_full(0, joined[0])
    out = put_in_place([0], shape, place, keep[:1], [swap(send[0])], [])
    order = [out]
    for i in range(1, count):
        state_of(i, order)
        order = sent[i]
    partial = {}
    for i in range(1, count):
        combine_of(i, order)
        (partial[i],) = call(
            functools.partial(local_kernel, first_head(i)),
            [(x[i].shape, F32)],
            [x[i]] + mixes + [Stay(o) for o in joined[i]],
            name="local",
        )
        order = [partial[i]]
    for i in range(1, count):
        finish_of(final_kernel, i, [partial[i]], order)
        order = [keep[i]]
    firsts = [first_head(i) * HEAD_DIM for i in range(1, count)]
    return put_in_place(firsts, shape, place, keep[1:], [swap(o) for o in send[1:]], [out])


def solution(mesh):
    in_specs = (P(("ctx", "head"), None), P(("ctx", "head"), None), P(), P(), P(), P(), P())
    out_specs = P("ctx", "head")
    shards, length = mesh.shape["head"], mesh.shape["ctx"]

    def program(xbc, *rest):
        slab = xbc.shape[0] // length
        fits = shards == GROUPS // PAIR and length == 4 * PAIR and slab == BLOCK
        return jax.shard_map(
            paired if fits else on_device,
            mesh=mesh,
            in_specs=in_specs,
            out_specs=out_specs,
            check_vma=False,
        )(xbc, *rest)

    return program
```

```python
import functools

import jax
import jax.numpy as jnp
from jax import lax
from jax.experimental import pallas as pl
from jax.experimental.pallas import tpu as pltpu
from jax.sharding import PartitionSpec as P

HEADS = 256
HEAD_DIM = 64
STATE = 256
GROUPS = 8
BLOCK = 256


def from_behind(block, axis, distance):
    devices = range(lax.axis_size(axis))
    route = [(i - distance, i) for i in devices if i - distance in devices]
    return lax.ppermute(block, axis, route)


def carried_in(array, axis, combine, identity):
    length, index = (lax.axis_size(axis), lax.axis_index(axis))
    everything = jax.tree.map(lambda part: lax.all_gather(part, axis), array)
    start = jax.tree.map(
        lambda part, zero: jnp.broadcast_to(jnp.asarray(zero, part.dtype), part.shape),
        array,
        identity,
    )

    def hop(k, before):
        reached = k < index
        new = combine(before, jax.tree.map(lambda part: part[k], everything))
        return jax.tree.map(lambda a, b: jnp.where(reached, a, b), new, before)

    return lax.fori_loop(0, length, hop, start)


def convolve(rows, edge, weight, bias):
    count = rows.shape[0]
    wide = jnp.concatenate([edge, rows], 0).astype(jnp.float32)
    acc = bias[None, :] + weight[0] * wide[0:count]
    acc = acc + weight[1] * wide[1 : count + 1]
    acc = acc + weight[2] * wide[2 : count + 2]
    acc = acc + weight[3] * wide[3 : count + 3]
    return jax.nn.silu(acc).astype(jnp.bfloat16)


def rearrange_heads(rows, shards, per_dev, groups_dev, per_group):
    count = rows.shape[0]
    inner = HEADS * HEAD_DIM
    replicate_groups = max(1, per_group // per_dev)
    heads_part = rows[:, :inner].reshape(count, shards, per_dev * HEAD_DIM)
    b_part = rows[:, inner : inner + GROUPS * STATE].reshape(count, GROUPS, STATE)
    c_part = rows[:, inner + GROUPS * STATE :].reshape(count, GROUPS, STATE)
    b_part = jnp.repeat(b_part, replicate_groups, axis=1).reshape(count, shards, groups_dev * STATE)
    c_part = jnp.repeat(c_part, replicate_groups, axis=1).reshape(count, shards, groups_dev * STATE)
    return jnp.concatenate([heads_part, b_part, c_part], axis=2)


def inner_block(xs, bmat, cmat, steps, cum):
    size = xs.shape[0]
    lower = jnp.arange(size)[:, None] >= jnp.arange(size)[None, :]
    scores = jnp.einsum("qgn,kgn->gqk", cmat, bmat, preferred_element_type=jnp.float32)
    order = jnp.transpose(cum, (1, 2, 0))
    gap = order[..., :, None] - order[..., None, :]
    decay = jnp.exp(jnp.where(lower, gap, -jnp.inf))
    mixing = (scores[:, None] * decay * jnp.transpose(steps, (1, 2, 0))[..., None, :]).astype(
        jnp.bfloat16
    )
    local = jnp.einsum("gjqk,kgjp->qgjp", mixing, xs, preferred_element_type=jnp.float32)
    tail = jnp.exp(cum[size - 1][None] - cum) * steps
    loaded = (bmat[:, :, None, :].astype(jnp.float32) * tail[..., None]).astype(jnp.bfloat16)
    block_state = jnp.einsum("kgjn,kgjp->gjnp", loaded, xs, preferred_element_type=jnp.float32)
    return (local, block_state)


def on_device(xbc, dt_raw, conv_weight, conv_bias, a_log, dt_bias, skip_gain):
    tok = xbc.shape[0]
    shards = lax.axis_size("head")
    per_dev = HEADS // shards
    per_group = HEADS // GROUPS
    groups_dev = max(1, per_dev // per_group)
    heads_per_cluster = per_dev // groups_dev
    sent = rearrange_heads(xbc, shards, per_dev, groups_dev, per_group)
    mine, rates = (
        lax.all_to_all(sent, "head", split_axis=1, concat_axis=0, tiled=True),
        lax.all_to_all(
            dt_raw.reshape(tok, shards, per_dev), "head", split_axis=1, concat_axis=0, tiled=True
        ),
    )
    slab = tok * shards
    mine = mine.reshape(slab, mine.shape[2])
    rates = rates.reshape(slab, per_dev)
    shard = lax.axis_index("head")
    taps = lax.dynamic_index_in_dim(
        rearrange_heads(conv_weight, shards, per_dev, groups_dev, per_group),
        shard,
        1,
        keepdims=False,
    )
    offset = lax.dynamic_index_in_dim(
        rearrange_heads(conv_bias[None, :], shards, per_dev, groups_dev, per_group),
        shard,
        1,
        keepdims=False,
    )
    edge = from_behind(mine[slab - 3 :], "ctx", 1)
    mine = convolve(mine, edge, taps, offset[0])
    nchunk = slab // BLOCK
    width = per_dev * HEAD_DIM
    xs = mine[:, :width].reshape(nchunk, BLOCK, groups_dev, heads_per_cluster, HEAD_DIM)
    bmat = mine[:, width : width + groups_dev * STATE].reshape(nchunk, BLOCK, groups_dev, STATE)
    cmat = mine[:, width + groups_dev * STATE :].reshape(nchunk, BLOCK, groups_dev, STATE)
    first = shard * per_dev
    rate = (-jnp.exp(lax.dynamic_slice_in_dim(a_log, first, per_dev))).reshape(
        groups_dev, heads_per_cluster
    )
    bias_dt = lax.dynamic_slice_in_dim(dt_bias, first, per_dev).reshape(
        groups_dev, heads_per_cluster
    )
    skip = lax.dynamic_slice_in_dim(skip_gain, first, per_dev).reshape(
        groups_dev, heads_per_cluster
    )
    steps = jax.nn.softplus(
        rates.astype(jnp.float32).reshape(nchunk, BLOCK, groups_dev, heads_per_cluster) + bias_dt
    )
    cum = jnp.cumsum(steps * rate, axis=1)

    def block_step(carry, item):
        held, product = carry
        x_part, b_part, c_part, step_part, cum_part = item
        local, block_state = inner_block(x_part, b_part, c_part, step_part, cum_part)
        lifted = c_part.astype(jnp.float32)[:, :, None, :] * jnp.exp(cum_part)[..., None]
        carried = jnp.einsum("qgjn,gjnp->qgjp", lifted, held, precision=lax.Precision.HIGHEST)
        partial_out = local + carried + skip[..., None] * x_part.astype(jnp.float32)
        end = jnp.exp(cum_part[BLOCK - 1])
        return ((end[..., None, None] * held + block_state, product * end), (partial_out, product))

    zero_state = jnp.zeros((groups_dev, heads_per_cluster, STATE, HEAD_DIM), jnp.float32)
    unit = jnp.ones((groups_dev, heads_per_cluster), jnp.float32)
    (slab_state, slab_decay), (partials, product_in) = lax.scan(
        block_step, (zero_state, unit), (xs, bmat, cmat, steps, cum)
    )

    def combine(preceding_state, later):
        return (
            preceding_state[0] * later[0],
            later[0][..., None, None] * preceding_state[1] + later[1],
        )

    _, entering = carried_in((slab_decay, slab_state), "ctx", combine, (unit, zero_state))
    projected = jnp.einsum(
        "cqgn,gjnp->cqgjp", cmat.astype(jnp.float32), entering, precision=lax.Precision.HIGHEST
    )
    factor = jnp.exp(cum) * product_in[:, None]
    total = partials + factor[..., None] * projected
    return total.astype(jnp.bfloat16).reshape(slab, width)


PAIR = 2
LANES = 128
LOG2E = 1.4426950408889634
F32, BF16 = jnp.float32, jnp.bfloat16
WIDTHS = (896, 640, 512)
RESTS = ("BCD", "", "")
GROUPED = ((0, 0, 896), (1, 0, 640), (2, 0, 512))
ROUNDS = ((896,), (640,), (512,))


def halves(value, count):
    parts = []
    for _ in range(count):
        part = value.astype(BF16)
        parts.append(part)
        value = value - part.astype(F32)
    return parts


def spread(first_head, width, copies):
    lane = lax.broadcasted_iota(jnp.int32, (copies * LANES, width), 0) % LANES
    column = lax.broadcasted_iota(jnp.int32, (copies * LANES, width), 1)
    return (lane == first_head + column // HEAD_DIM).astype(BF16)


def dot(a, b):
    return jnp.dot(a, b, preferred_element_type=F32)


def ds(start, width):
    return pl.ds(pl.multiple_of(start, LANES), width)


def run(copies, sems):
    started = []
    for i, (source, target) in enumerate(copies):
        copy = pltpu.make_async_copy(source, target, sems.at[i])
        copy.start()
        started.append(copy)
    return started


PER_GROUP = HEADS * HEAD_DIM // GROUPS
INNER = HEADS * HEAD_DIM


def channels(group, first, width):
    return ds(group * PER_GROUP + first, width)


def runs(group):
    yield group * PER_GROUP, PER_GROUP
    yield INNER + group * STATE, STATE
    yield INNER + (GROUPS + group) * STATE, STATE


def pack_kernel(shards, place, xbc, dt_raw, send, near, far, tail, sems):
    core, shard = place[2], place[4]
    count = xbc.shape[0]
    copies = [(xbc.at[count - 16 :], tail)]
    to = 0
    for r in range(shards):
        for start, width in runs(r * PAIR + 1 - core):
            copies.append((xbc.at[:, ds(start, width)], send.at[:, to : to + width]))
            to += width
    copies.append((dt_raw, send.at[:, to:]))
    started = run(copies, sems)
    started[0].wait()
    for edge, side in ((near, 1), (far, 0)):
        to = 0
        for r in range(shards):
            for start, width in runs(r * PAIR + side):
                rows = tail[:, start : start + width].astype(F32)
                edge[:, to : to + width] = rows[13:16].astype(BF16)
                to += width
    for copy in started[1:]:
        copy.wait()


def taps_kernel(place, weight, bias, order, taps, offset, sems):
    copies, to = [], 0
    for start, width in runs(place[0]):
        copies.append((weight.at[:, ds(start, width)], taps.at[:, to : to + width]))
        copies.append((bias.at[:, ds(start, width)], offset.at[:, to : to + width]))
        to += width
    for copy in run(copies, sems):
        copy.wait()


def total_of(piece):
    return WIDTHS[piece] + sum(LANES if kind == "D" else STATE for kind in RESTS[piece])


def merge_kernel(shards, plan, unread, place, xbc, dt_raw, got, near, far, *refs):
    outs, sems = refs[unread:]
    core, shard = place[2], place[4]
    count = xbc.shape[0]
    size = PER_GROUP + 2 * STATE
    mine = pl.ds(pl.multiple_of(core * count, count), count)
    other = pl.ds(pl.multiple_of((1 - core) * count, count), count)
    copies, steps = [], []
    for r in range(shards):
        out = outs.at[r]
        group = r * PAIR + core
        to = 0
        for piece in [plan]:
            first, width = sum(WIDTHS[:piece]), WIDTHS[piece]
            parts = [(group * PER_GROUP + first, r * size + first, width)]
            for i, kind in enumerate("BC"):
                if kind in RESTS[piece]:
                    at = INNER + (i * GROUPS + group) * STATE
                    parts.append((at, r * size + PER_GROUP + i * STATE, STATE))
            for own, theirs, width in parts:
                copies.append((xbc.at[:, ds(own, width)], out.at[mine, to : to + width]))
                copies.append((got.at[:, theirs : theirs + width], out.at[other, to : to + width]))
                to += width
            if "D" in RESTS[piece]:
                steps.append((out, r, to))
                to += LANES
    started = run(copies, sems)
    if steps:
        lane = lax.broadcasted_iota(jnp.int32, (count, LANES), 1)
        per_tile = LANES * GROUPS // HEADS
        heads = HEADS // GROUPS
        for out, r, to in steps:
            group = r * PAIR + core
            tile, shift = group // per_tile, (LANES - (group % per_tile) * heads) % LANES
            own = dt_raw[:, ds(tile * LANES, LANES)].astype(F32)
            theirs = got[:, ds(got.shape[1] - HEADS + tile * LANES, LANES)].astype(F32)
            low = jnp.where(core == 0, own, theirs)
            high = jnp.where(core == 0, theirs, own)
            packed = jnp.zeros((count // 2, LANES), F32)
            for j, rows in enumerate((low, high)):
                rows = jnp.where(lane < heads, pltpu.roll(rows, shift, 1), 0.0)
                for i in range(2):
                    part = rows[i * count // 2 : (i + 1) * count // 2]
                    packed = packed + pltpu.roll(part, (2 * j + i) * heads, 1)
            out[: count // 2, to : to + LANES] = packed.astype(BF16)
            size = PER_GROUP + 2 * STATE
            at = slice(r * size, (r + 1) * size)
            edge = near[:, at].astype(F32) + far[:, at].astype(F32)
            edge = jnp.concatenate([edge, jnp.zeros((1, size), F32)], 0)
            edge = jnp.concatenate([edge[:, q * LANES : (q + 1) * LANES] for q in range(size // LANES)], 0)
            fill = jnp.zeros((PAIR * count - count // 2 - edge.shape[0], LANES), F32)
            out[count // 2 :, to : to + LANES] = jnp.concatenate([edge, fill], 0).astype(BF16)
    for copy in started:
        copy.wait()


def convolve_in_order(blocks, columns, edge, tap, bias, wide, put):
    width = columns.stop - columns.start
    shards, rows, _ = blocks.shape
    count = rows // PAIR
    wide[5:8, :width] = edge
    for r in range(shards):
        for core in range(PAIR):
            at = (core * shards + r) * count + 8
            part = blocks[r, core * count : (core + 1) * count, columns]
            wide[at : at + count, :width] = part.astype(F32)
    tap, bias = tap * 0.5, bias * 0.5
    for start in range(0, PAIR * shards * count, count):
        acc = bias + tap[0:1] * wide[start + 5 : start + 5 + count, :width]
        acc = acc + tap[1:2] * wide[start + 6 : start + 6 + count, :width]
        acc = acc + tap[2:3] * wide[start + 7 : start + 7 + count, :width]
        acc = acc + tap[3:4] * wide[start + 8 : start + 8 + count, :width]
        put(start, count, (acc + acc * jnp.tanh(acc)).astype(BF16))


def prep_kernel(shards, place, blocks, *refs):
    taps, offset, a_ref, bias_ref, skip_ref, order = refs[:6]
    b_ref, edge_ref, cum_ref, row_ref, factor_ref, tail_ref, skip_out, dt_ref, wide = refs[6:]
    start = WIDTHS[0]
    last = total_of(0) - LANES
    size = edge_ref.shape[1]
    count = blocks.shape[1] // PAIR
    half, heads = count // 2, HEADS // GROUPS
    columns = [blocks[r, :, last : last + LANES].astype(F32) for r in range(shards)]
    edge = columns[0][half : half + 4 * size // LANES]
    for column in columns[1:]:
        edge = edge + column[half : half + 4 * size // LANES]
    for q in range(size // LANES):
        edge_ref[:, q * LANES : (q + 1) * LANES] = edge[4 * q : 4 * q + 4]
    for r, column in enumerate(columns):
        packed = column[:half]
        for j in range(2 * PAIR):
            at = ((j // 2) * shards + r) * count + (j % 2) * half
            rows = packed if j == 0 else pltpu.roll(packed, LANES - j * heads, 1)
            dt_ref[at : at + half] = rows

    def put(start, count, value):
        b_ref[start : start + count] = value

    at = slice(PER_GROUP, PER_GROUP + STATE)
    convolve_in_order(
        blocks, slice(start, start + STATE), edge_ref[0:3, at], taps[:, at], offset[:, at], wide, put
    )
    per_tile = LANES * GROUPS // HEADS
    group = place[0]
    tile = group // per_tile
    shift = (LANES - (group % per_tile) * heads) % LANES

    def lanes_of(ref):
        return pltpu.roll(jnp.broadcast_to(ref[pl.ds(tile, 1), :], (8, LANES)), shift, 1)

    rate = -jnp.exp(lanes_of(a_ref)[0:1])
    raw = dt_ref[...] + lanes_of(bias_ref)[0:1]
    step = jnp.maximum(raw, 0.0) + jnp.log1p(jnp.exp(-jnp.abs(raw)))
    skip = lanes_of(skip_ref)
    skip_out[...] = jnp.concatenate(halves(jnp.concatenate([skip, skip], 0), 3), 1)
    lower = (
        lax.broadcasted_iota(jnp.int32, (BLOCK, BLOCK), 0)
        >= lax.broadcasted_iota(jnp.int32, (BLOCK, BLOCK), 1)
    ).astype(BF16)
    valid = lax.broadcasted_iota(jnp.int32, (BLOCK, LANES), 1) < heads
    for block in range(PAIR):
        at = slice(block * BLOCK, (block + 1) * BLOCK)
        here = jnp.where(valid, step[at], 1.0)
        parts = halves(here * rate, 3)
        cum = dot(lower, parts[0]) + (dot(lower, parts[1]) + dot(lower, parts[2]))
        cum = cum * LOG2E
        cum_ref[at] = cum
        row_ref[:, at] = jnp.transpose(cum - jnp.log2(here))
        factor_ref[at] = jnp.concatenate(halves(jnp.exp2(cum), 2), 1)
        tail = jnp.exp2(cum[BLOCK - 1 :] - cum) * here
        tail_ref[at] = jnp.concatenate(halves(tail, 2), 1)


def score_kernel(blocks, *refs):
    taps, offset, edge_ref, b_ref, c_ref, score_ref, wide = (*refs[:4], *refs[-3:])
    start = WIDTHS[0] + STATE
    at = slice(PER_GROUP + STATE, PER_GROUP + 2 * STATE)

    def put(start, count, value):
        c_ref[start : start + count] = value

    convolve_in_order(
        blocks, slice(start, start + STATE), edge_ref[0:3, at], taps[:, at], offset[:, at], wide, put
    )
    for block in range(PAIR):
        at = slice(block * BLOCK, (block + 1) * BLOCK)
        score_ref[at] = lax.dot_general(
            c_ref[at], b_ref[at], (((1,), (1,)), ((), ())), preferred_element_type=F32
        )


def decay_of(ref):
    decay = ref[STATE : STATE + 16].astype(F32)
    return decay[0:1] + (decay[1:2] + decay[2:3])


def put_decay(ref, decay):
    row = lax.broadcasted_iota(jnp.int32, (16, ref.shape[1]), 0)
    high, middle, low = (part.astype(F32) for part in halves(decay, 3))
    packed = jnp.where(row == 0, high, jnp.where(row == 1, middle, jnp.where(row == 2, low, 0.0)))
    ref[STATE:] = packed.astype(BF16)


def state_kernel(part, sizes, blocks, *refs):
    taps, offset, edge_ref, b_ref, factor_ref, tail_ref = refs[:6]
    x_ref, own_ref, *sends, wide = refs[-3 - len(sizes) :]
    piece, start, width = part
    first = sum(WIDTHS[:piece]) + start
    at = slice(first, first + width)

    def put(row, count, value):
        x_ref[row : row + count] = value

    columns = slice(start, start + width)
    convolve_in_order(blocks, columns, edge_ref[0:3, at], taps[:, at], offset[:, at], wide, put)
    expand = spread(first // HEAD_DIM, width, 2)
    both = []
    for block in range(PAIR):
        at = slice(block * BLOCK, (block + 1) * BLOCK)
        loaded = (x_ref[at].astype(F32) * dot(tail_ref[at], expand)).astype(BF16)
        both.append(
            lax.dot_general(b_ref[at], loaded, (((0,), (0,)), ((), ())), preferred_element_type=F32)
        )
    ends = [dot(factor_ref[(i + 1) * BLOCK - 16 : (i + 1) * BLOCK], expand)[15:16] for i in range(PAIR)]
    own_ref[...] = both[0]
    end = (ends[1] * both[0] + both[1]).astype(BF16)
    decay = ends[0] * ends[1]
    start = 0
    for send_ref in sends:
        at = slice(start, start + send_ref.shape[1])
        send_ref[0:STATE] = end[:, at]
        put_decay(send_ref, decay[:, at])
        start = at.stop


def combine_kernel(count, *refs):
    early, late, out_ref = refs[:count], refs[count : 2 * count], refs[-1]
    start = 0
    for early_ref, late_ref in zip(early, late):
        at = slice(start, start + late_ref.shape[1])
        decay = decay_of(late_ref)
        total = decay * early_ref[:STATE].astype(F32) + late_ref[:STATE].astype(F32)
        out_ref[:STATE, at] = total.astype(BF16)
        put_decay(out_ref.at[:, at], decay * decay_of(early_ref))
        start = at.stop


def mix(first_head, x_ref, cum_ref, row_ref, score_ref, skip_ref, put):
    width = x_ref.shape[1]
    half = BLOCK // 2
    expand = spread(first_head, width, 3)
    skip = dot(skip_ref[...], expand)[0:1]
    lower = lax.broadcasted_iota(jnp.int32, (half, half), 0) >= lax.broadcasted_iota(
        jnp.int32, (half, half), 1
    )
    lane = lax.broadcasted_iota(jnp.int32, (BLOCK, LANES), 1)
    for block in range(PAIR):
        base = block * BLOCK
        for tile in range(width // LANES):
            columns = slice(tile * LANES, (tile + 1) * LANES)
            x = x_ref[base : base + BLOCK, columns]
            top = skip[:, columns] * x[:half].astype(F32)
            bottom = skip[:, columns] * x[half:].astype(F32)
            for side in range(LANES // HEAD_DIM):
                head = first_head + tile * (LANES // HEAD_DIM) + side
                own = jnp.where(lane // HEAD_DIM == side, x, jnp.zeros_like(x))
                cum = cum_ref[base : base + BLOCK, head : head + 1]
                row = row_ref[head : head + 1, base : base + BLOCK]
                diag = jnp.where(lower, cum[:half] - row[:, :half], -1e30)
                mixing = jnp.exp2(diag) * score_ref[base : base + half, :half]
                top = top + dot(mixing.astype(BF16), own[:half])
                left = jnp.exp2(cum[half:] - row[:, :half]) * score_ref[base + half : base + BLOCK, :half]
                diag = jnp.where(lower, cum[half:] - row[:, half:], -1e30)
                right = jnp.exp2(diag) * score_ref[base + half : base + BLOCK, half:]
                mixing = jnp.concatenate([left.astype(BF16), right.astype(BF16)], 1)
                bottom = bottom + dot(mixing, own)
            put(block, slice(base, base + half), columns, top)
            put(block, slice(base + half, base + BLOCK), columns, bottom)


def local_kernel(first_head, x_ref, cum_ref, row_ref, score_ref, skip_ref, *refs):
    out_ref = refs[-1]

    def put(block, rows, columns, value):
        out_ref[rows, columns] = value

    mix(first_head, x_ref, cum_ref, row_ref, score_ref, skip_ref, put)


def carry(first_head, core, lasts, befores, own_ref, c_ref, factor_ref, add, keep_ref, send_ref):
    expand = spread(first_head, own_ref.shape[1], 2)
    last, before = (
        refs[0][...] if len(refs) == 1 else jnp.concatenate([ref[...] for ref in refs], 1)
        for refs in (lasts, befores)
    )
    held = last[:STATE].astype(F32) + decay_of(last) * before[:STATE].astype(F32)
    factor = dot(factor_ref[...], expand)
    outs = []
    for block in range(PAIR):
        at = slice(block * BLOCK, (block + 1) * BLOCK)
        carried = dot(c_ref[at], held.astype(BF16))
        outs.append((add[at] + factor[at] * carried).astype(BF16))
        held = factor[BLOCK - 1 : BLOCK] * held + own_ref[...]

    @pl.when(core == 0)
    def _():
        keep_ref[...] = outs[0]
        send_ref[...] = outs[1]

    @pl.when(core == 1)
    def _():
        keep_ref[...] = outs[1]
        send_ref[...] = outs[0]


def final_kernel(first_head, lasts, befores, place, *refs):
    last, refs = refs[:lasts], refs[lasts:]
    before, refs = refs[:befores], refs[befores:]
    carry(first_head, place[2], last, before, *refs[:4], *refs[-2:])


def finish_kernel(first_head, lasts, befores, place, *refs):
    last, refs = refs[:lasts], refs[lasts:]
    before, refs = refs[:befores], refs[befores:]
    own_ref, c_ref, factor_ref = refs[:3]
    keep_ref, send_ref, partial = refs[-3:]
    local_kernel(first_head, *refs[3:8], partial)
    carry(first_head, place[2], last, before, own_ref, c_ref, factor_ref, partial, keep_ref, send_ref)


def place_kernel(firsts, place, *refs):
    count = len(firsts)
    keeps, gots = refs[:count], refs[count : 2 * count]
    out, sems = refs[-2:]
    core = place[2]
    half = out.shape[1] // PAIR
    copies = []
    for first, keep, got in zip(firsts, keeps, gots):
        width = keep.shape[1]
        copies.append((keep, out.at[:, ds(core * half + first, width)]))
        copies.append((got, out.at[:, ds((1 - core) * half + first, width)]))
    for copy in run(copies, sems):
        copy.wait()


def put_in_place(firsts, shape, place, keeps, gots, before):
    smem, vmem, hbm = (pl.BlockSpec(memory_space=m) for m in (pltpu.SMEM, pltpu.VMEM, pltpu.HBM))
    count = len(firsts)
    return pl.pallas_call(
        functools.partial(place_kernel, firsts),
        out_shape=jax.ShapeDtypeStruct(shape, BF16),
        in_specs=[smem] + [vmem] * (2 * count) + [hbm] * len(before),
        out_specs=hbm,
        input_output_aliases={2 * count + 1: 0} if before else {},
        scratch_shapes=[pltpu.SemaphoreType.DMA((2 * count,))],
        compiler_params=pltpu.CompilerParams(vmem_limit_bytes=16 << 20),
        cost_estimate=pl.CostEstimate(flops=1, bytes_accessed=1, transcendentals=0),
        name="place",
    )(place, *keeps, *gots, *before)


class Stay:
    def __init__(self, array):
        self.array = array


def call(body, outs, operands, scratch=(), flops=0, transcendentals=0, name=None, limit=16 << 20):
    shapes = [jax.ShapeDtypeStruct(shape, dtype) for shape, dtype in outs]
    smem, vmem, hbm = (pl.BlockSpec(memory_space=m) for m in (pltpu.SMEM, pltpu.VMEM, pltpu.HBM))
    specs = [
        hbm if isinstance(o, Stay) else smem if o.dtype == jnp.int32 else vmem for o in operands
    ]
    moved = sum(o.size * o.dtype.itemsize for o in shapes) * 2
    return pl.pallas_call(
        body,
        out_shape=shapes,
        in_specs=specs,
        out_specs=[vmem] * len(outs),
        scratch_shapes=scratch,
        compiler_params=pltpu.CompilerParams(vmem_limit_bytes=limit),
        cost_estimate=pl.CostEstimate(flops=1, bytes_accessed=1, transcendentals=0),
        name=name,
    )(*[o.array if isinstance(o, Stay) else o for o in operands])


def paired(xbc, dt_raw, conv_weight, conv_bias, a_log, dt_bias, skip_gain):
    axes = ("ctx", "head")
    shards, length = lax.axis_size("head"), lax.axis_size("ctx")
    devices, peers = shards * length, shards * PAIR
    tok = xbc.shape[0]
    slab = tok * peers
    context, shard = lax.axis_index("ctx"), lax.axis_index("head")
    pair, core = context // PAIR, context % PAIR
    group = shard * PAIR + core
    place = jnp.stack([group, pair, core, core * shards + shard, shard]).astype(jnp.int32)

    def over(block, target):
        route = [(i, target(i)) for i in range(devices)]
        return lax.ppermute(block, axes, [(i, j) for i, j in route if j is not None and j < devices])

    def swap(block):
        return over(block, lambda i: i ^ shards)

    rows = Stay(xbc)
    size = PER_GROUP + 2 * STATE
    sent, near, far = call(
        functools.partial(pack_kernel, shards),
        [((tok, shards * size + HEADS), BF16), ((3, shards * size), BF16), ((3, shards * size), BF16)],
        [place, rows, Stay(dt_raw)],
        scratch=[pltpu.VMEM((16, xbc.shape[1]), BF16), pltpu.SemaphoreType.DMA((3 * shards + 2,))],
        name="pack",
    )
    near = over(near, lambda i: i + peers if i % peers == peers - 1 else None)
    far = over(far, lambda i: i + shards if i % peers == peers - 1 else None)
    got = swap(sent)
    taps, offset = call(
        taps_kernel,
        [((4, size), F32), ((1, size), F32)],
        [place, Stay(conv_weight), Stay(conv_bias[None]), Stay(got)],
        scratch=[pltpu.SemaphoreType.DMA((6,))],
        name="taps",
    )

    def travel(piece, order):
        steps = "D" in RESTS[piece]
        (blocks,) = call(
            functools.partial(merge_kernel, shards, piece, len(order)),
            [((shards, PAIR * tok, total_of(piece)), BF16)],
            [place, rows, dt_raw if steps else Stay(dt_raw), got]
            + [o if steps else Stay(o) for o in (near, far)]
            + [Stay(o) for o in order],
            scratch=[pltpu.SemaphoreType.DMA((shards * (2 + 4 * ("C" in RESTS[piece])),))],
            name="merge",
        )
        return blocks, lax.all_to_all(blocks, "head", 0, 0, tiled=True)

    message, order = [], []
    for piece in range(len(WIDTHS)):
        blocks, arrived = travel(piece, order)
        message.append(arrived)
        order = [blocks]

    tiles = [p.reshape(HEADS // LANES, LANES) for p in (a_log, dt_bias, skip_gain)]
    b, edge, cum, row, factor, tail, skip = call(
        functools.partial(prep_kernel, shards),
        [
            ((slab, STATE), BF16),
            ((4, size), F32),
            ((slab, LANES), F32),
            ((LANES, slab), F32),
            ((slab, 2 * LANES), BF16),
            ((slab, 2 * LANES), BF16),
            ((16, 3 * LANES), BF16),
        ],
        [place, message[0], taps, offset] + tiles + [Stay(blocks)],
        scratch=[pltpu.VMEM((slab, LANES), F32), pltpu.VMEM((slab + 8, STATE), F32)],
        name="prep",
    )
    count = len(GROUPED)
    x, sent, own, last, joined, before, keep, send = ([None] * count for _ in range(8))

    def first_head(i):
        return (sum(WIDTHS[: GROUPED[i][0]]) + GROUPED[i][1]) // HEAD_DIM

    def state_of(i, order):
        piece, _, width = GROUPED[i]
        x[i], own[i], *sent[i] = call(
            functools.partial(state_kernel, GROUPED[i], ROUNDS[i]),
            [((slab, width), BF16), ((STATE, width), F32)] + [((STATE + 16, w), BF16) for w in ROUNDS[i]],
            [message[piece], taps, offset, edge, b, factor, tail] + [Stay(o) for o in order],
            scratch=[pltpu.VMEM((slab + 8, width), F32)],
            name="state",
        )
        last[i] = [over(part, lambda i: i + peers) for part in sent[i]]

    def combine_of(i, order):
        joined[i], before[i] = [], []
        for j, width in enumerate(ROUNDS[i]):
            (total,) = call(
                functools.partial(combine_kernel, 1),
                [((STATE + 16, width), BF16)],
                [last[i][j], sent[i][j]] + [Stay(o) for o in order],
                name="combine",
            )
            joined[i].append(total)
            before[i].append(over(total, lambda i: i + 2 * peers))
            order = [total]

    def finish_of(body, i, operands, order, **more):
        keep[i], send[i] = call(
            functools.partial(body, first_head(i), len(last[i]), len(before[i])),
            [((BLOCK, GROUPED[i][2]), BF16)] * 2,
            [place, *last[i], *before[i], own[i], c, factor] + operands + [Stay(o) for o in order],
            name="final",
            **more,
        )

    state_of(0, [])
    c, score = call(
        score_kernel,
        [((slab, STATE), BF16), ((slab, BLOCK), F32)],
        [message[0], taps, offset, edge, b] + [Stay(o) for o in sent[0]],
        scratch=[pltpu.VMEM((slab + 8, STATE), F32)],
        name="score",
    )
    mixes = [cum, row, score, skip]

    def in_full(i, order):
        wide = [pltpu.VMEM((slab, GROUPED[i][2]), F32)]
        finish_of(finish_kernel, i, [x[i]] + mixes, order, scratch=wide)

    shape = (BLOCK, PAIR * PER_GROUP)
    combine_of(0, [score])
    in_full(0, joined[0])
    out = put_in_place([0], shape, place, keep[:1], [swap(send[0])], [])
    state_of(1, [keep[0]])
    combine_of(1, [])
    (partial,) = call(
        functools.partial(local_kernel, first_head(1)),
        [(x[1].shape, F32)],
        [x[1]] + mixes + [Stay(o) for o in joined[1]],
        name="local",
    )
    state_of(2, [partial])
    finish_of(final_kernel, 1, [partial], sent[2])
    combine_of(2, [keep[1]])
    (partial,) = call(
        functools.partial(local_kernel, first_head(2)),
        [(x[2].shape, F32)],
        [x[2]] + mixes + [Stay(o) for o in joined[2]],
        name="local",
    )
    out = put_in_place([first_head(1) * HEAD_DIM], shape, place, keep[1:2], [swap(send[1])], [out])
    finish_of(final_kernel, 2, [partial], [out])
    return put_in_place([first_head(2) * HEAD_DIM], shape, place, keep[2:], [swap(send[2])], [out])


def solution(mesh):
    in_specs = (P(("ctx", "head"), None), P(("ctx", "head"), None), P(), P(), P(), P(), P())
    out_specs = P("ctx", "head")
    shards, length = mesh.shape["head"], mesh.shape["ctx"]

    def program(xbc, *rest):
        slab = xbc.shape[0] // length
        fits = shards == GROUPS // PAIR and length == 4 * PAIR and slab == BLOCK
        return jax.shard_map(
            paired if fits else on_device,
            mesh=mesh,
            in_specs=in_specs,
            out_specs=out_specs,
            check_vma=False,
        )(xbc, *rest)

    return program
```

```python
import functools

import jax
import jax.numpy as jnp
from jax import lax
from jax.experimental import pallas as pl
from jax.experimental.pallas import tpu as pltpu
from jax.sharding import PartitionSpec as P

HEADS = 256
HEAD_DIM = 64
STATE = 256
GROUPS = 8
BLOCK = 256


def from_behind(block, axis, distance):
    devices = range(lax.axis_size(axis))
    route = [(i - distance, i) for i in devices if i - distance in devices]
    return lax.ppermute(block, axis, route)


def carried_in(array, axis, combine, identity):
    length, index = (lax.axis_size(axis), lax.axis_index(axis))
    everything = jax.tree.map(lambda part: lax.all_gather(part, axis), array)
    start = jax.tree.map(
        lambda part, zero: jnp.broadcast_to(jnp.asarray(zero, part.dtype), part.shape),
        array,
        identity,
    )

    def hop(k, before):
        reached = k < index
        new = combine(before, jax.tree.map(lambda part: part[k], everything))
        return jax.tree.map(lambda a, b: jnp.where(reached, a, b), new, before)

    return lax.fori_loop(0, length, hop, start)


def convolve(rows, edge, weight, bias):
    count = rows.shape[0]
    wide = jnp.concatenate([edge, rows], 0).astype(jnp.float32)
    acc = bias[None, :] + weight[0] * wide[0:count]
    acc = acc + weight[1] * wide[1 : count + 1]
    acc = acc + weight[2] * wide[2 : count + 2]
    acc = acc + weight[3] * wide[3 : count + 3]
    return jax.nn.silu(acc).astype(jnp.bfloat16)


def rearrange_heads(rows, shards, per_dev, groups_dev, per_group):
    count = rows.shape[0]
    inner = HEADS * HEAD_DIM
    replicate_groups = max(1, per_group // per_dev)
    heads_part = rows[:, :inner].reshape(count, shards, per_dev * HEAD_DIM)
    b_part = rows[:, inner : inner + GROUPS * STATE].reshape(count, GROUPS, STATE)
    c_part = rows[:, inner + GROUPS * STATE :].reshape(count, GROUPS, STATE)
    b_part = jnp.repeat(b_part, replicate_groups, axis=1).reshape(count, shards, groups_dev * STATE)
    c_part = jnp.repeat(c_part, replicate_groups, axis=1).reshape(count, shards, groups_dev * STATE)
    return jnp.concatenate([heads_part, b_part, c_part], axis=2)


def inner_block(xs, bmat, cmat, steps, cum):
    size = xs.shape[0]
    lower = jnp.arange(size)[:, None] >= jnp.arange(size)[None, :]
    scores = jnp.einsum("qgn,kgn->gqk", cmat, bmat, preferred_element_type=jnp.float32)
    order = jnp.transpose(cum, (1, 2, 0))
    gap = order[..., :, None] - order[..., None, :]
    decay = jnp.exp(jnp.where(lower, gap, -jnp.inf))
    mixing = (scores[:, None] * decay * jnp.transpose(steps, (1, 2, 0))[..., None, :]).astype(
        jnp.bfloat16
    )
    local = jnp.einsum("gjqk,kgjp->qgjp", mixing, xs, preferred_element_type=jnp.float32)
    tail = jnp.exp(cum[size - 1][None] - cum) * steps
    loaded = (bmat[:, :, None, :].astype(jnp.float32) * tail[..., None]).astype(jnp.bfloat16)
    block_state = jnp.einsum("kgjn,kgjp->gjnp", loaded, xs, preferred_element_type=jnp.float32)
    return (local, block_state)


def on_device(xbc, dt_raw, conv_weight, conv_bias, a_log, dt_bias, skip_gain):
    tok = xbc.shape[0]
    shards = lax.axis_size("head")
    per_dev = HEADS // shards
    per_group = HEADS // GROUPS
    groups_dev = max(1, per_dev // per_group)
    heads_per_cluster = per_dev // groups_dev
    sent = rearrange_heads(xbc, shards, per_dev, groups_dev, per_group)
    mine, rates = (
        lax.all_to_all(sent, "head", split_axis=1, concat_axis=0, tiled=True),
        lax.all_to_all(
            dt_raw.reshape(tok, shards, per_dev), "head", split_axis=1, concat_axis=0, tiled=True
        ),
    )
    slab = tok * shards
    mine = mine.reshape(slab, mine.shape[2])
    rates = rates.reshape(slab, per_dev)
    shard = lax.axis_index("head")
    taps = lax.dynamic_index_in_dim(
        rearrange_heads(conv_weight, shards, per_dev, groups_dev, per_group),
        shard,
        1,
        keepdims=False,
    )
    offset = lax.dynamic_index_in_dim(
        rearrange_heads(conv_bias[None, :], shards, per_dev, groups_dev, per_group),
        shard,
        1,
        keepdims=False,
    )
    edge = from_behind(mine[slab - 3 :], "ctx", 1)
    mine = convolve(mine, edge, taps, offset[0])
    nchunk = slab // BLOCK
    width = per_dev * HEAD_DIM
    xs = mine[:, :width].reshape(nchunk, BLOCK, groups_dev, heads_per_cluster, HEAD_DIM)
    bmat = mine[:, width : width + groups_dev * STATE].reshape(nchunk, BLOCK, groups_dev, STATE)
    cmat = mine[:, width + groups_dev * STATE :].reshape(nchunk, BLOCK, groups_dev, STATE)
    first = shard * per_dev
    rate = (-jnp.exp(lax.dynamic_slice_in_dim(a_log, first, per_dev))).reshape(
        groups_dev, heads_per_cluster
    )
    bias_dt = lax.dynamic_slice_in_dim(dt_bias, first, per_dev).reshape(
        groups_dev, heads_per_cluster
    )
    skip = lax.dynamic_slice_in_dim(skip_gain, first, per_dev).reshape(
        groups_dev, heads_per_cluster
    )
    steps = jax.nn.softplus(
        rates.astype(jnp.float32).reshape(nchunk, BLOCK, groups_dev, heads_per_cluster) + bias_dt
    )
    cum = jnp.cumsum(steps * rate, axis=1)

    def block_step(carry, item):
        held, product = carry
        x_part, b_part, c_part, step_part, cum_part = item
        local, block_state = inner_block(x_part, b_part, c_part, step_part, cum_part)
        lifted = c_part.astype(jnp.float32)[:, :, None, :] * jnp.exp(cum_part)[..., None]
        carried = jnp.einsum("qgjn,gjnp->qgjp", lifted, held, precision=lax.Precision.HIGHEST)
        partial_out = local + carried + skip[..., None] * x_part.astype(jnp.float32)
        end = jnp.exp(cum_part[BLOCK - 1])
        return ((end[..., None, None] * held + block_state, product * end), (partial_out, product))

    zero_state = jnp.zeros((groups_dev, heads_per_cluster, STATE, HEAD_DIM), jnp.float32)
    unit = jnp.ones((groups_dev, heads_per_cluster), jnp.float32)
    (slab_state, slab_decay), (partials, product_in) = lax.scan(
        block_step, (zero_state, unit), (xs, bmat, cmat, steps, cum)
    )

    def combine(preceding_state, later):
        return (
            preceding_state[0] * later[0],
            later[0][..., None, None] * preceding_state[1] + later[1],
        )

    _, entering = carried_in((slab_decay, slab_state), "ctx", combine, (unit, zero_state))
    projected = jnp.einsum(
        "cqgn,gjnp->cqgjp", cmat.astype(jnp.float32), entering, precision=lax.Precision.HIGHEST
    )
    factor = jnp.exp(cum) * product_in[:, None]
    total = partials + factor[..., None] * projected
    return total.astype(jnp.bfloat16).reshape(slab, width)


PAIR = 2
LANES = 128
LOG2E = 1.4426950408889634
F32, BF16 = jnp.float32, jnp.bfloat16
WIDTHS = (768, 1280)
RESTS = ("BCD", "")
GROUPED = ((0, 0, 768), (1, 0, 512), (1, 512, 384), (1, 896, 384))
ROUNDS = ((256, 256, 256), (512,), (384,), (384,))


def halves(value, count):
    parts = []
    for _ in range(count):
        part = value.astype(BF16)
        parts.append(part)
        value = value - part.astype(F32)
    return parts


def spread(first_head, width, copies):
    lane = lax.broadcasted_iota(jnp.int32, (copies * LANES, width), 0) % LANES
    column = lax.broadcasted_iota(jnp.int32, (copies * LANES, width), 1)
    return (lane == first_head + column // HEAD_DIM).astype(BF16)


def dot(a, b):
    return jnp.dot(a, b, preferred_element_type=F32)


def ds(start, width):
    return pl.ds(pl.multiple_of(start, LANES), width)


def run(copies, sems):
    started = []
    for i, (source, target) in enumerate(copies):
        copy = pltpu.make_async_copy(source, target, sems.at[i])
        copy.start()
        started.append(copy)
    return started


PER_GROUP = HEADS * HEAD_DIM // GROUPS
INNER = HEADS * HEAD_DIM


def channels(group, first, width):
    return ds(group * PER_GROUP + first, width)


def runs(group):
    yield group * PER_GROUP, PER_GROUP
    yield INNER + group * STATE, STATE
    yield INNER + (GROUPS + group) * STATE, STATE


def pack_kernel(shards, place, xbc, dt_raw, send, near, far, tail, sems):
    core, shard = place[2], place[4]
    count = xbc.shape[0]
    copies = [(xbc.at[count - 16 :], tail)]
    to = 0
    for r in range(shards):
        for start, width in runs((shard ^ r) * PAIR + 1 - core):
            copies.append((xbc.at[:, ds(start, width)], send.at[:, to : to + width]))
            to += width
    copies.append((dt_raw, send.at[:, to:]))
    started = run(copies, sems)
    started[0].wait()
    for edge, side in ((near, 1), (far, 0)):
        to = 0
        for r in range(shards):
            for start, width in runs(((shards - 1) ^ r) * PAIR + side):
                rows = tail[:, start : start + width].astype(F32)
                edge[:, to : to + width] = rows[13:16].astype(BF16)
                to += width
    for copy in started[1:]:
        copy.wait()


def taps_kernel(place, weight, bias, order, taps, offset, sems):
    copies, to = [], 0
    for start, width in runs(place[0]):
        copies.append((weight.at[:, ds(start, width)], taps.at[:, to : to + width]))
        copies.append((bias.at[:, ds(start, width)], offset.at[:, to : to + width]))
        to += width
    for copy in run(copies, sems):
        copy.wait()


def total_of(piece):
    return WIDTHS[piece] + sum(LANES if kind == "D" else STATE for kind in RESTS[piece])


def view(refs, piece):
    origin = sum(map(total_of, range(piece)))
    return [(ref, origin if r < 2 else 0) for r, ref in enumerate(refs)]


def merge_kernel(shards, plan, unread, place, xbc, dt_raw, got, near, far, *refs):
    refs = refs[unread:]
    outs, sems = refs[: len(plan)], refs[len(plan)]
    core, shard = place[2], place[4]
    count = xbc.shape[0]
    size = PER_GROUP + 2 * STATE
    mine = pl.ds(pl.multiple_of(core * count, count), count)
    other = pl.ds(pl.multiple_of((1 - core) * count, count), count)
    copies, steps = [], []
    for out, (r, pieces) in zip(outs, plan):
        group = (shard ^ r) * PAIR + core
        to = 0
        for piece in pieces:
            first, width = sum(WIDTHS[:piece]), WIDTHS[piece]
            parts = [(group * PER_GROUP + first, r * size + first, width)]
            for i, kind in enumerate("BC"):
                if kind in RESTS[piece]:
                    at = INNER + (i * GROUPS + group) * STATE
                    parts.append((at, r * size + PER_GROUP + i * STATE, STATE))
            for own, theirs, width in parts:
                copies.append((xbc.at[:, ds(own, width)], out.at[mine, to : to + width]))
                copies.append((got.at[:, theirs : theirs + width], out.at[other, to : to + width]))
                to += width
            if "D" in RESTS[piece]:
                steps.append((out, r, to))
                to += LANES
    started = run(copies, sems)
    if steps:
        lane = lax.broadcasted_iota(jnp.int32, (count, LANES), 1)
        per_tile = LANES * GROUPS // HEADS
        heads = HEADS // GROUPS
        for out, r, to in steps:
            group = (shard ^ r) * PAIR + core
            tile, shift = group // per_tile, (LANES - (group % per_tile) * heads) % LANES
            own = dt_raw[:, ds(tile * LANES, LANES)].astype(F32)
            theirs = got[:, ds(got.shape[1] - HEADS + tile * LANES, LANES)].astype(F32)
            low = jnp.where(core == 0, own, theirs)
            high = jnp.where(core == 0, theirs, own)
            packed = jnp.zeros((count // 2, LANES), F32)
            for j, rows in enumerate((low, high)):
                rows = jnp.where(lane < heads, pltpu.roll(rows, shift, 1), 0.0)
                for i in range(2):
                    part = rows[i * count // 2 : (i + 1) * count // 2]
                    packed = packed + pltpu.roll(part, (2 * j + i) * heads, 1)
            out[: count // 2, to : to + LANES] = packed.astype(BF16)
            size = PER_GROUP + 2 * STATE
            at = slice(r * size, (r + 1) * size)
            edge = near[:, at].astype(F32) + far[:, at].astype(F32)
            edge = jnp.concatenate([edge, jnp.zeros((1, size), F32)], 0)
            edge = jnp.concatenate([edge[:, q * LANES : (q + 1) * LANES] for q in range(size // LANES)], 0)
            fill = jnp.zeros((PAIR * count - count // 2 - edge.shape[0], LANES), F32)
            out[count // 2 :, to : to + LANES] = jnp.concatenate([edge, fill], 0).astype(BF16)
    for copy in started:
        copy.wait()


def convolve_in_order(place, blocks, columns, edge, tap, bias, wide, put):
    width = columns.stop - columns.start
    count = blocks[0][0].shape[0] // PAIR
    wide[5:8, :width] = edge
    for r, (block, origin) in enumerate(blocks):
        for core in range(PAIR):
            at = pl.multiple_of((core * len(blocks) + (place[4] ^ r)) * count + 8, 8)
            part = block[core * count : (core + 1) * count, origin + columns.start : origin + columns.stop]
            wide[pl.ds(at, count), :width] = part.astype(F32)
    tap, bias = tap * 0.5, bias * 0.5
    for start in range(0, PAIR * len(blocks) * count, count):
        acc = bias + tap[0:1] * wide[start + 5 : start + 5 + count, :width]
        acc = acc + tap[1:2] * wide[start + 6 : start + 6 + count, :width]
        acc = acc + tap[2:3] * wide[start + 7 : start + 7 + count, :width]
        acc = acc + tap[3:4] * wide[start + 8 : start + 8 + count, :width]
        put(start, count, (acc + acc * jnp.tanh(acc)).astype(BF16))


def prep_kernel(shards, place, *refs):
    blocks, (taps, offset, a_ref, bias_ref, skip_ref, order) = refs[:shards], refs[shards : shards + 6]
    b_ref, edge_ref, cum_ref, row_ref, factor_ref, tail_ref, skip_out, dt_ref, wide = refs[shards + 6 :]
    blocks = view(blocks, 0)
    start = WIDTHS[0]
    last = total_of(0) - LANES
    size = edge_ref.shape[1]
    count = blocks[0][0].shape[0] // PAIR
    half, heads = count // 2, HEADS // GROUPS
    columns = [block[:, last : last + LANES].astype(F32) for block, _ in blocks]
    edge = columns[0][half : half + 4 * size // LANES]
    for column in columns[1:]:
        edge = edge + column[half : half + 4 * size // LANES]
    for q in range(size // LANES):
        edge_ref[:, q * LANES : (q + 1) * LANES] = edge[4 * q : 4 * q + 4]
    for r, column in enumerate(columns):
        packed = column[:half]
        for j in range(2 * PAIR):
            at = ((j // 2) * shards + (place[4] ^ r)) * count + (j % 2) * half
            rows = packed if j == 0 else pltpu.roll(packed, LANES - j * heads, 1)
            dt_ref[pl.ds(pl.multiple_of(at, half), half), :] = rows

    def put(start, count, value):
        b_ref[start : start + count] = value

    at = slice(PER_GROUP, PER_GROUP + STATE)
    convolve_in_order(
        place, blocks, slice(start, start + STATE), edge_ref[0:3, at], taps[:, at], offset[:, at], wide, put
    )
    per_tile = LANES * GROUPS // HEADS
    group = place[0]
    tile = group // per_tile
    shift = (LANES - (group % per_tile) * heads) % LANES

    def lanes_of(ref):
        return pltpu.roll(jnp.broadcast_to(ref[pl.ds(tile, 1), :], (8, LANES)), shift, 1)

    rate = -jnp.exp(lanes_of(a_ref)[0:1])
    raw = dt_ref[...] + lanes_of(bias_ref)[0:1]
    step = jnp.maximum(raw, 0.0) + jnp.log1p(jnp.exp(-jnp.abs(raw)))
    skip = lanes_of(skip_ref)
    skip_out[...] = jnp.concatenate(halves(jnp.concatenate([skip, skip], 0), 3), 1)
    lower = (
        lax.broadcasted_iota(jnp.int32, (BLOCK, BLOCK), 0)
        >= lax.broadcasted_iota(jnp.int32, (BLOCK, BLOCK), 1)
    ).astype(BF16)
    valid = lax.broadcasted_iota(jnp.int32, (BLOCK, LANES), 1) < heads
    for block in range(PAIR):
        at = slice(block * BLOCK, (block + 1) * BLOCK)
        here = jnp.where(valid, step[at], 1.0)
        parts = halves(here * rate, 3)
        cum = dot(lower, parts[0]) + (dot(lower, parts[1]) + dot(lower, parts[2]))
        cum = cum * LOG2E
        cum_ref[at] = cum
        row_ref[:, at] = jnp.transpose(cum - jnp.log2(here))
        factor_ref[at] = jnp.concatenate(halves(jnp.exp2(cum), 2), 1)
        tail = jnp.exp2(cum[BLOCK - 1 :] - cum) * here
        tail_ref[at] = jnp.concatenate(halves(tail, 2), 1)


def score_kernel(shards, place, *refs):
    blocks, refs = refs[:shards], refs[shards:]
    taps, offset, edge_ref, b_ref, c_ref, score_ref, wide = (*refs[:4], *refs[-3:])
    blocks = view(blocks, 0)
    start = WIDTHS[0] + STATE
    at = slice(PER_GROUP + STATE, PER_GROUP + 2 * STATE)

    def put(start, count, value):
        c_ref[start : start + count] = value

    convolve_in_order(
        place, blocks, slice(start, start + STATE), edge_ref[0:3, at], taps[:, at], offset[:, at], wide, put
    )
    for block in range(PAIR):
        at = slice(block * BLOCK, (block + 1) * BLOCK)
        score_ref[at] = lax.dot_general(
            c_ref[at], b_ref[at], (((1,), (1,)), ((), ())), preferred_element_type=F32
        )


def decay_of(ref):
    decay = ref[STATE : STATE + 16].astype(F32)
    return decay[0:1] + (decay[1:2] + decay[2:3])


def put_decay(ref, decay):
    row = lax.broadcasted_iota(jnp.int32, (16, ref.shape[1]), 0)
    high, middle, low = (part.astype(F32) for part in halves(decay, 3))
    packed = jnp.where(row == 0, high, jnp.where(row == 1, middle, jnp.where(row == 2, low, 0.0)))
    ref[STATE:] = packed.astype(BF16)


def state_kernel(shards, part, sizes, place, *refs):
    blocks, refs = refs[:shards], refs[shards:]
    taps, offset, edge_ref, b_ref, factor_ref, tail_ref = refs[:6]
    x_ref, own_ref, *sends, wide = refs[-3 - len(sizes) :]
    piece, start, width = part
    first = sum(WIDTHS[:piece]) + start
    at = slice(first, first + width)

    def put(row, count, value):
        x_ref[row : row + count] = value

    blocks = view(blocks, piece)
    columns = slice(start, start + width)
    convolve_in_order(place, blocks, columns, edge_ref[0:3, at], taps[:, at], offset[:, at], wide, put)
    expand = spread(first // HEAD_DIM, width, 2)
    both = []
    for block in range(PAIR):
        at = slice(block * BLOCK, (block + 1) * BLOCK)
        loaded = (x_ref[at].astype(F32) * dot(tail_ref[at], expand)).astype(BF16)
        both.append(
            lax.dot_general(b_ref[at], loaded, (((0,), (0,)), ((), ())), preferred_element_type=F32)
        )
    ends = [dot(factor_ref[(i + 1) * BLOCK - 16 : (i + 1) * BLOCK], expand)[15:16] for i in range(PAIR)]
    own_ref[...] = both[0]
    end = (ends[1] * both[0] + both[1]).astype(BF16)
    decay = ends[0] * ends[1]
    start = 0
    for send_ref in sends:
        at = slice(start, start + send_ref.shape[1])
        send_ref[0:STATE] = end[:, at]
        put_decay(send_ref, decay[:, at])
        start = at.stop


def combine_kernel(count, *refs):
    early, late, out_ref = refs[:count], refs[count : 2 * count], refs[-1]
    start = 0
    for early_ref, late_ref in zip(early, late):
        at = slice(start, start + late_ref.shape[1])
        decay = decay_of(late_ref)
        total = decay * early_ref[:STATE].astype(F32) + late_ref[:STATE].astype(F32)
        out_ref[:STATE, at] = total.astype(BF16)
        put_decay(out_ref.at[:, at], decay * decay_of(early_ref))
        start = at.stop


def mix(first_head, x_ref, cum_ref, row_ref, score_ref, skip_ref, put):
    width = x_ref.shape[1]
    half = BLOCK // 2
    expand = spread(first_head, width, 3)
    skip = dot(skip_ref[...], expand)[0:1]
    lower = lax.broadcasted_iota(jnp.int32, (half, half), 0) >= lax.broadcasted_iota(
        jnp.int32, (half, half), 1
    )
    lane = lax.broadcasted_iota(jnp.int32, (BLOCK, LANES), 1)
    for block in range(PAIR):
        base = block * BLOCK
        for tile in range(width // LANES):
            columns = slice(tile * LANES, (tile + 1) * LANES)
            x = x_ref[base : base + BLOCK, columns]
            top = skip[:, columns] * x[:half].astype(F32)
            bottom = skip[:, columns] * x[half:].astype(F32)
            for side in range(LANES // HEAD_DIM):
                head = first_head + tile * (LANES // HEAD_DIM) + side
                own = jnp.where(lane // HEAD_DIM == side, x, jnp.zeros_like(x))
                cum = cum_ref[base : base + BLOCK, head : head + 1]
                row = row_ref[head : head + 1, base : base + BLOCK]
                diag = jnp.where(lower, cum[:half] - row[:, :half], -1e30)
                mixing = jnp.exp2(diag) * score_ref[base : base + half, :half]
                top = top + dot(mixing.astype(BF16), own[:half])
                left = jnp.exp2(cum[half:] - row[:, :half]) * score_ref[base + half : base + BLOCK, :half]
                diag = jnp.where(lower, cum[half:] - row[:, half:], -1e30)
                right = jnp.exp2(diag) * score_ref[base + half : base + BLOCK, half:]
                mixing = jnp.concatenate([left.astype(BF16), right.astype(BF16)], 1)
                bottom = bottom + dot(mixing, own)
            put(block, slice(base, base + half), columns, top)
            put(block, slice(base + half, base + BLOCK), columns, bottom)


def local_kernel(first_head, x_ref, cum_ref, row_ref, score_ref, skip_ref, *refs):
    out_ref = refs[-1]

    def put(block, rows, columns, value):
        out_ref[rows, columns] = value

    mix(first_head, x_ref, cum_ref, row_ref, score_ref, skip_ref, put)


def carry(first_head, core, lasts, befores, own_ref, c_ref, factor_ref, add, keep_ref, send_ref):
    expand = spread(first_head, own_ref.shape[1], 2)
    last, before = (
        refs[0][...] if len(refs) == 1 else jnp.concatenate([ref[...] for ref in refs], 1)
        for refs in (lasts, befores)
    )
    held = last[:STATE].astype(F32) + decay_of(last) * before[:STATE].astype(F32)
    factor = dot(factor_ref[...], expand)
    outs = []
    for block in range(PAIR):
        at = slice(block * BLOCK, (block + 1) * BLOCK)
        carried = dot(c_ref[at], held.astype(BF16))
        outs.append((add[at] + factor[at] * carried).astype(BF16))
        held = factor[BLOCK - 1 : BLOCK] * held + own_ref[...]

    @pl.when(core == 0)
    def _():
        keep_ref[...] = outs[0]
        send_ref[...] = outs[1]

    @pl.when(core == 1)
    def _():
        keep_ref[...] = outs[1]
        send_ref[...] = outs[0]


def final_kernel(first_head, lasts, befores, place, *refs):
    last, refs = refs[:lasts], refs[lasts:]
    before, refs = refs[:befores], refs[befores:]
    carry(first_head, place[2], last, before, *refs[:4], *refs[-2:])


def finish_kernel(first_head, lasts, befores, place, *refs):
    last, refs = refs[:lasts], refs[lasts:]
    before, refs = refs[:befores], refs[befores:]
    own_ref, c_ref, factor_ref = refs[:3]
    keep_ref, send_ref, partial = refs[-3:]
    local_kernel(first_head, *refs[3:8], partial)
    carry(first_head, place[2], last, before, own_ref, c_ref, factor_ref, partial, keep_ref, send_ref)


def place_kernel(firsts, place, *refs):
    count = len(firsts)
    keeps, gots = refs[:count], refs[count : 2 * count]
    out, token, sems = refs[-3:]
    token[...] = jnp.zeros_like(token)
    core = place[2]
    half = out.shape[1] // PAIR
    copies = []
    for first, keep, got in zip(firsts, keeps, gots):
        width = keep.shape[1]
        copies.append((keep, out.at[:, ds(core * half + first, width)]))
        copies.append((got, out.at[:, ds((1 - core) * half + first, width)]))
    for copy in run(copies, sems):
        copy.wait()


def put_in_place(firsts, shape, place, keeps, gots, before):
    smem, vmem, hbm = (pl.BlockSpec(memory_space=m) for m in (pltpu.SMEM, pltpu.VMEM, pltpu.HBM))
    count = len(firsts)
    return pl.pallas_call(
        functools.partial(place_kernel, firsts),
        out_shape=[jax.ShapeDtypeStruct(shape, BF16), jax.ShapeDtypeStruct((8, LANES), F32)],
        in_specs=[smem] + [vmem] * (2 * count) + [hbm] * len(before),
        out_specs=[hbm, vmem],
        input_output_aliases={2 * count + 1: 0} if before else {},
        scratch_shapes=[pltpu.SemaphoreType.DMA((2 * count,))],
        compiler_params=pltpu.CompilerParams(vmem_limit_bytes=16 << 20),
        cost_estimate=pl.CostEstimate(flops=1, bytes_accessed=1, transcendentals=0),
        name="place",
    )(place, *keeps, *gots, *before)


class Stay:
    def __init__(self, array):
        self.array = array


def call(body, outs, operands, scratch=(), flops=0, transcendentals=0, name=None, limit=16 << 20):
    shapes = [jax.ShapeDtypeStruct(shape, dtype) for shape, dtype in outs]
    smem, vmem, hbm = (pl.BlockSpec(memory_space=m) for m in (pltpu.SMEM, pltpu.VMEM, pltpu.HBM))
    specs = [
        hbm if isinstance(o, Stay) else smem if o.dtype == jnp.int32 else vmem for o in operands
    ]
    moved = sum(o.size * o.dtype.itemsize for o in shapes) * 2
    return pl.pallas_call(
        body,
        out_shape=shapes,
        in_specs=specs,
        out_specs=[vmem] * len(outs),
        scratch_shapes=scratch,
        compiler_params=pltpu.CompilerParams(vmem_limit_bytes=limit),
        cost_estimate=pl.CostEstimate(flops=1, bytes_accessed=1, transcendentals=0),
        name=name,
    )(*[o.array if isinstance(o, Stay) else o for o in operands])


def paired(xbc, dt_raw, conv_weight, conv_bias, a_log, dt_bias, skip_gain):
    axes = ("ctx", "head")
    shards, length = lax.axis_size("head"), lax.axis_size("ctx")
    devices, peers = shards * length, shards * PAIR
    tok = xbc.shape[0]
    slab = tok * peers
    context, shard = lax.axis_index("ctx"), lax.axis_index("head")
    pair, core = context // PAIR, context % PAIR
    group = shard * PAIR + core
    place = jnp.stack([group, pair, core, core * shards + shard, shard]).astype(jnp.int32)

    def over(block, target):
        route = [(i, target(i)) for i in range(devices)]
        return lax.ppermute(block, axes, [(i, j) for i, j in route if j is not None and j < devices])

    def swap(block):
        return over(block, lambda i: i ^ shards)

    rows = Stay(xbc)
    size = PER_GROUP + 2 * STATE
    sent, near, far = call(
        functools.partial(pack_kernel, shards),
        [((tok, shards * size + HEADS), BF16), ((3, shards * size), BF16), ((3, shards * size), BF16)],
        [place, rows, Stay(dt_raw)],
        scratch=[pltpu.VMEM((16, xbc.shape[1]), BF16), pltpu.SemaphoreType.DMA((3 * shards + 2,))],
        name="pack",
    )
    near = over(near, lambda i: i + peers if i % peers == peers - 1 else None)
    far = over(far, lambda i: i + shards if i % peers == peers - 1 else None)
    got = swap(sent)
    taps, offset = call(
        taps_kernel,
        [((4, size), F32), ((1, size), F32)],
        [place, Stay(conv_weight), Stay(conv_bias[None]), Stay(got)],
        scratch=[pltpu.SemaphoreType.DMA((6,))],
        name="taps",
    )

    def merge(plan, order):
        steps = any("D" in RESTS[p] for _, pieces in plan for p in pieces)
        parts = [p for _, pieces in plan for p in pieces]
        return call(
            functools.partial(merge_kernel, shards, plan, len(order)),
            [((PAIR * tok, sum(map(total_of, pieces))), BF16) for _, pieces in plan],
            [place, rows] + [o if steps else Stay(o) for o in (dt_raw,)] + [got]
            + [o if steps else Stay(o) for o in (near, far)]
            + [Stay(o) for o in order],
            scratch=[pltpu.SemaphoreType.DMA((sum(2 + 4 * ("C" in RESTS[p]) for p in parts),))],
            name="merge",
        )

    def across(block, r):
        return over(block, lambda i: i ^ r)

    far_apart = list(range(2, shards))
    first_blocks = merge([(r, (0,)) for r in far_apart] + [(1, (0, 1))], [])
    *far_blocks, near_block = first_blocks
    arrived = [across(block, r) for r, block in zip(far_apart, far_blocks)]
    near_got = across(near_block, 1)
    *third_blocks, own_block = merge([(r, (1,)) for r in far_apart] + [(0, (0, 1))], [first_blocks[0]])
    message = [[own_block, near_got, *arrived]]
    message.append([own_block, near_got] + [across(block, r) for r, block in zip(far_apart, third_blocks)])

    tiles = [p.reshape(HEADS // LANES, LANES) for p in (a_log, dt_bias, skip_gain)]
    b, edge, cum, row, factor, tail, skip = call(
        functools.partial(prep_kernel, shards),
        [
            ((slab, STATE), BF16),
            ((4, size), F32),
            ((slab, LANES), F32),
            ((LANES, slab), F32),
            ((slab, 2 * LANES), BF16),
            ((slab, 2 * LANES), BF16),
            ((16, 3 * LANES), BF16),
        ],
        [place] + message[0] + [taps, offset] + tiles + [Stay(third_blocks[0])],
        scratch=[pltpu.VMEM((slab, LANES), F32), pltpu.VMEM((slab + 8, STATE), F32)],
        name="prep",
    )
    count = len(GROUPED)
    x, sent, own, last, joined, before, keep, send = ([None] * count for _ in range(8))

    def first_head(i):
        return (sum(WIDTHS[: GROUPED[i][0]]) + GROUPED[i][1]) // HEAD_DIM

    def state_of(i, order):
        piece, _, width = GROUPED[i]
        x[i], own[i], *sent[i] = call(
            functools.partial(state_kernel, shards, GROUPED[i], ROUNDS[i]),
            [((slab, width), BF16), ((STATE, width), F32)] + [((STATE + 16, w), BF16) for w in ROUNDS[i]],
            [place] + message[piece] + [taps, offset, edge, b, factor, tail] + [Stay(o) for o in order],
            scratch=[pltpu.VMEM((slab + 8, width), F32)],
            name="state",
        )
        last[i] = [over(part, lambda i: i + peers) for part in sent[i]]

    def combine_of(i, order):
        joined[i], before[i] = [], []
        for j, width in enumerate(ROUNDS[i]):
            (total,) = call(
                functools.partial(combine_kernel, 1),
                [((STATE + 16, width), BF16)],
                [last[i][j], sent[i][j]] + [Stay(o) for o in order],
                name="combine",
            )
            joined[i].append(total)
            before[i].append(over(total, lambda i: i + 2 * peers))
            order = [total]

    def finish_of(body, i, operands, order, **more):
        keep[i], send[i] = call(
            functools.partial(body, first_head(i), len(last[i]), len(before[i])),
            [((BLOCK, GROUPED[i][2]), BF16)] * 2,
            [place, *last[i], *before[i], own[i], c, factor] + operands + [Stay(o) for o in order],
            name="final",
            **more,
        )

    state_of(0, [])
    c, score = call(
        functools.partial(score_kernel, shards),
        [((slab, STATE), BF16), ((slab, BLOCK), F32)],
        [place] + message[0] + [taps, offset, edge, b] + [Stay(o) for o in sent[0]],
        scratch=[pltpu.VMEM((slab + 8, STATE), F32)],
        name="score",
    )
    mixes = [cum, row, score, skip]

    def in_full(i, order):
        wide = [pltpu.VMEM((slab, GROUPED[i][2]), F32)]
        finish_of(finish_kernel, i, [x[i]] + mixes, order, scratch=wide)

    shape = (BLOCK, PAIR * PER_GROUP)
    combine_of(0, [score])
    in_full(0, joined[0])
    out, token = put_in_place([0], shape, place, keep[:1], [swap(send[0])], [])
    partial = {}

    def local_of(i, order):
        (partial[i],) = call(
            functools.partial(local_kernel, first_head(i)),
            [(x[i].shape, F32)],
            [x[i]] + mixes + [Stay(o) for o in order],
            name="local",
        )

    state_of(1, [keep[0]])
    state_of(2, sent[1])
    state_of(3, sent[2])
    combine_of(1, sent[3])
    local_of(1, joined[1] + [token])
    combine_of(2, [partial[1]])
    local_of(2, joined[2])
    local_of(3, [partial[2]])
    combine_of(3, [partial[3]])
    for i in range(1, count):
        finish_of(final_kernel, i, [partial[i]], [keep[i - 1]] if i > 1 else joined[3])
    firsts = [first_head(i) * HEAD_DIM for i in range(1, count)]
    return put_in_place(firsts, shape, place, keep[1:], [swap(o) for o in send[1:]], [out])[0]


def solution(mesh):
    in_specs = (P(("ctx", "head"), None), P(("ctx", "head"), None), P(), P(), P(), P(), P())
    out_specs = P("ctx", "head")
    shards, length = mesh.shape["head"], mesh.shape["ctx"]

    def program(xbc, *rest):
        slab = xbc.shape[0] // length
        fits = shards == GROUPS // PAIR and length == 4 * PAIR and slab == BLOCK
        return jax.shard_map(
            paired if fits else on_device,
            mesh=mesh,
            in_specs=in_specs,
            out_specs=out_specs,
            check_vma=False,
        )(xbc, *rest)

    return program
```

```python
import functools

import jax
import jax.numpy as jnp
from jax import lax
from jax.experimental import pallas as pl
from jax.experimental.pallas import tpu as pltpu
from jax.sharding import PartitionSpec as P

HEADS = 256
HEAD_DIM = 64
STATE = 256
GROUPS = 8
BLOCK = 256


def from_behind(block, axis, distance):
    devices = range(lax.axis_size(axis))
    route = [(i - distance, i) for i in devices if i - distance in devices]
    return lax.ppermute(block, axis, route)


def carried_in(array, axis, combine, identity):
    length, index = (lax.axis_size(axis), lax.axis_index(axis))
    everything = jax.tree.map(lambda part: lax.all_gather(part, axis), array)
    start = jax.tree.map(
        lambda part, zero: jnp.broadcast_to(jnp.asarray(zero, part.dtype), part.shape),
        array,
        identity,
    )

    def hop(k, before):
        reached = k < index
        new = combine(before, jax.tree.map(lambda part: part[k], everything))
        return jax.tree.map(lambda a, b: jnp.where(reached, a, b), new, before)

    return lax.fori_loop(0, length, hop, start)


def convolve(rows, edge, weight, bias):
    count = rows.shape[0]
    wide = jnp.concatenate([edge, rows], 0).astype(jnp.float32)
    acc = bias[None, :] + weight[0] * wide[0:count]
    acc = acc + weight[1] * wide[1 : count + 1]
    acc = acc + weight[2] * wide[2 : count + 2]
    acc = acc + weight[3] * wide[3 : count + 3]
    return jax.nn.silu(acc).astype(jnp.bfloat16)


def rearrange_heads(rows, shards, per_dev, groups_dev, per_group):
    count = rows.shape[0]
    inner = HEADS * HEAD_DIM
    replicate_groups = max(1, per_group // per_dev)
    heads_part = rows[:, :inner].reshape(count, shards, per_dev * HEAD_DIM)
    b_part = rows[:, inner : inner + GROUPS * STATE].reshape(count, GROUPS, STATE)
    c_part = rows[:, inner + GROUPS * STATE :].reshape(count, GROUPS, STATE)
    b_part = jnp.repeat(b_part, replicate_groups, axis=1).reshape(count, shards, groups_dev * STATE)
    c_part = jnp.repeat(c_part, replicate_groups, axis=1).reshape(count, shards, groups_dev * STATE)
    return jnp.concatenate([heads_part, b_part, c_part], axis=2)


def inner_block(xs, bmat, cmat, steps, cum):
    size = xs.shape[0]
    lower = jnp.arange(size)[:, None] >= jnp.arange(size)[None, :]
    scores = jnp.einsum("qgn,kgn->gqk", cmat, bmat, preferred_element_type=jnp.float32)
    order = jnp.transpose(cum, (1, 2, 0))
    gap = order[..., :, None] - order[..., None, :]
    decay = jnp.exp(jnp.where(lower, gap, -jnp.inf))
    mixing = (scores[:, None] * decay * jnp.transpose(steps, (1, 2, 0))[..., None, :]).astype(
        jnp.bfloat16
    )
    local = jnp.einsum("gjqk,kgjp->qgjp", mixing, xs, preferred_element_type=jnp.float32)
    tail = jnp.exp(cum[size - 1][None] - cum) * steps
    loaded = (bmat[:, :, None, :].astype(jnp.float32) * tail[..., None]).astype(jnp.bfloat16)
    block_state = jnp.einsum("kgjn,kgjp->gjnp", loaded, xs, preferred_element_type=jnp.float32)
    return (local, block_state)


def on_device(xbc, dt_raw, conv_weight, conv_bias, a_log, dt_bias, skip_gain):
    tok = xbc.shape[0]
    shards = lax.axis_size("head")
    per_dev = HEADS // shards
    per_group = HEADS // GROUPS
    groups_dev = max(1, per_dev // per_group)
    heads_per_cluster = per_dev // groups_dev
    sent = rearrange_heads(xbc, shards, per_dev, groups_dev, per_group)
    mine, rates = (
        lax.all_to_all(sent, "head", split_axis=1, concat_axis=0, tiled=True),
        lax.all_to_all(
            dt_raw.reshape(tok, shards, per_dev), "head", split_axis=1, concat_axis=0, tiled=True
        ),
    )
    slab = tok * shards
    mine = mine.reshape(slab, mine.shape[2])
    rates = rates.reshape(slab, per_dev)
    shard = lax.axis_index("head")
    taps = lax.dynamic_index_in_dim(
        rearrange_heads(conv_weight, shards, per_dev, groups_dev, per_group),
        shard,
        1,
        keepdims=False,
    )
    offset = lax.dynamic_index_in_dim(
        rearrange_heads(conv_bias[None, :], shards, per_dev, groups_dev, per_group),
        shard,
        1,
        keepdims=False,
    )
    edge = from_behind(mine[slab - 3 :], "ctx", 1)
    mine = convolve(mine, edge, taps, offset[0])
    nchunk = slab // BLOCK
    width = per_dev * HEAD_DIM
    xs = mine[:, :width].reshape(nchunk, BLOCK, groups_dev, heads_per_cluster, HEAD_DIM)
    bmat = mine[:, width : width + groups_dev * STATE].reshape(nchunk, BLOCK, groups_dev, STATE)
    cmat = mine[:, width + groups_dev * STATE :].reshape(nchunk, BLOCK, groups_dev, STATE)
    first = shard * per_dev
    rate = (-jnp.exp(lax.dynamic_slice_in_dim(a_log, first, per_dev))).reshape(
        groups_dev, heads_per_cluster
    )
    bias_dt = lax.dynamic_slice_in_dim(dt_bias, first, per_dev).reshape(
        groups_dev, heads_per_cluster
    )
    skip = lax.dynamic_slice_in_dim(skip_gain, first, per_dev).reshape(
        groups_dev, heads_per_cluster
    )
    steps = jax.nn.softplus(
        rates.astype(jnp.float32).reshape(nchunk, BLOCK, groups_dev, heads_per_cluster) + bias_dt
    )
    cum = jnp.cumsum(steps * rate, axis=1)

    def block_step(carry, item):
        held, product = carry
        x_part, b_part, c_part, step_part, cum_part = item
        local, block_state = inner_block(x_part, b_part, c_part, step_part, cum_part)
        lifted = c_part.astype(jnp.float32)[:, :, None, :] * jnp.exp(cum_part)[..., None]
        carried = jnp.einsum("qgjn,gjnp->qgjp", lifted, held, precision=lax.Precision.HIGHEST)
        partial_out = local + carried + skip[..., None] * x_part.astype(jnp.float32)
        end = jnp.exp(cum_part[BLOCK - 1])
        return ((end[..., None, None] * held + block_state, product * end), (partial_out, product))

    zero_state = jnp.zeros((groups_dev, heads_per_cluster, STATE, HEAD_DIM), jnp.float32)
    unit = jnp.ones((groups_dev, heads_per_cluster), jnp.float32)
    (slab_state, slab_decay), (partials, product_in) = lax.scan(
        block_step, (zero_state, unit), (xs, bmat, cmat, steps, cum)
    )

    def combine(preceding_state, later):
        return (
            preceding_state[0] * later[0],
            later[0][..., None, None] * preceding_state[1] + later[1],
        )

    _, entering = carried_in((slab_decay, slab_state), "ctx", combine, (unit, zero_state))
    projected = jnp.einsum(
        "cqgn,gjnp->cqgjp", cmat.astype(jnp.float32), entering, precision=lax.Precision.HIGHEST
    )
    factor = jnp.exp(cum) * product_in[:, None]
    total = partials + factor[..., None] * projected
    return total.astype(jnp.bfloat16).reshape(slab, width)


PAIR = 2
LANES = 128
LOG2E = 1.4426950408889634
F32, BF16 = jnp.float32, jnp.bfloat16
WIDTHS = (512, 0, 768, 768)
RESTS = ("", "BD", "", "C")
GROUPED = ((0, 0, 512), (2, 0, 768), (3, 0, 384), (3, 384, 384))
FIRST_ROUND = ((256, 256), (384, 384), (384,), (384,))
SECOND_ROUND = ((512,), (384, 384), (384,), (384,))
ALONE = (2, 3)


def halves(value, count):
    parts = []
    for _ in range(count):
        part = value.astype(BF16)
        parts.append(part)
        value = value - part.astype(F32)
    return parts


def spread(first_head, width, copies):
    lane = lax.broadcasted_iota(jnp.int32, (copies * LANES, width), 0) % LANES
    column = lax.broadcasted_iota(jnp.int32, (copies * LANES, width), 1)
    return (lane == first_head + column // HEAD_DIM).astype(BF16)


def dot(a, b):
    return jnp.dot(a, b, preferred_element_type=F32)


def ds(start, width):
    return pl.ds(pl.multiple_of(start, LANES), width)


def run(copies, sems):
    started = []
    for i, (source, target) in enumerate(copies):
        copy = pltpu.make_async_copy(source, target, sems.at[i])
        copy.start()
        started.append(copy)
    return started


PER_GROUP = HEADS * HEAD_DIM // GROUPS
INNER = HEADS * HEAD_DIM


def channels(group, first, width):
    return ds(group * PER_GROUP + first, width)


def pack_first_kernel(shards, place, xbc, send, sems):
    core, shard = place[2], place[4]
    count = xbc.shape[0]
    width = WIDTHS[0]
    copies = []
    for r in range(shards):
        group = (shard ^ r) * PAIR + 1 - core
        copies.append((xbc.at[:, channels(group, 0, width)], send.at[:, r * width : (r + 1) * width]))
        last, rows = xbc.at[count - 16 :], slice(16 * r, 16 * r + 16)
        to = shards * width
        copies.append((last.at[:, channels(group, width, PER_GROUP - width)], send.at[rows, to : to + PER_GROUP - width]))
        to += PER_GROUP - width
        for i in range(2):
            at = ds(INNER + (i * GROUPS + group) * STATE, STATE)
            copies.append((last.at[:, at], send.at[rows, to + i * STATE : to + (i + 1) * STATE]))
    for copy in run(copies, sems):
        copy.wait()


def pack_kernel(shards, place, xbc, dt_raw, order, send, tail, sems):
    core, shard = place[2], place[4]
    count = xbc.shape[0]
    first = WIDTHS[0]
    width = PER_GROUP - first
    rest = width * shards
    size = PER_GROUP + 2 * STATE
    copies = []
    for r in range(shards):
        group = (shard ^ r) * PAIR + 1 - core
        copies.append((xbc.at[:, channels(group, first, width)], send.at[:, r * width : (r + 1) * width]))
        for i in range(2):
            to = rest + (i * shards + r) * STATE
            copies.append((xbc.at[:, ds(INNER + (i * GROUPS + group) * STATE, STATE)], send.at[:, to : to + STATE]))
    copies.append((dt_raw, send.at[:, send.shape[1] - HEADS :]))
    for r in range(shards):
        group, to = (shard ^ r) * PAIR + core, r * size
        last = xbc.at[count - 16 :]
        copies.append((last.at[:, channels(group, 0, PER_GROUP)], tail.at[:, to : to + PER_GROUP]))
        for i in range(2):
            at = ds(INNER + (i * GROUPS + group) * STATE, STATE)
            start = to + PER_GROUP + i * STATE
            copies.append((last.at[:, at], tail.at[:, start : start + STATE]))
    for copy in run(copies, sems):
        copy.wait()


def taps_kernel(place, weight, bias, order, taps, offset, sems):
    copies = []
    for source, target in ((weight, taps), (bias, offset)):
        copies.append((source.at[:, channels(place[0], 0, PER_GROUP)], target.at[:, :PER_GROUP]))
        for i in range(2):
            at = ds(INNER + (i * GROUPS + place[0]) * STATE, STATE)
            start = PER_GROUP + i * STATE
            copies.append((source.at[:, at], target.at[:, start : start + STATE]))
    for copy in run(copies, sems):
        copy.wait()


def put_edge(shards, place, got, tail, out):
    count = got.shape[0]
    first = WIDTHS[0]
    size = PER_GROUP + 2 * STATE
    for r in range(shards):
        theirs = [got[count - 16 :, r * first : (r + 1) * first]]
        theirs.append(got[16 * r : 16 * r + 16, shards * first :])
        to = r * size
        for part in theirs:
            at = slice(to, to + part.shape[1])
            rows = jnp.where(place[2] == 0, part.astype(F32), tail[:, at].astype(F32))
            out[:, at] = rows[13:16].astype(BF16)
            to = at.stop


def total_of(piece):
    return WIDTHS[piece] + sum(LANES if kind == "D" else STATE for kind in RESTS[piece])


def merge_kernel(shards, plan, unread, place, xbc, dt_raw, got_first, got, edges, *refs):
    refs = refs[unread:]
    outs, sems = refs[: len(plan)], refs[-1]
    core, shard = place[2], place[4]
    count = xbc.shape[0]
    stride = PER_GROUP - WIDTHS[0]
    mine = pl.ds(pl.multiple_of(core * count, count), count)
    other = pl.ds(pl.multiple_of((1 - core) * count, count), count)
    copies, steps = [], []
    for out, (r, pieces) in zip(outs, plan):
        group = (shard ^ r) * PAIR + core
        to = 0
        for piece in pieces:
            first, width = sum(WIDTHS[:piece]), WIDTHS[piece]
            if piece == 0:
                source = got_first.at[:, r * width : (r + 1) * width]
            else:
                at = r * stride + first - WIDTHS[0]
                source = got.at[:, at : at + width]
            if width:
                copies.append((xbc.at[:, channels(group, first, width)], out.at[mine, to : to + width]))
                copies.append((source, out.at[other, to : to + width]))
            to += width
            for kind in RESTS[piece]:
                if kind == "D":
                    steps.append((out, r, to))
                    to += LANES
                    continue
                i = "BC".index(kind)
                at = ds(INNER + (i * GROUPS + group) * STATE, STATE)
                copies.append((xbc.at[:, at], out.at[mine, to : to + STATE]))
                at = stride * shards + (i * shards + r) * STATE
                copies.append((got.at[:, at : at + STATE], out.at[other, to : to + STATE]))
                to += STATE
    started = run(copies, sems)
    if len(refs) > len(plan) + 1:
        put_edge(shards, place, got_first, edges, refs[-2])
    if steps:
        lane = lax.broadcasted_iota(jnp.int32, (count, LANES), 1)
        per_tile = LANES * GROUPS // HEADS
        heads = HEADS // GROUPS
        for out, r, to in steps:
            group = (shard ^ r) * PAIR + core
            tile, shift = group // per_tile, (LANES - (group % per_tile) * heads) % LANES
            own = dt_raw[:, ds(tile * LANES, LANES)].astype(F32)
            theirs = got[:, ds(got.shape[1] - HEADS + tile * LANES, LANES)].astype(F32)
            low = jnp.where(core == 0, own, theirs)
            high = jnp.where(core == 0, theirs, own)
            packed = jnp.zeros((count // 2, LANES), F32)
            for j, rows in enumerate((low, high)):
                rows = jnp.where(lane < heads, pltpu.roll(rows, shift, 1), 0.0)
                for i in range(2):
                    part = rows[i * count // 2 : (i + 1) * count // 2]
                    packed = packed + pltpu.roll(part, (2 * j + i) * heads, 1)
            out[: count // 2, to : to + LANES] = packed.astype(BF16)
            size = PER_GROUP + 2 * STATE
            at = slice(r * size, (r + 1) * size)
            edge = jnp.concatenate([edges[:, at].astype(F32), jnp.zeros((1, size), F32)], 0)
            edge = jnp.concatenate([edge[:, q * LANES : (q + 1) * LANES] for q in range(size // LANES)], 0)
            fill = jnp.zeros((PAIR * count - count // 2 - edge.shape[0], LANES), F32)
            out[count // 2 :, to : to + LANES] = jnp.concatenate([edge, fill], 0).astype(BF16)
    for copy in started:
        copy.wait()


def view(refs, piece):
    return [(ref, 0) for ref in refs]


def convolve_in_order(place, blocks, columns, edge, tap, bias, wide, put):
    width = columns.stop - columns.start
    count = blocks[0][0].shape[0] // PAIR
    wide[5:8, :width] = edge
    for r, (block, origin) in enumerate(blocks):
        for core in range(PAIR):
            at = pl.multiple_of((core * len(blocks) + (place[4] ^ r)) * count + 8, 8)
            part = block[core * count : (core + 1) * count, origin + columns.start : origin + columns.stop]
            wide[pl.ds(at, count), :width] = part.astype(F32)
    tap, bias = tap * 0.5, bias * 0.5
    for start in range(0, PAIR * len(blocks) * count, count):
        acc = bias + tap[0:1] * wide[start + 5 : start + 5 + count, :width]
        acc = acc + tap[1:2] * wide[start + 6 : start + 6 + count, :width]
        acc = acc + tap[2:3] * wide[start + 7 : start + 7 + count, :width]
        acc = acc + tap[3:4] * wide[start + 8 : start + 8 + count, :width]
        put(start, count, (acc + acc * jnp.tanh(acc)).astype(BF16))


def prep_kernel(shards, place, *refs):
    blocks, (taps, offset, a_ref, bias_ref, skip_ref, order) = refs[:shards], refs[shards : shards + 6]
    b_ref, edge_ref, cum_ref, row_ref, factor_ref, tail_ref, skip_out, dt_ref, wide = refs[shards + 6 :]
    blocks = view(blocks, 1)
    start = WIDTHS[1]
    last = total_of(1) - LANES
    size = edge_ref.shape[1]
    count = blocks[0][0].shape[0] // PAIR
    half, heads = count // 2, HEADS // GROUPS
    columns = [block[:, origin + last : origin + last + LANES].astype(F32) for block, origin in blocks]
    edge = columns[0][half : half + 4 * size // LANES]
    for column in columns[1:]:
        edge = edge + column[half : half + 4 * size // LANES]
    for q in range(size // LANES):
        edge_ref[:, q * LANES : (q + 1) * LANES] = edge[4 * q : 4 * q + 4]
    for r, column in enumerate(columns):
        packed = column[:half]
        for j in range(2 * PAIR):
            at = ((j // 2) * shards + (place[4] ^ r)) * count + (j % 2) * half
            rows = packed if j == 0 else pltpu.roll(packed, LANES - j * heads, 1)
            dt_ref[pl.ds(pl.multiple_of(at, half), half), :] = rows

    def put(start, count, value):
        b_ref[start : start + count] = value

    at = slice(PER_GROUP, PER_GROUP + STATE)
    convolve_in_order(
        place, blocks, slice(start, start + STATE), edge_ref[0:3, at], taps[:, at], offset[:, at], wide, put
    )
    per_tile = LANES * GROUPS // HEADS
    group = place[0]
    tile = group // per_tile
    shift = (LANES - (group % per_tile) * heads) % LANES

    def lanes_of(ref):
        return pltpu.roll(jnp.broadcast_to(ref[pl.ds(tile, 1), :], (8, LANES)), shift, 1)

    rate = -jnp.exp(lanes_of(a_ref)[0:1])
    raw = dt_ref[...] + lanes_of(bias_ref)[0:1]
    step = jnp.maximum(raw, 0.0) + jnp.log1p(jnp.exp(-jnp.abs(raw)))
    skip = lanes_of(skip_ref)
    skip_out[...] = jnp.concatenate(halves(jnp.concatenate([skip, skip], 0), 3), 1)
    lower = (
        lax.broadcasted_iota(jnp.int32, (BLOCK, BLOCK), 0)
        >= lax.broadcasted_iota(jnp.int32, (BLOCK, BLOCK), 1)
    ).astype(BF16)
    valid = lax.broadcasted_iota(jnp.int32, (BLOCK, LANES), 1) < heads
    for block in range(PAIR):
        at = slice(block * BLOCK, (block + 1) * BLOCK)
        here = jnp.where(valid, step[at], 1.0)
        parts = halves(here * rate, 3)
        cum = dot(lower, parts[0]) + (dot(lower, parts[1]) + dot(lower, parts[2]))
        cum = cum * LOG2E
        cum_ref[at] = cum
        row_ref[:, at] = jnp.transpose(cum - jnp.log2(here))
        factor_ref[at] = jnp.concatenate(halves(jnp.exp2(cum), 2), 1)
        tail = jnp.exp2(cum[BLOCK - 1 :] - cum) * here
        tail_ref[at] = jnp.concatenate(halves(tail, 2), 1)


def score_kernel(shards, place, *refs):
    blocks, refs = refs[:shards], refs[shards:]
    taps, offset, edge_ref, b_ref, c_ref, score_ref, wide = (*refs[:4], *refs[-3:])
    blocks = view(blocks, 3)
    start = WIDTHS[3]
    at = slice(PER_GROUP + STATE, PER_GROUP + 2 * STATE)

    def put(start, count, value):
        c_ref[start : start + count] = value

    convolve_in_order(
        place, blocks, slice(start, start + STATE), edge_ref[0:3, at], taps[:, at], offset[:, at], wide, put
    )
    for block in range(PAIR):
        at = slice(block * BLOCK, (block + 1) * BLOCK)
        score_ref[at] = lax.dot_general(
            c_ref[at], b_ref[at], (((1,), (1,)), ((), ())), preferred_element_type=F32
        )


def decay_of(ref):
    decay = ref[STATE : STATE + 16].astype(F32)
    return decay[0:1] + (decay[1:2] + decay[2:3])


def put_decay(ref, decay):
    row = lax.broadcasted_iota(jnp.int32, (16, ref.shape[1]), 0)
    high, middle, low = (part.astype(F32) for part in halves(decay, 3))
    packed = jnp.where(row == 0, high, jnp.where(row == 1, middle, jnp.where(row == 2, low, 0.0)))
    ref[STATE:] = packed.astype(BF16)


def state_kernel(shards, part, sizes, place, *refs):
    blocks, refs = refs[:shards], refs[shards:]
    taps, offset, edge_ref, b_ref, factor_ref, tail_ref = refs[:6]
    x_ref, own_ref, *sends, wide = refs[-3 - len(sizes) :]
    piece, start, width = part
    first = sum(WIDTHS[:piece]) + start
    at = slice(first, first + width)

    def put(row, count, value):
        x_ref[row : row + count] = value

    blocks = view(blocks, piece)
    columns = slice(start, start + width)
    convolve_in_order(place, blocks, columns, edge_ref[0:3, at], taps[:, at], offset[:, at], wide, put)
    expand = spread(first // HEAD_DIM, width, 2)
    both = []
    for block in range(PAIR):
        at = slice(block * BLOCK, (block + 1) * BLOCK)
        loaded = (x_ref[at].astype(F32) * dot(tail_ref[at], expand)).astype(BF16)
        both.append(
            lax.dot_general(b_ref[at], loaded, (((0,), (0,)), ((), ())), preferred_element_type=F32)
        )
    ends = [dot(factor_ref[(i + 1) * BLOCK - 16 : (i + 1) * BLOCK], expand)[15:16] for i in range(PAIR)]
    own_ref[...] = both[0]
    end = (ends[1] * both[0] + both[1]).astype(BF16)
    decay = ends[0] * ends[1]
    start = 0
    for send_ref in sends:
        at = slice(start, start + send_ref.shape[1])
        send_ref[0:STATE] = end[:, at]
        put_decay(send_ref, decay[:, at])
        start = at.stop


def combine_kernel(count, *refs):
    early, late, out_ref = refs[:count], refs[count : 2 * count], refs[-1]
    start = 0
    for early_ref, late_ref in zip(early, late):
        at = slice(start, start + late_ref.shape[1])
        decay = decay_of(late_ref)
        total = decay * early_ref[:STATE].astype(F32) + late_ref[:STATE].astype(F32)
        out_ref[:STATE, at] = total.astype(BF16)
        put_decay(out_ref.at[:, at], decay * decay_of(early_ref))
        start = at.stop


def mix(first_head, x_ref, cum_ref, row_ref, score_ref, skip_ref, put):
    width = x_ref.shape[1]
    half = BLOCK // 2
    expand = spread(first_head, width, 3)
    skip = dot(skip_ref[...], expand)[0:1]
    lower = lax.broadcasted_iota(jnp.int32, (half, half), 0) >= lax.broadcasted_iota(
        jnp.int32, (half, half), 1
    )
    lane = lax.broadcasted_iota(jnp.int32, (BLOCK, LANES), 1)
    for block in range(PAIR):
        base = block * BLOCK
        for tile in range(width // LANES):
            columns = slice(tile * LANES, (tile + 1) * LANES)
            x = x_ref[base : base + BLOCK, columns]
            top = skip[:, columns] * x[:half].astype(F32)
            bottom = skip[:, columns] * x[half:].astype(F32)
            for side in range(LANES // HEAD_DIM):
                head = first_head + tile * (LANES // HEAD_DIM) + side
                own = jnp.where(lane // HEAD_DIM == side, x, jnp.zeros_like(x))
                cum = cum_ref[base : base + BLOCK, head : head + 1]
                row = row_ref[head : head + 1, base : base + BLOCK]
                diag = jnp.where(lower, cum[:half] - row[:, :half], -1e30)
                mixing = jnp.exp2(diag) * score_ref[base : base + half, :half]
                top = top + dot(mixing.astype(BF16), own[:half])
                left = jnp.exp2(cum[half:] - row[:, :half]) * score_ref[base + half : base + BLOCK, :half]
                diag = jnp.where(lower, cum[half:] - row[:, half:], -1e30)
                right = jnp.exp2(diag) * score_ref[base + half : base + BLOCK, half:]
                mixing = jnp.concatenate([left.astype(BF16), right.astype(BF16)], 1)
                bottom = bottom + dot(mixing, own)
            put(block, slice(base, base + half), columns, top)
            put(block, slice(base + half, base + BLOCK), columns, bottom)


def local_kernel(first_head, x_ref, cum_ref, row_ref, score_ref, skip_ref, *refs):
    out_ref = refs[-1]

    def put(block, rows, columns, value):
        out_ref[rows, columns] = value

    mix(first_head, x_ref, cum_ref, row_ref, score_ref, skip_ref, put)


def carry(first_head, core, lasts, befores, alones, own_ref, c_ref, factor_ref, add, keep_ref, send_ref):
    expand = spread(first_head, own_ref.shape[1], 2)
    last, before = (
        refs[0][...] if len(refs) == 1 else jnp.concatenate([ref[...] for ref in refs], 1)
        for refs in (lasts, befores)
    )
    held = last[:STATE].astype(F32) + decay_of(last) * before[:STATE].astype(F32)
    for alone in alones:
        held = held + alone[:STATE].astype(F32)
    factor = dot(factor_ref[...], expand)
    outs = []
    for block in range(PAIR):
        at = slice(block * BLOCK, (block + 1) * BLOCK)
        carried = dot(c_ref[at], held.astype(BF16))
        outs.append((add[at] + factor[at] * carried).astype(BF16))
        held = factor[BLOCK - 1 : BLOCK] * held + own_ref[...]

    @pl.when(core == 0)
    def _():
        keep_ref[...] = outs[0]
        send_ref[...] = outs[1]

    @pl.when(core == 1)
    def _():
        keep_ref[...] = outs[1]
        send_ref[...] = outs[0]


def final_kernel(first_head, counts, place, *refs):
    groups = []
    for number in counts:
        groups.append(refs[:number])
        refs = refs[number:]
    carry(first_head, place[2], *groups, *refs[:4], *refs[-2:])


def finish_kernel(first_head, counts, place, *refs):
    groups = []
    for number in counts:
        groups.append(refs[:number])
        refs = refs[number:]
    own_ref, c_ref, factor_ref = refs[:3]
    keep_ref, send_ref, partial = refs[-3:]
    local_kernel(first_head, *refs[3:8], partial)
    carry(first_head, place[2], *groups, own_ref, c_ref, factor_ref, partial, keep_ref, send_ref)


def place_kernel(firsts, place, *refs):
    count = len(firsts)
    keeps, gots = refs[:count], refs[count : 2 * count]
    out, sems = refs[-2:]
    core = place[2]
    half = out.shape[1] // PAIR
    copies = []
    for first, keep, got in zip(firsts, keeps, gots):
        width = keep.shape[1]
        copies.append((keep, out.at[:, ds(core * half + first, width)]))
        copies.append((got, out.at[:, ds((1 - core) * half + first, width)]))
    for copy in run(copies, sems):
        copy.wait()


def put_in_place(firsts, shape, place, keeps, gots):
    smem, vmem, hbm = (pl.BlockSpec(memory_space=m) for m in (pltpu.SMEM, pltpu.VMEM, pltpu.HBM))
    count = len(firsts)
    return pl.pallas_call(
        functools.partial(place_kernel, firsts),
        out_shape=jax.ShapeDtypeStruct(shape, BF16),
        in_specs=[smem] + [vmem] * (2 * count),
        out_specs=hbm,
        scratch_shapes=[pltpu.SemaphoreType.DMA((2 * count,))],
        compiler_params=pltpu.CompilerParams(vmem_limit_bytes=16 << 20),
        cost_estimate=pl.CostEstimate(flops=1, bytes_accessed=1, transcendentals=0),
        name="place",
    )(place, *keeps, *gots)


class Stay:
    def __init__(self, array):
        self.array = array


def call(body, outs, operands, scratch=(), flops=0, transcendentals=0, name=None, limit=16 << 20):
    shapes = [jax.ShapeDtypeStruct(shape, dtype) for shape, dtype in outs]
    smem, vmem, hbm = (pl.BlockSpec(memory_space=m) for m in (pltpu.SMEM, pltpu.VMEM, pltpu.HBM))
    specs = [
        hbm if isinstance(o, Stay) else smem if o.dtype == jnp.int32 else vmem for o in operands
    ]
    moved = sum(o.size * o.dtype.itemsize for o in shapes) * 2
    return pl.pallas_call(
        body,
        out_shape=shapes,
        in_specs=specs,
        out_specs=[vmem] * len(outs),
        scratch_shapes=scratch,
        compiler_params=pltpu.CompilerParams(vmem_limit_bytes=limit),
        cost_estimate=pl.CostEstimate(flops=1, bytes_accessed=1, transcendentals=0),
        name=name,
    )(*[o.array if isinstance(o, Stay) else o for o in operands])


def paired(xbc, dt_raw, conv_weight, conv_bias, a_log, dt_bias, skip_gain):
    axes = ("ctx", "head")
    shards, length = lax.axis_size("head"), lax.axis_size("ctx")
    devices, peers = shards * length, shards * PAIR
    tok = xbc.shape[0]
    slab = tok * peers
    context, shard = lax.axis_index("ctx"), lax.axis_index("head")
    pair, core = context // PAIR, context % PAIR
    group = shard * PAIR + core
    place = jnp.stack([group, pair, core, core * shards + shard, shard]).astype(jnp.int32)

    def over(block, target):
        route = [(i, target(i)) for i in range(devices)]
        return lax.ppermute(block, axes, [(i, j) for i, j in route if j is not None and j < devices])

    def swap(block):
        return over(block, lambda i: i ^ shards)

    rows = Stay(xbc)
    size = PER_GROUP + 2 * STATE
    (sent,) = call(
        functools.partial(pack_first_kernel, shards),
        [((tok, shards * WIDTHS[0] + size - WIDTHS[0]), BF16)],
        [place, rows],
        scratch=[pltpu.SemaphoreType.DMA((4 * shards,))],
        name="pack_first",
    )
    got_first = swap(sent)
    sent, tail = call(
        functools.partial(pack_kernel, shards),
        [((tok, shards * (size - WIDTHS[0]) + HEADS), BF16), ((16, shards * size), BF16)],
        [place, rows, Stay(dt_raw), Stay(sent)],
        scratch=[pltpu.SemaphoreType.DMA((6 * shards + 1,))],
        name="pack",
    )
    got_rest = swap(sent)
    taps, offset = call(
        taps_kernel,
        [((4, size), F32), ((1, size), F32)],
        [place, Stay(conv_weight), Stay(conv_bias[None]), Stay(got_rest)],
        scratch=[pltpu.SemaphoreType.DMA((6,))],
        name="taps",
    )

    def send_on(plan, order, tail=None, edges=None):
        unused = Stay(got_first)
        parts = [p for _, pieces in plan for p in pieces]
        made = [] if tail is None else [((3, shards * size), BF16)]
        return call(
            functools.partial(merge_kernel, shards, plan, len(order)),
            [((PAIR * tok, sum(map(total_of, pieces))), BF16) for _, pieces in plan] + made,
            [
                place,
                rows,
                Stay(dt_raw) if edges is None else dt_raw,
                got_first if 0 in parts else unused,
                got_rest if any(parts) else unused,
                next((o for o in (tail, edges) if o is not None), unused),
            ]
            + [Stay(o) for o in order],
            scratch=[pltpu.SemaphoreType.DMA((sum(2 + 2 * len(RESTS[p]) for p in parts),))],
            name="merge",
        )

    def travel(blocks):
        return [blocks[0]] + [over(blocks[r], lambda i, r=r: i ^ r) for r in range(1, shards)]

    def plan(piece):
        return [(r, (piece,)) for r in range(shards)]

    *first_blocks, edges = send_on(plan(0), [], tail)
    message = [travel(first_blocks)]
    edges = over(edges, lambda i: i + peers if i % shards == shards - 1 else None)
    second_blocks = send_on(plan(1), [first_blocks[0], message[0][1]], None, edges)
    message.append(travel(second_blocks))
    third_blocks = send_on(plan(2), [second_blocks[0], *message[0][2:]])
    message.append(travel(third_blocks))

    def seen(piece):
        return message[piece]

    tiles = [p.reshape(HEADS // LANES, LANES) for p in (a_log, dt_bias, skip_gain)]
    b, edge, cum, row, factor, tail, skip = call(
        functools.partial(prep_kernel, shards),
        [
            ((slab, STATE), BF16),
            ((4, size), F32),
            ((slab, LANES), F32),
            ((LANES, slab), F32),
            ((slab, 2 * LANES), BF16),
            ((slab, 2 * LANES), BF16),
            ((16, 3 * LANES), BF16),
        ],
        [place] + seen(1) + [taps, offset] + tiles + [Stay(third_blocks[0])],
        scratch=[pltpu.VMEM((slab, LANES), F32), pltpu.VMEM((slab + 8, STATE), F32)],
        name="prep",
    )
    count = len(GROUPED)
    x, sent, own, last, joined, before, alone, keep, send = ([None] * count for _ in range(9))

    def first_head(i):
        return (sum(WIDTHS[: GROUPED[i][0]]) + GROUPED[i][1]) // HEAD_DIM

    def state_of(i, order):
        piece, _, width = GROUPED[i]
        x[i], own[i], *sent[i] = call(
            functools.partial(state_kernel, shards, GROUPED[i], FIRST_ROUND[i]),
            [((slab, width), BF16), ((STATE, width), F32)] + [((STATE + 16, w), BF16) for w in FIRST_ROUND[i]],
            [place] + seen(piece) + [taps, offset, edge, b, factor, tail] + [Stay(o) for o in order],
            scratch=[pltpu.VMEM((slab + 8, width), F32)],
            name="state",
        )
        every = i not in ALONE
        last[i] = [over(part, lambda i: i + peers if every or i // peers % 2 == 0 else None) for part in sent[i]]

    def combine_of(i, order):
        joined[i], before[i], alone[i] = [], [], []
        step = len(FIRST_ROUND[i]) // len(SECOND_ROUND[i])
        for j, width in enumerate(SECOND_ROUND[i]):
            early, late = last[i][j * step : (j + 1) * step], sent[i][j * step : (j + 1) * step]
            (total,) = call(
                functools.partial(combine_kernel, len(early)),
                [((STATE + 16, width), BF16)],
                early + late + [Stay(o) for o in order],
                name="combine",
            )
            joined[i].append(total)
            if i in ALONE:
                before[i].append(over(total, lambda i: i + 2 * peers if i // peers == 1 else None))
                alone[i].append(over(total, lambda i: i + peers if i // peers == 1 else None))
            else:
                before[i].append(over(total, lambda i: i + 2 * peers))
            order = [total]

    def finish_of(body, i, operands, order, **more):
        keep[i], send[i] = call(
            functools.partial(body, first_head(i), (len(last[i]), len(before[i]), len(alone[i]))),
            [((BLOCK, GROUPED[i][2]), BF16)] * 2,
            [place, *last[i], *before[i], *alone[i], own[i], c, factor] + operands + [Stay(o) for o in order],
            name="final",
            **more,
        )

    state_of(0, [])
    combine_of(0, [])
    fourth_blocks = send_on(plan(3), [joined[0][0]])
    message.append(travel(fourth_blocks))
    state_of(1, [fourth_blocks[0]])
    combine_of(1, [])
    state_of(2, joined[1])
    state_of(3, sent[2])
    c, score = call(
        functools.partial(score_kernel, shards),
        [((slab, STATE), BF16), ((slab, BLOCK), F32)],
        [place] + seen(3) + [taps, offset, edge, b] + [Stay(o) for o in sent[3] + before[1]],
        scratch=[pltpu.VMEM((slab + 8, STATE), F32)],
        name="score",
    )
    mixes = [cum, row, score, skip]

    def in_full(i, order):
        wide = [pltpu.VMEM((slab, GROUPED[i][2]), F32)]
        finish_of(finish_kernel, i, [x[i]] + mixes, order, scratch=wide)

    in_full(1, [score])
    combine_of(2, [keep[1]])
    combine_of(3, joined[2])
    order, partial = joined[3][0], {}
    for i in (2, 3):
        (partial[i],) = call(
            functools.partial(local_kernel, first_head(i)),
            [(x[i].shape, F32)],
            [x[i]] + mixes + [Stay(order)],
            name="local",
        )
        order = partial[i]
    in_full(0, [order])
    order = keep[0]
    for i in (2, 3):
        finish_of(final_kernel, i, [partial[i]], [order])
        order = keep[i]
    firsts = [first_head(i) * HEAD_DIM for i in range(count)]
    return put_in_place(firsts, (BLOCK, PAIR * PER_GROUP), place, keep, [swap(o) for o in send])


def solution(mesh):
    in_specs = (P(("ctx", "head"), None), P(("ctx", "head"), None), P(), P(), P(), P(), P())
    out_specs = P("ctx", "head")
    shards, length = mesh.shape["head"], mesh.shape["ctx"]

    def program(xbc, *rest):
        slab = xbc.shape[0] // length
        fits = shards == GROUPS // PAIR and length == 4 * PAIR and slab == BLOCK
        return jax.shard_map(
            paired if fits else on_device,
            mesh=mesh,
            in_specs=in_specs,
            out_specs=out_specs,
            check_vma=False,
        )(xbc, *rest)

    return program
```

```python
import functools

import jax
import jax.numpy as jnp
from jax import lax
from jax.experimental import pallas as pl
from jax.experimental.pallas import tpu as pltpu
from jax.sharding import PartitionSpec as P

HEADS = 256
HEAD_DIM = 64
STATE = 256
GROUPS = 8
BLOCK = 256


def from_behind(block, axis, distance):
    devices = range(lax.axis_size(axis))
    route = [(i - distance, i) for i in devices if i - distance in devices]
    return lax.ppermute(block, axis, route)


def carried_in(array, axis, combine, identity):
    length, index = (lax.axis_size(axis), lax.axis_index(axis))
    everything = jax.tree.map(lambda part: lax.all_gather(part, axis), array)
    start = jax.tree.map(
        lambda part, zero: jnp.broadcast_to(jnp.asarray(zero, part.dtype), part.shape),
        array,
        identity,
    )

    def hop(k, before):
        reached = k < index
        new = combine(before, jax.tree.map(lambda part: part[k], everything))
        return jax.tree.map(lambda a, b: jnp.where(reached, a, b), new, before)

    return lax.fori_loop(0, length, hop, start)


def convolve(rows, edge, weight, bias):
    count = rows.shape[0]
    wide = jnp.concatenate([edge, rows], 0).astype(jnp.float32)
    acc = bias[None, :] + weight[0] * wide[0:count]
    acc = acc + weight[1] * wide[1 : count + 1]
    acc = acc + weight[2] * wide[2 : count + 2]
    acc = acc + weight[3] * wide[3 : count + 3]
    return jax.nn.silu(acc).astype(jnp.bfloat16)


def rearrange_heads(rows, shards, per_dev, groups_dev, per_group):
    count = rows.shape[0]
    inner = HEADS * HEAD_DIM
    replicate_groups = max(1, per_group // per_dev)
    heads_part = rows[:, :inner].reshape(count, shards, per_dev * HEAD_DIM)
    b_part = rows[:, inner : inner + GROUPS * STATE].reshape(count, GROUPS, STATE)
    c_part = rows[:, inner + GROUPS * STATE :].reshape(count, GROUPS, STATE)
    b_part = jnp.repeat(b_part, replicate_groups, axis=1).reshape(count, shards, groups_dev * STATE)
    c_part = jnp.repeat(c_part, replicate_groups, axis=1).reshape(count, shards, groups_dev * STATE)
    return jnp.concatenate([heads_part, b_part, c_part], axis=2)


def inner_block(xs, bmat, cmat, steps, cum):
    size = xs.shape[0]
    lower = jnp.arange(size)[:, None] >= jnp.arange(size)[None, :]
    scores = jnp.einsum("qgn,kgn->gqk", cmat, bmat, preferred_element_type=jnp.float32)
    order = jnp.transpose(cum, (1, 2, 0))
    gap = order[..., :, None] - order[..., None, :]
    decay = jnp.exp(jnp.where(lower, gap, -jnp.inf))
    mixing = (scores[:, None] * decay * jnp.transpose(steps, (1, 2, 0))[..., None, :]).astype(
        jnp.bfloat16
    )
    local = jnp.einsum("gjqk,kgjp->qgjp", mixing, xs, preferred_element_type=jnp.float32)
    tail = jnp.exp(cum[size - 1][None] - cum) * steps
    loaded = (bmat[:, :, None, :].astype(jnp.float32) * tail[..., None]).astype(jnp.bfloat16)
    block_state = jnp.einsum("kgjn,kgjp->gjnp", loaded, xs, preferred_element_type=jnp.float32)
    return (local, block_state)


def on_device(xbc, dt_raw, conv_weight, conv_bias, a_log, dt_bias, skip_gain):
    tok = xbc.shape[0]
    shards = lax.axis_size("head")
    per_dev = HEADS // shards
    per_group = HEADS // GROUPS
    groups_dev = max(1, per_dev // per_group)
    heads_per_cluster = per_dev // groups_dev
    sent = rearrange_heads(xbc, shards, per_dev, groups_dev, per_group)
    mine, rates = (
        lax.all_to_all(sent, "head", split_axis=1, concat_axis=0, tiled=True),
        lax.all_to_all(
            dt_raw.reshape(tok, shards, per_dev), "head", split_axis=1, concat_axis=0, tiled=True
        ),
    )
    slab = tok * shards
    mine = mine.reshape(slab, mine.shape[2])
    rates = rates.reshape(slab, per_dev)
    shard = lax.axis_index("head")
    taps = lax.dynamic_index_in_dim(
        rearrange_heads(conv_weight, shards, per_dev, groups_dev, per_group),
        shard,
        1,
        keepdims=False,
    )
    offset = lax.dynamic_index_in_dim(
        rearrange_heads(conv_bias[None, :], shards, per_dev, groups_dev, per_group),
        shard,
        1,
        keepdims=False,
    )
    edge = from_behind(mine[slab - 3 :], "ctx", 1)
    mine = convolve(mine, edge, taps, offset[0])
    nchunk = slab // BLOCK
    width = per_dev * HEAD_DIM
    xs = mine[:, :width].reshape(nchunk, BLOCK, groups_dev, heads_per_cluster, HEAD_DIM)
    bmat = mine[:, width : width + groups_dev * STATE].reshape(nchunk, BLOCK, groups_dev, STATE)
    cmat = mine[:, width + groups_dev * STATE :].reshape(nchunk, BLOCK, groups_dev, STATE)
    first = shard * per_dev
    rate = (-jnp.exp(lax.dynamic_slice_in_dim(a_log, first, per_dev))).reshape(
        groups_dev, heads_per_cluster
    )
    bias_dt = lax.dynamic_slice_in_dim(dt_bias, first, per_dev).reshape(
        groups_dev, heads_per_cluster
    )
    skip = lax.dynamic_slice_in_dim(skip_gain, first, per_dev).reshape(
        groups_dev, heads_per_cluster
    )
    steps = jax.nn.softplus(
        rates.astype(jnp.float32).reshape(nchunk, BLOCK, groups_dev, heads_per_cluster) + bias_dt
    )
    cum = jnp.cumsum(steps * rate, axis=1)

    def block_step(carry, item):
        held, product = carry
        x_part, b_part, c_part, step_part, cum_part = item
        local, block_state = inner_block(x_part, b_part, c_part, step_part, cum_part)
        lifted = c_part.astype(jnp.float32)[:, :, None, :] * jnp.exp(cum_part)[..., None]
        carried = jnp.einsum("qgjn,gjnp->qgjp", lifted, held, precision=lax.Precision.HIGHEST)
        partial_out = local + carried + skip[..., None] * x_part.astype(jnp.float32)
        end = jnp.exp(cum_part[BLOCK - 1])
        return ((end[..., None, None] * held + block_state, product * end), (partial_out, product))

    zero_state = jnp.zeros((groups_dev, heads_per_cluster, STATE, HEAD_DIM), jnp.float32)
    unit = jnp.ones((groups_dev, heads_per_cluster), jnp.float32)
    (slab_state, slab_decay), (partials, product_in) = lax.scan(
        block_step, (zero_state, unit), (xs, bmat, cmat, steps, cum)
    )

    def combine(preceding_state, later):
        return (
            preceding_state[0] * later[0],
            later[0][..., None, None] * preceding_state[1] + later[1],
        )

    _, entering = carried_in((slab_decay, slab_state), "ctx", combine, (unit, zero_state))
    projected = jnp.einsum(
        "cqgn,gjnp->cqgjp", cmat.astype(jnp.float32), entering, precision=lax.Precision.HIGHEST
    )
    factor = jnp.exp(cum) * product_in[:, None]
    total = partials + factor[..., None] * projected
    return total.astype(jnp.bfloat16).reshape(slab, width)


PAIR = 2
LANES = 128
LOG2E = 1.4426950408889634
F32, BF16 = jnp.float32, jnp.bfloat16
WIDTHS = (512, 0, 768, 768)
RESTS = ("", "BD", "", "C")
GROUPED = ((0, 0, 512), (2, 0, 768), (3, 0, 384), (3, 384, 384))
FIRST_ROUND = ((256, 256), (384, 384), (384,), (384,))
SECOND_ROUND = ((512,), (384, 384), (384,), (384,))
ALONE = (2, 3)


def halves(value, count):
    parts = []
    for _ in range(count):
        part = value.astype(BF16)
        parts.append(part)
        value = value - part.astype(F32)
    return parts


def spread(first_head, width, copies):
    lane = lax.broadcasted_iota(jnp.int32, (copies * LANES, width), 0) % LANES
    column = lax.broadcasted_iota(jnp.int32, (copies * LANES, width), 1)
    return (lane == first_head + column // HEAD_DIM).astype(BF16)


def dot(a, b):
    return jnp.dot(a, b, preferred_element_type=F32)


def ds(start, width):
    return pl.ds(pl.multiple_of(start, LANES), width)


def run(copies, sems):
    started = []
    for i, (source, target) in enumerate(copies):
        copy = pltpu.make_async_copy(source, target, sems.at[i])
        copy.start()
        started.append(copy)
    return started


PER_GROUP = HEADS * HEAD_DIM // GROUPS
INNER = HEADS * HEAD_DIM


def channels(group, first, width):
    return ds(group * PER_GROUP + first, width)


def pack_first_kernel(shards, place, xbc, send, sems):
    core, shard = place[2], place[4]
    count = xbc.shape[0]
    width = WIDTHS[0]
    copies = []
    for r in range(shards):
        group = (shard ^ r) * PAIR + 1 - core
        copies.append((xbc.at[:, channels(group, 0, width)], send.at[:, r * width : (r + 1) * width]))
        last, rows = xbc.at[count - 16 :], slice(16 * r, 16 * r + 16)
        to = shards * width
        copies.append((last.at[:, channels(group, width, PER_GROUP - width)], send.at[rows, to : to + PER_GROUP - width]))
        to += PER_GROUP - width
        for i in range(2):
            at = ds(INNER + (i * GROUPS + group) * STATE, STATE)
            copies.append((last.at[:, at], send.at[rows, to + i * STATE : to + (i + 1) * STATE]))
    for copy in run(copies, sems):
        copy.wait()


def pack_kernel(shards, place, xbc, dt_raw, order, send, tail, sems):
    core, shard = place[2], place[4]
    count = xbc.shape[0]
    first = WIDTHS[0]
    width = PER_GROUP - first
    rest = width * shards
    size = PER_GROUP + 2 * STATE
    copies = []
    for r in range(shards):
        group = (shard ^ r) * PAIR + 1 - core
        copies.append((xbc.at[:, channels(group, first, width)], send.at[:, r * width : (r + 1) * width]))
        for i in range(2):
            to = rest + (i * shards + r) * STATE
            copies.append((xbc.at[:, ds(INNER + (i * GROUPS + group) * STATE, STATE)], send.at[:, to : to + STATE]))
    copies.append((dt_raw, send.at[:, send.shape[1] - HEADS :]))
    for r in range(shards):
        group, to = (shard ^ r) * PAIR + core, r * size
        last = xbc.at[count - 16 :]
        copies.append((last.at[:, channels(group, 0, PER_GROUP)], tail.at[:, to : to + PER_GROUP]))
        for i in range(2):
            at = ds(INNER + (i * GROUPS + group) * STATE, STATE)
            start = to + PER_GROUP + i * STATE
            copies.append((last.at[:, at], tail.at[:, start : start + STATE]))
    for copy in run(copies, sems):
        copy.wait()


def taps_kernel(place, weight, bias, order, taps, offset, sems):
    copies = []
    for source, target in ((weight, taps), (bias, offset)):
        copies.append((source.at[:, channels(place[0], 0, PER_GROUP)], target.at[:, :PER_GROUP]))
        for i in range(2):
            at = ds(INNER + (i * GROUPS + place[0]) * STATE, STATE)
            start = PER_GROUP + i * STATE
            copies.append((source.at[:, at], target.at[:, start : start + STATE]))
    for copy in run(copies, sems):
        copy.wait()


def put_edge(shards, place, got, tail, out):
    count = got.shape[0]
    first = WIDTHS[0]
    size = PER_GROUP + 2 * STATE
    for r in range(shards):
        theirs = [got[count - 16 :, r * first : (r + 1) * first]]
        theirs.append(got[16 * r : 16 * r + 16, shards * first :])
        to = r * size
        for part in theirs:
            at = slice(to, to + part.shape[1])
            rows = jnp.where(place[2] == 0, part.astype(F32), tail[:, at].astype(F32))
            out[:, at] = rows[13:16].astype(BF16)
            to = at.stop


def total_of(piece):
    return WIDTHS[piece] + sum(LANES if kind == "D" else STATE for kind in RESTS[piece])


def merge_kernel(shards, plan, unread, place, xbc, dt_raw, got_first, got, edges, *refs):
    refs = refs[unread:]
    outs, sems = refs[: len(plan)], refs[-1]
    core, shard = place[2], place[4]
    count = xbc.shape[0]
    stride = PER_GROUP - WIDTHS[0]
    mine = pl.ds(pl.multiple_of(core * count, count), count)
    other = pl.ds(pl.multiple_of((1 - core) * count, count), count)
    copies, steps = [], []
    for out, (r, pieces) in zip(outs, plan):
        group = (shard ^ r) * PAIR + core
        to = 0
        for piece in pieces:
            first, width = sum(WIDTHS[:piece]), WIDTHS[piece]
            if piece == 0:
                source = got_first.at[:, r * width : (r + 1) * width]
            else:
                at = r * stride + first - WIDTHS[0]
                source = got.at[:, at : at + width]
            if width:
                copies.append((xbc.at[:, channels(group, first, width)], out.at[mine, to : to + width]))
                copies.append((source, out.at[other, to : to + width]))
            to += width
            for kind in RESTS[piece]:
                if kind == "D":
                    steps.append((out, r, to))
                    to += LANES
                    continue
                i = "BC".index(kind)
                at = ds(INNER + (i * GROUPS + group) * STATE, STATE)
                copies.append((xbc.at[:, at], out.at[mine, to : to + STATE]))
                at = stride * shards + (i * shards + r) * STATE
                copies.append((got.at[:, at : at + STATE], out.at[other, to : to + STATE]))
                to += STATE
    started = run(copies, sems)
    if len(refs) > len(plan) + 1:
        put_edge(shards, place, got_first, edges, refs[-2])
    if steps:
        lane = lax.broadcasted_iota(jnp.int32, (count, LANES), 1)
        per_tile = LANES * GROUPS // HEADS
        heads = HEADS // GROUPS
        for out, r, to in steps:
            group = (shard ^ r) * PAIR + core
            tile, shift = group // per_tile, (LANES - (group % per_tile) * heads) % LANES
            own = dt_raw[:, ds(tile * LANES, LANES)].astype(F32)
            theirs = got[:, ds(got.shape[1] - HEADS + tile * LANES, LANES)].astype(F32)
            low = jnp.where(core == 0, own, theirs)
            high = jnp.where(core == 0, theirs, own)
            packed = jnp.zeros((count // 2, LANES), F32)
            for j, rows in enumerate((low, high)):
                rows = jnp.where(lane < heads, pltpu.roll(rows, shift, 1), 0.0)
                for i in range(2):
                    part = rows[i * count // 2 : (i + 1) * count // 2]
                    packed = packed + pltpu.roll(part, (2 * j + i) * heads, 1)
            out[: count // 2, to : to + LANES] = packed.astype(BF16)
            size = PER_GROUP + 2 * STATE
            at = slice(r * size, (r + 1) * size)
            edge = jnp.concatenate([edges[:, at].astype(F32), jnp.zeros((1, size), F32)], 0)
            edge = jnp.concatenate([edge[:, q * LANES : (q + 1) * LANES] for q in range(size // LANES)], 0)
            fill = jnp.zeros((PAIR * count - count // 2 - edge.shape[0], LANES), F32)
            out[count // 2 :, to : to + LANES] = jnp.concatenate([edge, fill], 0).astype(BF16)
    for copy in started:
        copy.wait()


def view(refs, piece):
    return [(ref, 0) for ref in refs]


def convolve_in_order(place, blocks, columns, edge, tap, bias, wide, put):
    width = columns.stop - columns.start
    count = blocks[0][0].shape[0] // PAIR
    wide[5:8, :width] = edge
    for r, (block, origin) in enumerate(blocks):
        for core in range(PAIR):
            at = pl.multiple_of((core * len(blocks) + (place[4] ^ r)) * count + 8, 8)
            part = block[core * count : (core + 1) * count, origin + columns.start : origin + columns.stop]
            wide[pl.ds(at, count), :width] = part.astype(F32)
    tap, bias = tap * 0.5, bias * 0.5
    for start in range(0, PAIR * len(blocks) * count, count):
        acc = bias + tap[0:1] * wide[start + 5 : start + 5 + count, :width]
        acc = acc + tap[1:2] * wide[start + 6 : start + 6 + count, :width]
        acc = acc + tap[2:3] * wide[start + 7 : start + 7 + count, :width]
        acc = acc + tap[3:4] * wide[start + 8 : start + 8 + count, :width]
        put(start, count, (acc + acc * jnp.tanh(acc)).astype(BF16))


def prep_kernel(shards, place, *refs):
    blocks, (taps, offset, a_ref, bias_ref, skip_ref, order) = refs[:shards], refs[shards : shards + 6]
    b_ref, edge_ref, cum_ref, row_ref, factor_ref, tail_ref, skip_out, dt_ref, wide = refs[shards + 6 :]
    blocks = view(blocks, 1)
    start = WIDTHS[1]
    last = total_of(1) - LANES
    size = edge_ref.shape[1]
    count = blocks[0][0].shape[0] // PAIR
    half, heads = count // 2, HEADS // GROUPS
    columns = [block[:, origin + last : origin + last + LANES].astype(F32) for block, origin in blocks]
    edge = columns[0][half : half + 4 * size // LANES]
    for column in columns[1:]:
        edge = edge + column[half : half + 4 * size // LANES]
    for q in range(size // LANES):
        edge_ref[:, q * LANES : (q + 1) * LANES] = edge[4 * q : 4 * q + 4]
    for r, column in enumerate(columns):
        packed = column[:half]
        for j in range(2 * PAIR):
            at = ((j // 2) * shards + (place[4] ^ r)) * count + (j % 2) * half
            rows = packed if j == 0 else pltpu.roll(packed, LANES - j * heads, 1)
            dt_ref[pl.ds(pl.multiple_of(at, half), half), :] = rows

    def put(start, count, value):
        b_ref[start : start + count] = value

    at = slice(PER_GROUP, PER_GROUP + STATE)
    convolve_in_order(
        place, blocks, slice(start, start + STATE), edge_ref[0:3, at], taps[:, at], offset[:, at], wide, put
    )
    per_tile = LANES * GROUPS // HEADS
    group = place[0]
    tile = group // per_tile
    shift = (LANES - (group % per_tile) * heads) % LANES

    def lanes_of(ref):
        return pltpu.roll(jnp.broadcast_to(ref[pl.ds(tile, 1), :], (8, LANES)), shift, 1)

    rate = -jnp.exp(lanes_of(a_ref)[0:1])
    raw = dt_ref[...] + lanes_of(bias_ref)[0:1]
    step = jnp.maximum(raw, 0.0) + jnp.log1p(jnp.exp(-jnp.abs(raw)))
    skip = lanes_of(skip_ref)
    skip_out[...] = jnp.concatenate(halves(jnp.concatenate([skip, skip], 0), 3), 1)
    lower = (
        lax.broadcasted_iota(jnp.int32, (BLOCK, BLOCK), 0)
        >= lax.broadcasted_iota(jnp.int32, (BLOCK, BLOCK), 1)
    ).astype(BF16)
    valid = lax.broadcasted_iota(jnp.int32, (BLOCK, LANES), 1) < heads
    for block in range(PAIR):
        at = slice(block * BLOCK, (block + 1) * BLOCK)
        here = jnp.where(valid, step[at], 1.0)
        parts = halves(here * rate, 3)
        cum = dot(lower, parts[0]) + (dot(lower, parts[1]) + dot(lower, parts[2]))
        cum = cum * LOG2E
        cum_ref[at] = cum
        row_ref[:, at] = jnp.transpose(cum - jnp.log2(here))
        factor_ref[at] = jnp.concatenate(halves(jnp.exp2(cum), 2), 1)
        tail = jnp.exp2(cum[BLOCK - 1 :] - cum) * here
        tail_ref[at] = jnp.concatenate(halves(tail, 2), 1)


def score_kernel(shards, place, *refs):
    blocks, refs = refs[:shards], refs[shards:]
    taps, offset, edge_ref, b_ref, c_ref, score_ref, wide = (*refs[:4], *refs[-3:])
    blocks = view(blocks, 3)
    start = WIDTHS[3]
    at = slice(PER_GROUP + STATE, PER_GROUP + 2 * STATE)

    def put(start, count, value):
        c_ref[start : start + count] = value

    convolve_in_order(
        place, blocks, slice(start, start + STATE), edge_ref[0:3, at], taps[:, at], offset[:, at], wide, put
    )
    for block in range(PAIR):
        at = slice(block * BLOCK, (block + 1) * BLOCK)
        score_ref[at] = lax.dot_general(
            c_ref[at], b_ref[at], (((1,), (1,)), ((), ())), preferred_element_type=F32
        )


def decay_of(ref):
    decay = ref[STATE : STATE + 16].astype(F32)
    return decay[0:1] + (decay[1:2] + decay[2:3])


def put_decay(ref, decay):
    row = lax.broadcasted_iota(jnp.int32, (16, ref.shape[1]), 0)
    high, middle, low = (part.astype(F32) for part in halves(decay, 3))
    packed = jnp.where(row == 0, high, jnp.where(row == 1, middle, jnp.where(row == 2, low, 0.0)))
    ref[STATE:] = packed.astype(BF16)


def state_kernel(shards, part, sizes, place, *refs):
    blocks, refs = refs[:shards], refs[shards:]
    taps, offset, edge_ref, b_ref, factor_ref, tail_ref = refs[:6]
    x_ref, own_ref, *sends, wide = refs[-3 - len(sizes) :]
    piece, start, width = part
    first = sum(WIDTHS[:piece]) + start
    at = slice(first, first + width)

    def put(row, count, value):
        x_ref[row : row + count] = value

    blocks = view(blocks, piece)
    columns = slice(start, start + width)
    convolve_in_order(place, blocks, columns, edge_ref[0:3, at], taps[:, at], offset[:, at], wide, put)
    expand = spread(first // HEAD_DIM, width, 2)
    both = []
    for block in range(PAIR):
        at = slice(block * BLOCK, (block + 1) * BLOCK)
        loaded = (x_ref[at].astype(F32) * dot(tail_ref[at], expand)).astype(BF16)
        both.append(
            lax.dot_general(b_ref[at], loaded, (((0,), (0,)), ((), ())), preferred_element_type=F32)
        )
    ends = [dot(factor_ref[(i + 1) * BLOCK - 16 : (i + 1) * BLOCK], expand)[15:16] for i in range(PAIR)]
    own_ref[...] = both[0]
    end = (ends[1] * both[0] + both[1]).astype(BF16)
    decay = ends[0] * ends[1]
    start = 0
    for send_ref in sends:
        at = slice(start, start + send_ref.shape[1])
        send_ref[0:STATE] = end[:, at]
        put_decay(send_ref, decay[:, at])
        start = at.stop


def combine_kernel(count, *refs):
    early, late, out_ref = refs[:count], refs[count : 2 * count], refs[-1]
    start = 0
    for early_ref, late_ref in zip(early, late):
        at = slice(start, start + late_ref.shape[1])
        decay = decay_of(late_ref)
        total = decay * early_ref[:STATE].astype(F32) + late_ref[:STATE].astype(F32)
        out_ref[:STATE, at] = total.astype(BF16)
        put_decay(out_ref.at[:, at], decay * decay_of(early_ref))
        start = at.stop


def mix(first_head, x_ref, cum_ref, row_ref, score_ref, skip_ref, put):
    width = x_ref.shape[1]
    half = BLOCK // 2
    expand = spread(first_head, width, 3)
    skip = dot(skip_ref[...], expand)[0:1]
    lower = lax.broadcasted_iota(jnp.int32, (half, half), 0) >= lax.broadcasted_iota(
        jnp.int32, (half, half), 1
    )
    lane = lax.broadcasted_iota(jnp.int32, (BLOCK, LANES), 1)
    for block in range(PAIR):
        base = block * BLOCK
        for tile in range(width // LANES):
            columns = slice(tile * LANES, (tile + 1) * LANES)
            x = x_ref[base : base + BLOCK, columns]
            top = skip[:, columns] * x[:half].astype(F32)
            bottom = skip[:, columns] * x[half:].astype(F32)
            for side in range(LANES // HEAD_DIM):
                head = first_head + tile * (LANES // HEAD_DIM) + side
                own = jnp.where(lane // HEAD_DIM == side, x, jnp.zeros_like(x))
                cum = cum_ref[base : base + BLOCK, head : head + 1]
                row = row_ref[head : head + 1, base : base + BLOCK]
                diag = jnp.where(lower, cum[:half] - row[:, :half], -1e30)
                mixing = jnp.exp2(diag) * score_ref[base : base + half, :half]
                top = top + dot(mixing.astype(BF16), own[:half])
                left = jnp.exp2(cum[half:] - row[:, :half]) * score_ref[base + half : base + BLOCK, :half]
                diag = jnp.where(lower, cum[half:] - row[:, half:], -1e30)
                right = jnp.exp2(diag) * score_ref[base + half : base + BLOCK, half:]
                mixing = jnp.concatenate([left.astype(BF16), right.astype(BF16)], 1)
                bottom = bottom + dot(mixing, own)
            put(block, slice(base, base + half), columns, top)
            put(block, slice(base + half, base + BLOCK), columns, bottom)


def local_kernel(first_head, x_ref, cum_ref, row_ref, score_ref, skip_ref, *refs):
    out_ref = refs[-1]

    def put(block, rows, columns, value):
        out_ref[rows, columns] = value

    mix(first_head, x_ref, cum_ref, row_ref, score_ref, skip_ref, put)


def carry(first_head, core, lasts, befores, alones, own_ref, c_ref, factor_ref, add, keep_ref, send_ref):
    expand = spread(first_head, own_ref.shape[1], 2)
    last, before = (
        refs[0][...] if len(refs) == 1 else jnp.concatenate([ref[...] for ref in refs], 1)
        for refs in (lasts, befores)
    )
    held = last[:STATE].astype(F32) + decay_of(last) * before[:STATE].astype(F32)
    for alone in alones:
        held = held + alone[:STATE].astype(F32)
    factor = dot(factor_ref[...], expand)
    outs = []
    for block in range(PAIR):
        at = slice(block * BLOCK, (block + 1) * BLOCK)
        carried = dot(c_ref[at], held.astype(BF16))
        outs.append((add[at] + factor[at] * carried).astype(BF16))
        held = factor[BLOCK - 1 : BLOCK] * held + own_ref[...]

    @pl.when(core == 0)
    def _():
        keep_ref[...] = outs[0]
        send_ref[...] = outs[1]

    @pl.when(core == 1)
    def _():
        keep_ref[...] = outs[1]
        send_ref[...] = outs[0]


def final_kernel(first_head, counts, place, *refs):
    groups = []
    for number in counts:
        groups.append(refs[:number])
        refs = refs[number:]
    carry(first_head, place[2], *groups, *refs[:4], *refs[-2:])


def finish_kernel(first_head, counts, place, *refs):
    groups = []
    for number in counts:
        groups.append(refs[:number])
        refs = refs[number:]
    own_ref, c_ref, factor_ref = refs[:3]
    keep_ref, send_ref, partial = refs[-3:]
    local_kernel(first_head, *refs[3:8], partial)
    carry(first_head, place[2], *groups, own_ref, c_ref, factor_ref, partial, keep_ref, send_ref)


def place_kernel(firsts, place, *refs):
    count = len(firsts)
    keeps, gots = refs[:count], refs[count : 2 * count]
    out, sems = refs[-2:]
    core = place[2]
    half = out.shape[1] // PAIR
    copies = []
    for first, keep, got in zip(firsts, keeps, gots):
        width = keep.shape[1]
        copies.append((keep, out.at[:, ds(core * half + first, width)]))
        copies.append((got, out.at[:, ds((1 - core) * half + first, width)]))
    for copy in run(copies, sems):
        copy.wait()


def put_in_place(firsts, shape, place, keeps, gots):
    smem, vmem, hbm = (pl.BlockSpec(memory_space=m) for m in (pltpu.SMEM, pltpu.VMEM, pltpu.HBM))
    count = len(firsts)
    return pl.pallas_call(
        functools.partial(place_kernel, firsts),
        out_shape=jax.ShapeDtypeStruct(shape, BF16),
        in_specs=[smem] + [vmem] * (2 * count),
        out_specs=hbm,
        scratch_shapes=[pltpu.SemaphoreType.DMA((2 * count,))],
        compiler_params=pltpu.CompilerParams(vmem_limit_bytes=16 << 20),
        cost_estimate=pl.CostEstimate(flops=1, bytes_accessed=1, transcendentals=0),
        name="place",
    )(place, *keeps, *gots)


class Stay:
    def __init__(self, array):
        self.array = array


def call(body, outs, operands, scratch=(), flops=0, transcendentals=0, name=None, limit=16 << 20):
    shapes = [jax.ShapeDtypeStruct(shape, dtype) for shape, dtype in outs]
    smem, vmem, hbm = (pl.BlockSpec(memory_space=m) for m in (pltpu.SMEM, pltpu.VMEM, pltpu.HBM))
    specs = [
        hbm if isinstance(o, Stay) else smem if o.dtype == jnp.int32 else vmem for o in operands
    ]
    moved = sum(o.size * o.dtype.itemsize for o in shapes) * 2
    return pl.pallas_call(
        body,
        out_shape=shapes,
        in_specs=specs,
        out_specs=[vmem] * len(outs),
        scratch_shapes=scratch,
        compiler_params=pltpu.CompilerParams(vmem_limit_bytes=limit),
        cost_estimate=pl.CostEstimate(flops=1, bytes_accessed=1, transcendentals=0),
        name=name,
    )(*[o.array if isinstance(o, Stay) else o for o in operands])


def paired(xbc, dt_raw, conv_weight, conv_bias, a_log, dt_bias, skip_gain):
    axes = ("ctx", "head")
    shards, length = lax.axis_size("head"), lax.axis_size("ctx")
    devices, peers = shards * length, shards * PAIR
    tok = xbc.shape[0]
    slab = tok * peers
    context, shard = lax.axis_index("ctx"), lax.axis_index("head")
    pair, core = context // PAIR, context % PAIR
    group = shard * PAIR + core
    place = jnp.stack([group, pair, core, core * shards + shard, shard]).astype(jnp.int32)

    def over(block, target):
        route = [(i, target(i)) for i in range(devices)]
        return lax.ppermute(block, axes, [(i, j) for i, j in route if j is not None and j < devices])

    def swap(block):
        return over(block, lambda i: i ^ shards)

    rows = Stay(xbc)
    size = PER_GROUP + 2 * STATE
    (sent,) = call(
        functools.partial(pack_first_kernel, shards),
        [((tok, shards * WIDTHS[0] + size - WIDTHS[0]), BF16)],
        [place, rows],
        scratch=[pltpu.SemaphoreType.DMA((4 * shards,))],
        name="pack_first",
    )
    got_first = swap(sent)
    sent, tail = call(
        functools.partial(pack_kernel, shards),
        [((tok, shards * (size - WIDTHS[0]) + HEADS), BF16), ((16, shards * size), BF16)],
        [place, rows, Stay(dt_raw), Stay(sent)],
        scratch=[pltpu.SemaphoreType.DMA((6 * shards + 1,))],
        name="pack",
    )
    got_rest = swap(sent)
    taps, offset = call(
        taps_kernel,
        [((4, size), F32), ((1, size), F32)],
        [place, Stay(conv_weight), Stay(conv_bias[None]), Stay(got_rest)],
        scratch=[pltpu.SemaphoreType.DMA((6,))],
        name="taps",
    )

    def send_on(plan, order, tail=None, edges=None):
        unused = Stay(got_first)
        parts = [p for _, pieces in plan for p in pieces]
        made = [] if tail is None else [((3, shards * size), BF16)]
        return call(
            functools.partial(merge_kernel, shards, plan, len(order)),
            [((PAIR * tok, sum(map(total_of, pieces))), BF16) for _, pieces in plan] + made,
            [
                place,
                rows,
                Stay(dt_raw) if edges is None else dt_raw,
                got_first if 0 in parts else unused,
                got_rest if any(parts) else unused,
                next((o for o in (tail, edges) if o is not None), unused),
            ]
            + [Stay(o) for o in order],
            scratch=[pltpu.SemaphoreType.DMA((sum(2 + 2 * len(RESTS[p]) for p in parts),))],
            name="merge",
        )

    def travel(blocks):
        return [blocks[0]] + [over(blocks[r], lambda i, r=r: i ^ r) for r in range(1, shards)]

    def plan(piece):
        return [(r, (piece,)) for r in range(shards)]

    *first_blocks, edges = send_on(plan(0), [], tail)
    message = [travel(first_blocks)]
    edges = over(edges, lambda i: i + peers if i % shards == shards - 1 else None)
    second_blocks = send_on(plan(1), [first_blocks[0]], None, edges)
    message.append(travel(second_blocks))
    third_blocks = send_on(plan(2), [*message[0][1:], *message[1][2:]])
    message.append(travel(third_blocks))

    def seen(piece):
        return message[piece]

    tiles = [p.reshape(HEADS // LANES, LANES) for p in (a_log, dt_bias, skip_gain)]
    b, edge, cum, row, factor, tail, skip = call(
        functools.partial(prep_kernel, shards),
        [
            ((slab, STATE), BF16),
            ((4, size), F32),
            ((slab, LANES), F32),
            ((LANES, slab), F32),
            ((slab, 2 * LANES), BF16),
            ((slab, 2 * LANES), BF16),
            ((16, 3 * LANES), BF16),
        ],
        [place] + seen(1) + [taps, offset] + tiles + [Stay(third_blocks[0])],
        scratch=[pltpu.VMEM((slab, LANES), F32), pltpu.VMEM((slab + 8, STATE), F32)],
        name="prep",
    )
    count = len(GROUPED)
    x, sent, own, last, joined, before, alone, keep, send = ([None] * count for _ in range(9))

    def first_head(i):
        return (sum(WIDTHS[: GROUPED[i][0]]) + GROUPED[i][1]) // HEAD_DIM

    def state_of(i, order):
        piece, _, width = GROUPED[i]
        x[i], own[i], *sent[i] = call(
            functools.partial(state_kernel, shards, GROUPED[i], FIRST_ROUND[i]),
            [((slab, width), BF16), ((STATE, width), F32)] + [((STATE + 16, w), BF16) for w in FIRST_ROUND[i]],
            [place] + seen(piece) + [taps, offset, edge, b, factor, tail] + [Stay(o) for o in order],
            scratch=[pltpu.VMEM((slab + 8, width), F32)],
            name="state",
        )
        every = i not in ALONE
        last[i] = [over(part, lambda i: i + peers if every or i // peers % 2 == 0 else None) for part in sent[i]]

    def combine_of(i, order):
        joined[i], before[i], alone[i] = [], [], []
        step = len(FIRST_ROUND[i]) // len(SECOND_ROUND[i])
        for j, width in enumerate(SECOND_ROUND[i]):
            early, late = last[i][j * step : (j + 1) * step], sent[i][j * step : (j + 1) * step]
            (total,) = call(
                functools.partial(combine_kernel, len(early)),
                [((STATE + 16, width), BF16)],
                early + late + [Stay(o) for o in order],
                name="combine",
            )
            joined[i].append(total)
            if i in ALONE:
                before[i].append(over(total, lambda i: i + 2 * peers if i // peers == 1 else None))
                alone[i].append(over(total, lambda i: i + peers if i // peers == 1 else None))
            else:
                before[i].append(over(total, lambda i: i + 2 * peers))
            order = [total]

    def finish_of(body, i, operands, order, **more):
        keep[i], send[i] = call(
            functools.partial(body, first_head(i), (len(last[i]), len(before[i]), len(alone[i]))),
            [((BLOCK, GROUPED[i][2]), BF16)] * 2,
            [place, *last[i], *before[i], *alone[i], own[i], c, factor] + operands + [Stay(o) for o in order],
            name="final",
            **more,
        )

    state_of(0, [])
    combine_of(0, [])
    fourth_blocks = send_on(plan(3), [joined[0][0]])
    message.append(travel(fourth_blocks))
    state_of(1, [fourth_blocks[0]])
    combine_of(1, [])
    state_of(2, joined[1])
    state_of(3, sent[2])
    c, score = call(
        functools.partial(score_kernel, shards),
        [((slab, STATE), BF16), ((slab, BLOCK), F32)],
        [place] + seen(3) + [taps, offset, edge, b] + [Stay(o) for o in sent[3] + before[1]],
        scratch=[pltpu.VMEM((slab + 8, STATE), F32)],
        name="score",
    )
    mixes = [cum, row, score, skip]

    def in_full(i, order):
        wide = [pltpu.VMEM((slab, GROUPED[i][2]), F32)]
        finish_of(finish_kernel, i, [x[i]] + mixes, order, scratch=wide)

    combine_of(2, [score])
    in_full(1, joined[2])
    combine_of(3, [keep[1]])
    order, partial = joined[3][0], {}
    for i in (2, 3):
        (partial[i],) = call(
            functools.partial(local_kernel, first_head(i)),
            [(x[i].shape, F32)],
            [x[i]] + mixes + [Stay(order)],
            name="local",
        )
        order = partial[i]
    in_full(0, [order])
    order = keep[0]
    for i in (2, 3):
        finish_of(final_kernel, i, [partial[i]], [order])
        order = keep[i]
    firsts = [first_head(i) * HEAD_DIM for i in range(count)]
    return put_in_place(firsts, (BLOCK, PAIR * PER_GROUP), place, keep, [swap(o) for o in send])


def solution(mesh):
    in_specs = (P(("ctx", "head"), None), P(("ctx", "head"), None), P(), P(), P(), P(), P())
    out_specs = P("ctx", "head")
    shards, length = mesh.shape["head"], mesh.shape["ctx"]

    def program(xbc, *rest):
        slab = xbc.shape[0] // length
        fits = shards == GROUPS // PAIR and length == 4 * PAIR and slab == BLOCK
        return jax.shard_map(
            paired if fits else on_device,
            mesh=mesh,
            in_specs=in_specs,
            out_specs=out_specs,
            check_vma=False,
        )(xbc, *rest)

    return program
```

```python
import functools

import jax
import jax.numpy as jnp
from jax import lax
from jax.experimental import pallas as pl
from jax.experimental.pallas import tpu as pltpu
from jax.sharding import PartitionSpec as P

HEADS = 256
HEAD_DIM = 64
STATE = 256
GROUPS = 8
BLOCK = 256


def from_behind(block, axis, distance):
    devices = range(lax.axis_size(axis))
    route = [(i - distance, i) for i in devices if i - distance in devices]
    return lax.ppermute(block, axis, route)


def carried_in(array, axis, combine, identity):
    length, index = (lax.axis_size(axis), lax.axis_index(axis))
    everything = jax.tree.map(lambda part: lax.all_gather(part, axis), array)
    start = jax.tree.map(
        lambda part, zero: jnp.broadcast_to(jnp.asarray(zero, part.dtype), part.shape),
        array,
        identity,
    )

    def hop(k, before):
        reached = k < index
        new = combine(before, jax.tree.map(lambda part: part[k], everything))
        return jax.tree.map(lambda a, b: jnp.where(reached, a, b), new, before)

    return lax.fori_loop(0, length, hop, start)


def convolve(rows, edge, weight, bias):
    count = rows.shape[0]
    wide = jnp.concatenate([edge, rows], 0).astype(jnp.float32)
    acc = bias[None, :] + weight[0] * wide[0:count]
    acc = acc + weight[1] * wide[1 : count + 1]
    acc = acc + weight[2] * wide[2 : count + 2]
    acc = acc + weight[3] * wide[3 : count + 3]
    return jax.nn.silu(acc).astype(jnp.bfloat16)


def rearrange_heads(rows, shards, per_dev, groups_dev, per_group):
    count = rows.shape[0]
    inner = HEADS * HEAD_DIM
    replicate_groups = max(1, per_group // per_dev)
    heads_part = rows[:, :inner].reshape(count, shards, per_dev * HEAD_DIM)
    b_part = rows[:, inner : inner + GROUPS * STATE].reshape(count, GROUPS, STATE)
    c_part = rows[:, inner + GROUPS * STATE :].reshape(count, GROUPS, STATE)
    b_part = jnp.repeat(b_part, replicate_groups, axis=1).reshape(count, shards, groups_dev * STATE)
    c_part = jnp.repeat(c_part, replicate_groups, axis=1).reshape(count, shards, groups_dev * STATE)
    return jnp.concatenate([heads_part, b_part, c_part], axis=2)


def inner_block(xs, bmat, cmat, steps, cum):
    size = xs.shape[0]
    lower = jnp.arange(size)[:, None] >= jnp.arange(size)[None, :]
    scores = jnp.einsum("qgn,kgn->gqk", cmat, bmat, preferred_element_type=jnp.float32)
    order = jnp.transpose(cum, (1, 2, 0))
    gap = order[..., :, None] - order[..., None, :]
    decay = jnp.exp(jnp.where(lower, gap, -jnp.inf))
    mixing = (scores[:, None] * decay * jnp.transpose(steps, (1, 2, 0))[..., None, :]).astype(
        jnp.bfloat16
    )
    local = jnp.einsum("gjqk,kgjp->qgjp", mixing, xs, preferred_element_type=jnp.float32)
    tail = jnp.exp(cum[size - 1][None] - cum) * steps
    loaded = (bmat[:, :, None, :].astype(jnp.float32) * tail[..., None]).astype(jnp.bfloat16)
    block_state = jnp.einsum("kgjn,kgjp->gjnp", loaded, xs, preferred_element_type=jnp.float32)
    return (local, block_state)


def on_device(xbc, dt_raw, conv_weight, conv_bias, a_log, dt_bias, skip_gain):
    tok = xbc.shape[0]
    shards = lax.axis_size("head")
    per_dev = HEADS // shards
    per_group = HEADS // GROUPS
    groups_dev = max(1, per_dev // per_group)
    heads_per_cluster = per_dev // groups_dev
    sent = rearrange_heads(xbc, shards, per_dev, groups_dev, per_group)
    mine, rates = (
        lax.all_to_all(sent, "head", split_axis=1, concat_axis=0, tiled=True),
        lax.all_to_all(
            dt_raw.reshape(tok, shards, per_dev), "head", split_axis=1, concat_axis=0, tiled=True
        ),
    )
    slab = tok * shards
    mine = mine.reshape(slab, mine.shape[2])
    rates = rates.reshape(slab, per_dev)
    shard = lax.axis_index("head")
    taps = lax.dynamic_index_in_dim(
        rearrange_heads(conv_weight, shards, per_dev, groups_dev, per_group),
        shard,
        1,
        keepdims=False,
    )
    offset = lax.dynamic_index_in_dim(
        rearrange_heads(conv_bias[None, :], shards, per_dev, groups_dev, per_group),
        shard,
        1,
        keepdims=False,
    )
    edge = from_behind(mine[slab - 3 :], "ctx", 1)
    mine = convolve(mine, edge, taps, offset[0])
    nchunk = slab // BLOCK
    width = per_dev * HEAD_DIM
    xs = mine[:, :width].reshape(nchunk, BLOCK, groups_dev, heads_per_cluster, HEAD_DIM)
    bmat = mine[:, width : width + groups_dev * STATE].reshape(nchunk, BLOCK, groups_dev, STATE)
    cmat = mine[:, width + groups_dev * STATE :].reshape(nchunk, BLOCK, groups_dev, STATE)
    first = shard * per_dev
    rate = (-jnp.exp(lax.dynamic_slice_in_dim(a_log, first, per_dev))).reshape(
        groups_dev, heads_per_cluster
    )
    bias_dt = lax.dynamic_slice_in_dim(dt_bias, first, per_dev).reshape(
        groups_dev, heads_per_cluster
    )
    skip = lax.dynamic_slice_in_dim(skip_gain, first, per_dev).reshape(
        groups_dev, heads_per_cluster
    )
    steps = jax.nn.softplus(
        rates.astype(jnp.float32).reshape(nchunk, BLOCK, groups_dev, heads_per_cluster) + bias_dt
    )
    cum = jnp.cumsum(steps * rate, axis=1)

    def block_step(carry, item):
        held, product = carry
        x_part, b_part, c_part, step_part, cum_part = item
        local, block_state = inner_block(x_part, b_part, c_part, step_part, cum_part)
        lifted = c_part.astype(jnp.float32)[:, :, None, :] * jnp.exp(cum_part)[..., None]
        carried = jnp.einsum("qgjn,gjnp->qgjp", lifted, held, precision=lax.Precision.HIGHEST)
        partial_out = local + carried + skip[..., None] * x_part.astype(jnp.float32)
        end = jnp.exp(cum_part[BLOCK - 1])
        return ((end[..., None, None] * held + block_state, product * end), (partial_out, product))

    zero_state = jnp.zeros((groups_dev, heads_per_cluster, STATE, HEAD_DIM), jnp.float32)
    unit = jnp.ones((groups_dev, heads_per_cluster), jnp.float32)
    (slab_state, slab_decay), (partials, product_in) = lax.scan(
        block_step, (zero_state, unit), (xs, bmat, cmat, steps, cum)
    )

    def combine(preceding_state, later):
        return (
            preceding_state[0] * later[0],
            later[0][..., None, None] * preceding_state[1] + later[1],
        )

    _, entering = carried_in((slab_decay, slab_state), "ctx", combine, (unit, zero_state))
    projected = jnp.einsum(
        "cqgn,gjnp->cqgjp", cmat.astype(jnp.float32), entering, precision=lax.Precision.HIGHEST
    )
    factor = jnp.exp(cum) * product_in[:, None]
    total = partials + factor[..., None] * projected
    return total.astype(jnp.bfloat16).reshape(slab, width)


PAIR = 2
LANES = 128
LOG2E = 1.4426950408889634
F32, BF16 = jnp.float32, jnp.bfloat16
WIDTHS = (512, 0, 640, 896)
RESTS = ("", "BCD", "", "")
GROUPED = ((0, 0, 512), (2, 0, 640), (3, 0, 512), (3, 512, 384))
FIRST_ROUND = ((256, 256), (384, 256), (512,), (384,))
SECOND_ROUND = ((512,), (384, 256), (512,), (384,))
ALONE = (2, 3)


def halves(value, count):
    parts = []
    for _ in range(count):
        part = value.astype(BF16)
        parts.append(part)
        value = value - part.astype(F32)
    return parts


def spread(first_head, width, copies):
    lane = lax.broadcasted_iota(jnp.int32, (copies * LANES, width), 0) % LANES
    column = lax.broadcasted_iota(jnp.int32, (copies * LANES, width), 1)
    return (lane == first_head + column // HEAD_DIM).astype(BF16)


def dot(a, b):
    return jnp.dot(a, b, preferred_element_type=F32)


def ds(start, width):
    return pl.ds(pl.multiple_of(start, LANES), width)


def run(copies, sems):
    started = []
    for i, (source, target) in enumerate(copies):
        copy = pltpu.make_async_copy(source, target, sems.at[i])
        copy.start()
        started.append(copy)
    return started


PER_GROUP = HEADS * HEAD_DIM // GROUPS
INNER = HEADS * HEAD_DIM


def channels(group, first, width):
    return ds(group * PER_GROUP + first, width)


def pack_first_kernel(shards, place, xbc, send, sems):
    core, shard = place[2], place[4]
    count = xbc.shape[0]
    width = WIDTHS[0]
    copies = []
    for r in range(shards):
        group = (shard ^ r) * PAIR + 1 - core
        copies.append((xbc.at[:, channels(group, 0, width)], send.at[:, r * width : (r + 1) * width]))
        last, rows = xbc.at[count - 16 :], slice(16 * r, 16 * r + 16)
        to = shards * width
        copies.append((last.at[:, channels(group, width, PER_GROUP - width)], send.at[rows, to : to + PER_GROUP - width]))
        to += PER_GROUP - width
        for i in range(2):
            at = ds(INNER + (i * GROUPS + group) * STATE, STATE)
            copies.append((last.at[:, at], send.at[rows, to + i * STATE : to + (i + 1) * STATE]))
    for copy in run(copies, sems):
        copy.wait()


def pack_kernel(shards, place, xbc, dt_raw, order, send, tail, sems):
    core, shard = place[2], place[4]
    count = xbc.shape[0]
    first = WIDTHS[0]
    width = PER_GROUP - first
    rest = width * shards
    size = PER_GROUP + 2 * STATE
    copies = []
    for r in range(shards):
        group = (shard ^ r) * PAIR + 1 - core
        copies.append((xbc.at[:, channels(group, first, width)], send.at[:, r * width : (r + 1) * width]))
        for i in range(2):
            to = rest + (i * shards + r) * STATE
            copies.append((xbc.at[:, ds(INNER + (i * GROUPS + group) * STATE, STATE)], send.at[:, to : to + STATE]))
    copies.append((dt_raw, send.at[:, send.shape[1] - HEADS :]))
    for r in range(shards):
        group, to = (shard ^ r) * PAIR + core, r * size
        last = xbc.at[count - 16 :]
        copies.append((last.at[:, channels(group, 0, PER_GROUP)], tail.at[:, to : to + PER_GROUP]))
        for i in range(2):
            at = ds(INNER + (i * GROUPS + group) * STATE, STATE)
            start = to + PER_GROUP + i * STATE
            copies.append((last.at[:, at], tail.at[:, start : start + STATE]))
    for copy in run(copies, sems):
        copy.wait()


def taps_kernel(place, weight, bias, order, taps, offset, sems):
    copies = []
    for source, target in ((weight, taps), (bias, offset)):
        copies.append((source.at[:, channels(place[0], 0, PER_GROUP)], target.at[:, :PER_GROUP]))
        for i in range(2):
            at = ds(INNER + (i * GROUPS + place[0]) * STATE, STATE)
            start = PER_GROUP + i * STATE
            copies.append((source.at[:, at], target.at[:, start : start + STATE]))
    for copy in run(copies, sems):
        copy.wait()


def put_edge(shards, place, got, tail, out):
    count = got.shape[0]
    first = WIDTHS[0]
    size = PER_GROUP + 2 * STATE
    for r in range(shards):
        theirs = [got[count - 16 :, r * first : (r + 1) * first]]
        theirs.append(got[16 * r : 16 * r + 16, shards * first :])
        to = r * size
        for part in theirs:
            at = slice(to, to + part.shape[1])
            rows = jnp.where(place[2] == 0, part.astype(F32), tail[:, at].astype(F32))
            out[:, at] = rows[13:16].astype(BF16)
            to = at.stop


def total_of(piece):
    return WIDTHS[piece] + sum(LANES if kind == "D" else STATE for kind in RESTS[piece])


def merge_kernel(shards, plan, unread, place, xbc, dt_raw, got_first, got, edges, *refs):
    refs = refs[unread:]
    outs, sems = refs[: len(plan)], refs[-1]
    core, shard = place[2], place[4]
    count = xbc.shape[0]
    stride = PER_GROUP - WIDTHS[0]
    mine = pl.ds(pl.multiple_of(core * count, count), count)
    other = pl.ds(pl.multiple_of((1 - core) * count, count), count)
    copies, steps = [], []
    for out, (r, pieces) in zip(outs, plan):
        group = (shard ^ r) * PAIR + core
        to = 0
        for piece in pieces:
            first, width = sum(WIDTHS[:piece]), WIDTHS[piece]
            if piece == 0:
                source = got_first.at[:, r * width : (r + 1) * width]
            else:
                at = r * stride + first - WIDTHS[0]
                source = got.at[:, at : at + width]
            if width:
                copies.append((xbc.at[:, channels(group, first, width)], out.at[mine, to : to + width]))
                copies.append((source, out.at[other, to : to + width]))
            to += width
            for kind in RESTS[piece]:
                if kind == "D":
                    steps.append((out, r, to))
                    to += LANES
                    continue
                i = "BC".index(kind)
                at = ds(INNER + (i * GROUPS + group) * STATE, STATE)
                copies.append((xbc.at[:, at], out.at[mine, to : to + STATE]))
                at = stride * shards + (i * shards + r) * STATE
                copies.append((got.at[:, at : at + STATE], out.at[other, to : to + STATE]))
                to += STATE
    started = run(copies, sems)
    if len(refs) > len(plan) + 1:
        put_edge(shards, place, got_first, edges, refs[-2])
    if steps:
        lane = lax.broadcasted_iota(jnp.int32, (count, LANES), 1)
        per_tile = LANES * GROUPS // HEADS
        heads = HEADS // GROUPS
        for out, r, to in steps:
            group = (shard ^ r) * PAIR + core
            tile, shift = group // per_tile, (LANES - (group % per_tile) * heads) % LANES
            own = dt_raw[:, ds(tile * LANES, LANES)].astype(F32)
            theirs = got[:, ds(got.shape[1] - HEADS + tile * LANES, LANES)].astype(F32)
            low = jnp.where(core == 0, own, theirs)
            high = jnp.where(core == 0, theirs, own)
            packed = jnp.zeros((count // 2, LANES), F32)
            for j, rows in enumerate((low, high)):
                rows = jnp.where(lane < heads, pltpu.roll(rows, shift, 1), 0.0)
                for i in range(2):
                    part = rows[i * count // 2 : (i + 1) * count // 2]
                    packed = packed + pltpu.roll(part, (2 * j + i) * heads, 1)
            out[: count // 2, to : to + LANES] = packed.astype(BF16)
            size = PER_GROUP + 2 * STATE
            at = slice(r * size, (r + 1) * size)
            edge = jnp.concatenate([edges[:, at].astype(F32), jnp.zeros((1, size), F32)], 0)
            edge = jnp.concatenate([edge[:, q * LANES : (q + 1) * LANES] for q in range(size // LANES)], 0)
            fill = jnp.zeros((PAIR * count - count // 2 - edge.shape[0], LANES), F32)
            out[count // 2 :, to : to + LANES] = jnp.concatenate([edge, fill], 0).astype(BF16)
    for copy in started:
        copy.wait()


def view(refs, piece):
    return [(ref, 0) for ref in refs]


def convolve_in_order(place, blocks, columns, edge, tap, bias, wide, put):
    width = columns.stop - columns.start
    count = blocks[0][0].shape[0] // PAIR
    wide[5:8, :width] = edge
    for r, (block, origin) in enumerate(blocks):
        for core in range(PAIR):
            at = pl.multiple_of((core * len(blocks) + (place[4] ^ r)) * count + 8, 8)
            part = block[core * count : (core + 1) * count, origin + columns.start : origin + columns.stop]
            wide[pl.ds(at, count), :width] = part.astype(F32)
    tap, bias = tap * 0.5, bias * 0.5
    for start in range(0, PAIR * len(blocks) * count, count):
        acc = bias + tap[0:1] * wide[start + 5 : start + 5 + count, :width]
        acc = acc + tap[1:2] * wide[start + 6 : start + 6 + count, :width]
        acc = acc + tap[2:3] * wide[start + 7 : start + 7 + count, :width]
        acc = acc + tap[3:4] * wide[start + 8 : start + 8 + count, :width]
        put(start, count, (acc + acc * jnp.tanh(acc)).astype(BF16))


def prep_kernel(shards, place, *refs):
    blocks, (taps, offset, a_ref, bias_ref, skip_ref, order) = refs[:shards], refs[shards : shards + 6]
    b_ref, edge_ref, cum_ref, row_ref, factor_ref, tail_ref, skip_out, dt_ref, wide = refs[shards + 6 :]
    blocks = view(blocks, 1)
    start = WIDTHS[1]
    last = total_of(1) - LANES
    size = edge_ref.shape[1]
    count = blocks[0][0].shape[0] // PAIR
    half, heads = count // 2, HEADS // GROUPS
    columns = [block[:, origin + last : origin + last + LANES].astype(F32) for block, origin in blocks]
    edge = columns[0][half : half + 4 * size // LANES]
    for column in columns[1:]:
        edge = edge + column[half : half + 4 * size // LANES]
    for q in range(size // LANES):
        edge_ref[:, q * LANES : (q + 1) * LANES] = edge[4 * q : 4 * q + 4]
    for r, column in enumerate(columns):
        packed = column[:half]
        for j in range(2 * PAIR):
            at = ((j // 2) * shards + (place[4] ^ r)) * count + (j % 2) * half
            rows = packed if j == 0 else pltpu.roll(packed, LANES - j * heads, 1)
            dt_ref[pl.ds(pl.multiple_of(at, half), half), :] = rows

    def put(start, count, value):
        b_ref[start : start + count] = value

    at = slice(PER_GROUP, PER_GROUP + STATE)
    convolve_in_order(
        place, blocks, slice(start, start + STATE), edge_ref[0:3, at], taps[:, at], offset[:, at], wide, put
    )
    per_tile = LANES * GROUPS // HEADS
    group = place[0]
    tile = group // per_tile
    shift = (LANES - (group % per_tile) * heads) % LANES

    def lanes_of(ref):
        return pltpu.roll(jnp.broadcast_to(ref[pl.ds(tile, 1), :], (8, LANES)), shift, 1)

    rate = -jnp.exp(lanes_of(a_ref)[0:1])
    raw = dt_ref[...] + lanes_of(bias_ref)[0:1]
    step = jnp.maximum(raw, 0.0) + jnp.log1p(jnp.exp(-jnp.abs(raw)))
    skip = lanes_of(skip_ref)
    skip_out[...] = jnp.concatenate(halves(jnp.concatenate([skip, skip], 0), 3), 1)
    lower = (
        lax.broadcasted_iota(jnp.int32, (BLOCK, BLOCK), 0)
        >= lax.broadcasted_iota(jnp.int32, (BLOCK, BLOCK), 1)
    ).astype(BF16)
    valid = lax.broadcasted_iota(jnp.int32, (BLOCK, LANES), 1) < heads
    for block in range(PAIR):
        at = slice(block * BLOCK, (block + 1) * BLOCK)
        here = jnp.where(valid, step[at], 1.0)
        parts = halves(here * rate, 3)
        cum = dot(lower, parts[0]) + (dot(lower, parts[1]) + dot(lower, parts[2]))
        cum = cum * LOG2E
        cum_ref[at] = cum
        row_ref[:, at] = jnp.transpose(cum - jnp.log2(here))
        factor_ref[at] = jnp.concatenate(halves(jnp.exp2(cum), 2), 1)
        tail = jnp.exp2(cum[BLOCK - 1 :] - cum) * here
        tail_ref[at] = jnp.concatenate(halves(tail, 2), 1)


def score_kernel(shards, place, *refs):
    blocks, refs = refs[:shards], refs[shards:]
    taps, offset, edge_ref, b_ref, c_ref, score_ref, wide = (*refs[:4], *refs[-3:])
    blocks = view(blocks, 1)
    start = WIDTHS[1] + STATE
    at = slice(PER_GROUP + STATE, PER_GROUP + 2 * STATE)

    def put(start, count, value):
        c_ref[start : start + count] = value

    convolve_in_order(
        place, blocks, slice(start, start + STATE), edge_ref[0:3, at], taps[:, at], offset[:, at], wide, put
    )
    for block in range(PAIR):
        at = slice(block * BLOCK, (block + 1) * BLOCK)
        score_ref[at] = lax.dot_general(
            c_ref[at], b_ref[at], (((1,), (1,)), ((), ())), preferred_element_type=F32
        )


def decay_of(ref):
    decay = ref[STATE : STATE + 16].astype(F32)
    return decay[0:1] + (decay[1:2] + decay[2:3])


def put_decay(ref, decay):
    row = lax.broadcasted_iota(jnp.int32, (16, ref.shape[1]), 0)
    high, middle, low = (part.astype(F32) for part in halves(decay, 3))
    packed = jnp.where(row == 0, high, jnp.where(row == 1, middle, jnp.where(row == 2, low, 0.0)))
    ref[STATE:] = packed.astype(BF16)


def state_kernel(shards, part, sizes, place, *refs):
    blocks, refs = refs[:shards], refs[shards:]
    taps, offset, edge_ref, b_ref, factor_ref, tail_ref = refs[:6]
    x_ref, own_ref, *sends, wide = refs[-3 - len(sizes) :]
    piece, start, width = part
    first = sum(WIDTHS[:piece]) + start
    at = slice(first, first + width)

    def put(row, count, value):
        x_ref[row : row + count] = value

    blocks = view(blocks, piece)
    columns = slice(start, start + width)
    convolve_in_order(place, blocks, columns, edge_ref[0:3, at], taps[:, at], offset[:, at], wide, put)
    expand = spread(first // HEAD_DIM, width, 2)
    both = []
    for block in range(PAIR):
        at = slice(block * BLOCK, (block + 1) * BLOCK)
        loaded = (x_ref[at].astype(F32) * dot(tail_ref[at], expand)).astype(BF16)
        both.append(
            lax.dot_general(b_ref[at], loaded, (((0,), (0,)), ((), ())), preferred_element_type=F32)
        )
    ends = [dot(factor_ref[(i + 1) * BLOCK - 16 : (i + 1) * BLOCK], expand)[15:16] for i in range(PAIR)]
    own_ref[...] = both[0]
    end = (ends[1] * both[0] + both[1]).astype(BF16)
    decay = ends[0] * ends[1]
    start = 0
    for send_ref in sends:
        at = slice(start, start + send_ref.shape[1])
        send_ref[0:STATE] = end[:, at]
        put_decay(send_ref, decay[:, at])
        start = at.stop


def combine_kernel(count, *refs):
    early, late, out_ref = refs[:count], refs[count : 2 * count], refs[-1]
    start = 0
    for early_ref, late_ref in zip(early, late):
        at = slice(start, start + late_ref.shape[1])
        decay = decay_of(late_ref)
        total = decay * early_ref[:STATE].astype(F32) + late_ref[:STATE].astype(F32)
        out_ref[:STATE, at] = total.astype(BF16)
        put_decay(out_ref.at[:, at], decay * decay_of(early_ref))
        start = at.stop


def mix(first_head, x_ref, cum_ref, row_ref, score_ref, skip_ref, put):
    width = x_ref.shape[1]
    half = BLOCK // 2
    expand = spread(first_head, width, 3)
    skip = dot(skip_ref[...], expand)[0:1]
    lower = lax.broadcasted_iota(jnp.int32, (half, half), 0) >= lax.broadcasted_iota(
        jnp.int32, (half, half), 1
    )
    lane = lax.broadcasted_iota(jnp.int32, (BLOCK, LANES), 1)
    for block in range(PAIR):
        base = block * BLOCK
        for tile in range(width // LANES):
            columns = slice(tile * LANES, (tile + 1) * LANES)
            x = x_ref[base : base + BLOCK, columns]
            top = skip[:, columns] * x[:half].astype(F32)
            bottom = skip[:, columns] * x[half:].astype(F32)
            for side in range(LANES // HEAD_DIM):
                head = first_head + tile * (LANES // HEAD_DIM) + side
                own = jnp.where(lane // HEAD_DIM == side, x, jnp.zeros_like(x))
                cum = cum_ref[base : base + BLOCK, head : head + 1]
                row = row_ref[head : head + 1, base : base + BLOCK]
                diag = jnp.where(lower, cum[:half] - row[:, :half], -1e30)
                mixing = jnp.exp2(diag) * score_ref[base : base + half, :half]
                top = top + dot(mixing.astype(BF16), own[:half])
                left = jnp.exp2(cum[half:] - row[:, :half]) * score_ref[base + half : base + BLOCK, :half]
                diag = jnp.where(lower, cum[half:] - row[:, half:], -1e30)
                right = jnp.exp2(diag) * score_ref[base + half : base + BLOCK, half:]
                mixing = jnp.concatenate([left.astype(BF16), right.astype(BF16)], 1)
                bottom = bottom + dot(mixing, own)
            put(block, slice(base, base + half), columns, top)
            put(block, slice(base + half, base + BLOCK), columns, bottom)


def local_kernel(first_head, x_ref, cum_ref, row_ref, score_ref, skip_ref, *refs):
    out_ref = refs[-1]

    def put(block, rows, columns, value):
        out_ref[rows, columns] = value

    mix(first_head, x_ref, cum_ref, row_ref, score_ref, skip_ref, put)


def carry(first_head, core, lasts, befores, alones, own_ref, c_ref, factor_ref, add, keep_ref, send_ref):
    expand = spread(first_head, own_ref.shape[1], 2)
    last, before = (
        refs[0][...] if len(refs) == 1 else jnp.concatenate([ref[...] for ref in refs], 1)
        for refs in (lasts, befores)
    )
    held = last[:STATE].astype(F32) + decay_of(last) * before[:STATE].astype(F32)
    for alone in alones:
        held = held + alone[:STATE].astype(F32)
    factor = dot(factor_ref[...], expand)
    outs = []
    for block in range(PAIR):
        at = slice(block * BLOCK, (block + 1) * BLOCK)
        carried = dot(c_ref[at], held.astype(BF16))
        outs.append((add[at] + factor[at] * carried).astype(BF16))
        held = factor[BLOCK - 1 : BLOCK] * held + own_ref[...]

    @pl.when(core == 0)
    def _():
        keep_ref[...] = outs[0]
        send_ref[...] = outs[1]

    @pl.when(core == 1)
    def _():
        keep_ref[...] = outs[1]
        send_ref[...] = outs[0]


def final_kernel(first_head, counts, place, *refs):
    groups = []
    for number in counts:
        groups.append(refs[:number])
        refs = refs[number:]
    carry(first_head, place[2], *groups, *refs[:4], *refs[-2:])


def finish_kernel(first_head, counts, place, *refs):
    groups = []
    for number in counts:
        groups.append(refs[:number])
        refs = refs[number:]
    own_ref, c_ref, factor_ref = refs[:3]
    keep_ref, send_ref, partial = refs[-3:]
    local_kernel(first_head, *refs[3:8], partial)
    carry(first_head, place[2], *groups, own_ref, c_ref, factor_ref, partial, keep_ref, send_ref)


def place_kernel(firsts, place, *refs):
    count = len(firsts)
    keeps, gots = refs[:count], refs[count : 2 * count]
    out, sems = refs[-2:]
    core = place[2]
    half = out.shape[1] // PAIR
    copies = []
    for first, keep, got in zip(firsts, keeps, gots):
        width = keep.shape[1]
        copies.append((keep, out.at[:, ds(core * half + first, width)]))
        copies.append((got, out.at[:, ds((1 - core) * half + first, width)]))
    for copy in run(copies, sems):
        copy.wait()


def put_in_place(firsts, shape, place, keeps, gots):
    smem, vmem, hbm = (pl.BlockSpec(memory_space=m) for m in (pltpu.SMEM, pltpu.VMEM, pltpu.HBM))
    count = len(firsts)
    return pl.pallas_call(
        functools.partial(place_kernel, firsts),
        out_shape=jax.ShapeDtypeStruct(shape, BF16),
        in_specs=[smem] + [vmem] * (2 * count),
        out_specs=hbm,
        scratch_shapes=[pltpu.SemaphoreType.DMA((2 * count,))],
        compiler_params=pltpu.CompilerParams(vmem_limit_bytes=16 << 20),
        cost_estimate=pl.CostEstimate(flops=1, bytes_accessed=1, transcendentals=0),
        name="place",
    )(place, *keeps, *gots)


class Stay:
    def __init__(self, array):
        self.array = array


def gate(blocks, order):
    anywhere = pl.BlockSpec(memory_space=pl.ANY)
    return pl.pallas_call(
        lambda *refs: None,
        out_shape=[jax.ShapeDtypeStruct(block.shape, block.dtype) for block in blocks],
        in_specs=[anywhere] * (len(blocks) + len(order)),
        out_specs=[anywhere] * len(blocks),
        input_output_aliases={i: i for i in range(len(blocks))},
        compiler_params=pltpu.CompilerParams(vmem_limit_bytes=16 << 20),
        cost_estimate=pl.CostEstimate(flops=1, bytes_accessed=1, transcendentals=0),
        name="gate",
    )(*blocks, *order)


def call(body, outs, operands, scratch=(), flops=0, transcendentals=0, name=None, limit=16 << 20):
    shapes = [jax.ShapeDtypeStruct(shape, dtype) for shape, dtype in outs]
    smem, vmem, hbm = (pl.BlockSpec(memory_space=m) for m in (pltpu.SMEM, pltpu.VMEM, pltpu.HBM))
    specs = [
        hbm if isinstance(o, Stay) else smem if o.dtype == jnp.int32 else vmem for o in operands
    ]
    moved = sum(o.size * o.dtype.itemsize for o in shapes) * 2
    return pl.pallas_call(
        body,
        out_shape=shapes,
        in_specs=specs,
        out_specs=[vmem] * len(outs),
        scratch_shapes=scratch,
        compiler_params=pltpu.CompilerParams(vmem_limit_bytes=limit),
        cost_estimate=pl.CostEstimate(flops=1, bytes_accessed=1, transcendentals=0),
        name=name,
    )(*[o.array if isinstance(o, Stay) else o for o in operands])


def paired(xbc, dt_raw, conv_weight, conv_bias, a_log, dt_bias, skip_gain):
    axes = ("ctx", "head")
    shards, length = lax.axis_size("head"), lax.axis_size("ctx")
    devices, peers = shards * length, shards * PAIR
    tok = xbc.shape[0]
    slab = tok * peers
    context, shard = lax.axis_index("ctx"), lax.axis_index("head")
    pair, core = context // PAIR, context % PAIR
    group = shard * PAIR + core
    place = jnp.stack([group, pair, core, core * shards + shard, shard]).astype(jnp.int32)

    def over(block, target):
        route = [(i, target(i)) for i in range(devices)]
        return lax.ppermute(block, axes, [(i, j) for i, j in route if j is not None and j < devices])

    def swap(block):
        return over(block, lambda i: i ^ shards)

    rows = Stay(xbc)
    size = PER_GROUP + 2 * STATE
    (sent,) = call(
        functools.partial(pack_first_kernel, shards),
        [((tok, shards * WIDTHS[0] + size - WIDTHS[0]), BF16)],
        [place, rows],
        scratch=[pltpu.SemaphoreType.DMA((4 * shards,))],
        name="pack_first",
    )
    got_first = swap(sent)
    sent, tail = call(
        functools.partial(pack_kernel, shards),
        [((tok, shards * (size - WIDTHS[0]) + HEADS), BF16), ((16, shards * size), BF16)],
        [place, rows, Stay(dt_raw), Stay(sent)],
        scratch=[pltpu.SemaphoreType.DMA((6 * shards + 1,))],
        name="pack",
    )
    got_rest = swap(sent)
    taps, offset = call(
        taps_kernel,
        [((4, size), F32), ((1, size), F32)],
        [place, Stay(conv_weight), Stay(conv_bias[None]), Stay(got_rest)],
        scratch=[pltpu.SemaphoreType.DMA((6,))],
        name="taps",
    )

    def send_on(plan, order, tail=None, edges=None):
        unused = Stay(got_first)
        parts = [p for _, pieces in plan for p in pieces]
        made = [] if tail is None else [((3, shards * size), BF16)]
        return call(
            functools.partial(merge_kernel, shards, plan, len(order)),
            [((PAIR * tok, sum(map(total_of, pieces))), BF16) for _, pieces in plan] + made,
            [
                place,
                rows,
                Stay(dt_raw) if edges is None else dt_raw,
                got_first if 0 in parts else unused,
                got_rest if any(parts) else unused,
                next((o for o in (tail, edges) if o is not None), unused),
            ]
            + [Stay(o) for o in order],
            scratch=[pltpu.SemaphoreType.DMA((sum(2 + 2 * len(RESTS[p]) for p in parts),))],
            name="merge",
        )

    def travel(blocks):
        return [blocks[0]] + [over(blocks[r], lambda i, r=r: i ^ r) for r in range(1, shards)]

    def plan(piece):
        return [(r, (piece,)) for r in range(shards)]

    *first_blocks, edges = send_on(plan(0), [], tail)
    message = [travel(first_blocks)]
    edges = over(edges, lambda i: i + peers if i % shards == shards - 1 else None)
    second_blocks = send_on(plan(1), [first_blocks[0]], None, edges)
    message.append(travel(second_blocks[:1] + gate(second_blocks[1:], message[0][1:])))
    third_blocks = send_on(plan(2), [second_blocks[0]])
    message.append(travel(third_blocks[:1] + gate(third_blocks[1:], message[1][2:])))

    def seen(piece):
        return message[piece]

    tiles = [p.reshape(HEADS // LANES, LANES) for p in (a_log, dt_bias, skip_gain)]
    b, edge, cum, row, factor, tail, skip = call(
        functools.partial(prep_kernel, shards),
        [
            ((slab, STATE), BF16),
            ((4, size), F32),
            ((slab, LANES), F32),
            ((LANES, slab), F32),
            ((slab, 2 * LANES), BF16),
            ((slab, 2 * LANES), BF16),
            ((16, 3 * LANES), BF16),
        ],
        [place] + seen(1) + [taps, offset] + tiles + [Stay(third_blocks[0])],
        scratch=[pltpu.VMEM((slab, LANES), F32), pltpu.VMEM((slab + 8, STATE), F32)],
        name="prep",
    )
    count = len(GROUPED)
    x, sent, own, last, joined, before, alone, keep, send = ([None] * count for _ in range(9))

    def first_head(i):
        return (sum(WIDTHS[: GROUPED[i][0]]) + GROUPED[i][1]) // HEAD_DIM

    def state_of(i, order):
        piece, _, width = GROUPED[i]
        x[i], own[i], *sent[i] = call(
            functools.partial(state_kernel, shards, GROUPED[i], FIRST_ROUND[i]),
            [((slab, width), BF16), ((STATE, width), F32)] + [((STATE + 16, w), BF16) for w in FIRST_ROUND[i]],
            [place] + seen(piece) + [taps, offset, edge, b, factor, tail] + [Stay(o) for o in order],
            scratch=[pltpu.VMEM((slab + 8, width), F32)],
            name="state",
        )
        every = i not in ALONE
        last[i] = [over(part, lambda i: i + peers if every or i // peers % 2 == 0 else None) for part in sent[i]]

    def combine_of(i, order):
        joined[i], before[i], alone[i] = [], [], []
        step = len(FIRST_ROUND[i]) // len(SECOND_ROUND[i])
        for j, width in enumerate(SECOND_ROUND[i]):
            early, late = last[i][j * step : (j + 1) * step], sent[i][j * step : (j + 1) * step]
            (total,) = call(
                functools.partial(combine_kernel, len(early)),
                [((STATE + 16, width), BF16)],
                early + late + [Stay(o) for o in order],
                name="combine",
            )
            joined[i].append(total)
            if i in ALONE:
                before[i].append(over(total, lambda i: i + 2 * peers if i // peers == 1 else None))
                alone[i].append(over(total, lambda i: i + peers if i // peers == 1 else None))
            else:
                before[i].append(over(total, lambda i: i + 2 * peers))
            order = [total]

    def finish_of(body, i, operands, order, **more):
        keep[i], send[i] = call(
            functools.partial(body, first_head(i), (len(last[i]), len(before[i]), len(alone[i]))),
            [((BLOCK, GROUPED[i][2]), BF16)] * 2,
            [place, *last[i], *before[i], *alone[i], own[i], c, factor] + operands + [Stay(o) for o in order],
            name="final",
            **more,
        )

    partial = [None] * count

    def local_of(i, order):
        (partial[i],) = call(
            functools.partial(local_kernel, first_head(i)),
            [(x[i].shape, F32)],
            [x[i], cum, row, score, skip] + [Stay(o) for o in order],
            name="local",
        )

    state_of(0, [])
    fourth_blocks = send_on(plan(3), sent[0])
    message.append(travel(fourth_blocks))
    c, score = call(
        functools.partial(score_kernel, shards),
        [((slab, STATE), BF16), ((slab, BLOCK), F32)],
        [place] + seen(1) + [taps, offset, edge, b] + [Stay(o) for o in sent[0]],
        scratch=[pltpu.VMEM((slab + 8, STATE), F32)],
        name="score",
    )
    local_of(0, [])
    combine_of(0, [partial[0]])
    state_of(1, joined[0])
    local_of(1, sent[1])
    combine_of(1, [partial[1]])
    state_of(2, joined[1])
    state_of(3, sent[2])
    finish_of(final_kernel, 0, [partial[0]], sent[3] + before[1])
    combine_of(2, [keep[0]])
    finish_of(final_kernel, 1, [partial[1]], joined[2])
    combine_of(3, [keep[1]])
    local_of(2, joined[3])
    local_of(3, [partial[2]])
    finish_of(final_kernel, 2, [partial[2]], [partial[3]])
    finish_of(final_kernel, 3, [partial[3]], [keep[2]])
    firsts = [first_head(i) * HEAD_DIM for i in range(count)]
    return put_in_place(firsts, (BLOCK, PAIR * PER_GROUP), place, keep, [swap(o) for o in send])


def solution(mesh):
    in_specs = (P(("ctx", "head"), None), P(("ctx", "head"), None), P(), P(), P(), P(), P())
    out_specs = P("ctx", "head")
    shards, length = mesh.shape["head"], mesh.shape["ctx"]

    def program(xbc, *rest):
        slab = xbc.shape[0] // length
        fits = shards == GROUPS // PAIR and length == 4 * PAIR and slab == BLOCK
        return jax.shard_map(
            paired if fits else on_device,
            mesh=mesh,
            in_specs=in_specs,
            out_specs=out_specs,
            check_vma=False,
        )(xbc, *rest)

    return program
```

```python
import functools

import jax
import jax.numpy as jnp
from jax import lax
from jax.experimental import pallas as pl
from jax.experimental.pallas import tpu as pltpu
from jax.sharding import PartitionSpec as P

HEADS = 256
HEAD_DIM = 64
STATE = 256
GROUPS = 8
BLOCK = 256


def from_behind(block, axis, distance):
    devices = range(lax.axis_size(axis))
    route = [(i - distance, i) for i in devices if i - distance in devices]
    return lax.ppermute(block, axis, route)


def carried_in(array, axis, combine, identity):
    length, index = (lax.axis_size(axis), lax.axis_index(axis))
    everything = jax.tree.map(lambda part: lax.all_gather(part, axis), array)
    start = jax.tree.map(
        lambda part, zero: jnp.broadcast_to(jnp.asarray(zero, part.dtype), part.shape),
        array,
        identity,
    )

    def hop(k, before):
        reached = k < index
        new = combine(before, jax.tree.map(lambda part: part[k], everything))
        return jax.tree.map(lambda a, b: jnp.where(reached, a, b), new, before)

    return lax.fori_loop(0, length, hop, start)


def convolve(rows, edge, weight, bias):
    count = rows.shape[0]
    wide = jnp.concatenate([edge, rows], 0).astype(jnp.float32)
    acc = bias[None, :] + weight[0] * wide[0:count]
    acc = acc + weight[1] * wide[1 : count + 1]
    acc = acc + weight[2] * wide[2 : count + 2]
    acc = acc + weight[3] * wide[3 : count + 3]
    return jax.nn.silu(acc).astype(jnp.bfloat16)


def rearrange_heads(rows, shards, per_dev, groups_dev, per_group):
    count = rows.shape[0]
    inner = HEADS * HEAD_DIM
    replicate_groups = max(1, per_group // per_dev)
    heads_part = rows[:, :inner].reshape(count, shards, per_dev * HEAD_DIM)
    b_part = rows[:, inner : inner + GROUPS * STATE].reshape(count, GROUPS, STATE)
    c_part = rows[:, inner + GROUPS * STATE :].reshape(count, GROUPS, STATE)
    b_part = jnp.repeat(b_part, replicate_groups, axis=1).reshape(count, shards, groups_dev * STATE)
    c_part = jnp.repeat(c_part, replicate_groups, axis=1).reshape(count, shards, groups_dev * STATE)
    return jnp.concatenate([heads_part, b_part, c_part], axis=2)


def inner_block(xs, bmat, cmat, steps, cum):
    size = xs.shape[0]
    lower = jnp.arange(size)[:, None] >= jnp.arange(size)[None, :]
    scores = jnp.einsum("qgn,kgn->gqk", cmat, bmat, preferred_element_type=jnp.float32)
    order = jnp.transpose(cum, (1, 2, 0))
    gap = order[..., :, None] - order[..., None, :]
    decay = jnp.exp(jnp.where(lower, gap, -jnp.inf))
    mixing = (scores[:, None] * decay * jnp.transpose(steps, (1, 2, 0))[..., None, :]).astype(
        jnp.bfloat16
    )
    local = jnp.einsum("gjqk,kgjp->qgjp", mixing, xs, preferred_element_type=jnp.float32)
    tail = jnp.exp(cum[size - 1][None] - cum) * steps
    loaded = (bmat[:, :, None, :].astype(jnp.float32) * tail[..., None]).astype(jnp.bfloat16)
    block_state = jnp.einsum("kgjn,kgjp->gjnp", loaded, xs, preferred_element_type=jnp.float32)
    return (local, block_state)


def on_device(xbc, dt_raw, conv_weight, conv_bias, a_log, dt_bias, skip_gain):
    tok = xbc.shape[0]
    shards = lax.axis_size("head")
    per_dev = HEADS // shards
    per_group = HEADS // GROUPS
    groups_dev = max(1, per_dev // per_group)
    heads_per_cluster = per_dev // groups_dev
    sent = rearrange_heads(xbc, shards, per_dev, groups_dev, per_group)
    mine, rates = (
        lax.all_to_all(sent, "head", split_axis=1, concat_axis=0, tiled=True),
        lax.all_to_all(
            dt_raw.reshape(tok, shards, per_dev), "head", split_axis=1, concat_axis=0, tiled=True
        ),
    )
    slab = tok * shards
    mine = mine.reshape(slab, mine.shape[2])
    rates = rates.reshape(slab, per_dev)
    shard = lax.axis_index("head")
    taps = lax.dynamic_index_in_dim(
        rearrange_heads(conv_weight, shards, per_dev, groups_dev, per_group),
        shard,
        1,
        keepdims=False,
    )
    offset = lax.dynamic_index_in_dim(
        rearrange_heads(conv_bias[None, :], shards, per_dev, groups_dev, per_group),
        shard,
        1,
        keepdims=False,
    )
    edge = from_behind(mine[slab - 3 :], "ctx", 1)
    mine = convolve(mine, edge, taps, offset[0])
    nchunk = slab // BLOCK
    width = per_dev * HEAD_DIM
    xs = mine[:, :width].reshape(nchunk, BLOCK, groups_dev, heads_per_cluster, HEAD_DIM)
    bmat = mine[:, width : width + groups_dev * STATE].reshape(nchunk, BLOCK, groups_dev, STATE)
    cmat = mine[:, width + groups_dev * STATE :].reshape(nchunk, BLOCK, groups_dev, STATE)
    first = shard * per_dev
    rate = (-jnp.exp(lax.dynamic_slice_in_dim(a_log, first, per_dev))).reshape(
        groups_dev, heads_per_cluster
    )
    bias_dt = lax.dynamic_slice_in_dim(dt_bias, first, per_dev).reshape(
        groups_dev, heads_per_cluster
    )
    skip = lax.dynamic_slice_in_dim(skip_gain, first, per_dev).reshape(
        groups_dev, heads_per_cluster
    )
    steps = jax.nn.softplus(
        rates.astype(jnp.float32).reshape(nchunk, BLOCK, groups_dev, heads_per_cluster) + bias_dt
    )
    cum = jnp.cumsum(steps * rate, axis=1)

    def block_step(carry, item):
        held, product = carry
        x_part, b_part, c_part, step_part, cum_part = item
        local, block_state = inner_block(x_part, b_part, c_part, step_part, cum_part)
        lifted = c_part.astype(jnp.float32)[:, :, None, :] * jnp.exp(cum_part)[..., None]
        carried = jnp.einsum("qgjn,gjnp->qgjp", lifted, held, precision=lax.Precision.HIGHEST)
        partial_out = local + carried + skip[..., None] * x_part.astype(jnp.float32)
        end = jnp.exp(cum_part[BLOCK - 1])
        return ((end[..., None, None] * held + block_state, product * end), (partial_out, product))

    zero_state = jnp.zeros((groups_dev, heads_per_cluster, STATE, HEAD_DIM), jnp.float32)
    unit = jnp.ones((groups_dev, heads_per_cluster), jnp.float32)
    (slab_state, slab_decay), (partials, product_in) = lax.scan(
        block_step, (zero_state, unit), (xs, bmat, cmat, steps, cum)
    )

    def combine(preceding_state, later):
        return (
            preceding_state[0] * later[0],
            later[0][..., None, None] * preceding_state[1] + later[1],
        )

    _, entering = carried_in((slab_decay, slab_state), "ctx", combine, (unit, zero_state))
    projected = jnp.einsum(
        "cqgn,gjnp->cqgjp", cmat.astype(jnp.float32), entering, precision=lax.Precision.HIGHEST
    )
    factor = jnp.exp(cum) * product_in[:, None]
    total = partials + factor[..., None] * projected
    return total.astype(jnp.bfloat16).reshape(slab, width)


PAIR = 2
LANES = 128
LOG2E = 1.4426950408889634
F32, BF16 = jnp.float32, jnp.bfloat16
WIDTHS = (512, 0, 768, 768)
RESTS = ("", "BD", "", "C")
GROUPED = ((0, 0, 512), (2, 0, 768), (3, 0, 384), (3, 384, 384))
FIRST_ROUND = ((256, 256), (384, 384), (384,), (384,))
SECOND_ROUND = ((512,), (384, 384), (384,), (384,))
ALONE = (2, 3)


def halves(value, count):
    parts = []
    for _ in range(count):
        part = value.astype(BF16)
        parts.append(part)
        value = value - part.astype(F32)
    return parts


def spread(first_head, width, copies):
    lane = lax.broadcasted_iota(jnp.int32, (copies * LANES, width), 0) % LANES
    column = lax.broadcasted_iota(jnp.int32, (copies * LANES, width), 1)
    return (lane == first_head + column // HEAD_DIM).astype(BF16)


def dot(a, b):
    return jnp.dot(a, b, preferred_element_type=F32)


def ds(start, width):
    return pl.ds(pl.multiple_of(start, LANES), width)


def run(copies, sems):
    started = []
    for i, (source, target) in enumerate(copies):
        copy = pltpu.make_async_copy(source, target, sems.at[i])
        copy.start()
        started.append(copy)
    return started


PER_GROUP = HEADS * HEAD_DIM // GROUPS
INNER = HEADS * HEAD_DIM


def channels(group, first, width):
    return ds(group * PER_GROUP + first, width)


def pack_first_kernel(shards, place, xbc, send, sems):
    core, shard = place[2], place[4]
    count = xbc.shape[0]
    width = WIDTHS[0]
    copies = []
    for r in range(shards):
        group = (shard ^ r) * PAIR + 1 - core
        copies.append((xbc.at[:, channels(group, 0, width)], send.at[:, r * width : (r + 1) * width]))
        last, rows = xbc.at[count - 16 :], slice(16 * r, 16 * r + 16)
        to = shards * width
        copies.append((last.at[:, channels(group, width, PER_GROUP - width)], send.at[rows, to : to + PER_GROUP - width]))
        to += PER_GROUP - width
        for i in range(2):
            at = ds(INNER + (i * GROUPS + group) * STATE, STATE)
            copies.append((last.at[:, at], send.at[rows, to + i * STATE : to + (i + 1) * STATE]))
    for copy in run(copies, sems):
        copy.wait()


def pack_kernel(shards, place, xbc, dt_raw, order, send, tail, sems):
    core, shard = place[2], place[4]
    count = xbc.shape[0]
    first = WIDTHS[0]
    width = PER_GROUP - first
    rest = width * shards
    size = PER_GROUP + 2 * STATE
    copies = []
    for r in range(shards):
        group = (shard ^ r) * PAIR + 1 - core
        copies.append((xbc.at[:, channels(group, first, width)], send.at[:, r * width : (r + 1) * width]))
        for i in range(2):
            to = rest + (i * shards + r) * STATE
            copies.append((xbc.at[:, ds(INNER + (i * GROUPS + group) * STATE, STATE)], send.at[:, to : to + STATE]))
    copies.append((dt_raw, send.at[:, send.shape[1] - HEADS :]))
    for r in range(shards):
        group, to = (shard ^ r) * PAIR + core, r * size
        last = xbc.at[count - 16 :]
        copies.append((last.at[:, channels(group, 0, PER_GROUP)], tail.at[:, to : to + PER_GROUP]))
        for i in range(2):
            at = ds(INNER + (i * GROUPS + group) * STATE, STATE)
            start = to + PER_GROUP + i * STATE
            copies.append((last.at[:, at], tail.at[:, start : start + STATE]))
    for copy in run(copies, sems):
        copy.wait()


def taps_kernel(place, weight, bias, order, taps, offset, sems):
    copies = []
    for source, target in ((weight, taps), (bias, offset)):
        copies.append((source.at[:, channels(place[0], 0, PER_GROUP)], target.at[:, :PER_GROUP]))
        for i in range(2):
            at = ds(INNER + (i * GROUPS + place[0]) * STATE, STATE)
            start = PER_GROUP + i * STATE
            copies.append((source.at[:, at], target.at[:, start : start + STATE]))
    for copy in run(copies, sems):
        copy.wait()


def put_edge(shards, place, got, tail, out):
    count = got.shape[0]
    first = WIDTHS[0]
    size = PER_GROUP + 2 * STATE
    for r in range(shards):
        theirs = [got[count - 16 :, r * first : (r + 1) * first]]
        theirs.append(got[16 * r : 16 * r + 16, shards * first :])
        to = r * size
        for part in theirs:
            at = slice(to, to + part.shape[1])
            rows = jnp.where(place[2] == 0, part.astype(F32), tail[:, at].astype(F32))
            out[:, at] = rows[13:16].astype(BF16)
            to = at.stop


def total_of(piece):
    return WIDTHS[piece] + sum(LANES if kind == "D" else STATE for kind in RESTS[piece])


def merge_kernel(shards, plan, unread, place, xbc, dt_raw, got_first, got, edges, *refs):
    refs = refs[unread:]
    outs, sems = refs[: len(plan)], refs[-1]
    core, shard = place[2], place[4]
    count = xbc.shape[0]
    stride = PER_GROUP - WIDTHS[0]
    mine = pl.ds(pl.multiple_of(core * count, count), count)
    other = pl.ds(pl.multiple_of((1 - core) * count, count), count)
    copies, steps = [], []
    for out, (r, pieces) in zip(outs, plan):
        group = (shard ^ r) * PAIR + core
        to = 0
        for piece in pieces:
            first, width = sum(WIDTHS[:piece]), WIDTHS[piece]
            if piece == 0:
                source = got_first.at[:, r * width : (r + 1) * width]
            else:
                at = r * stride + first - WIDTHS[0]
                source = got.at[:, at : at + width]
            if width:
                copies.append((xbc.at[:, channels(group, first, width)], out.at[mine, to : to + width]))
                copies.append((source, out.at[other, to : to + width]))
            to += width
            for kind in RESTS[piece]:
                if kind == "D":
                    steps.append((out, r, to))
                    to += LANES
                    continue
                i = "BC".index(kind)
                at = ds(INNER + (i * GROUPS + group) * STATE, STATE)
                copies.append((xbc.at[:, at], out.at[mine, to : to + STATE]))
                at = stride * shards + (i * shards + r) * STATE
                copies.append((got.at[:, at : at + STATE], out.at[other, to : to + STATE]))
                to += STATE
    started = run(copies, sems)
    if len(refs) > len(plan) + 1:
        put_edge(shards, place, got_first, edges, refs[-2])
    if steps:
        lane = lax.broadcasted_iota(jnp.int32, (count, LANES), 1)
        per_tile = LANES * GROUPS // HEADS
        heads = HEADS // GROUPS
        for out, r, to in steps:
            group = (shard ^ r) * PAIR + core
            tile, shift = group // per_tile, (LANES - (group % per_tile) * heads) % LANES
            own = dt_raw[:, ds(tile * LANES, LANES)].astype(F32)
            theirs = got[:, ds(got.shape[1] - HEADS + tile * LANES, LANES)].astype(F32)
            low = jnp.where(core == 0, own, theirs)
            high = jnp.where(core == 0, theirs, own)
            packed = jnp.zeros((count // 2, LANES), F32)
            for j, rows in enumerate((low, high)):
                rows = jnp.where(lane < heads, pltpu.roll(rows, shift, 1), 0.0)
                for i in range(2):
                    part = rows[i * count // 2 : (i + 1) * count // 2]
                    packed = packed + pltpu.roll(part, (2 * j + i) * heads, 1)
            out[: count // 2, to : to + LANES] = packed.astype(BF16)
            size = PER_GROUP + 2 * STATE
            at = slice(r * size, (r + 1) * size)
            edge = jnp.concatenate([edges[:, at].astype(F32), jnp.zeros((1, size), F32)], 0)
            edge = jnp.concatenate([edge[:, q * LANES : (q + 1) * LANES] for q in range(size // LANES)], 0)
            fill = jnp.zeros((PAIR * count - count // 2 - edge.shape[0], LANES), F32)
            out[count // 2 :, to : to + LANES] = jnp.concatenate([edge, fill], 0).astype(BF16)
    for copy in started:
        copy.wait()


def view(refs, piece):
    return [(ref, 0) for ref in refs]


def convolve_in_order(place, blocks, columns, edge, tap, bias, wide, put):
    width = columns.stop - columns.start
    count = blocks[0][0].shape[0] // PAIR
    wide[5:8, :width] = edge
    for r, (block, origin) in enumerate(blocks):
        for core in range(PAIR):
            at = pl.multiple_of((core * len(blocks) + (place[4] ^ r)) * count + 8, 8)
            part = block[core * count : (core + 1) * count, origin + columns.start : origin + columns.stop]
            wide[pl.ds(at, count), :width] = part.astype(F32)
    tap, bias = tap * 0.5, bias * 0.5
    for start in range(0, PAIR * len(blocks) * count, count):
        acc = bias + tap[0:1] * wide[start + 5 : start + 5 + count, :width]
        acc = acc + tap[1:2] * wide[start + 6 : start + 6 + count, :width]
        acc = acc + tap[2:3] * wide[start + 7 : start + 7 + count, :width]
        acc = acc + tap[3:4] * wide[start + 8 : start + 8 + count, :width]
        put(start, count, (acc + acc * jnp.tanh(acc)).astype(BF16))


def prep_kernel(shards, place, *refs):
    blocks, (taps, offset, a_ref, bias_ref, skip_ref, order) = refs[:shards], refs[shards : shards + 6]
    b_ref, edge_ref, cum_ref, row_ref, factor_ref, tail_ref, skip_out, dt_ref, wide = refs[shards + 6 :]
    blocks = view(blocks, 1)
    start = WIDTHS[1]
    last = total_of(1) - LANES
    size = edge_ref.shape[1]
    count = blocks[0][0].shape[0] // PAIR
    half, heads = count // 2, HEADS // GROUPS
    columns = [block[:, origin + last : origin + last + LANES].astype(F32) for block, origin in blocks]
    edge = columns[0][half : half + 4 * size // LANES]
    for column in columns[1:]:
        edge = edge + column[half : half + 4 * size // LANES]
    for q in range(size // LANES):
        edge_ref[:, q * LANES : (q + 1) * LANES] = edge[4 * q : 4 * q + 4]
    for r, column in enumerate(columns):
        packed = column[:half]
        for j in range(2 * PAIR):
            at = ((j // 2) * shards + (place[4] ^ r)) * count + (j % 2) * half
            rows = packed if j == 0 else pltpu.roll(packed, LANES - j * heads, 1)
            dt_ref[pl.ds(pl.multiple_of(at, half), half), :] = rows

    def put(start, count, value):
        b_ref[start : start + count] = value

    at = slice(PER_GROUP, PER_GROUP + STATE)
    convolve_in_order(
        place, blocks, slice(start, start + STATE), edge_ref[0:3, at], taps[:, at], offset[:, at], wide, put
    )
    per_tile = LANES * GROUPS // HEADS
    group = place[0]
    tile = group // per_tile
    shift = (LANES - (group % per_tile) * heads) % LANES

    def lanes_of(ref):
        return pltpu.roll(jnp.broadcast_to(ref[pl.ds(tile, 1), :], (8, LANES)), shift, 1)

    rate = -jnp.exp(lanes_of(a_ref)[0:1])
    raw = dt_ref[...] + lanes_of(bias_ref)[0:1]
    step = jnp.maximum(raw, 0.0) + jnp.log1p(jnp.exp(-jnp.abs(raw)))
    skip = lanes_of(skip_ref)
    skip_out[...] = jnp.concatenate(halves(jnp.concatenate([skip, skip], 0), 3), 1)
    lower = (
        lax.broadcasted_iota(jnp.int32, (BLOCK, BLOCK), 0)
        >= lax.broadcasted_iota(jnp.int32, (BLOCK, BLOCK), 1)
    ).astype(BF16)
    valid = lax.broadcasted_iota(jnp.int32, (BLOCK, LANES), 1) < heads
    for block in range(PAIR):
        at = slice(block * BLOCK, (block + 1) * BLOCK)
        here = jnp.where(valid, step[at], 1.0)
        parts = halves(here * rate, 3)
        cum = dot(lower, parts[0]) + (dot(lower, parts[1]) + dot(lower, parts[2]))
        cum = cum * LOG2E
        cum_ref[at] = cum
        row_ref[:, at] = jnp.transpose(cum - jnp.log2(here))
        factor_ref[at] = jnp.concatenate(halves(jnp.exp2(cum), 2), 1)
        tail = jnp.exp2(cum[BLOCK - 1 :] - cum) * here
        tail_ref[at] = jnp.concatenate(halves(tail, 2), 1)


def score_kernel(shards, place, *refs):
    blocks, refs = refs[:shards], refs[shards:]
    taps, offset, edge_ref, b_ref, c_ref, score_ref, wide = (*refs[:4], *refs[-3:])
    blocks = view(blocks, 3)
    start = WIDTHS[3]
    at = slice(PER_GROUP + STATE, PER_GROUP + 2 * STATE)

    def put(start, count, value):
        c_ref[start : start + count] = value

    convolve_in_order(
        place, blocks, slice(start, start + STATE), edge_ref[0:3, at], taps[:, at], offset[:, at], wide, put
    )
    for block in range(PAIR):
        at = slice(block * BLOCK, (block + 1) * BLOCK)
        score_ref[at] = lax.dot_general(
            c_ref[at], b_ref[at], (((1,), (1,)), ((), ())), preferred_element_type=F32
        )


def decay_of(ref):
    decay = ref[STATE : STATE + 16].astype(F32)
    return decay[0:1] + (decay[1:2] + decay[2:3])


def put_decay(ref, decay):
    row = lax.broadcasted_iota(jnp.int32, (16, ref.shape[1]), 0)
    high, middle, low = (part.astype(F32) for part in halves(decay, 3))
    packed = jnp.where(row == 0, high, jnp.where(row == 1, middle, jnp.where(row == 2, low, 0.0)))
    ref[STATE:] = packed.astype(BF16)


def state_kernel(shards, part, sizes, place, *refs):
    blocks, refs = refs[:shards], refs[shards:]
    taps, offset, edge_ref, b_ref, factor_ref, tail_ref = refs[:6]
    x_ref, own_ref, *sends, wide = refs[-3 - len(sizes) :]
    piece, start, width = part
    first = sum(WIDTHS[:piece]) + start
    at = slice(first, first + width)

    def put(row, count, value):
        x_ref[row : row + count] = value

    blocks = view(blocks, piece)
    columns = slice(start, start + width)
    convolve_in_order(place, blocks, columns, edge_ref[0:3, at], taps[:, at], offset[:, at], wide, put)
    expand = spread(first // HEAD_DIM, width, 2)
    both = []
    for block in range(PAIR):
        at = slice(block * BLOCK, (block + 1) * BLOCK)
        loaded = (x_ref[at].astype(F32) * dot(tail_ref[at], expand)).astype(BF16)
        both.append(
            lax.dot_general(b_ref[at], loaded, (((0,), (0,)), ((), ())), preferred_element_type=F32)
        )
    ends = [dot(factor_ref[(i + 1) * BLOCK - 16 : (i + 1) * BLOCK], expand)[15:16] for i in range(PAIR)]
    own_ref[...] = both[0]
    end = (ends[1] * both[0] + both[1]).astype(BF16)
    decay = ends[0] * ends[1]
    start = 0
    for send_ref in sends:
        at = slice(start, start + send_ref.shape[1])
        send_ref[0:STATE] = end[:, at]
        put_decay(send_ref, decay[:, at])
        start = at.stop


def combine_kernel(count, *refs):
    early, late, out_ref = refs[:count], refs[count : 2 * count], refs[-1]
    start = 0
    for early_ref, late_ref in zip(early, late):
        at = slice(start, start + late_ref.shape[1])
        decay = decay_of(late_ref)
        total = decay * early_ref[:STATE].astype(F32) + late_ref[:STATE].astype(F32)
        out_ref[:STATE, at] = total.astype(BF16)
        put_decay(out_ref.at[:, at], decay * decay_of(early_ref))
        start = at.stop


def mix(first_head, x_ref, cum_ref, row_ref, score_ref, skip_ref, put):
    width = x_ref.shape[1]
    half = BLOCK // 2
    expand = spread(first_head, width, 3)
    skip = dot(skip_ref[...], expand)[0:1]
    lower = lax.broadcasted_iota(jnp.int32, (half, half), 0) >= lax.broadcasted_iota(
        jnp.int32, (half, half), 1
    )
    lane = lax.broadcasted_iota(jnp.int32, (BLOCK, LANES), 1)
    for block in range(PAIR):
        base = block * BLOCK
        for tile in range(width // LANES):
            columns = slice(tile * LANES, (tile + 1) * LANES)
            x = x_ref[base : base + BLOCK, columns]
            top = skip[:, columns] * x[:half].astype(F32)
            bottom = skip[:, columns] * x[half:].astype(F32)
            for side in range(LANES // HEAD_DIM):
                head = first_head + tile * (LANES // HEAD_DIM) + side
                own = jnp.where(lane // HEAD_DIM == side, x, jnp.zeros_like(x))
                cum = cum_ref[base : base + BLOCK, head : head + 1]
                row = row_ref[head : head + 1, base : base + BLOCK]
                diag = jnp.where(lower, cum[:half] - row[:, :half], -1e30)
                mixing = jnp.exp2(diag) * score_ref[base : base + half, :half]
                top = top + dot(mixing.astype(BF16), own[:half])
                left = jnp.exp2(cum[half:] - row[:, :half]) * score_ref[base + half : base + BLOCK, :half]
                diag = jnp.where(lower, cum[half:] - row[:, half:], -1e30)
                right = jnp.exp2(diag) * score_ref[base + half : base + BLOCK, half:]
                mixing = jnp.concatenate([left.astype(BF16), right.astype(BF16)], 1)
                bottom = bottom + dot(mixing, own)
            put(block, slice(base, base + half), columns, top)
            put(block, slice(base + half, base + BLOCK), columns, bottom)


def local_kernel(first_head, x_ref, cum_ref, row_ref, score_ref, skip_ref, *refs):
    out_ref = refs[-1]

    def put(block, rows, columns, value):
        out_ref[rows, columns] = value

    mix(first_head, x_ref, cum_ref, row_ref, score_ref, skip_ref, put)


def carry(first_head, core, lasts, befores, alones, own_ref, c_ref, factor_ref, add, keep_ref, send_ref):
    expand = spread(first_head, own_ref.shape[1], 2)
    last, before = (
        refs[0][...] if len(refs) == 1 else jnp.concatenate([ref[...] for ref in refs], 1)
        for refs in (lasts, befores)
    )
    held = last[:STATE].astype(F32) + decay_of(last) * before[:STATE].astype(F32)
    for alone in alones:
        held = held + alone[:STATE].astype(F32)
    factor = dot(factor_ref[...], expand)
    outs = []
    for block in range(PAIR):
        at = slice(block * BLOCK, (block + 1) * BLOCK)
        carried = dot(c_ref[at], held.astype(BF16))
        outs.append((add[at] + factor[at] * carried).astype(BF16))
        held = factor[BLOCK - 1 : BLOCK] * held + own_ref[...]

    @pl.when(core == 0)
    def _():
        keep_ref[...] = outs[0]
        send_ref[...] = outs[1]

    @pl.when(core == 1)
    def _():
        keep_ref[...] = outs[1]
        send_ref[...] = outs[0]


def final_kernel(first_head, counts, place, *refs):
    groups = []
    for number in counts:
        groups.append(refs[:number])
        refs = refs[number:]
    carry(first_head, place[2], *groups, *refs[:4], *refs[-2:])


def finish_kernel(first_head, counts, place, *refs):
    groups = []
    for number in counts:
        groups.append(refs[:number])
        refs = refs[number:]
    own_ref, c_ref, factor_ref = refs[:3]
    keep_ref, send_ref, partial = refs[-3:]
    local_kernel(first_head, *refs[3:8], partial)
    carry(first_head, place[2], *groups, own_ref, c_ref, factor_ref, partial, keep_ref, send_ref)


def place_kernel(firsts, place, *refs):
    count = len(firsts)
    keeps, gots = refs[:count], refs[count : 2 * count]
    out, sems = refs[-2:]
    core = place[2]
    half = out.shape[1] // PAIR
    copies = []
    for first, keep, got in zip(firsts, keeps, gots):
        width = keep.shape[1]
        copies.append((keep, out.at[:, ds(core * half + first, width)]))
        copies.append((got, out.at[:, ds((1 - core) * half + first, width)]))
    for copy in run(copies, sems):
        copy.wait()


def put_in_place(firsts, shape, place, keeps, gots):
    smem, vmem, hbm = (pl.BlockSpec(memory_space=m) for m in (pltpu.SMEM, pltpu.VMEM, pltpu.HBM))
    count = len(firsts)
    return pl.pallas_call(
        functools.partial(place_kernel, firsts),
        out_shape=jax.ShapeDtypeStruct(shape, BF16),
        in_specs=[smem] + [vmem] * (2 * count),
        out_specs=hbm,
        scratch_shapes=[pltpu.SemaphoreType.DMA((2 * count,))],
        compiler_params=pltpu.CompilerParams(vmem_limit_bytes=16 << 20),
        cost_estimate=pl.CostEstimate(flops=1, bytes_accessed=1, transcendentals=0),
        name="place",
    )(place, *keeps, *gots)


class Stay:
    def __init__(self, array):
        self.array = array


def gate(blocks, order):
    anywhere = pl.BlockSpec(memory_space=pl.ANY)
    return pl.pallas_call(
        lambda *refs: None,
        out_shape=[jax.ShapeDtypeStruct(block.shape, block.dtype) for block in blocks],
        in_specs=[anywhere] * (len(blocks) + len(order)),
        out_specs=[anywhere] * len(blocks),
        input_output_aliases={i: i for i in range(len(blocks))},
        compiler_params=pltpu.CompilerParams(vmem_limit_bytes=16 << 20),
        cost_estimate=pl.CostEstimate(flops=1, bytes_accessed=1, transcendentals=0),
        name="gate",
    )(*blocks, *order)


def call(body, outs, operands, scratch=(), flops=0, transcendentals=0, name=None, limit=16 << 20):
    shapes = [jax.ShapeDtypeStruct(shape, dtype) for shape, dtype in outs]
    smem, vmem, hbm = (pl.BlockSpec(memory_space=m) for m in (pltpu.SMEM, pltpu.VMEM, pltpu.HBM))
    specs = [
        hbm if isinstance(o, Stay) else smem if o.dtype == jnp.int32 else vmem for o in operands
    ]
    moved = sum(o.size * o.dtype.itemsize for o in shapes) * 2
    return pl.pallas_call(
        body,
        out_shape=shapes,
        in_specs=specs,
        out_specs=[vmem] * len(outs),
        scratch_shapes=scratch,
        compiler_params=pltpu.CompilerParams(vmem_limit_bytes=limit),
        cost_estimate=pl.CostEstimate(flops=1, bytes_accessed=1, transcendentals=0),
        name=name,
    )(*[o.array if isinstance(o, Stay) else o for o in operands])


def paired(xbc, dt_raw, conv_weight, conv_bias, a_log, dt_bias, skip_gain):
    axes = ("ctx", "head")
    shards, length = lax.axis_size("head"), lax.axis_size("ctx")
    devices, peers = shards * length, shards * PAIR
    tok = xbc.shape[0]
    slab = tok * peers
    context, shard = lax.axis_index("ctx"), lax.axis_index("head")
    pair, core = context // PAIR, context % PAIR
    group = shard * PAIR + core
    place = jnp.stack([group, pair, core, core * shards + shard, shard]).astype(jnp.int32)

    def over(block, target):
        route = [(i, target(i)) for i in range(devices)]
        return lax.ppermute(block, axes, [(i, j) for i, j in route if j is not None and j < devices])

    def swap(block):
        return over(block, lambda i: i ^ shards)

    rows = Stay(xbc)
    size = PER_GROUP + 2 * STATE
    (sent,) = call(
        functools.partial(pack_first_kernel, shards),
        [((tok, shards * WIDTHS[0] + size - WIDTHS[0]), BF16)],
        [place, rows],
        scratch=[pltpu.SemaphoreType.DMA((4 * shards,))],
        name="pack_first",
    )
    got_first = swap(sent)
    sent, tail = call(
        functools.partial(pack_kernel, shards),
        [((tok, shards * (size - WIDTHS[0]) + HEADS), BF16), ((16, shards * size), BF16)],
        [place, rows, Stay(dt_raw), Stay(sent)],
        scratch=[pltpu.SemaphoreType.DMA((6 * shards + 1,))],
        name="pack",
    )
    got_rest = swap(sent)
    taps, offset = call(
        taps_kernel,
        [((4, size), F32), ((1, size), F32)],
        [place, Stay(conv_weight), Stay(conv_bias[None]), Stay(got_rest)],
        scratch=[pltpu.SemaphoreType.DMA((6,))],
        name="taps",
    )

    def send_on(plan, order, tail=None, edges=None):
        unused = Stay(got_first)
        parts = [p for _, pieces in plan for p in pieces]
        made = [] if tail is None else [((3, shards * size), BF16)]
        return call(
            functools.partial(merge_kernel, shards, plan, len(order)),
            [((PAIR * tok, sum(map(total_of, pieces))), BF16) for _, pieces in plan] + made,
            [
                place,
                rows,
                Stay(dt_raw) if edges is None else dt_raw,
                got_first if 0 in parts else unused,
                got_rest if any(parts) else unused,
                next((o for o in (tail, edges) if o is not None), unused),
            ]
            + [Stay(o) for o in order],
            scratch=[pltpu.SemaphoreType.DMA((sum(2 + 2 * len(RESTS[p]) for p in parts),))],
            name="merge",
        )

    def travel(blocks):
        return [blocks[0]] + [over(blocks[r], lambda i, r=r: i ^ r) for r in range(1, shards)]

    def plan(piece):
        return [(r, (piece,)) for r in range(shards)]

    *first_blocks, edges = send_on(plan(0), [], tail)
    message = [travel(first_blocks)]
    edges = over(edges, lambda i: i + peers if i % shards == shards - 1 else None)
    second_blocks = send_on(plan(1), [first_blocks[0]], None, edges)
    message.append(travel(second_blocks))
    third_blocks = send_on(plan(2), [second_blocks[0]])
    message.append(travel(third_blocks[:1] + gate(third_blocks[1:], message[0][1:] + message[1][1:])))

    def seen(piece):
        return message[piece]

    tiles = [p.reshape(HEADS // LANES, LANES) for p in (a_log, dt_bias, skip_gain)]
    b, edge, cum, row, factor, tail, skip = call(
        functools.partial(prep_kernel, shards),
        [
            ((slab, STATE), BF16),
            ((4, size), F32),
            ((slab, LANES), F32),
            ((LANES, slab), F32),
            ((slab, 2 * LANES), BF16),
            ((slab, 2 * LANES), BF16),
            ((16, 3 * LANES), BF16),
        ],
        [place] + seen(1) + [taps, offset] + tiles + [Stay(third_blocks[0])],
        scratch=[pltpu.VMEM((slab, LANES), F32), pltpu.VMEM((slab + 8, STATE), F32)],
        name="prep",
    )
    count = len(GROUPED)
    x, sent, own, last, joined, before, alone, keep, send = ([None] * count for _ in range(9))

    def first_head(i):
        return (sum(WIDTHS[: GROUPED[i][0]]) + GROUPED[i][1]) // HEAD_DIM

    def state_of(i, order):
        piece, _, width = GROUPED[i]
        x[i], own[i], *sent[i] = call(
            functools.partial(state_kernel, shards, GROUPED[i], FIRST_ROUND[i]),
            [((slab, width), BF16), ((STATE, width), F32)] + [((STATE + 16, w), BF16) for w in FIRST_ROUND[i]],
            [place] + seen(piece) + [taps, offset, edge, b, factor, tail] + [Stay(o) for o in order],
            scratch=[pltpu.VMEM((slab + 8, width), F32)],
            name="state",
        )
        every = i not in ALONE
        last[i] = [over(part, lambda i: i + peers if every or i // peers % 2 == 0 else None) for part in sent[i]]

    def combine_of(i, order):
        joined[i], before[i], alone[i] = [], [], []
        step = len(FIRST_ROUND[i]) // len(SECOND_ROUND[i])
        for j, width in enumerate(SECOND_ROUND[i]):
            early, late = last[i][j * step : (j + 1) * step], sent[i][j * step : (j + 1) * step]
            (total,) = call(
                functools.partial(combine_kernel, len(early)),
                [((STATE + 16, width), BF16)],
                early + late + [Stay(o) for o in order],
                name="combine",
            )
            joined[i].append(total)
            if i in ALONE:
                before[i].append(over(total, lambda i: i + 2 * peers if i // peers == 1 else None))
                alone[i].append(over(total, lambda i: i + peers if i // peers == 1 else None))
            else:
                before[i].append(over(total, lambda i: i + 2 * peers))
            order = [total]

    def finish_of(body, i, operands, order, **more):
        keep[i], send[i] = call(
            functools.partial(body, first_head(i), (len(last[i]), len(before[i]), len(alone[i]))),
            [((BLOCK, GROUPED[i][2]), BF16)] * 2,
            [place, *last[i], *before[i], *alone[i], own[i], c, factor] + operands + [Stay(o) for o in order],
            name="final",
            **more,
        )

    state_of(0, [])
    combine_of(0, [])
    fourth_blocks = send_on(plan(3), sent[0])
    message.append(travel(fourth_blocks))
    state_of(1, [fourth_blocks[0], joined[0][0]])
    combine_of(1, [])
    state_of(2, joined[1])
    state_of(3, sent[2])
    c, score = call(
        functools.partial(score_kernel, shards),
        [((slab, STATE), BF16), ((slab, BLOCK), F32)],
        [place] + seen(3) + [taps, offset, edge, b] + [Stay(o) for o in sent[3] + before[1]],
        scratch=[pltpu.VMEM((slab + 8, STATE), F32)],
        name="score",
    )
    mixes = [cum, row, score, skip]

    def in_full(i, order):
        wide = [pltpu.VMEM((slab, GROUPED[i][2]), F32)]
        finish_of(finish_kernel, i, [x[i]] + mixes, order, scratch=wide)

    combine_of(2, [score])
    in_full(1, joined[2])
    combine_of(3, [keep[1]])
    order, partial = joined[3][0], {}
    for i in (2, 3):
        (partial[i],) = call(
            functools.partial(local_kernel, first_head(i)),
            [(x[i].shape, F32)],
            [x[i]] + mixes + [Stay(order)],
            name="local",
        )
        order = partial[i]
    in_full(0, [order])
    order = keep[0]
    for i in (2, 3):
        finish_of(final_kernel, i, [partial[i]], [order])
        order = keep[i]
    firsts = [first_head(i) * HEAD_DIM for i in range(count)]
    return put_in_place(firsts, (BLOCK, PAIR * PER_GROUP), place, keep, [swap(o) for o in send])


def solution(mesh):
    in_specs = (P(("ctx", "head"), None), P(("ctx", "head"), None), P(), P(), P(), P(), P())
    out_specs = P("ctx", "head")
    shards, length = mesh.shape["head"], mesh.shape["ctx"]

    def program(xbc, *rest):
        slab = xbc.shape[0] // length
        fits = shards == GROUPS // PAIR and length == 4 * PAIR and slab == BLOCK
        return jax.shard_map(
            paired if fits else on_device,
            mesh=mesh,
            in_specs=in_specs,
            out_specs=out_specs,
            check_vma=False,
        )(xbc, *rest)

    return program
```

```python
import functools

import jax
import jax.numpy as jnp
from jax import lax
from jax.experimental import pallas as pl
from jax.experimental.pallas import tpu as pltpu
from jax.sharding import PartitionSpec as P

HEADS = 256
HEAD_DIM = 64
STATE = 256
GROUPS = 8
BLOCK = 256


def from_behind(block, axis, distance):
    devices = range(lax.axis_size(axis))
    route = [(i - distance, i) for i in devices if i - distance in devices]
    return lax.ppermute(block, axis, route)


def carried_in(array, axis, combine, identity):
    length, index = (lax.axis_size(axis), lax.axis_index(axis))
    everything = jax.tree.map(lambda part: lax.all_gather(part, axis), array)
    start = jax.tree.map(
        lambda part, zero: jnp.broadcast_to(jnp.asarray(zero, part.dtype), part.shape),
        array,
        identity,
    )

    def hop(k, before):
        reached = k < index
        new = combine(before, jax.tree.map(lambda part: part[k], everything))
        return jax.tree.map(lambda a, b: jnp.where(reached, a, b), new, before)

    return lax.fori_loop(0, length, hop, start)


def convolve(rows, edge, weight, bias):
    count = rows.shape[0]
    wide = jnp.concatenate([edge, rows], 0).astype(jnp.float32)
    acc = bias[None, :] + weight[0] * wide[0:count]
    acc = acc + weight[1] * wide[1 : count + 1]
    acc = acc + weight[2] * wide[2 : count + 2]
    acc = acc + weight[3] * wide[3 : count + 3]
    return jax.nn.silu(acc).astype(jnp.bfloat16)


def rearrange_heads(rows, shards, per_dev, groups_dev, per_group):
    count = rows.shape[0]
    inner = HEADS * HEAD_DIM
    replicate_groups = max(1, per_group // per_dev)
    heads_part = rows[:, :inner].reshape(count, shards, per_dev * HEAD_DIM)
    b_part = rows[:, inner : inner + GROUPS * STATE].reshape(count, GROUPS, STATE)
    c_part = rows[:, inner + GROUPS * STATE :].reshape(count, GROUPS, STATE)
    b_part = jnp.repeat(b_part, replicate_groups, axis=1).reshape(count, shards, groups_dev * STATE)
    c_part = jnp.repeat(c_part, replicate_groups, axis=1).reshape(count, shards, groups_dev * STATE)
    return jnp.concatenate([heads_part, b_part, c_part], axis=2)


def inner_block(xs, bmat, cmat, steps, cum):
    size = xs.shape[0]
    lower = jnp.arange(size)[:, None] >= jnp.arange(size)[None, :]
    scores = jnp.einsum("qgn,kgn->gqk", cmat, bmat, preferred_element_type=jnp.float32)
    order = jnp.transpose(cum, (1, 2, 0))
    gap = order[..., :, None] - order[..., None, :]
    decay = jnp.exp(jnp.where(lower, gap, -jnp.inf))
    mixing = (scores[:, None] * decay * jnp.transpose(steps, (1, 2, 0))[..., None, :]).astype(
        jnp.bfloat16
    )
    local = jnp.einsum("gjqk,kgjp->qgjp", mixing, xs, preferred_element_type=jnp.float32)
    tail = jnp.exp(cum[size - 1][None] - cum) * steps
    loaded = (bmat[:, :, None, :].astype(jnp.float32) * tail[..., None]).astype(jnp.bfloat16)
    block_state = jnp.einsum("kgjn,kgjp->gjnp", loaded, xs, preferred_element_type=jnp.float32)
    return (local, block_state)


def on_device(xbc, dt_raw, conv_weight, conv_bias, a_log, dt_bias, skip_gain):
    tok = xbc.shape[0]
    shards = lax.axis_size("head")
    per_dev = HEADS // shards
    per_group = HEADS // GROUPS
    groups_dev = max(1, per_dev // per_group)
    heads_per_cluster = per_dev // groups_dev
    sent = rearrange_heads(xbc, shards, per_dev, groups_dev, per_group)
    mine, rates = (
        lax.all_to_all(sent, "head", split_axis=1, concat_axis=0, tiled=True),
        lax.all_to_all(
            dt_raw.reshape(tok, shards, per_dev), "head", split_axis=1, concat_axis=0, tiled=True
        ),
    )
    slab = tok * shards
    mine = mine.reshape(slab, mine.shape[2])
    rates = rates.reshape(slab, per_dev)
    shard = lax.axis_index("head")
    taps = lax.dynamic_index_in_dim(
        rearrange_heads(conv_weight, shards, per_dev, groups_dev, per_group),
        shard,
        1,
        keepdims=False,
    )
    offset = lax.dynamic_index_in_dim(
        rearrange_heads(conv_bias[None, :], shards, per_dev, groups_dev, per_group),
        shard,
        1,
        keepdims=False,
    )
    edge = from_behind(mine[slab - 3 :], "ctx", 1)
    mine = convolve(mine, edge, taps, offset[0])
    nchunk = slab // BLOCK
    width = per_dev * HEAD_DIM
    xs = mine[:, :width].reshape(nchunk, BLOCK, groups_dev, heads_per_cluster, HEAD_DIM)
    bmat = mine[:, width : width + groups_dev * STATE].reshape(nchunk, BLOCK, groups_dev, STATE)
    cmat = mine[:, width + groups_dev * STATE :].reshape(nchunk, BLOCK, groups_dev, STATE)
    first = shard * per_dev
    rate = (-jnp.exp(lax.dynamic_slice_in_dim(a_log, first, per_dev))).reshape(
        groups_dev, heads_per_cluster
    )
    bias_dt = lax.dynamic_slice_in_dim(dt_bias, first, per_dev).reshape(
        groups_dev, heads_per_cluster
    )
    skip = lax.dynamic_slice_in_dim(skip_gain, first, per_dev).reshape(
        groups_dev, heads_per_cluster
    )
    steps = jax.nn.softplus(
        rates.astype(jnp.float32).reshape(nchunk, BLOCK, groups_dev, heads_per_cluster) + bias_dt
    )
    cum = jnp.cumsum(steps * rate, axis=1)

    def block_step(carry, item):
        held, product = carry
        x_part, b_part, c_part, step_part, cum_part = item
        local, block_state = inner_block(x_part, b_part, c_part, step_part, cum_part)
        lifted = c_part.astype(jnp.float32)[:, :, None, :] * jnp.exp(cum_part)[..., None]
        carried = jnp.einsum("qgjn,gjnp->qgjp", lifted, held, precision=lax.Precision.HIGHEST)
        partial_out = local + carried + skip[..., None] * x_part.astype(jnp.float32)
        end = jnp.exp(cum_part[BLOCK - 1])
        return ((end[..., None, None] * held + block_state, product * end), (partial_out, product))

    zero_state = jnp.zeros((groups_dev, heads_per_cluster, STATE, HEAD_DIM), jnp.float32)
    unit = jnp.ones((groups_dev, heads_per_cluster), jnp.float32)
    (slab_state, slab_decay), (partials, product_in) = lax.scan(
        block_step, (zero_state, unit), (xs, bmat, cmat, steps, cum)
    )

    def combine(preceding_state, later):
        return (
            preceding_state[0] * later[0],
            later[0][..., None, None] * preceding_state[1] + later[1],
        )

    _, entering = carried_in((slab_decay, slab_state), "ctx", combine, (unit, zero_state))
    projected = jnp.einsum(
        "cqgn,gjnp->cqgjp", cmat.astype(jnp.float32), entering, precision=lax.Precision.HIGHEST
    )
    factor = jnp.exp(cum) * product_in[:, None]
    total = partials + factor[..., None] * projected
    return total.astype(jnp.bfloat16).reshape(slab, width)


PAIR = 2
LANES = 128
LOG2E = 1.4426950408889634
F32, BF16 = jnp.float32, jnp.bfloat16
WIDTHS = (512, 0, 768, 768)
RESTS = ("", "BD", "", "C")
GROUPED = ((0, 0, 512), (2, 0, 768), (3, 0, 384), (3, 384, 384))
FIRST_ROUND = ((256, 256), (384, 384), (384,), (384,))
SECOND_ROUND = ((512,), (384, 384), (384,), (384,))


def halves(value, count):
    parts = []
    for _ in range(count):
        part = value.astype(BF16)
        parts.append(part)
        value = value - part.astype(F32)
    return parts


def spread(first_head, width, copies):
    lane = lax.broadcasted_iota(jnp.int32, (copies * LANES, width), 0) % LANES
    column = lax.broadcasted_iota(jnp.int32, (copies * LANES, width), 1)
    return (lane == first_head + column // HEAD_DIM).astype(BF16)


def dot(a, b):
    return jnp.dot(a, b, preferred_element_type=F32)


def ds(start, width):
    return pl.ds(pl.multiple_of(start, LANES), width)


def run(copies, sems):
    started = []
    for i, (source, target) in enumerate(copies):
        copy = pltpu.make_async_copy(source, target, sems.at[i])
        copy.start()
        started.append(copy)
    return started


PER_GROUP = HEADS * HEAD_DIM // GROUPS
INNER = HEADS * HEAD_DIM


def channels(group, first, width):
    return ds(group * PER_GROUP + first, width)


def pack_first_kernel(shards, place, xbc, send, sems):
    core, shard = place[2], place[4]
    count = xbc.shape[0]
    width = WIDTHS[0]
    copies = []
    for r in range(shards):
        group = (shard ^ r) * PAIR + 1 - core
        copies.append((xbc.at[:, channels(group, 0, width)], send.at[:, r * width : (r + 1) * width]))
        last, rows = xbc.at[count - 16 :], slice(16 * r, 16 * r + 16)
        to = shards * width
        copies.append((last.at[:, channels(group, width, PER_GROUP - width)], send.at[rows, to : to + PER_GROUP - width]))
        to += PER_GROUP - width
        for i in range(2):
            at = ds(INNER + (i * GROUPS + group) * STATE, STATE)
            copies.append((last.at[:, at], send.at[rows, to + i * STATE : to + (i + 1) * STATE]))
    for copy in run(copies, sems):
        copy.wait()


def pack_kernel(shards, place, xbc, dt_raw, order, send, tail, sems):
    core, shard = place[2], place[4]
    count = xbc.shape[0]
    first = WIDTHS[0]
    width = PER_GROUP - first
    rest = width * shards
    size = PER_GROUP + 2 * STATE
    copies = []
    for r in range(shards):
        group = (shard ^ r) * PAIR + 1 - core
        copies.append((xbc.at[:, channels(group, first, width)], send.at[:, r * width : (r + 1) * width]))
        for i in range(2):
            to = rest + (i * shards + r) * STATE
            copies.append((xbc.at[:, ds(INNER + (i * GROUPS + group) * STATE, STATE)], send.at[:, to : to + STATE]))
    copies.append((dt_raw, send.at[:, send.shape[1] - HEADS :]))
    for r in range(shards):
        group, to = (shard ^ r) * PAIR + core, r * size
        last = xbc.at[count - 16 :]
        copies.append((last.at[:, channels(group, 0, PER_GROUP)], tail.at[:, to : to + PER_GROUP]))
        for i in range(2):
            at = ds(INNER + (i * GROUPS + group) * STATE, STATE)
            start = to + PER_GROUP + i * STATE
            copies.append((last.at[:, at], tail.at[:, start : start + STATE]))
    for copy in run(copies, sems):
        copy.wait()


def taps_kernel(place, weight, bias, order, taps, offset, sems):
    copies = []
    for source, target in ((weight, taps), (bias, offset)):
        copies.append((source.at[:, channels(place[0], 0, PER_GROUP)], target.at[:, :PER_GROUP]))
        for i in range(2):
            at = ds(INNER + (i * GROUPS + place[0]) * STATE, STATE)
            start = PER_GROUP + i * STATE
            copies.append((source.at[:, at], target.at[:, start : start + STATE]))
    for copy in run(copies, sems):
        copy.wait()


def put_edge(shards, place, got, tail, out):
    count = got.shape[0]
    first = WIDTHS[0]
    size = PER_GROUP + 2 * STATE
    for r in range(shards):
        theirs = [got[count - 16 :, r * first : (r + 1) * first]]
        theirs.append(got[16 * r : 16 * r + 16, shards * first :])
        to = r * size
        for part in theirs:
            at = slice(to, to + part.shape[1])
            rows = jnp.where(place[2] == 0, part.astype(F32), tail[:, at].astype(F32))
            out[:, at] = rows[13:16].astype(BF16)
            to = at.stop


def total_of(piece):
    return WIDTHS[piece] + sum(LANES if kind == "D" else STATE for kind in RESTS[piece])


def merge_kernel(shards, plan, unread, place, xbc, dt_raw, got_first, got, edges, *refs):
    refs = refs[unread:]
    outs, sems = refs[: len(plan)], refs[-1]
    core, shard = place[2], place[4]
    count = xbc.shape[0]
    stride = PER_GROUP - WIDTHS[0]
    mine = pl.ds(pl.multiple_of(core * count, count), count)
    other = pl.ds(pl.multiple_of((1 - core) * count, count), count)
    copies, steps = [], []
    for out, (r, pieces) in zip(outs, plan):
        group = (shard ^ r) * PAIR + core
        to = 0
        for piece in pieces:
            first, width = sum(WIDTHS[:piece]), WIDTHS[piece]
            if piece == 0:
                source = got_first.at[:, r * width : (r + 1) * width]
            else:
                at = r * stride + first - WIDTHS[0]
                source = got.at[:, at : at + width]
            if width:
                copies.append((xbc.at[:, channels(group, first, width)], out.at[mine, to : to + width]))
                copies.append((source, out.at[other, to : to + width]))
            to += width
            for kind in RESTS[piece]:
                if kind == "D":
                    steps.append((out, r, to))
                    to += LANES
                    continue
                i = "BC".index(kind)
                at = ds(INNER + (i * GROUPS + group) * STATE, STATE)
                copies.append((xbc.at[:, at], out.at[mine, to : to + STATE]))
                at = stride * shards + (i * shards + r) * STATE
                copies.append((got.at[:, at : at + STATE], out.at[other, to : to + STATE]))
                to += STATE
    started = run(copies, sems)
    if len(refs) > len(plan) + 1:
        put_edge(shards, place, got_first, edges, refs[-2])
    if steps:
        lane = lax.broadcasted_iota(jnp.int32, (count, LANES), 1)
        per_tile = LANES * GROUPS // HEADS
        heads = HEADS // GROUPS
        for out, r, to in steps:
            group = (shard ^ r) * PAIR + core
            tile, shift = group // per_tile, (LANES - (group % per_tile) * heads) % LANES
            own = dt_raw[:, ds(tile * LANES, LANES)].astype(F32)
            theirs = got[:, ds(got.shape[1] - HEADS + tile * LANES, LANES)].astype(F32)
            low = jnp.where(core == 0, own, theirs)
            high = jnp.where(core == 0, theirs, own)
            packed = jnp.zeros((count // 2, LANES), F32)
            for j, rows in enumerate((low, high)):
                rows = jnp.where(lane < heads, pltpu.roll(rows, shift, 1), 0.0)
                for i in range(2):
                    part = rows[i * count // 2 : (i + 1) * count // 2]
                    packed = packed + pltpu.roll(part, (2 * j + i) * heads, 1)
            out[: count // 2, to : to + LANES] = packed.astype(BF16)
            size = PER_GROUP + 2 * STATE
            at = slice(r * size, (r + 1) * size)
            edge = jnp.concatenate([edges[:, at].astype(F32), jnp.zeros((1, size), F32)], 0)
            edge = jnp.concatenate([edge[:, q * LANES : (q + 1) * LANES] for q in range(size // LANES)], 0)
            fill = jnp.zeros((PAIR * count - count // 2 - edge.shape[0], LANES), F32)
            out[count // 2 :, to : to + LANES] = jnp.concatenate([edge, fill], 0).astype(BF16)
    for copy in started:
        copy.wait()


def view(refs, piece):
    return [(ref, 0) for ref in refs]


def convolve_in_order(place, blocks, columns, edge, tap, bias, wide, put):
    width = columns.stop - columns.start
    count = blocks[0][0].shape[0] // PAIR
    wide[5:8, :width] = edge
    for r, (block, origin) in enumerate(blocks):
        for core in range(PAIR):
            at = pl.multiple_of((core * len(blocks) + (place[4] ^ r)) * count + 8, 8)
            part = block[core * count : (core + 1) * count, origin + columns.start : origin + columns.stop]
            wide[pl.ds(at, count), :width] = part.astype(F32)
    tap, bias = tap * 0.5, bias * 0.5
    for start in range(0, PAIR * len(blocks) * count, count):
        acc = bias + tap[0:1] * wide[start + 5 : start + 5 + count, :width]
        acc = acc + tap[1:2] * wide[start + 6 : start + 6 + count, :width]
        acc = acc + tap[2:3] * wide[start + 7 : start + 7 + count, :width]
        acc = acc + tap[3:4] * wide[start + 8 : start + 8 + count, :width]
        put(start, count, (acc + acc * jnp.tanh(acc)).astype(BF16))


def prep_kernel(shards, place, *refs):
    blocks, (taps, offset, a_ref, bias_ref, skip_ref, order) = refs[:shards], refs[shards : shards + 6]
    b_ref, edge_ref, cum_ref, row_ref, factor_ref, tail_ref, skip_out, dt_ref, wide = refs[shards + 6 :]
    blocks = view(blocks, 1)
    start = WIDTHS[1]
    last = total_of(1) - LANES
    size = edge_ref.shape[1]
    count = blocks[0][0].shape[0] // PAIR
    half, heads = count // 2, HEADS // GROUPS
    columns = [block[:, origin + last : origin + last + LANES].astype(F32) for block, origin in blocks]
    edge = columns[0][half : half + 4 * size // LANES]
    for column in columns[1:]:
        edge = edge + column[half : half + 4 * size // LANES]
    for q in range(size // LANES):
        edge_ref[:, q * LANES : (q + 1) * LANES] = edge[4 * q : 4 * q + 4]
    for r, column in enumerate(columns):
        packed = column[:half]
        for j in range(2 * PAIR):
            at = ((j // 2) * shards + (place[4] ^ r)) * count + (j % 2) * half
            rows = packed if j == 0 else pltpu.roll(packed, LANES - j * heads, 1)
            dt_ref[pl.ds(pl.multiple_of(at, half), half), :] = rows

    def put(start, count, value):
        b_ref[start : start + count] = value

    at = slice(PER_GROUP, PER_GROUP + STATE)
    convolve_in_order(
        place, blocks, slice(start, start + STATE), edge_ref[0:3, at], taps[:, at], offset[:, at], wide, put
    )
    per_tile = LANES * GROUPS // HEADS
    group = place[0]
    tile = group // per_tile
    shift = (LANES - (group % per_tile) * heads) % LANES

    def lanes_of(ref):
        return pltpu.roll(jnp.broadcast_to(ref[pl.ds(tile, 1), :], (8, LANES)), shift, 1)

    rate = -jnp.exp(lanes_of(a_ref)[0:1])
    raw = dt_ref[...] + lanes_of(bias_ref)[0:1]
    step = jnp.maximum(raw, 0.0) + jnp.log1p(jnp.exp(-jnp.abs(raw)))
    skip = lanes_of(skip_ref)
    skip_out[...] = jnp.concatenate(halves(jnp.concatenate([skip, skip], 0), 3), 1)
    lower = (
        lax.broadcasted_iota(jnp.int32, (BLOCK, BLOCK), 0)
        >= lax.broadcasted_iota(jnp.int32, (BLOCK, BLOCK), 1)
    ).astype(BF16)
    valid = lax.broadcasted_iota(jnp.int32, (BLOCK, LANES), 1) < heads
    for block in range(PAIR):
        at = slice(block * BLOCK, (block + 1) * BLOCK)
        here = jnp.where(valid, step[at], 1.0)
        parts = halves(here * rate, 3)
        cum = dot(lower, parts[0]) + (dot(lower, parts[1]) + dot(lower, parts[2]))
        cum = cum * LOG2E
        cum_ref[at] = cum
        row_ref[:, at] = jnp.transpose(cum - jnp.log2(here))
        factor_ref[at] = jnp.concatenate(halves(jnp.exp2(cum), 2), 1)
        tail = jnp.exp2(cum[BLOCK - 1 :] - cum) * here
        tail_ref[at] = jnp.concatenate(halves(tail, 2), 1)


def score_kernel(shards, place, *refs):
    blocks, refs = refs[:shards], refs[shards:]
    taps, offset, edge_ref, b_ref, c_ref, score_ref, wide = (*refs[:4], *refs[-3:])
    blocks = view(blocks, 3)
    start = WIDTHS[3]
    at = slice(PER_GROUP + STATE, PER_GROUP + 2 * STATE)

    def put(start, count, value):
        c_ref[start : start + count] = value

    convolve_in_order(
        place, blocks, slice(start, start + STATE), edge_ref[0:3, at], taps[:, at], offset[:, at], wide, put
    )
    for block in range(PAIR):
        at = slice(block * BLOCK, (block + 1) * BLOCK)
        score_ref[at] = lax.dot_general(
            c_ref[at], b_ref[at], (((1,), (1,)), ((), ())), preferred_element_type=F32
        )


def decay_of(ref):
    decay = ref[STATE : STATE + 16].astype(F32)
    return decay[0:1] + (decay[1:2] + decay[2:3])


def put_decay(ref, decay):
    row = lax.broadcasted_iota(jnp.int32, (16, ref.shape[1]), 0)
    high, middle, low = (part.astype(F32) for part in halves(decay, 3))
    packed = jnp.where(row == 0, high, jnp.where(row == 1, middle, jnp.where(row == 2, low, 0.0)))
    ref[STATE:] = packed.astype(BF16)


def state_kernel(shards, part, sizes, place, *refs):
    blocks, refs = refs[:shards], refs[shards:]
    taps, offset, edge_ref, b_ref, factor_ref, tail_ref = refs[:6]
    x_ref, own_ref, *sends, wide = refs[-3 - len(sizes) :]
    piece, start, width = part
    first = sum(WIDTHS[:piece]) + start
    at = slice(first, first + width)

    def put(row, count, value):
        x_ref[row : row + count] = value

    blocks = view(blocks, piece)
    columns = slice(start, start + width)
    convolve_in_order(place, blocks, columns, edge_ref[0:3, at], taps[:, at], offset[:, at], wide, put)
    expand = spread(first // HEAD_DIM, width, 2)
    both = []
    for block in range(PAIR):
        at = slice(block * BLOCK, (block + 1) * BLOCK)
        loaded = (x_ref[at].astype(F32) * dot(tail_ref[at], expand)).astype(BF16)
        both.append(
            lax.dot_general(b_ref[at], loaded, (((0,), (0,)), ((), ())), preferred_element_type=F32)
        )
    ends = [dot(factor_ref[(i + 1) * BLOCK - 16 : (i + 1) * BLOCK], expand)[15:16] for i in range(PAIR)]
    own_ref[...] = both[0]
    end = (ends[1] * both[0] + both[1]).astype(BF16)
    decay = ends[0] * ends[1]
    start = 0
    for send_ref in sends:
        at = slice(start, start + send_ref.shape[1])
        send_ref[0:STATE] = end[:, at]
        put_decay(send_ref, decay[:, at])
        start = at.stop


def combine_kernel(count, place, *refs):
    got, own, out_ref = refs[:count], refs[count : 2 * count], refs[-1]
    odd = place[1] % 2 == 1
    start = 0
    for got_ref, own_ref in zip(got, own):
        at = slice(start, start + own_ref.shape[1])
        theirs, mine = got_ref[:STATE].astype(F32), own_ref[:STATE].astype(F32)
        decay, other = decay_of(own_ref), decay_of(got_ref)
        early, late = jnp.where(odd, theirs, mine), jnp.where(odd, mine, theirs)
        out_ref[:STATE, at] = (jnp.where(odd, decay, other) * early + late).astype(BF16)
        put_decay(out_ref.at[:, at], decay * other)
        start = at.stop


def mix(first_head, x_ref, cum_ref, row_ref, score_ref, skip_ref, put):
    width = x_ref.shape[1]
    half = BLOCK // 2
    expand = spread(first_head, width, 3)
    skip = dot(skip_ref[...], expand)[0:1]
    lower = lax.broadcasted_iota(jnp.int32, (half, half), 0) >= lax.broadcasted_iota(
        jnp.int32, (half, half), 1
    )
    lane = lax.broadcasted_iota(jnp.int32, (BLOCK, LANES), 1)
    for block in range(PAIR):
        base = block * BLOCK
        for tile in range(width // LANES):
            columns = slice(tile * LANES, (tile + 1) * LANES)
            x = x_ref[base : base + BLOCK, columns]
            top = skip[:, columns] * x[:half].astype(F32)
            bottom = skip[:, columns] * x[half:].astype(F32)
            for side in range(LANES // HEAD_DIM):
                head = first_head + tile * (LANES // HEAD_DIM) + side
                own = jnp.where(lane // HEAD_DIM == side, x, jnp.zeros_like(x))
                cum = cum_ref[base : base + BLOCK, head : head + 1]
                row = row_ref[head : head + 1, base : base + BLOCK]
                diag = jnp.where(lower, cum[:half] - row[:, :half], -1e30)
                mixing = jnp.exp2(diag) * score_ref[base : base + half, :half]
                top = top + dot(mixing.astype(BF16), own[:half])
                left = jnp.exp2(cum[half:] - row[:, :half]) * score_ref[base + half : base + BLOCK, :half]
                diag = jnp.where(lower, cum[half:] - row[:, half:], -1e30)
                right = jnp.exp2(diag) * score_ref[base + half : base + BLOCK, half:]
                mixing = jnp.concatenate([left.astype(BF16), right.astype(BF16)], 1)
                bottom = bottom + dot(mixing, own)
            put(block, slice(base, base + half), columns, top)
            put(block, slice(base + half, base + BLOCK), columns, bottom)


def local_kernel(first_head, x_ref, cum_ref, row_ref, score_ref, skip_ref, *refs):
    out_ref = refs[-1]

    def put(block, rows, columns, value):
        out_ref[rows, columns] = value

    mix(first_head, x_ref, cum_ref, row_ref, score_ref, skip_ref, put)


def carry(first_head, place, lasts, befores, own_ref, c_ref, factor_ref, add, keep_ref, send_ref):
    expand = spread(first_head, own_ref.shape[1], 2)
    last, before = (
        refs[0][...] if len(refs) == 1 else jnp.concatenate([ref[...] for ref in refs], 1)
        for refs in (lasts, befores)
    )
    odd, core = place[1] % 2 == 1, place[2]
    near = jnp.where(odd, last[:STATE].astype(F32), 0.0)
    held = near + jnp.where(odd, decay_of(last), 1.0) * before[:STATE].astype(F32)
    factor = dot(factor_ref[...], expand)
    outs = []
    for block in range(PAIR):
        at = slice(block * BLOCK, (block + 1) * BLOCK)
        carried = dot(c_ref[at], held.astype(BF16))
        outs.append((add[at] + factor[at] * carried).astype(BF16))
        held = factor[BLOCK - 1 : BLOCK] * held + own_ref[...]

    @pl.when(core == 0)
    def _():
        keep_ref[...] = outs[0]
        send_ref[...] = outs[1]

    @pl.when(core == 1)
    def _():
        keep_ref[...] = outs[1]
        send_ref[...] = outs[0]


def final_kernel(first_head, counts, place, *refs):
    groups = []
    for number in counts:
        groups.append(refs[:number])
        refs = refs[number:]
    carry(first_head, place, *groups, *refs[:4], *refs[-2:])


def finish_kernel(first_head, counts, place, *refs):
    groups = []
    for number in counts:
        groups.append(refs[:number])
        refs = refs[number:]
    own_ref, c_ref, factor_ref = refs[:3]
    keep_ref, send_ref, partial = refs[-3:]
    local_kernel(first_head, *refs[3:8], partial)
    carry(first_head, place, *groups, own_ref, c_ref, factor_ref, partial, keep_ref, send_ref)


def place_kernel(firsts, place, *refs):
    count = len(firsts)
    keeps, gots = refs[:count], refs[count : 2 * count]
    out, sems = refs[-2:]
    core = place[2]
    half = out.shape[1] // PAIR
    copies = []
    for first, keep, got in zip(firsts, keeps, gots):
        width = keep.shape[1]
        copies.append((keep, out.at[:, ds(core * half + first, width)]))
        copies.append((got, out.at[:, ds((1 - core) * half + first, width)]))
    for copy in run(copies, sems):
        copy.wait()


def put_in_place(firsts, shape, place, keeps, gots):
    smem, vmem, hbm = (pl.BlockSpec(memory_space=m) for m in (pltpu.SMEM, pltpu.VMEM, pltpu.HBM))
    count = len(firsts)
    return pl.pallas_call(
        functools.partial(place_kernel, firsts),
        out_shape=jax.ShapeDtypeStruct(shape, BF16),
        in_specs=[smem] + [vmem] * (2 * count),
        out_specs=hbm,
        scratch_shapes=[pltpu.SemaphoreType.DMA((2 * count,))],
        compiler_params=pltpu.CompilerParams(vmem_limit_bytes=16 << 20),
        cost_estimate=pl.CostEstimate(flops=1, bytes_accessed=1, transcendentals=0),
        name="place",
    )(place, *keeps, *gots)


class Stay:
    def __init__(self, array):
        self.array = array


def gate(blocks, order):
    anywhere = pl.BlockSpec(memory_space=pl.ANY)
    return pl.pallas_call(
        lambda *refs: None,
        out_shape=[jax.ShapeDtypeStruct(block.shape, block.dtype) for block in blocks],
        in_specs=[anywhere] * (len(blocks) + len(order)),
        out_specs=[anywhere] * len(blocks),
        input_output_aliases={i: i for i in range(len(blocks))},
        compiler_params=pltpu.CompilerParams(vmem_limit_bytes=16 << 20),
        cost_estimate=pl.CostEstimate(flops=1, bytes_accessed=1, transcendentals=0),
        name="gate",
    )(*blocks, *order)


def call(body, outs, operands, scratch=(), flops=0, transcendentals=0, name=None, limit=16 << 20):
    shapes = [jax.ShapeDtypeStruct(shape, dtype) for shape, dtype in outs]
    smem, vmem, hbm = (pl.BlockSpec(memory_space=m) for m in (pltpu.SMEM, pltpu.VMEM, pltpu.HBM))
    specs = [
        hbm if isinstance(o, Stay) else smem if o.dtype == jnp.int32 else vmem for o in operands
    ]
    moved = sum(o.size * o.dtype.itemsize for o in shapes) * 2
    return pl.pallas_call(
        body,
        out_shape=shapes,
        in_specs=specs,
        out_specs=[vmem] * len(outs),
        scratch_shapes=scratch,
        compiler_params=pltpu.CompilerParams(vmem_limit_bytes=limit),
        cost_estimate=pl.CostEstimate(flops=1, bytes_accessed=1, transcendentals=0),
        name=name,
    )(*[o.array if isinstance(o, Stay) else o for o in operands])


def paired(xbc, dt_raw, conv_weight, conv_bias, a_log, dt_bias, skip_gain):
    axes = ("ctx", "head")
    shards, length = lax.axis_size("head"), lax.axis_size("ctx")
    devices, peers = shards * length, shards * PAIR
    tok = xbc.shape[0]
    slab = tok * peers
    context, shard = lax.axis_index("ctx"), lax.axis_index("head")
    pair, core = context // PAIR, context % PAIR
    group = shard * PAIR + core
    place = jnp.stack([group, pair, core, core * shards + shard, shard]).astype(jnp.int32)

    def over(block, target):
        route = [(i, target(i)) for i in range(devices)]
        return lax.ppermute(block, axes, [(i, j) for i, j in route if j is not None and j < devices])

    def swap(block):
        return over(block, lambda i: i ^ shards)

    rows = Stay(xbc)
    size = PER_GROUP + 2 * STATE
    (sent,) = call(
        functools.partial(pack_first_kernel, shards),
        [((tok, shards * WIDTHS[0] + size - WIDTHS[0]), BF16)],
        [place, rows],
        scratch=[pltpu.SemaphoreType.DMA((4 * shards,))],
        name="pack_first",
    )
    got_first = swap(sent)
    sent, tail = call(
        functools.partial(pack_kernel, shards),
        [((tok, shards * (size - WIDTHS[0]) + HEADS), BF16), ((16, shards * size), BF16)],
        [place, rows, Stay(dt_raw), Stay(sent)],
        scratch=[pltpu.SemaphoreType.DMA((6 * shards + 1,))],
        name="pack",
    )
    got_rest = swap(sent)
    taps, offset = call(
        taps_kernel,
        [((4, size), F32), ((1, size), F32)],
        [place, Stay(conv_weight), Stay(conv_bias[None]), Stay(got_rest)],
        scratch=[pltpu.SemaphoreType.DMA((6,))],
        name="taps",
    )

    def send_on(plan, order, tail=None, edges=None):
        unused = Stay(got_first)
        parts = [p for _, pieces in plan for p in pieces]
        made = [] if tail is None else [((3, shards * size), BF16)]
        return call(
            functools.partial(merge_kernel, shards, plan, len(order)),
            [((PAIR * tok, sum(map(total_of, pieces))), BF16) for _, pieces in plan] + made,
            [
                place,
                rows,
                Stay(dt_raw) if edges is None else dt_raw,
                got_first if 0 in parts else unused,
                got_rest if any(parts) else unused,
                next((o for o in (tail, edges) if o is not None), unused),
            ]
            + [Stay(o) for o in order],
            scratch=[pltpu.SemaphoreType.DMA((sum(2 + 2 * len(RESTS[p]) for p in parts),))],
            name="merge",
        )

    def travel(blocks):
        return [blocks[0]] + [over(blocks[r], lambda i, r=r: i ^ r) for r in range(1, shards)]

    def plan(piece):
        return [(r, (piece,)) for r in range(shards)]

    *first_blocks, edges = send_on(plan(0), [], tail)
    message = [travel(first_blocks)]
    edges = over(edges, lambda i: i + peers if i % shards == shards - 1 else None)
    second_blocks = send_on(plan(1), [first_blocks[0]], None, edges)
    message.append(travel(second_blocks))
    third_blocks = send_on(plan(2), [second_blocks[0]])
    message.append(travel(third_blocks[:1] + gate(third_blocks[1:], message[0][1:] + message[1][1:])))

    def seen(piece):
        return message[piece]

    tiles = [p.reshape(HEADS // LANES, LANES) for p in (a_log, dt_bias, skip_gain)]
    b, edge, cum, row, factor, tail, skip = call(
        functools.partial(prep_kernel, shards),
        [
            ((slab, STATE), BF16),
            ((4, size), F32),
            ((slab, LANES), F32),
            ((LANES, slab), F32),
            ((slab, 2 * LANES), BF16),
            ((slab, 2 * LANES), BF16),
            ((16, 3 * LANES), BF16),
        ],
        [place] + seen(1) + [taps, offset] + tiles + [Stay(third_blocks[0])],
        scratch=[pltpu.VMEM((slab, LANES), F32), pltpu.VMEM((slab + 8, STATE), F32)],
        name="prep",
    )
    count = len(GROUPED)
    x, sent, own, last, joined, before, keep, send = ([None] * count for _ in range(8))

    def first_head(i):
        return (sum(WIDTHS[: GROUPED[i][0]]) + GROUPED[i][1]) // HEAD_DIM

    def state_of(i, order):
        piece, _, width = GROUPED[i]
        x[i], own[i], *sent[i] = call(
            functools.partial(state_kernel, shards, GROUPED[i], FIRST_ROUND[i]),
            [((slab, width), BF16), ((STATE, width), F32)] + [((STATE + 16, w), BF16) for w in FIRST_ROUND[i]],
            [place] + seen(piece) + [taps, offset, edge, b, factor, tail] + [Stay(o) for o in order],
            scratch=[pltpu.VMEM((slab + 8, width), F32)],
            name="state",
        )
        last[i] = [over(part, lambda i: i ^ peers if i // peers != 3 else None) for part in sent[i]]

    def combine_of(i, order):
        joined[i], before[i] = [], []
        step = len(FIRST_ROUND[i]) // len(SECOND_ROUND[i])
        for j, width in enumerate(SECOND_ROUND[i]):
            early, late = last[i][j * step : (j + 1) * step], sent[i][j * step : (j + 1) * step]
            (total,) = call(
                functools.partial(combine_kernel, len(early)),
                [((STATE + 16, width), BF16)],
                [place] + early + late + [Stay(o) for o in order],
                name="combine",
            )
            joined[i].append(total)
            before[i].append(over(total, lambda i: i + 2 * peers))
            order = [total]

    def finish_of(body, i, operands, order, **more):
        keep[i], send[i] = call(
            functools.partial(body, first_head(i), (len(last[i]), len(before[i]))),
            [((BLOCK, GROUPED[i][2]), BF16)] * 2,
            [place, *last[i], *before[i], own[i], c, factor] + operands + [Stay(o) for o in order],
            name="final",
            **more,
        )

    state_of(0, [])
    combine_of(0, [])
    fourth_blocks = send_on(plan(3), sent[0])
    message.append(travel(fourth_blocks))
    state_of(1, [fourth_blocks[0], joined[0][0]])
    combine_of(1, [])
    state_of(2, joined[1])
    state_of(3, sent[2])
    c, score = call(
        functools.partial(score_kernel, shards),
        [((slab, STATE), BF16), ((slab, BLOCK), F32)],
        [place] + seen(3) + [taps, offset, edge, b] + [Stay(o) for o in sent[3] + before[1]],
        scratch=[pltpu.VMEM((slab + 8, STATE), F32)],
        name="score",
    )
    mixes = [cum, row, score, skip]

    def in_full(i, order):
        wide = [pltpu.VMEM((slab, GROUPED[i][2]), F32)]
        finish_of(finish_kernel, i, [x[i]] + mixes, order, scratch=wide)

    combine_of(2, [score])
    in_full(1, joined[2])
    combine_of(3, [keep[1]])
    order, partial = joined[3][0], {}
    for i in (2, 3):
        (partial[i],) = call(
            functools.partial(local_kernel, first_head(i)),
            [(x[i].shape, F32)],
            [x[i]] + mixes + [Stay(order)],
            name="local",
        )
        order = partial[i]
    in_full(0, [order])
    order = keep[0]
    for i in (2, 3):
        finish_of(final_kernel, i, [partial[i]], [order])
        order = keep[i]
    firsts = [first_head(i) * HEAD_DIM for i in range(count)]
    return put_in_place(firsts, (BLOCK, PAIR * PER_GROUP), place, keep, [swap(o) for o in send])


def solution(mesh):
    in_specs = (P(("ctx", "head"), None), P(("ctx", "head"), None), P(), P(), P(), P(), P())
    out_specs = P("ctx", "head")
    shards, length = mesh.shape["head"], mesh.shape["ctx"]

    def program(xbc, *rest):
        slab = xbc.shape[0] // length
        fits = shards == GROUPS // PAIR and length == 4 * PAIR and slab == BLOCK
        return jax.shard_map(
            paired if fits else on_device,
            mesh=mesh,
            in_specs=in_specs,
            out_specs=out_specs,
            check_vma=False,
        )(xbc, *rest)

    return program
```

```python
import functools

import jax
import jax.numpy as jnp
from jax import lax
from jax.experimental import pallas as pl
from jax.experimental.pallas import tpu as pltpu
from jax.sharding import PartitionSpec as P

HEADS = 256
HEAD_DIM = 64
STATE = 256
GROUPS = 8
BLOCK = 256


def from_behind(block, axis, distance):
    devices = range(lax.axis_size(axis))
    route = [(i - distance, i) for i in devices if i - distance in devices]
    return lax.ppermute(block, axis, route)


def carried_in(array, axis, combine, identity):
    length, index = (lax.axis_size(axis), lax.axis_index(axis))
    everything = jax.tree.map(lambda part: lax.all_gather(part, axis), array)
    start = jax.tree.map(
        lambda part, zero: jnp.broadcast_to(jnp.asarray(zero, part.dtype), part.shape),
        array,
        identity,
    )

    def hop(k, before):
        reached = k < index
        new = combine(before, jax.tree.map(lambda part: part[k], everything))
        return jax.tree.map(lambda a, b: jnp.where(reached, a, b), new, before)

    return lax.fori_loop(0, length, hop, start)


def convolve(rows, edge, weight, bias):
    count = rows.shape[0]
    wide = jnp.concatenate([edge, rows], 0).astype(jnp.float32)
    acc = bias[None, :] + weight[0] * wide[0:count]
    acc = acc + weight[1] * wide[1 : count + 1]
    acc = acc + weight[2] * wide[2 : count + 2]
    acc = acc + weight[3] * wide[3 : count + 3]
    return jax.nn.silu(acc).astype(jnp.bfloat16)


def rearrange_heads(rows, shards, per_dev, groups_dev, per_group):
    count = rows.shape[0]
    inner = HEADS * HEAD_DIM
    replicate_groups = max(1, per_group // per_dev)
    heads_part = rows[:, :inner].reshape(count, shards, per_dev * HEAD_DIM)
    b_part = rows[:, inner : inner + GROUPS * STATE].reshape(count, GROUPS, STATE)
    c_part = rows[:, inner + GROUPS * STATE :].reshape(count, GROUPS, STATE)
    b_part = jnp.repeat(b_part, replicate_groups, axis=1).reshape(count, shards, groups_dev * STATE)
    c_part = jnp.repeat(c_part, replicate_groups, axis=1).reshape(count, shards, groups_dev * STATE)
    return jnp.concatenate([heads_part, b_part, c_part], axis=2)


def inner_block(xs, bmat, cmat, steps, cum):
    size = xs.shape[0]
    lower = jnp.arange(size)[:, None] >= jnp.arange(size)[None, :]
    scores = jnp.einsum("qgn,kgn->gqk", cmat, bmat, preferred_element_type=jnp.float32)
    order = jnp.transpose(cum, (1, 2, 0))
    gap = order[..., :, None] - order[..., None, :]
    decay = jnp.exp(jnp.where(lower, gap, -jnp.inf))
    mixing = (scores[:, None] * decay * jnp.transpose(steps, (1, 2, 0))[..., None, :]).astype(
        jnp.bfloat16
    )
    local = jnp.einsum("gjqk,kgjp->qgjp", mixing, xs, preferred_element_type=jnp.float32)
    tail = jnp.exp(cum[size - 1][None] - cum) * steps
    loaded = (bmat[:, :, None, :].astype(jnp.float32) * tail[..., None]).astype(jnp.bfloat16)
    block_state = jnp.einsum("kgjn,kgjp->gjnp", loaded, xs, preferred_element_type=jnp.float32)
    return (local, block_state)


def on_device(xbc, dt_raw, conv_weight, conv_bias, a_log, dt_bias, skip_gain):
    tok = xbc.shape[0]
    shards = lax.axis_size("head")
    per_dev = HEADS // shards
    per_group = HEADS // GROUPS
    groups_dev = max(1, per_dev // per_group)
    heads_per_cluster = per_dev // groups_dev
    sent = rearrange_heads(xbc, shards, per_dev, groups_dev, per_group)
    mine, rates = (
        lax.all_to_all(sent, "head", split_axis=1, concat_axis=0, tiled=True),
        lax.all_to_all(
            dt_raw.reshape(tok, shards, per_dev), "head", split_axis=1, concat_axis=0, tiled=True
        ),
    )
    slab = tok * shards
    mine = mine.reshape(slab, mine.shape[2])
    rates = rates.reshape(slab, per_dev)
    shard = lax.axis_index("head")
    taps = lax.dynamic_index_in_dim(
        rearrange_heads(conv_weight, shards, per_dev, groups_dev, per_group),
        shard,
        1,
        keepdims=False,
    )
    offset = lax.dynamic_index_in_dim(
        rearrange_heads(conv_bias[None, :], shards, per_dev, groups_dev, per_group),
        shard,
        1,
        keepdims=False,
    )
    edge = from_behind(mine[slab - 3 :], "ctx", 1)
    mine = convolve(mine, edge, taps, offset[0])
    nchunk = slab // BLOCK
    width = per_dev * HEAD_DIM
    xs = mine[:, :width].reshape(nchunk, BLOCK, groups_dev, heads_per_cluster, HEAD_DIM)
    bmat = mine[:, width : width + groups_dev * STATE].reshape(nchunk, BLOCK, groups_dev, STATE)
    cmat = mine[:, width + groups_dev * STATE :].reshape(nchunk, BLOCK, groups_dev, STATE)
    first = shard * per_dev
    rate = (-jnp.exp(lax.dynamic_slice_in_dim(a_log, first, per_dev))).reshape(
        groups_dev, heads_per_cluster
    )
    bias_dt = lax.dynamic_slice_in_dim(dt_bias, first, per_dev).reshape(
        groups_dev, heads_per_cluster
    )
    skip = lax.dynamic_slice_in_dim(skip_gain, first, per_dev).reshape(
        groups_dev, heads_per_cluster
    )
    steps = jax.nn.softplus(
        rates.astype(jnp.float32).reshape(nchunk, BLOCK, groups_dev, heads_per_cluster) + bias_dt
    )
    cum = jnp.cumsum(steps * rate, axis=1)

    def block_step(carry, item):
        held, product = carry
        x_part, b_part, c_part, step_part, cum_part = item
        local, block_state = inner_block(x_part, b_part, c_part, step_part, cum_part)
        lifted = c_part.astype(jnp.float32)[:, :, None, :] * jnp.exp(cum_part)[..., None]
        carried = jnp.einsum("qgjn,gjnp->qgjp", lifted, held, precision=lax.Precision.HIGHEST)
        partial_out = local + carried + skip[..., None] * x_part.astype(jnp.float32)
        end = jnp.exp(cum_part[BLOCK - 1])
        return ((end[..., None, None] * held + block_state, product * end), (partial_out, product))

    zero_state = jnp.zeros((groups_dev, heads_per_cluster, STATE, HEAD_DIM), jnp.float32)
    unit = jnp.ones((groups_dev, heads_per_cluster), jnp.float32)
    (slab_state, slab_decay), (partials, product_in) = lax.scan(
        block_step, (zero_state, unit), (xs, bmat, cmat, steps, cum)
    )

    def combine(preceding_state, later):
        return (
            preceding_state[0] * later[0],
            later[0][..., None, None] * preceding_state[1] + later[1],
        )

    _, entering = carried_in((slab_decay, slab_state), "ctx", combine, (unit, zero_state))
    projected = jnp.einsum(
        "cqgn,gjnp->cqgjp", cmat.astype(jnp.float32), entering, precision=lax.Precision.HIGHEST
    )
    factor = jnp.exp(cum) * product_in[:, None]
    total = partials + factor[..., None] * projected
    return total.astype(jnp.bfloat16).reshape(slab, width)


PAIR = 2
LANES = 128
LOG2E = 1.4426950408889634
F32, BF16 = jnp.float32, jnp.bfloat16
WIDTHS = (512, 0, 768, 768)
RESTS = ("", "BD", "", "C")
GROUPED = ((0, 0, 512), (2, 0, 768), (3, 0, 384), (3, 384, 384))
FIRST_ROUND = ((256, 256), (384, 384), (384,), (384,))
SECOND_ROUND = ((512,), (384, 384), (384,), (384,))


def halves(value, count):
    parts = []
    for _ in range(count):
        part = value.astype(BF16)
        parts.append(part)
        value = value - part.astype(F32)
    return parts


def spread(first_head, width, copies):
    lane = lax.broadcasted_iota(jnp.int32, (copies * LANES, width), 0) % LANES
    column = lax.broadcasted_iota(jnp.int32, (copies * LANES, width), 1)
    return (lane == first_head + column // HEAD_DIM).astype(BF16)


def dot(a, b):
    return jnp.dot(a, b, preferred_element_type=F32)


def ds(start, width):
    return pl.ds(pl.multiple_of(start, LANES), width)


def run(copies, sems):
    started = []
    for i, (source, target) in enumerate(copies):
        copy = pltpu.make_async_copy(source, target, sems.at[i])
        copy.start()
        started.append(copy)
    return started


PER_GROUP = HEADS * HEAD_DIM // GROUPS
INNER = HEADS * HEAD_DIM


def channels(group, first, width):
    return ds(group * PER_GROUP + first, width)


def pack_first_kernel(shards, place, xbc, send, sems):
    core, shard = place[2], place[4]
    count = xbc.shape[0]
    width = WIDTHS[0]
    copies = []
    for r in range(shards):
        group = (shard ^ r) * PAIR + 1 - core
        copies.append((xbc.at[:, channels(group, 0, width)], send.at[:, r * width : (r + 1) * width]))
        last, rows = xbc.at[count - 16 :], slice(16 * r, 16 * r + 16)
        to = shards * width
        copies.append((last.at[:, channels(group, width, PER_GROUP - width)], send.at[rows, to : to + PER_GROUP - width]))
        to += PER_GROUP - width
        for i in range(2):
            at = ds(INNER + (i * GROUPS + group) * STATE, STATE)
            copies.append((last.at[:, at], send.at[rows, to + i * STATE : to + (i + 1) * STATE]))
    for copy in run(copies, sems):
        copy.wait()


def pack_kernel(shards, place, xbc, dt_raw, order, send, tail, sems):
    core, shard = place[2], place[4]
    count = xbc.shape[0]
    first = WIDTHS[0]
    width = PER_GROUP - first
    rest = width * shards
    size = PER_GROUP + 2 * STATE
    copies = []
    for r in range(shards):
        group = (shard ^ r) * PAIR + 1 - core
        copies.append((xbc.at[:, channels(group, first, width)], send.at[:, r * width : (r + 1) * width]))
        for i in range(2):
            to = rest + (i * shards + r) * STATE
            copies.append((xbc.at[:, ds(INNER + (i * GROUPS + group) * STATE, STATE)], send.at[:, to : to + STATE]))
    copies.append((dt_raw, send.at[:, send.shape[1] - HEADS :]))
    for r in range(shards):
        group, to = (shard ^ r) * PAIR + core, r * size
        last = xbc.at[count - 16 :]
        copies.append((last.at[:, channels(group, 0, PER_GROUP)], tail.at[:, to : to + PER_GROUP]))
        for i in range(2):
            at = ds(INNER + (i * GROUPS + group) * STATE, STATE)
            start = to + PER_GROUP + i * STATE
            copies.append((last.at[:, at], tail.at[:, start : start + STATE]))
    for copy in run(copies, sems):
        copy.wait()


def taps_kernel(place, weight, bias, order, taps, offset, sems):
    copies = []
    for source, target in ((weight, taps), (bias, offset)):
        copies.append((source.at[:, channels(place[0], 0, PER_GROUP)], target.at[:, :PER_GROUP]))
        for i in range(2):
            at = ds(INNER + (i * GROUPS + place[0]) * STATE, STATE)
            start = PER_GROUP + i * STATE
            copies.append((source.at[:, at], target.at[:, start : start + STATE]))
    for copy in run(copies, sems):
        copy.wait()


def put_edge(shards, place, got, tail, out):
    count = got.shape[0]
    first = WIDTHS[0]
    size = PER_GROUP + 2 * STATE
    for r in range(shards):
        theirs = [got[count - 16 :, r * first : (r + 1) * first]]
        theirs.append(got[16 * r : 16 * r + 16, shards * first :])
        to = r * size
        for part in theirs:
            at = slice(to, to + part.shape[1])
            rows = jnp.where(place[2] == 0, part.astype(F32), tail[:, at].astype(F32))
            out[:, at] = rows[13:16].astype(BF16)
            to = at.stop


def total_of(piece):
    return WIDTHS[piece] + sum(LANES if kind == "D" else STATE for kind in RESTS[piece])


def merge_kernel(shards, plan, unread, place, xbc, dt_raw, got_first, got, edges, *refs):
    refs = refs[unread:]
    outs, sems = refs[: len(plan)], refs[-1]
    core, shard = place[2], place[4]
    count = xbc.shape[0]
    stride = PER_GROUP - WIDTHS[0]
    mine = pl.ds(pl.multiple_of(core * count, count), count)
    other = pl.ds(pl.multiple_of((1 - core) * count, count), count)
    copies, steps = [], []
    for out, (r, pieces) in zip(outs, plan):
        group = (shard ^ r) * PAIR + core
        to = 0
        for piece in pieces:
            first, width = sum(WIDTHS[:piece]), WIDTHS[piece]
            if piece == 0:
                source = got_first.at[:, r * width : (r + 1) * width]
            else:
                at = r * stride + first - WIDTHS[0]
                source = got.at[:, at : at + width]
            if width:
                copies.append((xbc.at[:, channels(group, first, width)], out.at[mine, to : to + width]))
                copies.append((source, out.at[other, to : to + width]))
            to += width
            for kind in RESTS[piece]:
                if kind == "D":
                    steps.append((out, r, to))
                    to += LANES
                    continue
                i = "BC".index(kind)
                at = ds(INNER + (i * GROUPS + group) * STATE, STATE)
                copies.append((xbc.at[:, at], out.at[mine, to : to + STATE]))
                at = stride * shards + (i * shards + r) * STATE
                copies.append((got.at[:, at : at + STATE], out.at[other, to : to + STATE]))
                to += STATE
    started = run(copies, sems)
    if len(refs) > len(plan) + 1:
        put_edge(shards, place, got_first, edges, refs[-2])
    if steps:
        lane = lax.broadcasted_iota(jnp.int32, (count, LANES), 1)
        per_tile = LANES * GROUPS // HEADS
        heads = HEADS // GROUPS
        for out, r, to in steps:
            group = (shard ^ r) * PAIR + core
            tile, shift = group // per_tile, (LANES - (group % per_tile) * heads) % LANES
            own = dt_raw[:, ds(tile * LANES, LANES)].astype(F32)
            theirs = got[:, ds(got.shape[1] - HEADS + tile * LANES, LANES)].astype(F32)
            low = jnp.where(core == 0, own, theirs)
            high = jnp.where(core == 0, theirs, own)
            packed = jnp.zeros((count // 2, LANES), F32)
            for j, rows in enumerate((low, high)):
                rows = jnp.where(lane < heads, pltpu.roll(rows, shift, 1), 0.0)
                for i in range(2):
                    part = rows[i * count // 2 : (i + 1) * count // 2]
                    packed = packed + pltpu.roll(part, (2 * j + i) * heads, 1)
            out[: count // 2, to : to + LANES] = packed.astype(BF16)
            size = PER_GROUP + 2 * STATE
            at = slice(r * size, (r + 1) * size)
            edge = jnp.concatenate([edges[:, at].astype(F32), jnp.zeros((1, size), F32)], 0)
            edge = jnp.concatenate([edge[:, q * LANES : (q + 1) * LANES] for q in range(size // LANES)], 0)
            fill = jnp.zeros((PAIR * count - count // 2 - edge.shape[0], LANES), F32)
            out[count // 2 :, to : to + LANES] = jnp.concatenate([edge, fill], 0).astype(BF16)
    for copy in started:
        copy.wait()


def view(refs, piece):
    return [(ref, 0) for ref in refs]


def convolve_in_order(place, blocks, columns, edge, tap, bias, wide, put):
    width = columns.stop - columns.start
    count = blocks[0][0].shape[0] // PAIR
    wide[5:8, :width] = edge
    for r, (block, origin) in enumerate(blocks):
        for core in range(PAIR):
            at = pl.multiple_of((core * len(blocks) + (place[4] ^ r)) * count + 8, 8)
            part = block[core * count : (core + 1) * count, origin + columns.start : origin + columns.stop]
            wide[pl.ds(at, count), :width] = part.astype(F32)
    tap, bias = tap * 0.5, bias * 0.5
    for start in range(0, PAIR * len(blocks) * count, count):
        acc = bias + tap[0:1] * wide[start + 5 : start + 5 + count, :width]
        acc = acc + tap[1:2] * wide[start + 6 : start + 6 + count, :width]
        acc = acc + tap[2:3] * wide[start + 7 : start + 7 + count, :width]
        acc = acc + tap[3:4] * wide[start + 8 : start + 8 + count, :width]
        put(start, count, (acc + acc * jnp.tanh(acc)).astype(BF16))


def prep_kernel(shards, place, *refs):
    blocks, (taps, offset, a_ref, bias_ref, skip_ref, order) = refs[:shards], refs[shards : shards + 6]
    b_ref, edge_ref, cum_ref, row_ref, factor_ref, tail_ref, skip_out, dt_ref, wide = refs[shards + 6 :]
    blocks = view(blocks, 1)
    start = WIDTHS[1]
    last = total_of(1) - LANES
    size = edge_ref.shape[1]
    count = blocks[0][0].shape[0] // PAIR
    half, heads = count // 2, HEADS // GROUPS
    columns = [block[:, origin + last : origin + last + LANES].astype(F32) for block, origin in blocks]
    edge = columns[0][half : half + 4 * size // LANES]
    for column in columns[1:]:
        edge = edge + column[half : half + 4 * size // LANES]
    for q in range(size // LANES):
        edge_ref[:, q * LANES : (q + 1) * LANES] = edge[4 * q : 4 * q + 4]
    for r, column in enumerate(columns):
        packed = column[:half]
        for j in range(2 * PAIR):
            at = ((j // 2) * shards + (place[4] ^ r)) * count + (j % 2) * half
            rows = packed if j == 0 else pltpu.roll(packed, LANES - j * heads, 1)
            dt_ref[pl.ds(pl.multiple_of(at, half), half), :] = rows

    def put(start, count, value):
        b_ref[start : start + count] = value

    at = slice(PER_GROUP, PER_GROUP + STATE)
    convolve_in_order(
        place, blocks, slice(start, start + STATE), edge_ref[0:3, at], taps[:, at], offset[:, at], wide, put
    )
    per_tile = LANES * GROUPS // HEADS
    group = place[0]
    tile = group // per_tile
    shift = (LANES - (group % per_tile) * heads) % LANES

    def lanes_of(ref):
        return pltpu.roll(jnp.broadcast_to(ref[pl.ds(tile, 1), :], (8, LANES)), shift, 1)

    rate = -jnp.exp(lanes_of(a_ref)[0:1])
    raw = dt_ref[...] + lanes_of(bias_ref)[0:1]
    step = jnp.maximum(raw, 0.0) + jnp.log1p(jnp.exp(-jnp.abs(raw)))
    skip = lanes_of(skip_ref)
    skip_out[...] = jnp.concatenate(halves(jnp.concatenate([skip, skip], 0), 3), 1)
    lower = (
        lax.broadcasted_iota(jnp.int32, (BLOCK, BLOCK), 0)
        >= lax.broadcasted_iota(jnp.int32, (BLOCK, BLOCK), 1)
    ).astype(BF16)
    valid = lax.broadcasted_iota(jnp.int32, (BLOCK, LANES), 1) < heads
    for block in range(PAIR):
        at = slice(block * BLOCK, (block + 1) * BLOCK)
        here = jnp.where(valid, step[at], 1.0)
        parts = halves(here * rate, 3)
        cum = dot(lower, parts[0]) + (dot(lower, parts[1]) + dot(lower, parts[2]))
        cum = cum * LOG2E
        cum_ref[at] = cum
        row_ref[:, at] = jnp.transpose(cum - jnp.log2(here))
        factor_ref[at] = jnp.concatenate(halves(jnp.exp2(cum), 2), 1)
        tail = jnp.exp2(cum[BLOCK - 1 :] - cum) * here
        tail_ref[at] = jnp.concatenate(halves(tail, 2), 1)


def score_kernel(shards, place, *refs):
    blocks, refs = refs[:shards], refs[shards:]
    taps, offset, edge_ref, b_ref, c_ref, score_ref, wide = (*refs[:4], *refs[-3:])
    blocks = view(blocks, 3)
    start = WIDTHS[3]
    at = slice(PER_GROUP + STATE, PER_GROUP + 2 * STATE)

    def put(start, count, value):
        c_ref[start : start + count] = value

    convolve_in_order(
        place, blocks, slice(start, start + STATE), edge_ref[0:3, at], taps[:, at], offset[:, at], wide, put
    )
    for block in range(PAIR):
        at = slice(block * BLOCK, (block + 1) * BLOCK)
        score_ref[at] = lax.dot_general(
            c_ref[at], b_ref[at], (((1,), (1,)), ((), ())), preferred_element_type=F32
        )


def decay_of(ref):
    decay = ref[STATE : STATE + 16].astype(F32)
    return decay[0:1] + (decay[1:2] + decay[2:3])


def put_decay(ref, decay):
    row = lax.broadcasted_iota(jnp.int32, (16, ref.shape[1]), 0)
    high, middle, low = (part.astype(F32) for part in halves(decay, 3))
    packed = jnp.where(row == 0, high, jnp.where(row == 1, middle, jnp.where(row == 2, low, 0.0)))
    ref[STATE:] = packed.astype(BF16)


def state_kernel(shards, part, sizes, place, *refs):
    blocks, refs = refs[:shards], refs[shards:]
    taps, offset, edge_ref, b_ref, factor_ref, tail_ref = refs[:6]
    x_ref, own_ref, *sends, wide = refs[-3 - len(sizes) :]
    piece, start, width = part
    first = sum(WIDTHS[:piece]) + start
    at = slice(first, first + width)

    def put(row, count, value):
        x_ref[row : row + count] = value

    blocks = view(blocks, piece)
    columns = slice(start, start + width)
    convolve_in_order(place, blocks, columns, edge_ref[0:3, at], taps[:, at], offset[:, at], wide, put)
    expand = spread(first // HEAD_DIM, width, 2)
    both = []
    for block in range(PAIR):
        at = slice(block * BLOCK, (block + 1) * BLOCK)
        loaded = (x_ref[at].astype(F32) * dot(tail_ref[at], expand)).astype(BF16)
        both.append(
            lax.dot_general(b_ref[at], loaded, (((0,), (0,)), ((), ())), preferred_element_type=F32)
        )
    ends = [dot(factor_ref[(i + 1) * BLOCK - 16 : (i + 1) * BLOCK], expand)[15:16] for i in range(PAIR)]
    own_ref[...] = both[0]
    end = (ends[1] * both[0] + both[1]).astype(BF16)
    decay = ends[0] * ends[1]
    start = 0
    for send_ref in sends:
        at = slice(start, start + send_ref.shape[1])
        send_ref[0:STATE] = end[:, at]
        put_decay(send_ref, decay[:, at])
        start = at.stop


def combine_kernel(count, place, *refs):
    got, own, out_ref = refs[:count], refs[count : 2 * count], refs[-1]
    odd = place[1] % 2 == 1
    start = 0
    for got_ref, own_ref in zip(got, own):
        at = slice(start, start + own_ref.shape[1])
        theirs, mine = got_ref[:STATE].astype(F32), own_ref[:STATE].astype(F32)
        decay, other = decay_of(own_ref), decay_of(got_ref)
        early, late = jnp.where(odd, theirs, mine), jnp.where(odd, mine, theirs)
        out_ref[:STATE, at] = (jnp.where(odd, decay, other) * early + late).astype(BF16)
        put_decay(out_ref.at[:, at], decay * other)
        start = at.stop


def mix(first_head, x_ref, cum_ref, row_ref, score_ref, skip_ref, put):
    width = x_ref.shape[1]
    half = BLOCK // 2
    expand = spread(first_head, width, 3)
    skip = dot(skip_ref[...], expand)[0:1]
    lower = lax.broadcasted_iota(jnp.int32, (half, half), 0) >= lax.broadcasted_iota(
        jnp.int32, (half, half), 1
    )
    lane = lax.broadcasted_iota(jnp.int32, (BLOCK, LANES), 1)
    for block in range(PAIR):
        base = block * BLOCK
        for tile in range(width // LANES):
            columns = slice(tile * LANES, (tile + 1) * LANES)
            x = x_ref[base : base + BLOCK, columns]
            top = skip[:, columns] * x[:half].astype(F32)
            bottom = skip[:, columns] * x[half:].astype(F32)
            for side in range(LANES // HEAD_DIM):
                head = first_head + tile * (LANES // HEAD_DIM) + side
                own = jnp.where(lane // HEAD_DIM == side, x, jnp.zeros_like(x))
                cum = cum_ref[base : base + BLOCK, head : head + 1]
                row = row_ref[head : head + 1, base : base + BLOCK]
                diag = jnp.where(lower, cum[:half] - row[:, :half], -1e30)
                mixing = jnp.exp2(diag) * score_ref[base : base + half, :half]
                top = top + dot(mixing.astype(BF16), own[:half])
                left = jnp.exp2(cum[half:] - row[:, :half]) * score_ref[base + half : base + BLOCK, :half]
                diag = jnp.where(lower, cum[half:] - row[:, half:], -1e30)
                right = jnp.exp2(diag) * score_ref[base + half : base + BLOCK, half:]
                mixing = jnp.concatenate([left.astype(BF16), right.astype(BF16)], 1)
                bottom = bottom + dot(mixing, own)
            put(block, slice(base, base + half), columns, top)
            put(block, slice(base + half, base + BLOCK), columns, bottom)


def local_kernel(first_head, x_ref, cum_ref, row_ref, score_ref, skip_ref, *refs):
    out_ref = refs[-1]

    def put(block, rows, columns, value):
        out_ref[rows, columns] = value

    mix(first_head, x_ref, cum_ref, row_ref, score_ref, skip_ref, put)


def carry(first_head, place, lasts, befores, own_ref, c_ref, factor_ref, add, keep_ref, send_ref):
    expand = spread(first_head, own_ref.shape[1], 2)
    last, before = (
        refs[0][...] if len(refs) == 1 else jnp.concatenate([ref[...] for ref in refs], 1)
        for refs in (lasts, befores)
    )
    odd, core = place[1] % 2 == 1, place[2]
    near = jnp.where(odd, last[:STATE].astype(F32), 0.0)
    held = near + jnp.where(odd, decay_of(last), 1.0) * before[:STATE].astype(F32)
    factor = dot(factor_ref[...], expand)
    outs = []
    for block in range(PAIR):
        at = slice(block * BLOCK, (block + 1) * BLOCK)
        carried = dot(c_ref[at], held.astype(BF16))
        outs.append((add[at] + factor[at] * carried).astype(BF16))
        held = factor[BLOCK - 1 : BLOCK] * held + own_ref[...]

    @pl.when(core == 0)
    def _():
        keep_ref[...] = outs[0]
        send_ref[...] = outs[1]

    @pl.when(core == 1)
    def _():
        keep_ref[...] = outs[1]
        send_ref[...] = outs[0]


def final_kernel(first_head, counts, place, *refs):
    groups = []
    for number in counts:
        groups.append(refs[:number])
        refs = refs[number:]
    carry(first_head, place, *groups, *refs[:4], *refs[-2:])


def finish_kernel(first_head, counts, place, *refs):
    groups = []
    for number in counts:
        groups.append(refs[:number])
        refs = refs[number:]
    own_ref, c_ref, factor_ref = refs[:3]
    keep_ref, send_ref, partial = refs[-3:]
    local_kernel(first_head, *refs[3:8], partial)
    carry(first_head, place, *groups, own_ref, c_ref, factor_ref, partial, keep_ref, send_ref)


def place_kernel(firsts, place, *refs):
    count = len(firsts)
    keeps, gots = refs[:count], refs[count : 2 * count]
    out, sems = refs[-2:]
    core = place[2]
    half = out.shape[1] // PAIR
    copies = []
    for first, keep, got in zip(firsts, keeps, gots):
        width = keep.shape[1]
        copies.append((keep, out.at[:, ds(core * half + first, width)]))
        copies.append((got, out.at[:, ds((1 - core) * half + first, width)]))
    for copy in run(copies, sems):
        copy.wait()


def put_in_place(firsts, shape, place, keeps, gots):
    smem, vmem, hbm = (pl.BlockSpec(memory_space=m) for m in (pltpu.SMEM, pltpu.VMEM, pltpu.HBM))
    count = len(firsts)
    return pl.pallas_call(
        functools.partial(place_kernel, firsts),
        out_shape=jax.ShapeDtypeStruct(shape, BF16),
        in_specs=[smem] + [vmem] * (2 * count),
        out_specs=hbm,
        scratch_shapes=[pltpu.SemaphoreType.DMA((2 * count,))],
        compiler_params=pltpu.CompilerParams(vmem_limit_bytes=16 << 20),
        cost_estimate=pl.CostEstimate(flops=1, bytes_accessed=1, transcendentals=0),
        name="place",
    )(place, *keeps, *gots)


class Stay:
    def __init__(self, array):
        self.array = array


def gate(blocks, order):
    anywhere = pl.BlockSpec(memory_space=pl.ANY)
    return pl.pallas_call(
        lambda *refs: None,
        out_shape=[jax.ShapeDtypeStruct(block.shape, block.dtype) for block in blocks],
        in_specs=[anywhere] * (len(blocks) + len(order)),
        out_specs=[anywhere] * len(blocks),
        input_output_aliases={i: i for i in range(len(blocks))},
        compiler_params=pltpu.CompilerParams(vmem_limit_bytes=16 << 20),
        cost_estimate=pl.CostEstimate(flops=1, bytes_accessed=1, transcendentals=0),
        name="gate",
    )(*blocks, *order)


def call(body, outs, operands, scratch=(), flops=0, transcendentals=0, name=None, limit=16 << 20):
    shapes = [jax.ShapeDtypeStruct(shape, dtype) for shape, dtype in outs]
    smem, vmem, hbm = (pl.BlockSpec(memory_space=m) for m in (pltpu.SMEM, pltpu.VMEM, pltpu.HBM))
    specs = [
        hbm if isinstance(o, Stay) else smem if o.dtype == jnp.int32 else vmem for o in operands
    ]
    moved = sum(o.size * o.dtype.itemsize for o in shapes) * 2
    return pl.pallas_call(
        body,
        out_shape=shapes,
        in_specs=specs,
        out_specs=[vmem] * len(outs),
        scratch_shapes=scratch,
        compiler_params=pltpu.CompilerParams(vmem_limit_bytes=limit),
        cost_estimate=pl.CostEstimate(flops=1, bytes_accessed=1, transcendentals=0),
        name=name,
    )(*[o.array if isinstance(o, Stay) else o for o in operands])


def paired(xbc, dt_raw, conv_weight, conv_bias, a_log, dt_bias, skip_gain):
    axes = ("ctx", "head")
    shards, length = lax.axis_size("head"), lax.axis_size("ctx")
    devices, peers = shards * length, shards * PAIR
    tok = xbc.shape[0]
    slab = tok * peers
    context, shard = lax.axis_index("ctx"), lax.axis_index("head")
    pair, core = context // PAIR, context % PAIR
    group = shard * PAIR + core
    place = jnp.stack([group, pair, core, core * shards + shard, shard]).astype(jnp.int32)

    def over(block, target):
        route = [(i, target(i)) for i in range(devices)]
        return lax.ppermute(block, axes, [(i, j) for i, j in route if j is not None and j < devices])

    def swap(block):
        return over(block, lambda i: i ^ shards)

    rows = Stay(xbc)
    size = PER_GROUP + 2 * STATE
    (sent,) = call(
        functools.partial(pack_first_kernel, shards),
        [((tok, shards * WIDTHS[0] + size - WIDTHS[0]), BF16)],
        [place, rows],
        scratch=[pltpu.SemaphoreType.DMA((4 * shards,))],
        name="pack_first",
    )
    got_first = swap(sent)
    sent, tail = call(
        functools.partial(pack_kernel, shards),
        [((tok, shards * (size - WIDTHS[0]) + HEADS), BF16), ((16, shards * size), BF16)],
        [place, rows, Stay(dt_raw), Stay(sent)],
        scratch=[pltpu.SemaphoreType.DMA((6 * shards + 1,))],
        name="pack",
    )
    got_rest = swap(sent)
    taps, offset = call(
        taps_kernel,
        [((4, size), F32), ((1, size), F32)],
        [place, Stay(conv_weight), Stay(conv_bias[None]), Stay(got_rest)],
        scratch=[pltpu.SemaphoreType.DMA((6,))],
        name="taps",
    )

    def send_on(plan, order, tail=None, edges=None):
        unused = Stay(got_first)
        parts = [p for _, pieces in plan for p in pieces]
        made = [] if tail is None else [((3, shards * size), BF16)]
        return call(
            functools.partial(merge_kernel, shards, plan, len(order)),
            [((PAIR * tok, sum(map(total_of, pieces))), BF16) for _, pieces in plan] + made,
            [
                place,
                rows,
                Stay(dt_raw) if edges is None else dt_raw,
                got_first if 0 in parts else unused,
                got_rest if any(parts) else unused,
                next((o for o in (tail, edges) if o is not None), unused),
            ]
            + [Stay(o) for o in order],
            scratch=[pltpu.SemaphoreType.DMA((sum(2 + 2 * len(RESTS[p]) for p in parts),))],
            name="merge",
        )

    def travel(blocks):
        return [blocks[0]] + [over(blocks[r], lambda i, r=r: i ^ r) for r in range(1, shards)]

    def plan(piece):
        return [(r, (piece,)) for r in range(shards)]

    *first_blocks, edges = send_on(plan(0), [], tail)
    message = [travel(first_blocks)]
    edges = over(edges, lambda i: i + peers if i % shards == shards - 1 else None)
    second_blocks = send_on(plan(1), [first_blocks[0]], None, edges)
    message.append(travel(second_blocks))
    third_blocks = send_on(plan(2), [second_blocks[0]])
    message.append(travel(third_blocks[:1] + gate(third_blocks[1:], message[0][1:] + message[1][1:])))

    def seen(piece):
        return message[piece]

    tiles = [p.reshape(HEADS // LANES, LANES) for p in (a_log, dt_bias, skip_gain)]
    b, edge, cum, row, factor, tail, skip = call(
        functools.partial(prep_kernel, shards),
        [
            ((slab, STATE), BF16),
            ((4, size), F32),
            ((slab, LANES), F32),
            ((LANES, slab), F32),
            ((slab, 2 * LANES), BF16),
            ((slab, 2 * LANES), BF16),
            ((16, 3 * LANES), BF16),
        ],
        [place] + seen(1) + [taps, offset] + tiles + [Stay(third_blocks[0])],
        scratch=[pltpu.VMEM((slab, LANES), F32), pltpu.VMEM((slab + 8, STATE), F32)],
        name="prep",
    )
    count = len(GROUPED)
    x, sent, own, last, joined, before, keep, send = ([None] * count for _ in range(8))

    def first_head(i):
        return (sum(WIDTHS[: GROUPED[i][0]]) + GROUPED[i][1]) // HEAD_DIM

    def state_of(i, order):
        piece, _, width = GROUPED[i]
        x[i], own[i], *sent[i] = call(
            functools.partial(state_kernel, shards, GROUPED[i], FIRST_ROUND[i]),
            [((slab, width), BF16), ((STATE, width), F32)] + [((STATE + 16, w), BF16) for w in FIRST_ROUND[i]],
            [place] + seen(piece) + [taps, offset, edge, b, factor, tail] + [Stay(o) for o in order],
            scratch=[pltpu.VMEM((slab + 8, width), F32)],
            name="state",
        )
        last[i] = [over(part, lambda i: i ^ peers if i // peers != 3 else None) for part in sent[i]]

    def combine_of(i, order):
        joined[i], before[i] = [], []
        step = len(FIRST_ROUND[i]) // len(SECOND_ROUND[i])
        for j, width in enumerate(SECOND_ROUND[i]):
            early, late = last[i][j * step : (j + 1) * step], sent[i][j * step : (j + 1) * step]
            (total,) = call(
                functools.partial(combine_kernel, len(early)),
                [((STATE + 16, width), BF16)],
                [place] + early + late + [Stay(o) for o in order],
                name="combine",
            )
            joined[i].append(total)
            before[i].append(over(total, lambda i: i + 2 * peers))
            order = [total]

    def finish_of(body, i, operands, order, **more):
        keep[i], send[i] = call(
            functools.partial(body, first_head(i), (len(last[i]), len(before[i]))),
            [((BLOCK, GROUPED[i][2]), BF16)] * 2,
            [place, *last[i], *before[i], own[i], c, factor] + operands + [Stay(o) for o in order],
            name="final",
            **more,
        )

    state_of(0, [])
    combine_of(0, [])
    fourth_blocks = send_on(plan(3), sent[0])
    message.append(travel(fourth_blocks[:1] + gate(fourth_blocks[1:], message[2][1:])))
    state_of(1, joined[0])
    combine_of(1, [])
    state_of(2, joined[1])
    state_of(3, sent[2])
    c, score = call(
        functools.partial(score_kernel, shards),
        [((slab, STATE), BF16), ((slab, BLOCK), F32)],
        [place] + seen(3) + [taps, offset, edge, b] + [Stay(o) for o in sent[3] + before[1]],
        scratch=[pltpu.VMEM((slab + 8, STATE), F32)],
        name="score",
    )
    mixes = [cum, row, score, skip]

    def in_full(i, order):
        wide = [pltpu.VMEM((slab, GROUPED[i][2]), F32)]
        finish_of(finish_kernel, i, [x[i]] + mixes, order, scratch=wide)

    combine_of(2, [score])
    in_full(1, joined[2])
    combine_of(3, [keep[1]])
    order, partial = joined[3][0], {}
    for i in (2, 3):
        (partial[i],) = call(
            functools.partial(local_kernel, first_head(i)),
            [(x[i].shape, F32)],
            [x[i]] + mixes + [Stay(order)],
            name="local",
        )
        order = partial[i]
    in_full(0, [order])
    order = keep[0]
    for i in (2, 3):
        finish_of(final_kernel, i, [partial[i]], [order])
        order = keep[i]
    firsts = [first_head(i) * HEAD_DIM for i in range(count)]
    return put_in_place(firsts, (BLOCK, PAIR * PER_GROUP), place, keep, [swap(o) for o in send])


def solution(mesh):
    in_specs = (P(("ctx", "head"), None), P(("ctx", "head"), None), P(), P(), P(), P(), P())
    out_specs = P("ctx", "head")
    shards, length = mesh.shape["head"], mesh.shape["ctx"]

    def program(xbc, *rest):
        slab = xbc.shape[0] // length
        fits = shards == GROUPS // PAIR and length == 4 * PAIR and slab == BLOCK
        return jax.shard_map(
            paired if fits else on_device,
            mesh=mesh,
            in_specs=in_specs,
            out_specs=out_specs,
            check_vma=False,
        )(xbc, *rest)

    return program
```

```python
import functools

import jax
import jax.numpy as jnp
from jax import lax
from jax.experimental import pallas as pl
from jax.experimental.pallas import tpu as pltpu
from jax.sharding import PartitionSpec as P

HEADS = 256
HEAD_DIM = 64
STATE = 256
GROUPS = 8
BLOCK = 256


def from_behind(block, axis, distance):
    devices = range(lax.axis_size(axis))
    route = [(i - distance, i) for i in devices if i - distance in devices]
    return lax.ppermute(block, axis, route)


def carried_in(array, axis, combine, identity):
    length, index = (lax.axis_size(axis), lax.axis_index(axis))
    everything = jax.tree.map(lambda part: lax.all_gather(part, axis), array)
    start = jax.tree.map(
        lambda part, zero: jnp.broadcast_to(jnp.asarray(zero, part.dtype), part.shape),
        array,
        identity,
    )

    def hop(k, before):
        reached = k < index
        new = combine(before, jax.tree.map(lambda part: part[k], everything))
        return jax.tree.map(lambda a, b: jnp.where(reached, a, b), new, before)

    return lax.fori_loop(0, length, hop, start)


def convolve(rows, edge, weight, bias):
    count = rows.shape[0]
    wide = jnp.concatenate([edge, rows], 0).astype(jnp.float32)
    acc = bias[None, :] + weight[0] * wide[0:count]
    acc = acc + weight[1] * wide[1 : count + 1]
    acc = acc + weight[2] * wide[2 : count + 2]
    acc = acc + weight[3] * wide[3 : count + 3]
    return jax.nn.silu(acc).astype(jnp.bfloat16)


def rearrange_heads(rows, shards, per_dev, groups_dev, per_group):
    count = rows.shape[0]
    inner = HEADS * HEAD_DIM
    replicate_groups = max(1, per_group // per_dev)
    heads_part = rows[:, :inner].reshape(count, shards, per_dev * HEAD_DIM)
    b_part = rows[:, inner : inner + GROUPS * STATE].reshape(count, GROUPS, STATE)
    c_part = rows[:, inner + GROUPS * STATE :].reshape(count, GROUPS, STATE)
    b_part = jnp.repeat(b_part, replicate_groups, axis=1).reshape(count, shards, groups_dev * STATE)
    c_part = jnp.repeat(c_part, replicate_groups, axis=1).reshape(count, shards, groups_dev * STATE)
    return jnp.concatenate([heads_part, b_part, c_part], axis=2)


def inner_block(xs, bmat, cmat, steps, cum):
    size = xs.shape[0]
    lower = jnp.arange(size)[:, None] >= jnp.arange(size)[None, :]
    scores = jnp.einsum("qgn,kgn->gqk", cmat, bmat, preferred_element_type=jnp.float32)
    order = jnp.transpose(cum, (1, 2, 0))
    gap = order[..., :, None] - order[..., None, :]
    decay = jnp.exp(jnp.where(lower, gap, -jnp.inf))
    mixing = (scores[:, None] * decay * jnp.transpose(steps, (1, 2, 0))[..., None, :]).astype(
        jnp.bfloat16
    )
    local = jnp.einsum("gjqk,kgjp->qgjp", mixing, xs, preferred_element_type=jnp.float32)
    tail = jnp.exp(cum[size - 1][None] - cum) * steps
    loaded = (bmat[:, :, None, :].astype(jnp.float32) * tail[..., None]).astype(jnp.bfloat16)
    block_state = jnp.einsum("kgjn,kgjp->gjnp", loaded, xs, preferred_element_type=jnp.float32)
    return (local, block_state)


def on_device(xbc, dt_raw, conv_weight, conv_bias, a_log, dt_bias, skip_gain):
    tok = xbc.shape[0]
    shards = lax.axis_size("head")
    per_dev = HEADS // shards
    per_group = HEADS // GROUPS
    groups_dev = max(1, per_dev // per_group)
    heads_per_cluster = per_dev // groups_dev
    sent = rearrange_heads(xbc, shards, per_dev, groups_dev, per_group)
    mine, rates = (
        lax.all_to_all(sent, "head", split_axis=1, concat_axis=0, tiled=True),
        lax.all_to_all(
            dt_raw.reshape(tok, shards, per_dev), "head", split_axis=1, concat_axis=0, tiled=True
        ),
    )
    slab = tok * shards
    mine = mine.reshape(slab, mine.shape[2])
    rates = rates.reshape(slab, per_dev)
    shard = lax.axis_index("head")
    taps = lax.dynamic_index_in_dim(
        rearrange_heads(conv_weight, shards, per_dev, groups_dev, per_group),
        shard,
        1,
        keepdims=False,
    )
    offset = lax.dynamic_index_in_dim(
        rearrange_heads(conv_bias[None, :], shards, per_dev, groups_dev, per_group),
        shard,
        1,
        keepdims=False,
    )
    edge = from_behind(mine[slab - 3 :], "ctx", 1)
    mine = convolve(mine, edge, taps, offset[0])
    nchunk = slab // BLOCK
    width = per_dev * HEAD_DIM
    xs = mine[:, :width].reshape(nchunk, BLOCK, groups_dev, heads_per_cluster, HEAD_DIM)
    bmat = mine[:, width : width + groups_dev * STATE].reshape(nchunk, BLOCK, groups_dev, STATE)
    cmat = mine[:, width + groups_dev * STATE :].reshape(nchunk, BLOCK, groups_dev, STATE)
    first = shard * per_dev
    rate = (-jnp.exp(lax.dynamic_slice_in_dim(a_log, first, per_dev))).reshape(
        groups_dev, heads_per_cluster
    )
    bias_dt = lax.dynamic_slice_in_dim(dt_bias, first, per_dev).reshape(
        groups_dev, heads_per_cluster
    )
    skip = lax.dynamic_slice_in_dim(skip_gain, first, per_dev).reshape(
        groups_dev, heads_per_cluster
    )
    steps = jax.nn.softplus(
        rates.astype(jnp.float32).reshape(nchunk, BLOCK, groups_dev, heads_per_cluster) + bias_dt
    )
    cum = jnp.cumsum(steps * rate, axis=1)

    def block_step(carry, item):
        held, product = carry
        x_part, b_part, c_part, step_part, cum_part = item
        local, block_state = inner_block(x_part, b_part, c_part, step_part, cum_part)
        lifted = c_part.astype(jnp.float32)[:, :, None, :] * jnp.exp(cum_part)[..., None]
        carried = jnp.einsum("qgjn,gjnp->qgjp", lifted, held, precision=lax.Precision.HIGHEST)
        partial_out = local + carried + skip[..., None] * x_part.astype(jnp.float32)
        end = jnp.exp(cum_part[BLOCK - 1])
        return ((end[..., None, None] * held + block_state, product * end), (partial_out, product))

    zero_state = jnp.zeros((groups_dev, heads_per_cluster, STATE, HEAD_DIM), jnp.float32)
    unit = jnp.ones((groups_dev, heads_per_cluster), jnp.float32)
    (slab_state, slab_decay), (partials, product_in) = lax.scan(
        block_step, (zero_state, unit), (xs, bmat, cmat, steps, cum)
    )

    def combine(preceding_state, later):
        return (
            preceding_state[0] * later[0],
            later[0][..., None, None] * preceding_state[1] + later[1],
        )

    _, entering = carried_in((slab_decay, slab_state), "ctx", combine, (unit, zero_state))
    projected = jnp.einsum(
        "cqgn,gjnp->cqgjp", cmat.astype(jnp.float32), entering, precision=lax.Precision.HIGHEST
    )
    factor = jnp.exp(cum) * product_in[:, None]
    total = partials + factor[..., None] * projected
    return total.astype(jnp.bfloat16).reshape(slab, width)


PAIR = 2
LANES = 128
LOG2E = 1.4426950408889634
F32, BF16 = jnp.float32, jnp.bfloat16
WIDTHS = (512, 0, 768, 768)
RESTS = ("", "BD", "C", "")
GROUPED = ((0, 0, 512), (2, 0, 768), (3, 0, 384), (3, 384, 384))
FIRST_ROUND = ((256, 256), (256, 256, 256), (384,), (384,))
SECOND_ROUND = ((512,), (384, 384), (384,), (384,))


def halves(value, count):
    parts = []
    for _ in range(count):
        part = value.astype(BF16)
        parts.append(part)
        value = value - part.astype(F32)
    return parts


def spread(first_head, width, copies):
    lane = lax.broadcasted_iota(jnp.int32, (copies * LANES, width), 0) % LANES
    column = lax.broadcasted_iota(jnp.int32, (copies * LANES, width), 1)
    return (lane == first_head + column // HEAD_DIM).astype(BF16)


def dot(a, b):
    return jnp.dot(a, b, preferred_element_type=F32)


def ds(start, width):
    return pl.ds(pl.multiple_of(start, LANES), width)


def run(copies, sems):
    started = []
    for i, (source, target) in enumerate(copies):
        copy = pltpu.make_async_copy(source, target, sems.at[i])
        copy.start()
        started.append(copy)
    return started


PER_GROUP = HEADS * HEAD_DIM // GROUPS
INNER = HEADS * HEAD_DIM


def channels(group, first, width):
    return ds(group * PER_GROUP + first, width)


def pack_first_kernel(shards, place, xbc, send, sems):
    core, shard = place[2], place[4]
    count = xbc.shape[0]
    width = WIDTHS[0]
    copies = []
    for r in range(shards):
        group = (shard ^ r) * PAIR + 1 - core
        copies.append((xbc.at[:, channels(group, 0, width)], send.at[:, r * width : (r + 1) * width]))
        last, rows = xbc.at[count - 16 :], slice(16 * r, 16 * r + 16)
        to = shards * width
        copies.append((last.at[:, channels(group, width, PER_GROUP - width)], send.at[rows, to : to + PER_GROUP - width]))
        to += PER_GROUP - width
        for i in range(2):
            at = ds(INNER + (i * GROUPS + group) * STATE, STATE)
            copies.append((last.at[:, at], send.at[rows, to + i * STATE : to + (i + 1) * STATE]))
    for copy in run(copies, sems):
        copy.wait()


def pack_kernel(shards, place, xbc, dt_raw, order, send, tail, sems):
    core, shard = place[2], place[4]
    count = xbc.shape[0]
    first = WIDTHS[0]
    width = PER_GROUP - first
    rest = width * shards
    size = PER_GROUP + 2 * STATE
    copies = []
    for r in range(shards):
        group = (shard ^ r) * PAIR + 1 - core
        copies.append((xbc.at[:, channels(group, first, width)], send.at[:, r * width : (r + 1) * width]))
        for i in range(2):
            to = rest + (i * shards + r) * STATE
            copies.append((xbc.at[:, ds(INNER + (i * GROUPS + group) * STATE, STATE)], send.at[:, to : to + STATE]))
    copies.append((dt_raw, send.at[:, send.shape[1] - HEADS :]))
    for r in range(shards):
        group, to = (shard ^ r) * PAIR + core, r * size
        last = xbc.at[count - 16 :]
        copies.append((last.at[:, channels(group, 0, PER_GROUP)], tail.at[:, to : to + PER_GROUP]))
        for i in range(2):
            at = ds(INNER + (i * GROUPS + group) * STATE, STATE)
            start = to + PER_GROUP + i * STATE
            copies.append((last.at[:, at], tail.at[:, start : start + STATE]))
    for copy in run(copies, sems):
        copy.wait()


def taps_kernel(place, weight, bias, order, taps, offset, sems):
    copies = []
    for source, target in ((weight, taps), (bias, offset)):
        copies.append((source.at[:, channels(place[0], 0, PER_GROUP)], target.at[:, :PER_GROUP]))
        for i in range(2):
            at = ds(INNER + (i * GROUPS + place[0]) * STATE, STATE)
            start = PER_GROUP + i * STATE
            copies.append((source.at[:, at], target.at[:, start : start + STATE]))
    for copy in run(copies, sems):
        copy.wait()


def put_edge(shards, place, got, tail, out):
    count = got.shape[0]
    first = WIDTHS[0]
    size = PER_GROUP + 2 * STATE
    for r in range(shards):
        theirs = [got[count - 16 :, r * first : (r + 1) * first]]
        theirs.append(got[16 * r : 16 * r + 16, shards * first :])
        to = r * size
        for part in theirs:
            at = slice(to, to + part.shape[1])
            rows = jnp.where(place[2] == 0, part.astype(F32), tail[:, at].astype(F32))
            out[:, at] = rows[13:16].astype(BF16)
            to = at.stop


def total_of(piece):
    return WIDTHS[piece] + sum(LANES if kind == "D" else STATE for kind in RESTS[piece])


def merge_kernel(shards, plan, unread, place, xbc, dt_raw, got_first, got, edges, *refs):
    refs = refs[unread:]
    outs, sems = refs[: len(plan)], refs[-1]
    core, shard = place[2], place[4]
    count = xbc.shape[0]
    stride = PER_GROUP - WIDTHS[0]
    mine = pl.ds(pl.multiple_of(core * count, count), count)
    other = pl.ds(pl.multiple_of((1 - core) * count, count), count)
    copies, steps = [], []
    for out, (r, pieces) in zip(outs, plan):
        group = (shard ^ r) * PAIR + core
        to = 0
        for piece in pieces:
            first, width = sum(WIDTHS[:piece]), WIDTHS[piece]
            if piece == 0:
                source = got_first.at[:, r * width : (r + 1) * width]
            else:
                at = r * stride + first - WIDTHS[0]
                source = got.at[:, at : at + width]
            if width:
                copies.append((xbc.at[:, channels(group, first, width)], out.at[mine, to : to + width]))
                copies.append((source, out.at[other, to : to + width]))
            to += width
            for kind in RESTS[piece]:
                if kind == "D":
                    steps.append((out, r, to))
                    to += LANES
                    continue
                i = "BC".index(kind)
                at = ds(INNER + (i * GROUPS + group) * STATE, STATE)
                copies.append((xbc.at[:, at], out.at[mine, to : to + STATE]))
                at = stride * shards + (i * shards + r) * STATE
                copies.append((got.at[:, at : at + STATE], out.at[other, to : to + STATE]))
                to += STATE
    started = run(copies, sems)
    if len(refs) > len(plan) + 1:
        put_edge(shards, place, got_first, edges, refs[-2])
    if steps:
        lane = lax.broadcasted_iota(jnp.int32, (count, LANES), 1)
        per_tile = LANES * GROUPS // HEADS
        heads = HEADS // GROUPS
        for out, r, to in steps:
            group = (shard ^ r) * PAIR + core
            tile, shift = group // per_tile, (LANES - (group % per_tile) * heads) % LANES
            own = dt_raw[:, ds(tile * LANES, LANES)].astype(F32)
            theirs = got[:, ds(got.shape[1] - HEADS + tile * LANES, LANES)].astype(F32)
            low = jnp.where(core == 0, own, theirs)
            high = jnp.where(core == 0, theirs, own)
            packed = jnp.zeros((count // 2, LANES), F32)
            for j, rows in enumerate((low, high)):
                rows = jnp.where(lane < heads, pltpu.roll(rows, shift, 1), 0.0)
                for i in range(2):
                    part = rows[i * count // 2 : (i + 1) * count // 2]
                    packed = packed + pltpu.roll(part, (2 * j + i) * heads, 1)
            out[: count // 2, to : to + LANES] = packed.astype(BF16)
            size = PER_GROUP + 2 * STATE
            at = slice(r * size, (r + 1) * size)
            edge = jnp.concatenate([edges[:, at].astype(F32), jnp.zeros((1, size), F32)], 0)
            edge = jnp.concatenate([edge[:, q * LANES : (q + 1) * LANES] for q in range(size // LANES)], 0)
            fill = jnp.zeros((PAIR * count - count // 2 - edge.shape[0], LANES), F32)
            out[count // 2 :, to : to + LANES] = jnp.concatenate([edge, fill], 0).astype(BF16)
    for copy in started:
        copy.wait()


def view(refs, piece):
    return [(ref, total_of(2) if piece == 3 and r == 1 else 0) for r, ref in enumerate(refs)]


def convolve_in_order(place, blocks, columns, edge, tap, bias, wide, put):
    width = columns.stop - columns.start
    count = blocks[0][0].shape[0] // PAIR
    wide[5:8, :width] = edge
    for r, (block, origin) in enumerate(blocks):
        for core in range(PAIR):
            at = pl.multiple_of((core * len(blocks) + (place[4] ^ r)) * count + 8, 8)
            part = block[core * count : (core + 1) * count, origin + columns.start : origin + columns.stop]
            wide[pl.ds(at, count), :width] = part.astype(F32)
    tap, bias = tap * 0.5, bias * 0.5
    for start in range(0, PAIR * len(blocks) * count, count):
        acc = bias + tap[0:1] * wide[start + 5 : start + 5 + count, :width]
        acc = acc + tap[1:2] * wide[start + 6 : start + 6 + count, :width]
        acc = acc + tap[2:3] * wide[start + 7 : start + 7 + count, :width]
        acc = acc + tap[3:4] * wide[start + 8 : start + 8 + count, :width]
        put(start, count, (acc + acc * jnp.tanh(acc)).astype(BF16))


def prep_kernel(shards, place, *refs):
    blocks, (taps, offset, a_ref, bias_ref, skip_ref, order) = refs[:shards], refs[shards : shards + 6]
    b_ref, edge_ref, cum_ref, row_ref, factor_ref, tail_ref, skip_out, dt_ref, wide = refs[shards + 6 :]
    blocks = view(blocks, 1)
    start = WIDTHS[1]
    last = total_of(1) - LANES
    size = edge_ref.shape[1]
    count = blocks[0][0].shape[0] // PAIR
    half, heads = count // 2, HEADS // GROUPS
    columns = [block[:, origin + last : origin + last + LANES].astype(F32) for block, origin in blocks]
    edge = columns[0][half : half + 4 * size // LANES]
    for column in columns[1:]:
        edge = edge + column[half : half + 4 * size // LANES]
    for q in range(size // LANES):
        edge_ref[:, q * LANES : (q + 1) * LANES] = edge[4 * q : 4 * q + 4]
    for r, column in enumerate(columns):
        packed = column[:half]
        for j in range(2 * PAIR):
            at = ((j // 2) * shards + (place[4] ^ r)) * count + (j % 2) * half
            rows = packed if j == 0 else pltpu.roll(packed, LANES - j * heads, 1)
            dt_ref[pl.ds(pl.multiple_of(at, half), half), :] = rows

    def put(start, count, value):
        b_ref[start : start + count] = value

    at = slice(PER_GROUP, PER_GROUP + STATE)
    convolve_in_order(
        place, blocks, slice(start, start + STATE), edge_ref[0:3, at], taps[:, at], offset[:, at], wide, put
    )
    per_tile = LANES * GROUPS // HEADS
    group = place[0]
    tile = group // per_tile
    shift = (LANES - (group % per_tile) * heads) % LANES

    def lanes_of(ref):
        return pltpu.roll(jnp.broadcast_to(ref[pl.ds(tile, 1), :], (8, LANES)), shift, 1)

    rate = -jnp.exp(lanes_of(a_ref)[0:1])
    raw = dt_ref[...] + lanes_of(bias_ref)[0:1]
    step = jnp.maximum(raw, 0.0) + jnp.log1p(jnp.exp(-jnp.abs(raw)))
    skip = lanes_of(skip_ref)
    skip_out[...] = jnp.concatenate(halves(jnp.concatenate([skip, skip], 0), 3), 1)
    lower = (
        lax.broadcasted_iota(jnp.int32, (BLOCK, BLOCK), 0)
        >= lax.broadcasted_iota(jnp.int32, (BLOCK, BLOCK), 1)
    ).astype(BF16)
    valid = lax.broadcasted_iota(jnp.int32, (BLOCK, LANES), 1) < heads
    for block in range(PAIR):
        at = slice(block * BLOCK, (block + 1) * BLOCK)
        here = jnp.where(valid, step[at], 1.0)
        parts = halves(here * rate, 3)
        cum = dot(lower, parts[0]) + (dot(lower, parts[1]) + dot(lower, parts[2]))
        cum = cum * LOG2E
        cum_ref[at] = cum
        row_ref[:, at] = jnp.transpose(cum - jnp.log2(here))
        factor_ref[at] = jnp.concatenate(halves(jnp.exp2(cum), 2), 1)
        tail = jnp.exp2(cum[BLOCK - 1 :] - cum) * here
        tail_ref[at] = jnp.concatenate(halves(tail, 2), 1)


def score_kernel(shards, place, *refs):
    blocks, refs = refs[:shards], refs[shards:]
    taps, offset, edge_ref, b_ref, c_ref, score_ref, wide = (*refs[:4], *refs[-3:])
    blocks = view(blocks, 2)
    start = WIDTHS[2]
    at = slice(PER_GROUP + STATE, PER_GROUP + 2 * STATE)

    def put(start, count, value):
        c_ref[start : start + count] = value

    convolve_in_order(
        place, blocks, slice(start, start + STATE), edge_ref[0:3, at], taps[:, at], offset[:, at], wide, put
    )
    for block in range(PAIR):
        at = slice(block * BLOCK, (block + 1) * BLOCK)
        score_ref[at] = lax.dot_general(
            c_ref[at], b_ref[at], (((1,), (1,)), ((), ())), preferred_element_type=F32
        )


def decay_of(ref):
    decay = ref[STATE : STATE + 16].astype(F32)
    return decay[0:1] + (decay[1:2] + decay[2:3])


def put_decay(ref, decay):
    row = lax.broadcasted_iota(jnp.int32, (16, ref.shape[1]), 0)
    high, middle, low = (part.astype(F32) for part in halves(decay, 3))
    packed = jnp.where(row == 0, high, jnp.where(row == 1, middle, jnp.where(row == 2, low, 0.0)))
    ref[STATE:] = packed.astype(BF16)


def state_kernel(shards, part, sizes, place, *refs):
    blocks, refs = refs[:shards], refs[shards:]
    taps, offset, edge_ref, b_ref, factor_ref, tail_ref = refs[:6]
    x_ref, own_ref, *sends, wide = refs[-3 - len(sizes) :]
    piece, start, width = part
    first = sum(WIDTHS[:piece]) + start
    at = slice(first, first + width)

    def put(row, count, value):
        x_ref[row : row + count] = value

    blocks = view(blocks, piece)
    columns = slice(start, start + width)
    convolve_in_order(place, blocks, columns, edge_ref[0:3, at], taps[:, at], offset[:, at], wide, put)
    expand = spread(first // HEAD_DIM, width, 2)
    both = []
    for block in range(PAIR):
        at = slice(block * BLOCK, (block + 1) * BLOCK)
        loaded = (x_ref[at].astype(F32) * dot(tail_ref[at], expand)).astype(BF16)
        both.append(
            lax.dot_general(b_ref[at], loaded, (((0,), (0,)), ((), ())), preferred_element_type=F32)
        )
    ends = [dot(factor_ref[(i + 1) * BLOCK - 16 : (i + 1) * BLOCK], expand)[15:16] for i in range(PAIR)]
    own_ref[...] = both[0]
    end = (ends[1] * both[0] + both[1]).astype(BF16)
    decay = ends[0] * ends[1]
    start = 0
    for send_ref in sends:
        at = slice(start, start + send_ref.shape[1])
        send_ref[0:STATE] = end[:, at]
        put_decay(send_ref, decay[:, at])
        start = at.stop


def combine_kernel(spans, place, *refs):
    count = len(spans)
    got, own, out_ref = refs[:count], refs[count : 2 * count], refs[-1]
    odd = place[1] % 2 == 1
    start = 0
    for got_ref, own_ref, span in zip(got, own, spans):
        at = slice(start, start + span.stop - span.start)
        theirs, mine = got_ref[:STATE, span].astype(F32), own_ref[:STATE, span].astype(F32)
        decay, other = decay_of(own_ref.at[:, span]), decay_of(got_ref.at[:, span])
        early, late = jnp.where(odd, theirs, mine), jnp.where(odd, mine, theirs)
        out_ref[:STATE, at] = (jnp.where(odd, decay, other) * early + late).astype(BF16)
        put_decay(out_ref.at[:, at], decay * other)
        start = at.stop


def mix(first_head, x_ref, cum_ref, row_ref, score_ref, skip_ref, put):
    width = x_ref.shape[1]
    half = BLOCK // 2
    expand = spread(first_head, width, 3)
    skip = dot(skip_ref[...], expand)[0:1]
    lower = lax.broadcasted_iota(jnp.int32, (half, half), 0) >= lax.broadcasted_iota(
        jnp.int32, (half, half), 1
    )
    lane = lax.broadcasted_iota(jnp.int32, (BLOCK, LANES), 1)
    for block in range(PAIR):
        base = block * BLOCK
        for tile in range(width // LANES):
            columns = slice(tile * LANES, (tile + 1) * LANES)
            x = x_ref[base : base + BLOCK, columns]
            top = skip[:, columns] * x[:half].astype(F32)
            bottom = skip[:, columns] * x[half:].astype(F32)
            for side in range(LANES // HEAD_DIM):
                head = first_head + tile * (LANES // HEAD_DIM) + side
                own = jnp.where(lane // HEAD_DIM == side, x, jnp.zeros_like(x))
                cum = cum_ref[base : base + BLOCK, head : head + 1]
                row = row_ref[head : head + 1, base : base + BLOCK]
                diag = jnp.where(lower, cum[:half] - row[:, :half], -1e30)
                mixing = jnp.exp2(diag) * score_ref[base : base + half, :half]
                top = top + dot(mixing.astype(BF16), own[:half])
                left = jnp.exp2(cum[half:] - row[:, :half]) * score_ref[base + half : base + BLOCK, :half]
                diag = jnp.where(lower, cum[half:] - row[:, half:], -1e30)
                right = jnp.exp2(diag) * score_ref[base + half : base + BLOCK, half:]
                mixing = jnp.concatenate([left.astype(BF16), right.astype(BF16)], 1)
                bottom = bottom + dot(mixing, own)
            put(block, slice(base, base + half), columns, top)
            put(block, slice(base + half, base + BLOCK), columns, bottom)


def local_kernel(first_head, x_ref, cum_ref, row_ref, score_ref, skip_ref, *refs):
    out_ref = refs[-1]

    def put(block, rows, columns, value):
        out_ref[rows, columns] = value

    mix(first_head, x_ref, cum_ref, row_ref, score_ref, skip_ref, put)


def carry(first_head, place, lasts, befores, own_ref, c_ref, factor_ref, add, keep_ref, send_ref):
    expand = spread(first_head, own_ref.shape[1], 2)
    last, before = (
        refs[0][...] if len(refs) == 1 else jnp.concatenate([ref[...] for ref in refs], 1)
        for refs in (lasts, befores)
    )
    odd, core = place[1] % 2 == 1, place[2]
    near = jnp.where(odd, last[:STATE].astype(F32), 0.0)
    held = near + jnp.where(odd, decay_of(last), 1.0) * before[:STATE].astype(F32)
    factor = dot(factor_ref[...], expand)
    outs = []
    for block in range(PAIR):
        at = slice(block * BLOCK, (block + 1) * BLOCK)
        carried = dot(c_ref[at], held.astype(BF16))
        outs.append((add[at] + factor[at] * carried).astype(BF16))
        held = factor[BLOCK - 1 : BLOCK] * held + own_ref[...]

    @pl.when(core == 0)
    def _():
        keep_ref[...] = outs[0]
        send_ref[...] = outs[1]

    @pl.when(core == 1)
    def _():
        keep_ref[...] = outs[1]
        send_ref[...] = outs[0]


def final_kernel(first_head, counts, place, *refs):
    groups = []
    for number in counts:
        groups.append(refs[:number])
        refs = refs[number:]
    carry(first_head, place, *groups, *refs[:4], *refs[-2:])


def finish_kernel(first_head, counts, place, *refs):
    groups = []
    for number in counts:
        groups.append(refs[:number])
        refs = refs[number:]
    own_ref, c_ref, factor_ref = refs[:3]
    keep_ref, send_ref, partial = refs[-3:]
    local_kernel(first_head, *refs[3:8], partial)
    carry(first_head, place, *groups, own_ref, c_ref, factor_ref, partial, keep_ref, send_ref)


def place_kernel(firsts, place, *refs):
    count = len(firsts)
    keeps, gots = refs[:count], refs[count : 2 * count]
    out, sems = refs[-2:]
    core = place[2]
    half = out.shape[1] // PAIR
    copies = []
    for first, keep, got in zip(firsts, keeps, gots):
        width = keep.shape[1]
        copies.append((keep, out.at[:, ds(core * half + first, width)]))
        copies.append((got, out.at[:, ds((1 - core) * half + first, width)]))
    for copy in run(copies, sems):
        copy.wait()


def put_in_place(firsts, shape, place, keeps, gots):
    smem, vmem, hbm = (pl.BlockSpec(memory_space=m) for m in (pltpu.SMEM, pltpu.VMEM, pltpu.HBM))
    count = len(firsts)
    return pl.pallas_call(
        functools.partial(place_kernel, firsts),
        out_shape=jax.ShapeDtypeStruct(shape, BF16),
        in_specs=[smem] + [vmem] * (2 * count),
        out_specs=hbm,
        scratch_shapes=[pltpu.SemaphoreType.DMA((2 * count,))],
        compiler_params=pltpu.CompilerParams(vmem_limit_bytes=16 << 20),
        cost_estimate=pl.CostEstimate(flops=1, bytes_accessed=1, transcendentals=0),
        name="place",
    )(place, *keeps, *gots)


class Stay:
    def __init__(self, array):
        self.array = array


def gate(blocks, order):
    anywhere = pl.BlockSpec(memory_space=pl.ANY)
    return pl.pallas_call(
        lambda *refs: None,
        out_shape=[jax.ShapeDtypeStruct(block.shape, block.dtype) for block in blocks],
        in_specs=[anywhere] * (len(blocks) + len(order)),
        out_specs=[anywhere] * len(blocks),
        input_output_aliases={i: i for i in range(len(blocks))},
        compiler_params=pltpu.CompilerParams(vmem_limit_bytes=16 << 20),
        cost_estimate=pl.CostEstimate(flops=1, bytes_accessed=1, transcendentals=0),
        name="gate",
    )(*blocks, *order)


def call(body, outs, operands, scratch=(), flops=0, transcendentals=0, name=None, limit=16 << 20):
    shapes = [jax.ShapeDtypeStruct(shape, dtype) for shape, dtype in outs]
    smem, vmem, hbm = (pl.BlockSpec(memory_space=m) for m in (pltpu.SMEM, pltpu.VMEM, pltpu.HBM))
    specs = [
        hbm if isinstance(o, Stay) else smem if o.dtype == jnp.int32 else vmem for o in operands
    ]
    moved = sum(o.size * o.dtype.itemsize for o in shapes) * 2
    return pl.pallas_call(
        body,
        out_shape=shapes,
        in_specs=specs,
        out_specs=[vmem] * len(outs),
        scratch_shapes=scratch,
        compiler_params=pltpu.CompilerParams(vmem_limit_bytes=limit),
        cost_estimate=pl.CostEstimate(flops=1, bytes_accessed=1, transcendentals=0),
        name=name,
    )(*[o.array if isinstance(o, Stay) else o for o in operands])


def paired(xbc, dt_raw, conv_weight, conv_bias, a_log, dt_bias, skip_gain):
    axes = ("ctx", "head")
    shards, length = lax.axis_size("head"), lax.axis_size("ctx")
    devices, peers = shards * length, shards * PAIR
    tok = xbc.shape[0]
    slab = tok * peers
    context, shard = lax.axis_index("ctx"), lax.axis_index("head")
    pair, core = context // PAIR, context % PAIR
    group = shard * PAIR + core
    place = jnp.stack([group, pair, core, core * shards + shard, shard]).astype(jnp.int32)

    def over(block, target):
        route = [(i, target(i)) for i in range(devices)]
        return lax.ppermute(block, axes, [(i, j) for i, j in route if j is not None and j < devices])

    def swap(block):
        return over(block, lambda i: i ^ shards)

    rows = Stay(xbc)
    size = PER_GROUP + 2 * STATE
    (sent,) = call(
        functools.partial(pack_first_kernel, shards),
        [((tok, shards * WIDTHS[0] + size - WIDTHS[0]), BF16)],
        [place, rows],
        scratch=[pltpu.SemaphoreType.DMA((4 * shards,))],
        name="pack_first",
    )
    got_first = swap(sent)
    sent, tail = call(
        functools.partial(pack_kernel, shards),
        [((tok, shards * (size - WIDTHS[0]) + HEADS), BF16), ((16, shards * size), BF16)],
        [place, rows, Stay(dt_raw), Stay(sent)],
        scratch=[pltpu.SemaphoreType.DMA((6 * shards + 1,))],
        name="pack",
    )
    got_rest = swap(sent)
    taps, offset = call(
        taps_kernel,
        [((4, size), F32), ((1, size), F32)],
        [place, Stay(conv_weight), Stay(conv_bias[None]), Stay(got_rest)],
        scratch=[pltpu.SemaphoreType.DMA((6,))],
        name="taps",
    )

    def send_on(plan, order, tail=None, edges=None):
        unused = Stay(got_first)
        parts = [p for _, pieces in plan for p in pieces]
        made = [] if tail is None else [((3, shards * size), BF16)]
        return call(
            functools.partial(merge_kernel, shards, plan, len(order)),
            [((PAIR * tok, sum(map(total_of, pieces))), BF16) for _, pieces in plan] + made,
            [
                place,
                rows,
                Stay(dt_raw) if edges is None else dt_raw,
                got_first if 0 in parts else unused,
                got_rest if any(parts) else unused,
                next((o for o in (tail, edges) if o is not None), unused),
            ]
            + [Stay(o) for o in order],
            scratch=[pltpu.SemaphoreType.DMA((sum(2 + 2 * len(RESTS[p]) for p in parts),))],
            name="merge",
        )

    def travel(blocks):
        return [blocks[0]] + [over(blocks[r], lambda i, r=r: i ^ r) for r in range(1, shards)]

    def plan(piece):
        return [(r, (piece,)) for r in range(shards)]

    *first_blocks, edges = send_on(plan(0), [], tail)
    message = [travel(first_blocks)]
    edges = over(edges, lambda i: i + peers if i % shards == shards - 1 else None)
    second_blocks = send_on(plan(1), [first_blocks[0]], None, edges)
    message.append(travel(second_blocks))
    third_plan = [(r, (2, 3) if r == 1 else (2,)) for r in range(shards)]
    third_blocks = send_on(third_plan, [second_blocks[0]])
    message.append(travel(third_blocks[:1] + gate(third_blocks[1:], message[0][1:] + message[1][1:])))

    def seen(piece):
        return message[piece]

    tiles = [p.reshape(HEADS // LANES, LANES) for p in (a_log, dt_bias, skip_gain)]
    b, edge, cum, row, factor, tail, skip = call(
        functools.partial(prep_kernel, shards),
        [
            ((slab, STATE), BF16),
            ((4, size), F32),
            ((slab, LANES), F32),
            ((LANES, slab), F32),
            ((slab, 2 * LANES), BF16),
            ((slab, 2 * LANES), BF16),
            ((16, 3 * LANES), BF16),
        ],
        [place] + seen(1) + [taps, offset] + tiles + [Stay(third_blocks[0])],
        scratch=[pltpu.VMEM((slab, LANES), F32), pltpu.VMEM((slab + 8, STATE), F32)],
        name="prep",
    )
    count = len(GROUPED)
    x, sent, own, last, joined, before, keep, send = ([None] * count for _ in range(8))

    def first_head(i):
        return (sum(WIDTHS[: GROUPED[i][0]]) + GROUPED[i][1]) // HEAD_DIM

    def state_of(i, order):
        piece, _, width = GROUPED[i]
        x[i], own[i], *sent[i] = call(
            functools.partial(state_kernel, shards, GROUPED[i], FIRST_ROUND[i]),
            [((slab, width), BF16), ((STATE, width), F32)] + [((STATE + 16, w), BF16) for w in FIRST_ROUND[i]],
            [place] + seen(piece) + [taps, offset, edge, b, factor, tail] + [Stay(o) for o in order],
            scratch=[pltpu.VMEM((slab + 8, width), F32)],
            name="state",
        )
        last[i] = [over(part, lambda i: i ^ peers if i // peers != 3 else None) for part in sent[i]]

    def combine_of(i, order):
        joined[i], before[i] = [], []
        end = 0
        for width in SECOND_ROUND[i]:
            begin, end = end, end + width
            early, late, spans, first = [], [], [], 0
            for got, mine, size_of in zip(last[i], sent[i], FIRST_ROUND[i]):
                low, high = max(begin - first, 0), min(end - first, size_of)
                first += size_of
                if low < high:
                    early.append(got)
                    late.append(mine)
                    spans.append(slice(low, high))
            (total,) = call(
                functools.partial(combine_kernel, spans),
                [((STATE + 16, width), BF16)],
                [place] + early + late + [Stay(o) for o in order],
                name="combine",
            )
            joined[i].append(total)
            before[i].append(over(total, lambda i: i + 2 * peers))
            order = [total]

    def finish_of(body, i, operands, order, **more):
        keep[i], send[i] = call(
            functools.partial(body, first_head(i), (len(last[i]), len(before[i]))),
            [((BLOCK, GROUPED[i][2]), BF16)] * 2,
            [place, *last[i], *before[i], own[i], c, factor] + operands + [Stay(o) for o in order],
            name="final",
            **more,
        )

    partial = [None] * count

    def local_of(i, order):
        (partial[i],) = call(
            functools.partial(local_kernel, first_head(i)),
            [(x[i].shape, F32)],
            [x[i], cum, row, score, skip] + [Stay(o) for o in order],
            name="local",
        )

    state_of(0, [])
    own_block, *fourth_blocks = send_on([(r, (3,)) for r in range(shards) if r != 1], sent[0])
    fourth_blocks = gate(fourth_blocks, message[2][1:])
    fourth_blocks = [over(block, lambda i, r=r: i ^ r) for r, block in enumerate(fourth_blocks, 2)]
    message.append([own_block, message[2][1], *fourth_blocks])
    combine_of(0, [])
    state_of(1, joined[0])
    c, score = call(
        functools.partial(score_kernel, shards),
        [((slab, STATE), BF16), ((slab, BLOCK), F32)],
        [place] + seen(2) + [taps, offset, edge, b] + [Stay(o) for o in sent[1]],
        scratch=[pltpu.VMEM((slab + 8, STATE), F32)],
        name="score",
    )
    local_of(0, [])
    combine_of(1, [partial[0]])
    local_of(1, joined[1])
    state_of(2, [partial[1]])
    state_of(3, sent[2])
    finish_of(final_kernel, 1, [partial[1]], sent[3])
    combine_of(2, [keep[1]])
    combine_of(3, joined[2])
    local_of(2, joined[3])
    local_of(3, [partial[2]])
    finish_of(final_kernel, 0, [partial[0]], [partial[3]])
    finish_of(final_kernel, 2, [partial[2]], [keep[0]])
    finish_of(final_kernel, 3, [partial[3]], [keep[2]])
    firsts = [first_head(i) * HEAD_DIM for i in range(count)]
    return put_in_place(firsts, (BLOCK, PAIR * PER_GROUP), place, keep, [swap(o) for o in send])


def solution(mesh):
    in_specs = (P(("ctx", "head"), None), P(("ctx", "head"), None), P(), P(), P(), P(), P())
    out_specs = P("ctx", "head")
    shards, length = mesh.shape["head"], mesh.shape["ctx"]

    def program(xbc, *rest):
        slab = xbc.shape[0] // length
        fits = shards == GROUPS // PAIR and length == 4 * PAIR and slab == BLOCK
        return jax.shard_map(
            paired if fits else on_device,
            mesh=mesh,
            in_specs=in_specs,
            out_specs=out_specs,
            check_vma=False,
        )(xbc, *rest)

    return program
```

```python
import functools

import jax
import jax.numpy as jnp
from jax import lax
from jax.experimental import pallas as pl
from jax.experimental.pallas import tpu as pltpu
from jax.sharding import PartitionSpec as P

HEADS = 256
HEAD_DIM = 64
STATE = 256
GROUPS = 8
BLOCK = 256


def from_behind(block, axis, distance):
    devices = range(lax.axis_size(axis))
    route = [(i - distance, i) for i in devices if i - distance in devices]
    return lax.ppermute(block, axis, route)


def carried_in(array, axis, combine, identity):
    length, index = (lax.axis_size(axis), lax.axis_index(axis))
    everything = jax.tree.map(lambda part: lax.all_gather(part, axis), array)
    start = jax.tree.map(
        lambda part, zero: jnp.broadcast_to(jnp.asarray(zero, part.dtype), part.shape),
        array,
        identity,
    )

    def hop(k, before):
        reached = k < index
        new = combine(before, jax.tree.map(lambda part: part[k], everything))
        return jax.tree.map(lambda a, b: jnp.where(reached, a, b), new, before)

    return lax.fori_loop(0, length, hop, start)


def convolve(rows, edge, weight, bias):
    count = rows.shape[0]
    wide = jnp.concatenate([edge, rows], 0).astype(jnp.float32)
    acc = bias[None, :] + weight[0] * wide[0:count]
    acc = acc + weight[1] * wide[1 : count + 1]
    acc = acc + weight[2] * wide[2 : count + 2]
    acc = acc + weight[3] * wide[3 : count + 3]
    return jax.nn.silu(acc).astype(jnp.bfloat16)


def rearrange_heads(rows, shards, per_dev, groups_dev, per_group):
    count = rows.shape[0]
    inner = HEADS * HEAD_DIM
    replicate_groups = max(1, per_group // per_dev)
    heads_part = rows[:, :inner].reshape(count, shards, per_dev * HEAD_DIM)
    b_part = rows[:, inner : inner + GROUPS * STATE].reshape(count, GROUPS, STATE)
    c_part = rows[:, inner + GROUPS * STATE :].reshape(count, GROUPS, STATE)
    b_part = jnp.repeat(b_part, replicate_groups, axis=1).reshape(count, shards, groups_dev * STATE)
    c_part = jnp.repeat(c_part, replicate_groups, axis=1).reshape(count, shards, groups_dev * STATE)
    return jnp.concatenate([heads_part, b_part, c_part], axis=2)


def inner_block(xs, bmat, cmat, steps, cum):
    size = xs.shape[0]
    lower = jnp.arange(size)[:, None] >= jnp.arange(size)[None, :]
    scores = jnp.einsum("qgn,kgn->gqk", cmat, bmat, preferred_element_type=jnp.float32)
    order = jnp.transpose(cum, (1, 2, 0))
    gap = order[..., :, None] - order[..., None, :]
    decay = jnp.exp(jnp.where(lower, gap, -jnp.inf))
    mixing = (scores[:, None] * decay * jnp.transpose(steps, (1, 2, 0))[..., None, :]).astype(
        jnp.bfloat16
    )
    local = jnp.einsum("gjqk,kgjp->qgjp", mixing, xs, preferred_element_type=jnp.float32)
    tail = jnp.exp(cum[size - 1][None] - cum) * steps
    loaded = (bmat[:, :, None, :].astype(jnp.float32) * tail[..., None]).astype(jnp.bfloat16)
    block_state = jnp.einsum("kgjn,kgjp->gjnp", loaded, xs, preferred_element_type=jnp.float32)
    return (local, block_state)


def on_device(xbc, dt_raw, conv_weight, conv_bias, a_log, dt_bias, skip_gain):
    tok = xbc.shape[0]
    shards = lax.axis_size("head")
    per_dev = HEADS // shards
    per_group = HEADS // GROUPS
    groups_dev = max(1, per_dev // per_group)
    heads_per_cluster = per_dev // groups_dev
    sent = rearrange_heads(xbc, shards, per_dev, groups_dev, per_group)
    mine, rates = (
        lax.all_to_all(sent, "head", split_axis=1, concat_axis=0, tiled=True),
        lax.all_to_all(
            dt_raw.reshape(tok, shards, per_dev), "head", split_axis=1, concat_axis=0, tiled=True
        ),
    )
    slab = tok * shards
    mine = mine.reshape(slab, mine.shape[2])
    rates = rates.reshape(slab, per_dev)
    shard = lax.axis_index("head")
    taps = lax.dynamic_index_in_dim(
        rearrange_heads(conv_weight, shards, per_dev, groups_dev, per_group),
        shard,
        1,
        keepdims=False,
    )
    offset = lax.dynamic_index_in_dim(
        rearrange_heads(conv_bias[None, :], shards, per_dev, groups_dev, per_group),
        shard,
        1,
        keepdims=False,
    )
    edge = from_behind(mine[slab - 3 :], "ctx", 1)
    mine = convolve(mine, edge, taps, offset[0])
    nchunk = slab // BLOCK
    width = per_dev * HEAD_DIM
    xs = mine[:, :width].reshape(nchunk, BLOCK, groups_dev, heads_per_cluster, HEAD_DIM)
    bmat = mine[:, width : width + groups_dev * STATE].reshape(nchunk, BLOCK, groups_dev, STATE)
    cmat = mine[:, width + groups_dev * STATE :].reshape(nchunk, BLOCK, groups_dev, STATE)
    first = shard * per_dev
    rate = (-jnp.exp(lax.dynamic_slice_in_dim(a_log, first, per_dev))).reshape(
        groups_dev, heads_per_cluster
    )
    bias_dt = lax.dynamic_slice_in_dim(dt_bias, first, per_dev).reshape(
        groups_dev, heads_per_cluster
    )
    skip = lax.dynamic_slice_in_dim(skip_gain, first, per_dev).reshape(
        groups_dev, heads_per_cluster
    )
    steps = jax.nn.softplus(
        rates.astype(jnp.float32).reshape(nchunk, BLOCK, groups_dev, heads_per_cluster) + bias_dt
    )
    cum = jnp.cumsum(steps * rate, axis=1)

    def block_step(carry, item):
        held, product = carry
        x_part, b_part, c_part, step_part, cum_part = item
        local, block_state = inner_block(x_part, b_part, c_part, step_part, cum_part)
        lifted = c_part.astype(jnp.float32)[:, :, None, :] * jnp.exp(cum_part)[..., None]
        carried = jnp.einsum("qgjn,gjnp->qgjp", lifted, held, precision=lax.Precision.HIGHEST)
        partial_out = local + carried + skip[..., None] * x_part.astype(jnp.float32)
        end = jnp.exp(cum_part[BLOCK - 1])
        return ((end[..., None, None] * held + block_state, product * end), (partial_out, product))

    zero_state = jnp.zeros((groups_dev, heads_per_cluster, STATE, HEAD_DIM), jnp.float32)
    unit = jnp.ones((groups_dev, heads_per_cluster), jnp.float32)
    (slab_state, slab_decay), (partials, product_in) = lax.scan(
        block_step, (zero_state, unit), (xs, bmat, cmat, steps, cum)
    )

    def combine(preceding_state, later):
        return (
            preceding_state[0] * later[0],
            later[0][..., None, None] * preceding_state[1] + later[1],
        )

    _, entering = carried_in((slab_decay, slab_state), "ctx", combine, (unit, zero_state))
    projected = jnp.einsum(
        "cqgn,gjnp->cqgjp", cmat.astype(jnp.float32), entering, precision=lax.Precision.HIGHEST
    )
    factor = jnp.exp(cum) * product_in[:, None]
    total = partials + factor[..., None] * projected
    return total.astype(jnp.bfloat16).reshape(slab, width)


PAIR = 2
LANES = 128
LOG2E = 1.4426950408889634
F32, BF16 = jnp.float32, jnp.bfloat16
WIDTHS = (512, 0, 768, 768)
RESTS = ("", "BD", "", "C")
GROUPED = ((0, 0, 512), (2, 0, 768), (3, 0, 384), (3, 384, 384))
FIRST_ROUND = ((256, 256), (384, 384), (384,), (384,))
SECOND_ROUND = ((512,), (384, 384), (384,), (384,))


def halves(value, count):
    parts = []
    for _ in range(count):
        part = value.astype(BF16)
        parts.append(part)
        value = value - part.astype(F32)
    return parts


def spread(first_head, width, copies):
    lane = lax.broadcasted_iota(jnp.int32, (copies * LANES, width), 0) % LANES
    column = lax.broadcasted_iota(jnp.int32, (copies * LANES, width), 1)
    return (lane == first_head + column // HEAD_DIM).astype(BF16)


def dot(a, b):
    return jnp.dot(a, b, preferred_element_type=F32)


def ds(start, width):
    return pl.ds(pl.multiple_of(start, LANES), width)


def run(copies, sems):
    started = []
    for i, (source, target) in enumerate(copies):
        copy = pltpu.make_async_copy(source, target, sems.at[i])
        copy.start()
        started.append(copy)
    return started


PER_GROUP = HEADS * HEAD_DIM // GROUPS
INNER = HEADS * HEAD_DIM


def channels(group, first, width):
    return ds(group * PER_GROUP + first, width)


def pack_first_kernel(shards, place, xbc, send, sems):
    core, shard = place[2], place[4]
    count = xbc.shape[0]
    width = WIDTHS[0]
    copies = []
    for r in range(shards):
        group = (shard ^ r) * PAIR + 1 - core
        copies.append((xbc.at[:, channels(group, 0, width)], send.at[:, r * width : (r + 1) * width]))
        last, rows = xbc.at[count - 16 :], slice(16 * r, 16 * r + 16)
        to = shards * width
        copies.append((last.at[:, channels(group, width, PER_GROUP - width)], send.at[rows, to : to + PER_GROUP - width]))
        to += PER_GROUP - width
        for i in range(2):
            at = ds(INNER + (i * GROUPS + group) * STATE, STATE)
            copies.append((last.at[:, at], send.at[rows, to + i * STATE : to + (i + 1) * STATE]))
    for copy in run(copies, sems):
        copy.wait()


def pack_kernel(shards, place, xbc, dt_raw, order, send, tail, sems):
    core, shard = place[2], place[4]
    count = xbc.shape[0]
    first = WIDTHS[0]
    width = PER_GROUP - first
    rest = width * shards
    size = PER_GROUP + 2 * STATE
    copies = []
    for r in range(shards):
        group = (shard ^ r) * PAIR + 1 - core
        copies.append((xbc.at[:, channels(group, first, width)], send.at[:, r * width : (r + 1) * width]))
        for i in range(2):
            to = rest + (i * shards + r) * STATE
            copies.append((xbc.at[:, ds(INNER + (i * GROUPS + group) * STATE, STATE)], send.at[:, to : to + STATE]))
    copies.append((dt_raw, send.at[:, send.shape[1] - HEADS :]))
    for r in range(shards):
        group, to = (shard ^ r) * PAIR + core, r * size
        last = xbc.at[count - 16 :]
        copies.append((last.at[:, channels(group, 0, PER_GROUP)], tail.at[:, to : to + PER_GROUP]))
        for i in range(2):
            at = ds(INNER + (i * GROUPS + group) * STATE, STATE)
            start = to + PER_GROUP + i * STATE
            copies.append((last.at[:, at], tail.at[:, start : start + STATE]))
    for copy in run(copies, sems):
        copy.wait()


def taps_kernel(place, weight, bias, order, taps, offset, sems):
    copies = []
    for source, target in ((weight, taps), (bias, offset)):
        copies.append((source.at[:, channels(place[0], 0, PER_GROUP)], target.at[:, :PER_GROUP]))
        for i in range(2):
            at = ds(INNER + (i * GROUPS + place[0]) * STATE, STATE)
            start = PER_GROUP + i * STATE
            copies.append((source.at[:, at], target.at[:, start : start + STATE]))
    for copy in run(copies, sems):
        copy.wait()


def put_edge(shards, place, got, tail, out):
    count = got.shape[0]
    first = WIDTHS[0]
    size = PER_GROUP + 2 * STATE
    for r in range(shards):
        theirs = [got[count - 16 :, r * first : (r + 1) * first]]
        theirs.append(got[16 * r : 16 * r + 16, shards * first :])
        to = r * size
        for part in theirs:
            at = slice(to, to + part.shape[1])
            rows = jnp.where(place[2] == 0, part.astype(F32), tail[:, at].astype(F32))
            out[:, at] = rows[13:16].astype(BF16)
            to = at.stop


def total_of(piece):
    return WIDTHS[piece] + sum(LANES if kind == "D" else STATE for kind in RESTS[piece])


def merge_kernel(shards, plan, unread, place, xbc, dt_raw, got_first, got, edges, *refs):
    refs = refs[unread:]
    outs, sems = refs[: len(plan)], refs[-1]
    core, shard = place[2], place[4]
    count = xbc.shape[0]
    stride = PER_GROUP - WIDTHS[0]
    mine = pl.ds(pl.multiple_of(core * count, count), count)
    other = pl.ds(pl.multiple_of((1 - core) * count, count), count)
    copies, steps = [], []
    for out, (r, pieces) in zip(outs, plan):
        group = (shard ^ r) * PAIR + core
        to = 0
        for piece in pieces:
            first, width = sum(WIDTHS[:piece]), WIDTHS[piece]
            if piece == 0:
                source = got_first.at[:, r * width : (r + 1) * width]
            else:
                at = r * stride + first - WIDTHS[0]
                source = got.at[:, at : at + width]
            if width:
                copies.append((xbc.at[:, channels(group, first, width)], out.at[mine, to : to + width]))
                copies.append((source, out.at[other, to : to + width]))
            to += width
            for kind in RESTS[piece]:
                if kind == "D":
                    steps.append((out, r, to))
                    to += LANES
                    continue
                i = "BC".index(kind)
                at = ds(INNER + (i * GROUPS + group) * STATE, STATE)
                copies.append((xbc.at[:, at], out.at[mine, to : to + STATE]))
                at = stride * shards + (i * shards + r) * STATE
                copies.append((got.at[:, at : at + STATE], out.at[other, to : to + STATE]))
                to += STATE
    started = run(copies, sems)
    if len(refs) > len(plan) + 1:
        put_edge(shards, place, got_first, edges, refs[-2])
    if steps:
        lane = lax.broadcasted_iota(jnp.int32, (count, LANES), 1)
        per_tile = LANES * GROUPS // HEADS
        heads = HEADS // GROUPS
        for out, r, to in steps:
            group = (shard ^ r) * PAIR + core
            tile, shift = group // per_tile, (LANES - (group % per_tile) * heads) % LANES
            own = dt_raw[:, ds(tile * LANES, LANES)].astype(F32)
            theirs = got[:, ds(got.shape[1] - HEADS + tile * LANES, LANES)].astype(F32)
            low = jnp.where(core == 0, own, theirs)
            high = jnp.where(core == 0, theirs, own)
            packed = jnp.zeros((count // 2, LANES), F32)
            for j, rows in enumerate((low, high)):
                rows = jnp.where(lane < heads, pltpu.roll(rows, shift, 1), 0.0)
                for i in range(2):
                    part = rows[i * count // 2 : (i + 1) * count // 2]
                    packed = packed + pltpu.roll(part, (2 * j + i) * heads, 1)
            out[: count // 2, to : to + LANES] = packed.astype(BF16)
            size = PER_GROUP + 2 * STATE
            at = slice(r * size, (r + 1) * size)
            edge = jnp.concatenate([edges[:, at].astype(F32), jnp.zeros((1, size), F32)], 0)
            edge = jnp.concatenate([edge[:, q * LANES : (q + 1) * LANES] for q in range(size // LANES)], 0)
            fill = jnp.zeros((PAIR * count - count // 2 - edge.shape[0], LANES), F32)
            out[count // 2 :, to : to + LANES] = jnp.concatenate([edge, fill], 0).astype(BF16)
    for copy in started:
        copy.wait()


def view(refs, piece):
    return [(ref, total_of(2) if piece == 3 and r == 1 else 0) for r, ref in enumerate(refs)]


def convolve_in_order(place, blocks, columns, edge, tap, bias, wide, put):
    width = columns.stop - columns.start
    count = blocks[0][0].shape[0] // PAIR
    wide[5:8, :width] = edge
    for r, (block, origin) in enumerate(blocks):
        for core in range(PAIR):
            at = pl.multiple_of((core * len(blocks) + (place[4] ^ r)) * count + 8, 8)
            part = block[core * count : (core + 1) * count, origin + columns.start : origin + columns.stop]
            wide[pl.ds(at, count), :width] = part.astype(F32)
    tap, bias = tap * 0.5, bias * 0.5
    for start in range(0, PAIR * len(blocks) * count, count):
        acc = bias + tap[0:1] * wide[start + 5 : start + 5 + count, :width]
        acc = acc + tap[1:2] * wide[start + 6 : start + 6 + count, :width]
        acc = acc + tap[2:3] * wide[start + 7 : start + 7 + count, :width]
        acc = acc + tap[3:4] * wide[start + 8 : start + 8 + count, :width]
        put(start, count, (acc + acc * jnp.tanh(acc)).astype(BF16))


def prep_kernel(shards, place, *refs):
    blocks, (taps, offset, a_ref, bias_ref, skip_ref, order) = refs[:shards], refs[shards : shards + 6]
    b_ref, edge_ref, cum_ref, row_ref, factor_ref, tail_ref, skip_out, dt_ref, wide = refs[shards + 6 :]
    blocks = view(blocks, 1)
    start = WIDTHS[1]
    last = total_of(1) - LANES
    size = edge_ref.shape[1]
    count = blocks[0][0].shape[0] // PAIR
    half, heads = count // 2, HEADS // GROUPS
    columns = [block[:, origin + last : origin + last + LANES].astype(F32) for block, origin in blocks]
    edge = columns[0][half : half + 4 * size // LANES]
    for column in columns[1:]:
        edge = edge + column[half : half + 4 * size // LANES]
    for q in range(size // LANES):
        edge_ref[:, q * LANES : (q + 1) * LANES] = edge[4 * q : 4 * q + 4]
    for r, column in enumerate(columns):
        packed = column[:half]
        for j in range(2 * PAIR):
            at = ((j // 2) * shards + (place[4] ^ r)) * count + (j % 2) * half
            rows = packed if j == 0 else pltpu.roll(packed, LANES - j * heads, 1)
            dt_ref[pl.ds(pl.multiple_of(at, half), half), :] = rows

    def put(start, count, value):
        b_ref[start : start + count] = value

    at = slice(PER_GROUP, PER_GROUP + STATE)
    convolve_in_order(
        place, blocks, slice(start, start + STATE), edge_ref[0:3, at], taps[:, at], offset[:, at], wide, put
    )
    per_tile = LANES * GROUPS // HEADS
    group = place[0]
    tile = group // per_tile
    shift = (LANES - (group % per_tile) * heads) % LANES

    def lanes_of(ref):
        return pltpu.roll(jnp.broadcast_to(ref[pl.ds(tile, 1), :], (8, LANES)), shift, 1)

    rate = -jnp.exp(lanes_of(a_ref)[0:1])
    raw = dt_ref[...] + lanes_of(bias_ref)[0:1]
    step = jnp.maximum(raw, 0.0) + jnp.log1p(jnp.exp(-jnp.abs(raw)))
    skip = lanes_of(skip_ref)
    skip_out[...] = jnp.concatenate(halves(jnp.concatenate([skip, skip], 0), 3), 1)
    lower = (
        lax.broadcasted_iota(jnp.int32, (BLOCK, BLOCK), 0)
        >= lax.broadcasted_iota(jnp.int32, (BLOCK, BLOCK), 1)
    ).astype(BF16)
    valid = lax.broadcasted_iota(jnp.int32, (BLOCK, LANES), 1) < heads
    for block in range(PAIR):
        at = slice(block * BLOCK, (block + 1) * BLOCK)
        here = jnp.where(valid, step[at], 1.0)
        parts = halves(here * rate, 3)
        cum = dot(lower, parts[0]) + (dot(lower, parts[1]) + dot(lower, parts[2]))
        cum = cum * LOG2E
        cum_ref[at] = cum
        row_ref[:, at] = jnp.transpose(cum - jnp.log2(here))
        factor_ref[at] = jnp.concatenate(halves(jnp.exp2(cum), 2), 1)
        tail = jnp.exp2(cum[BLOCK - 1 :] - cum) * here
        tail_ref[at] = jnp.concatenate(halves(tail, 2), 1)


def score_kernel(shards, place, *refs):
    blocks, refs = refs[:shards], refs[shards:]
    taps, offset, edge_ref, b_ref, c_ref, score_ref, wide = (*refs[:4], *refs[-3:])
    blocks = view(blocks, 3)
    start = WIDTHS[3]
    at = slice(PER_GROUP + STATE, PER_GROUP + 2 * STATE)

    def put(start, count, value):
        c_ref[start : start + count] = value

    convolve_in_order(
        place, blocks, slice(start, start + STATE), edge_ref[0:3, at], taps[:, at], offset[:, at], wide, put
    )
    for block in range(PAIR):
        at = slice(block * BLOCK, (block + 1) * BLOCK)
        score_ref[at] = lax.dot_general(
            c_ref[at], b_ref[at], (((1,), (1,)), ((), ())), preferred_element_type=F32
        )


def decay_of(ref):
    decay = ref[STATE : STATE + 16].astype(F32)
    return decay[0:1] + (decay[1:2] + decay[2:3])


def put_decay(ref, decay):
    row = lax.broadcasted_iota(jnp.int32, (16, ref.shape[1]), 0)
    high, middle, low = (part.astype(F32) for part in halves(decay, 3))
    packed = jnp.where(row == 0, high, jnp.where(row == 1, middle, jnp.where(row == 2, low, 0.0)))
    ref[STATE:] = packed.astype(BF16)


def state_kernel(shards, part, sizes, place, *refs):
    blocks, refs = refs[:shards], refs[shards:]
    taps, offset, edge_ref, b_ref, factor_ref, tail_ref = refs[:6]
    x_ref, own_ref, *sends, wide = refs[-3 - len(sizes) :]
    piece, start, width = part
    first = sum(WIDTHS[:piece]) + start
    at = slice(first, first + width)

    def put(row, count, value):
        x_ref[row : row + count] = value

    blocks = view(blocks, piece)
    columns = slice(start, start + width)
    convolve_in_order(place, blocks, columns, edge_ref[0:3, at], taps[:, at], offset[:, at], wide, put)
    expand = spread(first // HEAD_DIM, width, 2)
    both = []
    for block in range(PAIR):
        at = slice(block * BLOCK, (block + 1) * BLOCK)
        loaded = (x_ref[at].astype(F32) * dot(tail_ref[at], expand)).astype(BF16)
        both.append(
            lax.dot_general(b_ref[at], loaded, (((0,), (0,)), ((), ())), preferred_element_type=F32)
        )
    ends = [dot(factor_ref[(i + 1) * BLOCK - 16 : (i + 1) * BLOCK], expand)[15:16] for i in range(PAIR)]
    own_ref[...] = both[0]
    end = (ends[1] * both[0] + both[1]).astype(BF16)
    decay = ends[0] * ends[1]
    start = 0
    for send_ref in sends:
        at = slice(start, start + send_ref.shape[1])
        send_ref[0:STATE] = end[:, at]
        put_decay(send_ref, decay[:, at])
        start = at.stop


def combine_kernel(spans, place, *refs):
    count = len(spans)
    got, own, out_ref = refs[:count], refs[count : 2 * count], refs[-1]
    odd = place[1] % 2 == 1
    start = 0
    for got_ref, own_ref, span in zip(got, own, spans):
        at = slice(start, start + span.stop - span.start)
        theirs, mine = got_ref[:STATE, span].astype(F32), own_ref[:STATE, span].astype(F32)
        decay, other = decay_of(own_ref.at[:, span]), decay_of(got_ref.at[:, span])
        early, late = jnp.where(odd, theirs, mine), jnp.where(odd, mine, theirs)
        out_ref[:STATE, at] = (jnp.where(odd, decay, other) * early + late).astype(BF16)
        put_decay(out_ref.at[:, at], decay * other)
        start = at.stop


def mix(first_head, x_ref, cum_ref, row_ref, score_ref, skip_ref, put):
    width = x_ref.shape[1]
    half = BLOCK // 2
    expand = spread(first_head, width, 3)
    skip = dot(skip_ref[...], expand)[0:1]
    lower = lax.broadcasted_iota(jnp.int32, (half, half), 0) >= lax.broadcasted_iota(
        jnp.int32, (half, half), 1
    )
    lane = lax.broadcasted_iota(jnp.int32, (BLOCK, LANES), 1)
    for block in range(PAIR):
        base = block * BLOCK
        for tile in range(width // LANES):
            columns = slice(tile * LANES, (tile + 1) * LANES)
            x = x_ref[base : base + BLOCK, columns]
            top = skip[:, columns] * x[:half].astype(F32)
            bottom = skip[:, columns] * x[half:].astype(F32)
            for side in range(LANES // HEAD_DIM):
                head = first_head + tile * (LANES // HEAD_DIM) + side
                own = jnp.where(lane // HEAD_DIM == side, x, jnp.zeros_like(x))
                cum = cum_ref[base : base + BLOCK, head : head + 1]
                row = row_ref[head : head + 1, base : base + BLOCK]
                diag = jnp.where(lower, cum[:half] - row[:, :half], -1e30)
                mixing = jnp.exp2(diag) * score_ref[base : base + half, :half]
                top = top + dot(mixing.astype(BF16), own[:half])
                left = jnp.exp2(cum[half:] - row[:, :half]) * score_ref[base + half : base + BLOCK, :half]
                diag = jnp.where(lower, cum[half:] - row[:, half:], -1e30)
                right = jnp.exp2(diag) * score_ref[base + half : base + BLOCK, half:]
                mixing = jnp.concatenate([left.astype(BF16), right.astype(BF16)], 1)
                bottom = bottom + dot(mixing, own)
            put(block, slice(base, base + half), columns, top)
            put(block, slice(base + half, base + BLOCK), columns, bottom)


def local_kernel(first_head, x_ref, cum_ref, row_ref, score_ref, skip_ref, *refs):
    out_ref = refs[-1]

    def put(block, rows, columns, value):
        out_ref[rows, columns] = value

    mix(first_head, x_ref, cum_ref, row_ref, score_ref, skip_ref, put)


def carry(first_head, place, lasts, befores, own_ref, c_ref, factor_ref, add, keep_ref, send_ref):
    expand = spread(first_head, own_ref.shape[1], 2)
    last, before = (
        refs[0][...] if len(refs) == 1 else jnp.concatenate([ref[...] for ref in refs], 1)
        for refs in (lasts, befores)
    )
    odd, core = place[1] % 2 == 1, place[2]
    near = jnp.where(odd, last[:STATE].astype(F32), 0.0)
    held = near + jnp.where(odd, decay_of(last), 1.0) * before[:STATE].astype(F32)
    factor = dot(factor_ref[...], expand)
    outs = []
    for block in range(PAIR):
        at = slice(block * BLOCK, (block + 1) * BLOCK)
        carried = dot(c_ref[at], held.astype(BF16))
        outs.append((add[at] + factor[at] * carried).astype(BF16))
        held = factor[BLOCK - 1 : BLOCK] * held + own_ref[...]

    @pl.when(core == 0)
    def _():
        keep_ref[...] = outs[0]
        send_ref[...] = outs[1]

    @pl.when(core == 1)
    def _():
        keep_ref[...] = outs[1]
        send_ref[...] = outs[0]


def final_kernel(first_head, counts, place, *refs):
    groups = []
    for number in counts:
        groups.append(refs[:number])
        refs = refs[number:]
    carry(first_head, place, *groups, *refs[:4], *refs[-2:])


def finish_kernel(first_head, counts, place, *refs):
    groups = []
    for number in counts:
        groups.append(refs[:number])
        refs = refs[number:]
    own_ref, c_ref, factor_ref = refs[:3]
    keep_ref, send_ref, partial = refs[-3:]
    local_kernel(first_head, *refs[3:8], partial)
    carry(first_head, place, *groups, own_ref, c_ref, factor_ref, partial, keep_ref, send_ref)


def place_kernel(firsts, place, *refs):
    count = len(firsts)
    keeps, gots = refs[:count], refs[count : 2 * count]
    out, sems = refs[-2:]
    core = place[2]
    half = out.shape[1] // PAIR
    copies = []
    for first, keep, got in zip(firsts, keeps, gots):
        width = keep.shape[1]
        copies.append((keep, out.at[:, ds(core * half + first, width)]))
        copies.append((got, out.at[:, ds((1 - core) * half + first, width)]))
    for copy in run(copies, sems):
        copy.wait()


def put_in_place(firsts, shape, place, keeps, gots):
    smem, vmem, hbm = (pl.BlockSpec(memory_space=m) for m in (pltpu.SMEM, pltpu.VMEM, pltpu.HBM))
    count = len(firsts)
    return pl.pallas_call(
        functools.partial(place_kernel, firsts),
        out_shape=jax.ShapeDtypeStruct(shape, BF16),
        in_specs=[smem] + [vmem] * (2 * count),
        out_specs=hbm,
        scratch_shapes=[pltpu.SemaphoreType.DMA((2 * count,))],
        compiler_params=pltpu.CompilerParams(vmem_limit_bytes=16 << 20),
        cost_estimate=pl.CostEstimate(flops=1, bytes_accessed=1, transcendentals=0),
        name="place",
    )(place, *keeps, *gots)


class Stay:
    def __init__(self, array):
        self.array = array


def gate(blocks, order):
    anywhere = pl.BlockSpec(memory_space=pl.ANY)
    return pl.pallas_call(
        lambda *refs: None,
        out_shape=[jax.ShapeDtypeStruct(block.shape, block.dtype) for block in blocks],
        in_specs=[anywhere] * (len(blocks) + len(order)),
        out_specs=[anywhere] * len(blocks),
        input_output_aliases={i: i for i in range(len(blocks))},
        compiler_params=pltpu.CompilerParams(vmem_limit_bytes=16 << 20),
        cost_estimate=pl.CostEstimate(flops=1, bytes_accessed=1, transcendentals=0),
        name="gate",
    )(*blocks, *order)


def call(body, outs, operands, scratch=(), flops=0, transcendentals=0, name=None, limit=16 << 20):
    shapes = [jax.ShapeDtypeStruct(shape, dtype) for shape, dtype in outs]
    smem, vmem, hbm = (pl.BlockSpec(memory_space=m) for m in (pltpu.SMEM, pltpu.VMEM, pltpu.HBM))
    specs = [
        hbm if isinstance(o, Stay) else smem if o.dtype == jnp.int32 else vmem for o in operands
    ]
    moved = sum(o.size * o.dtype.itemsize for o in shapes) * 2
    return pl.pallas_call(
        body,
        out_shape=shapes,
        in_specs=specs,
        out_specs=[vmem] * len(outs),
        scratch_shapes=scratch,
        compiler_params=pltpu.CompilerParams(vmem_limit_bytes=limit),
        cost_estimate=pl.CostEstimate(flops=1, bytes_accessed=1, transcendentals=0),
        name=name,
    )(*[o.array if isinstance(o, Stay) else o for o in operands])


def paired(xbc, dt_raw, conv_weight, conv_bias, a_log, dt_bias, skip_gain):
    axes = ("ctx", "head")
    shards, length = lax.axis_size("head"), lax.axis_size("ctx")
    devices, peers = shards * length, shards * PAIR
    tok = xbc.shape[0]
    slab = tok * peers
    context, shard = lax.axis_index("ctx"), lax.axis_index("head")
    pair, core = context // PAIR, context % PAIR
    group = shard * PAIR + core
    place = jnp.stack([group, pair, core, core * shards + shard, shard]).astype(jnp.int32)

    def over(block, target):
        route = [(i, target(i)) for i in range(devices)]
        return lax.ppermute(block, axes, [(i, j) for i, j in route if j is not None and j < devices])

    def swap(block):
        return over(block, lambda i: i ^ shards)

    rows = Stay(xbc)
    size = PER_GROUP + 2 * STATE
    (sent,) = call(
        functools.partial(pack_first_kernel, shards),
        [((tok, shards * WIDTHS[0] + size - WIDTHS[0]), BF16)],
        [place, rows],
        scratch=[pltpu.SemaphoreType.DMA((4 * shards,))],
        name="pack_first",
    )
    got_first = swap(sent)
    sent, tail = call(
        functools.partial(pack_kernel, shards),
        [((tok, shards * (size - WIDTHS[0]) + HEADS), BF16), ((16, shards * size), BF16)],
        [place, rows, Stay(dt_raw), Stay(sent)],
        scratch=[pltpu.SemaphoreType.DMA((6 * shards + 1,))],
        name="pack",
    )
    got_rest = swap(sent)
    taps, offset = call(
        taps_kernel,
        [((4, size), F32), ((1, size), F32)],
        [place, Stay(conv_weight), Stay(conv_bias[None]), Stay(got_rest)],
        scratch=[pltpu.SemaphoreType.DMA((6,))],
        name="taps",
    )

    def send_on(plan, order, tail=None, edges=None):
        unused = Stay(got_first)
        parts = [p for _, pieces in plan for p in pieces]
        made = [] if tail is None else [((3, shards * size), BF16)]
        return call(
            functools.partial(merge_kernel, shards, plan, len(order)),
            [((PAIR * tok, sum(map(total_of, pieces))), BF16) for _, pieces in plan] + made,
            [
                place,
                rows,
                Stay(dt_raw) if edges is None else dt_raw,
                got_first if 0 in parts else unused,
                got_rest if any(parts) else unused,
                next((o for o in (tail, edges) if o is not None), unused),
            ]
            + [Stay(o) for o in order],
            scratch=[pltpu.SemaphoreType.DMA((sum(2 + 2 * len(RESTS[p]) for p in parts),))],
            name="merge",
        )

    def travel(blocks):
        return [blocks[0]] + [over(blocks[r], lambda i, r=r: i ^ r) for r in range(1, shards)]

    def plan(piece):
        return [(r, (piece,)) for r in range(shards)]

    *first_blocks, edges = send_on(plan(0), [], tail)
    message = [travel(first_blocks)]
    edges = over(edges, lambda i: i + peers if i % shards == shards - 1 else None)
    second_blocks = send_on(plan(1), [first_blocks[0]], None, edges)
    message.append(travel(second_blocks))
    third_plan = [(r, (2, 3) if r == 1 else (2,)) for r in range(shards)]
    third_blocks = send_on(third_plan, [second_blocks[0]])
    message.append(travel(third_blocks[:1] + gate(third_blocks[1:], message[0][1:] + message[1][1:])))

    def seen(piece):
        return message[piece]

    tiles = [p.reshape(HEADS // LANES, LANES) for p in (a_log, dt_bias, skip_gain)]
    b, edge, cum, row, factor, tail, skip = call(
        functools.partial(prep_kernel, shards),
        [
            ((slab, STATE), BF16),
            ((4, size), F32),
            ((slab, LANES), F32),
            ((LANES, slab), F32),
            ((slab, 2 * LANES), BF16),
            ((slab, 2 * LANES), BF16),
            ((16, 3 * LANES), BF16),
        ],
        [place] + seen(1) + [taps, offset] + tiles + [Stay(third_blocks[0])],
        scratch=[pltpu.VMEM((slab, LANES), F32), pltpu.VMEM((slab + 8, STATE), F32)],
        name="prep",
    )
    count = len(GROUPED)
    x, sent, own, last, joined, before, keep, send = ([None] * count for _ in range(8))

    def first_head(i):
        return (sum(WIDTHS[: GROUPED[i][0]]) + GROUPED[i][1]) // HEAD_DIM

    def state_of(i, order):
        piece, _, width = GROUPED[i]
        x[i], own[i], *sent[i] = call(
            functools.partial(state_kernel, shards, GROUPED[i], FIRST_ROUND[i]),
            [((slab, width), BF16), ((STATE, width), F32)] + [((STATE + 16, w), BF16) for w in FIRST_ROUND[i]],
            [place] + seen(piece) + [taps, offset, edge, b, factor, tail] + [Stay(o) for o in order],
            scratch=[pltpu.VMEM((slab + 8, width), F32)],
            name="state",
        )
        last[i] = [over(part, lambda i: i ^ peers if i // peers != 3 else None) for part in sent[i]]

    def combine_of(i, order):
        joined[i], before[i] = [], []
        end = 0
        for width in SECOND_ROUND[i]:
            begin, end = end, end + width
            early, late, spans, first = [], [], [], 0
            for got, mine, size_of in zip(last[i], sent[i], FIRST_ROUND[i]):
                low, high = max(begin - first, 0), min(end - first, size_of)
                first += size_of
                if low < high:
                    early.append(got)
                    late.append(mine)
                    spans.append(slice(low, high))
            (total,) = call(
                functools.partial(combine_kernel, spans),
                [((STATE + 16, width), BF16)],
                [place] + early + late + [Stay(o) for o in order],
                name="combine",
            )
            joined[i].append(total)
            before[i].append(over(total, lambda i: i + 2 * peers))
            order = [total]

    def finish_of(body, i, operands, order, **more):
        keep[i], send[i] = call(
            functools.partial(body, first_head(i), (len(last[i]), len(before[i]))),
            [((BLOCK, GROUPED[i][2]), BF16)] * 2,
            [place, *last[i], *before[i], own[i], c, factor] + operands + [Stay(o) for o in order],
            name="final",
            **more,
        )

    partial = [None] * count

    def local_of(i, order):
        (partial[i],) = call(
            functools.partial(local_kernel, first_head(i)),
            [(x[i].shape, F32)],
            [x[i], cum, row, score, skip] + [Stay(o) for o in order],
            name="local",
        )

    state_of(0, [])
    own_block, *fourth_blocks = send_on([(r, (3,)) for r in range(shards) if r != 1], sent[0])
    fourth_blocks = gate(fourth_blocks, message[2][1:])
    fourth_blocks = [over(block, lambda i, r=r: i ^ r) for r, block in enumerate(fourth_blocks, 2)]
    message.append([own_block, message[2][1], *fourth_blocks])
    combine_of(0, [])
    state_of(1, joined[0])
    combine_of(1, [])
    state_of(2, joined[1] + before[0])
    state_of(3, sent[2])
    c, score = call(
        functools.partial(score_kernel, shards),
        [((slab, STATE), BF16), ((slab, BLOCK), F32)],
        [place] + seen(3) + [taps, offset, edge, b] + [Stay(o) for o in sent[3] + before[1]],
        scratch=[pltpu.VMEM((slab + 8, STATE), F32)],
        name="score",
    )

    def in_full(i, order):
        wide = [pltpu.VMEM((slab, GROUPED[i][2]), F32)]
        finish_of(finish_kernel, i, [x[i], cum, row, score, skip], order, scratch=wide)

    combine_of(2, [score])
    in_full(1, joined[2])
    combine_of(3, [keep[1]])
    in_full(0, joined[3])
    local_of(2, [keep[0]])
    local_of(3, [partial[2]])
    finish_of(final_kernel, 2, [partial[2]], [partial[3]])
    finish_of(final_kernel, 3, [partial[3]], [keep[2]])
    firsts = [first_head(i) * HEAD_DIM for i in range(count)]
    return put_in_place(firsts, (BLOCK, PAIR * PER_GROUP), place, keep, [swap(o) for o in send])


def solution(mesh):
    in_specs = (P(("ctx", "head"), None), P(("ctx", "head"), None), P(), P(), P(), P(), P())
    out_specs = P("ctx", "head")
    shards, length = mesh.shape["head"], mesh.shape["ctx"]

    def program(xbc, *rest):
        slab = xbc.shape[0] // length
        fits = shards == GROUPS // PAIR and length == 4 * PAIR and slab == BLOCK
        return jax.shard_map(
            paired if fits else on_device,
            mesh=mesh,
            in_specs=in_specs,
            out_specs=out_specs,
            check_vma=False,
        )(xbc, *rest)

    return program
```

```python
import functools

import jax
import jax.numpy as jnp
from jax import lax
from jax.experimental import pallas as pl
from jax.experimental.pallas import tpu as pltpu
from jax.sharding import PartitionSpec as P

HEADS = 256
HEAD_DIM = 64
STATE = 256
GROUPS = 8
BLOCK = 256


def from_behind(block, axis, distance):
    devices = range(lax.axis_size(axis))
    route = [(i - distance, i) for i in devices if i - distance in devices]
    return lax.ppermute(block, axis, route)


def carried_in(array, axis, combine, identity):
    length, index = (lax.axis_size(axis), lax.axis_index(axis))
    everything = jax.tree.map(lambda part: lax.all_gather(part, axis), array)
    start = jax.tree.map(
        lambda part, zero: jnp.broadcast_to(jnp.asarray(zero, part.dtype), part.shape),
        array,
        identity,
    )

    def hop(k, before):
        reached = k < index
        new = combine(before, jax.tree.map(lambda part: part[k], everything))
        return jax.tree.map(lambda a, b: jnp.where(reached, a, b), new, before)

    return lax.fori_loop(0, length, hop, start)


def convolve(rows, edge, weight, bias):
    count = rows.shape[0]
    wide = jnp.concatenate([edge, rows], 0).astype(jnp.float32)
    acc = bias[None, :] + weight[0] * wide[0:count]
    acc = acc + weight[1] * wide[1 : count + 1]
    acc = acc + weight[2] * wide[2 : count + 2]
    acc = acc + weight[3] * wide[3 : count + 3]
    return jax.nn.silu(acc).astype(jnp.bfloat16)


def rearrange_heads(rows, shards, per_dev, groups_dev, per_group):
    count = rows.shape[0]
    inner = HEADS * HEAD_DIM
    replicate_groups = max(1, per_group // per_dev)
    heads_part = rows[:, :inner].reshape(count, shards, per_dev * HEAD_DIM)
    b_part = rows[:, inner : inner + GROUPS * STATE].reshape(count, GROUPS, STATE)
    c_part = rows[:, inner + GROUPS * STATE :].reshape(count, GROUPS, STATE)
    b_part = jnp.repeat(b_part, replicate_groups, axis=1).reshape(count, shards, groups_dev * STATE)
    c_part = jnp.repeat(c_part, replicate_groups, axis=1).reshape(count, shards, groups_dev * STATE)
    return jnp.concatenate([heads_part, b_part, c_part], axis=2)


def inner_block(xs, bmat, cmat, steps, cum):
    size = xs.shape[0]
    lower = jnp.arange(size)[:, None] >= jnp.arange(size)[None, :]
    scores = jnp.einsum("qgn,kgn->gqk", cmat, bmat, preferred_element_type=jnp.float32)
    order = jnp.transpose(cum, (1, 2, 0))
    gap = order[..., :, None] - order[..., None, :]
    decay = jnp.exp(jnp.where(lower, gap, -jnp.inf))
    mixing = (scores[:, None] * decay * jnp.transpose(steps, (1, 2, 0))[..., None, :]).astype(
        jnp.bfloat16
    )
    local = jnp.einsum("gjqk,kgjp->qgjp", mixing, xs, preferred_element_type=jnp.float32)
    tail = jnp.exp(cum[size - 1][None] - cum) * steps
    loaded = (bmat[:, :, None, :].astype(jnp.float32) * tail[..., None]).astype(jnp.bfloat16)
    block_state = jnp.einsum("kgjn,kgjp->gjnp", loaded, xs, preferred_element_type=jnp.float32)
    return (local, block_state)


def on_device(xbc, dt_raw, conv_weight, conv_bias, a_log, dt_bias, skip_gain):
    tok = xbc.shape[0]
    shards = lax.axis_size("head")
    per_dev = HEADS // shards
    per_group = HEADS // GROUPS
    groups_dev = max(1, per_dev // per_group)
    heads_per_cluster = per_dev // groups_dev
    sent = rearrange_heads(xbc, shards, per_dev, groups_dev, per_group)
    mine, rates = (
        lax.all_to_all(sent, "head", split_axis=1, concat_axis=0, tiled=True),
        lax.all_to_all(
            dt_raw.reshape(tok, shards, per_dev), "head", split_axis=1, concat_axis=0, tiled=True
        ),
    )
    slab = tok * shards
    mine = mine.reshape(slab, mine.shape[2])
    rates = rates.reshape(slab, per_dev)
    shard = lax.axis_index("head")
    taps = lax.dynamic_index_in_dim(
        rearrange_heads(conv_weight, shards, per_dev, groups_dev, per_group),
        shard,
        1,
        keepdims=False,
    )
    offset = lax.dynamic_index_in_dim(
        rearrange_heads(conv_bias[None, :], shards, per_dev, groups_dev, per_group),
        shard,
        1,
        keepdims=False,
    )
    edge = from_behind(mine[slab - 3 :], "ctx", 1)
    mine = convolve(mine, edge, taps, offset[0])
    nchunk = slab // BLOCK
    width = per_dev * HEAD_DIM
    xs = mine[:, :width].reshape(nchunk, BLOCK, groups_dev, heads_per_cluster, HEAD_DIM)
    bmat = mine[:, width : width + groups_dev * STATE].reshape(nchunk, BLOCK, groups_dev, STATE)
    cmat = mine[:, width + groups_dev * STATE :].reshape(nchunk, BLOCK, groups_dev, STATE)
    first = shard * per_dev
    rate = (-jnp.exp(lax.dynamic_slice_in_dim(a_log, first, per_dev))).reshape(
        groups_dev, heads_per_cluster
    )
    bias_dt = lax.dynamic_slice_in_dim(dt_bias, first, per_dev).reshape(
        groups_dev, heads_per_cluster
    )
    skip = lax.dynamic_slice_in_dim(skip_gain, first, per_dev).reshape(
        groups_dev, heads_per_cluster
    )
    steps = jax.nn.softplus(
        rates.astype(jnp.float32).reshape(nchunk, BLOCK, groups_dev, heads_per_cluster) + bias_dt
    )
    cum = jnp.cumsum(steps * rate, axis=1)

    def block_step(carry, item):
        held, product = carry
        x_part, b_part, c_part, step_part, cum_part = item
        local, block_state = inner_block(x_part, b_part, c_part, step_part, cum_part)
        lifted = c_part.astype(jnp.float32)[:, :, None, :] * jnp.exp(cum_part)[..., None]
        carried = jnp.einsum("qgjn,gjnp->qgjp", lifted, held, precision=lax.Precision.HIGHEST)
        partial_out = local + carried + skip[..., None] * x_part.astype(jnp.float32)
        end = jnp.exp(cum_part[BLOCK - 1])
        return ((end[..., None, None] * held + block_state, product * end), (partial_out, product))

    zero_state = jnp.zeros((groups_dev, heads_per_cluster, STATE, HEAD_DIM), jnp.float32)
    unit = jnp.ones((groups_dev, heads_per_cluster), jnp.float32)
    (slab_state, slab_decay), (partials, product_in) = lax.scan(
        block_step, (zero_state, unit), (xs, bmat, cmat, steps, cum)
    )

    def combine(preceding_state, later):
        return (
            preceding_state[0] * later[0],
            later[0][..., None, None] * preceding_state[1] + later[1],
        )

    _, entering = carried_in((slab_decay, slab_state), "ctx", combine, (unit, zero_state))
    projected = jnp.einsum(
        "cqgn,gjnp->cqgjp", cmat.astype(jnp.float32), entering, precision=lax.Precision.HIGHEST
    )
    factor = jnp.exp(cum) * product_in[:, None]
    total = partials + factor[..., None] * projected
    return total.astype(jnp.bfloat16).reshape(slab, width)


PAIR = 2
LANES = 128
LOG2E = 1.4426950408889634
F32, BF16 = jnp.float32, jnp.bfloat16
WIDTHS = (512, 0, 768, 768)
RESTS = ("", "BD", "", "C")
GROUPED = ((0, 0, 512), (2, 0, 768), (3, 0, 384), (3, 384, 384))
FIRST_ROUND = ((256, 256), (384, 384), (384,), (384,))
SECOND_ROUND = ((512,), (384, 384), (384,), (384,))


FLIP = (0, 2, 3, 1)
NEAR = 3


def halves(value, count):
    parts = []
    for _ in range(count):
        part = value.astype(BF16)
        parts.append(part)
        value = value - part.astype(F32)
    return parts


def spread(first_head, width, copies):
    lane = lax.broadcasted_iota(jnp.int32, (copies * LANES, width), 0) % LANES
    column = lax.broadcasted_iota(jnp.int32, (copies * LANES, width), 1)
    return (lane == first_head + column // HEAD_DIM).astype(BF16)


def dot(a, b):
    return jnp.dot(a, b, preferred_element_type=F32)


def ds(start, width):
    return pl.ds(pl.multiple_of(start, LANES), width)


def run(copies, sems):
    started = []
    for i, (source, target) in enumerate(copies):
        copy = pltpu.make_async_copy(source, target, sems.at[i])
        copy.start()
        started.append(copy)
    return started


PER_GROUP = HEADS * HEAD_DIM // GROUPS
INNER = HEADS * HEAD_DIM


def channels(group, first, width):
    return ds(group * PER_GROUP + first, width)


def pack_first_kernel(shards, place, xbc, send, sems):
    core, shard = place[2], place[4]
    count = xbc.shape[0]
    width = WIDTHS[0]
    copies = []
    for r in range(shards):
        group = (shard ^ FLIP[r]) * PAIR + 1 - core
        copies.append((xbc.at[:, channels(group, 0, width)], send.at[:, r * width : (r + 1) * width]))
        last, rows = xbc.at[count - 16 :], slice(16 * r, 16 * r + 16)
        to = shards * width
        copies.append((last.at[:, channels(group, width, PER_GROUP - width)], send.at[rows, to : to + PER_GROUP - width]))
        to += PER_GROUP - width
        for i in range(2):
            at = ds(INNER + (i * GROUPS + group) * STATE, STATE)
            copies.append((last.at[:, at], send.at[rows, to + i * STATE : to + (i + 1) * STATE]))
    for copy in run(copies, sems):
        copy.wait()


def pack_kernel(shards, place, xbc, dt_raw, order, send, tail, sems):
    core, shard = place[2], place[4]
    count = xbc.shape[0]
    first = WIDTHS[0]
    width = PER_GROUP - first
    rest = width * shards
    size = PER_GROUP + 2 * STATE
    copies = []
    for r in range(shards):
        group = (shard ^ FLIP[r]) * PAIR + 1 - core
        copies.append((xbc.at[:, channels(group, first, width)], send.at[:, r * width : (r + 1) * width]))
        for i in range(2):
            to = rest + (i * shards + r) * STATE
            copies.append((xbc.at[:, ds(INNER + (i * GROUPS + group) * STATE, STATE)], send.at[:, to : to + STATE]))
    copies.append((dt_raw, send.at[:, send.shape[1] - HEADS :]))
    for r in range(shards):
        group, to = (shard ^ FLIP[r]) * PAIR + core, r * size
        last = xbc.at[count - 16 :]
        copies.append((last.at[:, channels(group, 0, PER_GROUP)], tail.at[:, to : to + PER_GROUP]))
        for i in range(2):
            at = ds(INNER + (i * GROUPS + group) * STATE, STATE)
            start = to + PER_GROUP + i * STATE
            copies.append((last.at[:, at], tail.at[:, start : start + STATE]))
    for copy in run(copies, sems):
        copy.wait()


def taps_kernel(place, weight, bias, order, taps, offset, sems):
    copies = []
    for source, target in ((weight, taps), (bias, offset)):
        copies.append((source.at[:, channels(place[0], 0, PER_GROUP)], target.at[:, :PER_GROUP]))
        for i in range(2):
            at = ds(INNER + (i * GROUPS + place[0]) * STATE, STATE)
            start = PER_GROUP + i * STATE
            copies.append((source.at[:, at], target.at[:, start : start + STATE]))
    for copy in run(copies, sems):
        copy.wait()


def put_edge(shards, place, got, tail, out):
    count = got.shape[0]
    first = WIDTHS[0]
    size = PER_GROUP + 2 * STATE
    for r in range(shards):
        theirs = [got[count - 16 :, r * first : (r + 1) * first]]
        theirs.append(got[16 * r : 16 * r + 16, shards * first :])
        to = r * size
        for part in theirs:
            at = slice(to, to + part.shape[1])
            rows = jnp.where(place[2] == 0, part.astype(F32), tail[:, at].astype(F32))
            out[:, at] = rows[13:16].astype(BF16)
            to = at.stop


def total_of(piece):
    return WIDTHS[piece] + sum(LANES if kind == "D" else STATE for kind in RESTS[piece])


def merge_kernel(shards, plan, unread, place, xbc, dt_raw, got_first, got, edges, *refs):
    refs = refs[unread:]
    outs, sems = refs[: len(plan)], refs[-1]
    core, shard = place[2], place[4]
    count = xbc.shape[0]
    stride = PER_GROUP - WIDTHS[0]
    mine = pl.ds(pl.multiple_of(core * count, count), count)
    other = pl.ds(pl.multiple_of((1 - core) * count, count), count)
    copies, steps = [], []
    for out, (r, pieces) in zip(outs, plan):
        group = (shard ^ FLIP[r]) * PAIR + core
        to = 0
        for piece in pieces:
            first, width = sum(WIDTHS[:piece]), WIDTHS[piece]
            if piece == 0:
                source = got_first.at[:, r * width : (r + 1) * width]
            else:
                at = r * stride + first - WIDTHS[0]
                source = got.at[:, at : at + width]
            if width:
                copies.append((xbc.at[:, channels(group, first, width)], out.at[mine, to : to + width]))
                copies.append((source, out.at[other, to : to + width]))
            to += width
            for kind in RESTS[piece]:
                if kind == "D":
                    steps.append((out, r, to))
                    to += LANES
                    continue
                i = "BC".index(kind)
                at = ds(INNER + (i * GROUPS + group) * STATE, STATE)
                copies.append((xbc.at[:, at], out.at[mine, to : to + STATE]))
                at = stride * shards + (i * shards + r) * STATE
                copies.append((got.at[:, at : at + STATE], out.at[other, to : to + STATE]))
                to += STATE
    started = run(copies, sems)
    if len(refs) > len(plan) + 1:
        put_edge(shards, place, got_first, edges, refs[-2])
    if steps:
        lane = lax.broadcasted_iota(jnp.int32, (count, LANES), 1)
        per_tile = LANES * GROUPS // HEADS
        heads = HEADS // GROUPS
        for out, r, to in steps:
            group = (shard ^ FLIP[r]) * PAIR + core
            tile, shift = group // per_tile, (LANES - (group % per_tile) * heads) % LANES
            own = dt_raw[:, ds(tile * LANES, LANES)].astype(F32)
            theirs = got[:, ds(got.shape[1] - HEADS + tile * LANES, LANES)].astype(F32)
            low = jnp.where(core == 0, own, theirs)
            high = jnp.where(core == 0, theirs, own)
            packed = jnp.zeros((count // 2, LANES), F32)
            for j, rows in enumerate((low, high)):
                rows = jnp.where(lane < heads, pltpu.roll(rows, shift, 1), 0.0)
                for i in range(2):
                    part = rows[i * count // 2 : (i + 1) * count // 2]
                    packed = packed + pltpu.roll(part, (2 * j + i) * heads, 1)
            out[: count // 2, to : to + LANES] = packed.astype(BF16)
            size = PER_GROUP + 2 * STATE
            at = slice(r * size, (r + 1) * size)
            edge = jnp.concatenate([edges[:, at].astype(F32), jnp.zeros((1, size), F32)], 0)
            edge = jnp.concatenate([edge[:, q * LANES : (q + 1) * LANES] for q in range(size // LANES)], 0)
            fill = jnp.zeros((PAIR * count - count // 2 - edge.shape[0], LANES), F32)
            out[count // 2 :, to : to + LANES] = jnp.concatenate([edge, fill], 0).astype(BF16)
    for copy in started:
        copy.wait()


def view(refs, piece):
    return [(ref, total_of(2) if piece == 3 and r == NEAR else 0) for r, ref in enumerate(refs)]


def convolve_in_order(place, blocks, columns, edge, tap, bias, wide, put):
    width = columns.stop - columns.start
    count = blocks[0][0].shape[0] // PAIR
    wide[5:8, :width] = edge
    for r, (block, origin) in enumerate(blocks):
        for core in range(PAIR):
            at = pl.multiple_of((core * len(blocks) + (place[4] ^ FLIP[r])) * count + 8, 8)
            part = block[core * count : (core + 1) * count, origin + columns.start : origin + columns.stop]
            wide[pl.ds(at, count), :width] = part.astype(F32)
    tap, bias = tap * 0.5, bias * 0.5
    for start in range(0, PAIR * len(blocks) * count, count):
        acc = bias + tap[0:1] * wide[start + 5 : start + 5 + count, :width]
        acc = acc + tap[1:2] * wide[start + 6 : start + 6 + count, :width]
        acc = acc + tap[2:3] * wide[start + 7 : start + 7 + count, :width]
        acc = acc + tap[3:4] * wide[start + 8 : start + 8 + count, :width]
        put(start, count, (acc + acc * jnp.tanh(acc)).astype(BF16))


def prep_kernel(shards, place, *refs):
    blocks, (taps, offset, a_ref, bias_ref, skip_ref, order) = refs[:shards], refs[shards : shards + 6]
    b_ref, edge_ref, cum_ref, row_ref, factor_ref, tail_ref, skip_out, dt_ref, wide = refs[shards + 6 :]
    blocks = view(blocks, 1)
    start = WIDTHS[1]
    last = total_of(1) - LANES
    size = edge_ref.shape[1]
    count = blocks[0][0].shape[0] // PAIR
    half, heads = count // 2, HEADS // GROUPS
    columns = [block[:, origin + last : origin + last + LANES].astype(F32) for block, origin in blocks]
    edge = columns[0][half : half + 4 * size // LANES]
    for column in columns[1:]:
        edge = edge + column[half : half + 4 * size // LANES]
    for q in range(size // LANES):
        edge_ref[:, q * LANES : (q + 1) * LANES] = edge[4 * q : 4 * q + 4]
    for r, column in enumerate(columns):
        packed = column[:half]
        for j in range(2 * PAIR):
            at = ((j // 2) * shards + (place[4] ^ FLIP[r])) * count + (j % 2) * half
            rows = packed if j == 0 else pltpu.roll(packed, LANES - j * heads, 1)
            dt_ref[pl.ds(pl.multiple_of(at, half), half), :] = rows

    def put(start, count, value):
        b_ref[start : start + count] = value

    at = slice(PER_GROUP, PER_GROUP + STATE)
    convolve_in_order(
        place, blocks, slice(start, start + STATE), edge_ref[0:3, at], taps[:, at], offset[:, at], wide, put
    )
    per_tile = LANES * GROUPS // HEADS
    group = place[0]
    tile = group // per_tile
    shift = (LANES - (group % per_tile) * heads) % LANES

    def lanes_of(ref):
        return pltpu.roll(jnp.broadcast_to(ref[pl.ds(tile, 1), :], (8, LANES)), shift, 1)

    rate = -jnp.exp(lanes_of(a_ref)[0:1])
    raw = dt_ref[...] + lanes_of(bias_ref)[0:1]
    step = jnp.maximum(raw, 0.0) + jnp.log1p(jnp.exp(-jnp.abs(raw)))
    skip = lanes_of(skip_ref)
    skip_out[...] = jnp.concatenate(halves(jnp.concatenate([skip, skip], 0), 3), 1)
    lower = (
        lax.broadcasted_iota(jnp.int32, (BLOCK, BLOCK), 0)
        >= lax.broadcasted_iota(jnp.int32, (BLOCK, BLOCK), 1)
    ).astype(BF16)
    valid = lax.broadcasted_iota(jnp.int32, (BLOCK, LANES), 1) < heads
    for block in range(PAIR):
        at = slice(block * BLOCK, (block + 1) * BLOCK)
        here = jnp.where(valid, step[at], 1.0)
        parts = halves(here * rate, 3)
        cum = dot(lower, parts[0]) + (dot(lower, parts[1]) + dot(lower, parts[2]))
        cum = cum * LOG2E
        cum_ref[at] = cum
        row_ref[:, at] = jnp.transpose(cum - jnp.log2(here))
        factor_ref[at] = jnp.concatenate(halves(jnp.exp2(cum), 2), 1)
        tail = jnp.exp2(cum[BLOCK - 1 :] - cum) * here
        tail_ref[at] = jnp.concatenate(halves(tail, 2), 1)


def score_kernel(shards, place, *refs):
    blocks, refs = refs[:shards], refs[shards:]
    taps, offset, edge_ref, b_ref, c_ref, score_ref, wide = (*refs[:4], *refs[-3:])
    blocks = view(blocks, 3)
    start = WIDTHS[3]
    at = slice(PER_GROUP + STATE, PER_GROUP + 2 * STATE)

    def put(start, count, value):
        c_ref[start : start + count] = value

    convolve_in_order(
        place, blocks, slice(start, start + STATE), edge_ref[0:3, at], taps[:, at], offset[:, at], wide, put
    )
    for block in range(PAIR):
        at = slice(block * BLOCK, (block + 1) * BLOCK)
        score_ref[at] = lax.dot_general(
            c_ref[at], b_ref[at], (((1,), (1,)), ((), ())), preferred_element_type=F32
        )


def decay_of(ref):
    decay = ref[STATE : STATE + 16].astype(F32)
    return decay[0:1] + (decay[1:2] + decay[2:3])


def put_decay(ref, decay):
    row = lax.broadcasted_iota(jnp.int32, (16, ref.shape[1]), 0)
    high, middle, low = (part.astype(F32) for part in halves(decay, 3))
    packed = jnp.where(row == 0, high, jnp.where(row == 1, middle, jnp.where(row == 2, low, 0.0)))
    ref[STATE:] = packed.astype(BF16)


def state_kernel(shards, part, sizes, place, *refs):
    blocks, refs = refs[:shards], refs[shards:]
    taps, offset, edge_ref, b_ref, factor_ref, tail_ref = refs[:6]
    x_ref, own_ref, *sends, wide = refs[-3 - len(sizes) :]
    piece, start, width = part
    first = sum(WIDTHS[:piece]) + start
    at = slice(first, first + width)

    def put(row, count, value):
        x_ref[row : row + count] = value

    blocks = view(blocks, piece)
    columns = slice(start, start + width)
    convolve_in_order(place, blocks, columns, edge_ref[0:3, at], taps[:, at], offset[:, at], wide, put)
    expand = spread(first // HEAD_DIM, width, 2)
    both = []
    for block in range(PAIR):
        at = slice(block * BLOCK, (block + 1) * BLOCK)
        loaded = (x_ref[at].astype(F32) * dot(tail_ref[at], expand)).astype(BF16)
        both.append(
            lax.dot_general(b_ref[at], loaded, (((0,), (0,)), ((), ())), preferred_element_type=F32)
        )
    ends = [dot(factor_ref[(i + 1) * BLOCK - 16 : (i + 1) * BLOCK], expand)[15:16] for i in range(PAIR)]
    own_ref[...] = both[0]
    end = (ends[1] * both[0] + both[1]).astype(BF16)
    decay = ends[0] * ends[1]
    start = 0
    for send_ref in sends:
        at = slice(start, start + send_ref.shape[1])
        send_ref[0:STATE] = end[:, at]
        put_decay(send_ref, decay[:, at])
        start = at.stop


def combine_kernel(spans, place, *refs):
    count = len(spans)
    got, own, out_ref = refs[:count], refs[count : 2 * count], refs[-1]
    odd = place[1] % 2 == 1
    start = 0
    for got_ref, own_ref, span in zip(got, own, spans):
        at = slice(start, start + span.stop - span.start)
        theirs, mine = got_ref[:STATE, span].astype(F32), own_ref[:STATE, span].astype(F32)
        decay, other = decay_of(own_ref.at[:, span]), decay_of(got_ref.at[:, span])
        early, late = jnp.where(odd, theirs, mine), jnp.where(odd, mine, theirs)
        out_ref[:STATE, at] = (jnp.where(odd, decay, other) * early + late).astype(BF16)
        put_decay(out_ref.at[:, at], decay * other)
        start = at.stop


def mix(first_head, x_ref, cum_ref, row_ref, score_ref, skip_ref, put):
    width = x_ref.shape[1]
    half = BLOCK // 2
    expand = spread(first_head, width, 3)
    skip = dot(skip_ref[...], expand)[0:1]
    lower = lax.broadcasted_iota(jnp.int32, (half, half), 0) >= lax.broadcasted_iota(
        jnp.int32, (half, half), 1
    )
    lane = lax.broadcasted_iota(jnp.int32, (BLOCK, LANES), 1)
    for block in range(PAIR):
        base = block * BLOCK
        for tile in range(width // LANES):
            columns = slice(tile * LANES, (tile + 1) * LANES)
            x = x_ref[base : base + BLOCK, columns]
            top = skip[:, columns] * x[:half].astype(F32)
            bottom = skip[:, columns] * x[half:].astype(F32)
            for side in range(LANES // HEAD_DIM):
                head = first_head + tile * (LANES // HEAD_DIM) + side
                own = jnp.where(lane // HEAD_DIM == side, x, jnp.zeros_like(x))
                cum = cum_ref[base : base + BLOCK, head : head + 1]
                row = row_ref[head : head + 1, base : base + BLOCK]
                diag = jnp.where(lower, cum[:half] - row[:, :half], -1e30)
                mixing = jnp.exp2(diag) * score_ref[base : base + half, :half]
                top = top + dot(mixing.astype(BF16), own[:half])
                left = jnp.exp2(cum[half:] - row[:, :half]) * score_ref[base + half : base + BLOCK, :half]
                diag = jnp.where(lower, cum[half:] - row[:, half:], -1e30)
                right = jnp.exp2(diag) * score_ref[base + half : base + BLOCK, half:]
                mixing = jnp.concatenate([left.astype(BF16), right.astype(BF16)], 1)
                bottom = bottom + dot(mixing, own)
            put(block, slice(base, base + half), columns, top)
            put(block, slice(base + half, base + BLOCK), columns, bottom)


def local_kernel(first_head, x_ref, cum_ref, row_ref, score_ref, skip_ref, *refs):
    out_ref = refs[-1]

    def put(block, rows, columns, value):
        out_ref[rows, columns] = value

    mix(first_head, x_ref, cum_ref, row_ref, score_ref, skip_ref, put)


def carry(first_head, place, lasts, befores, own_ref, c_ref, factor_ref, add, keep_ref, send_ref):
    expand = spread(first_head, own_ref.shape[1], 2)
    last, before = (
        refs[0][...] if len(refs) == 1 else jnp.concatenate([ref[...] for ref in refs], 1)
        for refs in (lasts, befores)
    )
    odd, core = place[1] % 2 == 1, place[2]
    near = jnp.where(odd, last[:STATE].astype(F32), 0.0)
    held = near + jnp.where(odd, decay_of(last), 1.0) * before[:STATE].astype(F32)
    factor = dot(factor_ref[...], expand)
    outs = []
    for block in range(PAIR):
        at = slice(block * BLOCK, (block + 1) * BLOCK)
        carried = dot(c_ref[at], held.astype(BF16))
        outs.append((add[at] + factor[at] * carried).astype(BF16))
        held = factor[BLOCK - 1 : BLOCK] * held + own_ref[...]

    @pl.when(core == 0)
    def _():
        keep_ref[...] = outs[0]
        send_ref[...] = outs[1]

    @pl.when(core == 1)
    def _():
        keep_ref[...] = outs[1]
        send_ref[...] = outs[0]


def final_kernel(first_head, counts, place, *refs):
    groups = []
    for number in counts:
        groups.append(refs[:number])
        refs = refs[number:]
    carry(first_head, place, *groups, *refs[:4], *refs[-2:])


def finish_kernel(first_head, counts, place, *refs):
    groups = []
    for number in counts:
        groups.append(refs[:number])
        refs = refs[number:]
    own_ref, c_ref, factor_ref = refs[:3]
    keep_ref, send_ref, partial = refs[-3:]
    local_kernel(first_head, *refs[3:8], partial)
    carry(first_head, place, *groups, own_ref, c_ref, factor_ref, partial, keep_ref, send_ref)


def place_kernel(firsts, place, *refs):
    count = len(firsts)
    keeps, gots = refs[:count], refs[count : 2 * count]
    out, sems = refs[-2:]
    core = place[2]
    half = out.shape[1] // PAIR
    copies = []
    for first, keep, got in zip(firsts, keeps, gots):
        width = keep.shape[1]
        copies.append((keep, out.at[:, ds(core * half + first, width)]))
        copies.append((got, out.at[:, ds((1 - core) * half + first, width)]))
    for copy in run(copies, sems):
        copy.wait()


def put_in_place(firsts, shape, place, keeps, gots):
    smem, vmem, hbm = (pl.BlockSpec(memory_space=m) for m in (pltpu.SMEM, pltpu.VMEM, pltpu.HBM))
    count = len(firsts)
    return pl.pallas_call(
        functools.partial(place_kernel, firsts),
        out_shape=jax.ShapeDtypeStruct(shape, BF16),
        in_specs=[smem] + [vmem] * (2 * count),
        out_specs=hbm,
        scratch_shapes=[pltpu.SemaphoreType.DMA((2 * count,))],
        compiler_params=pltpu.CompilerParams(vmem_limit_bytes=16 << 20),
        cost_estimate=pl.CostEstimate(flops=1, bytes_accessed=1, transcendentals=0),
        name="place",
    )(place, *keeps, *gots)


class Stay:
    def __init__(self, array):
        self.array = array


def gate(blocks, order):
    anywhere = pl.BlockSpec(memory_space=pl.ANY)
    return pl.pallas_call(
        lambda *refs: None,
        out_shape=[jax.ShapeDtypeStruct(block.shape, block.dtype) for block in blocks],
        in_specs=[anywhere] * (len(blocks) + len(order)),
        out_specs=[anywhere] * len(blocks),
        input_output_aliases={i: i for i in range(len(blocks))},
        compiler_params=pltpu.CompilerParams(vmem_limit_bytes=16 << 20),
        cost_estimate=pl.CostEstimate(flops=1, bytes_accessed=1, transcendentals=0),
        name="gate",
    )(*blocks, *order)


def call(body, outs, operands, scratch=(), flops=0, transcendentals=0, name=None, limit=16 << 20):
    shapes = [jax.ShapeDtypeStruct(shape, dtype) for shape, dtype in outs]
    smem, vmem, hbm = (pl.BlockSpec(memory_space=m) for m in (pltpu.SMEM, pltpu.VMEM, pltpu.HBM))
    specs = [
        hbm if isinstance(o, Stay) else smem if o.dtype == jnp.int32 else vmem for o in operands
    ]
    moved = sum(o.size * o.dtype.itemsize for o in shapes) * 2
    return pl.pallas_call(
        body,
        out_shape=shapes,
        in_specs=specs,
        out_specs=[vmem] * len(outs),
        scratch_shapes=scratch,
        compiler_params=pltpu.CompilerParams(vmem_limit_bytes=limit),
        cost_estimate=pl.CostEstimate(flops=1, bytes_accessed=1, transcendentals=0),
        name=name,
    )(*[o.array if isinstance(o, Stay) else o for o in operands])


def paired(xbc, dt_raw, conv_weight, conv_bias, a_log, dt_bias, skip_gain):
    axes = ("ctx", "head")
    shards, length = lax.axis_size("head"), lax.axis_size("ctx")
    devices, peers = shards * length, shards * PAIR
    tok = xbc.shape[0]
    slab = tok * peers
    context, shard = lax.axis_index("ctx"), lax.axis_index("head")
    pair, core = context // PAIR, context % PAIR
    group = shard * PAIR + core
    place = jnp.stack([group, pair, core, core * shards + shard, shard]).astype(jnp.int32)

    def over(block, target):
        route = [(i, target(i)) for i in range(devices)]
        return lax.ppermute(block, axes, [(i, j) for i, j in route if j is not None and j < devices])

    def swap(block):
        return over(block, lambda i: i ^ shards)

    rows = Stay(xbc)
    size = PER_GROUP + 2 * STATE
    (sent,) = call(
        functools.partial(pack_first_kernel, shards),
        [((tok, shards * WIDTHS[0] + size - WIDTHS[0]), BF16)],
        [place, rows],
        scratch=[pltpu.SemaphoreType.DMA((4 * shards,))],
        name="pack_first",
    )
    got_first = swap(sent)
    sent, tail = call(
        functools.partial(pack_kernel, shards),
        [((tok, shards * (size - WIDTHS[0]) + HEADS), BF16), ((16, shards * size), BF16)],
        [place, rows, Stay(dt_raw), Stay(sent)],
        scratch=[pltpu.SemaphoreType.DMA((6 * shards + 1,))],
        name="pack",
    )
    got_rest = swap(sent)
    taps, offset = call(
        taps_kernel,
        [((4, size), F32), ((1, size), F32)],
        [place, Stay(conv_weight), Stay(conv_bias[None]), Stay(got_rest)],
        scratch=[pltpu.SemaphoreType.DMA((6,))],
        name="taps",
    )

    def send_on(plan, order, tail=None, edges=None):
        unused = Stay(got_first)
        parts = [p for _, pieces in plan for p in pieces]
        made = [] if tail is None else [((3, shards * size), BF16)]
        return call(
            functools.partial(merge_kernel, shards, plan, len(order)),
            [((PAIR * tok, sum(map(total_of, pieces))), BF16) for _, pieces in plan] + made,
            [
                place,
                rows,
                Stay(dt_raw) if edges is None else dt_raw,
                got_first if 0 in parts else unused,
                got_rest if any(parts) else unused,
                next((o for o in (tail, edges) if o is not None), unused),
            ]
            + [Stay(o) for o in order],
            scratch=[pltpu.SemaphoreType.DMA((sum(2 + 2 * len(RESTS[p]) for p in parts),))],
            name="merge",
        )

    def travel(blocks):
        return [blocks[0]] + [over(blocks[r], lambda i, r=r: i ^ FLIP[r]) for r in range(1, shards)]

    def plan(piece):
        return [(r, (piece,)) for r in range(shards)]

    *first_blocks, edges = send_on(plan(0), [], tail)
    message = [travel(first_blocks)]
    edges = over(edges, lambda i: i + peers if i % shards == shards - 1 else None)
    second_blocks = send_on(plan(1), [first_blocks[0]], None, edges)
    message.append(travel(second_blocks))
    third_plan = [(r, (2, 3) if r == NEAR else (2,)) for r in range(shards)]
    third_blocks = send_on(third_plan, [second_blocks[0]])
    message.append(travel(third_blocks[:1] + gate(third_blocks[1:], message[0][1:] + message[1][1:])))

    def seen(piece):
        return message[piece]

    tiles = [p.reshape(HEADS // LANES, LANES) for p in (a_log, dt_bias, skip_gain)]
    b, edge, cum, row, factor, tail, skip = call(
        functools.partial(prep_kernel, shards),
        [
            ((slab, STATE), BF16),
            ((4, size), F32),
            ((slab, LANES), F32),
            ((LANES, slab), F32),
            ((slab, 2 * LANES), BF16),
            ((slab, 2 * LANES), BF16),
            ((16, 3 * LANES), BF16),
        ],
        [place] + seen(1) + [taps, offset] + tiles + [Stay(third_blocks[0])],
        scratch=[pltpu.VMEM((slab, LANES), F32), pltpu.VMEM((slab + 8, STATE), F32)],
        name="prep",
    )
    count = len(GROUPED)
    x, sent, own, last, joined, before, keep, send = ([None] * count for _ in range(8))

    def first_head(i):
        return (sum(WIDTHS[: GROUPED[i][0]]) + GROUPED[i][1]) // HEAD_DIM

    def state_of(i, order):
        piece, _, width = GROUPED[i]
        x[i], own[i], *sent[i] = call(
            functools.partial(state_kernel, shards, GROUPED[i], FIRST_ROUND[i]),
            [((slab, width), BF16), ((STATE, width), F32)] + [((STATE + 16, w), BF16) for w in FIRST_ROUND[i]],
            [place] + seen(piece) + [taps, offset, edge, b, factor, tail] + [Stay(o) for o in order],
            scratch=[pltpu.VMEM((slab + 8, width), F32)],
            name="state",
        )
        last[i] = [over(part, lambda i: i ^ peers if i // peers != 3 else None) for part in sent[i]]

    def combine_of(i, order):
        joined[i], before[i] = [], []
        end = 0
        for width in SECOND_ROUND[i]:
            begin, end = end, end + width
            early, late, spans, first = [], [], [], 0
            for got, mine, size_of in zip(last[i], sent[i], FIRST_ROUND[i]):
                low, high = max(begin - first, 0), min(end - first, size_of)
                first += size_of
                if low < high:
                    early.append(got)
                    late.append(mine)
                    spans.append(slice(low, high))
            (total,) = call(
                functools.partial(combine_kernel, spans),
                [((STATE + 16, width), BF16)],
                [place] + early + late + [Stay(o) for o in order],
                name="combine",
            )
            joined[i].append(total)
            before[i].append(over(total, lambda i: i + 2 * peers))
            order = [total]

    def finish_of(body, i, operands, order, **more):
        keep[i], send[i] = call(
            functools.partial(body, first_head(i), (len(last[i]), len(before[i]))),
            [((BLOCK, GROUPED[i][2]), BF16)] * 2,
            [place, *last[i], *before[i], own[i], c, factor] + operands + [Stay(o) for o in order],
            name="final",
            **more,
        )

    partial = [None] * count

    def local_of(i, order):
        (partial[i],) = call(
            functools.partial(local_kernel, first_head(i)),
            [(x[i].shape, F32)],
            [x[i], cum, row, score, skip] + [Stay(o) for o in order],
            name="local",
        )

    state_of(0, [])
    own_block, *fourth_blocks = send_on([(r, (3,)) for r in range(shards) if r != NEAR], sent[0])
    fourth_blocks = gate(fourth_blocks, message[2][1:])
    fourth_blocks = [over(block, lambda i, r=r: i ^ FLIP[r]) for r, block in enumerate(fourth_blocks, 1)]
    message.append([own_block, *fourth_blocks, message[2][NEAR]])
    combine_of(0, [])
    state_of(1, joined[0])
    combine_of(1, [])
    state_of(2, joined[1] + before[0])
    state_of(3, sent[2])
    c, score = call(
        functools.partial(score_kernel, shards),
        [((slab, STATE), BF16), ((slab, BLOCK), F32)],
        [place] + seen(3) + [taps, offset, edge, b] + [Stay(o) for o in sent[3] + before[1]],
        scratch=[pltpu.VMEM((slab + 8, STATE), F32)],
        name="score",
    )

    def in_full(i, order):
        wide = [pltpu.VMEM((slab, GROUPED[i][2]), F32)]
        finish_of(finish_kernel, i, [x[i], cum, row, score, skip], order, scratch=wide)

    combine_of(2, [score])
    in_full(1, joined[2])
    combine_of(3, [keep[1]])
    in_full(0, joined[3])
    local_of(2, [keep[0]])
    local_of(3, [partial[2]])
    finish_of(final_kernel, 2, [partial[2]], [partial[3]])
    finish_of(final_kernel, 3, [partial[3]], [keep[2]])
    firsts = [first_head(i) * HEAD_DIM for i in range(count)]
    return put_in_place(firsts, (BLOCK, PAIR * PER_GROUP), place, keep, [swap(o) for o in send])


def solution(mesh):
    in_specs = (P(("ctx", "head"), None), P(("ctx", "head"), None), P(), P(), P(), P(), P())
    out_specs = P("ctx", "head")
    shards, length = mesh.shape["head"], mesh.shape["ctx"]

    def program(xbc, *rest):
        slab = xbc.shape[0] // length
        fits = shards == GROUPS // PAIR and length == 4 * PAIR and slab == BLOCK
        return jax.shard_map(
            paired if fits else on_device,
            mesh=mesh,
            in_specs=in_specs,
            out_specs=out_specs,
            check_vma=False,
        )(xbc, *rest)

    return program
```

```python
import functools

import jax
import jax.numpy as jnp
from jax import lax
from jax.experimental import pallas as pl
from jax.experimental.pallas import tpu as pltpu
from jax.sharding import PartitionSpec as P

HEADS = 256
HEAD_DIM = 64
STATE = 256
GROUPS = 8
BLOCK = 256


def from_behind(block, axis, distance):
    devices = range(lax.axis_size(axis))
    route = [(i - distance, i) for i in devices if i - distance in devices]
    return lax.ppermute(block, axis, route)


def carried_in(array, axis, combine, identity):
    length, index = (lax.axis_size(axis), lax.axis_index(axis))
    everything = jax.tree.map(lambda part: lax.all_gather(part, axis), array)
    start = jax.tree.map(
        lambda part, zero: jnp.broadcast_to(jnp.asarray(zero, part.dtype), part.shape),
        array,
        identity,
    )

    def hop(k, before):
        reached = k < index
        new = combine(before, jax.tree.map(lambda part: part[k], everything))
        return jax.tree.map(lambda a, b: jnp.where(reached, a, b), new, before)

    return lax.fori_loop(0, length, hop, start)


def convolve(rows, edge, weight, bias):
    count = rows.shape[0]
    wide = jnp.concatenate([edge, rows], 0).astype(jnp.float32)
    acc = bias[None, :] + weight[0] * wide[0:count]
    acc = acc + weight[1] * wide[1 : count + 1]
    acc = acc + weight[2] * wide[2 : count + 2]
    acc = acc + weight[3] * wide[3 : count + 3]
    return jax.nn.silu(acc).astype(jnp.bfloat16)


def rearrange_heads(rows, shards, per_dev, groups_dev, per_group):
    count = rows.shape[0]
    inner = HEADS * HEAD_DIM
    replicate_groups = max(1, per_group // per_dev)
    heads_part = rows[:, :inner].reshape(count, shards, per_dev * HEAD_DIM)
    b_part = rows[:, inner : inner + GROUPS * STATE].reshape(count, GROUPS, STATE)
    c_part = rows[:, inner + GROUPS * STATE :].reshape(count, GROUPS, STATE)
    b_part = jnp.repeat(b_part, replicate_groups, axis=1).reshape(count, shards, groups_dev * STATE)
    c_part = jnp.repeat(c_part, replicate_groups, axis=1).reshape(count, shards, groups_dev * STATE)
    return jnp.concatenate([heads_part, b_part, c_part], axis=2)


def inner_block(xs, bmat, cmat, steps, cum):
    size = xs.shape[0]
    lower = jnp.arange(size)[:, None] >= jnp.arange(size)[None, :]
    scores = jnp.einsum("qgn,kgn->gqk", cmat, bmat, preferred_element_type=jnp.float32)
    order = jnp.transpose(cum, (1, 2, 0))
    gap = order[..., :, None] - order[..., None, :]
    decay = jnp.exp(jnp.where(lower, gap, -jnp.inf))
    mixing = (scores[:, None] * decay * jnp.transpose(steps, (1, 2, 0))[..., None, :]).astype(
        jnp.bfloat16
    )
    local = jnp.einsum("gjqk,kgjp->qgjp", mixing, xs, preferred_element_type=jnp.float32)
    tail = jnp.exp(cum[size - 1][None] - cum) * steps
    loaded = (bmat[:, :, None, :].astype(jnp.float32) * tail[..., None]).astype(jnp.bfloat16)
    block_state = jnp.einsum("kgjn,kgjp->gjnp", loaded, xs, preferred_element_type=jnp.float32)
    return (local, block_state)


def on_device(xbc, dt_raw, conv_weight, conv_bias, a_log, dt_bias, skip_gain):
    tok = xbc.shape[0]
    shards = lax.axis_size("head")
    per_dev = HEADS // shards
    per_group = HEADS // GROUPS
    groups_dev = max(1, per_dev // per_group)
    heads_per_cluster = per_dev // groups_dev
    sent = rearrange_heads(xbc, shards, per_dev, groups_dev, per_group)
    mine, rates = (
        lax.all_to_all(sent, "head", split_axis=1, concat_axis=0, tiled=True),
        lax.all_to_all(
            dt_raw.reshape(tok, shards, per_dev), "head", split_axis=1, concat_axis=0, tiled=True
        ),
    )
    slab = tok * shards
    mine = mine.reshape(slab, mine.shape[2])
    rates = rates.reshape(slab, per_dev)
    shard = lax.axis_index("head")
    taps = lax.dynamic_index_in_dim(
        rearrange_heads(conv_weight, shards, per_dev, groups_dev, per_group),
        shard,
        1,
        keepdims=False,
    )
    offset = lax.dynamic_index_in_dim(
        rearrange_heads(conv_bias[None, :], shards, per_dev, groups_dev, per_group),
        shard,
        1,
        keepdims=False,
    )
    edge = from_behind(mine[slab - 3 :], "ctx", 1)
    mine = convolve(mine, edge, taps, offset[0])
    nchunk = slab // BLOCK
    width = per_dev * HEAD_DIM
    xs = mine[:, :width].reshape(nchunk, BLOCK, groups_dev, heads_per_cluster, HEAD_DIM)
    bmat = mine[:, width : width + groups_dev * STATE].reshape(nchunk, BLOCK, groups_dev, STATE)
    cmat = mine[:, width + groups_dev * STATE :].reshape(nchunk, BLOCK, groups_dev, STATE)
    first = shard * per_dev
    rate = (-jnp.exp(lax.dynamic_slice_in_dim(a_log, first, per_dev))).reshape(
        groups_dev, heads_per_cluster
    )
    bias_dt = lax.dynamic_slice_in_dim(dt_bias, first, per_dev).reshape(
        groups_dev, heads_per_cluster
    )
    skip = lax.dynamic_slice_in_dim(skip_gain, first, per_dev).reshape(
        groups_dev, heads_per_cluster
    )
    steps = jax.nn.softplus(
        rates.astype(jnp.float32).reshape(nchunk, BLOCK, groups_dev, heads_per_cluster) + bias_dt
    )
    cum = jnp.cumsum(steps * rate, axis=1)

    def block_step(carry, item):
        held, product = carry
        x_part, b_part, c_part, step_part, cum_part = item
        local, block_state = inner_block(x_part, b_part, c_part, step_part, cum_part)
        lifted = c_part.astype(jnp.float32)[:, :, None, :] * jnp.exp(cum_part)[..., None]
        carried = jnp.einsum("qgjn,gjnp->qgjp", lifted, held, precision=lax.Precision.HIGHEST)
        partial_out = local + carried + skip[..., None] * x_part.astype(jnp.float32)
        end = jnp.exp(cum_part[BLOCK - 1])
        return ((end[..., None, None] * held + block_state, product * end), (partial_out, product))

    zero_state = jnp.zeros((groups_dev, heads_per_cluster, STATE, HEAD_DIM), jnp.float32)
    unit = jnp.ones((groups_dev, heads_per_cluster), jnp.float32)
    (slab_state, slab_decay), (partials, product_in) = lax.scan(
        block_step, (zero_state, unit), (xs, bmat, cmat, steps, cum)
    )

    def combine(preceding_state, later):
        return (
            preceding_state[0] * later[0],
            later[0][..., None, None] * preceding_state[1] + later[1],
        )

    _, entering = carried_in((slab_decay, slab_state), "ctx", combine, (unit, zero_state))
    projected = jnp.einsum(
        "cqgn,gjnp->cqgjp", cmat.astype(jnp.float32), entering, precision=lax.Precision.HIGHEST
    )
    factor = jnp.exp(cum) * product_in[:, None]
    total = partials + factor[..., None] * projected
    return total.astype(jnp.bfloat16).reshape(slab, width)


PAIR = 2
LANES = 128
LOG2E = 1.4426950408889634
F32, BF16 = jnp.float32, jnp.bfloat16
WIDTHS = (512, 0, 768, 768)
RESTS = ("", "BD", "", "C")
GROUPED = ((0, 0, 512), (2, 0, 768), (3, 0, 384), (3, 384, 384))
FIRST_ROUND = ((256, 256), (384, 384), (384,), (384,))
SECOND_ROUND = ((512,), (384, 384), (384,), (384,))


FLIP = (0, 2, 3, 1)
NEAR = 3


def halves(value, count):
    parts = []
    for _ in range(count):
        part = value.astype(BF16)
        parts.append(part)
        value = value - part.astype(F32)
    return parts


def spread(first_head, width, copies):
    lane = lax.broadcasted_iota(jnp.int32, (copies * LANES, width), 0) % LANES
    column = lax.broadcasted_iota(jnp.int32, (copies * LANES, width), 1)
    return (lane == first_head + column // HEAD_DIM).astype(BF16)


def dot(a, b):
    return jnp.dot(a, b, preferred_element_type=F32)


def ds(start, width):
    return pl.ds(pl.multiple_of(start, LANES), width)


def run(copies, sems):
    started = []
    for i, (source, target) in enumerate(copies):
        copy = pltpu.make_async_copy(source, target, sems.at[i])
        copy.start()
        started.append(copy)
    return started


PER_GROUP = HEADS * HEAD_DIM // GROUPS
INNER = HEADS * HEAD_DIM


def channels(group, first, width):
    return ds(group * PER_GROUP + first, width)


def pack_first_kernel(shards, place, xbc, send, sems):
    core, shard = place[2], place[4]
    count = xbc.shape[0]
    width = WIDTHS[0]
    copies = []
    for r in range(shards):
        group = (shard ^ FLIP[r]) * PAIR + 1 - core
        copies.append((xbc.at[:, channels(group, 0, width)], send.at[:, r * width : (r + 1) * width]))
        last, rows = xbc.at[count - 16 :], slice(16 * r, 16 * r + 16)
        to = shards * width
        copies.append((last.at[:, channels(group, width, PER_GROUP - width)], send.at[rows, to : to + PER_GROUP - width]))
        to += PER_GROUP - width
        for i in range(2):
            at = ds(INNER + (i * GROUPS + group) * STATE, STATE)
            copies.append((last.at[:, at], send.at[rows, to + i * STATE : to + (i + 1) * STATE]))
    for copy in run(copies, sems):
        copy.wait()


def pack_kernel(shards, place, xbc, dt_raw, order, send, tail, sems):
    core, shard = place[2], place[4]
    count = xbc.shape[0]
    first = WIDTHS[0]
    width = PER_GROUP - first
    rest = width * shards
    size = PER_GROUP + 2 * STATE
    copies = []
    for r in range(shards):
        group = (shard ^ FLIP[r]) * PAIR + 1 - core
        copies.append((xbc.at[:, channels(group, first, width)], send.at[:, r * width : (r + 1) * width]))
        for i in range(2):
            to = rest + (i * shards + r) * STATE
            copies.append((xbc.at[:, ds(INNER + (i * GROUPS + group) * STATE, STATE)], send.at[:, to : to + STATE]))
    copies.append((dt_raw, send.at[:, send.shape[1] - HEADS :]))
    for r in range(shards):
        group, to = (shard ^ FLIP[r]) * PAIR + core, r * size
        last = xbc.at[count - 16 :]
        copies.append((last.at[:, channels(group, 0, PER_GROUP)], tail.at[:, to : to + PER_GROUP]))
        for i in range(2):
            at = ds(INNER + (i * GROUPS + group) * STATE, STATE)
            start = to + PER_GROUP + i * STATE
            copies.append((last.at[:, at], tail.at[:, start : start + STATE]))
    for copy in run(copies, sems):
        copy.wait()


def taps_kernel(place, weight, bias, order, taps, offset, sems):
    copies = []
    for source, target in ((weight, taps), (bias, offset)):
        copies.append((source.at[:, channels(place[0], 0, PER_GROUP)], target.at[:, :PER_GROUP]))
        for i in range(2):
            at = ds(INNER + (i * GROUPS + place[0]) * STATE, STATE)
            start = PER_GROUP + i * STATE
            copies.append((source.at[:, at], target.at[:, start : start + STATE]))
    for copy in run(copies, sems):
        copy.wait()


def put_edge(shards, place, got, tail, out):
    count = got.shape[0]
    first = WIDTHS[0]
    size = PER_GROUP + 2 * STATE
    for r in range(shards):
        theirs = [got[count - 16 :, r * first : (r + 1) * first]]
        theirs.append(got[16 * r : 16 * r + 16, shards * first :])
        to = r * size
        for part in theirs:
            at = slice(to, to + part.shape[1])
            rows = jnp.where(place[2] == 0, part.astype(F32), tail[:, at].astype(F32))
            out[:, at] = rows[13:16].astype(BF16)
            to = at.stop


def total_of(piece):
    return WIDTHS[piece] + sum(LANES if kind == "D" else STATE for kind in RESTS[piece])


def merge_kernel(shards, plan, unread, place, xbc, dt_raw, got_first, got, edges, *refs):
    refs = refs[unread:]
    outs, sems = refs[: len(plan)], refs[-1]
    core, shard = place[2], place[4]
    count = xbc.shape[0]
    stride = PER_GROUP - WIDTHS[0]
    mine = pl.ds(pl.multiple_of(core * count, count), count)
    other = pl.ds(pl.multiple_of((1 - core) * count, count), count)
    copies, steps = [], []
    for out, (r, pieces) in zip(outs, plan):
        group = (shard ^ FLIP[r]) * PAIR + core
        to = 0
        for piece in pieces:
            first, width = sum(WIDTHS[:piece]), WIDTHS[piece]
            if piece == 0:
                source = got_first.at[:, r * width : (r + 1) * width]
            else:
                at = r * stride + first - WIDTHS[0]
                source = got.at[:, at : at + width]
            if width:
                copies.append((xbc.at[:, channels(group, first, width)], out.at[mine, to : to + width]))
                copies.append((source, out.at[other, to : to + width]))
            to += width
            for kind in RESTS[piece]:
                if kind == "D":
                    steps.append((out, r, to))
                    to += LANES
                    continue
                i = "BC".index(kind)
                at = ds(INNER + (i * GROUPS + group) * STATE, STATE)
                copies.append((xbc.at[:, at], out.at[mine, to : to + STATE]))
                at = stride * shards + (i * shards + r) * STATE
                copies.append((got.at[:, at : at + STATE], out.at[other, to : to + STATE]))
                to += STATE
    started = run(copies, sems)
    if len(refs) > len(plan) + 1:
        put_edge(shards, place, got_first, edges, refs[-2])
    if steps:
        lane = lax.broadcasted_iota(jnp.int32, (count, LANES), 1)
        per_tile = LANES * GROUPS // HEADS
        heads = HEADS // GROUPS
        for out, r, to in steps:
            group = (shard ^ FLIP[r]) * PAIR + core
            tile, shift = group // per_tile, (LANES - (group % per_tile) * heads) % LANES
            own = dt_raw[:, ds(tile * LANES, LANES)].astype(F32)
            theirs = got[:, ds(got.shape[1] - HEADS + tile * LANES, LANES)].astype(F32)
            low = jnp.where(core == 0, own, theirs)
            high = jnp.where(core == 0, theirs, own)
            packed = jnp.zeros((count // 2, LANES), F32)
            for j, rows in enumerate((low, high)):
                rows = jnp.where(lane < heads, pltpu.roll(rows, shift, 1), 0.0)
                for i in range(2):
                    part = rows[i * count // 2 : (i + 1) * count // 2]
                    packed = packed + pltpu.roll(part, (2 * j + i) * heads, 1)
            out[: count // 2, to : to + LANES] = packed.astype(BF16)
            size = PER_GROUP + 2 * STATE
            at = slice(r * size, (r + 1) * size)
            edge = jnp.concatenate([edges[:, at].astype(F32), jnp.zeros((1, size), F32)], 0)
            edge = jnp.concatenate([edge[:, q * LANES : (q + 1) * LANES] for q in range(size // LANES)], 0)
            fill = jnp.zeros((PAIR * count - count // 2 - edge.shape[0], LANES), F32)
            out[count // 2 :, to : to + LANES] = jnp.concatenate([edge, fill], 0).astype(BF16)
    for copy in started:
        copy.wait()


def view(refs, piece):
    return [(ref, total_of(2) if piece == 3 and r == NEAR else 0) for r, ref in enumerate(refs)]


def convolve_in_order(place, blocks, columns, edge, tap, bias, wide, put):
    width = columns.stop - columns.start
    count = blocks[0][0].shape[0] // PAIR
    wide[5:8, :width] = edge
    for r, (block, origin) in enumerate(blocks):
        for core in range(PAIR):
            at = pl.multiple_of((core * len(blocks) + (place[4] ^ FLIP[r])) * count + 8, 8)
            part = block[core * count : (core + 1) * count, origin + columns.start : origin + columns.stop]
            wide[pl.ds(at, count), :width] = part.astype(F32)
    tap, bias = tap * 0.5, bias * 0.5
    for start in range(0, PAIR * len(blocks) * count, count):
        acc = bias + tap[0:1] * wide[start + 5 : start + 5 + count, :width]
        acc = acc + tap[1:2] * wide[start + 6 : start + 6 + count, :width]
        acc = acc + tap[2:3] * wide[start + 7 : start + 7 + count, :width]
        acc = acc + tap[3:4] * wide[start + 8 : start + 8 + count, :width]
        put(start, count, (acc + acc * jnp.tanh(acc)).astype(BF16))


def prep_kernel(shards, place, *refs):
    blocks, (taps, offset, a_ref, bias_ref, skip_ref, order) = refs[:shards], refs[shards : shards + 6]
    b_ref, edge_ref, cum_ref, row_ref, factor_ref, tail_ref, skip_out, dt_ref, wide = refs[shards + 6 :]
    blocks = view(blocks, 1)
    start = WIDTHS[1]
    last = total_of(1) - LANES
    size = edge_ref.shape[1]
    count = blocks[0][0].shape[0] // PAIR
    half, heads = count // 2, HEADS // GROUPS
    columns = [block[:, origin + last : origin + last + LANES].astype(F32) for block, origin in blocks]
    edge = columns[0][half : half + 4 * size // LANES]
    for column in columns[1:]:
        edge = edge + column[half : half + 4 * size // LANES]
    for q in range(size // LANES):
        edge_ref[:, q * LANES : (q + 1) * LANES] = edge[4 * q : 4 * q + 4]
    for r, column in enumerate(columns):
        packed = column[:half]
        for j in range(2 * PAIR):
            at = ((j // 2) * shards + (place[4] ^ FLIP[r])) * count + (j % 2) * half
            rows = packed if j == 0 else pltpu.roll(packed, LANES - j * heads, 1)
            dt_ref[pl.ds(pl.multiple_of(at, half), half), :] = rows

    def put(start, count, value):
        b_ref[start : start + count] = value

    at = slice(PER_GROUP, PER_GROUP + STATE)
    convolve_in_order(
        place, blocks, slice(start, start + STATE), edge_ref[0:3, at], taps[:, at], offset[:, at], wide, put
    )
    per_tile = LANES * GROUPS // HEADS
    group = place[0]
    tile = group // per_tile
    shift = (LANES - (group % per_tile) * heads) % LANES

    def lanes_of(ref):
        return pltpu.roll(jnp.broadcast_to(ref[pl.ds(tile, 1), :], (8, LANES)), shift, 1)

    rate = -jnp.exp(lanes_of(a_ref)[0:1])
    raw = dt_ref[...] + lanes_of(bias_ref)[0:1]
    step = jnp.maximum(raw, 0.0) + jnp.log1p(jnp.exp(-jnp.abs(raw)))
    skip = lanes_of(skip_ref)
    skip_out[...] = jnp.concatenate(halves(jnp.concatenate([skip, skip], 0), 3), 1)
    lower = (
        lax.broadcasted_iota(jnp.int32, (BLOCK, BLOCK), 0)
        >= lax.broadcasted_iota(jnp.int32, (BLOCK, BLOCK), 1)
    ).astype(BF16)
    valid = lax.broadcasted_iota(jnp.int32, (BLOCK, LANES), 1) < heads
    for block in range(PAIR):
        at = slice(block * BLOCK, (block + 1) * BLOCK)
        here = jnp.where(valid, step[at], 1.0)
        parts = halves(here * rate, 3)
        cum = dot(lower, parts[0]) + (dot(lower, parts[1]) + dot(lower, parts[2]))
        cum = cum * LOG2E
        cum_ref[at] = cum
        row_ref[:, at] = jnp.transpose(cum - jnp.log2(here))
        factor_ref[at] = jnp.concatenate(halves(jnp.exp2(cum), 2), 1)
        tail = jnp.exp2(cum[BLOCK - 1 :] - cum) * here
        tail_ref[at] = jnp.concatenate(halves(tail, 2), 1)


def score_kernel(shards, place, *refs):
    blocks, refs = refs[:shards], refs[shards:]
    taps, offset, edge_ref, b_ref, c_ref, score_ref, wide = (*refs[:4], *refs[-3:])
    blocks = view(blocks, 3)
    start = WIDTHS[3]
    at = slice(PER_GROUP + STATE, PER_GROUP + 2 * STATE)

    def put(start, count, value):
        c_ref[start : start + count] = value

    convolve_in_order(
        place, blocks, slice(start, start + STATE), edge_ref[0:3, at], taps[:, at], offset[:, at], wide, put
    )
    for block in range(PAIR):
        at = slice(block * BLOCK, (block + 1) * BLOCK)
        score_ref[at] = lax.dot_general(
            c_ref[at], b_ref[at], (((1,), (1,)), ((), ())), preferred_element_type=F32
        )


def decay_of(ref):
    decay = ref[STATE : STATE + 16].astype(F32)
    return decay[0:1] + (decay[1:2] + decay[2:3])


def put_decay(ref, decay):
    row = lax.broadcasted_iota(jnp.int32, (16, ref.shape[1]), 0)
    high, middle, low = (part.astype(F32) for part in halves(decay, 3))
    packed = jnp.where(row == 0, high, jnp.where(row == 1, middle, jnp.where(row == 2, low, 0.0)))
    ref[STATE:] = packed.astype(BF16)


def state_kernel(shards, part, sizes, place, *refs):
    blocks, refs = refs[:shards], refs[shards:]
    taps, offset, edge_ref, b_ref, factor_ref, tail_ref = refs[:6]
    x_ref, own_ref, *sends, wide = refs[-3 - len(sizes) :]
    piece, start, width = part
    first = sum(WIDTHS[:piece]) + start
    at = slice(first, first + width)

    def put(row, count, value):
        x_ref[row : row + count] = value

    blocks = view(blocks, piece)
    columns = slice(start, start + width)
    convolve_in_order(place, blocks, columns, edge_ref[0:3, at], taps[:, at], offset[:, at], wide, put)
    expand = spread(first // HEAD_DIM, width, 2)
    both = []
    for block in range(PAIR):
        at = slice(block * BLOCK, (block + 1) * BLOCK)
        loaded = (x_ref[at].astype(F32) * dot(tail_ref[at], expand)).astype(BF16)
        both.append(
            lax.dot_general(b_ref[at], loaded, (((0,), (0,)), ((), ())), preferred_element_type=F32)
        )
    ends = [dot(factor_ref[(i + 1) * BLOCK - 16 : (i + 1) * BLOCK], expand)[15:16] for i in range(PAIR)]
    own_ref[...] = both[0]
    end = (ends[1] * both[0] + both[1]).astype(BF16)
    decay = ends[0] * ends[1]
    start = 0
    for send_ref in sends:
        at = slice(start, start + send_ref.shape[1])
        send_ref[0:STATE] = end[:, at]
        put_decay(send_ref, decay[:, at])
        start = at.stop


def combine_kernel(spans, place, *refs):
    count = len(spans)
    got, own, out_ref = refs[:count], refs[count : 2 * count], refs[-1]
    odd = place[1] % 2 == 1
    start = 0
    for got_ref, own_ref, span in zip(got, own, spans):
        at = slice(start, start + span.stop - span.start)
        theirs, mine = got_ref[:STATE, span].astype(F32), own_ref[:STATE, span].astype(F32)
        decay, other = decay_of(own_ref.at[:, span]), decay_of(got_ref.at[:, span])
        early, late = jnp.where(odd, theirs, mine), jnp.where(odd, mine, theirs)
        out_ref[:STATE, at] = (jnp.where(odd, decay, other) * early + late).astype(BF16)
        put_decay(out_ref.at[:, at], decay * other)
        start = at.stop


def mix(first_head, x_ref, cum_ref, row_ref, score_ref, skip_ref, put):
    width = x_ref.shape[1]
    half = BLOCK // 2
    expand = spread(first_head, width, 3)
    skip = dot(skip_ref[...], expand)[0:1]
    lower = lax.broadcasted_iota(jnp.int32, (half, half), 0) >= lax.broadcasted_iota(
        jnp.int32, (half, half), 1
    )
    lane = lax.broadcasted_iota(jnp.int32, (BLOCK, LANES), 1)
    for block in range(PAIR):
        base = block * BLOCK
        for tile in range(width // LANES):
            columns = slice(tile * LANES, (tile + 1) * LANES)
            x = x_ref[base : base + BLOCK, columns]
            top = skip[:, columns] * x[:half].astype(F32)
            bottom = skip[:, columns] * x[half:].astype(F32)
            for side in range(LANES // HEAD_DIM):
                head = first_head + tile * (LANES // HEAD_DIM) + side
                own = jnp.where(lane // HEAD_DIM == side, x, jnp.zeros_like(x))
                cum = cum_ref[base : base + BLOCK, head : head + 1]
                row = row_ref[head : head + 1, base : base + BLOCK]
                diag = jnp.where(lower, cum[:half] - row[:, :half], -1e30)
                mixing = jnp.exp2(diag) * score_ref[base : base + half, :half]
                top = top + dot(mixing.astype(BF16), own[:half])
                left = jnp.exp2(cum[half:] - row[:, :half]) * score_ref[base + half : base + BLOCK, :half]
                diag = jnp.where(lower, cum[half:] - row[:, half:], -1e30)
                right = jnp.exp2(diag) * score_ref[base + half : base + BLOCK, half:]
                mixing = jnp.concatenate([left.astype(BF16), right.astype(BF16)], 1)
                bottom = bottom + dot(mixing, own)
            put(block, slice(base, base + half), columns, top)
            put(block, slice(base + half, base + BLOCK), columns, bottom)


def local_kernel(first_head, x_ref, cum_ref, row_ref, score_ref, skip_ref, *refs):
    out_ref = refs[-1]

    def put(block, rows, columns, value):
        out_ref[rows, columns] = value

    mix(first_head, x_ref, cum_ref, row_ref, score_ref, skip_ref, put)


def carry(first_head, place, lasts, befores, own_ref, c_ref, factor_ref, add, keep_ref, send_ref):
    expand = spread(first_head, own_ref.shape[1], 2)
    last, before = (
        refs[0][...] if len(refs) == 1 else jnp.concatenate([ref[...] for ref in refs], 1)
        for refs in (lasts, befores)
    )
    odd, core = place[1] % 2 == 1, place[2]
    near = jnp.where(odd, last[:STATE].astype(F32), 0.0)
    held = near + jnp.where(odd, decay_of(last), 1.0) * before[:STATE].astype(F32)
    factor = dot(factor_ref[...], expand)
    outs = []
    for block in range(PAIR):
        at = slice(block * BLOCK, (block + 1) * BLOCK)
        carried = dot(c_ref[at], held.astype(BF16))
        outs.append((add[at] + factor[at] * carried).astype(BF16))
        held = factor[BLOCK - 1 : BLOCK] * held + own_ref[...]

    @pl.when(core == 0)
    def _():
        keep_ref[...] = outs[0]
        send_ref[...] = outs[1]

    @pl.when(core == 1)
    def _():
        keep_ref[...] = outs[1]
        send_ref[...] = outs[0]


def final_kernel(first_head, counts, place, *refs):
    groups = []
    for number in counts:
        groups.append(refs[:number])
        refs = refs[number:]
    carry(first_head, place, *groups, *refs[:4], *refs[-2:])


def finish_kernel(first_head, counts, place, *refs):
    groups = []
    for number in counts:
        groups.append(refs[:number])
        refs = refs[number:]
    own_ref, c_ref, factor_ref = refs[:3]
    keep_ref, send_ref, partial = refs[-3:]
    local_kernel(first_head, *refs[3:8], partial)
    carry(first_head, place, *groups, own_ref, c_ref, factor_ref, partial, keep_ref, send_ref)


def place_kernel(firsts, place, *refs):
    count = len(firsts)
    keeps, gots = refs[:count], refs[count : 2 * count]
    out, sems = refs[-2:]
    core = place[2]
    half = out.shape[1] // PAIR
    copies = []
    for first, keep, got in zip(firsts, keeps, gots):
        width = keep.shape[1]
        copies.append((keep, out.at[:, ds(core * half + first, width)]))
        copies.append((got, out.at[:, ds((1 - core) * half + first, width)]))
    for copy in run(copies, sems):
        copy.wait()


def put_in_place(firsts, shape, place, keeps, gots):
    smem, vmem, hbm = (pl.BlockSpec(memory_space=m) for m in (pltpu.SMEM, pltpu.VMEM, pltpu.HBM))
    count = len(firsts)
    return pl.pallas_call(
        functools.partial(place_kernel, firsts),
        out_shape=jax.ShapeDtypeStruct(shape, BF16),
        in_specs=[smem] + [vmem] * (2 * count),
        out_specs=hbm,
        scratch_shapes=[pltpu.SemaphoreType.DMA((2 * count,))],
        compiler_params=pltpu.CompilerParams(vmem_limit_bytes=16 << 20),
        cost_estimate=pl.CostEstimate(flops=1, bytes_accessed=1, transcendentals=0),
        name="place",
    )(place, *keeps, *gots)


class Stay:
    def __init__(self, array):
        self.array = array


def gate(blocks, order):
    anywhere = pl.BlockSpec(memory_space=pl.ANY)
    return pl.pallas_call(
        lambda *refs: None,
        out_shape=[jax.ShapeDtypeStruct(block.shape, block.dtype) for block in blocks],
        in_specs=[anywhere] * (len(blocks) + len(order)),
        out_specs=[anywhere] * len(blocks),
        input_output_aliases={i: i for i in range(len(blocks))},
        compiler_params=pltpu.CompilerParams(vmem_limit_bytes=16 << 20),
        cost_estimate=pl.CostEstimate(flops=1, bytes_accessed=1, transcendentals=0),
        name="gate",
    )(*blocks, *order)


def call(body, outs, operands, scratch=(), flops=0, transcendentals=0, name=None, limit=16 << 20):
    shapes = [jax.ShapeDtypeStruct(shape, dtype) for shape, dtype in outs]
    smem, vmem, hbm = (pl.BlockSpec(memory_space=m) for m in (pltpu.SMEM, pltpu.VMEM, pltpu.HBM))
    specs = [
        hbm if isinstance(o, Stay) else smem if o.dtype == jnp.int32 else vmem for o in operands
    ]
    moved = sum(o.size * o.dtype.itemsize for o in shapes) * 2
    return pl.pallas_call(
        body,
        out_shape=shapes,
        in_specs=specs,
        out_specs=[vmem] * len(outs),
        scratch_shapes=scratch,
        compiler_params=pltpu.CompilerParams(vmem_limit_bytes=limit),
        cost_estimate=pl.CostEstimate(flops=1, bytes_accessed=1, transcendentals=0),
        name=name,
    )(*[o.array if isinstance(o, Stay) else o for o in operands])


def paired(xbc, dt_raw, conv_weight, conv_bias, a_log, dt_bias, skip_gain):
    axes = ("ctx", "head")
    shards, length = lax.axis_size("head"), lax.axis_size("ctx")
    devices, peers = shards * length, shards * PAIR
    tok = xbc.shape[0]
    slab = tok * peers
    context, shard = lax.axis_index("ctx"), lax.axis_index("head")
    pair, core = context // PAIR, context % PAIR
    group = shard * PAIR + core
    place = jnp.stack([group, pair, core, core * shards + shard, shard]).astype(jnp.int32)

    def over(block, target):
        route = [(i, target(i)) for i in range(devices)]
        return lax.ppermute(block, axes, [(i, j) for i, j in route if j is not None and j < devices])

    def swap(block):
        return over(block, lambda i: i ^ shards)

    rows = Stay(xbc)
    size = PER_GROUP + 2 * STATE
    (sent,) = call(
        functools.partial(pack_first_kernel, shards),
        [((tok, shards * WIDTHS[0] + size - WIDTHS[0]), BF16)],
        [place, rows],
        scratch=[pltpu.SemaphoreType.DMA((4 * shards,))],
        name="pack_first",
    )
    got_first = swap(sent)
    sent, tail = call(
        functools.partial(pack_kernel, shards),
        [((tok, shards * (size - WIDTHS[0]) + HEADS), BF16), ((16, shards * size), BF16)],
        [place, rows, Stay(dt_raw), Stay(sent)],
        scratch=[pltpu.SemaphoreType.DMA((6 * shards + 1,))],
        name="pack",
    )
    got_rest = swap(sent)
    taps, offset = call(
        taps_kernel,
        [((4, size), F32), ((1, size), F32)],
        [place, Stay(conv_weight), Stay(conv_bias[None]), Stay(got_rest)],
        scratch=[pltpu.SemaphoreType.DMA((6,))],
        name="taps",
    )

    def send_on(plan, order, tail=None, edges=None):
        unused = Stay(got_first)
        parts = [p for _, pieces in plan for p in pieces]
        made = [] if tail is None else [((3, shards * size), BF16)]
        return call(
            functools.partial(merge_kernel, shards, plan, len(order)),
            [((PAIR * tok, sum(map(total_of, pieces))), BF16) for _, pieces in plan] + made,
            [
                place,
                rows,
                Stay(dt_raw) if edges is None else dt_raw,
                got_first if 0 in parts else unused,
                got_rest if any(parts) else unused,
                next((o for o in (tail, edges) if o is not None), unused),
            ]
            + [Stay(o) for o in order],
            scratch=[pltpu.SemaphoreType.DMA((sum(2 + 2 * len(RESTS[p]) for p in parts),))],
            name="merge",
        )

    def travel(blocks):
        return [blocks[0]] + [over(blocks[r], lambda i, r=r: i ^ FLIP[r]) for r in range(1, shards)]

    def plan(piece):
        return [(r, (piece,)) for r in range(shards)]

    *first_blocks, edges = send_on(plan(0), [], tail)
    message = [travel(first_blocks)]
    edges = over(edges, lambda i: i + peers if i % shards == shards - 1 else None)
    second_blocks = send_on(plan(1), [first_blocks[0]], None, edges)
    message.append(travel(second_blocks))
    third_plan = [(r, (2, 3) if r == NEAR else (2,)) for r in range(shards)]
    third_blocks = send_on(third_plan, [second_blocks[0]])
    message.append(travel(third_blocks[:1] + gate(third_blocks[1:], message[0][1:] + message[1][1:] + [taps])))

    def seen(piece):
        return message[piece]

    tiles = [p.reshape(HEADS // LANES, LANES) for p in (a_log, dt_bias, skip_gain)]
    b, edge, cum, row, factor, tail, skip = call(
        functools.partial(prep_kernel, shards),
        [
            ((slab, STATE), BF16),
            ((4, size), F32),
            ((slab, LANES), F32),
            ((LANES, slab), F32),
            ((slab, 2 * LANES), BF16),
            ((slab, 2 * LANES), BF16),
            ((16, 3 * LANES), BF16),
        ],
        [place] + seen(1) + [taps, offset] + tiles + [Stay(third_blocks[0])],
        scratch=[pltpu.VMEM((slab, LANES), F32), pltpu.VMEM((slab + 8, STATE), F32)],
        name="prep",
    )
    count = len(GROUPED)
    x, sent, own, last, joined, before, keep, send = ([None] * count for _ in range(8))

    def first_head(i):
        return (sum(WIDTHS[: GROUPED[i][0]]) + GROUPED[i][1]) // HEAD_DIM

    def state_of(i, order):
        piece, _, width = GROUPED[i]
        x[i], own[i], *sent[i] = call(
            functools.partial(state_kernel, shards, GROUPED[i], FIRST_ROUND[i]),
            [((slab, width), BF16), ((STATE, width), F32)] + [((STATE + 16, w), BF16) for w in FIRST_ROUND[i]],
            [place] + seen(piece) + [taps, offset, edge, b, factor, tail] + [Stay(o) for o in order],
            scratch=[pltpu.VMEM((slab + 8, width), F32)],
            name="state",
        )
        last[i] = [over(part, lambda i: i ^ peers if i // peers != 3 else None) for part in sent[i]]

    def combine_of(i, order):
        joined[i], before[i] = [], []
        end = 0
        for width in SECOND_ROUND[i]:
            begin, end = end, end + width
            early, late, spans, first = [], [], [], 0
            for got, mine, size_of in zip(last[i], sent[i], FIRST_ROUND[i]):
                low, high = max(begin - first, 0), min(end - first, size_of)
                first += size_of
                if low < high:
                    early.append(got)
                    late.append(mine)
                    spans.append(slice(low, high))
            (total,) = call(
                functools.partial(combine_kernel, spans),
                [((STATE + 16, width), BF16)],
                [place] + early + late + [Stay(o) for o in order],
                name="combine",
            )
            joined[i].append(total)
            before[i].append(over(total, lambda i: i + 2 * peers))
            order = [total]

    def finish_of(body, i, operands, order, **more):
        keep[i], send[i] = call(
            functools.partial(body, first_head(i), (len(last[i]), len(before[i]))),
            [((BLOCK, GROUPED[i][2]), BF16)] * 2,
            [place, *last[i], *before[i], own[i], c, factor] + operands + [Stay(o) for o in order],
            name="final",
            **more,
        )

    partial = [None] * count

    def local_of(i, order):
        (partial[i],) = call(
            functools.partial(local_kernel, first_head(i)),
            [(x[i].shape, F32)],
            [x[i], cum, row, score, skip] + [Stay(o) for o in order],
            name="local",
        )

    state_of(0, [])
    own_block, *fourth_blocks = send_on([(r, (3,)) for r in range(shards) if r != NEAR], sent[0])
    fourth_blocks = gate(fourth_blocks, message[2][1:])
    fourth_blocks = [over(block, lambda i, r=r: i ^ FLIP[r]) for r, block in enumerate(fourth_blocks, 1)]
    message.append([own_block, *fourth_blocks, message[2][NEAR]])
    combine_of(0, [own_block])
    state_of(1, joined[0])
    combine_of(1, [])
    state_of(2, joined[1] + before[0])
    c, score = call(
        functools.partial(score_kernel, shards),
        [((slab, STATE), BF16), ((slab, BLOCK), F32)],
        [place] + seen(3) + [taps, offset, edge, b] + [Stay(o) for o in sent[2]],
        scratch=[pltpu.VMEM((slab + 8, STATE), F32)],
        name="score",
    )
    local_of(0, [])
    state_of(3, [partial[0]])

    def in_full(i, order):
        wide = [pltpu.VMEM((slab, GROUPED[i][2]), F32)]
        finish_of(finish_kernel, i, [x[i], cum, row, score, skip], order, scratch=wide)

    combine_of(2, sent[3] + before[1])
    in_full(1, joined[2])
    combine_of(3, [keep[1]])
    local_of(2, joined[3])
    local_of(3, [partial[2]])
    finish_of(final_kernel, 0, [partial[0]], [partial[3]])
    finish_of(final_kernel, 2, [partial[2]], [keep[0]])
    finish_of(final_kernel, 3, [partial[3]], [keep[2]])
    firsts = [first_head(i) * HEAD_DIM for i in range(count)]
    return put_in_place(firsts, (BLOCK, PAIR * PER_GROUP), place, keep, [swap(o) for o in send])


def solution(mesh):
    in_specs = (P(("ctx", "head"), None), P(("ctx", "head"), None), P(), P(), P(), P(), P())
    out_specs = P("ctx", "head")
    shards, length = mesh.shape["head"], mesh.shape["ctx"]

    def program(xbc, *rest):
        slab = xbc.shape[0] // length
        fits = shards == GROUPS // PAIR and length == 4 * PAIR and slab == BLOCK
        return jax.shard_map(
            paired if fits else on_device,
            mesh=mesh,
            in_specs=in_specs,
            out_specs=out_specs,
            check_vma=False,
        )(xbc, *rest)

    return program
```

```python
import functools

import jax
import jax.numpy as jnp
from jax import lax
from jax.experimental import pallas as pl
from jax.experimental.pallas import tpu as pltpu
from jax.sharding import PartitionSpec as P

HEADS = 256
HEAD_DIM = 64
STATE = 256
GROUPS = 8
BLOCK = 256


def from_behind(block, axis, distance):
    devices = range(lax.axis_size(axis))
    route = [(i - distance, i) for i in devices if i - distance in devices]
    return lax.ppermute(block, axis, route)


def carried_in(array, axis, combine, identity):
    length, index = (lax.axis_size(axis), lax.axis_index(axis))
    everything = jax.tree.map(lambda part: lax.all_gather(part, axis), array)
    start = jax.tree.map(
        lambda part, zero: jnp.broadcast_to(jnp.asarray(zero, part.dtype), part.shape),
        array,
        identity,
    )

    def hop(k, before):
        reached = k < index
        new = combine(before, jax.tree.map(lambda part: part[k], everything))
        return jax.tree.map(lambda a, b: jnp.where(reached, a, b), new, before)

    return lax.fori_loop(0, length, hop, start)


def convolve(rows, edge, weight, bias):
    count = rows.shape[0]
    wide = jnp.concatenate([edge, rows], 0).astype(jnp.float32)
    acc = bias[None, :] + weight[0] * wide[0:count]
    acc = acc + weight[1] * wide[1 : count + 1]
    acc = acc + weight[2] * wide[2 : count + 2]
    acc = acc + weight[3] * wide[3 : count + 3]
    return jax.nn.silu(acc).astype(jnp.bfloat16)


def rearrange_heads(rows, shards, per_dev, groups_dev, per_group):
    count = rows.shape[0]
    inner = HEADS * HEAD_DIM
    replicate_groups = max(1, per_group // per_dev)
    heads_part = rows[:, :inner].reshape(count, shards, per_dev * HEAD_DIM)
    b_part = rows[:, inner : inner + GROUPS * STATE].reshape(count, GROUPS, STATE)
    c_part = rows[:, inner + GROUPS * STATE :].reshape(count, GROUPS, STATE)
    b_part = jnp.repeat(b_part, replicate_groups, axis=1).reshape(count, shards, groups_dev * STATE)
    c_part = jnp.repeat(c_part, replicate_groups, axis=1).reshape(count, shards, groups_dev * STATE)
    return jnp.concatenate([heads_part, b_part, c_part], axis=2)


def inner_block(xs, bmat, cmat, steps, cum):
    size = xs.shape[0]
    lower = jnp.arange(size)[:, None] >= jnp.arange(size)[None, :]
    scores = jnp.einsum("qgn,kgn->gqk", cmat, bmat, preferred_element_type=jnp.float32)
    order = jnp.transpose(cum, (1, 2, 0))
    gap = order[..., :, None] - order[..., None, :]
    decay = jnp.exp(jnp.where(lower, gap, -jnp.inf))
    mixing = (scores[:, None] * decay * jnp.transpose(steps, (1, 2, 0))[..., None, :]).astype(
        jnp.bfloat16
    )
    local = jnp.einsum("gjqk,kgjp->qgjp", mixing, xs, preferred_element_type=jnp.float32)
    tail = jnp.exp(cum[size - 1][None] - cum) * steps
    loaded = (bmat[:, :, None, :].astype(jnp.float32) * tail[..., None]).astype(jnp.bfloat16)
    block_state = jnp.einsum("kgjn,kgjp->gjnp", loaded, xs, preferred_element_type=jnp.float32)
    return (local, block_state)


def on_device(xbc, dt_raw, conv_weight, conv_bias, a_log, dt_bias, skip_gain):
    tok = xbc.shape[0]
    shards = lax.axis_size("head")
    per_dev = HEADS // shards
    per_group = HEADS // GROUPS
    groups_dev = max(1, per_dev // per_group)
    heads_per_cluster = per_dev // groups_dev
    sent = rearrange_heads(xbc, shards, per_dev, groups_dev, per_group)
    mine, rates = (
        lax.all_to_all(sent, "head", split_axis=1, concat_axis=0, tiled=True),
        lax.all_to_all(
            dt_raw.reshape(tok, shards, per_dev), "head", split_axis=1, concat_axis=0, tiled=True
        ),
    )
    slab = tok * shards
    mine = mine.reshape(slab, mine.shape[2])
    rates = rates.reshape(slab, per_dev)
    shard = lax.axis_index("head")
    taps = lax.dynamic_index_in_dim(
        rearrange_heads(conv_weight, shards, per_dev, groups_dev, per_group),
        shard,
        1,
        keepdims=False,
    )
    offset = lax.dynamic_index_in_dim(
        rearrange_heads(conv_bias[None, :], shards, per_dev, groups_dev, per_group),
        shard,
        1,
        keepdims=False,
    )
    edge = from_behind(mine[slab - 3 :], "ctx", 1)
    mine = convolve(mine, edge, taps, offset[0])
    nchunk = slab // BLOCK
    width = per_dev * HEAD_DIM
    xs = mine[:, :width].reshape(nchunk, BLOCK, groups_dev, heads_per_cluster, HEAD_DIM)
    bmat = mine[:, width : width + groups_dev * STATE].reshape(nchunk, BLOCK, groups_dev, STATE)
    cmat = mine[:, width + groups_dev * STATE :].reshape(nchunk, BLOCK, groups_dev, STATE)
    first = shard * per_dev
    rate = (-jnp.exp(lax.dynamic_slice_in_dim(a_log, first, per_dev))).reshape(
        groups_dev, heads_per_cluster
    )
    bias_dt = lax.dynamic_slice_in_dim(dt_bias, first, per_dev).reshape(
        groups_dev, heads_per_cluster
    )
    skip = lax.dynamic_slice_in_dim(skip_gain, first, per_dev).reshape(
        groups_dev, heads_per_cluster
    )
    steps = jax.nn.softplus(
        rates.astype(jnp.float32).reshape(nchunk, BLOCK, groups_dev, heads_per_cluster) + bias_dt
    )
    cum = jnp.cumsum(steps * rate, axis=1)

    def block_step(carry, item):
        held, product = carry
        x_part, b_part, c_part, step_part, cum_part = item
        local, block_state = inner_block(x_part, b_part, c_part, step_part, cum_part)
        lifted = c_part.astype(jnp.float32)[:, :, None, :] * jnp.exp(cum_part)[..., None]
        carried = jnp.einsum("qgjn,gjnp->qgjp", lifted, held, precision=lax.Precision.HIGHEST)
        partial_out = local + carried + skip[..., None] * x_part.astype(jnp.float32)
        end = jnp.exp(cum_part[BLOCK - 1])
        return ((end[..., None, None] * held + block_state, product * end), (partial_out, product))

    zero_state = jnp.zeros((groups_dev, heads_per_cluster, STATE, HEAD_DIM), jnp.float32)
    unit = jnp.ones((groups_dev, heads_per_cluster), jnp.float32)
    (slab_state, slab_decay), (partials, product_in) = lax.scan(
        block_step, (zero_state, unit), (xs, bmat, cmat, steps, cum)
    )

    def combine(preceding_state, later):
        return (
            preceding_state[0] * later[0],
            later[0][..., None, None] * preceding_state[1] + later[1],
        )

    _, entering = carried_in((slab_decay, slab_state), "ctx", combine, (unit, zero_state))
    projected = jnp.einsum(
        "cqgn,gjnp->cqgjp", cmat.astype(jnp.float32), entering, precision=lax.Precision.HIGHEST
    )
    factor = jnp.exp(cum) * product_in[:, None]
    total = partials + factor[..., None] * projected
    return total.astype(jnp.bfloat16).reshape(slab, width)


PAIR = 2
LANES = 128
LOG2E = 1.4426950408889634
F32, BF16 = jnp.float32, jnp.bfloat16
WIDTHS = (512, 0, 768, 768)
RESTS = ("", "BD", "", "C")
GROUPED = ((0, 0, 512), (2, 0, 768), (3, 0, 384), (3, 384, 384))
FIRST_ROUND = ((256, 256), (384, 384), (384,), (384,))
SECOND_ROUND = ((512,), (384, 384), (384,), (384,))


FLIP = (0, 2, 3, 1)
NEAR = 3


def halves(value, count):
    parts = []
    for _ in range(count):
        part = value.astype(BF16)
        parts.append(part)
        value = value - part.astype(F32)
    return parts


def spread(first_head, width, copies):
    lane = lax.broadcasted_iota(jnp.int32, (copies * LANES, width), 0) % LANES
    column = lax.broadcasted_iota(jnp.int32, (copies * LANES, width), 1)
    return (lane == first_head + column // HEAD_DIM).astype(BF16)


def dot(a, b):
    return jnp.dot(a, b, preferred_element_type=F32)


def ds(start, width):
    return pl.ds(pl.multiple_of(start, LANES), width)


def run(copies, sems):
    started = []
    for i, (source, target) in enumerate(copies):
        copy = pltpu.make_async_copy(source, target, sems.at[i])
        copy.start()
        started.append(copy)
    return started


PER_GROUP = HEADS * HEAD_DIM // GROUPS
INNER = HEADS * HEAD_DIM


def channels(group, first, width):
    return ds(group * PER_GROUP + first, width)


def pack_first_kernel(shards, place, xbc, send, sems):
    core, shard = place[2], place[4]
    width = WIDTHS[0]
    copies = []
    for r in range(shards):
        group = (shard ^ FLIP[r]) * PAIR + 1 - core
        copies.append((xbc.at[:, channels(group, 0, width)], send.at[:, r * width : (r + 1) * width]))
    for copy in run(copies, sems):
        copy.wait()


def pack_kernel(shards, place, xbc, dt_raw, order, send, tail, sems):
    core, shard = place[2], place[4]
    count = xbc.shape[0]
    first = WIDTHS[0]
    width = PER_GROUP - first
    rest = width * shards
    size = PER_GROUP + 2 * STATE
    copies = []
    for r in range(shards):
        group = (shard ^ FLIP[r]) * PAIR + 1 - core
        copies.append((xbc.at[:, channels(group, first, width)], send.at[:, r * width : (r + 1) * width]))
        for i in range(2):
            to = rest + (i * shards + r) * STATE
            copies.append((xbc.at[:, ds(INNER + (i * GROUPS + group) * STATE, STATE)], send.at[:, to : to + STATE]))
    copies.append((dt_raw, send.at[:, send.shape[1] - HEADS :]))
    for r in range(shards):
        group, to = (shard ^ FLIP[r]) * PAIR + core, r * size
        last = xbc.at[count - 16 :]
        copies.append((last.at[:, channels(group, 0, PER_GROUP)], tail.at[:, to : to + PER_GROUP]))
        for i in range(2):
            at = ds(INNER + (i * GROUPS + group) * STATE, STATE)
            start = to + PER_GROUP + i * STATE
            copies.append((last.at[:, at], tail.at[:, start : start + STATE]))
    for copy in run(copies, sems):
        copy.wait()


def taps_kernel(place, weight, bias, order, taps, offset, sems):
    copies = []
    for source, target in ((weight, taps), (bias, offset)):
        copies.append((source.at[:, channels(place[0], 0, PER_GROUP)], target.at[:, :PER_GROUP]))
        for i in range(2):
            at = ds(INNER + (i * GROUPS + place[0]) * STATE, STATE)
            start = PER_GROUP + i * STATE
            copies.append((source.at[:, at], target.at[:, start : start + STATE]))
    for copy in run(copies, sems):
        copy.wait()


def edge_kernel(shards, place, got_first, got, tail, out):
    count = got.shape[0]
    first = WIDTHS[0]
    width = PER_GROUP - first
    size = PER_GROUP + 2 * STATE
    for r in range(shards):
        theirs = [(got_first, r * first, first), (got, r * width, width)]
        theirs += [(got, width * shards + (i * shards + r) * STATE, STATE) for i in range(2)]
        to = r * size
        for ref, start, size_of in theirs:
            a = ref[count - 16 :, start : start + size_of].astype(F32)
            b = tail[:, to : to + size_of].astype(F32)
            out[:, to : to + size_of] = jnp.where(place[2] == 0, a, b)[13:16].astype(BF16)
            to += size_of


def total_of(piece):
    return WIDTHS[piece] + sum(LANES if kind == "D" else STATE for kind in RESTS[piece])


def merge_kernel(shards, plan, unread, place, xbc, dt_raw, got_first, got, edges, *refs):
    refs = refs[unread:]
    outs, sems = refs[: len(plan)], refs[-1]
    core, shard = place[2], place[4]
    count = xbc.shape[0]
    stride = PER_GROUP - WIDTHS[0]
    mine = pl.ds(pl.multiple_of(core * count, count), count)
    other = pl.ds(pl.multiple_of((1 - core) * count, count), count)
    copies, steps = [], []
    for out, (r, pieces) in zip(outs, plan):
        group = (shard ^ FLIP[r]) * PAIR + core
        to = 0
        for piece in pieces:
            first, width = sum(WIDTHS[:piece]), WIDTHS[piece]
            if piece == 0:
                source = got_first.at[:, r * width : (r + 1) * width]
            else:
                at = r * stride + first - WIDTHS[0]
                source = got.at[:, at : at + width]
            if width:
                copies.append((xbc.at[:, channels(group, first, width)], out.at[mine, to : to + width]))
                copies.append((source, out.at[other, to : to + width]))
            to += width
            for kind in RESTS[piece]:
                if kind == "D":
                    steps.append((out, r, to))
                    to += LANES
                    continue
                i = "BC".index(kind)
                at = ds(INNER + (i * GROUPS + group) * STATE, STATE)
                copies.append((xbc.at[:, at], out.at[mine, to : to + STATE]))
                at = stride * shards + (i * shards + r) * STATE
                copies.append((got.at[:, at : at + STATE], out.at[other, to : to + STATE]))
                to += STATE
    started = run(copies, sems)
    if steps:
        lane = lax.broadcasted_iota(jnp.int32, (count, LANES), 1)
        per_tile = LANES * GROUPS // HEADS
        heads = HEADS // GROUPS
        for out, r, to in steps:
            group = (shard ^ FLIP[r]) * PAIR + core
            tile, shift = group // per_tile, (LANES - (group % per_tile) * heads) % LANES
            own = dt_raw[:, ds(tile * LANES, LANES)].astype(F32)
            theirs = got[:, ds(got.shape[1] - HEADS + tile * LANES, LANES)].astype(F32)
            low = jnp.where(core == 0, own, theirs)
            high = jnp.where(core == 0, theirs, own)
            packed = jnp.zeros((count // 2, LANES), F32)
            for j, rows in enumerate((low, high)):
                rows = jnp.where(lane < heads, pltpu.roll(rows, shift, 1), 0.0)
                for i in range(2):
                    part = rows[i * count // 2 : (i + 1) * count // 2]
                    packed = packed + pltpu.roll(part, (2 * j + i) * heads, 1)
            out[: count // 2, to : to + LANES] = packed.astype(BF16)
            size = PER_GROUP + 2 * STATE
            at = slice(r * size, (r + 1) * size)
            edge = jnp.concatenate([edges[:, at].astype(F32), jnp.zeros((1, size), F32)], 0)
            edge = jnp.concatenate([edge[:, q * LANES : (q + 1) * LANES] for q in range(size // LANES)], 0)
            fill = jnp.zeros((PAIR * count - count // 2 - edge.shape[0], LANES), F32)
            out[count // 2 :, to : to + LANES] = jnp.concatenate([edge, fill], 0).astype(BF16)
    for copy in started:
        copy.wait()


def view(refs, piece):
    return [(ref, total_of(2) if piece == 3 and r == NEAR else 0) for r, ref in enumerate(refs)]


def convolve_in_order(place, blocks, columns, edge, tap, bias, wide, put):
    width = columns.stop - columns.start
    count = blocks[0][0].shape[0] // PAIR
    wide[5:8, :width] = edge
    for r, (block, origin) in enumerate(blocks):
        for core in range(PAIR):
            at = pl.multiple_of((core * len(blocks) + (place[4] ^ FLIP[r])) * count + 8, 8)
            part = block[core * count : (core + 1) * count, origin + columns.start : origin + columns.stop]
            wide[pl.ds(at, count), :width] = part.astype(F32)
    tap, bias = tap * 0.5, bias * 0.5
    for start in range(0, PAIR * len(blocks) * count, count):
        acc = bias + tap[0:1] * wide[start + 5 : start + 5 + count, :width]
        acc = acc + tap[1:2] * wide[start + 6 : start + 6 + count, :width]
        acc = acc + tap[2:3] * wide[start + 7 : start + 7 + count, :width]
        acc = acc + tap[3:4] * wide[start + 8 : start + 8 + count, :width]
        put(start, count, (acc + acc * jnp.tanh(acc)).astype(BF16))


def prep_kernel(shards, place, *refs):
    blocks, (taps, offset, a_ref, bias_ref, skip_ref, order) = refs[:shards], refs[shards : shards + 6]
    b_ref, edge_ref, cum_ref, row_ref, factor_ref, tail_ref, skip_out, dt_ref, wide = refs[shards + 6 :]
    blocks = view(blocks, 1)
    start = WIDTHS[1]
    last = total_of(1) - LANES
    size = edge_ref.shape[1]
    count = blocks[0][0].shape[0] // PAIR
    half, heads = count // 2, HEADS // GROUPS
    columns = [block[:, origin + last : origin + last + LANES].astype(F32) for block, origin in blocks]
    edge = columns[0][half : half + 4 * size // LANES]
    for column in columns[1:]:
        edge = edge + column[half : half + 4 * size // LANES]
    for q in range(size // LANES):
        edge_ref[:, q * LANES : (q + 1) * LANES] = edge[4 * q : 4 * q + 4]
    for r, column in enumerate(columns):
        packed = column[:half]
        for j in range(2 * PAIR):
            at = ((j // 2) * shards + (place[4] ^ FLIP[r])) * count + (j % 2) * half
            rows = packed if j == 0 else pltpu.roll(packed, LANES - j * heads, 1)
            dt_ref[pl.ds(pl.multiple_of(at, half), half), :] = rows

    def put(start, count, value):
        b_ref[start : start + count] = value

    at = slice(PER_GROUP, PER_GROUP + STATE)
    convolve_in_order(
        place, blocks, slice(start, start + STATE), edge_ref[0:3, at], taps[:, at], offset[:, at], wide, put
    )
    per_tile = LANES * GROUPS // HEADS
    group = place[0]
    tile = group // per_tile
    shift = (LANES - (group % per_tile) * heads) % LANES

    def lanes_of(ref):
        return pltpu.roll(jnp.broadcast_to(ref[pl.ds(tile, 1), :], (8, LANES)), shift, 1)

    rate = -jnp.exp(lanes_of(a_ref)[0:1])
    raw = dt_ref[...] + lanes_of(bias_ref)[0:1]
    step = jnp.maximum(raw, 0.0) + jnp.log1p(jnp.exp(-jnp.abs(raw)))
    skip = lanes_of(skip_ref)
    skip_out[...] = jnp.concatenate(halves(jnp.concatenate([skip, skip], 0), 3), 1)
    lower = (
        lax.broadcasted_iota(jnp.int32, (BLOCK, BLOCK), 0)
        >= lax.broadcasted_iota(jnp.int32, (BLOCK, BLOCK), 1)
    ).astype(BF16)
    valid = lax.broadcasted_iota(jnp.int32, (BLOCK, LANES), 1) < heads
    for block in range(PAIR):
        at = slice(block * BLOCK, (block + 1) * BLOCK)
        here = jnp.where(valid, step[at], 1.0)
        parts = halves(here * rate, 3)
        cum = dot(lower, parts[0]) + (dot(lower, parts[1]) + dot(lower, parts[2]))
        cum = cum * LOG2E
        cum_ref[at] = cum
        row_ref[:, at] = jnp.transpose(cum - jnp.log2(here))
        factor_ref[at] = jnp.concatenate(halves(jnp.exp2(cum), 2), 1)
        tail = jnp.exp2(cum[BLOCK - 1 :] - cum) * here
        tail_ref[at] = jnp.concatenate(halves(tail, 2), 1)


def score_kernel(shards, place, *refs):
    blocks, refs = refs[:shards], refs[shards:]
    taps, offset, edge_ref, b_ref, c_ref, score_ref, wide = (*refs[:4], *refs[-3:])
    blocks = view(blocks, 3)
    start = WIDTHS[3]
    at = slice(PER_GROUP + STATE, PER_GROUP + 2 * STATE)

    def put(start, count, value):
        c_ref[start : start + count] = value

    convolve_in_order(
        place, blocks, slice(start, start + STATE), edge_ref[0:3, at], taps[:, at], offset[:, at], wide, put
    )
    for block in range(PAIR):
        at = slice(block * BLOCK, (block + 1) * BLOCK)
        score_ref[at] = lax.dot_general(
            c_ref[at], b_ref[at], (((1,), (1,)), ((), ())), preferred_element_type=F32
        )


def decay_of(ref):
    decay = ref[STATE : STATE + 16].astype(F32)
    return decay[0:1] + (decay[1:2] + decay[2:3])


def put_decay(ref, decay):
    row = lax.broadcasted_iota(jnp.int32, (16, ref.shape[1]), 0)
    high, middle, low = (part.astype(F32) for part in halves(decay, 3))
    packed = jnp.where(row == 0, high, jnp.where(row == 1, middle, jnp.where(row == 2, low, 0.0)))
    ref[STATE:] = packed.astype(BF16)


def state_kernel(shards, part, sizes, place, *refs):
    blocks, refs = refs[:shards], refs[shards:]
    taps, offset, edge_ref, b_ref, factor_ref, tail_ref = refs[:6]
    x_ref, own_ref, *sends, wide = refs[-3 - len(sizes) :]
    piece, start, width = part
    first = sum(WIDTHS[:piece]) + start
    at = slice(first, first + width)

    def put(row, count, value):
        x_ref[row : row + count] = value

    blocks = view(blocks, piece)
    columns = slice(start, start + width)
    convolve_in_order(place, blocks, columns, edge_ref[0:3, at], taps[:, at], offset[:, at], wide, put)
    expand = spread(first // HEAD_DIM, width, 2)
    both = []
    for block in range(PAIR):
        at = slice(block * BLOCK, (block + 1) * BLOCK)
        loaded = (x_ref[at].astype(F32) * dot(tail_ref[at], expand)).astype(BF16)
        both.append(
            lax.dot_general(b_ref[at], loaded, (((0,), (0,)), ((), ())), preferred_element_type=F32)
        )
    ends = [dot(factor_ref[(i + 1) * BLOCK - 16 : (i + 1) * BLOCK], expand)[15:16] for i in range(PAIR)]
    own_ref[...] = both[0]
    end = (ends[1] * both[0] + both[1]).astype(BF16)
    decay = ends[0] * ends[1]
    start = 0
    for send_ref in sends:
        at = slice(start, start + send_ref.shape[1])
        send_ref[0:STATE] = end[:, at]
        put_decay(send_ref, decay[:, at])
        start = at.stop


def combine_kernel(spans, place, *refs):
    count = len(spans)
    got, own, out_ref = refs[:count], refs[count : 2 * count], refs[-1]
    odd = place[1] % 2 == 1
    start = 0
    for got_ref, own_ref, span in zip(got, own, spans):
        at = slice(start, start + span.stop - span.start)
        theirs, mine = got_ref[:STATE, span].astype(F32), own_ref[:STATE, span].astype(F32)
        decay, other = decay_of(own_ref.at[:, span]), decay_of(got_ref.at[:, span])
        early, late = jnp.where(odd, theirs, mine), jnp.where(odd, mine, theirs)
        out_ref[:STATE, at] = (jnp.where(odd, decay, other) * early + late).astype(BF16)
        put_decay(out_ref.at[:, at], decay * other)
        start = at.stop


def mix(first_head, x_ref, cum_ref, row_ref, score_ref, skip_ref, put):
    width = x_ref.shape[1]
    half = BLOCK // 2
    expand = spread(first_head, width, 3)
    skip = dot(skip_ref[...], expand)[0:1]
    lower = lax.broadcasted_iota(jnp.int32, (half, half), 0) >= lax.broadcasted_iota(
        jnp.int32, (half, half), 1
    )
    lane = lax.broadcasted_iota(jnp.int32, (BLOCK, LANES), 1)
    for block in range(PAIR):
        base = block * BLOCK
        for tile in range(width // LANES):
            columns = slice(tile * LANES, (tile + 1) * LANES)
            x = x_ref[base : base + BLOCK, columns]
            top = skip[:, columns] * x[:half].astype(F32)
            bottom = skip[:, columns] * x[half:].astype(F32)
            for side in range(LANES // HEAD_DIM):
                head = first_head + tile * (LANES // HEAD_DIM) + side
                own = jnp.where(lane // HEAD_DIM == side, x, jnp.zeros_like(x))
                cum = cum_ref[base : base + BLOCK, head : head + 1]
                row = row_ref[head : head + 1, base : base + BLOCK]
                diag = jnp.where(lower, cum[:half] - row[:, :half], -1e30)
                mixing = jnp.exp2(diag) * score_ref[base : base + half, :half]
                top = top + dot(mixing.astype(BF16), own[:half])
                left = jnp.exp2(cum[half:] - row[:, :half]) * score_ref[base + half : base + BLOCK, :half]
                diag = jnp.where(lower, cum[half:] - row[:, half:], -1e30)
                right = jnp.exp2(diag) * score_ref[base + half : base + BLOCK, half:]
                mixing = jnp.concatenate([left.astype(BF16), right.astype(BF16)], 1)
                bottom = bottom + dot(mixing, own)
            put(block, slice(base, base + half), columns, top)
            put(block, slice(base + half, base + BLOCK), columns, bottom)


def local_kernel(first_head, x_ref, cum_ref, row_ref, score_ref, skip_ref, *refs):
    out_ref = refs[-1]

    def put(block, rows, columns, value):
        out_ref[rows, columns] = value

    mix(first_head, x_ref, cum_ref, row_ref, score_ref, skip_ref, put)


def carry(first_head, place, lasts, befores, own_ref, c_ref, factor_ref, add, keep_ref, send_ref):
    expand = spread(first_head, own_ref.shape[1], 2)
    last, before = (
        refs[0][...] if len(refs) == 1 else jnp.concatenate([ref[...] for ref in refs], 1)
        for refs in (lasts, befores)
    )
    odd, core = place[1] % 2 == 1, place[2]
    near = jnp.where(odd, last[:STATE].astype(F32), 0.0)
    held = near + jnp.where(odd, decay_of(last), 1.0) * before[:STATE].astype(F32)
    factor = dot(factor_ref[...], expand)
    outs = []
    for block in range(PAIR):
        at = slice(block * BLOCK, (block + 1) * BLOCK)
        carried = dot(c_ref[at], held.astype(BF16))
        outs.append((add[at] + factor[at] * carried).astype(BF16))
        held = factor[BLOCK - 1 : BLOCK] * held + own_ref[...]

    @pl.when(core == 0)
    def _():
        keep_ref[...] = outs[0]
        send_ref[...] = outs[1]

    @pl.when(core == 1)
    def _():
        keep_ref[...] = outs[1]
        send_ref[...] = outs[0]


def final_kernel(first_head, counts, place, *refs):
    groups = []
    for number in counts:
        groups.append(refs[:number])
        refs = refs[number:]
    carry(first_head, place, *groups, *refs[:4], *refs[-2:])


def finish_kernel(first_head, counts, place, *refs):
    groups = []
    for number in counts:
        groups.append(refs[:number])
        refs = refs[number:]
    own_ref, c_ref, factor_ref = refs[:3]
    keep_ref, send_ref, partial = refs[-3:]
    local_kernel(first_head, *refs[3:8], partial)
    carry(first_head, place, *groups, own_ref, c_ref, factor_ref, partial, keep_ref, send_ref)


def place_kernel(firsts, place, *refs):
    count = len(firsts)
    keeps, gots = refs[:count], refs[count : 2 * count]
    out, sems = refs[-2:]
    core = place[2]
    half = out.shape[1] // PAIR
    copies = []
    for first, keep, got in zip(firsts, keeps, gots):
        width = keep.shape[1]
        copies.append((keep, out.at[:, ds(core * half + first, width)]))
        copies.append((got, out.at[:, ds((1 - core) * half + first, width)]))
    for copy in run(copies, sems):
        copy.wait()


def put_in_place(firsts, shape, place, keeps, gots):
    smem, vmem, hbm = (pl.BlockSpec(memory_space=m) for m in (pltpu.SMEM, pltpu.VMEM, pltpu.HBM))
    count = len(firsts)
    return pl.pallas_call(
        functools.partial(place_kernel, firsts),
        out_shape=jax.ShapeDtypeStruct(shape, BF16),
        in_specs=[smem] + [vmem] * (2 * count),
        out_specs=hbm,
        scratch_shapes=[pltpu.SemaphoreType.DMA((2 * count,))],
        compiler_params=pltpu.CompilerParams(vmem_limit_bytes=16 << 20),
        cost_estimate=pl.CostEstimate(flops=1, bytes_accessed=1, transcendentals=0),
        name="place",
    )(place, *keeps, *gots)


class Stay:
    def __init__(self, array):
        self.array = array


def gate(blocks, order):
    anywhere = pl.BlockSpec(memory_space=pl.ANY)
    return pl.pallas_call(
        lambda *refs: None,
        out_shape=[jax.ShapeDtypeStruct(block.shape, block.dtype) for block in blocks],
        in_specs=[anywhere] * (len(blocks) + len(order)),
        out_specs=[anywhere] * len(blocks),
        input_output_aliases={i: i for i in range(len(blocks))},
        compiler_params=pltpu.CompilerParams(vmem_limit_bytes=16 << 20),
        cost_estimate=pl.CostEstimate(flops=1, bytes_accessed=1, transcendentals=0),
        name="gate",
    )(*blocks, *order)


def call(body, outs, operands, scratch=(), flops=0, transcendentals=0, name=None, limit=16 << 20):
    shapes = [jax.ShapeDtypeStruct(shape, dtype) for shape, dtype in outs]
    smem, vmem, hbm = (pl.BlockSpec(memory_space=m) for m in (pltpu.SMEM, pltpu.VMEM, pltpu.HBM))
    specs = [
        hbm if isinstance(o, Stay) else smem if o.dtype == jnp.int32 else vmem for o in operands
    ]
    moved = sum(o.size * o.dtype.itemsize for o in shapes) * 2
    return pl.pallas_call(
        body,
        out_shape=shapes,
        in_specs=specs,
        out_specs=[vmem] * len(outs),
        scratch_shapes=scratch,
        compiler_params=pltpu.CompilerParams(vmem_limit_bytes=limit),
        cost_estimate=pl.CostEstimate(flops=1, bytes_accessed=1, transcendentals=0),
        name=name,
    )(*[o.array if isinstance(o, Stay) else o for o in operands])


def paired(xbc, dt_raw, conv_weight, conv_bias, a_log, dt_bias, skip_gain):
    axes = ("ctx", "head")
    shards, length = lax.axis_size("head"), lax.axis_size("ctx")
    devices, peers = shards * length, shards * PAIR
    tok = xbc.shape[0]
    slab = tok * peers
    context, shard = lax.axis_index("ctx"), lax.axis_index("head")
    pair, core = context // PAIR, context % PAIR
    group = shard * PAIR + core
    place = jnp.stack([group, pair, core, core * shards + shard, shard]).astype(jnp.int32)

    def over(block, target):
        route = [(i, target(i)) for i in range(devices)]
        return lax.ppermute(block, axes, [(i, j) for i, j in route if j is not None and j < devices])

    def swap(block):
        return over(block, lambda i: i ^ shards)

    rows = Stay(xbc)
    size = PER_GROUP + 2 * STATE
    (sent,) = call(
        functools.partial(pack_first_kernel, shards),
        [((tok, shards * WIDTHS[0]), BF16)],
        [place, rows],
        scratch=[pltpu.SemaphoreType.DMA((shards,))],
        name="pack_first",
    )
    got_first = swap(sent)
    sent, tail = call(
        functools.partial(pack_kernel, shards),
        [((tok, shards * (size - WIDTHS[0]) + HEADS), BF16), ((16, shards * size), BF16)],
        [place, rows, Stay(dt_raw), Stay(sent)],
        scratch=[pltpu.SemaphoreType.DMA((6 * shards + 1,))],
        name="pack",
    )
    got_rest = swap(sent)
    taps, offset = call(
        taps_kernel,
        [((4, size), F32), ((1, size), F32)],
        [place, Stay(conv_weight), Stay(conv_bias[None]), Stay(got_rest)],
        scratch=[pltpu.SemaphoreType.DMA((6,))],
        name="taps",
    )

    def send_on(plan, order, edges=None):
        unused = Stay(got_first)
        parts = [p for _, pieces in plan for p in pieces]
        return call(
            functools.partial(merge_kernel, shards, plan, len(order)),
            [((PAIR * tok, sum(map(total_of, pieces))), BF16) for _, pieces in plan],
            [
                place,
                rows,
                Stay(dt_raw) if edges is None else dt_raw,
                got_first if 0 in parts else unused,
                got_rest if any(parts) else unused,
                unused if edges is None else edges,
            ]
            + [Stay(o) for o in order],
            scratch=[pltpu.SemaphoreType.DMA((sum(2 + 2 * len(RESTS[p]) for p in parts),))],
            name="merge",
        )

    def travel(blocks):
        return [blocks[0]] + [over(blocks[r], lambda i, r=r: i ^ FLIP[r]) for r in range(1, shards)]

    def plan(piece):
        return [(r, (piece,)) for r in range(shards)]

    first_blocks = send_on(plan(0), [])
    message = [travel(first_blocks)]
    (edges,) = call(
        functools.partial(edge_kernel, shards),
        [((3, shards * size), BF16)],
        [place, got_first, got_rest, tail],
        name="edge",
    )
    edges = over(edges, lambda i: i + peers if i % shards == shards - 1 else None)
    second_blocks = send_on(plan(1), [first_blocks[0]], edges)
    message.append(travel(second_blocks))
    third_plan = [(r, (2, 3) if r == NEAR else (2,)) for r in range(shards)]
    third_blocks = send_on(third_plan, [second_blocks[0]])
    message.append(travel(third_blocks[:1] + gate(third_blocks[1:], message[0][1:] + message[1][1:] + [taps])))

    def seen(piece):
        return message[piece]

    tiles = [p.reshape(HEADS // LANES, LANES) for p in (a_log, dt_bias, skip_gain)]
    b, edge, cum, row, factor, tail, skip = call(
        functools.partial(prep_kernel, shards),
        [
            ((slab, STATE), BF16),
            ((4, size), F32),
            ((slab, LANES), F32),
            ((LANES, slab), F32),
            ((slab, 2 * LANES), BF16),
            ((slab, 2 * LANES), BF16),
            ((16, 3 * LANES), BF16),
        ],
        [place] + seen(1) + [taps, offset] + tiles + [Stay(third_blocks[0])],
        scratch=[pltpu.VMEM((slab, LANES), F32), pltpu.VMEM((slab + 8, STATE), F32)],
        name="prep",
    )
    count = len(GROUPED)
    x, sent, own, last, joined, before, keep, send = ([None] * count for _ in range(8))

    def first_head(i):
        return (sum(WIDTHS[: GROUPED[i][0]]) + GROUPED[i][1]) // HEAD_DIM

    def state_of(i, order):
        piece, _, width = GROUPED[i]
        x[i], own[i], *sent[i] = call(
            functools.partial(state_kernel, shards, GROUPED[i], FIRST_ROUND[i]),
            [((slab, width), BF16), ((STATE, width), F32)] + [((STATE + 16, w), BF16) for w in FIRST_ROUND[i]],
            [place] + seen(piece) + [taps, offset, edge, b, factor, tail] + [Stay(o) for o in order],
            scratch=[pltpu.VMEM((slab + 8, width), F32)],
            name="state",
        )
        last[i] = [over(part, lambda i: i ^ peers if i // peers != 3 else None) for part in sent[i]]

    def combine_of(i, order):
        joined[i], before[i] = [], []
        end = 0
        for width in SECOND_ROUND[i]:
            begin, end = end, end + width
            early, late, spans, first = [], [], [], 0
            for got, mine, size_of in zip(last[i], sent[i], FIRST_ROUND[i]):
                low, high = max(begin - first, 0), min(end - first, size_of)
                first += size_of
                if low < high:
                    early.append(got)
                    late.append(mine)
                    spans.append(slice(low, high))
            (total,) = call(
                functools.partial(combine_kernel, spans),
                [((STATE + 16, width), BF16)],
                [place] + early + late + [Stay(o) for o in order],
                name="combine",
            )
            joined[i].append(total)
            before[i].append(over(total, lambda i: i + 2 * peers))
            order = [total]

    def finish_of(body, i, operands, order, **more):
        keep[i], send[i] = call(
            functools.partial(body, first_head(i), (len(last[i]), len(before[i]))),
            [((BLOCK, GROUPED[i][2]), BF16)] * 2,
            [place, *last[i], *before[i], own[i], c, factor] + operands + [Stay(o) for o in order],
            name="final",
            **more,
        )

    partial = [None] * count

    def local_of(i, order):
        (partial[i],) = call(
            functools.partial(local_kernel, first_head(i)),
            [(x[i].shape, F32)],
            [x[i], cum, row, score, skip] + [Stay(o) for o in order],
            name="local",
        )

    state_of(0, [])
    own_block, *fourth_blocks = send_on([(r, (3,)) for r in range(shards) if r != NEAR], sent[0])
    fourth_blocks = gate(fourth_blocks, message[2][1:])
    fourth_blocks = [over(block, lambda i, r=r: i ^ FLIP[r]) for r, block in enumerate(fourth_blocks, 1)]
    message.append([own_block, *fourth_blocks, message[2][NEAR]])
    combine_of(0, [own_block])
    state_of(1, joined[0])
    combine_of(1, [])
    state_of(2, joined[1] + before[0])
    c, score = call(
        functools.partial(score_kernel, shards),
        [((slab, STATE), BF16), ((slab, BLOCK), F32)],
        [place] + seen(3) + [taps, offset, edge, b] + [Stay(o) for o in sent[2]],
        scratch=[pltpu.VMEM((slab + 8, STATE), F32)],
        name="score",
    )
    local_of(0, [])
    state_of(3, [partial[0]])

    def in_full(i, order):
        wide = [pltpu.VMEM((slab, GROUPED[i][2]), F32)]
        finish_of(finish_kernel, i, [x[i], cum, row, score, skip], order, scratch=wide)

    combine_of(2, sent[3] + before[1])
    in_full(1, joined[2])
    combine_of(3, [keep[1]])
    local_of(2, joined[3])
    local_of(3, [partial[2]])
    finish_of(final_kernel, 0, [partial[0]], [partial[3]])
    finish_of(final_kernel, 2, [partial[2]], [keep[0]])
    finish_of(final_kernel, 3, [partial[3]], [keep[2]])
    firsts = [first_head(i) * HEAD_DIM for i in range(count)]
    return put_in_place(firsts, (BLOCK, PAIR * PER_GROUP), place, keep, [swap(o) for o in send])


def solution(mesh):
    in_specs = (P(("ctx", "head"), None), P(("ctx", "head"), None), P(), P(), P(), P(), P())
    out_specs = P("ctx", "head")
    shards, length = mesh.shape["head"], mesh.shape["ctx"]

    def program(xbc, *rest):
        slab = xbc.shape[0] // length
        fits = shards == GROUPS // PAIR and length == 4 * PAIR and slab == BLOCK
        return jax.shard_map(
            paired if fits else on_device,
            mesh=mesh,
            in_specs=in_specs,
            out_specs=out_specs,
            check_vma=False,
        )(xbc, *rest)

    return program
```

```python
import functools

import jax
import jax.numpy as jnp
from jax import lax
from jax.experimental import pallas as pl
from jax.experimental.pallas import tpu as pltpu
from jax.sharding import PartitionSpec as P

HEADS = 256
HEAD_DIM = 64
STATE = 256
GROUPS = 8
BLOCK = 256


def from_behind(block, axis, distance):
    devices = range(lax.axis_size(axis))
    route = [(i - distance, i) for i in devices if i - distance in devices]
    return lax.ppermute(block, axis, route)


def carried_in(array, axis, combine, identity):
    length, index = (lax.axis_size(axis), lax.axis_index(axis))
    everything = jax.tree.map(lambda part: lax.all_gather(part, axis), array)
    start = jax.tree.map(
        lambda part, zero: jnp.broadcast_to(jnp.asarray(zero, part.dtype), part.shape),
        array,
        identity,
    )

    def hop(k, before):
        reached = k < index
        new = combine(before, jax.tree.map(lambda part: part[k], everything))
        return jax.tree.map(lambda a, b: jnp.where(reached, a, b), new, before)

    return lax.fori_loop(0, length, hop, start)


def convolve(rows, edge, weight, bias):
    count = rows.shape[0]
    wide = jnp.concatenate([edge, rows], 0).astype(jnp.float32)
    acc = bias[None, :] + weight[0] * wide[0:count]
    acc = acc + weight[1] * wide[1 : count + 1]
    acc = acc + weight[2] * wide[2 : count + 2]
    acc = acc + weight[3] * wide[3 : count + 3]
    return jax.nn.silu(acc).astype(jnp.bfloat16)


def rearrange_heads(rows, shards, per_dev, groups_dev, per_group):
    count = rows.shape[0]
    inner = HEADS * HEAD_DIM
    replicate_groups = max(1, per_group // per_dev)
    heads_part = rows[:, :inner].reshape(count, shards, per_dev * HEAD_DIM)
    b_part = rows[:, inner : inner + GROUPS * STATE].reshape(count, GROUPS, STATE)
    c_part = rows[:, inner + GROUPS * STATE :].reshape(count, GROUPS, STATE)
    b_part = jnp.repeat(b_part, replicate_groups, axis=1).reshape(count, shards, groups_dev * STATE)
    c_part = jnp.repeat(c_part, replicate_groups, axis=1).reshape(count, shards, groups_dev * STATE)
    return jnp.concatenate([heads_part, b_part, c_part], axis=2)


def inner_block(xs, bmat, cmat, steps, cum):
    size = xs.shape[0]
    lower = jnp.arange(size)[:, None] >= jnp.arange(size)[None, :]
    scores = jnp.einsum("qgn,kgn->gqk", cmat, bmat, preferred_element_type=jnp.float32)
    order = jnp.transpose(cum, (1, 2, 0))
    gap = order[..., :, None] - order[..., None, :]
    decay = jnp.exp(jnp.where(lower, gap, -jnp.inf))
    mixing = (scores[:, None] * decay * jnp.transpose(steps, (1, 2, 0))[..., None, :]).astype(
        jnp.bfloat16
    )
    local = jnp.einsum("gjqk,kgjp->qgjp", mixing, xs, preferred_element_type=jnp.float32)
    tail = jnp.exp(cum[size - 1][None] - cum) * steps
    loaded = (bmat[:, :, None, :].astype(jnp.float32) * tail[..., None]).astype(jnp.bfloat16)
    block_state = jnp.einsum("kgjn,kgjp->gjnp", loaded, xs, preferred_element_type=jnp.float32)
    return (local, block_state)


def on_device(xbc, dt_raw, conv_weight, conv_bias, a_log, dt_bias, skip_gain):
    tok = xbc.shape[0]
    shards = lax.axis_size("head")
    per_dev = HEADS // shards
    per_group = HEADS // GROUPS
    groups_dev = max(1, per_dev // per_group)
    heads_per_cluster = per_dev // groups_dev
    sent = rearrange_heads(xbc, shards, per_dev, groups_dev, per_group)
    mine, rates = (
        lax.all_to_all(sent, "head", split_axis=1, concat_axis=0, tiled=True),
        lax.all_to_all(
            dt_raw.reshape(tok, shards, per_dev), "head", split_axis=1, concat_axis=0, tiled=True
        ),
    )
    slab = tok * shards
    mine = mine.reshape(slab, mine.shape[2])
    rates = rates.reshape(slab, per_dev)
    shard = lax.axis_index("head")
    taps = lax.dynamic_index_in_dim(
        rearrange_heads(conv_weight, shards, per_dev, groups_dev, per_group),
        shard,
        1,
        keepdims=False,
    )
    offset = lax.dynamic_index_in_dim(
        rearrange_heads(conv_bias[None, :], shards, per_dev, groups_dev, per_group),
        shard,
        1,
        keepdims=False,
    )
    edge = from_behind(mine[slab - 3 :], "ctx", 1)
    mine = convolve(mine, edge, taps, offset[0])
    nchunk = slab // BLOCK
    width = per_dev * HEAD_DIM
    xs = mine[:, :width].reshape(nchunk, BLOCK, groups_dev, heads_per_cluster, HEAD_DIM)
    bmat = mine[:, width : width + groups_dev * STATE].reshape(nchunk, BLOCK, groups_dev, STATE)
    cmat = mine[:, width + groups_dev * STATE :].reshape(nchunk, BLOCK, groups_dev, STATE)
    first = shard * per_dev
    rate = (-jnp.exp(lax.dynamic_slice_in_dim(a_log, first, per_dev))).reshape(
        groups_dev, heads_per_cluster
    )
    bias_dt = lax.dynamic_slice_in_dim(dt_bias, first, per_dev).reshape(
        groups_dev, heads_per_cluster
    )
    skip = lax.dynamic_slice_in_dim(skip_gain, first, per_dev).reshape(
        groups_dev, heads_per_cluster
    )
    steps = jax.nn.softplus(
        rates.astype(jnp.float32).reshape(nchunk, BLOCK, groups_dev, heads_per_cluster) + bias_dt
    )
    cum = jnp.cumsum(steps * rate, axis=1)

    def block_step(carry, item):
        held, product = carry
        x_part, b_part, c_part, step_part, cum_part = item
        local, block_state = inner_block(x_part, b_part, c_part, step_part, cum_part)
        lifted = c_part.astype(jnp.float32)[:, :, None, :] * jnp.exp(cum_part)[..., None]
        carried = jnp.einsum("qgjn,gjnp->qgjp", lifted, held, precision=lax.Precision.HIGHEST)
        partial_out = local + carried + skip[..., None] * x_part.astype(jnp.float32)
        end = jnp.exp(cum_part[BLOCK - 1])
        return ((end[..., None, None] * held + block_state, product * end), (partial_out, product))

    zero_state = jnp.zeros((groups_dev, heads_per_cluster, STATE, HEAD_DIM), jnp.float32)
    unit = jnp.ones((groups_dev, heads_per_cluster), jnp.float32)
    (slab_state, slab_decay), (partials, product_in) = lax.scan(
        block_step, (zero_state, unit), (xs, bmat, cmat, steps, cum)
    )

    def combine(preceding_state, later):
        return (
            preceding_state[0] * later[0],
            later[0][..., None, None] * preceding_state[1] + later[1],
        )

    _, entering = carried_in((slab_decay, slab_state), "ctx", combine, (unit, zero_state))
    projected = jnp.einsum(
        "cqgn,gjnp->cqgjp", cmat.astype(jnp.float32), entering, precision=lax.Precision.HIGHEST
    )
    factor = jnp.exp(cum) * product_in[:, None]
    total = partials + factor[..., None] * projected
    return total.astype(jnp.bfloat16).reshape(slab, width)


PAIR = 2
LANES = 128
LOG2E = 1.4426950408889634
F32, BF16 = jnp.float32, jnp.bfloat16
WIDTHS = (512, 0, 768, 768)
RESTS = ("", "BD", "", "C")
GROUPED = ((0, 0, 512), (2, 0, 768), (3, 0, 384), (3, 384, 384))
FIRST_ROUND = ((256, 256), (384, 384), (384,), (384,))
SECOND_ROUND = ((512,), (384, 384), (384,), (384,))


FLIP = (0, 2, 3, 1)
NEAR = 3


def halves(value, count):
    parts = []
    for _ in range(count):
        part = value.astype(BF16)
        parts.append(part)
        value = value - part.astype(F32)
    return parts


def spread(first_head, width, copies):
    lane = lax.broadcasted_iota(jnp.int32, (copies * LANES, width), 0) % LANES
    column = lax.broadcasted_iota(jnp.int32, (copies * LANES, width), 1)
    return (lane == first_head + column // HEAD_DIM).astype(BF16)


def dot(a, b):
    return jnp.dot(a, b, preferred_element_type=F32)


def ds(start, width):
    return pl.ds(pl.multiple_of(start, LANES), width)


def run(copies, sems):
    started = []
    for i, (source, target) in enumerate(copies):
        copy = pltpu.make_async_copy(source, target, sems.at[i])
        copy.start()
        started.append(copy)
    return started


PER_GROUP = HEADS * HEAD_DIM // GROUPS
INNER = HEADS * HEAD_DIM


def channels(group, first, width):
    return ds(group * PER_GROUP + first, width)


def pack_first_kernel(shards, place, xbc, send, sems):
    core, shard = place[2], place[4]
    width = WIDTHS[0]
    copies = []
    for r in range(shards):
        group = (shard ^ FLIP[r]) * PAIR + 1 - core
        copies.append((xbc.at[:, channels(group, 0, width)], send.at[:, r * width : (r + 1) * width]))
    for copy in run(copies, sems):
        copy.wait()


def pack_kernel(shards, place, xbc, dt_raw, order, send, tail, sems):
    core, shard = place[2], place[4]
    count = xbc.shape[0]
    first = WIDTHS[0]
    width = PER_GROUP - first
    rest = width * shards
    size = PER_GROUP + 2 * STATE
    copies = []
    for r in range(shards):
        group = (shard ^ FLIP[r]) * PAIR + 1 - core
        copies.append((xbc.at[:, channels(group, first, width)], send.at[:, r * width : (r + 1) * width]))
        for i in range(2):
            to = rest + (i * shards + r) * STATE
            copies.append((xbc.at[:, ds(INNER + (i * GROUPS + group) * STATE, STATE)], send.at[:, to : to + STATE]))
    copies.append((dt_raw, send.at[:, send.shape[1] - HEADS :]))
    for r in range(shards):
        group, to = (shard ^ FLIP[r]) * PAIR + core, r * size
        last = xbc.at[count - 16 :]
        copies.append((last.at[:, channels(group, 0, PER_GROUP)], tail.at[:, to : to + PER_GROUP]))
        for i in range(2):
            at = ds(INNER + (i * GROUPS + group) * STATE, STATE)
            start = to + PER_GROUP + i * STATE
            copies.append((last.at[:, at], tail.at[:, start : start + STATE]))
    for copy in run(copies, sems):
        copy.wait()


def taps_kernel(place, weight, bias, order, taps, offset, sems):
    copies = []
    for source, target in ((weight, taps), (bias, offset)):
        copies.append((source.at[:, channels(place[0], 0, PER_GROUP)], target.at[:, :PER_GROUP]))
        for i in range(2):
            at = ds(INNER + (i * GROUPS + place[0]) * STATE, STATE)
            start = PER_GROUP + i * STATE
            copies.append((source.at[:, at], target.at[:, start : start + STATE]))
    for copy in run(copies, sems):
        copy.wait()


def edge_kernel(shards, place, got_first, got, tail, out):
    count = got.shape[0]
    first = WIDTHS[0]
    width = PER_GROUP - first
    size = PER_GROUP + 2 * STATE
    for r in range(shards):
        theirs = [(got_first, r * first, first), (got, r * width, width)]
        theirs += [(got, width * shards + (i * shards + r) * STATE, STATE) for i in range(2)]
        to = r * size
        for ref, start, size_of in theirs:
            a = ref[count - 16 :, start : start + size_of].astype(F32)
            b = tail[:, to : to + size_of].astype(F32)
            out[:, to : to + size_of] = jnp.where(place[2] == 0, a, b)[13:16].astype(BF16)
            to += size_of


def total_of(piece):
    return WIDTHS[piece] + sum(LANES if kind == "D" else STATE for kind in RESTS[piece])


def merge_kernel(shards, plan, unread, place, xbc, dt_raw, got_first, got, edges, *refs):
    refs = refs[unread:]
    outs, sems = refs[: len(plan)], refs[-1]
    core, shard = place[2], place[4]
    count = xbc.shape[0]
    stride = PER_GROUP - WIDTHS[0]
    mine = pl.ds(pl.multiple_of(core * count, count), count)
    other = pl.ds(pl.multiple_of((1 - core) * count, count), count)
    copies, steps = [], []
    for out, (r, pieces) in zip(outs, plan):
        group = (shard ^ FLIP[r]) * PAIR + core
        to = 0
        for piece in pieces:
            first, width = sum(WIDTHS[:piece]), WIDTHS[piece]
            if piece == 0:
                source = got_first.at[:, r * width : (r + 1) * width]
            else:
                at = r * stride + first - WIDTHS[0]
                source = got.at[:, at : at + width]
            if width:
                copies.append((xbc.at[:, channels(group, first, width)], out.at[mine, to : to + width]))
                copies.append((source, out.at[other, to : to + width]))
            to += width
            for kind in RESTS[piece]:
                if kind == "D":
                    steps.append((out, r, to))
                    to += LANES
                    continue
                i = "BC".index(kind)
                at = ds(INNER + (i * GROUPS + group) * STATE, STATE)
                copies.append((xbc.at[:, at], out.at[mine, to : to + STATE]))
                at = stride * shards + (i * shards + r) * STATE
                copies.append((got.at[:, at : at + STATE], out.at[other, to : to + STATE]))
                to += STATE
    started = run(copies, sems)
    if steps:
        lane = lax.broadcasted_iota(jnp.int32, (count, LANES), 1)
        per_tile = LANES * GROUPS // HEADS
        heads = HEADS // GROUPS
        for out, r, to in steps:
            group = (shard ^ FLIP[r]) * PAIR + core
            tile, shift = group // per_tile, (LANES - (group % per_tile) * heads) % LANES
            own = dt_raw[:, ds(tile * LANES, LANES)].astype(F32)
            theirs = got[:, ds(got.shape[1] - HEADS + tile * LANES, LANES)].astype(F32)
            low = jnp.where(core == 0, own, theirs)
            high = jnp.where(core == 0, theirs, own)
            packed = jnp.zeros((count // 2, LANES), F32)
            for j, rows in enumerate((low, high)):
                rows = jnp.where(lane < heads, pltpu.roll(rows, shift, 1), 0.0)
                for i in range(2):
                    part = rows[i * count // 2 : (i + 1) * count // 2]
                    packed = packed + pltpu.roll(part, (2 * j + i) * heads, 1)
            out[: count // 2, to : to + LANES] = packed.astype(BF16)
            size = PER_GROUP + 2 * STATE
            at = slice(r * size, (r + 1) * size)
            edge = jnp.concatenate([edges[:, at].astype(F32), jnp.zeros((1, size), F32)], 0)
            edge = jnp.concatenate([edge[:, q * LANES : (q + 1) * LANES] for q in range(size // LANES)], 0)
            fill = jnp.zeros((PAIR * count - count // 2 - edge.shape[0], LANES), F32)
            out[count // 2 :, to : to + LANES] = jnp.concatenate([edge, fill], 0).astype(BF16)
    for copy in started:
        copy.wait()


def view(refs, piece):
    return [(ref, total_of(2) if piece == 3 and r == NEAR else 0) for r, ref in enumerate(refs)]


def convolve_in_order(place, blocks, columns, edge, tap, bias, wide, put):
    width = columns.stop - columns.start
    count = blocks[0][0].shape[0] // PAIR
    wide[5:8, :width] = edge
    for r, (block, origin) in enumerate(blocks):
        for core in range(PAIR):
            at = pl.multiple_of((core * len(blocks) + (place[4] ^ FLIP[r])) * count + 8, 8)
            part = block[core * count : (core + 1) * count, origin + columns.start : origin + columns.stop]
            wide[pl.ds(at, count), :width] = part.astype(F32)
    tap, bias = tap * 0.5, bias * 0.5
    for start in range(0, PAIR * len(blocks) * count, count):
        acc = bias + tap[0:1] * wide[start + 5 : start + 5 + count, :width]
        acc = acc + tap[1:2] * wide[start + 6 : start + 6 + count, :width]
        acc = acc + tap[2:3] * wide[start + 7 : start + 7 + count, :width]
        acc = acc + tap[3:4] * wide[start + 8 : start + 8 + count, :width]
        put(start, count, (acc + acc * jnp.tanh(acc)).astype(BF16))


def prep_kernel(shards, place, *refs):
    blocks, (taps, offset, a_ref, bias_ref, skip_ref, order) = refs[:shards], refs[shards : shards + 6]
    b_ref, edge_ref, cum_ref, row_ref, factor_ref, tail_ref, skip_out, dt_ref, wide = refs[shards + 6 :]
    blocks = view(blocks, 1)
    start = WIDTHS[1]
    last = total_of(1) - LANES
    size = edge_ref.shape[1]
    count = blocks[0][0].shape[0] // PAIR
    half, heads = count // 2, HEADS // GROUPS
    columns = [block[:, origin + last : origin + last + LANES].astype(F32) for block, origin in blocks]
    edge = columns[0][half : half + 4 * size // LANES]
    for column in columns[1:]:
        edge = edge + column[half : half + 4 * size // LANES]
    for q in range(size // LANES):
        edge_ref[:, q * LANES : (q + 1) * LANES] = edge[4 * q : 4 * q + 4]
    for r, column in enumerate(columns):
        packed = column[:half]
        for j in range(2 * PAIR):
            at = ((j // 2) * shards + (place[4] ^ FLIP[r])) * count + (j % 2) * half
            rows = packed if j == 0 else pltpu.roll(packed, LANES - j * heads, 1)
            dt_ref[pl.ds(pl.multiple_of(at, half), half), :] = rows

    def put(start, count, value):
        b_ref[start : start + count] = value

    at = slice(PER_GROUP, PER_GROUP + STATE)
    convolve_in_order(
        place, blocks, slice(start, start + STATE), edge_ref[0:3, at], taps[:, at], offset[:, at], wide, put
    )
    per_tile = LANES * GROUPS // HEADS
    group = place[0]
    tile = group // per_tile
    shift = (LANES - (group % per_tile) * heads) % LANES

    def lanes_of(ref):
        return pltpu.roll(jnp.broadcast_to(ref[pl.ds(tile, 1), :], (8, LANES)), shift, 1)

    rate = -jnp.exp(lanes_of(a_ref)[0:1])
    raw = dt_ref[...] + lanes_of(bias_ref)[0:1]
    step = jnp.maximum(raw, 0.0) + jnp.log1p(jnp.exp(-jnp.abs(raw)))
    skip = lanes_of(skip_ref)
    skip_out[...] = jnp.concatenate(halves(jnp.concatenate([skip, skip], 0), 3), 1)
    lower = (
        lax.broadcasted_iota(jnp.int32, (BLOCK, BLOCK), 0)
        >= lax.broadcasted_iota(jnp.int32, (BLOCK, BLOCK), 1)
    ).astype(BF16)
    valid = lax.broadcasted_iota(jnp.int32, (BLOCK, LANES), 1) < heads
    for block in range(PAIR):
        at = slice(block * BLOCK, (block + 1) * BLOCK)
        here = jnp.where(valid, step[at], 1.0)
        parts = halves(here * rate, 3)
        cum = dot(lower, parts[0]) + (dot(lower, parts[1]) + dot(lower, parts[2]))
        cum = cum * LOG2E
        cum_ref[at] = cum
        row_ref[:, at] = jnp.transpose(cum - jnp.log2(here))
        factor_ref[at] = jnp.concatenate(halves(jnp.exp2(cum), 2), 1)
        tail = jnp.exp2(cum[BLOCK - 1 :] - cum) * here
        tail_ref[at] = jnp.concatenate(halves(tail, 2), 1)


def score_kernel(shards, place, *refs):
    blocks, refs = refs[:shards], refs[shards:]
    taps, offset, edge_ref, b_ref, c_ref, score_ref, wide = (*refs[:4], *refs[-3:])
    blocks = view(blocks, 3)
    start = WIDTHS[3]
    at = slice(PER_GROUP + STATE, PER_GROUP + 2 * STATE)

    def put(start, count, value):
        c_ref[start : start + count] = value

    convolve_in_order(
        place, blocks, slice(start, start + STATE), edge_ref[0:3, at], taps[:, at], offset[:, at], wide, put
    )
    for block in range(PAIR):
        at = slice(block * BLOCK, (block + 1) * BLOCK)
        score_ref[at] = lax.dot_general(
            c_ref[at], b_ref[at], (((1,), (1,)), ((), ())), preferred_element_type=F32
        )


def decay_of(ref):
    decay = ref[STATE : STATE + 16].astype(F32)
    return decay[0:1] + (decay[1:2] + decay[2:3])


def put_decay(ref, decay):
    row = lax.broadcasted_iota(jnp.int32, (16, ref.shape[1]), 0)
    high, middle, low = (part.astype(F32) for part in halves(decay, 3))
    packed = jnp.where(row == 0, high, jnp.where(row == 1, middle, jnp.where(row == 2, low, 0.0)))
    ref[STATE:] = packed.astype(BF16)


def state_kernel(shards, part, sizes, place, *refs):
    blocks, refs = refs[:shards], refs[shards:]
    taps, offset, edge_ref, b_ref, factor_ref, tail_ref = refs[:6]
    x_ref, own_ref, *sends, wide = refs[-3 - len(sizes) :]
    piece, start, width = part
    first = sum(WIDTHS[:piece]) + start
    at = slice(first, first + width)

    def put(row, count, value):
        x_ref[row : row + count] = value

    blocks = view(blocks, piece)
    columns = slice(start, start + width)
    convolve_in_order(place, blocks, columns, edge_ref[0:3, at], taps[:, at], offset[:, at], wide, put)
    expand = spread(first // HEAD_DIM, width, 2)
    both = []
    for block in range(PAIR):
        at = slice(block * BLOCK, (block + 1) * BLOCK)
        loaded = (x_ref[at].astype(F32) * dot(tail_ref[at], expand)).astype(BF16)
        both.append(
            lax.dot_general(b_ref[at], loaded, (((0,), (0,)), ((), ())), preferred_element_type=F32)
        )
    ends = [dot(factor_ref[(i + 1) * BLOCK - 16 : (i + 1) * BLOCK], expand)[15:16] for i in range(PAIR)]
    own_ref[...] = both[0]
    end = (ends[1] * both[0] + both[1]).astype(BF16)
    decay = ends[0] * ends[1]
    start = 0
    for send_ref in sends:
        at = slice(start, start + send_ref.shape[1])
        send_ref[0:STATE] = end[:, at]
        put_decay(send_ref, decay[:, at])
        start = at.stop


def combine_kernel(spans, place, *refs):
    count = len(spans)
    got, own, out_ref = refs[:count], refs[count : 2 * count], refs[-1]
    odd = place[1] % 2 == 1
    start = 0
    for got_ref, own_ref, span in zip(got, own, spans):
        at = slice(start, start + span.stop - span.start)
        theirs, mine = got_ref[:STATE, span].astype(F32), own_ref[:STATE, span].astype(F32)
        decay, other = decay_of(own_ref.at[:, span]), decay_of(got_ref.at[:, span])
        early, late = jnp.where(odd, theirs, mine), jnp.where(odd, mine, theirs)
        out_ref[:STATE, at] = (jnp.where(odd, decay, other) * early + late).astype(BF16)
        put_decay(out_ref.at[:, at], decay * other)
        start = at.stop


def mix(first_head, x_ref, cum_ref, row_ref, score_ref, skip_ref, put):
    width = x_ref.shape[1]
    half = BLOCK // 2
    expand = spread(first_head, width, 3)
    skip = dot(skip_ref[...], expand)[0:1]
    lower = lax.broadcasted_iota(jnp.int32, (half, half), 0) >= lax.broadcasted_iota(
        jnp.int32, (half, half), 1
    )
    lane = lax.broadcasted_iota(jnp.int32, (BLOCK, LANES), 1)
    for block in range(PAIR):
        base = block * BLOCK
        for tile in range(width // LANES):
            columns = slice(tile * LANES, (tile + 1) * LANES)
            x = x_ref[base : base + BLOCK, columns]
            top = skip[:, columns] * x[:half].astype(F32)
            bottom = skip[:, columns] * x[half:].astype(F32)
            for side in range(LANES // HEAD_DIM):
                head = first_head + tile * (LANES // HEAD_DIM) + side
                own = jnp.where(lane // HEAD_DIM == side, x, jnp.zeros_like(x))
                cum = cum_ref[base : base + BLOCK, head : head + 1]
                row = row_ref[head : head + 1, base : base + BLOCK]
                diag = jnp.where(lower, cum[:half] - row[:, :half], -1e30)
                mixing = jnp.exp2(diag) * score_ref[base : base + half, :half]
                top = top + dot(mixing.astype(BF16), own[:half])
                left = jnp.exp2(cum[half:] - row[:, :half]) * score_ref[base + half : base + BLOCK, :half]
                diag = jnp.where(lower, cum[half:] - row[:, half:], -1e30)
                right = jnp.exp2(diag) * score_ref[base + half : base + BLOCK, half:]
                mixing = jnp.concatenate([left.astype(BF16), right.astype(BF16)], 1)
                bottom = bottom + dot(mixing, own)
            put(block, slice(base, base + half), columns, top)
            put(block, slice(base + half, base + BLOCK), columns, bottom)


def local_kernel(first_head, x_ref, cum_ref, row_ref, score_ref, skip_ref, *refs):
    out_ref = refs[-1]

    def put(block, rows, columns, value):
        out_ref[rows, columns] = value

    mix(first_head, x_ref, cum_ref, row_ref, score_ref, skip_ref, put)


def carry(first_head, place, lasts, befores, own_ref, c_ref, factor_ref, add, keep_ref, send_ref):
    expand = spread(first_head, own_ref.shape[1], 2)
    last, before = (
        refs[0][...] if len(refs) == 1 else jnp.concatenate([ref[...] for ref in refs], 1)
        for refs in (lasts, befores)
    )
    odd, core = place[1] % 2 == 1, place[2]
    near = jnp.where(odd, last[:STATE].astype(F32), 0.0)
    held = near + jnp.where(odd, decay_of(last), 1.0) * before[:STATE].astype(F32)
    factor = dot(factor_ref[...], expand)
    outs = []
    for block in range(PAIR):
        at = slice(block * BLOCK, (block + 1) * BLOCK)
        carried = dot(c_ref[at], held.astype(BF16))
        outs.append((add[at] + factor[at] * carried).astype(BF16))
        held = factor[BLOCK - 1 : BLOCK] * held + own_ref[...]

    @pl.when(core == 0)
    def _():
        keep_ref[...] = outs[0]
        send_ref[...] = outs[1]

    @pl.when(core == 1)
    def _():
        keep_ref[...] = outs[1]
        send_ref[...] = outs[0]


def final_kernel(first_head, counts, place, *refs):
    groups = []
    for number in counts:
        groups.append(refs[:number])
        refs = refs[number:]
    carry(first_head, place, *groups, *refs[:4], *refs[-2:])


def finish_kernel(first_head, counts, place, *refs):
    groups = []
    for number in counts:
        groups.append(refs[:number])
        refs = refs[number:]
    own_ref, c_ref, factor_ref = refs[:3]
    keep_ref, send_ref, partial = refs[-3:]
    local_kernel(first_head, *refs[3:8], partial)
    carry(first_head, place, *groups, own_ref, c_ref, factor_ref, partial, keep_ref, send_ref)


def place_kernel(firsts, place, *refs):
    count = len(firsts)
    keeps, gots = refs[:count], refs[count : 2 * count]
    out, sems = refs[-2:]
    core = place[2]
    half = out.shape[1] // PAIR
    copies = []
    for first, keep, got in zip(firsts, keeps, gots):
        width = keep.shape[1]
        copies.append((keep, out.at[:, ds(core * half + first, width)]))
        copies.append((got, out.at[:, ds((1 - core) * half + first, width)]))
    for copy in run(copies, sems):
        copy.wait()


def put_in_place(firsts, shape, place, keeps, gots):
    smem, vmem, hbm = (pl.BlockSpec(memory_space=m) for m in (pltpu.SMEM, pltpu.VMEM, pltpu.HBM))
    count = len(firsts)
    return pl.pallas_call(
        functools.partial(place_kernel, firsts),
        out_shape=jax.ShapeDtypeStruct(shape, BF16),
        in_specs=[smem] + [vmem] * (2 * count),
        out_specs=hbm,
        scratch_shapes=[pltpu.SemaphoreType.DMA((2 * count,))],
        compiler_params=pltpu.CompilerParams(vmem_limit_bytes=16 << 20),
        cost_estimate=pl.CostEstimate(flops=1, bytes_accessed=1, transcendentals=0),
        name="place",
    )(place, *keeps, *gots)


class Stay:
    def __init__(self, array):
        self.array = array


def gate(blocks, order):
    anywhere = pl.BlockSpec(memory_space=pl.ANY)
    return pl.pallas_call(
        lambda *refs: None,
        out_shape=[jax.ShapeDtypeStruct(block.shape, block.dtype) for block in blocks],
        in_specs=[anywhere] * (len(blocks) + len(order)),
        out_specs=[anywhere] * len(blocks),
        input_output_aliases={i: i for i in range(len(blocks))},
        compiler_params=pltpu.CompilerParams(vmem_limit_bytes=16 << 20),
        cost_estimate=pl.CostEstimate(flops=1, bytes_accessed=1, transcendentals=0),
        name="gate",
    )(*blocks, *order)


def call(body, outs, operands, scratch=(), flops=0, transcendentals=0, name=None, limit=16 << 20):
    shapes = [jax.ShapeDtypeStruct(shape, dtype) for shape, dtype in outs]
    smem, vmem, hbm = (pl.BlockSpec(memory_space=m) for m in (pltpu.SMEM, pltpu.VMEM, pltpu.HBM))
    specs = [
        hbm if isinstance(o, Stay) else smem if o.dtype == jnp.int32 else vmem for o in operands
    ]
    moved = sum(o.size * o.dtype.itemsize for o in shapes) * 2
    return pl.pallas_call(
        body,
        out_shape=shapes,
        in_specs=specs,
        out_specs=[vmem] * len(outs),
        scratch_shapes=scratch,
        compiler_params=pltpu.CompilerParams(vmem_limit_bytes=limit),
        cost_estimate=pl.CostEstimate(flops=1, bytes_accessed=1, transcendentals=0),
        name=name,
    )(*[o.array if isinstance(o, Stay) else o for o in operands])


def paired(xbc, dt_raw, conv_weight, conv_bias, a_log, dt_bias, skip_gain):
    axes = ("ctx", "head")
    shards, length = lax.axis_size("head"), lax.axis_size("ctx")
    devices, peers = shards * length, shards * PAIR
    tok = xbc.shape[0]
    slab = tok * peers
    context, shard = lax.axis_index("ctx"), lax.axis_index("head")
    pair, core = context // PAIR, context % PAIR
    group = shard * PAIR + core
    place = jnp.stack([group, pair, core, core * shards + shard, shard]).astype(jnp.int32)

    def over(block, target):
        route = [(i, target(i)) for i in range(devices)]
        return lax.ppermute(block, axes, [(i, j) for i, j in route if j is not None and j < devices])

    def swap(block):
        return over(block, lambda i: i ^ shards)

    rows = Stay(xbc)
    size = PER_GROUP + 2 * STATE
    (sent,) = call(
        functools.partial(pack_first_kernel, shards),
        [((tok, shards * WIDTHS[0]), BF16)],
        [place, rows],
        scratch=[pltpu.SemaphoreType.DMA((shards,))],
        name="pack_first",
    )
    got_first = swap(sent)
    sent, tail = call(
        functools.partial(pack_kernel, shards),
        [((tok, shards * (size - WIDTHS[0]) + HEADS), BF16), ((16, shards * size), BF16)],
        [place, rows, Stay(dt_raw), Stay(sent)],
        scratch=[pltpu.SemaphoreType.DMA((6 * shards + 1,))],
        name="pack",
    )
    got_rest = swap(gate([sent], [got_first])[0])
    taps, offset = call(
        taps_kernel,
        [((4, size), F32), ((1, size), F32)],
        [place, Stay(conv_weight), Stay(conv_bias[None]), Stay(got_rest)],
        scratch=[pltpu.SemaphoreType.DMA((6,))],
        name="taps",
    )

    def send_on(plan, order, edges=None):
        unused = Stay(got_first)
        parts = [p for _, pieces in plan for p in pieces]
        return call(
            functools.partial(merge_kernel, shards, plan, len(order)),
            [((PAIR * tok, sum(map(total_of, pieces))), BF16) for _, pieces in plan],
            [
                place,
                rows,
                Stay(dt_raw) if edges is None else dt_raw,
                got_first if 0 in parts else unused,
                got_rest if any(parts) else unused,
                unused if edges is None else edges,
            ]
            + [Stay(o) for o in order],
            scratch=[pltpu.SemaphoreType.DMA((sum(2 + 2 * len(RESTS[p]) for p in parts),))],
            name="merge",
        )

    def travel(blocks):
        return [blocks[0]] + [over(blocks[r], lambda i, r=r: i ^ FLIP[r]) for r in range(1, shards)]

    def plan(piece):
        return [(r, (piece,)) for r in range(shards)]

    first_blocks = send_on(plan(0), [])
    message = [travel(first_blocks)]
    (edges,) = call(
        functools.partial(edge_kernel, shards),
        [((3, shards * size), BF16)],
        [place, got_first, got_rest, tail],
        name="edge",
    )
    edges = over(edges, lambda i: i + peers if i % shards == shards - 1 else None)
    second_blocks = send_on(plan(1), [first_blocks[0]], edges)
    message.append(travel(second_blocks))
    third_plan = [(r, (2, 3) if r == NEAR else (2,)) for r in range(shards)]
    third_blocks = send_on(third_plan, [second_blocks[0]])
    message.append(travel(third_blocks[:1] + gate(third_blocks[1:], message[0][1:] + message[1][1:] + [taps])))

    def seen(piece):
        return message[piece]

    tiles = [p.reshape(HEADS // LANES, LANES) for p in (a_log, dt_bias, skip_gain)]
    b, edge, cum, row, factor, tail, skip = call(
        functools.partial(prep_kernel, shards),
        [
            ((slab, STATE), BF16),
            ((4, size), F32),
            ((slab, LANES), F32),
            ((LANES, slab), F32),
            ((slab, 2 * LANES), BF16),
            ((slab, 2 * LANES), BF16),
            ((16, 3 * LANES), BF16),
        ],
        [place] + seen(1) + [taps, offset] + tiles + [Stay(third_blocks[0])],
        scratch=[pltpu.VMEM((slab, LANES), F32), pltpu.VMEM((slab + 8, STATE), F32)],
        name="prep",
    )
    count = len(GROUPED)
    x, sent, own, last, joined, before, keep, send = ([None] * count for _ in range(8))

    def first_head(i):
        return (sum(WIDTHS[: GROUPED[i][0]]) + GROUPED[i][1]) // HEAD_DIM

    def state_of(i, order):
        piece, _, width = GROUPED[i]
        x[i], own[i], *sent[i] = call(
            functools.partial(state_kernel, shards, GROUPED[i], FIRST_ROUND[i]),
            [((slab, width), BF16), ((STATE, width), F32)] + [((STATE + 16, w), BF16) for w in FIRST_ROUND[i]],
            [place] + seen(piece) + [taps, offset, edge, b, factor, tail] + [Stay(o) for o in order],
            scratch=[pltpu.VMEM((slab + 8, width), F32)],
            name="state",
        )
        last[i] = [over(part, lambda i: i ^ peers if i // peers != 3 else None) for part in sent[i]]

    def combine_of(i, order):
        joined[i], before[i] = [], []
        end = 0
        for width in SECOND_ROUND[i]:
            begin, end = end, end + width
            early, late, spans, first = [], [], [], 0
            for got, mine, size_of in zip(last[i], sent[i], FIRST_ROUND[i]):
                low, high = max(begin - first, 0), min(end - first, size_of)
                first += size_of
                if low < high:
                    early.append(got)
                    late.append(mine)
                    spans.append(slice(low, high))
            (total,) = call(
                functools.partial(combine_kernel, spans),
                [((STATE + 16, width), BF16)],
                [place] + early + late + [Stay(o) for o in order],
                name="combine",
            )
            joined[i].append(total)
            before[i].append(over(total, lambda i: i + 2 * peers))
            order = [total]

    def finish_of(body, i, operands, order, **more):
        keep[i], send[i] = call(
            functools.partial(body, first_head(i), (len(last[i]), len(before[i]))),
            [((BLOCK, GROUPED[i][2]), BF16)] * 2,
            [place, *last[i], *before[i], own[i], c, factor] + operands + [Stay(o) for o in order],
            name="final",
            **more,
        )

    partial = [None] * count

    def local_of(i, order):
        (partial[i],) = call(
            functools.partial(local_kernel, first_head(i)),
            [(x[i].shape, F32)],
            [x[i], cum, row, score, skip] + [Stay(o) for o in order],
            name="local",
        )

    state_of(0, [])
    own_block, *fourth_blocks = send_on([(r, (3,)) for r in range(shards) if r != NEAR], sent[0])
    fourth_blocks = gate(fourth_blocks, message[2][1:])
    fourth_blocks = [over(block, lambda i, r=r: i ^ FLIP[r]) for r, block in enumerate(fourth_blocks, 1)]
    message.append([own_block, *fourth_blocks, message[2][NEAR]])
    combine_of(0, [own_block])
    state_of(1, joined[0])
    combine_of(1, [])
    state_of(2, joined[1] + before[0])
    c, score = call(
        functools.partial(score_kernel, shards),
        [((slab, STATE), BF16), ((slab, BLOCK), F32)],
        [place] + seen(3) + [taps, offset, edge, b] + [Stay(o) for o in sent[2]],
        scratch=[pltpu.VMEM((slab + 8, STATE), F32)],
        name="score",
    )
    local_of(0, [])
    state_of(3, [partial[0]])

    def in_full(i, order):
        wide = [pltpu.VMEM((slab, GROUPED[i][2]), F32)]
        finish_of(finish_kernel, i, [x[i], cum, row, score, skip], order, scratch=wide)

    combine_of(2, sent[3] + before[1])
    in_full(1, joined[2])
    combine_of(3, [keep[1]])
    local_of(2, joined[3])
    local_of(3, [partial[2]])
    finish_of(final_kernel, 0, [partial[0]], [partial[3]])
    finish_of(final_kernel, 2, [partial[2]], [keep[0]])
    finish_of(final_kernel, 3, [partial[3]], [keep[2]])
    firsts = [first_head(i) * HEAD_DIM for i in range(count)]
    return put_in_place(firsts, (BLOCK, PAIR * PER_GROUP), place, keep, [swap(o) for o in send])


def solution(mesh):
    in_specs = (P(("ctx", "head"), None), P(("ctx", "head"), None), P(), P(), P(), P(), P())
    out_specs = P("ctx", "head")
    shards, length = mesh.shape["head"], mesh.shape["ctx"]

    def program(xbc, *rest):
        slab = xbc.shape[0] // length
        fits = shards == GROUPS // PAIR and length == 4 * PAIR and slab == BLOCK
        return jax.shard_map(
            paired if fits else on_device,
            mesh=mesh,
            in_specs=in_specs,
            out_specs=out_specs,
            check_vma=False,
        )(xbc, *rest)

    return program
```

```python
import functools

import jax
import jax.numpy as jnp
from jax import lax
from jax.experimental import pallas as pl
from jax.experimental.pallas import tpu as pltpu
from jax.sharding import PartitionSpec as P

HEADS = 256
HEAD_DIM = 64
STATE = 256
GROUPS = 8
BLOCK = 256


def from_behind(block, axis, distance):
    devices = range(lax.axis_size(axis))
    route = [(i - distance, i) for i in devices if i - distance in devices]
    return lax.ppermute(block, axis, route)


def carried_in(array, axis, combine, identity):
    length, index = (lax.axis_size(axis), lax.axis_index(axis))
    everything = jax.tree.map(lambda part: lax.all_gather(part, axis), array)
    start = jax.tree.map(
        lambda part, zero: jnp.broadcast_to(jnp.asarray(zero, part.dtype), part.shape),
        array,
        identity,
    )

    def hop(k, before):
        reached = k < index
        new = combine(before, jax.tree.map(lambda part: part[k], everything))
        return jax.tree.map(lambda a, b: jnp.where(reached, a, b), new, before)

    return lax.fori_loop(0, length, hop, start)


def convolve(rows, edge, weight, bias):
    count = rows.shape[0]
    wide = jnp.concatenate([edge, rows], 0).astype(jnp.float32)
    acc = bias[None, :] + weight[0] * wide[0:count]
    acc = acc + weight[1] * wide[1 : count + 1]
    acc = acc + weight[2] * wide[2 : count + 2]
    acc = acc + weight[3] * wide[3 : count + 3]
    return jax.nn.silu(acc).astype(jnp.bfloat16)


def rearrange_heads(rows, shards, per_dev, groups_dev, per_group):
    count = rows.shape[0]
    inner = HEADS * HEAD_DIM
    replicate_groups = max(1, per_group // per_dev)
    heads_part = rows[:, :inner].reshape(count, shards, per_dev * HEAD_DIM)
    b_part = rows[:, inner : inner + GROUPS * STATE].reshape(count, GROUPS, STATE)
    c_part = rows[:, inner + GROUPS * STATE :].reshape(count, GROUPS, STATE)
    b_part = jnp.repeat(b_part, replicate_groups, axis=1).reshape(count, shards, groups_dev * STATE)
    c_part = jnp.repeat(c_part, replicate_groups, axis=1).reshape(count, shards, groups_dev * STATE)
    return jnp.concatenate([heads_part, b_part, c_part], axis=2)


def inner_block(xs, bmat, cmat, steps, cum):
    size = xs.shape[0]
    lower = jnp.arange(size)[:, None] >= jnp.arange(size)[None, :]
    scores = jnp.einsum("qgn,kgn->gqk", cmat, bmat, preferred_element_type=jnp.float32)
    order = jnp.transpose(cum, (1, 2, 0))
    gap = order[..., :, None] - order[..., None, :]
    decay = jnp.exp(jnp.where(lower, gap, -jnp.inf))
    mixing = (scores[:, None] * decay * jnp.transpose(steps, (1, 2, 0))[..., None, :]).astype(
        jnp.bfloat16
    )
    local = jnp.einsum("gjqk,kgjp->qgjp", mixing, xs, preferred_element_type=jnp.float32)
    tail = jnp.exp(cum[size - 1][None] - cum) * steps
    loaded = (bmat[:, :, None, :].astype(jnp.float32) * tail[..., None]).astype(jnp.bfloat16)
    block_state = jnp.einsum("kgjn,kgjp->gjnp", loaded, xs, preferred_element_type=jnp.float32)
    return (local, block_state)


def on_device(xbc, dt_raw, conv_weight, conv_bias, a_log, dt_bias, skip_gain):
    tok = xbc.shape[0]
    shards = lax.axis_size("head")
    per_dev = HEADS // shards
    per_group = HEADS // GROUPS
    groups_dev = max(1, per_dev // per_group)
    heads_per_cluster = per_dev // groups_dev
    sent = rearrange_heads(xbc, shards, per_dev, groups_dev, per_group)
    mine, rates = (
        lax.all_to_all(sent, "head", split_axis=1, concat_axis=0, tiled=True),
        lax.all_to_all(
            dt_raw.reshape(tok, shards, per_dev), "head", split_axis=1, concat_axis=0, tiled=True
        ),
    )
    slab = tok * shards
    mine = mine.reshape(slab, mine.shape[2])
    rates = rates.reshape(slab, per_dev)
    shard = lax.axis_index("head")
    taps = lax.dynamic_index_in_dim(
        rearrange_heads(conv_weight, shards, per_dev, groups_dev, per_group),
        shard,
        1,
        keepdims=False,
    )
    offset = lax.dynamic_index_in_dim(
        rearrange_heads(conv_bias[None, :], shards, per_dev, groups_dev, per_group),
        shard,
        1,
        keepdims=False,
    )
    edge = from_behind(mine[slab - 3 :], "ctx", 1)
    mine = convolve(mine, edge, taps, offset[0])
    nchunk = slab // BLOCK
    width = per_dev * HEAD_DIM
    xs = mine[:, :width].reshape(nchunk, BLOCK, groups_dev, heads_per_cluster, HEAD_DIM)
    bmat = mine[:, width : width + groups_dev * STATE].reshape(nchunk, BLOCK, groups_dev, STATE)
    cmat = mine[:, width + groups_dev * STATE :].reshape(nchunk, BLOCK, groups_dev, STATE)
    first = shard * per_dev
    rate = (-jnp.exp(lax.dynamic_slice_in_dim(a_log, first, per_dev))).reshape(
        groups_dev, heads_per_cluster
    )
    bias_dt = lax.dynamic_slice_in_dim(dt_bias, first, per_dev).reshape(
        groups_dev, heads_per_cluster
    )
    skip = lax.dynamic_slice_in_dim(skip_gain, first, per_dev).reshape(
        groups_dev, heads_per_cluster
    )
    steps = jax.nn.softplus(
        rates.astype(jnp.float32).reshape(nchunk, BLOCK, groups_dev, heads_per_cluster) + bias_dt
    )
    cum = jnp.cumsum(steps * rate, axis=1)

    def block_step(carry, item):
        held, product = carry
        x_part, b_part, c_part, step_part, cum_part = item
        local, block_state = inner_block(x_part, b_part, c_part, step_part, cum_part)
        lifted = c_part.astype(jnp.float32)[:, :, None, :] * jnp.exp(cum_part)[..., None]
        carried = jnp.einsum("qgjn,gjnp->qgjp", lifted, held, precision=lax.Precision.HIGHEST)
        partial_out = local + carried + skip[..., None] * x_part.astype(jnp.float32)
        end = jnp.exp(cum_part[BLOCK - 1])
        return ((end[..., None, None] * held + block_state, product * end), (partial_out, product))

    zero_state = jnp.zeros((groups_dev, heads_per_cluster, STATE, HEAD_DIM), jnp.float32)
    unit = jnp.ones((groups_dev, heads_per_cluster), jnp.float32)
    (slab_state, slab_decay), (partials, product_in) = lax.scan(
        block_step, (zero_state, unit), (xs, bmat, cmat, steps, cum)
    )

    def combine(preceding_state, later):
        return (
            preceding_state[0] * later[0],
            later[0][..., None, None] * preceding_state[1] + later[1],
        )

    _, entering = carried_in((slab_decay, slab_state), "ctx", combine, (unit, zero_state))
    projected = jnp.einsum(
        "cqgn,gjnp->cqgjp", cmat.astype(jnp.float32), entering, precision=lax.Precision.HIGHEST
    )
    factor = jnp.exp(cum) * product_in[:, None]
    total = partials + factor[..., None] * projected
    return total.astype(jnp.bfloat16).reshape(slab, width)


PAIR = 2
LANES = 128
LOG2E = 1.4426950408889634
F32, BF16 = jnp.float32, jnp.bfloat16
WIDTHS = (512, 0, 768, 768)
RESTS = ("", "BD", "", "C")
GROUPED = ((0, 0, 512), (2, 0, 768), (3, 0, 384), (3, 384, 384))
FIRST_ROUND = ((256, 256), (384, 384), (384,), (384,))
SECOND_ROUND = ((512,), (384, 384), (384,), (384,))


FLIP = (0, 2, 3, 1)
NEAR = 3


def halves(value, count):
    parts = []
    for _ in range(count):
        part = value.astype(BF16)
        parts.append(part)
        value = value - part.astype(F32)
    return parts


def spread(first_head, width, copies):
    lane = lax.broadcasted_iota(jnp.int32, (copies * LANES, width), 0) % LANES
    column = lax.broadcasted_iota(jnp.int32, (copies * LANES, width), 1)
    return (lane == first_head + column // HEAD_DIM).astype(BF16)


def dot(a, b):
    return jnp.dot(a, b, preferred_element_type=F32)


def ds(start, width):
    return pl.ds(pl.multiple_of(start, LANES), width)


def run(copies, sems):
    started = []
    for i, (source, target) in enumerate(copies):
        copy = pltpu.make_async_copy(source, target, sems.at[i])
        copy.start()
        started.append(copy)
    return started


PER_GROUP = HEADS * HEAD_DIM // GROUPS
INNER = HEADS * HEAD_DIM


def channels(group, first, width):
    return ds(group * PER_GROUP + first, width)


def pack_first_kernel(shards, place, xbc, send, sems):
    core, shard = place[2], place[4]
    width = WIDTHS[0]
    copies = []
    for r in range(shards):
        group = (shard ^ FLIP[r]) * PAIR + 1 - core
        copies.append((xbc.at[:, channels(group, 0, width)], send.at[:, r * width : (r + 1) * width]))
    for copy in run(copies, sems):
        copy.wait()


def pack_kernel(shards, place, xbc, dt_raw, order, send, tail, sems):
    core, shard = place[2], place[4]
    count = xbc.shape[0]
    first = WIDTHS[0]
    width = PER_GROUP - first
    rest = width * shards
    size = PER_GROUP + 2 * STATE
    copies = []
    for r in range(shards):
        group = (shard ^ FLIP[r]) * PAIR + 1 - core
        copies.append((xbc.at[:, channels(group, first, width)], send.at[:, r * width : (r + 1) * width]))
        for i in range(2):
            to = rest + (i * shards + r) * STATE
            copies.append((xbc.at[:, ds(INNER + (i * GROUPS + group) * STATE, STATE)], send.at[:, to : to + STATE]))
    copies.append((dt_raw, send.at[:, send.shape[1] - HEADS :]))
    for r in range(shards):
        group, to = (shard ^ FLIP[r]) * PAIR + core, r * size
        last = xbc.at[count - 16 :]
        copies.append((last.at[:, channels(group, 0, PER_GROUP)], tail.at[:, to : to + PER_GROUP]))
        for i in range(2):
            at = ds(INNER + (i * GROUPS + group) * STATE, STATE)
            start = to + PER_GROUP + i * STATE
            copies.append((last.at[:, at], tail.at[:, start : start + STATE]))
    for copy in run(copies, sems):
        copy.wait()


def taps_kernel(place, weight, bias, order, taps, offset, sems):
    copies = []
    for source, target in ((weight, taps), (bias, offset)):
        copies.append((source.at[:, channels(place[0], 0, PER_GROUP)], target.at[:, :PER_GROUP]))
        for i in range(2):
            at = ds(INNER + (i * GROUPS + place[0]) * STATE, STATE)
            start = PER_GROUP + i * STATE
            copies.append((source.at[:, at], target.at[:, start : start + STATE]))
    for copy in run(copies, sems):
        copy.wait()


def edge_kernel(shards, place, got_first, got, tail, out):
    count = got.shape[0]
    first = WIDTHS[0]
    width = PER_GROUP - first
    size = PER_GROUP + 2 * STATE
    for r in range(shards):
        theirs = [(got_first, r * first, first), (got, r * width, width)]
        theirs += [(got, width * shards + (i * shards + r) * STATE, STATE) for i in range(2)]
        to = r * size
        for ref, start, size_of in theirs:
            a = ref[count - 16 :, start : start + size_of].astype(F32)
            b = tail[:, to : to + size_of].astype(F32)
            out[:, to : to + size_of] = jnp.where(place[2] == 0, a, b)[13:16].astype(BF16)
            to += size_of


def total_of(piece):
    return WIDTHS[piece] + sum(LANES if kind == "D" else STATE for kind in RESTS[piece])


def merge_kernel(shards, plan, unread, place, xbc, dt_raw, got_first, got, edges, *refs):
    refs = refs[unread:]
    outs, sems = refs[: len(plan)], refs[-1]
    core, shard = place[2], place[4]
    count = xbc.shape[0]
    stride = PER_GROUP - WIDTHS[0]
    mine = pl.ds(pl.multiple_of(core * count, count), count)
    other = pl.ds(pl.multiple_of((1 - core) * count, count), count)
    copies, steps = [], []
    for out, (r, pieces) in zip(outs, plan):
        group = (shard ^ FLIP[r]) * PAIR + core
        to = 0
        for piece in pieces:
            first, width = sum(WIDTHS[:piece]), WIDTHS[piece]
            if piece == 0:
                source = got_first.at[:, r * width : (r + 1) * width]
            else:
                at = r * stride + first - WIDTHS[0]
                source = got.at[:, at : at + width]
            if width:
                copies.append((xbc.at[:, channels(group, first, width)], out.at[mine, to : to + width]))
                copies.append((source, out.at[other, to : to + width]))
            to += width
            for kind in RESTS[piece]:
                if kind == "D":
                    steps.append((out, r, to))
                    to += LANES
                    continue
                i = "BC".index(kind)
                at = ds(INNER + (i * GROUPS + group) * STATE, STATE)
                copies.append((xbc.at[:, at], out.at[mine, to : to + STATE]))
                at = stride * shards + (i * shards + r) * STATE
                copies.append((got.at[:, at : at + STATE], out.at[other, to : to + STATE]))
                to += STATE
    started = run(copies, sems)
    if steps:
        lane = lax.broadcasted_iota(jnp.int32, (count, LANES), 1)
        per_tile = LANES * GROUPS // HEADS
        heads = HEADS // GROUPS
        for out, r, to in steps:
            group = (shard ^ FLIP[r]) * PAIR + core
            tile, shift = group // per_tile, (LANES - (group % per_tile) * heads) % LANES
            own = dt_raw[:, ds(tile * LANES, LANES)].astype(F32)
            theirs = got[:, ds(got.shape[1] - HEADS + tile * LANES, LANES)].astype(F32)
            low = jnp.where(core == 0, own, theirs)
            high = jnp.where(core == 0, theirs, own)
            packed = jnp.zeros((count // 2, LANES), F32)
            for j, rows in enumerate((low, high)):
                rows = jnp.where(lane < heads, pltpu.roll(rows, shift, 1), 0.0)
                for i in range(2):
                    part = rows[i * count // 2 : (i + 1) * count // 2]
                    packed = packed + pltpu.roll(part, (2 * j + i) * heads, 1)
            out[: count // 2, to : to + LANES] = packed.astype(BF16)
            size = PER_GROUP + 2 * STATE
            at = slice(r * size, (r + 1) * size)
            edge = jnp.concatenate([edges[:, at].astype(F32), jnp.zeros((1, size), F32)], 0)
            edge = jnp.concatenate([edge[:, q * LANES : (q + 1) * LANES] for q in range(size // LANES)], 0)
            fill = jnp.zeros((PAIR * count - count // 2 - edge.shape[0], LANES), F32)
            out[count // 2 :, to : to + LANES] = jnp.concatenate([edge, fill], 0).astype(BF16)
    for copy in started:
        copy.wait()


def view(refs, piece):
    return [(ref, total_of(2) if piece == 3 and r == NEAR else 0) for r, ref in enumerate(refs)]


def convolve_in_order(place, blocks, columns, edge, tap, bias, wide, put):
    width = columns.stop - columns.start
    count = blocks[0][0].shape[0] // PAIR
    wide[5:8, :width] = edge
    for r, (block, origin) in enumerate(blocks):
        for core in range(PAIR):
            at = pl.multiple_of((core * len(blocks) + (place[4] ^ FLIP[r])) * count + 8, 8)
            part = block[core * count : (core + 1) * count, origin + columns.start : origin + columns.stop]
            wide[pl.ds(at, count), :width] = part.astype(F32)
    tap, bias = tap * 0.5, bias * 0.5
    for start in range(0, PAIR * len(blocks) * count, count):
        acc = bias + tap[0:1] * wide[start + 5 : start + 5 + count, :width]
        acc = acc + tap[1:2] * wide[start + 6 : start + 6 + count, :width]
        acc = acc + tap[2:3] * wide[start + 7 : start + 7 + count, :width]
        acc = acc + tap[3:4] * wide[start + 8 : start + 8 + count, :width]
        put(start, count, (acc + acc * jnp.tanh(acc)).astype(BF16))


def prep_kernel(shards, place, *refs):
    blocks, (taps, offset, a_ref, bias_ref, skip_ref, order) = refs[:shards], refs[shards : shards + 6]
    b_ref, edge_ref, cum_ref, row_ref, factor_ref, tail_ref, skip_out, dt_ref, wide = refs[shards + 6 :]
    blocks = view(blocks, 1)
    start = WIDTHS[1]
    last = total_of(1) - LANES
    size = edge_ref.shape[1]
    count = blocks[0][0].shape[0] // PAIR
    half, heads = count // 2, HEADS // GROUPS
    columns = [block[:, origin + last : origin + last + LANES].astype(F32) for block, origin in blocks]
    edge = columns[0][half : half + 4 * size // LANES]
    for column in columns[1:]:
        edge = edge + column[half : half + 4 * size // LANES]
    for q in range(size // LANES):
        edge_ref[:, q * LANES : (q + 1) * LANES] = edge[4 * q : 4 * q + 4]
    for r, column in enumerate(columns):
        packed = column[:half]
        for j in range(2 * PAIR):
            at = ((j // 2) * shards + (place[4] ^ FLIP[r])) * count + (j % 2) * half
            rows = packed if j == 0 else pltpu.roll(packed, LANES - j * heads, 1)
            dt_ref[pl.ds(pl.multiple_of(at, half), half), :] = rows

    def put(start, count, value):
        b_ref[start : start + count] = value

    at = slice(PER_GROUP, PER_GROUP + STATE)
    convolve_in_order(
        place, blocks, slice(start, start + STATE), edge_ref[0:3, at], taps[:, at], offset[:, at], wide, put
    )
    per_tile = LANES * GROUPS // HEADS
    group = place[0]
    tile = group // per_tile
    shift = (LANES - (group % per_tile) * heads) % LANES

    def lanes_of(ref):
        return pltpu.roll(jnp.broadcast_to(ref[pl.ds(tile, 1), :], (8, LANES)), shift, 1)

    rate = -jnp.exp(lanes_of(a_ref)[0:1])
    raw = dt_ref[...] + lanes_of(bias_ref)[0:1]
    step = jnp.maximum(raw, 0.0) + jnp.log1p(jnp.exp(-jnp.abs(raw)))
    skip = lanes_of(skip_ref)
    skip_out[...] = jnp.concatenate(halves(jnp.concatenate([skip, skip], 0), 3), 1)
    lower = (
        lax.broadcasted_iota(jnp.int32, (BLOCK, BLOCK), 0)
        >= lax.broadcasted_iota(jnp.int32, (BLOCK, BLOCK), 1)
    ).astype(BF16)
    valid = lax.broadcasted_iota(jnp.int32, (BLOCK, LANES), 1) < heads
    for block in range(PAIR):
        at = slice(block * BLOCK, (block + 1) * BLOCK)
        here = jnp.where(valid, step[at], 1.0)
        parts = halves(here * rate, 3)
        cum = dot(lower, parts[0]) + (dot(lower, parts[1]) + dot(lower, parts[2]))
        cum = cum * LOG2E
        cum_ref[at] = cum
        row_ref[:, at] = jnp.transpose(cum - jnp.log2(here))
        factor_ref[at] = jnp.concatenate(halves(jnp.exp2(cum), 2), 1)
        tail = jnp.exp2(cum[BLOCK - 1 :] - cum) * here
        tail_ref[at] = jnp.concatenate(halves(tail, 2), 1)


def score_kernel(shards, place, *refs):
    blocks, refs = refs[:shards], refs[shards:]
    taps, offset, edge_ref, b_ref, c_ref, score_ref, wide = (*refs[:4], *refs[-3:])
    blocks = view(blocks, 3)
    start = WIDTHS[3]
    at = slice(PER_GROUP + STATE, PER_GROUP + 2 * STATE)

    def put(start, count, value):
        c_ref[start : start + count] = value

    convolve_in_order(
        place, blocks, slice(start, start + STATE), edge_ref[0:3, at], taps[:, at], offset[:, at], wide, put
    )
    for block in range(PAIR):
        at = slice(block * BLOCK, (block + 1) * BLOCK)
        score_ref[at] = lax.dot_general(
            c_ref[at], b_ref[at], (((1,), (1,)), ((), ())), preferred_element_type=F32
        )


def decay_of(ref):
    decay = ref[STATE : STATE + 16].astype(F32)
    return decay[0:1] + (decay[1:2] + decay[2:3])


def put_decay(ref, decay):
    row = lax.broadcasted_iota(jnp.int32, (16, ref.shape[1]), 0)
    high, middle, low = (part.astype(F32) for part in halves(decay, 3))
    packed = jnp.where(row == 0, high, jnp.where(row == 1, middle, jnp.where(row == 2, low, 0.0)))
    ref[STATE:] = packed.astype(BF16)


def state_kernel(shards, part, sizes, place, *refs):
    blocks, refs = refs[:shards], refs[shards:]
    taps, offset, edge_ref, b_ref, factor_ref, tail_ref = refs[:6]
    x_ref, own_ref, *sends, wide = refs[-3 - len(sizes) :]
    piece, start, width = part
    first = sum(WIDTHS[:piece]) + start
    at = slice(first, first + width)

    def put(row, count, value):
        x_ref[row : row + count] = value

    blocks = view(blocks, piece)
    columns = slice(start, start + width)
    convolve_in_order(place, blocks, columns, edge_ref[0:3, at], taps[:, at], offset[:, at], wide, put)
    expand = spread(first // HEAD_DIM, width, 2)
    both = []
    for block in range(PAIR):
        at = slice(block * BLOCK, (block + 1) * BLOCK)
        loaded = (x_ref[at].astype(F32) * dot(tail_ref[at], expand)).astype(BF16)
        both.append(
            lax.dot_general(b_ref[at], loaded, (((0,), (0,)), ((), ())), preferred_element_type=F32)
        )
    ends = [dot(factor_ref[(i + 1) * BLOCK - 16 : (i + 1) * BLOCK], expand)[15:16] for i in range(PAIR)]
    own_ref[...] = both[0]
    end = (ends[1] * both[0] + both[1]).astype(BF16)
    decay = ends[0] * ends[1]
    start = 0
    for send_ref in sends:
        at = slice(start, start + send_ref.shape[1])
        send_ref[0:STATE] = end[:, at]
        put_decay(send_ref, decay[:, at])
        start = at.stop


def combine_kernel(spans, place, *refs):
    count = len(spans)
    got, own, out_ref = refs[:count], refs[count : 2 * count], refs[-1]
    odd = place[1] % 2 == 1
    start = 0
    for got_ref, own_ref, span in zip(got, own, spans):
        at = slice(start, start + span.stop - span.start)
        theirs, mine = got_ref[:STATE, span].astype(F32), own_ref[:STATE, span].astype(F32)
        decay, other = decay_of(own_ref.at[:, span]), decay_of(got_ref.at[:, span])
        early, late = jnp.where(odd, theirs, mine), jnp.where(odd, mine, theirs)
        out_ref[:STATE, at] = (jnp.where(odd, decay, other) * early + late).astype(BF16)
        put_decay(out_ref.at[:, at], decay * other)
        start = at.stop


def mix(first_head, x_ref, cum_ref, row_ref, score_ref, skip_ref, put):
    width = x_ref.shape[1]
    half = BLOCK // 2
    expand = spread(first_head, width, 3)
    skip = dot(skip_ref[...], expand)[0:1]
    lower = lax.broadcasted_iota(jnp.int32, (half, half), 0) >= lax.broadcasted_iota(
        jnp.int32, (half, half), 1
    )
    lane = lax.broadcasted_iota(jnp.int32, (BLOCK, LANES), 1)
    for block in range(PAIR):
        base = block * BLOCK
        for tile in range(width // LANES):
            columns = slice(tile * LANES, (tile + 1) * LANES)
            x = x_ref[base : base + BLOCK, columns]
            top = skip[:, columns] * x[:half].astype(F32)
            bottom = skip[:, columns] * x[half:].astype(F32)
            for side in range(LANES // HEAD_DIM):
                head = first_head + tile * (LANES // HEAD_DIM) + side
                own = jnp.where(lane // HEAD_DIM == side, x, jnp.zeros_like(x))
                cum = cum_ref[base : base + BLOCK, head : head + 1]
                row = row_ref[head : head + 1, base : base + BLOCK]
                diag = jnp.where(lower, cum[:half] - row[:, :half], -1e30)
                mixing = jnp.exp2(diag) * score_ref[base : base + half, :half]
                top = top + dot(mixing.astype(BF16), own[:half])
                left = jnp.exp2(cum[half:] - row[:, :half]) * score_ref[base + half : base + BLOCK, :half]
                diag = jnp.where(lower, cum[half:] - row[:, half:], -1e30)
                right = jnp.exp2(diag) * score_ref[base + half : base + BLOCK, half:]
                mixing = jnp.concatenate([left.astype(BF16), right.astype(BF16)], 1)
                bottom = bottom + dot(mixing, own)
            put(block, slice(base, base + half), columns, top)
            put(block, slice(base + half, base + BLOCK), columns, bottom)


def local_kernel(first_head, x_ref, cum_ref, row_ref, score_ref, skip_ref, *refs):
    out_ref = refs[-1]

    def put(block, rows, columns, value):
        out_ref[rows, columns] = value

    mix(first_head, x_ref, cum_ref, row_ref, score_ref, skip_ref, put)


def carry(first_head, place, lasts, befores, own_ref, c_ref, factor_ref, add, keep_ref, send_ref):
    expand = spread(first_head, own_ref.shape[1], 2)
    last, before = (
        refs[0][...] if len(refs) == 1 else jnp.concatenate([ref[...] for ref in refs], 1)
        for refs in (lasts, befores)
    )
    odd, core = place[1] % 2 == 1, place[2]
    near = jnp.where(odd, last[:STATE].astype(F32), 0.0)
    held = near + jnp.where(odd, decay_of(last), 1.0) * before[:STATE].astype(F32)
    factor = dot(factor_ref[...], expand)
    outs = []
    for block in range(PAIR):
        at = slice(block * BLOCK, (block + 1) * BLOCK)
        carried = dot(c_ref[at], held.astype(BF16))
        outs.append((add[at] + factor[at] * carried).astype(BF16))
        held = factor[BLOCK - 1 : BLOCK] * held + own_ref[...]

    @pl.when(core == 0)
    def _():
        keep_ref[...] = outs[0]
        send_ref[...] = outs[1]

    @pl.when(core == 1)
    def _():
        keep_ref[...] = outs[1]
        send_ref[...] = outs[0]


def final_kernel(first_head, counts, place, *refs):
    groups = []
    for number in counts:
        groups.append(refs[:number])
        refs = refs[number:]
    carry(first_head, place, *groups, *refs[:4], *refs[-2:])


def finish_kernel(first_head, counts, place, *refs):
    groups = []
    for number in counts:
        groups.append(refs[:number])
        refs = refs[number:]
    own_ref, c_ref, factor_ref = refs[:3]
    keep_ref, send_ref, partial = refs[-3:]
    local_kernel(first_head, *refs[3:8], partial)
    carry(first_head, place, *groups, own_ref, c_ref, factor_ref, partial, keep_ref, send_ref)


def place_kernel(firsts, place, *refs):
    count = len(firsts)
    keeps, gots = refs[:count], refs[count : 2 * count]
    out, sems = refs[-2:]
    core = place[2]
    half = out.shape[1] // PAIR
    copies = []
    for first, keep, got in zip(firsts, keeps, gots):
        width = keep.shape[1]
        copies.append((keep, out.at[:, ds(core * half + first, width)]))
        copies.append((got, out.at[:, ds((1 - core) * half + first, width)]))
    for copy in run(copies, sems):
        copy.wait()


def put_in_place(firsts, shape, place, keeps, gots):
    smem, vmem, hbm = (pl.BlockSpec(memory_space=m) for m in (pltpu.SMEM, pltpu.VMEM, pltpu.HBM))
    count = len(firsts)
    return pl.pallas_call(
        functools.partial(place_kernel, firsts),
        out_shape=jax.ShapeDtypeStruct(shape, BF16),
        in_specs=[smem] + [vmem] * (2 * count),
        out_specs=hbm,
        scratch_shapes=[pltpu.SemaphoreType.DMA((2 * count,))],
        compiler_params=pltpu.CompilerParams(vmem_limit_bytes=16 << 20),
        cost_estimate=pl.CostEstimate(flops=1, bytes_accessed=1, transcendentals=0),
        name="place",
    )(place, *keeps, *gots)


class Stay:
    def __init__(self, array):
        self.array = array


def gate(blocks, order):
    anywhere = pl.BlockSpec(memory_space=pl.ANY)
    return pl.pallas_call(
        lambda *refs: None,
        out_shape=[jax.ShapeDtypeStruct(block.shape, block.dtype) for block in blocks],
        in_specs=[anywhere] * (len(blocks) + len(order)),
        out_specs=[anywhere] * len(blocks),
        input_output_aliases={i: i for i in range(len(blocks))},
        compiler_params=pltpu.CompilerParams(vmem_limit_bytes=16 << 20),
        cost_estimate=pl.CostEstimate(flops=1, bytes_accessed=1, transcendentals=0),
        name="gate",
    )(*blocks, *order)


def call(body, outs, operands, scratch=(), flops=0, transcendentals=0, name=None, limit=16 << 20):
    shapes = [jax.ShapeDtypeStruct(shape, dtype) for shape, dtype in outs]
    smem, vmem, hbm = (pl.BlockSpec(memory_space=m) for m in (pltpu.SMEM, pltpu.VMEM, pltpu.HBM))
    specs = [
        hbm if isinstance(o, Stay) else smem if o.dtype == jnp.int32 else vmem for o in operands
    ]
    moved = sum(o.size * o.dtype.itemsize for o in shapes) * 2
    return pl.pallas_call(
        body,
        out_shape=shapes,
        in_specs=specs,
        out_specs=[vmem] * len(outs),
        scratch_shapes=scratch,
        compiler_params=pltpu.CompilerParams(vmem_limit_bytes=limit),
        cost_estimate=pl.CostEstimate(flops=1, bytes_accessed=1, transcendentals=0),
        name=name,
    )(*[o.array if isinstance(o, Stay) else o for o in operands])


def paired(xbc, dt_raw, conv_weight, conv_bias, a_log, dt_bias, skip_gain):
    axes = ("ctx", "head")
    shards, length = lax.axis_size("head"), lax.axis_size("ctx")
    devices, peers = shards * length, shards * PAIR
    tok = xbc.shape[0]
    slab = tok * peers
    context, shard = lax.axis_index("ctx"), lax.axis_index("head")
    pair, core = context // PAIR, context % PAIR
    group = shard * PAIR + core
    place = jnp.stack([group, pair, core, core * shards + shard, shard]).astype(jnp.int32)

    def over(block, target):
        route = [(i, target(i)) for i in range(devices)]
        return lax.ppermute(block, axes, [(i, j) for i, j in route if j is not None and j < devices])

    def swap(block):
        return over(block, lambda i: i ^ shards)

    rows = Stay(xbc)
    size = PER_GROUP + 2 * STATE
    (sent,) = call(
        functools.partial(pack_first_kernel, shards),
        [((tok, shards * WIDTHS[0]), BF16)],
        [place, rows],
        scratch=[pltpu.SemaphoreType.DMA((shards,))],
        name="pack_first",
    )
    got_first = swap(sent)
    sent, tail = call(
        functools.partial(pack_kernel, shards),
        [((tok, shards * (size - WIDTHS[0]) + HEADS), BF16), ((16, shards * size), BF16)],
        [place, rows, Stay(dt_raw), Stay(sent)],
        scratch=[pltpu.SemaphoreType.DMA((6 * shards + 1,))],
        name="pack",
    )
    got_rest = swap(gate([sent], [got_first])[0])
    taps, offset = call(
        taps_kernel,
        [((4, size), F32), ((1, size), F32)],
        [place, Stay(conv_weight), Stay(conv_bias[None]), Stay(got_rest)],
        scratch=[pltpu.SemaphoreType.DMA((6,))],
        name="taps",
    )

    def send_on(plan, order, edges=None):
        unused = Stay(got_first)
        parts = [p for _, pieces in plan for p in pieces]
        return call(
            functools.partial(merge_kernel, shards, plan, len(order)),
            [((PAIR * tok, sum(map(total_of, pieces))), BF16) for _, pieces in plan],
            [
                place,
                rows,
                Stay(dt_raw) if edges is None else dt_raw,
                got_first if 0 in parts else unused,
                got_rest if any(parts) else unused,
                unused if edges is None else edges,
            ]
            + [Stay(o) for o in order],
            scratch=[pltpu.SemaphoreType.DMA((sum(2 + 2 * len(RESTS[p]) for p in parts),))],
            name="merge",
        )

    def travel(blocks):
        return [blocks[0]] + [over(blocks[r], lambda i, r=r: i ^ FLIP[r]) for r in range(1, shards)]

    def plan(piece):
        return [(r, (piece,)) for r in range(shards)]

    first_blocks = send_on(plan(0), [])
    message = [travel(first_blocks)]
    (edges,) = call(
        functools.partial(edge_kernel, shards),
        [((3, shards * size), BF16)],
        [place, got_first, got_rest, tail],
        name="edge",
    )
    edges = over(edges, lambda i: i + peers if i % shards == shards - 1 else None)
    second_blocks = send_on(plan(1), [first_blocks[0]], edges)
    message.append(travel(second_blocks))
    third_plan = [(r, (2, 3) if r == NEAR else (2,)) for r in range(shards)]
    third_blocks = send_on(third_plan, [second_blocks[0]])
    message.append(travel(third_blocks[:1] + gate(third_blocks[1:], message[0][1:] + message[1][1:] + [taps])))

    def seen(piece):
        return message[piece]

    tiles = [p.reshape(HEADS // LANES, LANES) for p in (a_log, dt_bias, skip_gain)]
    b, edge, cum, row, factor, tail, skip = call(
        functools.partial(prep_kernel, shards),
        [
            ((slab, STATE), BF16),
            ((4, size), F32),
            ((slab, LANES), F32),
            ((LANES, slab), F32),
            ((slab, 2 * LANES), BF16),
            ((slab, 2 * LANES), BF16),
            ((16, 3 * LANES), BF16),
        ],
        [place] + seen(1) + [taps, offset] + tiles + [Stay(third_blocks[0])],
        scratch=[pltpu.VMEM((slab, LANES), F32), pltpu.VMEM((slab + 8, STATE), F32)],
        name="prep",
    )
    count = len(GROUPED)
    x, sent, own, last, joined, before, keep, send = ([None] * count for _ in range(8))

    def first_head(i):
        return (sum(WIDTHS[: GROUPED[i][0]]) + GROUPED[i][1]) // HEAD_DIM

    def state_of(i, order):
        piece, _, width = GROUPED[i]
        x[i], own[i], *sent[i] = call(
            functools.partial(state_kernel, shards, GROUPED[i], FIRST_ROUND[i]),
            [((slab, width), BF16), ((STATE, width), F32)] + [((STATE + 16, w), BF16) for w in FIRST_ROUND[i]],
            [place] + seen(piece) + [taps, offset, edge, b, factor, tail] + [Stay(o) for o in order],
            scratch=[pltpu.VMEM((slab + 8, width), F32)],
            name="state",
        )
        last[i] = [over(part, lambda i: i ^ peers if i // peers != 3 else None) for part in sent[i]]

    def combine_of(i, order):
        joined[i], before[i] = [], []
        end = 0
        for width in SECOND_ROUND[i]:
            begin, end = end, end + width
            early, late, spans, first = [], [], [], 0
            for got, mine, size_of in zip(last[i], sent[i], FIRST_ROUND[i]):
                low, high = max(begin - first, 0), min(end - first, size_of)
                first += size_of
                if low < high:
                    early.append(got)
                    late.append(mine)
                    spans.append(slice(low, high))
            (total,) = call(
                functools.partial(combine_kernel, spans),
                [((STATE + 16, width), BF16)],
                [place] + early + late + [Stay(o) for o in order],
                name="combine",
            )
            joined[i].append(total)
            before[i].append(over(total, lambda i: i + 2 * peers))
            order = [total]

    def finish_of(body, i, operands, order, **more):
        keep[i], send[i] = call(
            functools.partial(body, first_head(i), (len(last[i]), len(before[i]))),
            [((BLOCK, GROUPED[i][2]), BF16)] * 2,
            [place, *last[i], *before[i], own[i], c, factor] + operands + [Stay(o) for o in order],
            name="final",
            **more,
        )

    partial = [None] * count

    def local_of(i, order):
        (partial[i],) = call(
            functools.partial(local_kernel, first_head(i)),
            [(x[i].shape, F32)],
            [x[i], cum, row, score, skip] + [Stay(o) for o in order],
            name="local",
        )

    state_of(0, [])
    own_block, *fourth_blocks = send_on([(r, (3,)) for r in range(shards) if r != NEAR], sent[0])
    fourth_blocks = gate(fourth_blocks, message[2][1:])
    fourth_blocks = [over(block, lambda i, r=r: i ^ FLIP[r]) for r, block in enumerate(fourth_blocks, 1)]
    message.append([own_block, *fourth_blocks, message[2][NEAR]])
    combine_of(0, [own_block])
    state_of(1, joined[0])
    combine_of(1, [])
    state_of(2, joined[1])
    c, score = call(
        functools.partial(score_kernel, shards),
        [((slab, STATE), BF16), ((slab, BLOCK), F32)],
        [place] + seen(3) + [taps, offset, edge, b] + [Stay(o) for o in sent[2]],
        scratch=[pltpu.VMEM((slab + 8, STATE), F32)],
        name="score",
    )
    local_of(0, [])
    state_of(3, [partial[0]])

    def in_full(i, order):
        wide = [pltpu.VMEM((slab, GROUPED[i][2]), F32)]
        finish_of(finish_kernel, i, [x[i], cum, row, score, skip], order, scratch=wide)

    combine_of(2, sent[3] + before[1] + before[0])
    in_full(1, joined[2])
    combine_of(3, [keep[1]])
    local_of(2, joined[3])
    local_of(3, [partial[2]])
    finish_of(final_kernel, 0, [partial[0]], [partial[3]])
    finish_of(final_kernel, 2, [partial[2]], [keep[0]])
    finish_of(final_kernel, 3, [partial[3]], [keep[2]])
    firsts = [first_head(i) * HEAD_DIM for i in range(count)]
    return put_in_place(firsts, (BLOCK, PAIR * PER_GROUP), place, keep, [swap(o) for o in send])


def solution(mesh):
    in_specs = (P(("ctx", "head"), None), P(("ctx", "head"), None), P(), P(), P(), P(), P())
    out_specs = P("ctx", "head")
    shards, length = mesh.shape["head"], mesh.shape["ctx"]

    def program(xbc, *rest):
        slab = xbc.shape[0] // length
        fits = shards == GROUPS // PAIR and length == 4 * PAIR and slab == BLOCK
        return jax.shard_map(
            paired if fits else on_device,
            mesh=mesh,
            in_specs=in_specs,
            out_specs=out_specs,
            check_vma=False,
        )(xbc, *rest)

    return program
```

```python
import functools

import jax
import jax.numpy as jnp
from jax import lax
from jax.experimental import pallas as pl
from jax.experimental.pallas import tpu as pltpu
from jax.sharding import PartitionSpec as P

HEADS = 256
HEAD_DIM = 64
STATE = 256
GROUPS = 8
BLOCK = 256


def from_behind(block, axis, distance):
    devices = range(lax.axis_size(axis))
    route = [(i - distance, i) for i in devices if i - distance in devices]
    return lax.ppermute(block, axis, route)


def carried_in(array, axis, combine, identity):
    length, index = (lax.axis_size(axis), lax.axis_index(axis))
    everything = jax.tree.map(lambda part: lax.all_gather(part, axis), array)
    start = jax.tree.map(
        lambda part, zero: jnp.broadcast_to(jnp.asarray(zero, part.dtype), part.shape),
        array,
        identity,
    )

    def hop(k, before):
        reached = k < index
        new = combine(before, jax.tree.map(lambda part: part[k], everything))
        return jax.tree.map(lambda a, b: jnp.where(reached, a, b), new, before)

    return lax.fori_loop(0, length, hop, start)


def convolve(rows, edge, weight, bias):
    count = rows.shape[0]
    wide = jnp.concatenate([edge, rows], 0).astype(jnp.float32)
    acc = bias[None, :] + weight[0] * wide[0:count]
    acc = acc + weight[1] * wide[1 : count + 1]
    acc = acc + weight[2] * wide[2 : count + 2]
    acc = acc + weight[3] * wide[3 : count + 3]
    return jax.nn.silu(acc).astype(jnp.bfloat16)


def rearrange_heads(rows, shards, per_dev, groups_dev, per_group):
    count = rows.shape[0]
    inner = HEADS * HEAD_DIM
    replicate_groups = max(1, per_group // per_dev)
    heads_part = rows[:, :inner].reshape(count, shards, per_dev * HEAD_DIM)
    b_part = rows[:, inner : inner + GROUPS * STATE].reshape(count, GROUPS, STATE)
    c_part = rows[:, inner + GROUPS * STATE :].reshape(count, GROUPS, STATE)
    b_part = jnp.repeat(b_part, replicate_groups, axis=1).reshape(count, shards, groups_dev * STATE)
    c_part = jnp.repeat(c_part, replicate_groups, axis=1).reshape(count, shards, groups_dev * STATE)
    return jnp.concatenate([heads_part, b_part, c_part], axis=2)


def inner_block(xs, bmat, cmat, steps, cum):
    size = xs.shape[0]
    lower = jnp.arange(size)[:, None] >= jnp.arange(size)[None, :]
    scores = jnp.einsum("qgn,kgn->gqk", cmat, bmat, preferred_element_type=jnp.float32)
    order = jnp.transpose(cum, (1, 2, 0))
    gap = order[..., :, None] - order[..., None, :]
    decay = jnp.exp(jnp.where(lower, gap, -jnp.inf))
    mixing = (scores[:, None] * decay * jnp.transpose(steps, (1, 2, 0))[..., None, :]).astype(
        jnp.bfloat16
    )
    local = jnp.einsum("gjqk,kgjp->qgjp", mixing, xs, preferred_element_type=jnp.float32)
    tail = jnp.exp(cum[size - 1][None] - cum) * steps
    loaded = (bmat[:, :, None, :].astype(jnp.float32) * tail[..., None]).astype(jnp.bfloat16)
    block_state = jnp.einsum("kgjn,kgjp->gjnp", loaded, xs, preferred_element_type=jnp.float32)
    return (local, block_state)


def on_device(xbc, dt_raw, conv_weight, conv_bias, a_log, dt_bias, skip_gain):
    tok = xbc.shape[0]
    shards = lax.axis_size("head")
    per_dev = HEADS // shards
    per_group = HEADS // GROUPS
    groups_dev = max(1, per_dev // per_group)
    heads_per_cluster = per_dev // groups_dev
    sent = rearrange_heads(xbc, shards, per_dev, groups_dev, per_group)
    mine, rates = (
        lax.all_to_all(sent, "head", split_axis=1, concat_axis=0, tiled=True),
        lax.all_to_all(
            dt_raw.reshape(tok, shards, per_dev), "head", split_axis=1, concat_axis=0, tiled=True
        ),
    )
    slab = tok * shards
    mine = mine.reshape(slab, mine.shape[2])
    rates = rates.reshape(slab, per_dev)
    shard = lax.axis_index("head")
    taps = lax.dynamic_index_in_dim(
        rearrange_heads(conv_weight, shards, per_dev, groups_dev, per_group),
        shard,
        1,
        keepdims=False,
    )
    offset = lax.dynamic_index_in_dim(
        rearrange_heads(conv_bias[None, :], shards, per_dev, groups_dev, per_group),
        shard,
        1,
        keepdims=False,
    )
    edge = from_behind(mine[slab - 3 :], "ctx", 1)
    mine = convolve(mine, edge, taps, offset[0])
    nchunk = slab // BLOCK
    width = per_dev * HEAD_DIM
    xs = mine[:, :width].reshape(nchunk, BLOCK, groups_dev, heads_per_cluster, HEAD_DIM)
    bmat = mine[:, width : width + groups_dev * STATE].reshape(nchunk, BLOCK, groups_dev, STATE)
    cmat = mine[:, width + groups_dev * STATE :].reshape(nchunk, BLOCK, groups_dev, STATE)
    first = shard * per_dev
    rate = (-jnp.exp(lax.dynamic_slice_in_dim(a_log, first, per_dev))).reshape(
        groups_dev, heads_per_cluster
    )
    bias_dt = lax.dynamic_slice_in_dim(dt_bias, first, per_dev).reshape(
        groups_dev, heads_per_cluster
    )
    skip = lax.dynamic_slice_in_dim(skip_gain, first, per_dev).reshape(
        groups_dev, heads_per_cluster
    )
    steps = jax.nn.softplus(
        rates.astype(jnp.float32).reshape(nchunk, BLOCK, groups_dev, heads_per_cluster) + bias_dt
    )
    cum = jnp.cumsum(steps * rate, axis=1)

    def block_step(carry, item):
        held, product = carry
        x_part, b_part, c_part, step_part, cum_part = item
        local, block_state = inner_block(x_part, b_part, c_part, step_part, cum_part)
        lifted = c_part.astype(jnp.float32)[:, :, None, :] * jnp.exp(cum_part)[..., None]
        carried = jnp.einsum("qgjn,gjnp->qgjp", lifted, held, precision=lax.Precision.HIGHEST)
        partial_out = local + carried + skip[..., None] * x_part.astype(jnp.float32)
        end = jnp.exp(cum_part[BLOCK - 1])
        return ((end[..., None, None] * held + block_state, product * end), (partial_out, product))

    zero_state = jnp.zeros((groups_dev, heads_per_cluster, STATE, HEAD_DIM), jnp.float32)
    unit = jnp.ones((groups_dev, heads_per_cluster), jnp.float32)
    (slab_state, slab_decay), (partials, product_in) = lax.scan(
        block_step, (zero_state, unit), (xs, bmat, cmat, steps, cum)
    )

    def combine(preceding_state, later):
        return (
            preceding_state[0] * later[0],
            later[0][..., None, None] * preceding_state[1] + later[1],
        )

    _, entering = carried_in((slab_decay, slab_state), "ctx", combine, (unit, zero_state))
    projected = jnp.einsum(
        "cqgn,gjnp->cqgjp", cmat.astype(jnp.float32), entering, precision=lax.Precision.HIGHEST
    )
    factor = jnp.exp(cum) * product_in[:, None]
    total = partials + factor[..., None] * projected
    return total.astype(jnp.bfloat16).reshape(slab, width)


PAIR = 2
LANES = 128
LOG2E = 1.4426950408889634
F32, BF16 = jnp.float32, jnp.bfloat16
WIDTHS = (512, 0, 768, 768)
RESTS = ("", "BD", "", "C")
GROUPED = ((0, 0, 512), (2, 0, 768), (3, 0, 384), (3, 384, 384))
FIRST_ROUND = ((256, 256), (384, 384), (384,), (384,))
SECOND_ROUND = ((512,), (384, 384), (384,), (384,))


FLIP = (0, 2, 3, 1)
NEAR = 3


def halves(value, count):
    parts = []
    for _ in range(count):
        part = value.astype(BF16)
        parts.append(part)
        value = value - part.astype(F32)
    return parts


def spread(first_head, width, copies):
    lane = lax.broadcasted_iota(jnp.int32, (copies * LANES, width), 0) % LANES
    column = lax.broadcasted_iota(jnp.int32, (copies * LANES, width), 1)
    return (lane == first_head + column // HEAD_DIM).astype(BF16)


def dot(a, b):
    return jnp.dot(a, b, preferred_element_type=F32)


def ds(start, width):
    return pl.ds(pl.multiple_of(start, LANES), width)


def run(copies, sems):
    started = []
    for i, (source, target) in enumerate(copies):
        copy = pltpu.make_async_copy(source, target, sems.at[i])
        copy.start()
        started.append(copy)
    return started


PER_GROUP = HEADS * HEAD_DIM // GROUPS
INNER = HEADS * HEAD_DIM


def channels(group, first, width):
    return ds(group * PER_GROUP + first, width)


def pack_first_kernel(shards, place, xbc, send, sems):
    core, shard = place[2], place[4]
    width = WIDTHS[0]
    copies = []
    for r in range(shards):
        group = (shard ^ FLIP[r]) * PAIR + 1 - core
        copies.append((xbc.at[:, channels(group, 0, width)], send.at[:, r * width : (r + 1) * width]))
    for copy in run(copies, sems):
        copy.wait()


def pack_kernel(shards, place, xbc, dt_raw, order, send, tail, sems):
    core, shard = place[2], place[4]
    count = xbc.shape[0]
    first = WIDTHS[0]
    width = PER_GROUP - first
    rest = width * shards
    size = PER_GROUP + 2 * STATE
    copies = []
    for r in range(shards):
        group = (shard ^ FLIP[r]) * PAIR + 1 - core
        copies.append((xbc.at[:, channels(group, first, width)], send.at[:, r * width : (r + 1) * width]))
        for i in range(2):
            to = rest + (i * shards + r) * STATE
            copies.append((xbc.at[:, ds(INNER + (i * GROUPS + group) * STATE, STATE)], send.at[:, to : to + STATE]))
    copies.append((dt_raw, send.at[:, send.shape[1] - HEADS :]))
    for r in range(shards):
        group, to = (shard ^ FLIP[r]) * PAIR + core, r * size
        last = xbc.at[count - 16 :]
        copies.append((last.at[:, channels(group, 0, PER_GROUP)], tail.at[:, to : to + PER_GROUP]))
        for i in range(2):
            at = ds(INNER + (i * GROUPS + group) * STATE, STATE)
            start = to + PER_GROUP + i * STATE
            copies.append((last.at[:, at], tail.at[:, start : start + STATE]))
    for copy in run(copies, sems):
        copy.wait()


def taps_kernel(place, weight, bias, order, taps, offset, sems):
    copies = []
    for source, target in ((weight, taps), (bias, offset)):
        copies.append((source.at[:, channels(place[0], 0, PER_GROUP)], target.at[:, :PER_GROUP]))
        for i in range(2):
            at = ds(INNER + (i * GROUPS + place[0]) * STATE, STATE)
            start = PER_GROUP + i * STATE
            copies.append((source.at[:, at], target.at[:, start : start + STATE]))
    for copy in run(copies, sems):
        copy.wait()


def edge_kernel(shards, place, got_first, got, tail, out):
    count = got.shape[0]
    first = WIDTHS[0]
    width = PER_GROUP - first
    size = PER_GROUP + 2 * STATE
    for r in range(shards):
        theirs = [(got_first, r * first, first), (got, r * width, width)]
        theirs += [(got, width * shards + (i * shards + r) * STATE, STATE) for i in range(2)]
        to = r * size
        for ref, start, size_of in theirs:
            a = ref[count - 16 :, start : start + size_of].astype(F32)
            b = tail[:, to : to + size_of].astype(F32)
            out[:, to : to + size_of] = jnp.where(place[2] == 0, a, b)[13:16].astype(BF16)
            to += size_of


def total_of(piece):
    return WIDTHS[piece] + sum(LANES if kind == "D" else STATE for kind in RESTS[piece])


def merge_kernel(shards, plan, unread, place, xbc, dt_raw, got_first, got, edges, *refs):
    refs = refs[unread:]
    outs, sems = refs[: len(plan)], refs[-1]
    core, shard = place[2], place[4]
    count = xbc.shape[0]
    stride = PER_GROUP - WIDTHS[0]
    mine = pl.ds(pl.multiple_of(core * count, count), count)
    other = pl.ds(pl.multiple_of((1 - core) * count, count), count)
    copies, steps = [], []
    for out, (r, pieces) in zip(outs, plan):
        group = (shard ^ FLIP[r]) * PAIR + core
        to = 0
        for piece in pieces:
            first, width = sum(WIDTHS[:piece]), WIDTHS[piece]
            if piece == 0:
                source = got_first.at[:, r * width : (r + 1) * width]
            else:
                at = r * stride + first - WIDTHS[0]
                source = got.at[:, at : at + width]
            if width:
                copies.append((xbc.at[:, channels(group, first, width)], out.at[mine, to : to + width]))
                copies.append((source, out.at[other, to : to + width]))
            to += width
            for kind in RESTS[piece]:
                if kind == "D":
                    steps.append((out, r, to))
                    to += LANES
                    continue
                i = "BC".index(kind)
                at = ds(INNER + (i * GROUPS + group) * STATE, STATE)
                copies.append((xbc.at[:, at], out.at[mine, to : to + STATE]))
                at = stride * shards + (i * shards + r) * STATE
                copies.append((got.at[:, at : at + STATE], out.at[other, to : to + STATE]))
                to += STATE
    started = run(copies, sems)
    if steps:
        lane = lax.broadcasted_iota(jnp.int32, (count, LANES), 1)
        per_tile = LANES * GROUPS // HEADS
        heads = HEADS // GROUPS
        for out, r, to in steps:
            group = (shard ^ FLIP[r]) * PAIR + core
            tile, shift = group // per_tile, (LANES - (group % per_tile) * heads) % LANES
            own = dt_raw[:, ds(tile * LANES, LANES)].astype(F32)
            theirs = got[:, ds(got.shape[1] - HEADS + tile * LANES, LANES)].astype(F32)
            low = jnp.where(core == 0, own, theirs)
            high = jnp.where(core == 0, theirs, own)
            packed = jnp.zeros((count // 2, LANES), F32)
            for j, rows in enumerate((low, high)):
                rows = jnp.where(lane < heads, pltpu.roll(rows, shift, 1), 0.0)
                for i in range(2):
                    part = rows[i * count // 2 : (i + 1) * count // 2]
                    packed = packed + pltpu.roll(part, (2 * j + i) * heads, 1)
            out[: count // 2, to : to + LANES] = packed.astype(BF16)
            size = PER_GROUP + 2 * STATE
            at = slice(r * size, (r + 1) * size)
            edge = jnp.concatenate([edges[:, at].astype(F32), jnp.zeros((1, size), F32)], 0)
            edge = jnp.concatenate([edge[:, q * LANES : (q + 1) * LANES] for q in range(size // LANES)], 0)
            fill = jnp.zeros((PAIR * count - count // 2 - edge.shape[0], LANES), F32)
            out[count // 2 :, to : to + LANES] = jnp.concatenate([edge, fill], 0).astype(BF16)
    for copy in started:
        copy.wait()


def view(refs, piece):
    return [(ref, total_of(2) if piece == 3 and r == NEAR else 0) for r, ref in enumerate(refs)]


def convolve_in_order(place, blocks, columns, edge, tap, bias, wide, put):
    width = columns.stop - columns.start
    count = blocks[0][0].shape[0] // PAIR
    wide[5:8, :width] = edge
    for r, (block, origin) in enumerate(blocks):
        for core in range(PAIR):
            at = pl.multiple_of((core * len(blocks) + (place[4] ^ FLIP[r])) * count + 8, 8)
            part = block[core * count : (core + 1) * count, origin + columns.start : origin + columns.stop]
            wide[pl.ds(at, count), :width] = part.astype(F32)
    tap, bias = tap * 0.5, bias * 0.5
    for start in range(0, PAIR * len(blocks) * count, count):
        acc = bias + tap[0:1] * wide[start + 5 : start + 5 + count, :width]
        acc = acc + tap[1:2] * wide[start + 6 : start + 6 + count, :width]
        acc = acc + tap[2:3] * wide[start + 7 : start + 7 + count, :width]
        acc = acc + tap[3:4] * wide[start + 8 : start + 8 + count, :width]
        put(start, count, (acc + acc * jnp.tanh(acc)).astype(BF16))


def prep_kernel(shards, place, *refs):
    blocks, (taps, offset, a_ref, bias_ref, skip_ref, order) = refs[:shards], refs[shards : shards + 6]
    b_ref, edge_ref, cum_ref, row_ref, factor_ref, tail_ref, skip_out, dt_ref, wide = refs[shards + 6 :]
    blocks = view(blocks, 1)
    start = WIDTHS[1]
    last = total_of(1) - LANES
    size = edge_ref.shape[1]
    count = blocks[0][0].shape[0] // PAIR
    half, heads = count // 2, HEADS // GROUPS
    columns = [block[:, origin + last : origin + last + LANES].astype(F32) for block, origin in blocks]
    edge = columns[0][half : half + 4 * size // LANES]
    for column in columns[1:]:
        edge = edge + column[half : half + 4 * size // LANES]
    for q in range(size // LANES):
        edge_ref[:, q * LANES : (q + 1) * LANES] = edge[4 * q : 4 * q + 4]
    for r, column in enumerate(columns):
        packed = column[:half]
        for j in range(2 * PAIR):
            at = ((j // 2) * shards + (place[4] ^ FLIP[r])) * count + (j % 2) * half
            rows = packed if j == 0 else pltpu.roll(packed, LANES - j * heads, 1)
            dt_ref[pl.ds(pl.multiple_of(at, half), half), :] = rows

    def put(start, count, value):
        b_ref[start : start + count] = value

    at = slice(PER_GROUP, PER_GROUP + STATE)
    convolve_in_order(
        place, blocks, slice(start, start + STATE), edge_ref[0:3, at], taps[:, at], offset[:, at], wide, put
    )
    per_tile = LANES * GROUPS // HEADS
    group = place[0]
    tile = group // per_tile
    shift = (LANES - (group % per_tile) * heads) % LANES

    def lanes_of(ref):
        return pltpu.roll(jnp.broadcast_to(ref[pl.ds(tile, 1), :], (8, LANES)), shift, 1)

    rate = -jnp.exp(lanes_of(a_ref)[0:1])
    raw = dt_ref[...] + lanes_of(bias_ref)[0:1]
    step = jnp.maximum(raw, 0.0) + jnp.log1p(jnp.exp(-jnp.abs(raw)))
    skip = lanes_of(skip_ref)
    skip_out[...] = jnp.concatenate(halves(jnp.concatenate([skip, skip], 0), 3), 1)
    lower = (
        lax.broadcasted_iota(jnp.int32, (BLOCK, BLOCK), 0)
        >= lax.broadcasted_iota(jnp.int32, (BLOCK, BLOCK), 1)
    ).astype(BF16)
    valid = lax.broadcasted_iota(jnp.int32, (BLOCK, LANES), 1) < heads
    for block in range(PAIR):
        at = slice(block * BLOCK, (block + 1) * BLOCK)
        here = jnp.where(valid, step[at], 1.0)
        parts = halves(here * rate, 3)
        cum = dot(lower, parts[0]) + (dot(lower, parts[1]) + dot(lower, parts[2]))
        cum = cum * LOG2E
        cum_ref[at] = cum
        row_ref[:, at] = jnp.transpose(cum - jnp.log2(here))
        factor_ref[at] = jnp.concatenate(halves(jnp.exp2(cum), 2), 1)
        tail = jnp.exp2(cum[BLOCK - 1 :] - cum) * here
        tail_ref[at] = jnp.concatenate(halves(tail, 2), 1)


def score_kernel(shards, place, *refs):
    blocks, refs = refs[:shards], refs[shards:]
    taps, offset, edge_ref, b_ref, c_ref, score_ref, wide = (*refs[:4], *refs[-3:])
    blocks = view(blocks, 3)
    start = WIDTHS[3]
    at = slice(PER_GROUP + STATE, PER_GROUP + 2 * STATE)

    def put(start, count, value):
        c_ref[start : start + count] = value

    convolve_in_order(
        place, blocks, slice(start, start + STATE), edge_ref[0:3, at], taps[:, at], offset[:, at], wide, put
    )
    for block in range(PAIR):
        at = slice(block * BLOCK, (block + 1) * BLOCK)
        score_ref[at] = lax.dot_general(
            c_ref[at], b_ref[at], (((1,), (1,)), ((), ())), preferred_element_type=F32
        )


def decay_of(ref):
    decay = ref[STATE : STATE + 16].astype(F32)
    return decay[0:1] + (decay[1:2] + decay[2:3])


def put_decay(ref, decay):
    row = lax.broadcasted_iota(jnp.int32, (16, ref.shape[1]), 0)
    high, middle, low = (part.astype(F32) for part in halves(decay, 3))
    packed = jnp.where(row == 0, high, jnp.where(row == 1, middle, jnp.where(row == 2, low, 0.0)))
    ref[STATE:] = packed.astype(BF16)


def state_kernel(shards, part, sizes, place, *refs):
    blocks, refs = refs[:shards], refs[shards:]
    taps, offset, edge_ref, b_ref, factor_ref, tail_ref = refs[:6]
    x_ref, own_ref, *sends, wide = refs[-3 - len(sizes) :]
    piece, start, width = part
    first = sum(WIDTHS[:piece]) + start
    at = slice(first, first + width)

    def put(row, count, value):
        x_ref[row : row + count] = value

    blocks = view(blocks, piece)
    columns = slice(start, start + width)
    convolve_in_order(place, blocks, columns, edge_ref[0:3, at], taps[:, at], offset[:, at], wide, put)
    expand = spread(first // HEAD_DIM, width, 2)
    both = []
    for block in range(PAIR):
        at = slice(block * BLOCK, (block + 1) * BLOCK)
        loaded = (x_ref[at].astype(F32) * dot(tail_ref[at], expand)).astype(BF16)
        both.append(
            lax.dot_general(b_ref[at], loaded, (((0,), (0,)), ((), ())), preferred_element_type=F32)
        )
    ends = [dot(factor_ref[(i + 1) * BLOCK - 16 : (i + 1) * BLOCK], expand)[15:16] for i in range(PAIR)]
    own_ref[...] = both[0]
    end = (ends[1] * both[0] + both[1]).astype(BF16)
    decay = ends[0] * ends[1]
    start = 0
    for send_ref in sends:
        at = slice(start, start + send_ref.shape[1])
        send_ref[0:STATE] = end[:, at]
        put_decay(send_ref, decay[:, at])
        start = at.stop


def combine_kernel(spans, place, *refs):
    count = len(spans)
    got, own, out_ref = refs[:count], refs[count : 2 * count], refs[-1]
    odd = place[1] % 2 == 1
    start = 0
    for got_ref, own_ref, span in zip(got, own, spans):
        at = slice(start, start + span.stop - span.start)
        theirs, mine = got_ref[:STATE, span].astype(F32), own_ref[:STATE, span].astype(F32)
        decay, other = decay_of(own_ref.at[:, span]), decay_of(got_ref.at[:, span])
        total = jnp.where(odd, decay, 1.0) * theirs + jnp.where(odd, 1.0, other) * mine
        out_ref[:STATE, at] = total.astype(BF16)
        put_decay(out_ref.at[:, at], decay * other)
        start = at.stop


def mix(first_head, x_ref, cum_ref, row_ref, score_ref, skip_ref, put):
    width = x_ref.shape[1]
    half = BLOCK // 2
    expand = spread(first_head, width, 3)
    skip = dot(skip_ref[...], expand)[0:1]
    lower = lax.broadcasted_iota(jnp.int32, (half, half), 0) >= lax.broadcasted_iota(
        jnp.int32, (half, half), 1
    )
    lane = lax.broadcasted_iota(jnp.int32, (BLOCK, LANES), 1)
    for block in range(PAIR):
        base = block * BLOCK
        for tile in range(width // LANES):
            columns = slice(tile * LANES, (tile + 1) * LANES)
            x = x_ref[base : base + BLOCK, columns]
            top = skip[:, columns] * x[:half].astype(F32)
            bottom = skip[:, columns] * x[half:].astype(F32)
            for side in range(LANES // HEAD_DIM):
                head = first_head + tile * (LANES // HEAD_DIM) + side
                own = jnp.where(lane // HEAD_DIM == side, x, jnp.zeros_like(x))
                cum = cum_ref[base : base + BLOCK, head : head + 1]
                row = row_ref[head : head + 1, base : base + BLOCK]
                diag = jnp.where(lower, cum[:half] - row[:, :half], -1e30)
                mixing = jnp.exp2(diag) * score_ref[base : base + half, :half]
                top = top + dot(mixing.astype(BF16), own[:half])
                left = jnp.exp2(cum[half:] - row[:, :half]) * score_ref[base + half : base + BLOCK, :half]
                diag = jnp.where(lower, cum[half:] - row[:, half:], -1e30)
                right = jnp.exp2(diag) * score_ref[base + half : base + BLOCK, half:]
                mixing = jnp.concatenate([left.astype(BF16), right.astype(BF16)], 1)
                bottom = bottom + dot(mixing, own)
            put(block, slice(base, base + half), columns, top)
            put(block, slice(base + half, base + BLOCK), columns, bottom)


def local_kernel(first_head, x_ref, cum_ref, row_ref, score_ref, skip_ref, *refs):
    out_ref = refs[-1]

    def put(block, rows, columns, value):
        out_ref[rows, columns] = value

    mix(first_head, x_ref, cum_ref, row_ref, score_ref, skip_ref, put)


def carry(first_head, place, lasts, befores, own_ref, c_ref, factor_ref, add, keep_ref, send_ref):
    expand = spread(first_head, own_ref.shape[1], 2)
    last, before = (
        refs[0][...] if len(refs) == 1 else jnp.concatenate([ref[...] for ref in refs], 1)
        for refs in (lasts, befores)
    )
    odd, core = place[1] % 2 == 1, place[2]
    near = jnp.where(odd, last[:STATE].astype(F32), 0.0)
    held = near + jnp.where(odd, decay_of(last), 1.0) * before[:STATE].astype(F32)
    factor = dot(factor_ref[...], expand)
    outs = []
    for block in range(PAIR):
        at = slice(block * BLOCK, (block + 1) * BLOCK)
        carried = dot(c_ref[at], held.astype(BF16))
        outs.append((add[at] + factor[at] * carried).astype(BF16))
        held = factor[BLOCK - 1 : BLOCK] * held + own_ref[...]

    @pl.when(core == 0)
    def _():
        keep_ref[...] = outs[0]
        send_ref[...] = outs[1]

    @pl.when(core == 1)
    def _():
        keep_ref[...] = outs[1]
        send_ref[...] = outs[0]


def final_kernel(first_head, counts, place, *refs):
    groups = []
    for number in counts:
        groups.append(refs[:number])
        refs = refs[number:]
    carry(first_head, place, *groups, *refs[:4], *refs[-2:])


def finish_kernel(first_head, counts, place, *refs):
    groups = []
    for number in counts:
        groups.append(refs[:number])
        refs = refs[number:]
    own_ref, c_ref, factor_ref = refs[:3]
    keep_ref, send_ref, partial = refs[-3:]
    local_kernel(first_head, *refs[3:8], partial)
    carry(first_head, place, *groups, own_ref, c_ref, factor_ref, partial, keep_ref, send_ref)


def place_kernel(firsts, place, *refs):
    count = len(firsts)
    keeps, gots = refs[:count], refs[count : 2 * count]
    out, sems = refs[-2:]
    core = place[2]
    half = out.shape[1] // PAIR
    copies = []
    for first, keep, got in zip(firsts, keeps, gots):
        width = keep.shape[1]
        for top in range(0, keep.shape[0], 64):
            rows = slice(top, top + 64)
            copies.append((keep.at[rows], out.at[rows, ds(core * half + first, width)]))
            copies.append((got.at[rows], out.at[rows, ds((1 - core) * half + first, width)]))
    for copy in run(copies, sems):
        copy.wait()


def put_in_place(firsts, shape, place, keeps, gots):
    smem, vmem, hbm = (pl.BlockSpec(memory_space=m) for m in (pltpu.SMEM, pltpu.VMEM, pltpu.HBM))
    count = len(firsts)
    return pl.pallas_call(
        functools.partial(place_kernel, firsts),
        out_shape=jax.ShapeDtypeStruct(shape, BF16),
        in_specs=[smem] + [vmem] * (2 * count),
        out_specs=hbm,
        scratch_shapes=[pltpu.SemaphoreType.DMA((2 * count * (shape[0] // 64),))],
        compiler_params=pltpu.CompilerParams(vmem_limit_bytes=16 << 20),
        cost_estimate=pl.CostEstimate(flops=1, bytes_accessed=1, transcendentals=0),
        name="place",
    )(place, *keeps, *gots)


class Stay:
    def __init__(self, array):
        self.array = array


def gate(blocks, order):
    anywhere = pl.BlockSpec(memory_space=pl.ANY)
    return pl.pallas_call(
        lambda *refs: None,
        out_shape=[jax.ShapeDtypeStruct(block.shape, block.dtype) for block in blocks],
        in_specs=[anywhere] * (len(blocks) + len(order)),
        out_specs=[anywhere] * len(blocks),
        input_output_aliases={i: i for i in range(len(blocks))},
        compiler_params=pltpu.CompilerParams(vmem_limit_bytes=16 << 20),
        cost_estimate=pl.CostEstimate(flops=1, bytes_accessed=1, transcendentals=0),
        name="gate",
    )(*blocks, *order)


def call(body, outs, operands, scratch=(), flops=0, transcendentals=0, name=None, limit=16 << 20):
    shapes = [jax.ShapeDtypeStruct(shape, dtype) for shape, dtype in outs]
    smem, vmem, hbm = (pl.BlockSpec(memory_space=m) for m in (pltpu.SMEM, pltpu.VMEM, pltpu.HBM))
    specs = [
        hbm if isinstance(o, Stay) else smem if o.dtype == jnp.int32 else vmem for o in operands
    ]
    moved = sum(o.size * o.dtype.itemsize for o in shapes) * 2
    return pl.pallas_call(
        body,
        out_shape=shapes,
        in_specs=specs,
        out_specs=[vmem] * len(outs),
        scratch_shapes=scratch,
        compiler_params=pltpu.CompilerParams(vmem_limit_bytes=limit),
        cost_estimate=pl.CostEstimate(flops=1, bytes_accessed=1, transcendentals=0),
        name=name,
    )(*[o.array if isinstance(o, Stay) else o for o in operands])


def paired(xbc, dt_raw, conv_weight, conv_bias, a_log, dt_bias, skip_gain):
    axes = ("ctx", "head")
    shards, length = lax.axis_size("head"), lax.axis_size("ctx")
    devices, peers = shards * length, shards * PAIR
    tok = xbc.shape[0]
    slab = tok * peers
    context, shard = lax.axis_index("ctx"), lax.axis_index("head")
    pair, core = context // PAIR, context % PAIR
    group = shard * PAIR + core
    place = jnp.stack([group, pair, core, core * shards + shard, shard]).astype(jnp.int32)

    def over(block, target):
        route = [(i, target(i)) for i in range(devices)]
        return lax.ppermute(block, axes, [(i, j) for i, j in route if j is not None and j < devices])

    def swap(block):
        return over(block, lambda i: i ^ shards)

    rows = Stay(xbc)
    size = PER_GROUP + 2 * STATE
    (sent,) = call(
        functools.partial(pack_first_kernel, shards),
        [((tok, shards * WIDTHS[0]), BF16)],
        [place, rows],
        scratch=[pltpu.SemaphoreType.DMA((shards,))],
        name="pack_first",
    )
    got_first = swap(sent)
    sent, tail = call(
        functools.partial(pack_kernel, shards),
        [((tok, shards * (size - WIDTHS[0]) + HEADS), BF16), ((16, shards * size), BF16)],
        [place, rows, Stay(dt_raw), Stay(sent)],
        scratch=[pltpu.SemaphoreType.DMA((6 * shards + 1,))],
        name="pack",
    )
    got_rest = swap(gate([sent], [got_first])[0])
    taps, offset = call(
        taps_kernel,
        [((4, size), F32), ((1, size), F32)],
        [place, Stay(conv_weight), Stay(conv_bias[None]), Stay(got_rest)],
        scratch=[pltpu.SemaphoreType.DMA((6,))],
        name="taps",
    )

    def send_on(plan, order, edges=None):
        unused = Stay(got_first)
        parts = [p for _, pieces in plan for p in pieces]
        return call(
            functools.partial(merge_kernel, shards, plan, len(order)),
            [((PAIR * tok, sum(map(total_of, pieces))), BF16) for _, pieces in plan],
            [
                place,
                rows,
                Stay(dt_raw) if edges is None else dt_raw,
                got_first if 0 in parts else unused,
                got_rest if any(parts) else unused,
                unused if edges is None else edges,
            ]
            + [Stay(o) for o in order],
            scratch=[pltpu.SemaphoreType.DMA((sum(2 + 2 * len(RESTS[p]) for p in parts),))],
            name="merge",
        )

    def travel(blocks):
        return [blocks[0]] + [over(blocks[r], lambda i, r=r: i ^ FLIP[r]) for r in range(1, shards)]

    def plan(piece):
        return [(r, (piece,)) for r in range(shards)]

    first_blocks = send_on(plan(0), [])
    message = [travel(first_blocks)]
    (edges,) = call(
        functools.partial(edge_kernel, shards),
        [((3, shards * size), BF16)],
        [place, got_first, got_rest, tail],
        name="edge",
    )
    edges = over(edges, lambda i: i + peers if i % shards == shards - 1 else None)
    second_blocks = send_on(plan(1), [first_blocks[0]], edges)
    message.append(travel(second_blocks))
    third_plan = [(r, (2, 3) if r == NEAR else (2,)) for r in range(shards)]
    third_blocks = send_on(third_plan, [second_blocks[0]])
    message.append(travel(third_blocks[:1] + gate(third_blocks[1:], message[0][1:] + message[1][1:] + [taps])))

    def seen(piece):
        return message[piece]

    tiles = [p.reshape(HEADS // LANES, LANES) for p in (a_log, dt_bias, skip_gain)]
    b, edge, cum, row, factor, tail, skip = call(
        functools.partial(prep_kernel, shards),
        [
            ((slab, STATE), BF16),
            ((4, size), F32),
            ((slab, LANES), F32),
            ((LANES, slab), F32),
            ((slab, 2 * LANES), BF16),
            ((slab, 2 * LANES), BF16),
            ((16, 3 * LANES), BF16),
        ],
        [place] + seen(1) + [taps, offset] + tiles + [Stay(third_blocks[0])],
        scratch=[pltpu.VMEM((slab, LANES), F32), pltpu.VMEM((slab + 8, STATE), F32)],
        name="prep",
    )
    count = len(GROUPED)
    x, sent, own, last, joined, before, keep, send = ([None] * count for _ in range(8))

    def first_head(i):
        return (sum(WIDTHS[: GROUPED[i][0]]) + GROUPED[i][1]) // HEAD_DIM

    def state_of(i, order):
        piece, _, width = GROUPED[i]
        x[i], own[i], *sent[i] = call(
            functools.partial(state_kernel, shards, GROUPED[i], FIRST_ROUND[i]),
            [((slab, width), BF16), ((STATE, width), F32)] + [((STATE + 16, w), BF16) for w in FIRST_ROUND[i]],
            [place] + seen(piece) + [taps, offset, edge, b, factor, tail] + [Stay(o) for o in order],
            scratch=[pltpu.VMEM((slab + 8, width), F32)],
            name="state",
        )
        last[i] = [over(part, lambda i: i ^ peers if i // peers != 3 else None) for part in sent[i]]

    def combine_of(i, order):
        joined[i], before[i] = [], []
        end = 0
        for width in SECOND_ROUND[i]:
            begin, end = end, end + width
            early, late, spans, first = [], [], [], 0
            for got, mine, size_of in zip(last[i], sent[i], FIRST_ROUND[i]):
                low, high = max(begin - first, 0), min(end - first, size_of)
                first += size_of
                if low < high:
                    early.append(got)
                    late.append(mine)
                    spans.append(slice(low, high))
            (total,) = call(
                functools.partial(combine_kernel, spans),
                [((STATE + 16, width), BF16)],
                [place] + early + late + [Stay(o) for o in order],
                name="combine",
            )
            joined[i].append(total)
            before[i].append(over(total, lambda i: i + 2 * peers))
            order = [total]

    def finish_of(body, i, operands, order, **more):
        keep[i], send[i] = call(
            functools.partial(body, first_head(i), (len(last[i]), len(before[i]))),
            [((BLOCK, GROUPED[i][2]), BF16)] * 2,
            [place, *last[i], *before[i], own[i], c, factor] + operands + [Stay(o) for o in order],
            name="final",
            **more,
        )

    partial = [None] * count

    def local_of(i, order):
        (partial[i],) = call(
            functools.partial(local_kernel, first_head(i)),
            [(x[i].shape, F32)],
            [x[i], cum, row, score, skip] + [Stay(o) for o in order],
            name="local",
        )

    state_of(0, [])
    own_block, *fourth_blocks = send_on([(r, (3,)) for r in range(shards) if r != NEAR], sent[0])
    fourth_blocks = gate(fourth_blocks, message[2][1:])
    fourth_blocks = [over(block, lambda i, r=r: i ^ FLIP[r]) for r, block in enumerate(fourth_blocks, 1)]
    message.append([own_block, *fourth_blocks, message[2][NEAR]])
    combine_of(0, [own_block])
    state_of(1, joined[0])
    combine_of(1, [])
    state_of(2, joined[1])
    c, score = call(
        functools.partial(score_kernel, shards),
        [((slab, STATE), BF16), ((slab, BLOCK), F32)],
        [place] + seen(3) + [taps, offset, edge, b] + [Stay(o) for o in sent[2]],
        scratch=[pltpu.VMEM((slab + 8, STATE), F32)],
        name="score",
    )
    local_of(0, [])
    local_of(1, [partial[0]])
    state_of(3, [partial[1]])

    combine_of(2, sent[3] + before[1] + before[0])
    finish_of(final_kernel, 1, [partial[1]], joined[2])
    combine_of(3, [keep[1]])
    local_of(2, joined[3])
    local_of(3, [partial[2]])
    finish_of(final_kernel, 0, [partial[0]], [partial[3]])
    finish_of(final_kernel, 2, [partial[2]], [keep[0]])
    finish_of(final_kernel, 3, [partial[3]], [keep[2]])
    firsts = [first_head(i) * HEAD_DIM for i in range(count)]
    return put_in_place(firsts, (BLOCK, PAIR * PER_GROUP), place, keep, [swap(o) for o in send])


def solution(mesh):
    in_specs = (P(("ctx", "head"), None), P(("ctx", "head"), None), P(), P(), P(), P(), P())
    out_specs = P("ctx", "head")
    shards, length = mesh.shape["head"], mesh.shape["ctx"]

    def program(xbc, *rest):
        slab = xbc.shape[0] // length
        fits = shards == GROUPS // PAIR and length == 4 * PAIR and slab == BLOCK
        return jax.shard_map(
            paired if fits else on_device,
            mesh=mesh,
            in_specs=in_specs,
            out_specs=out_specs,
            check_vma=False,
        )(xbc, *rest)

    return program
```

```python
import functools

import jax
import jax.numpy as jnp
from jax import lax
from jax.experimental import pallas as pl
from jax.experimental.pallas import tpu as pltpu
from jax.sharding import PartitionSpec as P

HEADS = 256
HEAD_DIM = 64
STATE = 256
GROUPS = 8
BLOCK = 256


def from_behind(block, axis, distance):
    devices = range(lax.axis_size(axis))
    route = [(i - distance, i) for i in devices if i - distance in devices]
    return lax.ppermute(block, axis, route)


def carried_in(array, axis, combine, identity):
    length, index = (lax.axis_size(axis), lax.axis_index(axis))
    everything = jax.tree.map(lambda part: lax.all_gather(part, axis), array)
    start = jax.tree.map(
        lambda part, zero: jnp.broadcast_to(jnp.asarray(zero, part.dtype), part.shape),
        array,
        identity,
    )

    def hop(k, before):
        reached = k < index
        new = combine(before, jax.tree.map(lambda part: part[k], everything))
        return jax.tree.map(lambda a, b: jnp.where(reached, a, b), new, before)

    return lax.fori_loop(0, length, hop, start)


def convolve(rows, edge, weight, bias):
    count = rows.shape[0]
    wide = jnp.concatenate([edge, rows], 0).astype(jnp.float32)
    acc = bias[None, :] + weight[0] * wide[0:count]
    acc = acc + weight[1] * wide[1 : count + 1]
    acc = acc + weight[2] * wide[2 : count + 2]
    acc = acc + weight[3] * wide[3 : count + 3]
    return jax.nn.silu(acc).astype(jnp.bfloat16)


def rearrange_heads(rows, shards, per_dev, groups_dev, per_group):
    count = rows.shape[0]
    inner = HEADS * HEAD_DIM
    replicate_groups = max(1, per_group // per_dev)
    heads_part = rows[:, :inner].reshape(count, shards, per_dev * HEAD_DIM)
    b_part = rows[:, inner : inner + GROUPS * STATE].reshape(count, GROUPS, STATE)
    c_part = rows[:, inner + GROUPS * STATE :].reshape(count, GROUPS, STATE)
    b_part = jnp.repeat(b_part, replicate_groups, axis=1).reshape(count, shards, groups_dev * STATE)
    c_part = jnp.repeat(c_part, replicate_groups, axis=1).reshape(count, shards, groups_dev * STATE)
    return jnp.concatenate([heads_part, b_part, c_part], axis=2)


def inner_block(xs, bmat, cmat, steps, cum):
    size = xs.shape[0]
    lower = jnp.arange(size)[:, None] >= jnp.arange(size)[None, :]
    scores = jnp.einsum("qgn,kgn->gqk", cmat, bmat, preferred_element_type=jnp.float32)
    order = jnp.transpose(cum, (1, 2, 0))
    gap = order[..., :, None] - order[..., None, :]
    decay = jnp.exp(jnp.where(lower, gap, -jnp.inf))
    mixing = (scores[:, None] * decay * jnp.transpose(steps, (1, 2, 0))[..., None, :]).astype(
        jnp.bfloat16
    )
    local = jnp.einsum("gjqk,kgjp->qgjp", mixing, xs, preferred_element_type=jnp.float32)
    tail = jnp.exp(cum[size - 1][None] - cum) * steps
    loaded = (bmat[:, :, None, :].astype(jnp.float32) * tail[..., None]).astype(jnp.bfloat16)
    block_state = jnp.einsum("kgjn,kgjp->gjnp", loaded, xs, preferred_element_type=jnp.float32)
    return (local, block_state)


def on_device(xbc, dt_raw, conv_weight, conv_bias, a_log, dt_bias, skip_gain):
    tok = xbc.shape[0]
    shards = lax.axis_size("head")
    per_dev = HEADS // shards
    per_group = HEADS // GROUPS
    groups_dev = max(1, per_dev // per_group)
    heads_per_cluster = per_dev // groups_dev
    sent = rearrange_heads(xbc, shards, per_dev, groups_dev, per_group)
    mine, rates = (
        lax.all_to_all(sent, "head", split_axis=1, concat_axis=0, tiled=True),
        lax.all_to_all(
            dt_raw.reshape(tok, shards, per_dev), "head", split_axis=1, concat_axis=0, tiled=True
        ),
    )
    slab = tok * shards
    mine = mine.reshape(slab, mine.shape[2])
    rates = rates.reshape(slab, per_dev)
    shard = lax.axis_index("head")
    taps = lax.dynamic_index_in_dim(
        rearrange_heads(conv_weight, shards, per_dev, groups_dev, per_group),
        shard,
        1,
        keepdims=False,
    )
    offset = lax.dynamic_index_in_dim(
        rearrange_heads(conv_bias[None, :], shards, per_dev, groups_dev, per_group),
        shard,
        1,
        keepdims=False,
    )
    edge = from_behind(mine[slab - 3 :], "ctx", 1)
    mine = convolve(mine, edge, taps, offset[0])
    nchunk = slab // BLOCK
    width = per_dev * HEAD_DIM
    xs = mine[:, :width].reshape(nchunk, BLOCK, groups_dev, heads_per_cluster, HEAD_DIM)
    bmat = mine[:, width : width + groups_dev * STATE].reshape(nchunk, BLOCK, groups_dev, STATE)
    cmat = mine[:, width + groups_dev * STATE :].reshape(nchunk, BLOCK, groups_dev, STATE)
    first = shard * per_dev
    rate = (-jnp.exp(lax.dynamic_slice_in_dim(a_log, first, per_dev))).reshape(
        groups_dev, heads_per_cluster
    )
    bias_dt = lax.dynamic_slice_in_dim(dt_bias, first, per_dev).reshape(
        groups_dev, heads_per_cluster
    )
    skip = lax.dynamic_slice_in_dim(skip_gain, first, per_dev).reshape(
        groups_dev, heads_per_cluster
    )
    steps = jax.nn.softplus(
        rates.astype(jnp.float32).reshape(nchunk, BLOCK, groups_dev, heads_per_cluster) + bias_dt
    )
    cum = jnp.cumsum(steps * rate, axis=1)

    def block_step(carry, item):
        held, product = carry
        x_part, b_part, c_part, step_part, cum_part = item
        local, block_state = inner_block(x_part, b_part, c_part, step_part, cum_part)
        lifted = c_part.astype(jnp.float32)[:, :, None, :] * jnp.exp(cum_part)[..., None]
        carried = jnp.einsum("qgjn,gjnp->qgjp", lifted, held, precision=lax.Precision.HIGHEST)
        partial_out = local + carried + skip[..., None] * x_part.astype(jnp.float32)
        end = jnp.exp(cum_part[BLOCK - 1])
        return ((end[..., None, None] * held + block_state, product * end), (partial_out, product))

    zero_state = jnp.zeros((groups_dev, heads_per_cluster, STATE, HEAD_DIM), jnp.float32)
    unit = jnp.ones((groups_dev, heads_per_cluster), jnp.float32)
    (slab_state, slab_decay), (partials, product_in) = lax.scan(
        block_step, (zero_state, unit), (xs, bmat, cmat, steps, cum)
    )

    def combine(preceding_state, later):
        return (
            preceding_state[0] * later[0],
            later[0][..., None, None] * preceding_state[1] + later[1],
        )

    _, entering = carried_in((slab_decay, slab_state), "ctx", combine, (unit, zero_state))
    projected = jnp.einsum(
        "cqgn,gjnp->cqgjp", cmat.astype(jnp.float32), entering, precision=lax.Precision.HIGHEST
    )
    factor = jnp.exp(cum) * product_in[:, None]
    total = partials + factor[..., None] * projected
    return total.astype(jnp.bfloat16).reshape(slab, width)


PAIR = 2
LANES = 128
LOG2E = 1.4426950408889634
F32, BF16 = jnp.float32, jnp.bfloat16
WIDTHS = (512, 0, 768, 768)
RESTS = ("", "BD", "", "C")
GROUPED = ((0, 0, 512), (2, 0, 768), (3, 0, 384), (3, 384, 384))
FIRST_ROUND = ((256, 256), (384, 384), (384,), (384,))
SECOND_ROUND = ((512,), (384, 384), (384,), (384,))


FLIP = (0, 2, 3, 1)
NEAR = 3


def halves(value, count):
    parts = []
    for _ in range(count):
        part = value.astype(BF16)
        parts.append(part)
        value = value - part.astype(F32)
    return parts


def spread(first_head, width, copies):
    lane = lax.broadcasted_iota(jnp.int32, (copies * LANES, width), 0) % LANES
    column = lax.broadcasted_iota(jnp.int32, (copies * LANES, width), 1)
    return (lane == first_head + column // HEAD_DIM).astype(BF16)


def dot(a, b):
    return jnp.dot(a, b, preferred_element_type=F32)


def ds(start, width):
    return pl.ds(pl.multiple_of(start, LANES), width)


def run(copies, sems):
    started = []
    for i, (source, target) in enumerate(copies):
        copy = pltpu.make_async_copy(source, target, sems.at[i])
        copy.start()
        started.append(copy)
    return started


PER_GROUP = HEADS * HEAD_DIM // GROUPS
INNER = HEADS * HEAD_DIM


def channels(group, first, width):
    return ds(group * PER_GROUP + first, width)


def pack_first_kernel(shards, place, xbc, send, sems):
    core, shard = place[2], place[4]
    width = WIDTHS[0]
    copies = []
    for r in range(shards):
        group = (shard ^ FLIP[r]) * PAIR + 1 - core
        copies.append((xbc.at[:, channels(group, 0, width)], send.at[:, r * width : (r + 1) * width]))
    for copy in run(copies, sems):
        copy.wait()


def pack_kernel(shards, place, xbc, dt_raw, order, send, tail, sems):
    core, shard = place[2], place[4]
    count = xbc.shape[0]
    first = WIDTHS[0]
    width = PER_GROUP - first
    rest = width * shards
    size = PER_GROUP + 2 * STATE
    copies = []
    for r in range(shards):
        group = (shard ^ FLIP[r]) * PAIR + 1 - core
        copies.append((xbc.at[:, channels(group, first, width)], send.at[:, r * width : (r + 1) * width]))
        for i in range(2):
            to = rest + (i * shards + r) * STATE
            copies.append((xbc.at[:, ds(INNER + (i * GROUPS + group) * STATE, STATE)], send.at[:, to : to + STATE]))
    copies.append((dt_raw, send.at[:, send.shape[1] - HEADS :]))
    for r in range(shards):
        group, to = (shard ^ FLIP[r]) * PAIR + core, r * size
        last = xbc.at[count - 16 :]
        copies.append((last.at[:, channels(group, 0, PER_GROUP)], tail.at[:, to : to + PER_GROUP]))
        for i in range(2):
            at = ds(INNER + (i * GROUPS + group) * STATE, STATE)
            start = to + PER_GROUP + i * STATE
            copies.append((last.at[:, at], tail.at[:, start : start + STATE]))
    for copy in run(copies, sems):
        copy.wait()


def taps_kernel(place, weight, bias, order, taps, offset, sems):
    copies = []
    for source, target in ((weight, taps), (bias, offset)):
        copies.append((source.at[:, channels(place[0], 0, PER_GROUP)], target.at[:, :PER_GROUP]))
        for i in range(2):
            at = ds(INNER + (i * GROUPS + place[0]) * STATE, STATE)
            start = PER_GROUP + i * STATE
            copies.append((source.at[:, at], target.at[:, start : start + STATE]))
    for copy in run(copies, sems):
        copy.wait()


def edge_kernel(shards, place, got_first, got, tail, out):
    count = got.shape[0]
    first = WIDTHS[0]
    width = PER_GROUP - first
    size = PER_GROUP + 2 * STATE
    for r in range(shards):
        theirs = [(got_first, r * first, first), (got, r * width, width)]
        theirs += [(got, width * shards + (i * shards + r) * STATE, STATE) for i in range(2)]
        to = r * size
        for ref, start, size_of in theirs:
            a = ref[count - 16 :, start : start + size_of].astype(F32)
            b = tail[:, to : to + size_of].astype(F32)
            out[:, to : to + size_of] = jnp.where(place[2] == 0, a, b)[13:16].astype(BF16)
            to += size_of


def total_of(piece):
    return WIDTHS[piece] + sum(LANES if kind == "D" else STATE for kind in RESTS[piece])


def merge_kernel(shards, plan, unread, place, xbc, dt_raw, got_first, got, edges, *refs):
    refs = refs[unread:]
    outs, sems = refs[: len(plan)], refs[-1]
    core, shard = place[2], place[4]
    count = xbc.shape[0]
    stride = PER_GROUP - WIDTHS[0]
    mine = pl.ds(pl.multiple_of(core * count, count), count)
    other = pl.ds(pl.multiple_of((1 - core) * count, count), count)
    copies, steps = [], []
    for out, (r, pieces) in zip(outs, plan):
        group = (shard ^ FLIP[r]) * PAIR + core
        to = 0
        for piece in pieces:
            first, width = sum(WIDTHS[:piece]), WIDTHS[piece]
            if piece == 0:
                source = got_first.at[:, r * width : (r + 1) * width]
            else:
                at = r * stride + first - WIDTHS[0]
                source = got.at[:, at : at + width]
            if width:
                copies.append((xbc.at[:, channels(group, first, width)], out.at[mine, to : to + width]))
                copies.append((source, out.at[other, to : to + width]))
            to += width
            for kind in RESTS[piece]:
                if kind == "D":
                    steps.append((out, r, to))
                    to += LANES
                    continue
                i = "BC".index(kind)
                at = ds(INNER + (i * GROUPS + group) * STATE, STATE)
                copies.append((xbc.at[:, at], out.at[mine, to : to + STATE]))
                at = stride * shards + (i * shards + r) * STATE
                copies.append((got.at[:, at : at + STATE], out.at[other, to : to + STATE]))
                to += STATE
    started = run(copies, sems)
    if steps:
        lane = lax.broadcasted_iota(jnp.int32, (count, LANES), 1)
        per_tile = LANES * GROUPS // HEADS
        heads = HEADS // GROUPS
        for out, r, to in steps:
            group = (shard ^ FLIP[r]) * PAIR + core
            tile, shift = group // per_tile, (LANES - (group % per_tile) * heads) % LANES
            own = dt_raw[:, ds(tile * LANES, LANES)].astype(F32)
            theirs = got[:, ds(got.shape[1] - HEADS + tile * LANES, LANES)].astype(F32)
            low = jnp.where(core == 0, own, theirs)
            high = jnp.where(core == 0, theirs, own)
            packed = jnp.zeros((count // 2, LANES), F32)
            for j, rows in enumerate((low, high)):
                rows = jnp.where(lane < heads, pltpu.roll(rows, shift, 1), 0.0)
                for i in range(2):
                    part = rows[i * count // 2 : (i + 1) * count // 2]
                    packed = packed + pltpu.roll(part, (2 * j + i) * heads, 1)
            out[: count // 2, to : to + LANES] = packed.astype(BF16)
            size = PER_GROUP + 2 * STATE
            at = slice(r * size, (r + 1) * size)
            edge = jnp.concatenate([edges[:, at].astype(F32), jnp.zeros((1, size), F32)], 0)
            edge = jnp.concatenate([edge[:, q * LANES : (q + 1) * LANES] for q in range(size // LANES)], 0)
            fill = jnp.zeros((PAIR * count - count // 2 - edge.shape[0], LANES), F32)
            out[count // 2 :, to : to + LANES] = jnp.concatenate([edge, fill], 0).astype(BF16)
    for copy in started:
        copy.wait()


def view(refs, piece):
    return [(ref, total_of(2) if piece == 3 and r == NEAR else 0) for r, ref in enumerate(refs)]


def convolve_in_order(place, blocks, columns, edge, tap, bias, wide, put):
    width = columns.stop - columns.start
    count = blocks[0][0].shape[0] // PAIR
    wide[5:8, :width] = edge
    for r, (block, origin) in enumerate(blocks):
        for core in range(PAIR):
            at = pl.multiple_of((core * len(blocks) + (place[4] ^ FLIP[r])) * count + 8, 8)
            part = block[core * count : (core + 1) * count, origin + columns.start : origin + columns.stop]
            wide[pl.ds(at, count), :width] = part.astype(F32)
    tap, bias = tap * 0.5, bias * 0.5
    for start in range(0, PAIR * len(blocks) * count, count):
        acc = bias + tap[0:1] * wide[start + 5 : start + 5 + count, :width]
        acc = acc + tap[1:2] * wide[start + 6 : start + 6 + count, :width]
        acc = acc + tap[2:3] * wide[start + 7 : start + 7 + count, :width]
        acc = acc + tap[3:4] * wide[start + 8 : start + 8 + count, :width]
        put(start, count, (acc + acc * jnp.tanh(acc)).astype(BF16))


def prep_kernel(shards, place, *refs):
    blocks, (taps, offset, a_ref, bias_ref, skip_ref, order) = refs[:shards], refs[shards : shards + 6]
    b_ref, edge_ref, cum_ref, row_ref, factor_ref, tail_ref, skip_out, dt_ref, wide = refs[shards + 6 :]
    blocks = view(blocks, 1)
    start = WIDTHS[1]
    last = total_of(1) - LANES
    size = edge_ref.shape[1]
    count = blocks[0][0].shape[0] // PAIR
    half, heads = count // 2, HEADS // GROUPS
    columns = [block[:, origin + last : origin + last + LANES].astype(F32) for block, origin in blocks]
    edge = columns[0][half : half + 4 * size // LANES]
    for column in columns[1:]:
        edge = edge + column[half : half + 4 * size // LANES]
    for q in range(size // LANES):
        edge_ref[:, q * LANES : (q + 1) * LANES] = edge[4 * q : 4 * q + 4]
    for r, column in enumerate(columns):
        packed = column[:half]
        for j in range(2 * PAIR):
            at = ((j // 2) * shards + (place[4] ^ FLIP[r])) * count + (j % 2) * half
            rows = packed if j == 0 else pltpu.roll(packed, LANES - j * heads, 1)
            dt_ref[pl.ds(pl.multiple_of(at, half), half), :] = rows

    def put(start, count, value):
        b_ref[start : start + count] = value

    at = slice(PER_GROUP, PER_GROUP + STATE)
    convolve_in_order(
        place, blocks, slice(start, start + STATE), edge_ref[0:3, at], taps[:, at], offset[:, at], wide, put
    )
    per_tile = LANES * GROUPS // HEADS
    group = place[0]
    tile = group // per_tile
    shift = (LANES - (group % per_tile) * heads) % LANES

    def lanes_of(ref):
        return pltpu.roll(jnp.broadcast_to(ref[pl.ds(tile, 1), :], (8, LANES)), shift, 1)

    rate = -jnp.exp(lanes_of(a_ref)[0:1])
    raw = dt_ref[...] + lanes_of(bias_ref)[0:1]
    step = jnp.maximum(raw, 0.0) + jnp.log1p(jnp.exp(-jnp.abs(raw)))
    skip = lanes_of(skip_ref)
    skip_out[...] = jnp.concatenate(halves(jnp.concatenate([skip, skip], 0), 3), 1)
    lower = (
        lax.broadcasted_iota(jnp.int32, (BLOCK, BLOCK), 0)
        >= lax.broadcasted_iota(jnp.int32, (BLOCK, BLOCK), 1)
    ).astype(BF16)
    valid = lax.broadcasted_iota(jnp.int32, (BLOCK, LANES), 1) < heads
    for block in range(PAIR):
        at = slice(block * BLOCK, (block + 1) * BLOCK)
        here = jnp.where(valid, step[at], 1.0)
        parts = halves(here * rate, 3)
        cum = dot(lower, parts[0]) + (dot(lower, parts[1]) + dot(lower, parts[2]))
        cum = cum * LOG2E
        cum_ref[at] = cum
        row_ref[:, at] = jnp.transpose(cum - jnp.log2(here))
        factor_ref[at] = jnp.concatenate(halves(jnp.exp2(cum), 2), 1)
        tail = jnp.exp2(cum[BLOCK - 1 :] - cum) * here
        tail_ref[at] = jnp.concatenate(halves(tail, 2), 1)


def score_kernel(shards, place, *refs):
    blocks, refs = refs[:shards], refs[shards:]
    taps, offset, edge_ref, b_ref, c_ref, score_ref, wide = (*refs[:4], *refs[-3:])
    blocks = view(blocks, 3)
    start = WIDTHS[3]
    at = slice(PER_GROUP + STATE, PER_GROUP + 2 * STATE)

    def put(start, count, value):
        c_ref[start : start + count] = value

    convolve_in_order(
        place, blocks, slice(start, start + STATE), edge_ref[0:3, at], taps[:, at], offset[:, at], wide, put
    )
    for block in range(PAIR):
        at = slice(block * BLOCK, (block + 1) * BLOCK)
        score_ref[at] = lax.dot_general(
            c_ref[at], b_ref[at], (((1,), (1,)), ((), ())), preferred_element_type=F32
        )


def decay_of(ref):
    decay = ref[STATE : STATE + 16].astype(F32)
    return decay[0:1] + (decay[1:2] + decay[2:3])


def put_decay(ref, decay):
    row = lax.broadcasted_iota(jnp.int32, (16, ref.shape[1]), 0)
    high, middle, low = (part.astype(F32) for part in halves(decay, 3))
    packed = jnp.where(row == 0, high, jnp.where(row == 1, middle, jnp.where(row == 2, low, 0.0)))
    ref[STATE:] = packed.astype(BF16)


def state_kernel(shards, part, sizes, place, *refs):
    blocks, refs = refs[:shards], refs[shards:]
    taps, offset, edge_ref, b_ref, factor_ref, tail_ref = refs[:6]
    x_ref, own_ref, *sends, wide = refs[-3 - len(sizes) :]
    piece, start, width = part
    first = sum(WIDTHS[:piece]) + start
    at = slice(first, first + width)

    def put(row, count, value):
        x_ref[row : row + count] = value

    blocks = view(blocks, piece)
    columns = slice(start, start + width)
    convolve_in_order(place, blocks, columns, edge_ref[0:3, at], taps[:, at], offset[:, at], wide, put)
    expand = spread(first // HEAD_DIM, width, 2)
    both = []
    for block in range(PAIR):
        at = slice(block * BLOCK, (block + 1) * BLOCK)
        loaded = (x_ref[at].astype(F32) * dot(tail_ref[at], expand)).astype(BF16)
        both.append(
            lax.dot_general(b_ref[at], loaded, (((0,), (0,)), ((), ())), preferred_element_type=F32)
        )
    ends = [dot(factor_ref[(i + 1) * BLOCK - 16 : (i + 1) * BLOCK], expand)[15:16] for i in range(PAIR)]
    own_ref[...] = both[0]
    end = (ends[1] * both[0] + both[1]).astype(BF16)
    decay = ends[0] * ends[1]
    start = 0
    for send_ref in sends:
        at = slice(start, start + send_ref.shape[1])
        send_ref[0:STATE] = end[:, at]
        put_decay(send_ref, decay[:, at])
        start = at.stop


def combine_kernel(spans, place, *refs):
    count = len(spans)
    got, own, out_ref = refs[:count], refs[count : 2 * count], refs[-1]
    odd = place[1] % 2 == 1
    start = 0
    for got_ref, own_ref, span in zip(got, own, spans):
        at = slice(start, start + span.stop - span.start)
        theirs, mine = got_ref[:STATE, span].astype(F32), own_ref[:STATE, span].astype(F32)
        decay, other = decay_of(own_ref.at[:, span]), decay_of(got_ref.at[:, span])
        total = jnp.where(odd, decay, 1.0) * theirs + jnp.where(odd, 1.0, other) * mine
        out_ref[:STATE, at] = total.astype(BF16)
        put_decay(out_ref.at[:, at], decay * other)
        start = at.stop


def mix(first_head, x_ref, cum_ref, row_ref, score_ref, skip_ref, put):
    width = x_ref.shape[1]
    half = BLOCK // 2
    expand = spread(first_head, width, 3)
    skip = dot(skip_ref[...], expand)[0:1]
    lower = lax.broadcasted_iota(jnp.int32, (half, half), 0) >= lax.broadcasted_iota(
        jnp.int32, (half, half), 1
    )
    lane = lax.broadcasted_iota(jnp.int32, (BLOCK, LANES), 1)
    for block in range(PAIR):
        base = block * BLOCK
        for tile in range(width // LANES):
            columns = slice(tile * LANES, (tile + 1) * LANES)
            x = x_ref[base : base + BLOCK, columns]
            top = skip[:, columns] * x[:half].astype(F32)
            bottom = skip[:, columns] * x[half:].astype(F32)
            for side in range(LANES // HEAD_DIM):
                head = first_head + tile * (LANES // HEAD_DIM) + side
                own = jnp.where(lane // HEAD_DIM == side, x, jnp.zeros_like(x))
                cum = cum_ref[base : base + BLOCK, head : head + 1]
                row = row_ref[head : head + 1, base : base + BLOCK]
                diag = jnp.where(lower, cum[:half] - row[:, :half], -1e30)
                mixing = jnp.exp2(diag) * score_ref[base : base + half, :half]
                top = top + dot(mixing.astype(BF16), own[:half])
                left = jnp.exp2(cum[half:] - row[:, :half]) * score_ref[base + half : base + BLOCK, :half]
                diag = jnp.where(lower, cum[half:] - row[:, half:], -1e30)
                right = jnp.exp2(diag) * score_ref[base + half : base + BLOCK, half:]
                mixing = jnp.concatenate([left.astype(BF16), right.astype(BF16)], 1)
                bottom = bottom + dot(mixing, own)
            put(block, slice(base, base + half), columns, top)
            put(block, slice(base + half, base + BLOCK), columns, bottom)


def local_kernel(first_head, x_ref, cum_ref, row_ref, score_ref, skip_ref, *refs):
    out_ref = refs[-1]

    def put(block, rows, columns, value):
        out_ref[rows, columns] = value

    mix(first_head, x_ref, cum_ref, row_ref, score_ref, skip_ref, put)


def carry(first_head, place, lasts, befores, own_ref, c_ref, factor_ref, add, keep_ref, send_ref):
    expand = spread(first_head, own_ref.shape[1], 2)
    last, before = (
        refs[0][...] if len(refs) == 1 else jnp.concatenate([ref[...] for ref in refs], 1)
        for refs in (lasts, befores)
    )
    odd, core = place[1] % 2 == 1, place[2]
    near = jnp.where(odd, last[:STATE].astype(F32), 0.0)
    held = near + jnp.where(odd, decay_of(last), 1.0) * before[:STATE].astype(F32)
    factor = dot(factor_ref[...], expand)
    outs = []
    for block in range(PAIR):
        at = slice(block * BLOCK, (block + 1) * BLOCK)
        carried = dot(c_ref[at], held.astype(BF16))
        outs.append((add[at] + factor[at] * carried).astype(BF16))
        held = factor[BLOCK - 1 : BLOCK] * held + own_ref[...]

    @pl.when(core == 0)
    def _():
        keep_ref[...] = outs[0]
        send_ref[...] = outs[1]

    @pl.when(core == 1)
    def _():
        keep_ref[...] = outs[1]
        send_ref[...] = outs[0]


def final_kernel(first_head, counts, place, *refs):
    groups = []
    for number in counts:
        groups.append(refs[:number])
        refs = refs[number:]
    carry(first_head, place, *groups, *refs[:4], *refs[-2:])


def finish_kernel(first_head, counts, place, *refs):
    groups = []
    for number in counts:
        groups.append(refs[:number])
        refs = refs[number:]
    own_ref, c_ref, factor_ref = refs[:3]
    keep_ref, send_ref, partial = refs[-3:]
    local_kernel(first_head, *refs[3:8], partial)
    carry(first_head, place, *groups, own_ref, c_ref, factor_ref, partial, keep_ref, send_ref)


def place_kernel(firsts, place, *refs):
    count = len(firsts)
    keeps, gots = refs[:count], refs[count : 2 * count]
    out, sems = refs[-2:]
    core = place[2]
    half = out.shape[1] // PAIR
    copies = []
    for first, keep, got in zip(firsts, keeps, gots):
        width = keep.shape[1]
        copies.append((keep, out.at[:, ds(core * half + first, width)]))
        copies.append((got, out.at[:, ds((1 - core) * half + first, width)]))
    for copy in run(copies, sems):
        copy.wait()


def put_in_place(firsts, shape, place, keeps, gots):
    smem, vmem, hbm = (pl.BlockSpec(memory_space=m) for m in (pltpu.SMEM, pltpu.VMEM, pltpu.HBM))
    count = len(firsts)
    return pl.pallas_call(
        functools.partial(place_kernel, firsts),
        out_shape=jax.ShapeDtypeStruct(shape, BF16),
        in_specs=[smem] + [vmem] * (2 * count),
        out_specs=hbm,
        scratch_shapes=[pltpu.SemaphoreType.DMA((2 * count,))],
        compiler_params=pltpu.CompilerParams(vmem_limit_bytes=16 << 20),
        cost_estimate=pl.CostEstimate(flops=1, bytes_accessed=1, transcendentals=0),
        name="place",
    )(place, *keeps, *gots)


class Stay:
    def __init__(self, array):
        self.array = array


def gate(blocks, order):
    anywhere = pl.BlockSpec(memory_space=pl.ANY)
    return pl.pallas_call(
        lambda *refs: None,
        out_shape=[jax.ShapeDtypeStruct(block.shape, block.dtype) for block in blocks],
        in_specs=[anywhere] * (len(blocks) + len(order)),
        out_specs=[anywhere] * len(blocks),
        input_output_aliases={i: i for i in range(len(blocks))},
        compiler_params=pltpu.CompilerParams(vmem_limit_bytes=16 << 20),
        cost_estimate=pl.CostEstimate(flops=1, bytes_accessed=1, transcendentals=0),
        name="gate",
    )(*blocks, *order)


def call(body, outs, operands, scratch=(), flops=0, transcendentals=0, name=None, limit=16 << 20):
    shapes = [jax.ShapeDtypeStruct(shape, dtype) for shape, dtype in outs]
    smem, vmem, hbm = (pl.BlockSpec(memory_space=m) for m in (pltpu.SMEM, pltpu.VMEM, pltpu.HBM))
    specs = [
        hbm if isinstance(o, Stay) else smem if o.dtype == jnp.int32 else vmem for o in operands
    ]
    moved = sum(o.size * o.dtype.itemsize for o in shapes) * 2
    return pl.pallas_call(
        body,
        out_shape=shapes,
        in_specs=specs,
        out_specs=[vmem] * len(outs),
        scratch_shapes=scratch,
        compiler_params=pltpu.CompilerParams(vmem_limit_bytes=limit),
        cost_estimate=pl.CostEstimate(flops=1, bytes_accessed=1, transcendentals=0),
        name=name,
    )(*[o.array if isinstance(o, Stay) else o for o in operands])


def paired(xbc, dt_raw, conv_weight, conv_bias, a_log, dt_bias, skip_gain):
    axes = ("ctx", "head")
    shards, length = lax.axis_size("head"), lax.axis_size("ctx")
    devices, peers = shards * length, shards * PAIR
    tok = xbc.shape[0]
    slab = tok * peers
    context, shard = lax.axis_index("ctx"), lax.axis_index("head")
    pair, core = context // PAIR, context % PAIR
    group = shard * PAIR + core
    place = jnp.stack([group, pair, core, core * shards + shard, shard]).astype(jnp.int32)

    def over(block, target):
        route = [(i, target(i)) for i in range(devices)]
        return lax.ppermute(block, axes, [(i, j) for i, j in route if j is not None and j < devices])

    def swap(block):
        return over(block, lambda i: i ^ shards)

    rows = Stay(xbc)
    size = PER_GROUP + 2 * STATE
    (sent,) = call(
        functools.partial(pack_first_kernel, shards),
        [((tok, shards * WIDTHS[0]), BF16)],
        [place, rows],
        scratch=[pltpu.SemaphoreType.DMA((shards,))],
        name="pack_first",
    )
    got_first = swap(sent)
    sent, tail = call(
        functools.partial(pack_kernel, shards),
        [((tok, shards * (size - WIDTHS[0]) + HEADS), BF16), ((16, shards * size), BF16)],
        [place, rows, Stay(dt_raw), Stay(sent)],
        scratch=[pltpu.SemaphoreType.DMA((6 * shards + 1,))],
        name="pack",
    )
    got_rest = swap(gate([sent], [got_first])[0])
    taps, offset = call(
        taps_kernel,
        [((4, size), F32), ((1, size), F32)],
        [place, Stay(conv_weight), Stay(conv_bias[None]), Stay(got_rest)],
        scratch=[pltpu.SemaphoreType.DMA((6,))],
        name="taps",
    )

    def send_on(plan, order, edges=None):
        unused = Stay(got_first)
        parts = [p for _, pieces in plan for p in pieces]
        return call(
            functools.partial(merge_kernel, shards, plan, len(order)),
            [((PAIR * tok, sum(map(total_of, pieces))), BF16) for _, pieces in plan],
            [
                place,
                rows,
                Stay(dt_raw) if edges is None else dt_raw,
                got_first if 0 in parts else unused,
                got_rest if any(parts) else unused,
                unused if edges is None else edges,
            ]
            + [Stay(o) for o in order],
            scratch=[pltpu.SemaphoreType.DMA((sum(2 + 2 * len(RESTS[p]) for p in parts),))],
            name="merge",
        )

    def travel(blocks):
        return [blocks[0]] + [over(blocks[r], lambda i, r=r: i ^ FLIP[r]) for r in range(1, shards)]

    def plan(piece):
        return [(r, (piece,)) for r in range(shards)]

    first_blocks = send_on(plan(0), [])
    message = [travel(first_blocks)]
    (edges,) = call(
        functools.partial(edge_kernel, shards),
        [((3, shards * size), BF16)],
        [place, got_first, got_rest, tail],
        name="edge",
    )
    edges = over(edges, lambda i: i + peers if i % shards == shards - 1 else None)
    second_blocks = send_on(plan(1), [first_blocks[0]], edges)
    message.append(travel(second_blocks))
    third_plan = [(r, (2, 3) if r == NEAR else (2,)) for r in range(shards)]
    third_blocks = send_on(third_plan, [second_blocks[0]])
    message.append(travel(third_blocks[:1] + gate(third_blocks[1:], message[0][1:] + message[1][1:] + [taps])))

    def seen(piece):
        return message[piece]

    tiles = [p.reshape(HEADS // LANES, LANES) for p in (a_log, dt_bias, skip_gain)]
    b, edge, cum, row, factor, tail, skip = call(
        functools.partial(prep_kernel, shards),
        [
            ((slab, STATE), BF16),
            ((4, size), F32),
            ((slab, LANES), F32),
            ((LANES, slab), F32),
            ((slab, 2 * LANES), BF16),
            ((slab, 2 * LANES), BF16),
            ((16, 3 * LANES), BF16),
        ],
        [place] + seen(1) + [taps, offset] + tiles + [Stay(third_blocks[0])],
        scratch=[pltpu.VMEM((slab, LANES), F32), pltpu.VMEM((slab + 8, STATE), F32)],
        name="prep",
    )
    count = len(GROUPED)
    x, sent, own, last, joined, before, keep, send = ([None] * count for _ in range(8))

    def first_head(i):
        return (sum(WIDTHS[: GROUPED[i][0]]) + GROUPED[i][1]) // HEAD_DIM

    def state_of(i, order):
        piece, _, width = GROUPED[i]
        x[i], own[i], *sent[i] = call(
            functools.partial(state_kernel, shards, GROUPED[i], FIRST_ROUND[i]),
            [((slab, width), BF16), ((STATE, width), F32)] + [((STATE + 16, w), BF16) for w in FIRST_ROUND[i]],
            [place] + seen(piece) + [taps, offset, edge, b, factor, tail] + [Stay(o) for o in order],
            scratch=[pltpu.VMEM((slab + 8, width), F32)],
            name="state",
        )
        last[i] = [over(part, lambda i: i ^ peers if i // peers != 3 else None) for part in sent[i]]

    def combine_of(i, order):
        joined[i], before[i] = [], []
        end = 0
        for width in SECOND_ROUND[i]:
            begin, end = end, end + width
            early, late, spans, first = [], [], [], 0
            for got, mine, size_of in zip(last[i], sent[i], FIRST_ROUND[i]):
                low, high = max(begin - first, 0), min(end - first, size_of)
                first += size_of
                if low < high:
                    early.append(got)
                    late.append(mine)
                    spans.append(slice(low, high))
            (total,) = call(
                functools.partial(combine_kernel, spans),
                [((STATE + 16, width), BF16)],
                [place] + early + late + [Stay(o) for o in order],
                name="combine",
            )
            joined[i].append(total)
            before[i].append(over(total, lambda i: i + 2 * peers))
            order = [total]

    def finish_of(body, i, operands, order, **more):
        keep[i], send[i] = call(
            functools.partial(body, first_head(i), (len(last[i]), len(before[i]))),
            [((BLOCK, GROUPED[i][2]), BF16)] * 2,
            [place, *last[i], *before[i], own[i], c, factor] + operands + [Stay(o) for o in order],
            name="final",
            **more,
        )

    partial = [None] * count

    def local_of(i, order):
        (partial[i],) = call(
            functools.partial(local_kernel, first_head(i)),
            [(x[i].shape, F32)],
            [x[i], cum, row, score, skip] + [Stay(o) for o in order],
            name="local",
        )

    state_of(0, [])
    own_block, *fourth_blocks = send_on([(r, (3,)) for r in range(shards) if r != NEAR], sent[0])
    fourth_blocks = gate(fourth_blocks, message[2][1:])
    fourth_blocks = [over(block, lambda i, r=r: i ^ FLIP[r]) for r, block in enumerate(fourth_blocks, 1)]
    message.append([own_block, *fourth_blocks, message[2][NEAR]])
    combine_of(0, [own_block])
    state_of(1, joined[0])
    combine_of(1, [])
    state_of(2, joined[1])
    c, score = call(
        functools.partial(score_kernel, shards),
        [((slab, STATE), BF16), ((slab, BLOCK), F32)],
        [place] + seen(3) + [taps, offset, edge, b] + [Stay(o) for o in sent[2]],
        scratch=[pltpu.VMEM((slab + 8, STATE), F32)],
        name="score",
    )
    state_of(3, [score])
    local_of(0, sent[3])

    def in_full(i, order):
        wide = [pltpu.VMEM((slab, GROUPED[i][2]), F32)]
        finish_of(finish_kernel, i, [x[i], cum, row, score, skip], order, scratch=wide)

    combine_of(2, [partial[0]] + before[1] + before[0])
    in_full(1, joined[2])
    combine_of(3, [keep[1]])
    local_of(2, joined[3])
    local_of(3, [partial[2]])
    finish_of(final_kernel, 0, [partial[0]], [partial[3]])
    finish_of(final_kernel, 2, [partial[2]], [keep[0]])
    finish_of(final_kernel, 3, [partial[3]], [keep[2]])
    firsts = [first_head(i) * HEAD_DIM for i in range(count)]
    return put_in_place(firsts, (BLOCK, PAIR * PER_GROUP), place, keep, [swap(o) for o in send])


def solution(mesh):
    in_specs = (P(("ctx", "head"), None), P(("ctx", "head"), None), P(), P(), P(), P(), P())
    out_specs = P("ctx", "head")
    shards, length = mesh.shape["head"], mesh.shape["ctx"]

    def program(xbc, *rest):
        slab = xbc.shape[0] // length
        fits = shards == GROUPS // PAIR and length == 4 * PAIR and slab == BLOCK
        return jax.shard_map(
            paired if fits else on_device,
            mesh=mesh,
            in_specs=in_specs,
            out_specs=out_specs,
            check_vma=False,
        )(xbc, *rest)

    return program
```

```python
import functools

import jax
import jax.numpy as jnp
from jax import lax
from jax.experimental import pallas as pl
from jax.experimental.pallas import tpu as pltpu
from jax.sharding import PartitionSpec as P

HEADS = 256
HEAD_DIM = 64
STATE = 256
GROUPS = 8
BLOCK = 256


def from_behind(block, axis, distance):
    devices = range(lax.axis_size(axis))
    route = [(i - distance, i) for i in devices if i - distance in devices]
    return lax.ppermute(block, axis, route)


def carried_in(array, axis, combine, identity):
    length, index = (lax.axis_size(axis), lax.axis_index(axis))
    everything = jax.tree.map(lambda part: lax.all_gather(part, axis), array)
    start = jax.tree.map(
        lambda part, zero: jnp.broadcast_to(jnp.asarray(zero, part.dtype), part.shape),
        array,
        identity,
    )

    def hop(k, before):
        reached = k < index
        new = combine(before, jax.tree.map(lambda part: part[k], everything))
        return jax.tree.map(lambda a, b: jnp.where(reached, a, b), new, before)

    return lax.fori_loop(0, length, hop, start)


def convolve(rows, edge, weight, bias):
    count = rows.shape[0]
    wide = jnp.concatenate([edge, rows], 0).astype(jnp.float32)
    acc = bias[None, :] + weight[0] * wide[0:count]
    acc = acc + weight[1] * wide[1 : count + 1]
    acc = acc + weight[2] * wide[2 : count + 2]
    acc = acc + weight[3] * wide[3 : count + 3]
    return jax.nn.silu(acc).astype(jnp.bfloat16)


def rearrange_heads(rows, shards, per_dev, groups_dev, per_group):
    count = rows.shape[0]
    inner = HEADS * HEAD_DIM
    replicate_groups = max(1, per_group // per_dev)
    heads_part = rows[:, :inner].reshape(count, shards, per_dev * HEAD_DIM)
    b_part = rows[:, inner : inner + GROUPS * STATE].reshape(count, GROUPS, STATE)
    c_part = rows[:, inner + GROUPS * STATE :].reshape(count, GROUPS, STATE)
    b_part = jnp.repeat(b_part, replicate_groups, axis=1).reshape(count, shards, groups_dev * STATE)
    c_part = jnp.repeat(c_part, replicate_groups, axis=1).reshape(count, shards, groups_dev * STATE)
    return jnp.concatenate([heads_part, b_part, c_part], axis=2)


def inner_block(xs, bmat, cmat, steps, cum):
    size = xs.shape[0]
    lower = jnp.arange(size)[:, None] >= jnp.arange(size)[None, :]
    scores = jnp.einsum("qgn,kgn->gqk", cmat, bmat, preferred_element_type=jnp.float32)
    order = jnp.transpose(cum, (1, 2, 0))
    gap = order[..., :, None] - order[..., None, :]
    decay = jnp.exp(jnp.where(lower, gap, -jnp.inf))
    mixing = (scores[:, None] * decay * jnp.transpose(steps, (1, 2, 0))[..., None, :]).astype(
        jnp.bfloat16
    )
    local = jnp.einsum("gjqk,kgjp->qgjp", mixing, xs, preferred_element_type=jnp.float32)
    tail = jnp.exp(cum[size - 1][None] - cum) * steps
    loaded = (bmat[:, :, None, :].astype(jnp.float32) * tail[..., None]).astype(jnp.bfloat16)
    block_state = jnp.einsum("kgjn,kgjp->gjnp", loaded, xs, preferred_element_type=jnp.float32)
    return (local, block_state)


def on_device(xbc, dt_raw, conv_weight, conv_bias, a_log, dt_bias, skip_gain):
    tok = xbc.shape[0]
    shards = lax.axis_size("head")
    per_dev = HEADS // shards
    per_group = HEADS // GROUPS
    groups_dev = max(1, per_dev // per_group)
    heads_per_cluster = per_dev // groups_dev
    sent = rearrange_heads(xbc, shards, per_dev, groups_dev, per_group)
    mine, rates = (
        lax.all_to_all(sent, "head", split_axis=1, concat_axis=0, tiled=True),
        lax.all_to_all(
            dt_raw.reshape(tok, shards, per_dev), "head", split_axis=1, concat_axis=0, tiled=True
        ),
    )
    slab = tok * shards
    mine = mine.reshape(slab, mine.shape[2])
    rates = rates.reshape(slab, per_dev)
    shard = lax.axis_index("head")
    taps = lax.dynamic_index_in_dim(
        rearrange_heads(conv_weight, shards, per_dev, groups_dev, per_group),
        shard,
        1,
        keepdims=False,
    )
    offset = lax.dynamic_index_in_dim(
        rearrange_heads(conv_bias[None, :], shards, per_dev, groups_dev, per_group),
        shard,
        1,
        keepdims=False,
    )
    edge = from_behind(mine[slab - 3 :], "ctx", 1)
    mine = convolve(mine, edge, taps, offset[0])
    nchunk = slab // BLOCK
    width = per_dev * HEAD_DIM
    xs = mine[:, :width].reshape(nchunk, BLOCK, groups_dev, heads_per_cluster, HEAD_DIM)
    bmat = mine[:, width : width + groups_dev * STATE].reshape(nchunk, BLOCK, groups_dev, STATE)
    cmat = mine[:, width + groups_dev * STATE :].reshape(nchunk, BLOCK, groups_dev, STATE)
    first = shard * per_dev
    rate = (-jnp.exp(lax.dynamic_slice_in_dim(a_log, first, per_dev))).reshape(
        groups_dev, heads_per_cluster
    )
    bias_dt = lax.dynamic_slice_in_dim(dt_bias, first, per_dev).reshape(
        groups_dev, heads_per_cluster
    )
    skip = lax.dynamic_slice_in_dim(skip_gain, first, per_dev).reshape(
        groups_dev, heads_per_cluster
    )
    steps = jax.nn.softplus(
        rates.astype(jnp.float32).reshape(nchunk, BLOCK, groups_dev, heads_per_cluster) + bias_dt
    )
    cum = jnp.cumsum(steps * rate, axis=1)

    def block_step(carry, item):
        held, product = carry
        x_part, b_part, c_part, step_part, cum_part = item
        local, block_state = inner_block(x_part, b_part, c_part, step_part, cum_part)
        lifted = c_part.astype(jnp.float32)[:, :, None, :] * jnp.exp(cum_part)[..., None]
        carried = jnp.einsum("qgjn,gjnp->qgjp", lifted, held, precision=lax.Precision.HIGHEST)
        partial_out = local + carried + skip[..., None] * x_part.astype(jnp.float32)
        end = jnp.exp(cum_part[BLOCK - 1])
        return ((end[..., None, None] * held + block_state, product * end), (partial_out, product))

    zero_state = jnp.zeros((groups_dev, heads_per_cluster, STATE, HEAD_DIM), jnp.float32)
    unit = jnp.ones((groups_dev, heads_per_cluster), jnp.float32)
    (slab_state, slab_decay), (partials, product_in) = lax.scan(
        block_step, (zero_state, unit), (xs, bmat, cmat, steps, cum)
    )

    def combine(preceding_state, later):
        return (
            preceding_state[0] * later[0],
            later[0][..., None, None] * preceding_state[1] + later[1],
        )

    _, entering = carried_in((slab_decay, slab_state), "ctx", combine, (unit, zero_state))
    projected = jnp.einsum(
        "cqgn,gjnp->cqgjp", cmat.astype(jnp.float32), entering, precision=lax.Precision.HIGHEST
    )
    factor = jnp.exp(cum) * product_in[:, None]
    total = partials + factor[..., None] * projected
    return total.astype(jnp.bfloat16).reshape(slab, width)


PAIR = 2
LANES = 128
LOG2E = 1.4426950408889634
F32, BF16 = jnp.float32, jnp.bfloat16
WIDTHS = (512, 0, 768, 768)
RESTS = ("", "BD", "", "C")
GROUPED = ((0, 0, 512), (2, 0, 768), (3, 0, 384), (3, 384, 384))
FIRST_ROUND = ((256, 256), (384, 384), (384,), (384,))
SECOND_ROUND = ((512,), (384, 384), (384,), (384,))


FLIP = (0, 2, 3, 1)


def halves(value, count):
    parts = []
    for _ in range(count):
        part = value.astype(BF16)
        parts.append(part)
        value = value - part.astype(F32)
    return parts


def spread(first_head, width, copies):
    lane = lax.broadcasted_iota(jnp.int32, (copies * LANES, width), 0) % LANES
    column = lax.broadcasted_iota(jnp.int32, (copies * LANES, width), 1)
    return (lane == first_head + column // HEAD_DIM).astype(BF16)


def dot(a, b):
    return jnp.dot(a, b, preferred_element_type=F32)


def ds(start, width):
    return pl.ds(pl.multiple_of(start, LANES), width)


def run(copies, sems):
    started = []
    for i, (source, target) in enumerate(copies):
        copy = pltpu.make_async_copy(source, target, sems.at[i])
        copy.start()
        started.append(copy)
    return started


PER_GROUP = HEADS * HEAD_DIM // GROUPS
INNER = HEADS * HEAD_DIM


def channels(group, first, width):
    return ds(group * PER_GROUP + first, width)


def pack_first_kernel(shards, place, xbc, send, sems):
    core, shard = place[2], place[4]
    width = WIDTHS[0]
    copies = []
    for r in range(shards):
        group = (shard ^ FLIP[r]) * PAIR + 1 - core
        copies.append((xbc.at[:, channels(group, 0, width)], send.at[:, r * width : (r + 1) * width]))
    for copy in run(copies, sems):
        copy.wait()


def pack_kernel(shards, place, xbc, dt_raw, order, send, tail, sems):
    core, shard = place[2], place[4]
    count = xbc.shape[0]
    first = WIDTHS[0]
    width = PER_GROUP - first
    rest = width * shards
    size = PER_GROUP + 2 * STATE
    copies = []
    for r in range(shards):
        group = (shard ^ FLIP[r]) * PAIR + 1 - core
        copies.append((xbc.at[:, channels(group, first, width)], send.at[:, r * width : (r + 1) * width]))
        for i in range(2):
            to = rest + (i * shards + r) * STATE
            copies.append((xbc.at[:, ds(INNER + (i * GROUPS + group) * STATE, STATE)], send.at[:, to : to + STATE]))
    copies.append((dt_raw, send.at[:, send.shape[1] - HEADS :]))
    for r in range(shards):
        group, to = (shard ^ FLIP[r]) * PAIR + core, r * size
        last = xbc.at[count - 16 :]
        copies.append((last.at[:, channels(group, 0, PER_GROUP)], tail.at[:, to : to + PER_GROUP]))
        for i in range(2):
            at = ds(INNER + (i * GROUPS + group) * STATE, STATE)
            start = to + PER_GROUP + i * STATE
            copies.append((last.at[:, at], tail.at[:, start : start + STATE]))
    for copy in run(copies, sems):
        copy.wait()


def taps_kernel(place, weight, bias, order, taps, offset, sems):
    copies = []
    for source, target in ((weight, taps), (bias, offset)):
        copies.append((source.at[:, channels(place[0], 0, PER_GROUP)], target.at[:, :PER_GROUP]))
        for i in range(2):
            at = ds(INNER + (i * GROUPS + place[0]) * STATE, STATE)
            start = PER_GROUP + i * STATE
            copies.append((source.at[:, at], target.at[:, start : start + STATE]))
    for copy in run(copies, sems):
        copy.wait()


def edge_kernel(shards, place, got_first, got, tail, out):
    count = got.shape[0]
    first = WIDTHS[0]
    width = PER_GROUP - first
    size = PER_GROUP + 2 * STATE
    for r in range(shards):
        theirs = [(got_first, r * first, first), (got, r * width, width)]
        theirs += [(got, width * shards + (i * shards + r) * STATE, STATE) for i in range(2)]
        to = r * size
        for ref, start, size_of in theirs:
            a = ref[count - 16 :, start : start + size_of].astype(F32)
            b = tail[:, to : to + size_of].astype(F32)
            out[:, to : to + size_of] = jnp.where(place[2] == 0, a, b)[13:16].astype(BF16)
            to += size_of


def total_of(piece):
    return WIDTHS[piece] + sum(LANES if kind == "D" else STATE for kind in RESTS[piece])


def merge_kernel(shards, plan, unread, place, xbc, dt_raw, got_first, got, edges, *refs):
    refs = refs[unread:]
    outs, sems = refs[: len(plan)], refs[-1]
    core, shard = place[2], place[4]
    count = xbc.shape[0]
    stride = PER_GROUP - WIDTHS[0]
    mine = pl.ds(pl.multiple_of(core * count, count), count)
    other = pl.ds(pl.multiple_of((1 - core) * count, count), count)
    copies, steps = [], []
    for out, (r, pieces) in zip(outs, plan):
        group = (shard ^ FLIP[r]) * PAIR + core
        to = 0
        for piece in pieces:
            first, width = sum(WIDTHS[:piece]), WIDTHS[piece]
            if piece == 0:
                source = got_first.at[:, r * width : (r + 1) * width]
            else:
                at = r * stride + first - WIDTHS[0]
                source = got.at[:, at : at + width]
            if width:
                copies.append((xbc.at[:, channels(group, first, width)], out.at[mine, to : to + width]))
                copies.append((source, out.at[other, to : to + width]))
            to += width
            for kind in RESTS[piece]:
                if kind == "D":
                    steps.append((out, r, to))
                    to += LANES
                    continue
                i = "BC".index(kind)
                at = ds(INNER + (i * GROUPS + group) * STATE, STATE)
                copies.append((xbc.at[:, at], out.at[mine, to : to + STATE]))
                at = stride * shards + (i * shards + r) * STATE
                copies.append((got.at[:, at : at + STATE], out.at[other, to : to + STATE]))
                to += STATE
    started = run(copies, sems)
    if steps:
        lane = lax.broadcasted_iota(jnp.int32, (count, LANES), 1)
        per_tile = LANES * GROUPS // HEADS
        heads = HEADS // GROUPS
        for out, r, to in steps:
            group = (shard ^ FLIP[r]) * PAIR + core
            tile, shift = group // per_tile, (LANES - (group % per_tile) * heads) % LANES
            own = dt_raw[:, ds(tile * LANES, LANES)].astype(F32)
            theirs = got[:, ds(got.shape[1] - HEADS + tile * LANES, LANES)].astype(F32)
            low = jnp.where(core == 0, own, theirs)
            high = jnp.where(core == 0, theirs, own)
            packed = jnp.zeros((count // 2, LANES), F32)
            for j, rows in enumerate((low, high)):
                rows = jnp.where(lane < heads, pltpu.roll(rows, shift, 1), 0.0)
                for i in range(2):
                    part = rows[i * count // 2 : (i + 1) * count // 2]
                    packed = packed + pltpu.roll(part, (2 * j + i) * heads, 1)
            out[: count // 2, to : to + LANES] = packed.astype(BF16)
            size = PER_GROUP + 2 * STATE
            at = slice(r * size, (r + 1) * size)
            edge = jnp.concatenate([edges[:, at].astype(F32), jnp.zeros((1, size), F32)], 0)
            edge = jnp.concatenate([edge[:, q * LANES : (q + 1) * LANES] for q in range(size // LANES)], 0)
            fill = jnp.zeros((PAIR * count - count // 2 - edge.shape[0], LANES), F32)
            out[count // 2 :, to : to + LANES] = jnp.concatenate([edge, fill], 0).astype(BF16)
    for copy in started:
        copy.wait()


def view(refs, piece):
    return [(ref, 0) for ref in refs]


def convolve_in_order(place, blocks, columns, edge, tap, bias, wide, put):
    width = columns.stop - columns.start
    count = blocks[0][0].shape[0] // PAIR
    wide[5:8, :width] = edge
    for r, (block, origin) in enumerate(blocks):
        for core in range(PAIR):
            at = pl.multiple_of((core * len(blocks) + (place[4] ^ FLIP[r])) * count + 8, 8)
            part = block[core * count : (core + 1) * count, origin + columns.start : origin + columns.stop]
            wide[pl.ds(at, count), :width] = part.astype(F32)
    tap, bias = tap * 0.5, bias * 0.5
    for start in range(0, PAIR * len(blocks) * count, count):
        acc = bias + tap[0:1] * wide[start + 5 : start + 5 + count, :width]
        acc = acc + tap[1:2] * wide[start + 6 : start + 6 + count, :width]
        acc = acc + tap[2:3] * wide[start + 7 : start + 7 + count, :width]
        acc = acc + tap[3:4] * wide[start + 8 : start + 8 + count, :width]
        put(start, count, (acc + acc * jnp.tanh(acc)).astype(BF16))


def prep_kernel(shards, place, *refs):
    blocks, (taps, offset, a_ref, bias_ref, skip_ref, order) = refs[:shards], refs[shards : shards + 6]
    b_ref, edge_ref, cum_ref, row_ref, factor_ref, tail_ref, skip_out, dt_ref, wide = refs[shards + 6 :]
    blocks = view(blocks, 1)
    start = WIDTHS[1]
    last = total_of(1) - LANES
    size = edge_ref.shape[1]
    count = blocks[0][0].shape[0] // PAIR
    half, heads = count // 2, HEADS // GROUPS
    columns = [block[:, origin + last : origin + last + LANES].astype(F32) for block, origin in blocks]
    edge = columns[0][half : half + 4 * size // LANES]
    for column in columns[1:]:
        edge = edge + column[half : half + 4 * size // LANES]
    for q in range(size // LANES):
        edge_ref[:, q * LANES : (q + 1) * LANES] = edge[4 * q : 4 * q + 4]
    for r, column in enumerate(columns):
        packed = column[:half]
        for j in range(2 * PAIR):
            at = ((j // 2) * shards + (place[4] ^ FLIP[r])) * count + (j % 2) * half
            rows = packed if j == 0 else pltpu.roll(packed, LANES - j * heads, 1)
            dt_ref[pl.ds(pl.multiple_of(at, half), half), :] = rows

    def put(start, count, value):
        b_ref[start : start + count] = value

    at = slice(PER_GROUP, PER_GROUP + STATE)
    convolve_in_order(
        place, blocks, slice(start, start + STATE), edge_ref[0:3, at], taps[:, at], offset[:, at], wide, put
    )
    per_tile = LANES * GROUPS // HEADS
    group = place[0]
    tile = group // per_tile
    shift = (LANES - (group % per_tile) * heads) % LANES

    def lanes_of(ref):
        return pltpu.roll(jnp.broadcast_to(ref[pl.ds(tile, 1), :], (8, LANES)), shift, 1)

    rate = -jnp.exp(lanes_of(a_ref)[0:1])
    raw = dt_ref[...] + lanes_of(bias_ref)[0:1]
    step = jnp.maximum(raw, 0.0) + jnp.log1p(jnp.exp(-jnp.abs(raw)))
    skip = lanes_of(skip_ref)
    skip_out[...] = jnp.concatenate(halves(jnp.concatenate([skip, skip], 0), 3), 1)
    lower = (
        lax.broadcasted_iota(jnp.int32, (BLOCK, BLOCK), 0)
        >= lax.broadcasted_iota(jnp.int32, (BLOCK, BLOCK), 1)
    ).astype(BF16)
    valid = lax.broadcasted_iota(jnp.int32, (BLOCK, LANES), 1) < heads
    for block in range(PAIR):
        at = slice(block * BLOCK, (block + 1) * BLOCK)
        here = jnp.where(valid, step[at], 1.0)
        parts = halves(here * rate, 3)
        cum = dot(lower, parts[0]) + (dot(lower, parts[1]) + dot(lower, parts[2]))
        cum = cum * LOG2E
        cum_ref[at] = cum
        row_ref[:, at] = jnp.transpose(cum - jnp.log2(here))
        factor_ref[at] = jnp.concatenate(halves(jnp.exp2(cum), 2), 1)
        tail = jnp.exp2(cum[BLOCK - 1 :] - cum) * here
        tail_ref[at] = jnp.concatenate(halves(tail, 2), 1)


def score_kernel(shards, place, *refs):
    blocks, refs = refs[:shards], refs[shards:]
    taps, offset, edge_ref, b_ref, c_ref, score_ref, wide = (*refs[:4], *refs[-3:])
    blocks = view(blocks, 3)
    start = WIDTHS[3]
    at = slice(PER_GROUP + STATE, PER_GROUP + 2 * STATE)

    def put(start, count, value):
        c_ref[start : start + count] = value

    convolve_in_order(
        place, blocks, slice(start, start + STATE), edge_ref[0:3, at], taps[:, at], offset[:, at], wide, put
    )
    for block in range(PAIR):
        at = slice(block * BLOCK, (block + 1) * BLOCK)
        score_ref[at] = lax.dot_general(
            c_ref[at], b_ref[at], (((1,), (1,)), ((), ())), preferred_element_type=F32
        )


def decay_of(ref):
    decay = ref[STATE : STATE + 16].astype(F32)
    return decay[0:1] + (decay[1:2] + decay[2:3])


def put_decay(ref, decay):
    row = lax.broadcasted_iota(jnp.int32, (16, ref.shape[1]), 0)
    high, middle, low = (part.astype(F32) for part in halves(decay, 3))
    packed = jnp.where(row == 0, high, jnp.where(row == 1, middle, jnp.where(row == 2, low, 0.0)))
    ref[STATE:] = packed.astype(BF16)


def state_kernel(shards, part, sizes, place, *refs):
    blocks, refs = refs[:shards], refs[shards:]
    taps, offset, edge_ref, b_ref, factor_ref, tail_ref = refs[:6]
    x_ref, own_ref, *sends, wide = refs[-3 - len(sizes) :]
    piece, start, width = part
    first = sum(WIDTHS[:piece]) + start
    at = slice(first, first + width)

    def put(row, count, value):
        x_ref[row : row + count] = value

    blocks = view(blocks, piece)
    columns = slice(start, start + width)
    convolve_in_order(place, blocks, columns, edge_ref[0:3, at], taps[:, at], offset[:, at], wide, put)
    expand = spread(first // HEAD_DIM, width, 2)
    both = []
    for block in range(PAIR):
        at = slice(block * BLOCK, (block + 1) * BLOCK)
        loaded = (x_ref[at].astype(F32) * dot(tail_ref[at], expand)).astype(BF16)
        both.append(
            lax.dot_general(b_ref[at], loaded, (((0,), (0,)), ((), ())), preferred_element_type=F32)
        )
    ends = [dot(factor_ref[(i + 1) * BLOCK - 16 : (i + 1) * BLOCK], expand)[15:16] for i in range(PAIR)]
    own_ref[...] = both[0]
    end = (ends[1] * both[0] + both[1]).astype(BF16)
    decay = ends[0] * ends[1]
    start = 0
    for send_ref in sends:
        at = slice(start, start + send_ref.shape[1])
        send_ref[0:STATE] = end[:, at]
        put_decay(send_ref, decay[:, at])
        start = at.stop


def combine_kernel(spans, place, *refs):
    count = len(spans)
    got, own, out_ref = refs[:count], refs[count : 2 * count], refs[-1]
    odd = place[1] % 2 == 1
    start = 0
    for got_ref, own_ref, span in zip(got, own, spans):
        at = slice(start, start + span.stop - span.start)
        theirs, mine = got_ref[:STATE, span].astype(F32), own_ref[:STATE, span].astype(F32)
        decay, other = decay_of(own_ref.at[:, span]), decay_of(got_ref.at[:, span])
        total = jnp.where(odd, decay, 1.0) * theirs + jnp.where(odd, 1.0, other) * mine
        out_ref[:STATE, at] = total.astype(BF16)
        put_decay(out_ref.at[:, at], decay * other)
        start = at.stop


def mix(first_head, x_ref, cum_ref, row_ref, score_ref, skip_ref, put):
    width = x_ref.shape[1]
    half = BLOCK // 2
    expand = spread(first_head, width, 3)
    skip = dot(skip_ref[...], expand)[0:1]
    lower = lax.broadcasted_iota(jnp.int32, (half, half), 0) >= lax.broadcasted_iota(
        jnp.int32, (half, half), 1
    )
    lane = lax.broadcasted_iota(jnp.int32, (BLOCK, LANES), 1)
    for block in range(PAIR):
        base = block * BLOCK
        for tile in range(width // LANES):
            columns = slice(tile * LANES, (tile + 1) * LANES)
            x = x_ref[base : base + BLOCK, columns]
            top = skip[:, columns] * x[:half].astype(F32)
            bottom = skip[:, columns] * x[half:].astype(F32)
            for side in range(LANES // HEAD_DIM):
                head = first_head + tile * (LANES // HEAD_DIM) + side
                own = jnp.where(lane // HEAD_DIM == side, x, jnp.zeros_like(x))
                cum = cum_ref[base : base + BLOCK, head : head + 1]
                row = row_ref[head : head + 1, base : base + BLOCK]
                diag = jnp.where(lower, cum[:half] - row[:, :half], -1e30)
                mixing = jnp.exp2(diag) * score_ref[base : base + half, :half]
                top = top + dot(mixing.astype(BF16), own[:half])
                left = jnp.exp2(cum[half:] - row[:, :half]) * score_ref[base + half : base + BLOCK, :half]
                diag = jnp.where(lower, cum[half:] - row[:, half:], -1e30)
                right = jnp.exp2(diag) * score_ref[base + half : base + BLOCK, half:]
                mixing = jnp.concatenate([left.astype(BF16), right.astype(BF16)], 1)
                bottom = bottom + dot(mixing, own)
            put(block, slice(base, base + half), columns, top)
            put(block, slice(base + half, base + BLOCK), columns, bottom)


def local_kernel(first_head, x_ref, cum_ref, row_ref, score_ref, skip_ref, *refs):
    out_ref = refs[-1]

    def put(block, rows, columns, value):
        out_ref[rows, columns] = value

    mix(first_head, x_ref, cum_ref, row_ref, score_ref, skip_ref, put)


def carry(first_head, place, lasts, befores, own_ref, c_ref, factor_ref, add, keep_ref, send_ref):
    expand = spread(first_head, own_ref.shape[1], 2)
    last, before = (
        refs[0][...] if len(refs) == 1 else jnp.concatenate([ref[...] for ref in refs], 1)
        for refs in (lasts, befores)
    )
    odd, core = place[1] % 2 == 1, place[2]
    near = jnp.where(odd, last[:STATE].astype(F32), 0.0)
    held = near + jnp.where(odd, decay_of(last), 1.0) * before[:STATE].astype(F32)
    factor = dot(factor_ref[...], expand)
    outs = []
    for block in range(PAIR):
        at = slice(block * BLOCK, (block + 1) * BLOCK)
        carried = dot(c_ref[at], held.astype(BF16))
        outs.append((add[at] + factor[at] * carried).astype(BF16))
        held = factor[BLOCK - 1 : BLOCK] * held + own_ref[...]

    @pl.when(core == 0)
    def _():
        keep_ref[...] = outs[0]
        send_ref[...] = outs[1]

    @pl.when(core == 1)
    def _():
        keep_ref[...] = outs[1]
        send_ref[...] = outs[0]


def final_kernel(first_head, counts, place, *refs):
    groups = []
    for number in counts:
        groups.append(refs[:number])
        refs = refs[number:]
    carry(first_head, place, *groups, *refs[:4], *refs[-2:])


def finish_kernel(first_head, counts, place, *refs):
    groups = []
    for number in counts:
        groups.append(refs[:number])
        refs = refs[number:]
    own_ref, c_ref, factor_ref = refs[:3]
    keep_ref, send_ref, partial = refs[-3:]
    local_kernel(first_head, *refs[3:8], partial)
    carry(first_head, place, *groups, own_ref, c_ref, factor_ref, partial, keep_ref, send_ref)


def place_kernel(firsts, place, *refs):
    count = len(firsts)
    keeps, gots = refs[:count], refs[count : 2 * count]
    out, sems = refs[-2:]
    core = place[2]
    half = out.shape[1] // PAIR
    copies = []
    for first, keep, got in zip(firsts, keeps, gots):
        width = keep.shape[1]
        copies.append((keep, out.at[:, ds(core * half + first, width)]))
        copies.append((got, out.at[:, ds((1 - core) * half + first, width)]))
    for copy in run(copies, sems):
        copy.wait()


def put_in_place(firsts, shape, place, keeps, gots):
    smem, vmem, hbm = (pl.BlockSpec(memory_space=m) for m in (pltpu.SMEM, pltpu.VMEM, pltpu.HBM))
    count = len(firsts)
    return pl.pallas_call(
        functools.partial(place_kernel, firsts),
        out_shape=jax.ShapeDtypeStruct(shape, BF16),
        in_specs=[smem] + [vmem] * (2 * count),
        out_specs=hbm,
        scratch_shapes=[pltpu.SemaphoreType.DMA((2 * count,))],
        compiler_params=pltpu.CompilerParams(vmem_limit_bytes=16 << 20),
        cost_estimate=pl.CostEstimate(flops=1, bytes_accessed=1, transcendentals=0),
        name="place",
    )(place, *keeps, *gots)


class Stay:
    def __init__(self, array):
        self.array = array


def gate(blocks, order):
    anywhere = pl.BlockSpec(memory_space=pl.ANY)
    return pl.pallas_call(
        lambda *refs: None,
        out_shape=[jax.ShapeDtypeStruct(block.shape, block.dtype) for block in blocks],
        in_specs=[anywhere] * (len(blocks) + len(order)),
        out_specs=[anywhere] * len(blocks),
        input_output_aliases={i: i for i in range(len(blocks))},
        compiler_params=pltpu.CompilerParams(vmem_limit_bytes=16 << 20),
        cost_estimate=pl.CostEstimate(flops=1, bytes_accessed=1, transcendentals=0),
        name="gate",
    )(*blocks, *order)


def call(body, outs, operands, scratch=(), flops=0, transcendentals=0, name=None, limit=16 << 20):
    shapes = [jax.ShapeDtypeStruct(shape, dtype) for shape, dtype in outs]
    smem, vmem, hbm = (pl.BlockSpec(memory_space=m) for m in (pltpu.SMEM, pltpu.VMEM, pltpu.HBM))
    specs = [
        hbm if isinstance(o, Stay) else smem if o.dtype == jnp.int32 else vmem for o in operands
    ]
    moved = sum(o.size * o.dtype.itemsize for o in shapes) * 2
    return pl.pallas_call(
        body,
        out_shape=shapes,
        in_specs=specs,
        out_specs=[vmem] * len(outs),
        scratch_shapes=scratch,
        compiler_params=pltpu.CompilerParams(vmem_limit_bytes=limit),
        cost_estimate=pl.CostEstimate(flops=1, bytes_accessed=1, transcendentals=0),
        name=name,
    )(*[o.array if isinstance(o, Stay) else o for o in operands])


def paired(xbc, dt_raw, conv_weight, conv_bias, a_log, dt_bias, skip_gain):
    axes = ("ctx", "head")
    shards, length = lax.axis_size("head"), lax.axis_size("ctx")
    devices, peers = shards * length, shards * PAIR
    tok = xbc.shape[0]
    slab = tok * peers
    context, shard = lax.axis_index("ctx"), lax.axis_index("head")
    pair, core = context // PAIR, context % PAIR
    group = shard * PAIR + core
    place = jnp.stack([group, pair, core, core * shards + shard, shard]).astype(jnp.int32)

    def over(block, target):
        route = [(i, target(i)) for i in range(devices)]
        return lax.ppermute(block, axes, [(i, j) for i, j in route if j is not None and j < devices])

    def swap(block):
        return over(block, lambda i: i ^ shards)

    rows = Stay(xbc)
    size = PER_GROUP + 2 * STATE
    (sent,) = call(
        functools.partial(pack_first_kernel, shards),
        [((tok, shards * WIDTHS[0]), BF16)],
        [place, rows],
        scratch=[pltpu.SemaphoreType.DMA((shards,))],
        name="pack_first",
    )
    got_first = swap(sent)
    sent, tail = call(
        functools.partial(pack_kernel, shards),
        [((tok, shards * (size - WIDTHS[0]) + HEADS), BF16), ((16, shards * size), BF16)],
        [place, rows, Stay(dt_raw), Stay(sent)],
        scratch=[pltpu.SemaphoreType.DMA((6 * shards + 1,))],
        name="pack",
    )
    got_rest = swap(gate([sent], [got_first])[0])
    taps, offset = call(
        taps_kernel,
        [((4, size), F32), ((1, size), F32)],
        [place, Stay(conv_weight), Stay(conv_bias[None]), Stay(got_rest)],
        scratch=[pltpu.SemaphoreType.DMA((6,))],
        name="taps",
    )

    def send_on(plan, order, edges=None):
        unused = Stay(got_first)
        parts = [p for _, pieces in plan for p in pieces]
        return call(
            functools.partial(merge_kernel, shards, plan, len(order)),
            [((PAIR * tok, sum(map(total_of, pieces))), BF16) for _, pieces in plan],
            [
                place,
                rows,
                Stay(dt_raw) if edges is None else dt_raw,
                got_first if 0 in parts else unused,
                got_rest if any(parts) else unused,
                unused if edges is None else edges,
            ]
            + [Stay(o) for o in order],
            scratch=[pltpu.SemaphoreType.DMA((sum(2 + 2 * len(RESTS[p]) for p in parts),))],
            name="merge",
        )

    def travel(blocks):
        return [blocks[0]] + [over(blocks[r], lambda i, r=r: i ^ FLIP[r]) for r in range(1, shards)]

    def plan(piece):
        return [(r, (piece,)) for r in range(shards)]

    first_blocks = send_on(plan(0), [])
    message = [travel(first_blocks)]
    (edges,) = call(
        functools.partial(edge_kernel, shards),
        [((3, shards * size), BF16)],
        [place, got_first, got_rest, tail],
        name="edge",
    )
    edges = over(edges, lambda i: i + peers if i % shards == shards - 1 else None)
    second_blocks = send_on(plan(1), [first_blocks[0]], edges)
    message.append(travel(second_blocks))
    third_blocks = send_on(plan(2), [second_blocks[0]])
    message.append(travel(third_blocks[:1] + gate(third_blocks[1:], message[0][1:] + message[1][1:] + [taps])))

    def seen(piece):
        return message[piece]

    tiles = [p.reshape(HEADS // LANES, LANES) for p in (a_log, dt_bias, skip_gain)]
    b, edge, cum, row, factor, tail, skip = call(
        functools.partial(prep_kernel, shards),
        [
            ((slab, STATE), BF16),
            ((4, size), F32),
            ((slab, LANES), F32),
            ((LANES, slab), F32),
            ((slab, 2 * LANES), BF16),
            ((slab, 2 * LANES), BF16),
            ((16, 3 * LANES), BF16),
        ],
        [place] + seen(1) + [taps, offset] + tiles + [Stay(third_blocks[0])],
        scratch=[pltpu.VMEM((slab, LANES), F32), pltpu.VMEM((slab + 8, STATE), F32)],
        name="prep",
    )
    count = len(GROUPED)
    x, sent, own, last, joined, before, keep, send = ([None] * count for _ in range(8))

    def first_head(i):
        return (sum(WIDTHS[: GROUPED[i][0]]) + GROUPED[i][1]) // HEAD_DIM

    def state_of(i, order):
        piece, _, width = GROUPED[i]
        x[i], own[i], *sent[i] = call(
            functools.partial(state_kernel, shards, GROUPED[i], FIRST_ROUND[i]),
            [((slab, width), BF16), ((STATE, width), F32)] + [((STATE + 16, w), BF16) for w in FIRST_ROUND[i]],
            [place] + seen(piece) + [taps, offset, edge, b, factor, tail] + [Stay(o) for o in order],
            scratch=[pltpu.VMEM((slab + 8, width), F32)],
            name="state",
        )
        last[i] = [over(part, lambda i: i ^ peers if i // peers != 3 else None) for part in sent[i]]

    def combine_of(i, order):
        joined[i], before[i] = [], []
        end = 0
        for width in SECOND_ROUND[i]:
            begin, end = end, end + width
            early, late, spans, first = [], [], [], 0
            for got, mine, size_of in zip(last[i], sent[i], FIRST_ROUND[i]):
                low, high = max(begin - first, 0), min(end - first, size_of)
                first += size_of
                if low < high:
                    early.append(got)
                    late.append(mine)
                    spans.append(slice(low, high))
            (total,) = call(
                functools.partial(combine_kernel, spans),
                [((STATE + 16, width), BF16)],
                [place] + early + late + [Stay(o) for o in order],
                name="combine",
            )
            joined[i].append(total)
            before[i].append(over(total, lambda i: i + 2 * peers))
            order = [total]

    def finish_of(body, i, operands, order, **more):
        keep[i], send[i] = call(
            functools.partial(body, first_head(i), (len(last[i]), len(before[i]))),
            [((BLOCK, GROUPED[i][2]), BF16)] * 2,
            [place, *last[i], *before[i], own[i], c, factor] + operands + [Stay(o) for o in order],
            name="final",
            **more,
        )

    partial = [None] * count

    def local_of(i, order):
        (partial[i],) = call(
            functools.partial(local_kernel, first_head(i)),
            [(x[i].shape, F32)],
            [x[i], cum, row, score, skip] + [Stay(o) for o in order],
            name="local",
        )

    state_of(0, [])
    own_block, *fourth_blocks = send_on(plan(3), sent[0])
    message.append(travel([own_block, *gate(fourth_blocks, message[2][1:])]))
    combine_of(0, [own_block])
    state_of(1, joined[0])
    combine_of(1, [])
    state_of(2, joined[1])
    c, score = call(
        functools.partial(score_kernel, shards),
        [((slab, STATE), BF16), ((slab, BLOCK), F32)],
        [place] + seen(3) + [taps, offset, edge, b] + [Stay(o) for o in sent[2]],
        scratch=[pltpu.VMEM((slab + 8, STATE), F32)],
        name="score",
    )
    state_of(3, [score])
    local_of(0, sent[3])

    def in_full(i, order):
        wide = [pltpu.VMEM((slab, GROUPED[i][2]), F32)]
        finish_of(finish_kernel, i, [x[i], cum, row, score, skip], order, scratch=wide)

    combine_of(2, [partial[0]] + before[1])
    in_full(1, joined[2])
    combine_of(3, [keep[1]])
    local_of(2, joined[3])
    local_of(3, [partial[2]])
    finish_of(final_kernel, 0, [partial[0]], [partial[3]])
    finish_of(final_kernel, 2, [partial[2]], [keep[0]])
    finish_of(final_kernel, 3, [partial[3]], [keep[2]])
    firsts = [first_head(i) * HEAD_DIM for i in range(count)]
    return put_in_place(firsts, (BLOCK, PAIR * PER_GROUP), place, keep, [swap(o) for o in send])


def solution(mesh):
    in_specs = (P(("ctx", "head"), None), P(("ctx", "head"), None), P(), P(), P(), P(), P())
    out_specs = P("ctx", "head")
    shards, length = mesh.shape["head"], mesh.shape["ctx"]

    def program(xbc, *rest):
        slab = xbc.shape[0] // length
        fits = shards == GROUPS // PAIR and length == 4 * PAIR and slab == BLOCK
        return jax.shard_map(
            paired if fits else on_device,
            mesh=mesh,
            in_specs=in_specs,
            out_specs=out_specs,
            check_vma=False,
        )(xbc, *rest)

    return program
```

```python
import functools

import jax
import jax.numpy as jnp
from jax import lax
from jax.experimental import pallas as pl
from jax.experimental.pallas import tpu as pltpu
from jax.sharding import PartitionSpec as P

HEADS = 256
HEAD_DIM = 64
STATE = 256
GROUPS = 8
BLOCK = 256


def from_behind(block, axis, distance):
    devices = range(lax.axis_size(axis))
    route = [(i - distance, i) for i in devices if i - distance in devices]
    return lax.ppermute(block, axis, route)


def carried_in(array, axis, combine, identity):
    length, index = (lax.axis_size(axis), lax.axis_index(axis))
    everything = jax.tree.map(lambda part: lax.all_gather(part, axis), array)
    start = jax.tree.map(
        lambda part, zero: jnp.broadcast_to(jnp.asarray(zero, part.dtype), part.shape),
        array,
        identity,
    )

    def hop(k, before):
        reached = k < index
        new = combine(before, jax.tree.map(lambda part: part[k], everything))
        return jax.tree.map(lambda a, b: jnp.where(reached, a, b), new, before)

    return lax.fori_loop(0, length, hop, start)


def convolve(rows, edge, weight, bias):
    count = rows.shape[0]
    wide = jnp.concatenate([edge, rows], 0).astype(jnp.float32)
    acc = bias[None, :] + weight[0] * wide[0:count]
    acc = acc + weight[1] * wide[1 : count + 1]
    acc = acc + weight[2] * wide[2 : count + 2]
    acc = acc + weight[3] * wide[3 : count + 3]
    return jax.nn.silu(acc).astype(jnp.bfloat16)


def rearrange_heads(rows, shards, per_dev, groups_dev, per_group):
    count = rows.shape[0]
    inner = HEADS * HEAD_DIM
    replicate_groups = max(1, per_group // per_dev)
    heads_part = rows[:, :inner].reshape(count, shards, per_dev * HEAD_DIM)
    b_part = rows[:, inner : inner + GROUPS * STATE].reshape(count, GROUPS, STATE)
    c_part = rows[:, inner + GROUPS * STATE :].reshape(count, GROUPS, STATE)
    b_part = jnp.repeat(b_part, replicate_groups, axis=1).reshape(count, shards, groups_dev * STATE)
    c_part = jnp.repeat(c_part, replicate_groups, axis=1).reshape(count, shards, groups_dev * STATE)
    return jnp.concatenate([heads_part, b_part, c_part], axis=2)


def inner_block(xs, bmat, cmat, steps, cum):
    size = xs.shape[0]
    lower = jnp.arange(size)[:, None] >= jnp.arange(size)[None, :]
    scores = jnp.einsum("qgn,kgn->gqk", cmat, bmat, preferred_element_type=jnp.float32)
    order = jnp.transpose(cum, (1, 2, 0))
    gap = order[..., :, None] - order[..., None, :]
    decay = jnp.exp(jnp.where(lower, gap, -jnp.inf))
    mixing = (scores[:, None] * decay * jnp.transpose(steps, (1, 2, 0))[..., None, :]).astype(
        jnp.bfloat16
    )
    local = jnp.einsum("gjqk,kgjp->qgjp", mixing, xs, preferred_element_type=jnp.float32)
    tail = jnp.exp(cum[size - 1][None] - cum) * steps
    loaded = (bmat[:, :, None, :].astype(jnp.float32) * tail[..., None]).astype(jnp.bfloat16)
    block_state = jnp.einsum("kgjn,kgjp->gjnp", loaded, xs, preferred_element_type=jnp.float32)
    return (local, block_state)


def on_device(xbc, dt_raw, conv_weight, conv_bias, a_log, dt_bias, skip_gain):
    tok = xbc.shape[0]
    shards = lax.axis_size("head")
    per_dev = HEADS // shards
    per_group = HEADS // GROUPS
    groups_dev = max(1, per_dev // per_group)
    heads_per_cluster = per_dev // groups_dev
    sent = rearrange_heads(xbc, shards, per_dev, groups_dev, per_group)
    mine, rates = (
        lax.all_to_all(sent, "head", split_axis=1, concat_axis=0, tiled=True),
        lax.all_to_all(
            dt_raw.reshape(tok, shards, per_dev), "head", split_axis=1, concat_axis=0, tiled=True
        ),
    )
    slab = tok * shards
    mine = mine.reshape(slab, mine.shape[2])
    rates = rates.reshape(slab, per_dev)
    shard = lax.axis_index("head")
    taps = lax.dynamic_index_in_dim(
        rearrange_heads(conv_weight, shards, per_dev, groups_dev, per_group),
        shard,
        1,
        keepdims=False,
    )
    offset = lax.dynamic_index_in_dim(
        rearrange_heads(conv_bias[None, :], shards, per_dev, groups_dev, per_group),
        shard,
        1,
        keepdims=False,
    )
    edge = from_behind(mine[slab - 3 :], "ctx", 1)
    mine = convolve(mine, edge, taps, offset[0])
    nchunk = slab // BLOCK
    width = per_dev * HEAD_DIM
    xs = mine[:, :width].reshape(nchunk, BLOCK, groups_dev, heads_per_cluster, HEAD_DIM)
    bmat = mine[:, width : width + groups_dev * STATE].reshape(nchunk, BLOCK, groups_dev, STATE)
    cmat = mine[:, width + groups_dev * STATE :].reshape(nchunk, BLOCK, groups_dev, STATE)
    first = shard * per_dev
    rate = (-jnp.exp(lax.dynamic_slice_in_dim(a_log, first, per_dev))).reshape(
        groups_dev, heads_per_cluster
    )
    bias_dt = lax.dynamic_slice_in_dim(dt_bias, first, per_dev).reshape(
        groups_dev, heads_per_cluster
    )
    skip = lax.dynamic_slice_in_dim(skip_gain, first, per_dev).reshape(
        groups_dev, heads_per_cluster
    )
    steps = jax.nn.softplus(
        rates.astype(jnp.float32).reshape(nchunk, BLOCK, groups_dev, heads_per_cluster) + bias_dt
    )
    cum = jnp.cumsum(steps * rate, axis=1)

    def block_step(carry, item):
        held, product = carry
        x_part, b_part, c_part, step_part, cum_part = item
        local, block_state = inner_block(x_part, b_part, c_part, step_part, cum_part)
        lifted = c_part.astype(jnp.float32)[:, :, None, :] * jnp.exp(cum_part)[..., None]
        carried = jnp.einsum("qgjn,gjnp->qgjp", lifted, held, precision=lax.Precision.HIGHEST)
        partial_out = local + carried + skip[..., None] * x_part.astype(jnp.float32)
        end = jnp.exp(cum_part[BLOCK - 1])
        return ((end[..., None, None] * held + block_state, product * end), (partial_out, product))

    zero_state = jnp.zeros((groups_dev, heads_per_cluster, STATE, HEAD_DIM), jnp.float32)
    unit = jnp.ones((groups_dev, heads_per_cluster), jnp.float32)
    (slab_state, slab_decay), (partials, product_in) = lax.scan(
        block_step, (zero_state, unit), (xs, bmat, cmat, steps, cum)
    )

    def combine(preceding_state, later):
        return (
            preceding_state[0] * later[0],
            later[0][..., None, None] * preceding_state[1] + later[1],
        )

    _, entering = carried_in((slab_decay, slab_state), "ctx", combine, (unit, zero_state))
    projected = jnp.einsum(
        "cqgn,gjnp->cqgjp", cmat.astype(jnp.float32), entering, precision=lax.Precision.HIGHEST
    )
    factor = jnp.exp(cum) * product_in[:, None]
    total = partials + factor[..., None] * projected
    return total.astype(jnp.bfloat16).reshape(slab, width)


PAIR = 2
LANES = 128
LOG2E = 1.4426950408889634
F32, BF16 = jnp.float32, jnp.bfloat16
WIDTHS = (512, 0, 768, 768)
RESTS = ("", "BD", "", "C")
GROUPED = ((0, 0, 512), (2, 0, 768), (3, 0, 384), (3, 384, 384))
FIRST_ROUND = ((256, 256), (384, 384), (384,), (384,))
SECOND_ROUND = ((512,), (384, 384), (384,), (384,))


FLIP = (0, 2, 3, 1)
NEAR = 3


def halves(value, count):
    parts = []
    for _ in range(count):
        part = value.astype(BF16)
        parts.append(part)
        value = value - part.astype(F32)
    return parts


def spread(first_head, width, copies):
    lane = lax.broadcasted_iota(jnp.int32, (copies * LANES, width), 0) % LANES
    column = lax.broadcasted_iota(jnp.int32, (copies * LANES, width), 1)
    return (lane == first_head + column // HEAD_DIM).astype(BF16)


def dot(a, b):
    return jnp.dot(a, b, preferred_element_type=F32)


def ds(start, width):
    return pl.ds(pl.multiple_of(start, LANES), width)


def run(copies, sems):
    started = []
    for i, (source, target) in enumerate(copies):
        copy = pltpu.make_async_copy(source, target, sems.at[i])
        copy.start()
        started.append(copy)
    return started


PER_GROUP = HEADS * HEAD_DIM // GROUPS
INNER = HEADS * HEAD_DIM


def channels(group, first, width):
    return ds(group * PER_GROUP + first, width)


def pack_first_kernel(shards, place, xbc, send, sems):
    core, shard = place[2], place[4]
    width = WIDTHS[0]
    copies = []
    for r in range(shards):
        group = (shard ^ FLIP[r]) * PAIR + 1 - core
        copies.append((xbc.at[:, channels(group, 0, width)], send.at[:, r * width : (r + 1) * width]))
    for copy in run(copies, sems):
        copy.wait()


def pack_kernel(shards, place, xbc, dt_raw, order, send, tail, sems):
    core, shard = place[2], place[4]
    count = xbc.shape[0]
    first = WIDTHS[0]
    width = PER_GROUP - first
    rest = width * shards
    size = PER_GROUP + 2 * STATE
    copies = []
    for r in range(shards):
        group = (shard ^ FLIP[r]) * PAIR + 1 - core
        copies.append((xbc.at[:, channels(group, first, width)], send.at[:, r * width : (r + 1) * width]))
        for i in range(2):
            to = rest + (i * shards + r) * STATE
            copies.append((xbc.at[:, ds(INNER + (i * GROUPS + group) * STATE, STATE)], send.at[:, to : to + STATE]))
    copies.append((dt_raw, send.at[:, send.shape[1] - HEADS :]))
    for r in range(shards):
        group, to = (shard ^ FLIP[r]) * PAIR + core, r * size
        last = xbc.at[count - 16 :]
        copies.append((last.at[:, channels(group, 0, PER_GROUP)], tail.at[:, to : to + PER_GROUP]))
        for i in range(2):
            at = ds(INNER + (i * GROUPS + group) * STATE, STATE)
            start = to + PER_GROUP + i * STATE
            copies.append((last.at[:, at], tail.at[:, start : start + STATE]))
    for copy in run(copies, sems):
        copy.wait()


def taps_kernel(place, weight, bias, order, taps, offset, sems):
    copies = []
    for source, target in ((weight, taps), (bias, offset)):
        copies.append((source.at[:, channels(place[0], 0, PER_GROUP)], target.at[:, :PER_GROUP]))
        for i in range(2):
            at = ds(INNER + (i * GROUPS + place[0]) * STATE, STATE)
            start = PER_GROUP + i * STATE
            copies.append((source.at[:, at], target.at[:, start : start + STATE]))
    for copy in run(copies, sems):
        copy.wait()


def edge_kernel(shards, place, got_first, got, tail, out):
    count = got.shape[0]
    first = WIDTHS[0]
    width = PER_GROUP - first
    size = PER_GROUP + 2 * STATE
    for r in range(shards):
        theirs = [(got_first, r * first, first), (got, r * width, width)]
        theirs += [(got, width * shards + (i * shards + r) * STATE, STATE) for i in range(2)]
        to = r * size
        for ref, start, size_of in theirs:
            a = ref[count - 16 :, start : start + size_of].astype(F32)
            b = tail[:, to : to + size_of].astype(F32)
            out[:, to : to + size_of] = jnp.where(place[2] == 0, a, b)[13:16].astype(BF16)
            to += size_of


def total_of(piece):
    return WIDTHS[piece] + sum(LANES if kind == "D" else STATE for kind in RESTS[piece])


def merge_kernel(shards, plan, unread, place, xbc, dt_raw, got_first, got, edges, *refs):
    refs = refs[unread:]
    outs, sems = refs[: len(plan)], refs[-1]
    core, shard = place[2], place[4]
    count = xbc.shape[0]
    stride = PER_GROUP - WIDTHS[0]
    mine = pl.ds(pl.multiple_of(core * count, count), count)
    other = pl.ds(pl.multiple_of((1 - core) * count, count), count)
    copies, steps = [], []
    for out, (r, pieces) in zip(outs, plan):
        group = (shard ^ FLIP[r]) * PAIR + core
        to = 0
        for piece in pieces:
            first, width = sum(WIDTHS[:piece]), WIDTHS[piece]
            if piece == 0:
                source = got_first.at[:, r * width : (r + 1) * width]
            else:
                at = r * stride + first - WIDTHS[0]
                source = got.at[:, at : at + width]
            if width:
                copies.append((xbc.at[:, channels(group, first, width)], out.at[mine, to : to + width]))
                copies.append((source, out.at[other, to : to + width]))
            to += width
            for kind in RESTS[piece]:
                if kind == "D":
                    steps.append((out, r, to))
                    to += LANES
                    continue
                i = "BC".index(kind)
                at = ds(INNER + (i * GROUPS + group) * STATE, STATE)
                copies.append((xbc.at[:, at], out.at[mine, to : to + STATE]))
                at = stride * shards + (i * shards + r) * STATE
                copies.append((got.at[:, at : at + STATE], out.at[other, to : to + STATE]))
                to += STATE
    started = run(copies, sems)
    if steps:
        lane = lax.broadcasted_iota(jnp.int32, (count, LANES), 1)
        per_tile = LANES * GROUPS // HEADS
        heads = HEADS // GROUPS
        for out, r, to in steps:
            group = (shard ^ FLIP[r]) * PAIR + core
            tile, shift = group // per_tile, (LANES - (group % per_tile) * heads) % LANES
            own = dt_raw[:, ds(tile * LANES, LANES)].astype(F32)
            theirs = got[:, ds(got.shape[1] - HEADS + tile * LANES, LANES)].astype(F32)
            low = jnp.where(core == 0, own, theirs)
            high = jnp.where(core == 0, theirs, own)
            packed = jnp.zeros((count // 2, LANES), F32)
            for j, rows in enumerate((low, high)):
                rows = jnp.where(lane < heads, pltpu.roll(rows, shift, 1), 0.0)
                for i in range(2):
                    part = rows[i * count // 2 : (i + 1) * count // 2]
                    packed = packed + pltpu.roll(part, (2 * j + i) * heads, 1)
            out[: count // 2, to : to + LANES] = packed.astype(BF16)
            size = PER_GROUP + 2 * STATE
            at = slice(r * size, (r + 1) * size)
            edge = jnp.concatenate([edges[:, at].astype(F32), jnp.zeros((1, size), F32)], 0)
            edge = jnp.concatenate([edge[:, q * LANES : (q + 1) * LANES] for q in range(size // LANES)], 0)
            fill = jnp.zeros((PAIR * count - count // 2 - edge.shape[0], LANES), F32)
            out[count // 2 :, to : to + LANES] = jnp.concatenate([edge, fill], 0).astype(BF16)
    for copy in started:
        copy.wait()


def view(refs, piece):
    return [(ref, total_of(2) if piece == 3 and r == NEAR else 0) for r, ref in enumerate(refs)]


def convolve_in_order(place, blocks, columns, edge, tap, bias, wide, put):
    width = columns.stop - columns.start
    count = blocks[0][0].shape[0] // PAIR
    wide[5:8, :width] = edge
    for r, (block, origin) in enumerate(blocks):
        for core in range(PAIR):
            at = pl.multiple_of((core * len(blocks) + (place[4] ^ FLIP[r])) * count + 8, 8)
            part = block[core * count : (core + 1) * count, origin + columns.start : origin + columns.stop]
            wide[pl.ds(at, count), :width] = part.astype(F32)
    tap, bias = tap * 0.5, bias * 0.5
    for start in range(0, PAIR * len(blocks) * count, count):
        acc = bias + tap[0:1] * wide[start + 5 : start + 5 + count, :width]
        acc = acc + tap[1:2] * wide[start + 6 : start + 6 + count, :width]
        acc = acc + tap[2:3] * wide[start + 7 : start + 7 + count, :width]
        acc = acc + tap[3:4] * wide[start + 8 : start + 8 + count, :width]
        put(start, count, (acc + acc * jnp.tanh(acc)).astype(BF16))


def prep_kernel(shards, place, *refs):
    blocks, (taps, offset, a_ref, bias_ref, skip_ref, order) = refs[:shards], refs[shards : shards + 6]
    b_ref, edge_ref, cum_ref, row_ref, factor_ref, tail_ref, skip_out, dt_ref, wide = refs[shards + 6 :]
    blocks = view(blocks, 1)
    start = WIDTHS[1]
    last = total_of(1) - LANES
    size = edge_ref.shape[1]
    count = blocks[0][0].shape[0] // PAIR
    half, heads = count // 2, HEADS // GROUPS
    columns = [block[:, origin + last : origin + last + LANES].astype(F32) for block, origin in blocks]
    edge = columns[0][half : half + 4 * size // LANES]
    for column in columns[1:]:
        edge = edge + column[half : half + 4 * size // LANES]
    for q in range(size // LANES):
        edge_ref[:, q * LANES : (q + 1) * LANES] = edge[4 * q : 4 * q + 4]
    for r, column in enumerate(columns):
        packed = column[:half]
        for j in range(2 * PAIR):
            at = ((j // 2) * shards + (place[4] ^ FLIP[r])) * count + (j % 2) * half
            rows = packed if j == 0 else pltpu.roll(packed, LANES - j * heads, 1)
            dt_ref[pl.ds(pl.multiple_of(at, half), half), :] = rows

    def put(start, count, value):
        b_ref[start : start + count] = value

    at = slice(PER_GROUP, PER_GROUP + STATE)
    convolve_in_order(
        place, blocks, slice(start, start + STATE), edge_ref[0:3, at], taps[:, at], offset[:, at], wide, put
    )
    per_tile = LANES * GROUPS // HEADS
    group = place[0]
    tile = group // per_tile
    shift = (LANES - (group % per_tile) * heads) % LANES

    def lanes_of(ref):
        return pltpu.roll(jnp.broadcast_to(ref[pl.ds(tile, 1), :], (8, LANES)), shift, 1)

    rate = -jnp.exp(lanes_of(a_ref)[0:1])
    raw = dt_ref[...] + lanes_of(bias_ref)[0:1]
    step = jnp.maximum(raw, 0.0) + jnp.log1p(jnp.exp(-jnp.abs(raw)))
    skip = lanes_of(skip_ref)
    skip_out[...] = jnp.concatenate(halves(jnp.concatenate([skip, skip], 0), 3), 1)
    lower = (
        lax.broadcasted_iota(jnp.int32, (BLOCK, BLOCK), 0)
        >= lax.broadcasted_iota(jnp.int32, (BLOCK, BLOCK), 1)
    ).astype(BF16)
    valid = lax.broadcasted_iota(jnp.int32, (BLOCK, LANES), 1) < heads
    for block in range(PAIR):
        at = slice(block * BLOCK, (block + 1) * BLOCK)
        here = jnp.where(valid, step[at], 1.0)
        parts = halves(here * rate, 3)
        cum = dot(lower, parts[0]) + (dot(lower, parts[1]) + dot(lower, parts[2]))
        cum = cum * LOG2E
        cum_ref[at] = cum
        row_ref[:, at] = jnp.transpose(cum - jnp.log2(here))
        factor_ref[at] = jnp.concatenate(halves(jnp.exp2(cum), 2), 1)
        tail = jnp.exp2(cum[BLOCK - 1 :] - cum) * here
        tail_ref[at] = jnp.concatenate(halves(tail, 2), 1)


def score_kernel(shards, place, *refs):
    blocks, refs = refs[:shards], refs[shards:]
    taps, offset, edge_ref, b_ref, c_ref, score_ref, wide = (*refs[:4], *refs[-3:])
    blocks = view(blocks, 3)
    start = WIDTHS[3]
    at = slice(PER_GROUP + STATE, PER_GROUP + 2 * STATE)

    def put(start, count, value):
        c_ref[start : start + count] = value

    convolve_in_order(
        place, blocks, slice(start, start + STATE), edge_ref[0:3, at], taps[:, at], offset[:, at], wide, put
    )
    for block in range(PAIR):
        at = slice(block * BLOCK, (block + 1) * BLOCK)
        score_ref[at] = lax.dot_general(
            c_ref[at], b_ref[at], (((1,), (1,)), ((), ())), preferred_element_type=F32
        )


def decay_of(ref):
    decay = ref[STATE : STATE + 16].astype(F32)
    return decay[0:1] + (decay[1:2] + decay[2:3])


def put_decay(ref, decay):
    row = lax.broadcasted_iota(jnp.int32, (16, ref.shape[1]), 0)
    high, middle, low = (part.astype(F32) for part in halves(decay, 3))
    packed = jnp.where(row == 0, high, jnp.where(row == 1, middle, jnp.where(row == 2, low, 0.0)))
    ref[STATE:] = packed.astype(BF16)


def state_kernel(shards, part, sizes, place, *refs):
    blocks, refs = refs[:shards], refs[shards:]
    taps, offset, edge_ref, b_ref, factor_ref, tail_ref = refs[:6]
    x_ref, own_ref, *sends, wide = refs[-3 - len(sizes) :]
    piece, start, width = part
    first = sum(WIDTHS[:piece]) + start
    at = slice(first, first + width)

    def put(row, count, value):
        x_ref[row : row + count] = value

    blocks = view(blocks, piece)
    columns = slice(start, start + width)
    convolve_in_order(place, blocks, columns, edge_ref[0:3, at], taps[:, at], offset[:, at], wide, put)
    expand = spread(first // HEAD_DIM, width, 2)
    both = []
    for block in range(PAIR):
        at = slice(block * BLOCK, (block + 1) * BLOCK)
        loaded = (x_ref[at].astype(F32) * dot(tail_ref[at], expand)).astype(BF16)
        both.append(
            lax.dot_general(b_ref[at], loaded, (((0,), (0,)), ((), ())), preferred_element_type=F32)
        )
    ends = [dot(factor_ref[(i + 1) * BLOCK - 16 : (i + 1) * BLOCK], expand)[15:16] for i in range(PAIR)]
    own_ref[...] = both[0]
    end = (ends[1] * both[0] + both[1]).astype(BF16)
    decay = ends[0] * ends[1]
    start = 0
    for send_ref in sends:
        at = slice(start, start + send_ref.shape[1])
        send_ref[0:STATE] = end[:, at]
        put_decay(send_ref, decay[:, at])
        start = at.stop


def combine_kernel(spans, place, *refs):
    count = len(spans)
    got, own, out_ref = refs[:count], refs[count : 2 * count], refs[-1]
    odd = place[1] % 2 == 1
    start = 0
    for got_ref, own_ref, span in zip(got, own, spans):
        at = slice(start, start + span.stop - span.start)
        theirs, mine = got_ref[:STATE, span].astype(F32), own_ref[:STATE, span].astype(F32)
        decay, other = decay_of(own_ref.at[:, span]), decay_of(got_ref.at[:, span])
        total = jnp.where(odd, decay, 1.0) * theirs + jnp.where(odd, 1.0, other) * mine
        out_ref[:STATE, at] = total.astype(BF16)
        put_decay(out_ref.at[:, at], decay * other)
        start = at.stop


def mix(first_head, x_ref, cum_ref, row_ref, score_ref, skip_ref, put):
    width = x_ref.shape[1]
    half = BLOCK // 2
    expand = spread(first_head, width, 3)
    skip = dot(skip_ref[...], expand)[0:1]
    lower = lax.broadcasted_iota(jnp.int32, (half, half), 0) >= lax.broadcasted_iota(
        jnp.int32, (half, half), 1
    )
    lane = lax.broadcasted_iota(jnp.int32, (BLOCK, LANES), 1)
    for block in range(PAIR):
        base = block * BLOCK
        for tile in range(width // LANES):
            columns = slice(tile * LANES, (tile + 1) * LANES)
            x = x_ref[base : base + BLOCK, columns]
            top = skip[:, columns] * x[:half].astype(F32)
            bottom = skip[:, columns] * x[half:].astype(F32)
            for side in range(LANES // HEAD_DIM):
                head = first_head + tile * (LANES // HEAD_DIM) + side
                own = jnp.where(lane // HEAD_DIM == side, x, jnp.zeros_like(x))
                cum = cum_ref[base : base + BLOCK, head : head + 1]
                row = row_ref[head : head + 1, base : base + BLOCK]
                diag = jnp.where(lower, cum[:half] - row[:, :half], -1e30)
                mixing = jnp.exp2(diag) * score_ref[base : base + half, :half]
                top = top + dot(mixing.astype(BF16), own[:half])
                left = jnp.exp2(cum[half:] - row[:, :half]) * score_ref[base + half : base + BLOCK, :half]
                diag = jnp.where(lower, cum[half:] - row[:, half:], -1e30)
                right = jnp.exp2(diag) * score_ref[base + half : base + BLOCK, half:]
                mixing = jnp.concatenate([left.astype(BF16), right.astype(BF16)], 1)
                bottom = bottom + dot(mixing, own)
            put(block, slice(base, base + half), columns, top)
            put(block, slice(base + half, base + BLOCK), columns, bottom)


def local_kernel(first_head, x_ref, cum_ref, row_ref, score_ref, skip_ref, *refs):
    out_ref = refs[-1]

    def put(block, rows, columns, value):
        out_ref[rows, columns] = value

    mix(first_head, x_ref, cum_ref, row_ref, score_ref, skip_ref, put)


def carry(first_head, place, lasts, befores, own_ref, c_ref, factor_ref, add, keep_ref, send_ref):
    expand = spread(first_head, own_ref.shape[1], 2)
    last, before = (
        refs[0][...] if len(refs) == 1 else jnp.concatenate([ref[...] for ref in refs], 1)
        for refs in (lasts, befores)
    )
    odd, core = place[1] % 2 == 1, place[2]
    near = jnp.where(odd, last[:STATE].astype(F32), 0.0)
    held = near + jnp.where(odd, decay_of(last), 1.0) * before[:STATE].astype(F32)
    factor = dot(factor_ref[...], expand)
    outs = []
    for block in range(PAIR):
        at = slice(block * BLOCK, (block + 1) * BLOCK)
        carried = dot(c_ref[at], held.astype(BF16))
        outs.append((add[at] + factor[at] * carried).astype(BF16))
        held = factor[BLOCK - 1 : BLOCK] * held + own_ref[...]

    @pl.when(core == 0)
    def _():
        keep_ref[...] = outs[0]
        send_ref[...] = outs[1]

    @pl.when(core == 1)
    def _():
        keep_ref[...] = outs[1]
        send_ref[...] = outs[0]


def final_kernel(first_head, counts, place, *refs):
    groups = []
    for number in counts:
        groups.append(refs[:number])
        refs = refs[number:]
    carry(first_head, place, *groups, *refs[:4], *refs[-2:])


def finish_kernel(first_head, counts, place, *refs):
    groups = []
    for number in counts:
        groups.append(refs[:number])
        refs = refs[number:]
    own_ref, c_ref, factor_ref = refs[:3]
    keep_ref, send_ref, partial = refs[-3:]
    local_kernel(first_head, *refs[3:8], partial)
    carry(first_head, place, *groups, own_ref, c_ref, factor_ref, partial, keep_ref, send_ref)


def place_kernel(firsts, place, *refs):
    count = len(firsts)
    keeps, gots = refs[:count], refs[count : 2 * count]
    out, sems = refs[-2:]
    core = place[2]
    half = out.shape[1] // PAIR
    copies = []
    for first, keep, got in zip(firsts, keeps, gots):
        width = keep.shape[1]
        copies.append((keep, out.at[:, ds(core * half + first, width)]))
        copies.append((got, out.at[:, ds((1 - core) * half + first, width)]))
    for copy in run(copies, sems):
        copy.wait()


def put_in_place(firsts, shape, place, keeps, gots):
    smem, vmem, hbm = (pl.BlockSpec(memory_space=m) for m in (pltpu.SMEM, pltpu.VMEM, pltpu.HBM))
    count = len(firsts)
    return pl.pallas_call(
        functools.partial(place_kernel, firsts),
        out_shape=jax.ShapeDtypeStruct(shape, BF16),
        in_specs=[smem] + [vmem] * (2 * count),
        out_specs=hbm,
        scratch_shapes=[pltpu.SemaphoreType.DMA((2 * count,))],
        compiler_params=pltpu.CompilerParams(vmem_limit_bytes=16 << 20),
        cost_estimate=pl.CostEstimate(flops=1, bytes_accessed=1, transcendentals=0),
        name="place",
    )(place, *keeps, *gots)


class Stay:
    def __init__(self, array):
        self.array = array


def gate(blocks, order):
    anywhere = pl.BlockSpec(memory_space=pl.ANY)
    return pl.pallas_call(
        lambda *refs: None,
        out_shape=[jax.ShapeDtypeStruct(block.shape, block.dtype) for block in blocks],
        in_specs=[anywhere] * (len(blocks) + len(order)),
        out_specs=[anywhere] * len(blocks),
        input_output_aliases={i: i for i in range(len(blocks))},
        compiler_params=pltpu.CompilerParams(vmem_limit_bytes=16 << 20),
        cost_estimate=pl.CostEstimate(flops=1, bytes_accessed=1, transcendentals=0),
        name="gate",
    )(*blocks, *order)


def call(body, outs, operands, scratch=(), flops=0, transcendentals=0, name=None, limit=16 << 20):
    shapes = [jax.ShapeDtypeStruct(shape, dtype) for shape, dtype in outs]
    smem, vmem, hbm = (pl.BlockSpec(memory_space=m) for m in (pltpu.SMEM, pltpu.VMEM, pltpu.HBM))
    specs = [
        hbm if isinstance(o, Stay) else smem if o.dtype == jnp.int32 else vmem for o in operands
    ]
    moved = sum(o.size * o.dtype.itemsize for o in shapes) * 2
    return pl.pallas_call(
        body,
        out_shape=shapes,
        in_specs=specs,
        out_specs=[vmem] * len(outs),
        scratch_shapes=scratch,
        compiler_params=pltpu.CompilerParams(vmem_limit_bytes=limit),
        cost_estimate=pl.CostEstimate(flops=1, bytes_accessed=1, transcendentals=0),
        name=name,
    )(*[o.array if isinstance(o, Stay) else o for o in operands])


def paired(xbc, dt_raw, conv_weight, conv_bias, a_log, dt_bias, skip_gain):
    axes = ("ctx", "head")
    shards, length = lax.axis_size("head"), lax.axis_size("ctx")
    devices, peers = shards * length, shards * PAIR
    tok = xbc.shape[0]
    slab = tok * peers
    context, shard = lax.axis_index("ctx"), lax.axis_index("head")
    pair, core = context // PAIR, context % PAIR
    group = shard * PAIR + core
    place = jnp.stack([group, pair, core, core * shards + shard, shard]).astype(jnp.int32)

    def over(block, target):
        route = [(i, target(i)) for i in range(devices)]
        return lax.ppermute(block, axes, [(i, j) for i, j in route if j is not None and j < devices])

    def swap(block):
        return over(block, lambda i: i ^ shards)

    rows = Stay(xbc)
    size = PER_GROUP + 2 * STATE
    (sent,) = call(
        functools.partial(pack_first_kernel, shards),
        [((tok, shards * WIDTHS[0]), BF16)],
        [place, rows],
        scratch=[pltpu.SemaphoreType.DMA((shards,))],
        name="pack_first",
    )
    got_first = swap(sent)
    sent, tail = call(
        functools.partial(pack_kernel, shards),
        [((tok, shards * (size - WIDTHS[0]) + HEADS), BF16), ((16, shards * size), BF16)],
        [place, rows, Stay(dt_raw), Stay(sent)],
        scratch=[pltpu.SemaphoreType.DMA((6 * shards + 1,))],
        name="pack",
    )
    got_rest = swap(gate([sent], [got_first])[0])
    taps, offset = call(
        taps_kernel,
        [((4, size), F32), ((1, size), F32)],
        [place, Stay(conv_weight), Stay(conv_bias[None]), Stay(got_rest)],
        scratch=[pltpu.SemaphoreType.DMA((6,))],
        name="taps",
    )

    def send_on(plan, order, edges=None):
        unused = Stay(got_first)
        parts = [p for _, pieces in plan for p in pieces]
        return call(
            functools.partial(merge_kernel, shards, plan, len(order)),
            [((PAIR * tok, sum(map(total_of, pieces))), BF16) for _, pieces in plan],
            [
                place,
                rows,
                Stay(dt_raw) if edges is None else dt_raw,
                got_first if 0 in parts else unused,
                got_rest if any(parts) else unused,
                unused if edges is None else edges,
            ]
            + [Stay(o) for o in order],
            scratch=[pltpu.SemaphoreType.DMA((sum(2 + 2 * len(RESTS[p]) for p in parts),))],
            name="merge",
        )

    def travel(blocks):
        return [blocks[0]] + [over(blocks[r], lambda i, r=r: i ^ FLIP[r]) for r in range(1, shards)]

    def plan(piece):
        return [(r, (piece,)) for r in range(shards)]

    first_blocks = send_on(plan(0), [])
    message = [travel(first_blocks)]
    (edges,) = call(
        functools.partial(edge_kernel, shards),
        [((3, shards * size), BF16)],
        [place, got_first, got_rest, tail],
        name="edge",
    )
    edges = over(edges, lambda i: i + peers if i % shards == shards - 1 else None)
    second_blocks = send_on(plan(1), [first_blocks[0]], edges)
    message.append(travel(second_blocks))
    third_plan = [(r, (2, 3) if r == NEAR else (2,)) for r in range(shards)]
    third_blocks = send_on(third_plan, [second_blocks[0]])
    message.append(travel(third_blocks[:1] + gate(third_blocks[1:], message[0][1:] + message[1][1:] + [taps])))

    def seen(piece):
        return message[piece]

    tiles = [p.reshape(HEADS // LANES, LANES) for p in (a_log, dt_bias, skip_gain)]
    b, edge, cum, row, factor, tail, skip = call(
        functools.partial(prep_kernel, shards),
        [
            ((slab, STATE), BF16),
            ((4, size), F32),
            ((slab, LANES), F32),
            ((LANES, slab), F32),
            ((slab, 2 * LANES), BF16),
            ((slab, 2 * LANES), BF16),
            ((16, 3 * LANES), BF16),
        ],
        [place] + seen(1) + [taps, offset] + tiles + [Stay(third_blocks[0])],
        scratch=[pltpu.VMEM((slab, LANES), F32), pltpu.VMEM((slab + 8, STATE), F32)],
        name="prep",
    )
    count = len(GROUPED)
    x, sent, own, last, joined, before, keep, send = ([None] * count for _ in range(8))

    def first_head(i):
        return (sum(WIDTHS[: GROUPED[i][0]]) + GROUPED[i][1]) // HEAD_DIM

    def state_of(i, order):
        piece, _, width = GROUPED[i]
        x[i], own[i], *sent[i] = call(
            functools.partial(state_kernel, shards, GROUPED[i], FIRST_ROUND[i]),
            [((slab, width), BF16), ((STATE, width), F32)] + [((STATE + 16, w), BF16) for w in FIRST_ROUND[i]],
            [place] + seen(piece) + [taps, offset, edge, b, factor, tail] + [Stay(o) for o in order],
            scratch=[pltpu.VMEM((slab + 8, width), F32)],
            name="state",
        )
        last[i] = [over(part, lambda i: i ^ peers if i // peers != 3 else None) for part in sent[i]]

    def combine_of(i, order):
        joined[i], before[i] = [], []
        end = 0
        for width in SECOND_ROUND[i]:
            begin, end = end, end + width
            early, late, spans, first = [], [], [], 0
            for got, mine, size_of in zip(last[i], sent[i], FIRST_ROUND[i]):
                low, high = max(begin - first, 0), min(end - first, size_of)
                first += size_of
                if low < high:
                    early.append(got)
                    late.append(mine)
                    spans.append(slice(low, high))
            (total,) = call(
                functools.partial(combine_kernel, spans),
                [((STATE + 16, width), BF16)],
                [place] + early + late + [Stay(o) for o in order],
                name="combine",
            )
            joined[i].append(total)
            before[i].append(over(total, lambda i: i + 2 * peers))
            order = [total]

    def finish_of(body, i, operands, order, **more):
        keep[i], send[i] = call(
            functools.partial(body, first_head(i), (len(last[i]), len(before[i]))),
            [((BLOCK, GROUPED[i][2]), BF16)] * 2,
            [place, *last[i], *before[i], own[i], c, factor] + operands + [Stay(o) for o in order],
            name="final",
            **more,
        )

    partial = [None] * count

    def local_of(i, order):
        (partial[i],) = call(
            functools.partial(local_kernel, first_head(i)),
            [(x[i].shape, F32)],
            [x[i], cum, row, score, skip] + [Stay(o) for o in order],
            name="local",
        )

    state_of(0, [])
    own_block, *fourth_blocks = send_on([(r, (3,)) for r in range(shards) if r != NEAR], sent[0])
    fourth_blocks = gate(fourth_blocks, message[2][1:])
    fourth_blocks = [over(block, lambda i, r=r: i ^ FLIP[r]) for r, block in enumerate(fourth_blocks, 1)]
    message.append([own_block, *fourth_blocks, message[2][NEAR]])
    combine_of(0, [own_block])
    state_of(1, joined[0])
    combine_of(1, [])
    state_of(2, joined[1])
    state_of(3, sent[2])
    c, score = call(
        functools.partial(score_kernel, shards),
        [((slab, STATE), BF16), ((slab, BLOCK), F32)],
        [place] + seen(3) + [taps, offset, edge, b] + [Stay(o) for o in sent[3]],
        scratch=[pltpu.VMEM((slab + 8, STATE), F32)],
        name="score",
    )
    local_of(0, [score])

    def in_full(i, order):
        wide = [pltpu.VMEM((slab, GROUPED[i][2]), F32)]
        finish_of(finish_kernel, i, [x[i], cum, row, score, skip], order, scratch=wide)

    combine_of(2, [partial[0]] + before[1] + before[0])
    in_full(1, joined[2])
    combine_of(3, [keep[1]])
    local_of(2, joined[3])
    local_of(3, [partial[2]])
    finish_of(final_kernel, 0, [partial[0]], [partial[3]])
    finish_of(final_kernel, 2, [partial[2]], [keep[0]])
    finish_of(final_kernel, 3, [partial[3]], [keep[2]])
    firsts = [first_head(i) * HEAD_DIM for i in range(count)]
    return put_in_place(firsts, (BLOCK, PAIR * PER_GROUP), place, keep, [swap(o) for o in send])


def solution(mesh):
    in_specs = (P(("ctx", "head"), None), P(("ctx", "head"), None), P(), P(), P(), P(), P())
    out_specs = P("ctx", "head")
    shards, length = mesh.shape["head"], mesh.shape["ctx"]

    def program(xbc, *rest):
        slab = xbc.shape[0] // length
        fits = shards == GROUPS // PAIR and length == 4 * PAIR and slab == BLOCK
        return jax.shard_map(
            paired if fits else on_device,
            mesh=mesh,
            in_specs=in_specs,
            out_specs=out_specs,
            check_vma=False,
        )(xbc, *rest)

    return program
```

```python
import functools

import jax
import jax.numpy as jnp
from jax import lax
from jax.experimental import pallas as pl
from jax.experimental.pallas import tpu as pltpu
from jax.sharding import PartitionSpec as P

HEADS = 256
HEAD_DIM = 64
STATE = 256
GROUPS = 8
BLOCK = 256


def from_behind(block, axis, distance):
    devices = range(lax.axis_size(axis))
    route = [(i - distance, i) for i in devices if i - distance in devices]
    return lax.ppermute(block, axis, route)


def carried_in(array, axis, combine, identity):
    length, index = (lax.axis_size(axis), lax.axis_index(axis))
    everything = jax.tree.map(lambda part: lax.all_gather(part, axis), array)
    start = jax.tree.map(
        lambda part, zero: jnp.broadcast_to(jnp.asarray(zero, part.dtype), part.shape),
        array,
        identity,
    )

    def hop(k, before):
        reached = k < index
        new = combine(before, jax.tree.map(lambda part: part[k], everything))
        return jax.tree.map(lambda a, b: jnp.where(reached, a, b), new, before)

    return lax.fori_loop(0, length, hop, start)


def convolve(rows, edge, weight, bias):
    count = rows.shape[0]
    wide = jnp.concatenate([edge, rows], 0).astype(jnp.float32)
    acc = bias[None, :] + weight[0] * wide[0:count]
    acc = acc + weight[1] * wide[1 : count + 1]
    acc = acc + weight[2] * wide[2 : count + 2]
    acc = acc + weight[3] * wide[3 : count + 3]
    return jax.nn.silu(acc).astype(jnp.bfloat16)


def rearrange_heads(rows, shards, per_dev, groups_dev, per_group):
    count = rows.shape[0]
    inner = HEADS * HEAD_DIM
    replicate_groups = max(1, per_group // per_dev)
    heads_part = rows[:, :inner].reshape(count, shards, per_dev * HEAD_DIM)
    b_part = rows[:, inner : inner + GROUPS * STATE].reshape(count, GROUPS, STATE)
    c_part = rows[:, inner + GROUPS * STATE :].reshape(count, GROUPS, STATE)
    b_part = jnp.repeat(b_part, replicate_groups, axis=1).reshape(count, shards, groups_dev * STATE)
    c_part = jnp.repeat(c_part, replicate_groups, axis=1).reshape(count, shards, groups_dev * STATE)
    return jnp.concatenate([heads_part, b_part, c_part], axis=2)


def inner_block(xs, bmat, cmat, steps, cum):
    size = xs.shape[0]
    lower = jnp.arange(size)[:, None] >= jnp.arange(size)[None, :]
    scores = jnp.einsum("qgn,kgn->gqk", cmat, bmat, preferred_element_type=jnp.float32)
    order = jnp.transpose(cum, (1, 2, 0))
    gap = order[..., :, None] - order[..., None, :]
    decay = jnp.exp(jnp.where(lower, gap, -jnp.inf))
    mixing = (scores[:, None] * decay * jnp.transpose(steps, (1, 2, 0))[..., None, :]).astype(
        jnp.bfloat16
    )
    local = jnp.einsum("gjqk,kgjp->qgjp", mixing, xs, preferred_element_type=jnp.float32)
    tail = jnp.exp(cum[size - 1][None] - cum) * steps
    loaded = (bmat[:, :, None, :].astype(jnp.float32) * tail[..., None]).astype(jnp.bfloat16)
    block_state = jnp.einsum("kgjn,kgjp->gjnp", loaded, xs, preferred_element_type=jnp.float32)
    return (local, block_state)


def on_device(xbc, dt_raw, conv_weight, conv_bias, a_log, dt_bias, skip_gain):
    tok = xbc.shape[0]
    shards = lax.axis_size("head")
    per_dev = HEADS // shards
    per_group = HEADS // GROUPS
    groups_dev = max(1, per_dev // per_group)
    heads_per_cluster = per_dev // groups_dev
    sent = rearrange_heads(xbc, shards, per_dev, groups_dev, per_group)
    mine, rates = (
        lax.all_to_all(sent, "head", split_axis=1, concat_axis=0, tiled=True),
        lax.all_to_all(
            dt_raw.reshape(tok, shards, per_dev), "head", split_axis=1, concat_axis=0, tiled=True
        ),
    )
    slab = tok * shards
    mine = mine.reshape(slab, mine.shape[2])
    rates = rates.reshape(slab, per_dev)
    shard = lax.axis_index("head")
    taps = lax.dynamic_index_in_dim(
        rearrange_heads(conv_weight, shards, per_dev, groups_dev, per_group),
        shard,
        1,
        keepdims=False,
    )
    offset = lax.dynamic_index_in_dim(
        rearrange_heads(conv_bias[None, :], shards, per_dev, groups_dev, per_group),
        shard,
        1,
        keepdims=False,
    )
    edge = from_behind(mine[slab - 3 :], "ctx", 1)
    mine = convolve(mine, edge, taps, offset[0])
    nchunk = slab // BLOCK
    width = per_dev * HEAD_DIM
    xs = mine[:, :width].reshape(nchunk, BLOCK, groups_dev, heads_per_cluster, HEAD_DIM)
    bmat = mine[:, width : width + groups_dev * STATE].reshape(nchunk, BLOCK, groups_dev, STATE)
    cmat = mine[:, width + groups_dev * STATE :].reshape(nchunk, BLOCK, groups_dev, STATE)
    first = shard * per_dev
    rate = (-jnp.exp(lax.dynamic_slice_in_dim(a_log, first, per_dev))).reshape(
        groups_dev, heads_per_cluster
    )
    bias_dt = lax.dynamic_slice_in_dim(dt_bias, first, per_dev).reshape(
        groups_dev, heads_per_cluster
    )
    skip = lax.dynamic_slice_in_dim(skip_gain, first, per_dev).reshape(
        groups_dev, heads_per_cluster
    )
    steps = jax.nn.softplus(
        rates.astype(jnp.float32).reshape(nchunk, BLOCK, groups_dev, heads_per_cluster) + bias_dt
    )
    cum = jnp.cumsum(steps * rate, axis=1)

    def block_step(carry, item):
        held, product = carry
        x_part, b_part, c_part, step_part, cum_part = item
        local, block_state = inner_block(x_part, b_part, c_part, step_part, cum_part)
        lifted = c_part.astype(jnp.float32)[:, :, None, :] * jnp.exp(cum_part)[..., None]
        carried = jnp.einsum("qgjn,gjnp->qgjp", lifted, held, precision=lax.Precision.HIGHEST)
        partial_out = local + carried + skip[..., None] * x_part.astype(jnp.float32)
        end = jnp.exp(cum_part[BLOCK - 1])
        return ((end[..., None, None] * held + block_state, product * end), (partial_out, product))

    zero_state = jnp.zeros((groups_dev, heads_per_cluster, STATE, HEAD_DIM), jnp.float32)
    unit = jnp.ones((groups_dev, heads_per_cluster), jnp.float32)
    (slab_state, slab_decay), (partials, product_in) = lax.scan(
        block_step, (zero_state, unit), (xs, bmat, cmat, steps, cum)
    )

    def combine(preceding_state, later):
        return (
            preceding_state[0] * later[0],
            later[0][..., None, None] * preceding_state[1] + later[1],
        )

    _, entering = carried_in((slab_decay, slab_state), "ctx", combine, (unit, zero_state))
    projected = jnp.einsum(
        "cqgn,gjnp->cqgjp", cmat.astype(jnp.float32), entering, precision=lax.Precision.HIGHEST
    )
    factor = jnp.exp(cum) * product_in[:, None]
    total = partials + factor[..., None] * projected
    return total.astype(jnp.bfloat16).reshape(slab, width)


PAIR = 2
LANES = 128
LOG2E = 1.4426950408889634
F32, BF16 = jnp.float32, jnp.bfloat16
WIDTHS = (512, 0, 768, 768)
RESTS = ("", "BD", "", "C")
GROUPED = ((0, 0, 512), (2, 0, 768), (3, 0, 384), (3, 384, 384))
FIRST_ROUND = ((256, 256), (384, 384), (384,), (384,))
SECOND_ROUND = ((512,), (384, 384), (384,), (384,))


FLIP = (0, 2, 3, 1)
NEAR = 3


def halves(value, count):
    parts = []
    for _ in range(count):
        part = value.astype(BF16)
        parts.append(part)
        value = value - part.astype(F32)
    return parts


def spread(first_head, width, copies):
    lane = lax.broadcasted_iota(jnp.int32, (copies * LANES, width), 0) % LANES
    column = lax.broadcasted_iota(jnp.int32, (copies * LANES, width), 1)
    return (lane == first_head + column // HEAD_DIM).astype(BF16)


def dot(a, b):
    return jnp.dot(a, b, preferred_element_type=F32)


def ds(start, width):
    return pl.ds(pl.multiple_of(start, LANES), width)


def run(copies, sems):
    started = []
    for i, (source, target) in enumerate(copies):
        copy = pltpu.make_async_copy(source, target, sems.at[i])
        copy.start()
        started.append(copy)
    return started


PER_GROUP = HEADS * HEAD_DIM // GROUPS
INNER = HEADS * HEAD_DIM


def channels(group, first, width):
    return ds(group * PER_GROUP + first, width)


def pack_first_kernel(shards, place, xbc, send, sems):
    core, shard = place[2], place[4]
    width = WIDTHS[0]
    copies = []
    for r in range(shards):
        group = (shard ^ FLIP[r]) * PAIR + 1 - core
        copies.append((xbc.at[:, channels(group, 0, width)], send.at[:, r * width : (r + 1) * width]))
    for copy in run(copies, sems):
        copy.wait()


def pack_kernel(shards, place, xbc, dt_raw, order, send, tail, sems):
    core, shard = place[2], place[4]
    count = xbc.shape[0]
    first = WIDTHS[0]
    width = PER_GROUP - first
    rest = width * shards
    size = PER_GROUP + 2 * STATE
    copies = []
    for r in range(shards):
        group = (shard ^ FLIP[r]) * PAIR + 1 - core
        copies.append((xbc.at[:, channels(group, first, width)], send.at[:, r * width : (r + 1) * width]))
        for i in range(2):
            to = rest + (i * shards + r) * STATE
            copies.append((xbc.at[:, ds(INNER + (i * GROUPS + group) * STATE, STATE)], send.at[:, to : to + STATE]))
    copies.append((dt_raw, send.at[:, send.shape[1] - HEADS :]))
    for r in range(shards):
        group, to = (shard ^ FLIP[r]) * PAIR + core, r * size
        last = xbc.at[count - 16 :]
        copies.append((last.at[:, channels(group, 0, PER_GROUP)], tail.at[:, to : to + PER_GROUP]))
        for i in range(2):
            at = ds(INNER + (i * GROUPS + group) * STATE, STATE)
            start = to + PER_GROUP + i * STATE
            copies.append((last.at[:, at], tail.at[:, start : start + STATE]))
    for copy in run(copies, sems):
        copy.wait()


def taps_kernel(place, weight, bias, order, taps, offset, sems):
    copies = []
    for source, target in ((weight, taps), (bias, offset)):
        copies.append((source.at[:, channels(place[0], 0, PER_GROUP)], target.at[:, :PER_GROUP]))
        for i in range(2):
            at = ds(INNER + (i * GROUPS + place[0]) * STATE, STATE)
            start = PER_GROUP + i * STATE
            copies.append((source.at[:, at], target.at[:, start : start + STATE]))
    for copy in run(copies, sems):
        copy.wait()


def edge_kernel(shards, place, got_first, got, tail, out):
    count = got.shape[0]
    first = WIDTHS[0]
    width = PER_GROUP - first
    size = PER_GROUP + 2 * STATE
    for r in range(shards):
        theirs = [(got_first, r * first, first), (got, r * width, width)]
        theirs += [(got, width * shards + (i * shards + r) * STATE, STATE) for i in range(2)]
        to = r * size
        for ref, start, size_of in theirs:
            a = ref[count - 16 :, start : start + size_of].astype(F32)
            b = tail[:, to : to + size_of].astype(F32)
            out[:, to : to + size_of] = jnp.where(place[2] == 0, a, b)[13:16].astype(BF16)
            to += size_of


def total_of(piece):
    return WIDTHS[piece] + sum(LANES if kind == "D" else STATE for kind in RESTS[piece])


def merge_kernel(shards, plan, unread, place, xbc, dt_raw, got_first, got, edges, *refs):
    refs = refs[unread:]
    outs, sems = refs[: len(plan)], refs[-1]
    core, shard = place[2], place[4]
    count = xbc.shape[0]
    stride = PER_GROUP - WIDTHS[0]
    mine = pl.ds(pl.multiple_of(core * count, count), count)
    other = pl.ds(pl.multiple_of((1 - core) * count, count), count)
    copies, steps = [], []
    for out, (r, pieces) in zip(outs, plan):
        group = (shard ^ FLIP[r]) * PAIR + core
        to = 0
        for piece in pieces:
            first, width = sum(WIDTHS[:piece]), WIDTHS[piece]
            if piece == 0:
                source = got_first.at[:, r * width : (r + 1) * width]
            else:
                at = r * stride + first - WIDTHS[0]
                source = got.at[:, at : at + width]
            if width:
                copies.append((xbc.at[:, channels(group, first, width)], out.at[mine, to : to + width]))
                copies.append((source, out.at[other, to : to + width]))
            to += width
            for kind in RESTS[piece]:
                if kind == "D":
                    steps.append((out, r, to))
                    to += LANES
                    continue
                i = "BC".index(kind)
                at = ds(INNER + (i * GROUPS + group) * STATE, STATE)
                copies.append((xbc.at[:, at], out.at[mine, to : to + STATE]))
                at = stride * shards + (i * shards + r) * STATE
                copies.append((got.at[:, at : at + STATE], out.at[other, to : to + STATE]))
                to += STATE
    started = run(copies, sems)
    if steps:
        lane = lax.broadcasted_iota(jnp.int32, (count, LANES), 1)
        per_tile = LANES * GROUPS // HEADS
        heads = HEADS // GROUPS
        for out, r, to in steps:
            group = (shard ^ FLIP[r]) * PAIR + core
            tile, shift = group // per_tile, (LANES - (group % per_tile) * heads) % LANES
            own = dt_raw[:, ds(tile * LANES, LANES)].astype(F32)
            theirs = got[:, ds(got.shape[1] - HEADS + tile * LANES, LANES)].astype(F32)
            low = jnp.where(core == 0, own, theirs)
            high = jnp.where(core == 0, theirs, own)
            packed = jnp.zeros((count // 2, LANES), F32)
            for j, rows in enumerate((low, high)):
                rows = jnp.where(lane < heads, pltpu.roll(rows, shift, 1), 0.0)
                for i in range(2):
                    part = rows[i * count // 2 : (i + 1) * count // 2]
                    packed = packed + pltpu.roll(part, (2 * j + i) * heads, 1)
            out[: count // 2, to : to + LANES] = packed.astype(BF16)
            size = PER_GROUP + 2 * STATE
            at = slice(r * size, (r + 1) * size)
            edge = jnp.concatenate([edges[:, at].astype(F32), jnp.zeros((1, size), F32)], 0)
            edge = jnp.concatenate([edge[:, q * LANES : (q + 1) * LANES] for q in range(size // LANES)], 0)
            fill = jnp.zeros((PAIR * count - count // 2 - edge.shape[0], LANES), F32)
            out[count // 2 :, to : to + LANES] = jnp.concatenate([edge, fill], 0).astype(BF16)
    for copy in started:
        copy.wait()


def view(refs, piece):
    return [(ref, total_of(2) if piece == 3 and r == NEAR else 0) for r, ref in enumerate(refs)]


def convolve_in_order(place, blocks, columns, edge, tap, bias, wide, put):
    width = columns.stop - columns.start
    count = blocks[0][0].shape[0] // PAIR
    wide[5:8, :width] = edge
    for r, (block, origin) in enumerate(blocks):
        for core in range(PAIR):
            at = pl.multiple_of((core * len(blocks) + (place[4] ^ FLIP[r])) * count + 8, 8)
            part = block[core * count : (core + 1) * count, origin + columns.start : origin + columns.stop]
            wide[pl.ds(at, count), :width] = part.astype(F32)
    tap, bias = tap * 0.5, bias * 0.5
    for start in range(0, PAIR * len(blocks) * count, count):
        acc = bias + tap[0:1] * wide[start + 5 : start + 5 + count, :width]
        acc = acc + tap[1:2] * wide[start + 6 : start + 6 + count, :width]
        acc = acc + tap[2:3] * wide[start + 7 : start + 7 + count, :width]
        acc = acc + tap[3:4] * wide[start + 8 : start + 8 + count, :width]
        put(start, count, (acc + acc * jnp.tanh(acc)).astype(BF16))


def prep_kernel(shards, place, *refs):
    blocks, (taps, offset, a_ref, bias_ref, skip_ref, order) = refs[:shards], refs[shards : shards + 6]
    b_ref, edge_ref, cum_ref, row_ref, factor_ref, tail_ref, skip_out, dt_ref, wide = refs[shards + 6 :]
    blocks = view(blocks, 1)
    start = WIDTHS[1]
    last = total_of(1) - LANES
    size = edge_ref.shape[1]
    count = blocks[0][0].shape[0] // PAIR
    half, heads = count // 2, HEADS // GROUPS
    columns = [block[:, origin + last : origin + last + LANES].astype(F32) for block, origin in blocks]
    edge = columns[0][half : half + 4 * size // LANES]
    for column in columns[1:]:
        edge = edge + column[half : half + 4 * size // LANES]
    for q in range(size // LANES):
        edge_ref[:, q * LANES : (q + 1) * LANES] = edge[4 * q : 4 * q + 4]
    for r, column in enumerate(columns):
        packed = column[:half]
        for j in range(2 * PAIR):
            at = ((j // 2) * shards + (place[4] ^ FLIP[r])) * count + (j % 2) * half
            rows = packed if j == 0 else pltpu.roll(packed, LANES - j * heads, 1)
            dt_ref[pl.ds(pl.multiple_of(at, half), half), :] = rows

    def put(start, count, value):
        b_ref[start : start + count] = value

    at = slice(PER_GROUP, PER_GROUP + STATE)
    convolve_in_order(
        place, blocks, slice(start, start + STATE), edge_ref[0:3, at], taps[:, at], offset[:, at], wide, put
    )
    per_tile = LANES * GROUPS // HEADS
    group = place[0]
    tile = group // per_tile
    shift = (LANES - (group % per_tile) * heads) % LANES

    def lanes_of(ref):
        return pltpu.roll(jnp.broadcast_to(ref[pl.ds(tile, 1), :], (8, LANES)), shift, 1)

    rate = -jnp.exp(lanes_of(a_ref)[0:1])
    raw = dt_ref[...] + lanes_of(bias_ref)[0:1]
    step = jnp.maximum(raw, 0.0) + jnp.log1p(jnp.exp(-jnp.abs(raw)))
    skip = lanes_of(skip_ref)
    skip_out[...] = jnp.concatenate(halves(jnp.concatenate([skip, skip], 0), 3), 1)
    lower = (
        lax.broadcasted_iota(jnp.int32, (BLOCK, BLOCK), 0)
        >= lax.broadcasted_iota(jnp.int32, (BLOCK, BLOCK), 1)
    ).astype(BF16)
    valid = lax.broadcasted_iota(jnp.int32, (BLOCK, LANES), 1) < heads
    for block in range(PAIR):
        at = slice(block * BLOCK, (block + 1) * BLOCK)
        here = jnp.where(valid, step[at], 1.0)
        parts = halves(here * rate, 3)
        cum = dot(lower, parts[0]) + (dot(lower, parts[1]) + dot(lower, parts[2]))
        cum = cum * LOG2E
        cum_ref[at] = cum
        row_ref[:, at] = jnp.transpose(cum - jnp.log2(here))
        factor_ref[at] = jnp.concatenate(halves(jnp.exp2(cum), 2), 1)
        tail = jnp.exp2(cum[BLOCK - 1 :] - cum) * here
        tail_ref[at] = jnp.concatenate(halves(tail, 2), 1)


def score_kernel(shards, place, *refs):
    blocks, refs = refs[:shards], refs[shards:]
    taps, offset, edge_ref, b_ref, c_ref, score_ref, wide = (*refs[:4], *refs[-3:])
    blocks = view(blocks, 3)
    start = WIDTHS[3]
    at = slice(PER_GROUP + STATE, PER_GROUP + 2 * STATE)

    def put(start, count, value):
        c_ref[start : start + count] = value

    convolve_in_order(
        place, blocks, slice(start, start + STATE), edge_ref[0:3, at], taps[:, at], offset[:, at], wide, put
    )
    for block in range(PAIR):
        at = slice(block * BLOCK, (block + 1) * BLOCK)
        score_ref[at] = lax.dot_general(
            c_ref[at], b_ref[at], (((1,), (1,)), ((), ())), preferred_element_type=F32
        )


def decay_of(ref):
    decay = ref[STATE : STATE + 16].astype(F32)
    return decay[0:1] + (decay[1:2] + decay[2:3])


def put_decay(ref, decay):
    row = lax.broadcasted_iota(jnp.int32, (16, ref.shape[1]), 0)
    high, middle, low = (part.astype(F32) for part in halves(decay, 3))
    packed = jnp.where(row == 0, high, jnp.where(row == 1, middle, jnp.where(row == 2, low, 0.0)))
    ref[STATE:] = packed.astype(BF16)


def state_kernel(shards, part, sizes, place, *refs):
    blocks, refs = refs[:shards], refs[shards:]
    taps, offset, edge_ref, b_ref, factor_ref, tail_ref = refs[:6]
    x_ref, own_ref, *sends, wide = refs[-3 - len(sizes) :]
    piece, start, width = part
    first = sum(WIDTHS[:piece]) + start
    at = slice(first, first + width)

    def put(row, count, value):
        x_ref[row : row + count] = value

    blocks = view(blocks, piece)
    columns = slice(start, start + width)
    convolve_in_order(place, blocks, columns, edge_ref[0:3, at], taps[:, at], offset[:, at], wide, put)
    expand = spread(first // HEAD_DIM, width, 2)
    both = []
    for block in range(PAIR):
        at = slice(block * BLOCK, (block + 1) * BLOCK)
        loaded = (x_ref[at].astype(F32) * dot(tail_ref[at], expand)).astype(BF16)
        both.append(
            lax.dot_general(b_ref[at], loaded, (((0,), (0,)), ((), ())), preferred_element_type=F32)
        )
    ends = [dot(factor_ref[(i + 1) * BLOCK - 16 : (i + 1) * BLOCK], expand)[15:16] for i in range(PAIR)]
    own_ref[...] = both[0]
    end = (ends[1] * both[0] + both[1]).astype(BF16)
    decay = ends[0] * ends[1]
    start = 0
    for send_ref in sends:
        at = slice(start, start + send_ref.shape[1])
        send_ref[0:STATE] = end[:, at]
        put_decay(send_ref, decay[:, at])
        start = at.stop


def combine_kernel(spans, place, *refs):
    count = len(spans)
    got, own, out_ref = refs[:count], refs[count : 2 * count], refs[-1]
    odd = place[1] % 2 == 1
    start = 0
    for got_ref, own_ref, span in zip(got, own, spans):
        at = slice(start, start + span.stop - span.start)
        theirs, mine = got_ref[:STATE, span].astype(F32), own_ref[:STATE, span].astype(F32)
        decay, other = decay_of(own_ref.at[:, span]), decay_of(got_ref.at[:, span])
        total = jnp.where(odd, decay, 1.0) * theirs + jnp.where(odd, 1.0, other) * mine
        out_ref[:STATE, at] = total.astype(BF16)
        put_decay(out_ref.at[:, at], decay * other)
        start = at.stop


def mix(first_head, x_ref, cum_ref, row_ref, score_ref, skip_ref, put):
    width = x_ref.shape[1]
    half = BLOCK // 2
    expand = spread(first_head, width, 3)
    skip = dot(skip_ref[...], expand)[0:1]
    lower = lax.broadcasted_iota(jnp.int32, (half, half), 0) >= lax.broadcasted_iota(
        jnp.int32, (half, half), 1
    )
    lane = lax.broadcasted_iota(jnp.int32, (BLOCK, LANES), 1)
    for block in range(PAIR):
        base = block * BLOCK
        for tile in range(width // LANES):
            columns = slice(tile * LANES, (tile + 1) * LANES)
            x = x_ref[base : base + BLOCK, columns]
            top = skip[:, columns] * x[:half].astype(F32)
            bottom = skip[:, columns] * x[half:].astype(F32)
            for side in range(LANES // HEAD_DIM):
                head = first_head + tile * (LANES // HEAD_DIM) + side
                own = jnp.where(lane // HEAD_DIM == side, x, jnp.zeros_like(x))
                cum = cum_ref[base : base + BLOCK, head : head + 1]
                row = row_ref[head : head + 1, base : base + BLOCK]
                diag = jnp.where(lower, cum[:half] - row[:, :half], -1e30)
                mixing = jnp.exp2(diag) * score_ref[base : base + half, :half]
                top = top + dot(mixing.astype(BF16), own[:half])
                left = jnp.exp2(cum[half:] - row[:, :half]) * score_ref[base + half : base + BLOCK, :half]
                diag = jnp.where(lower, cum[half:] - row[:, half:], -1e30)
                right = jnp.exp2(diag) * score_ref[base + half : base + BLOCK, half:]
                mixing = jnp.concatenate([left.astype(BF16), right.astype(BF16)], 1)
                bottom = bottom + dot(mixing, own)
            put(block, slice(base, base + half), columns, top)
            put(block, slice(base + half, base + BLOCK), columns, bottom)


def local_kernel(first_head, x_ref, cum_ref, row_ref, score_ref, skip_ref, *refs):
    out_ref = refs[-1]

    def put(block, rows, columns, value):
        out_ref[rows, columns] = value

    mix(first_head, x_ref, cum_ref, row_ref, score_ref, skip_ref, put)


def carry(first_head, place, lasts, befores, own_ref, c_ref, factor_ref, add, keep_ref, send_ref):
    expand = spread(first_head, own_ref.shape[1], 2)
    last, before = (
        refs[0][...] if len(refs) == 1 else jnp.concatenate([ref[...] for ref in refs], 1)
        for refs in (lasts, befores)
    )
    odd, core = place[1] % 2 == 1, place[2]
    near = jnp.where(odd, last[:STATE].astype(F32), 0.0)
    held = near + jnp.where(odd, decay_of(last), 1.0) * before[:STATE].astype(F32)
    factor = dot(factor_ref[...], expand)
    outs = []
    for block in range(PAIR):
        at = slice(block * BLOCK, (block + 1) * BLOCK)
        carried = dot(c_ref[at], held.astype(BF16))
        outs.append((add[at] + factor[at] * carried).astype(BF16))
        held = factor[BLOCK - 1 : BLOCK] * held + own_ref[...]

    @pl.when(core == 0)
    def _():
        keep_ref[...] = outs[0]
        send_ref[...] = outs[1]

    @pl.when(core == 1)
    def _():
        keep_ref[...] = outs[1]
        send_ref[...] = outs[0]


def final_kernel(first_head, counts, place, *refs):
    groups = []
    for number in counts:
        groups.append(refs[:number])
        refs = refs[number:]
    carry(first_head, place, *groups, *refs[:4], *refs[-2:])


def finish_kernel(first_head, counts, place, *refs):
    groups = []
    for number in counts:
        groups.append(refs[:number])
        refs = refs[number:]
    own_ref, c_ref, factor_ref = refs[:3]
    keep_ref, send_ref, partial = refs[-3:]
    local_kernel(first_head, *refs[3:8], partial)
    carry(first_head, place, *groups, own_ref, c_ref, factor_ref, partial, keep_ref, send_ref)


def place_kernel(firsts, place, *refs):
    count = len(firsts)
    keeps, gots = refs[:count], refs[count : 2 * count]
    out, sems = refs[-2:]
    core = place[2]
    half = out.shape[1] // PAIR
    copies = []
    for first, keep, got in zip(firsts, keeps, gots):
        width = keep.shape[1]
        copies.append((keep, out.at[:, ds(core * half + first, width)]))
        copies.append((got, out.at[:, ds((1 - core) * half + first, width)]))
    for copy in run(copies, sems):
        copy.wait()


def put_in_place(firsts, shape, place, keeps, gots):
    smem, vmem, hbm = (pl.BlockSpec(memory_space=m) for m in (pltpu.SMEM, pltpu.VMEM, pltpu.HBM))
    count = len(firsts)
    return pl.pallas_call(
        functools.partial(place_kernel, firsts),
        out_shape=jax.ShapeDtypeStruct(shape, BF16),
        in_specs=[smem] + [vmem] * (2 * count),
        out_specs=hbm,
        scratch_shapes=[pltpu.SemaphoreType.DMA((2 * count,))],
        compiler_params=pltpu.CompilerParams(vmem_limit_bytes=16 << 20),
        cost_estimate=pl.CostEstimate(flops=1, bytes_accessed=1, transcendentals=0),
        name="place",
    )(place, *keeps, *gots)


class Stay:
    def __init__(self, array):
        self.array = array


def gate(blocks, order):
    anywhere = pl.BlockSpec(memory_space=pl.ANY)
    return pl.pallas_call(
        lambda *refs: None,
        out_shape=[jax.ShapeDtypeStruct(block.shape, block.dtype) for block in blocks],
        in_specs=[anywhere] * (len(blocks) + len(order)),
        out_specs=[anywhere] * len(blocks),
        input_output_aliases={i: i for i in range(len(blocks))},
        compiler_params=pltpu.CompilerParams(vmem_limit_bytes=16 << 20),
        cost_estimate=pl.CostEstimate(flops=1, bytes_accessed=1, transcendentals=0),
        name="gate",
    )(*blocks, *order)


def call(body, outs, operands, scratch=(), flops=0, transcendentals=0, name=None, limit=16 << 20):
    shapes = [jax.ShapeDtypeStruct(shape, dtype) for shape, dtype in outs]
    smem, vmem, hbm = (pl.BlockSpec(memory_space=m) for m in (pltpu.SMEM, pltpu.VMEM, pltpu.HBM))
    specs = [
        hbm if isinstance(o, Stay) else smem if o.dtype == jnp.int32 else vmem for o in operands
    ]
    moved = sum(o.size * o.dtype.itemsize for o in shapes) * 2
    return pl.pallas_call(
        body,
        out_shape=shapes,
        in_specs=specs,
        out_specs=[vmem] * len(outs),
        scratch_shapes=scratch,
        compiler_params=pltpu.CompilerParams(vmem_limit_bytes=limit),
        cost_estimate=pl.CostEstimate(flops=1, bytes_accessed=1, transcendentals=0),
        name=name,
    )(*[o.array if isinstance(o, Stay) else o for o in operands])


def paired(xbc, dt_raw, conv_weight, conv_bias, a_log, dt_bias, skip_gain):
    axes = ("ctx", "head")
    shards, length = lax.axis_size("head"), lax.axis_size("ctx")
    devices, peers = shards * length, shards * PAIR
    tok = xbc.shape[0]
    slab = tok * peers
    context, shard = lax.axis_index("ctx"), lax.axis_index("head")
    pair, core = context // PAIR, context % PAIR
    group = shard * PAIR + core
    place = jnp.stack([group, pair, core, core * shards + shard, shard]).astype(jnp.int32)

    def over(block, target):
        route = [(i, target(i)) for i in range(devices)]
        return lax.ppermute(block, axes, [(i, j) for i, j in route if j is not None and j < devices])

    def swap(block):
        return over(block, lambda i: i ^ shards)

    rows = Stay(xbc)
    size = PER_GROUP + 2 * STATE
    (sent,) = call(
        functools.partial(pack_first_kernel, shards),
        [((tok, shards * WIDTHS[0]), BF16)],
        [place, rows],
        scratch=[pltpu.SemaphoreType.DMA((shards,))],
        name="pack_first",
    )
    got_first = swap(sent)
    sent, tail = call(
        functools.partial(pack_kernel, shards),
        [((tok, shards * (size - WIDTHS[0]) + HEADS), BF16), ((16, shards * size), BF16)],
        [place, rows, Stay(dt_raw), Stay(sent)],
        scratch=[pltpu.SemaphoreType.DMA((6 * shards + 1,))],
        name="pack",
    )
    got_rest = swap(gate([sent], [got_first])[0])
    taps, offset = call(
        taps_kernel,
        [((4, size), F32), ((1, size), F32)],
        [place, Stay(conv_weight), Stay(conv_bias[None]), Stay(got_rest)],
        scratch=[pltpu.SemaphoreType.DMA((6,))],
        name="taps",
    )

    def send_on(plan, order, edges=None):
        unused = Stay(got_first)
        parts = [p for _, pieces in plan for p in pieces]
        return call(
            functools.partial(merge_kernel, shards, plan, len(order)),
            [((PAIR * tok, sum(map(total_of, pieces))), BF16) for _, pieces in plan],
            [
                place,
                rows,
                Stay(dt_raw) if edges is None else dt_raw,
                got_first if 0 in parts else unused,
                got_rest if any(parts) else unused,
                unused if edges is None else edges,
            ]
            + [Stay(o) for o in order],
            scratch=[pltpu.SemaphoreType.DMA((sum(2 + 2 * len(RESTS[p]) for p in parts),))],
            name="merge",
        )

    def travel(blocks):
        return [blocks[0]] + [over(blocks[r], lambda i, r=r: i ^ FLIP[r]) for r in range(1, shards)]

    def plan(piece):
        return [(r, (piece,)) for r in range(shards)]

    first_blocks = send_on(plan(0), [])
    message = [travel(first_blocks)]
    (edges,) = call(
        functools.partial(edge_kernel, shards),
        [((3, shards * size), BF16)],
        [place, got_first, got_rest, tail],
        name="edge",
    )
    edges = over(edges, lambda i: i + peers if i % shards == shards - 1 else None)
    second_blocks = send_on(plan(1), [first_blocks[0]], edges)
    message.append(travel(second_blocks))
    third_plan = [(r, (2, 3) if r == NEAR else (2,)) for r in range(shards)]
    third_blocks = send_on(third_plan, [second_blocks[0]])
    message.append(travel(third_blocks[:1] + gate(third_blocks[1:], message[0][1:] + message[1][1:] + [taps])))

    def seen(piece):
        return message[piece]

    tiles = [p.reshape(HEADS // LANES, LANES) for p in (a_log, dt_bias, skip_gain)]
    b, edge, cum, row, factor, tail, skip = call(
        functools.partial(prep_kernel, shards),
        [
            ((slab, STATE), BF16),
            ((4, size), F32),
            ((slab, LANES), F32),
            ((LANES, slab), F32),
            ((slab, 2 * LANES), BF16),
            ((slab, 2 * LANES), BF16),
            ((16, 3 * LANES), BF16),
        ],
        [place] + seen(1) + [taps, offset] + tiles + [Stay(third_blocks[0])],
        scratch=[pltpu.VMEM((slab, LANES), F32), pltpu.VMEM((slab + 8, STATE), F32)],
        name="prep",
    )
    count = len(GROUPED)
    x, sent, own, last, joined, before, keep, send = ([None] * count for _ in range(8))

    def first_head(i):
        return (sum(WIDTHS[: GROUPED[i][0]]) + GROUPED[i][1]) // HEAD_DIM

    def state_of(i, order):
        piece, _, width = GROUPED[i]
        x[i], own[i], *sent[i] = call(
            functools.partial(state_kernel, shards, GROUPED[i], FIRST_ROUND[i]),
            [((slab, width), BF16), ((STATE, width), F32)] + [((STATE + 16, w), BF16) for w in FIRST_ROUND[i]],
            [place] + seen(piece) + [taps, offset, edge, b, factor, tail] + [Stay(o) for o in order],
            scratch=[pltpu.VMEM((slab + 8, width), F32)],
            name="state",
        )
        last[i] = [over(part, lambda i: i ^ peers if i // peers != 3 else None) for part in sent[i]]

    def combine_of(i, order):
        joined[i], before[i] = [], []
        end = 0
        for width in SECOND_ROUND[i]:
            begin, end = end, end + width
            early, late, spans, first = [], [], [], 0
            for got, mine, size_of in zip(last[i], sent[i], FIRST_ROUND[i]):
                low, high = max(begin - first, 0), min(end - first, size_of)
                first += size_of
                if low < high:
                    early.append(got)
                    late.append(mine)
                    spans.append(slice(low, high))
            (total,) = call(
                functools.partial(combine_kernel, spans),
                [((STATE + 16, width), BF16)],
                [place] + early + late + [Stay(o) for o in order],
                name="combine",
            )
            joined[i].append(total)
            before[i].append(over(total, lambda i: i + 2 * peers))
            order = [total]

    def finish_of(body, i, operands, order, **more):
        keep[i], send[i] = call(
            functools.partial(body, first_head(i), (len(last[i]), len(before[i]))),
            [((BLOCK, GROUPED[i][2]), BF16)] * 2,
            [place, *last[i], *before[i], own[i], c, factor] + operands + [Stay(o) for o in order],
            name="final",
            **more,
        )

    partial = [None] * count

    def local_of(i, order):
        (partial[i],) = call(
            functools.partial(local_kernel, first_head(i)),
            [(x[i].shape, F32)],
            [x[i], cum, row, score, skip] + [Stay(o) for o in order],
            name="local",
        )

    state_of(0, [])
    own_block, *fourth_blocks = send_on([(r, (3,)) for r in range(shards) if r != NEAR], sent[0])
    fourth_blocks = gate(fourth_blocks, message[2][1:NEAR])
    fourth_blocks = [over(block, lambda i, r=r: i ^ FLIP[r]) for r, block in enumerate(fourth_blocks, 1)]
    message.append([own_block, *fourth_blocks, message[2][NEAR]])
    combine_of(0, [own_block])
    state_of(1, joined[0])
    combine_of(1, [])
    state_of(2, joined[1])
    c, score = call(
        functools.partial(score_kernel, shards),
        [((slab, STATE), BF16), ((slab, BLOCK), F32)],
        [place] + seen(3) + [taps, offset, edge, b] + [Stay(o) for o in sent[2]],
        scratch=[pltpu.VMEM((slab + 8, STATE), F32)],
        name="score",
    )
    state_of(3, [score])
    local_of(0, sent[3])

    def in_full(i, order):
        wide = [pltpu.VMEM((slab, GROUPED[i][2]), F32)]
        finish_of(finish_kernel, i, [x[i], cum, row, score, skip], order, scratch=wide)

    combine_of(2, [partial[0]] + before[1] + before[0])
    in_full(1, joined[2])
    combine_of(3, [keep[1]])
    local_of(2, joined[3])
    local_of(3, [partial[2]])
    finish_of(final_kernel, 0, [partial[0]], [partial[3]])
    finish_of(final_kernel, 2, [partial[2]], [keep[0]])
    finish_of(final_kernel, 3, [partial[3]], [keep[2]])
    firsts = [first_head(i) * HEAD_DIM for i in range(count)]
    return put_in_place(firsts, (BLOCK, PAIR * PER_GROUP), place, keep, [swap(o) for o in send])


def solution(mesh):
    in_specs = (P(("ctx", "head"), None), P(("ctx", "head"), None), P(), P(), P(), P(), P())
    out_specs = P("ctx", "head")
    shards, length = mesh.shape["head"], mesh.shape["ctx"]

    def program(xbc, *rest):
        slab = xbc.shape[0] // length
        fits = shards == GROUPS // PAIR and length == 4 * PAIR and slab == BLOCK
        return jax.shard_map(
            paired if fits else on_device,
            mesh=mesh,
            in_specs=in_specs,
            out_specs=out_specs,
            check_vma=False,
        )(xbc, *rest)

    return program
```
